32 devices in a mesh: expert: 8 (over z, core), tensor: 4 (over y, x).
Axes of the slice: x: 2, y: 2, z: 4, core: 2. Of those that a mesh axis runs over, the one named last changes fastest.
Arguments:
- layer_input: bfloat16 [1024, 16384], P(None, 'expert'), may hold values from -18 to 18
- gain_one: float32 [1024], replicated, may hold values from 0.1 to 1.9
- attn_in: bfloat16 [3, 1024, 1024], P(None, 'tensor'), may hold values from -0.1875 to 0.1875
- rel_bias: float32 [32, 16], P(None, 'tensor'), may hold values from -4 to 4
- attn_out: bfloat16 [1024, 1024], P('tensor'), may hold values from -0.75 to 0.75
- gain_two: float32 [1024], replicated, may hold values from 0.1 to 1.9
- router: bfloat16 [1024, 16], replicated, may hold values from -0.375 to 0.375
- expert_gate: bfloat16 [16, 2816, 1024], P('expert', 'tensor'), may hold values from -0.1875 to 0.1875
- expert_up: bfloat16 [16, 2816, 1024], P('expert', 'tensor'), may hold values from -0.1875 to 0.1875
- expert_down: bfloat16 [16, 2816, 1024], P('expert', 'tensor'), may hold values from -0.21875 to 0.21875
- routes: int32 [16384, 2], P('expert'), may hold values from 0 to 15, all different within a row
- piece_starts: int32 [16, 2], P('expert'), may hold values from 0 to 768, as said below
- grad_out: bfloat16 [1024, 16384], P(None, 'expert'), may hold values from -6 to 6
Outputs:
- layer_output: bfloat16 [1024, 16384], P(None, 'expert')
- grad_input: float32 [1024, 16384], P(None, 'expert')
- grad_gain_one: float32 [1024], replicated
- grad_attn_in: float32 [3, 1024, 1024], P(None, 'tensor')
- grad_rel_bias: float32 [32, 16], P(None, 'tensor')
- grad_attn_out: float32 [1024, 1024], P('tensor')
- grad_gain_two: float32 [1024], replicated
- grad_router: float32 [1024, 16], replicated
- grad_expert_gate: float32 [16, 2816, 1024], P('expert', 'tensor')
- grad_expert_up: float32 [16, 2816, 1024], P('expert', 'tensor')
- grad_expert_down: float32 [16, 2816, 1024], P('expert', 'tensor')
The draws below stay inside these ranges and needn't reach their ends.
Inputs may be any that keep to these rules, and one draw needn't show every extreme that they name: `piece_starts`: start i of a sequence lies in [2 * 256 * i, 2 * 256 * i + 256], so the pieces of a sequence never intersect and lie inside it. `routes`: the 2 experts of a token differ.
All inputs are finite; a program needn't handle non-finite values.
Results may differ from the reference program's by a relative error of at most 0.019.
Values may be sent and summed in bfloat16 or wider, within the bound.
A program may use at most 384 MiB of HBM per device.

```python
import jax
import jax.numpy as jnp
from jax import lax

D = 1024
HEADS = 16
HEAD_DIM = 64
FF = 2816
EXPERTS = 16
BUCKETS = 32
TOP = 2
PIECE = 256
SEQ = 1024
TOK_DEV = 2048
TOKENS = 16384
SEQS = 16
PIECES = 2
CAP = 320
N_EXPERT = 8


def draw_layer_input(key, part):
    key_main = jax.random.fold_in(key, 0)
    column = 10.0 ** (jnp.arange(D, dtype=jnp.float32) / D - 0.5)
    values = jnp.clip(jax.random.normal(key_main, (D, TOKENS), jnp.float32), -4.0, 4.0)
    return (values * column[:, None]).astype(jnp.bfloat16)


def draw_piece_starts(key, part):
    offsets = jax.random.randint(key, (SEQS, PIECES), 0, PIECE + 1)
    offsets = offsets.at[0, 0].set(0).at[SEQS - 1, PIECES - 1].set(PIECE)
    spacing = 2 * PIECE * jnp.arange(PIECES, dtype=jnp.int32)
    return (offsets + spacing[None, :]).astype(jnp.int32)


def block_scale(own_key, extent, cuts, low, top_value):
    level = 1.0
    for dim, parts in cuts:
        steps = jax.random.uniform(jax.random.fold_in(jax.random.fold_in(own_key, 6), dim), (parts,), jnp.float32, low / len(cuts), top_value / len(cuts))
        level = level * jnp.repeat(jnp.exp(steps), extent[dim] // parts).reshape((-1,) + (1,) * (len(extent) - 1 - dim))
    return level


def choose_distinct(key, rows, count, top, lift):
    ranking = jax.random.permutation(jax.random.fold_in(key, 1), count)
    pull = ranking
    for power in range(3):
        pull = pull * pull // count
    pull = pull * lift // count
    chance = jax.random.randint(jax.random.fold_in(key, 2), (rows, count), 0, 4096) + pull
    fixed_rows = jax.random.permutation(jax.random.fold_in(key, 3), rows)[jnp.arange(count) % rows]
    chance = jnp.where(jnp.arange(rows)[:, None] == fixed_rows[None, :], 1 << 14, chance)
    score = chance * count + jnp.arange(count)
    return lax.top_k(score.astype(jnp.int32), top)[1].astype(jnp.int32)


def gaussian(key, dims, width, bound, pieces=(), kind=jnp.bfloat16):
    drawn = width * jax.random.normal(key, dims, jnp.float32)
    if pieces:
        drawn = drawn * block_scale(key, dims, pieces, -0.22, 0.18)
    return jnp.clip(drawn, -bound, bound).astype(kind)


def setup_inputs(seed: int = 0) -> dict:
    keys = jax.random.split(jax.random.key(seed), 14)
    return {
        "layer_input": draw_layer_input(jax.random.fold_in(keys[13], 71), 0),
        "gain_one": jnp.clip(1.0 + 0.18 * jax.random.normal(keys[1], (D,), jnp.float32), 0.1, 1.9),
        "attn_in": gaussian(keys[2], (3, HEADS * HEAD_DIM, D), D ** -0.5, 0.1875, ((1, 4),)),
        "rel_bias": gaussian(keys[3], (BUCKETS, HEADS), 1.0, 4.0, ((1, 4),), jnp.float32),
        "attn_out": gaussian(keys[4], (HEADS * HEAD_DIM, D), (HEADS * HEAD_DIM // 16) ** -0.5, 0.75, ((0, 4),)),
        "gain_two": jnp.clip(1.0 + 0.18 * jax.random.normal(keys[5], (D,), jnp.float32), 0.1, 1.9),
        "router": gaussian(keys[6], (D, EXPERTS), (D // 4) ** -0.5, 0.375),
        "expert_gate": gaussian(keys[7], (EXPERTS, FF, D), D ** -0.5, 0.1875, ((0, 8), (1, 4))),
        "expert_up": gaussian(keys[8], (EXPERTS, FF, D), D ** -0.5, 0.1875, ((0, 8), (1, 4))),
        "expert_down": gaussian(keys[9], (EXPERTS, FF, D), (FF // 4) ** -0.5, 0.21875, ((0, 8), (1, 4))),
        "routes": choose_distinct(keys[10], TOKENS, EXPERTS, TOP, 1024),
        "piece_starts": draw_piece_starts(jax.random.fold_in(keys[13], 71), 0),
        "grad_out": gaussian(keys[12], (D, TOKENS), 1.0, 6.0, ((1, 8),)),
    }


EPS = 1e-06
NEG = -1e+30
THRESHOLDS = (12, 16, 23, 32, 46, 64, 91)
HIGH = lax.Precision.HIGHEST

@jax.custom_vjp
def low(v):
    return lax.optimization_barrier(v.astype(jnp.bfloat16)).astype(jnp.float32)

@jax.custom_vjp
def low_back(v):
    return v

def low_keep(v):
    return (low(v), None)

def low_pass(kept, grad):
    return (grad,)

def back_keep(v):
    return (v, None)

def back_low(kept, grad):
    return (low(grad),)
low.defvjp(low_keep, low_pass)
low_back.defvjp(back_keep, back_low)

def both_ways(tensor_value):
    return low(low_back(tensor_value))

def bucket_of(offset):
    magnitude = jnp.abs(offset)
    beyond = sum(((magnitude >= threshold).astype(jnp.int32) for threshold in THRESHOLDS))
    lower_part = jnp.where(magnitude < 8, magnitude, 8 + beyond)
    return lower_part + 16 * (offset > 0).astype(jnp.int32)

def allowed_pairs(seq_starts):
    position = jnp.arange(SEQ, dtype=jnp.int32)
    inside = (position[:, None] >= seq_starts[None, :]) & (position[:, None] < seq_starts[None, :] + PIECE)
    numbers = jnp.arange(seq_starts.shape[0], dtype=jnp.int32) + 1
    piece_label = lax.optimization_barrier(jnp.sum(inside.astype(jnp.int32) * numbers[None, :], axis=1))
    causal = position[None, :] <= position[:, None]
    shared = (piece_label[:, None] == piece_label[None, :]) & (piece_label[:, None] > 0)
    return causal | shared

def slot_table(routes):
    flat_routes = routes.reshape(-1)
    onehot = (flat_routes[:, None] == jnp.arange(EXPERTS, dtype=jnp.int32)[None, :]).astype(jnp.int32)
    before = jnp.cumsum(onehot, axis=0) - onehot
    slot_number = lax.optimization_barrier(jnp.sum(before * onehot, axis=1))
    kept_pairs = slot_number < CAP
    slot_index = jnp.where(kept_pairs, flat_routes * CAP + slot_number, EXPERTS * CAP)
    return (slot_index.reshape(routes.shape), kept_pairs.reshape(routes.shape))

def rms_scale(tensor_value):
    return lax.rsqrt(lax.optimization_barrier(jnp.mean(tensor_value * tensor_value, axis=-1, keepdims=True)) + EPS)

def forward(params, tokens, routes, starts):
    gain_one, attn_in, rel_bias, attn_out, gain_two, router, expert_gate, expert_up, expert_down = params
    tok_count = tokens.shape[0]
    normed = low(tokens * rms_scale(tokens) * gain_one)
    project = jnp.einsum('td,chd->cth', normed, attn_in, precision=HIGH)
    project = both_ways(project).reshape(3, tok_count // SEQ, SEQ, HEADS, HEAD_DIM)
    offsets = jnp.arange(SEQ, dtype=jnp.int32)[None, :] - jnp.arange(SEQ, dtype=jnp.int32)[:, None]
    bias_full = jnp.transpose(rel_bias[bucket_of(offsets)], (2, 0, 1))

    def attend(inputs):
        queries, key_rows, value_rows, seq_starts = inputs
        scores = jnp.einsum('qhe,khe->hqk', queries, key_rows, precision=HIGH) * 0.125 + bias_full
        scores = low_back(scores)
        scores = jnp.where(allowed_pairs(seq_starts)[None], scores, NEG)
        weights = low(jax.nn.softmax(scores, axis=-1))
        return jnp.einsum('hqk,khe->qhe', weights, value_rows, precision=HIGH)
    mixed_heads = lax.map(jax.checkpoint(attend), (project[0], project[1], project[2], starts))
    mixed_heads = both_ways(mixed_heads.reshape(tok_count, HEADS * HEAD_DIM))
    resid = tokens + low_back(jnp.dot(mixed_heads, attn_out, precision=HIGH))
    normed_two = low(resid * rms_scale(resid) * gain_two)
    logits = jnp.dot(normed_two, router, precision=HIGH)
    chosen = (routes[:, :, None] == jnp.arange(EXPERTS, dtype=jnp.int32)[None, None, :]).astype(logits.dtype)
    picked = jnp.einsum('tke,te->tk', chosen, logits, precision=HIGH)
    gate_weights = jax.nn.softmax(picked, axis=-1)
    slot_index, kept_pairs = slot_table(routes)
    token_rows = jnp.repeat(normed_two, TOP, axis=0)
    buffer = jnp.zeros((EXPERTS * CAP + 1, D), logits.dtype).at[slot_index.reshape(-1)].set(token_rows)
    buffer = low_back(buffer[:EXPERTS * CAP].reshape(EXPERTS, CAP, D))
    gate_part = low_back(jnp.einsum('ecd,efd->ecf', buffer, expert_gate, precision=HIGH))
    up_part = low_back(jnp.einsum('ecd,efd->ecf', buffer, expert_up, precision=HIGH))
    hidden = low(jax.nn.gelu(gate_part, approximate=True) * up_part)
    outputs = both_ways(jnp.einsum('ecf,efd->ecd', hidden, expert_down, precision=HIGH)).reshape(EXPERTS * CAP, D)
    fetched = outputs[jnp.minimum(slot_index, EXPERTS * CAP - 1)]
    mix_weight = gate_weights * kept_pairs.astype(gate_weights.dtype)
    return resid + jnp.einsum('tk,tkd->td', mix_weight, fetched, precision=HIGH)

def reference(layer_input, gain_one, attn_in, rel_bias, attn_out, gain_two, router, expert_gate, expert_up, expert_down, routes, piece_starts, grad_out):
    params = (gain_one, attn_in.astype(jnp.float32), rel_bias, attn_out.astype(jnp.float32), gain_two, router.astype(jnp.float32), expert_gate.astype(jnp.float32), expert_up.astype(jnp.float32), expert_down.astype(jnp.float32))
    tokens = layer_input.astype(jnp.float32).T.reshape(N_EXPERT, TOK_DEV, D)
    cotangent = grad_out.astype(jnp.float32).T.reshape(N_EXPERT, TOK_DEV, D)
    route_groups = routes.reshape(N_EXPERT, TOK_DEV, TOP)
    start_groups = piece_starts.reshape(N_EXPERT, TOK_DEV // SEQ, PIECES)
    zeroed = jax.tree.map(jnp.zeros_like, params)

    def per_group(running, items):
        group_tokens, group_routes, group_starts, group_cot = items

        def apply(param_set, token_set):
            return forward(param_set, token_set, group_routes, group_starts)
        result, pullback = jax.vjp(apply, params, group_tokens)
        grad_params, grad_tokens = pullback(group_cot)
        running = jax.tree.map(jnp.add, running, grad_params)
        return (running, (result.astype(jnp.bfloat16), grad_tokens))
    running, (outputs, grad_tokens) = lax.scan(per_group, zeroed, (tokens, route_groups, start_groups, cotangent))
    return (outputs.reshape(TOKENS, D).T, grad_tokens.reshape(TOKENS, D).T, running[0], running[1], running[2], running[3], running[4], running[5], running[6], running[7], running[8])
```

```python
from functools import partial

import jax
import jax.numpy as jnp
from jax import lax
from jax.experimental import pallas as pl
from jax.experimental.pallas import tpu as pltpu
from jax.sharding import PartitionSpec as P

EXPERTS = 16
BUCKETS = 32
TOP = 2
PIECE = 256
SEQ = 1024
CAP = 320
BLK = 256


EPS = 1e-06
NEG = -1e30
THRESHOLDS = (12, 16, 23, 32, 46, 64, 91)
HIGH = lax.Precision.HIGHEST
F32 = jnp.float32
BF16 = jnp.bfloat16
NN = (((1,), (0,)), ((), ()))
NT = (((1,), (1,)), ((), ()))
TN = (((0,), (0,)), ((), ()))
MIB = 1 << 20


def mm(left, right, dims=NN):
    return lax.dot_general(left, right, dims, preferred_element_type=F32)


def params(limit=56):
    return pltpu.CompilerParams(vmem_limit_bytes=limit * MIB)


def cost(flops, bytes_accessed, transcendentals=0):
    return pl.CostEstimate(
        flops=int(flops), bytes_accessed=int(bytes_accessed), transcendentals=int(transcendentals)
    )


def bucket_of(offset):
    magnitude = jnp.abs(offset)
    beyond = sum(((magnitude >= threshold).astype(jnp.int32) for threshold in THRESHOLDS))
    lower_part = jnp.where(magnitude < 8, magnitude, 8 + beyond)
    return lower_part + 16 * (offset > 0).astype(jnp.int32)


def project_kernel(x_ref, gain_ref, w_ref, out_ref, scale_ref):
    x = x_ref[...].astype(F32)
    scale = lax.rsqrt(jnp.sum(x * x, axis=0, keepdims=True) / x.shape[0] + EPS)
    normed = (x * scale * gain_ref[...]).astype(BF16)
    out_ref[...] = mm(w_ref[...], normed).astype(BF16)
    scale_ref[...] = scale


def project(x, gain, weights):
    width, tokens = x.shape
    rows = weights.shape[0]
    tile = 512
    return pl.pallas_call(
        project_kernel,
        grid=(tokens // tile,),
        in_specs=[
            pl.BlockSpec((width, tile), lambda i: (0, i)),
            pl.BlockSpec((width, 1), lambda i: (0, 0)),
            pl.BlockSpec((rows, width), lambda i: (0, 0)),
        ],
        out_specs=[
            pl.BlockSpec((rows, tile), lambda i: (0, i)),
            pl.BlockSpec((1, tile), lambda i: (0, i)),
        ],
        out_shape=[
            jax.ShapeDtypeStruct((rows, tokens), BF16),
            jax.ShapeDtypeStruct((1, tokens), F32),
        ],
        compiler_params=params(),
        cost_estimate=cost(2 * width * tokens * rows, 2 * width * tokens * 2),
    )(x, gain, weights)


def bias_tiles_kernel(table_ref, tiles_ref):
    key_at = lax.broadcasted_iota(jnp.int32, (BLK, BLK), 0)
    query_at = lax.broadcasted_iota(jnp.int32, (BLK, BLK), 1)
    for number, shift in enumerate((-1, 0, 1)):
        offset = key_at - query_at + shift * BLK
        bucket = bucket_of(offset)
        low, high = {-1: (0, 16), 0: (0, 32), 1: (16, 32)}[shift]
        for head in range(tiles_ref.shape[0]):
            far = table_ref[15, head]
            value = jnp.zeros((BLK, BLK), F32)
            for index in range(low, high):
                value = jnp.where(bucket == index, table_ref[index, head] - far, value)
            tiles_ref[head, number] = value


def bias_tiles(table):
    heads = table.shape[1]
    return pl.pallas_call(
        bias_tiles_kernel,
        in_specs=[pl.BlockSpec(memory_space=pltpu.SMEM)],
        out_specs=pl.BlockSpec(memory_space=pltpu.VMEM),
        out_shape=jax.ShapeDtypeStruct((heads, 3, BLK, BLK), F32),
        compiler_params=params(),
        cost_estimate=cost(heads * 3 * BLK * BLK * 60, heads * 3 * BLK * BLK * 4),
    )(table)


def bias_fold_kernel(near_ref, far_ref, out_ref):
    heads = near_ref.shape[1]
    key_at = lax.broadcasted_iota(jnp.int32, (BLK, BLK), 0)
    query_at = lax.broadcasted_iota(jnp.int32, (BLK, BLK), 1)
    totals = [[jnp.zeros((8, BLK), F32) for _ in range(BUCKETS)] for _ in range(heads)]
    for number, shift in enumerate((-1, 0, 1)):
        bucket = bucket_of(key_at - query_at + shift * BLK)
        low, high = {-1: (0, 16), 0: (0, 32), 1: (16, 32)}[shift]
        for head in range(heads):
            grads = near_ref[0, head, number] + near_ref[1, head, number]
            for index in range(low, high):
                kept = jnp.where(bucket == index, grads, 0.0)
                totals[head][index] = totals[head][index] + jnp.sum(
                    kept.reshape(BLK // 8, 8, BLK), axis=0
                )
    for head in range(heads):
        totals[head][15] = totals[head][15] + far_ref[0, head] + far_ref[1, head]
        for index in range(BUCKETS):
            line = jnp.sum(totals[head][index], axis=0, keepdims=True)
            out_ref[head, index : index + 1, :] = jnp.broadcast_to(
                jnp.sum(line, axis=1, keepdims=True), (1, 128)
            )


def bias_fold(near, far):
    heads = near.shape[1]
    return pl.pallas_call(
        bias_fold_kernel,
        in_specs=[pl.BlockSpec(memory_space=pltpu.VMEM)] * 2,
        out_specs=pl.BlockSpec(memory_space=pltpu.VMEM),
        out_shape=jax.ShapeDtypeStruct((heads, BUCKETS, 128), F32),
        compiler_params=params(),
        cost_estimate=cost(heads * 3 * BLK * BLK * 60, heads * 6 * BLK * BLK * 4),
    )(near, far)


def key_count(query_block):
    return 2 * BLK if query_block < 2 else 4 * BLK


def block_scores(keys, queries, tiles_ref, limit, block):
    count = key_count(block)
    parts = []
    whole = mm(keys[:, :count], queries, TN)
    for key_block in range(count // BLK):
        part = whole[key_block * BLK : (key_block + 1) * BLK]
        shift = key_block - block
        if -1 <= shift <= 1:
            part = part + tiles_ref[0, shift + 1]
        if shift >= 0:
            key_at = lax.broadcasted_iota(jnp.int32, (BLK, BLK), 0) + key_block * BLK
            part = jnp.where(key_at <= limit, part, NEG)
        parts.append(part)
    return jnp.concatenate(parts, axis=0)


def attend_kernel(q_ref, k_ref, v_ref, tiles_ref, limit_ref, w_ref, out_ref, lse_ref, sent_ref, held):
    head = pl.program_id(0)
    width = q_ref.shape[0]
    queries = q_ref[...] * BF16(0.125)
    keys, values = k_ref[...], v_ref[...]
    for block in range(SEQ // BLK):
        cols = slice(block * BLK, (block + 1) * BLK)
        scores = block_scores(keys, queries[:, cols], tiles_ref, limit_ref[0, :, cols], block)
        top = jnp.max(scores, axis=0, keepdims=True)
        exponent = jnp.exp(scores - top)
        total = jnp.sum(exponent, axis=0, keepdims=True)
        mixed = mm(values[:, : key_count(block)], exponent.astype(BF16)) / total
        mixed = mixed.astype(BF16)
        out_ref[:, cols] = mixed
        held[pl.ds(pl.multiple_of(head * width, width), width), cols] = mixed
        lse_ref[0, :, cols] = top + jnp.log(total)

    @pl.when(head == pl.num_programs(0) - 1)
    def _():
        sent_ref[...] = mm(held[...], w_ref[...], TN).astype(BF16)


def attend(qkv, tiles, limits, attn_out, seq):
    heads = tiles.shape[0]
    width = qkv.shape[0] // (3 * heads)
    model_width = attn_out.shape[1]
    return pl.pallas_call(
        attend_kernel,
        grid=(heads,),
        in_specs=[
            pl.BlockSpec((width, SEQ), lambda h: (h, seq)),
            pl.BlockSpec((width, SEQ), lambda h: (heads + h, seq)),
            pl.BlockSpec((width, SEQ), lambda h: (2 * heads + h, seq)),
            pl.BlockSpec((1, 3, BLK, BLK), lambda h: (h, 0, 0, 0)),
            pl.BlockSpec((1, 1, SEQ), lambda h: (seq, 0, 0)),
            pl.BlockSpec((heads * width, model_width), lambda h: (0, 0)),
        ],
        out_specs=[
            pl.BlockSpec((width, SEQ), lambda h: (h, 0)),
            pl.BlockSpec((1, 1, SEQ), lambda h: (h, 0, 0)),
            pl.BlockSpec((SEQ, model_width), lambda h: (0, 0)),
        ],
        out_shape=[
            jax.ShapeDtypeStruct((heads * width, SEQ), BF16),
            jax.ShapeDtypeStruct((heads, 1, SEQ), F32),
            jax.ShapeDtypeStruct((SEQ, model_width), BF16),
        ],
        scratch_shapes=[pltpu.VMEM((heads * width, SEQ), BF16)],
        compiler_params=params(),
        cost_estimate=cost(heads * SEQ * SEQ * 512, heads * SEQ * 2048, heads * SEQ * SEQ),
    )(qkv, qkv, qkv, tiles, limits, attn_out)


def attend_back_kernel(
    q_ref, k_ref, v_ref, tiles_ref, limit_ref, w_ref, grad_ref, lse_ref,
    dq_ref, dk_ref, dv_ref, near_ref, far_ref, held,
):
    head = pl.program_id(0)
    width = q_ref.shape[0]

    @pl.when(head == 0)
    def _():
        held[...] = mm(w_ref[...], grad_ref[...], NT).astype(BF16)

    queries = q_ref[...] * BF16(0.125)
    keys, values = k_ref[...], v_ref[...]
    grads = held[pl.ds(pl.multiple_of(head * width, width), width), :]
    near_ref[...] = jnp.zeros_like(near_ref)
    far = jnp.zeros((8, BLK), F32)
    grad_keys = jnp.zeros((width, SEQ), F32)
    grad_values = jnp.zeros((width, SEQ), F32)
    for block in range(SEQ // BLK):
        count = key_count(block)
        cols = slice(block * BLK, (block + 1) * BLK)
        scores = block_scores(keys, queries[:, cols], tiles_ref, limit_ref[0, :, cols], block)
        probs = jnp.exp(scores - lse_ref[0, :, cols])
        grad_probs = mm(values[:, :count], grads[:, cols], TN)
        inner = jnp.sum(probs * grad_probs, axis=0, keepdims=True)
        grad_scores = probs * (grad_probs - inner)
        for key_block in range(count // BLK):
            part = grad_scores[key_block * BLK : (key_block + 1) * BLK]
            shift = key_block - block
            if -1 <= shift <= 1:
                near_ref[0, shift + 1] += part
            elif shift < -1:
                far = far + jnp.sum(part.reshape(BLK // 8, 8, BLK), axis=0)
        rounded = grad_scores.astype(BF16)
        add_values = mm(grads[:, cols], probs.astype(BF16), NT)
        add_keys = mm(queries[:, cols], rounded, NT)
        if count == SEQ:
            grad_values = grad_values + add_values
            grad_keys = grad_keys + add_keys
        else:
            filler = jnp.zeros((width, SEQ - count), F32)
            grad_values = grad_values + jnp.concatenate([add_values, filler], axis=1)
            grad_keys = grad_keys + jnp.concatenate([add_keys, filler], axis=1)
        dq_ref[0, :, cols] = (mm(keys[:, :count], rounded) * 0.125).astype(BF16)
    dk_ref[0] = grad_keys.astype(BF16)
    dv_ref[0] = grad_values.astype(BF16)
    far_ref[0] = far


def attend_back(qkv, tiles, limits, attn_out, grad_attn, lse, seq):
    heads = tiles.shape[0]
    width = qkv.shape[0] // (3 * heads)
    model_width = attn_out.shape[1]
    grad_spec = pl.BlockSpec((1, width, SEQ), lambda h: (h, 0, 0))
    return pl.pallas_call(
        attend_back_kernel,
        grid=(heads,),
        in_specs=[
            pl.BlockSpec((width, SEQ), lambda h: (h, seq)),
            pl.BlockSpec((width, SEQ), lambda h: (heads + h, seq)),
            pl.BlockSpec((width, SEQ), lambda h: (2 * heads + h, seq)),
            pl.BlockSpec((1, 3, BLK, BLK), lambda h: (h, 0, 0, 0)),
            pl.BlockSpec((1, 1, SEQ), lambda h: (seq, 0, 0)),
            pl.BlockSpec((heads * width, model_width), lambda h: (0, 0)),
            pl.BlockSpec((SEQ, model_width), lambda h: (0, 0)),
            pl.BlockSpec((1, 1, SEQ), lambda h: (h, 0, 0)),
        ],
        out_specs=[
            grad_spec,
            grad_spec,
            grad_spec,
            pl.BlockSpec((1, 3, BLK, BLK), lambda h: (h, 0, 0, 0)),
            pl.BlockSpec((1, 8, BLK), lambda h: (h, 0, 0)),
        ],
        out_shape=[jax.ShapeDtypeStruct((heads, width, SEQ), BF16)] * 3
        + [
            jax.ShapeDtypeStruct((heads, 3, BLK, BLK), F32),
            jax.ShapeDtypeStruct((heads, 8, BLK), F32),
        ],
        scratch_shapes=[pltpu.VMEM((heads * width, SEQ), BF16)],
        compiler_params=params(),
        cost_estimate=cost(heads * SEQ * SEQ * 1280, heads * SEQ * 4096, heads * SEQ * SEQ),
    )(qkv, qkv, qkv, tiles, limits, attn_out, grad_attn, lse)


def project_back_kernel(
    x_ref, gain_ref, scale_ref, w_ref, *refs
):
    grad_refs, (weight_ref, out_ref) = refs[:3], refs[3:]
    grads = jnp.concatenate([ref[...] for ref in grad_refs], axis=0)
    normed = (x_ref[...].astype(F32) * scale_ref[...] * gain_ref[...]).astype(BF16)
    update = mm(grads, normed, NT)

    @pl.when(pl.program_id(0) == 0)
    def _():
        weight_ref[...] = update

    @pl.when(pl.program_id(0) > 0)
    def _():
        weight_ref[...] += update

    out_ref[0] = mm(w_ref[...], grads).astype(BF16)


def project_back(x, gain, scale, weights_t, grads, seq, ranks):
    width = x.shape[0]
    rows = weights_t.shape[1]
    tile = SEQ // ranks
    return pl.pallas_call(
        project_back_kernel,
        grid=(ranks,),
        in_specs=[
            pl.BlockSpec((width, tile), lambda i: (0, seq * ranks + i)),
            pl.BlockSpec((width, 1), lambda i: (0, 0)),
            pl.BlockSpec((1, tile), lambda i: (0, seq * ranks + i)),
            pl.BlockSpec((width, rows), lambda i: (0, 0)),
        ]
        + [pl.BlockSpec((rows // 3, tile), lambda i: (0, i))] * 3,
        out_specs=[
            pl.BlockSpec((rows, width), lambda i: (0, 0)),
            pl.BlockSpec((1, width, tile), lambda i: (i, 0, 0)),
        ],
        out_shape=[
            jax.ShapeDtypeStruct((rows, width), F32),
            jax.ShapeDtypeStruct((ranks, width, tile), BF16),
        ],
        compiler_params=params(),
        cost_estimate=cost(4 * width * SEQ * rows, 6 * width * SEQ),
    )(x, gain, scale, weights_t, *grads)


def code_kernel(place_ref, routes_ref, code_ref, half, groups):
    pair_class, half_index = place_ref[0], place_ref[1]
    tokens = routes_ref.shape[1]
    expert = lax.broadcasted_iota(jnp.int32, (EXPERTS, BLK), 0)
    earlier = (
        lax.broadcasted_iota(jnp.int32, (BLK, BLK), 0) < lax.broadcasted_iota(jnp.int32, (BLK, BLK), 1)
    ).astype(F32).astype(BF16)
    carry = jnp.zeros((EXPERTS, 1), F32)
    for block in range(tokens // BLK):
        cols = slice(block * BLK, (block + 1) * BLK)
        routes = routes_ref[:, cols]
        hits = [(routes[i : i + 1] == expert) for i in range(TOP)]
        chosen = sum(hit.astype(F32) for hit in hits)
        before = mm(chosen.astype(BF16), earlier) + carry
        carry = carry + jnp.sum(chosen, axis=1, keepdims=True)
        for i in range(TOP):
            slot = jnp.sum(jnp.where(hits[i], before, 0.0), axis=0, keepdims=True).astype(jnp.int32)
            route = routes[i : i + 1]
            owner = route // 2
            local = slot - half_index * half
            mine = (route - 2 * owner == pair_class) & (local >= 0) & (local < half)
            code_ref[i : i + 1, cols] = jnp.where(mine, owner * half + local, -1)


def local_codes(place, routes_t, half, groups):
    return pl.pallas_call(
        partial(code_kernel, half=half, groups=groups),
        in_specs=[
            pl.BlockSpec(memory_space=pltpu.SMEM),
            pl.BlockSpec(memory_space=pltpu.VMEM),
        ],
        out_specs=pl.BlockSpec(memory_space=pltpu.VMEM),
        out_shape=jax.ShapeDtypeStruct(routes_t.shape, jnp.int32),
        compiler_params=params(),
    )(place, routes_t)


def gates_kernel(h0_ref, h1_ref, router_ref, routes_ref, gates_ref):
    expert = lax.broadcasted_iota(jnp.int32, (EXPERTS, SEQ), 0)
    for seq, ref in enumerate((h0_ref, h1_ref)):
        cols = slice(seq * SEQ, (seq + 1) * SEQ)
        logits = mm(router_ref[...], ref[...], NT)
        picked = [
            jnp.sum(jnp.where(routes_ref[i : i + 1, cols] == expert, logits, 0.0), axis=0, keepdims=True)
            for i in range(TOP)
        ]
        top = jnp.maximum(picked[0], picked[1])
        raised = [jnp.exp(value - top) for value in picked]
        total = raised[0] + raised[1]
        for i in range(TOP):
            gates_ref[i : i + 1, cols] = raised[i] / total


def pair_gates(h0, h1, router_t, routes_t):
    return pl.pallas_call(
        gates_kernel,
        in_specs=[pl.BlockSpec(memory_space=pltpu.VMEM)] * 4,
        out_specs=pl.BlockSpec(memory_space=pltpu.VMEM),
        out_shape=jax.ShapeDtypeStruct(routes_t.shape, F32),
        compiler_params=params(),
        cost_estimate=cost(2 * routes_t.shape[1] * EXPERTS * 1024 * 8, 4 * MIB),
    )(h0, h1, router_t, routes_t)


def dispatch_kernel(code_ref, gates_ref, h0_ref, h1_ref, dy_ref, rows_ref, grads_ref, dy_rows_ref, gate_ref):
    count = rows_ref.shape[0]
    slot = lax.broadcasted_iota(jnp.int32, (count, SEQ), 0) + pl.program_id(0) * count
    rows = jnp.zeros(rows_ref.shape, F32)
    dy_rows = jnp.zeros(rows_ref.shape, F32)
    gate = jnp.zeros((count, 1), F32)
    for seq, ref in enumerate((h0_ref, h1_ref)):
        cols = slice(seq * SEQ, (seq + 1) * SEQ)
        hits = [slot == code_ref[i : i + 1, cols] for i in range(TOP)]
        take = jnp.where(hits[0] | hits[1], 1.0, 0.0).astype(BF16)
        weighted = jnp.where(hits[0], gates_ref[0:1, cols], jnp.where(hits[1], gates_ref[1:2, cols], 0.0))
        gate = gate + jnp.sum(weighted, axis=1, keepdims=True)
        rows = rows + mm(take, ref[...])
        dy_rows = dy_rows + mm(take, dy_ref[cols, :])
    rows_ref[...] = rows.astype(BF16)
    dy_rows_ref[...] = dy_rows.astype(BF16)
    grads_ref[...] = (dy_rows * gate).astype(BF16)
    gate_ref[...] = gate


def dispatch(code, gates, h0, h1, dy, slots):
    width = h0.shape[1]
    tile = slots // 4
    row_spec = pl.BlockSpec((tile, width), lambda i: (i, 0))
    whole = lambda shape: pl.BlockSpec(shape, lambda i: (0, 0))
    return pl.pallas_call(
        dispatch_kernel,
        grid=(4,),
        in_specs=[whole(code.shape), whole(gates.shape), whole(h0.shape), whole(h1.shape), whole(dy.shape)],
        out_specs=[row_spec, row_spec, row_spec, pl.BlockSpec((tile, 1), lambda i: (i, 0))],
        out_shape=[jax.ShapeDtypeStruct((slots, width), BF16)] * 3
        + [jax.ShapeDtypeStruct((slots, 1), F32)],
        compiler_params=params(),
        cost_estimate=cost(8 * slots * SEQ * width, 8 * MIB + 6 * slots * width),
    )(code, gates, h0, h1, dy)


def gelu_parts(x):
    inner = 0.7978845608028654 * (x + 0.044715 * (x * x * x))
    bend = jnp.tanh(inner)
    half = 0.5 * (1.0 + bend)
    slope = half + 0.5 * x * (1.0 - bend * bend) * (
        0.7978845608028654 * (1.0 + 3.0 * 0.044715 * (x * x))
    )
    return x * half, slope


def expert_kernel(
    rows_ref, grads_ref, gate_ref, up_ref, down_ref, ret_ref, back_ref,
    own_gate, own_up, own_down, far_gate, far_up, far_down,
    acc_gate, acc_up, acc_down, far_buf, sems,
):
    step = pl.program_id(0)
    rows, grads = rows_ref[...], grads_ref[...]
    half = gate_ref.shape[1]

    @pl.when(step == 0)
    def _():
        for acc in (acc_gate, acc_up, acc_down):
            acc[...] = jnp.zeros_like(acc)

    ret = jnp.zeros(rows.shape, F32)
    back = jnp.zeros(rows.shape, F32)
    for part in range(2):
        w_gate, w_up, w_down = gate_ref[part], up_ref[part], down_ref[part]
        gate_part = mm(rows, w_gate, NT)
        up_part = mm(rows, w_up, NT)
        grad_hidden = mm(grads, w_down, NT)
        bent, slope = gelu_parts(gate_part)
        hidden = (bent * up_part).astype(BF16)
        grad_gate = (grad_hidden * up_part * slope).astype(BF16)
        grad_up = (grad_hidden * bent).astype(BF16)
        ret = ret + mm(hidden, w_down)
        back = back + mm(grad_gate, w_gate) + mm(grad_up, w_up)
        acc_down[part] += mm(hidden, grads, TN)
        acc_gate[part] += mm(grad_gate, rows, TN)
        acc_up[part] += mm(grad_up, rows, TN)
    ret_ref[...] = ret.astype(BF16)
    back_ref[...] = back.astype(BF16)

    @pl.when(step == pl.num_programs(0) - 1)
    def _():
        copies = []
        triples = ((acc_gate, own_gate, far_gate), (acc_up, own_up, far_up), (acc_down, own_down, far_down))
        for number, (acc, own, far) in enumerate(triples):
            copies.append(pltpu.make_async_copy(acc.at[0], own, sems.at[2 * number]))
            copies[-1].start()
            far_buf[number] = acc[1].astype(BF16)
            copies.append(pltpu.make_async_copy(far_buf.at[number], far, sems.at[2 * number + 1]))
            copies[-1].start()
        for copy in copies:
            copy.wait()


def run_experts(rows, grads, w_gate, w_up, w_down):
    total, width = rows.shape
    units = w_gate.shape[1]
    tile = total // 5
    weight_spec = pl.BlockSpec((2, units, width), lambda i: (0, 0, 0), pipeline_mode=pl.Buffered(1))
    row_spec = pl.BlockSpec((tile, width), lambda i: (i, 0))
    anywhere = pl.BlockSpec(memory_space=pl.ANY)
    return pl.pallas_call(
        expert_kernel,
        grid=(5,),
        in_specs=[row_spec, row_spec, weight_spec, weight_spec, weight_spec],
        out_specs=[row_spec, row_spec] + [anywhere] * 6,
        out_shape=[jax.ShapeDtypeStruct((total, width), BF16)] * 2
        + [jax.ShapeDtypeStruct((units, width), F32)] * 3
        + [jax.ShapeDtypeStruct((units, width), BF16)] * 3,
        scratch_shapes=[pltpu.VMEM((2, units, width), F32)] * 3
        + [pltpu.VMEM((3, units, width), BF16), pltpu.SemaphoreType.DMA((6,))],
        compiler_params=params(60),
        cost_estimate=cost(36 * total * units * width, 8 * total * width + 30 * units * width),
    )(rows, grads, w_gate, w_up, w_down)


def pair_grads_kernel(code_ref, gates_ref, routes_ref, dy_rows_ref, ret_ref, gate_ref, logit_ref, scaled_ref):
    slots = ret_ref.shape[0]
    tokens = code_ref.shape[1]
    found = [jnp.zeros((1, tokens), F32) for _ in range(TOP)]
    tile = 320
    for start in range(0, slots, tile):
        span = slice(start, start + tile)
        ret = ret_ref[span, :].astype(F32)
        slot_grad = jnp.sum(dy_rows_ref[span, :].astype(F32) * ret, axis=1, keepdims=True)
        scaled_ref[span, :] = (ret * gate_ref[span, :]).astype(BF16)
        slot = lax.broadcasted_iota(jnp.int32, (tile, tokens), 0) + start
        for i in range(TOP):
            found[i] = found[i] + jnp.sum(
                jnp.where(slot == code_ref[i : i + 1, :], slot_grad, 0.0), axis=0, keepdims=True
            )
    mean = gates_ref[0:1] * found[0] + gates_ref[1:2] * found[1]
    expert = lax.broadcasted_iota(jnp.int32, (EXPERTS, tokens), 0)
    logit_ref[...] = sum(
        jnp.where(routes_ref[i : i + 1] == expert, gates_ref[i : i + 1] * (found[i] - mean), 0.0)
        for i in range(TOP)
    )


def pair_grads(code, gates, routes_t, dy_rows, ret, gate_rows):
    return pl.pallas_call(
        pair_grads_kernel,
        in_specs=[pl.BlockSpec(memory_space=pltpu.VMEM)] * 6,
        out_specs=[pl.BlockSpec(memory_space=pltpu.VMEM)] * 2,
        out_shape=[
            jax.ShapeDtypeStruct((EXPERTS, code.shape[1]), F32),
            jax.ShapeDtypeStruct(ret.shape, BF16),
        ],
        compiler_params=params(),
        cost_estimate=cost(ret.shape[0] * code.shape[1] * 16, 6 * ret.size),
    )(code, gates, routes_t, dy_rows, ret, gate_rows)


def spread_kernel(code_ref, rows_ref, *refs):
    out_ref = refs[-1]
    tile = out_ref.shape[0]
    slot = lax.broadcasted_iota(jnp.int32, (tile, rows_ref.shape[0]), 1)
    code = code_ref[...]
    place = jnp.where((slot == code[:, 0:1]) | (slot == code[:, 1:2]), 1.0, 0.0).astype(BF16)
    value = mm(place, rows_ref[...])
    if len(refs) == 3:
        logit, router = refs[0][...], refs[1][...]
        coarse = logit.astype(BF16)
        fine = (logit - coarse.astype(F32)).astype(BF16)
        value = value + mm(coarse, router, NT) + mm(fine, router, NT)
    out_ref[...] = value.astype(BF16)


def spread(code_cols, rows, logit=None, router=None):
    tokens, width = code_cols.shape[0], rows.shape[1]
    tile = 512
    specs = [
        pl.BlockSpec((tile, TOP), lambda i: (i, 0)),
        pl.BlockSpec(rows.shape, lambda i: (0, 0)),
    ]
    operands = [code_cols, rows]
    if logit is not None:
        specs += [
            pl.BlockSpec((tile, EXPERTS), lambda i: (i, 0)),
            pl.BlockSpec(router.shape, lambda i: (0, 0)),
        ]
        operands += [logit, router]
    return pl.pallas_call(
        spread_kernel,
        grid=(tokens // tile,),
        in_specs=specs,
        out_specs=pl.BlockSpec((tile, width), lambda i: (i, 0)),
        out_shape=jax.ShapeDtypeStruct((tokens, width), BF16),
        compiler_params=params(),
        cost_estimate=cost(2 * tokens * width * rows.shape[0], 2 * rows.size + 2 * tokens * width),
    )(*operands)


def assemble_kernel(in_ref, out_ref):
    out_ref[...] = in_ref[0].astype(out_ref.dtype)


def assemble(shards, kind):
    count, width, tile = shards.shape
    return pl.pallas_call(
        assemble_kernel,
        grid=(count,),
        in_specs=[pl.BlockSpec((1, width, tile), lambda i: (i, 0, 0))],
        out_specs=pl.BlockSpec((width, tile), lambda i: (0, i)),
        out_shape=jax.ShapeDtypeStruct((width, count * tile), kind),
        compiler_params=params(),
        cost_estimate=cost(0, 6 * shards.size),
    )(shards)


def on_device(
    layer_input, gain_one, attn_in, rel_bias, attn_out, gain_two, router,
    expert_gate, expert_up, expert_down, routes, piece_starts, grad_out,
):
    width, tokens = layer_input.shape
    ranks = lax.axis_size("tensor")
    groups = lax.axis_size("expert")
    seqs = piece_starts.shape[0]
    rank = lax.axis_index("tensor")
    pair_class, half_index = rank % 2, rank // 2
    half = CAP // 2
    share = SEQ // ranks
    across = [(r, r ^ 1) for r in range(ranks)]
    along = [(r, r ^ 2) for r in range(ranks)]

    def trade(weights):
        mine = lax.dynamic_index_in_dim(weights, pair_class, 0, keepdims=True)
        other = lax.dynamic_index_in_dim(weights, 1 - pair_class, 0, keepdims=True)
        return jnp.concatenate([mine, lax.ppermute(other, "tensor", across)], axis=0)

    w_gate, w_up, w_down = trade(expert_gate), trade(expert_up), trade(expert_down)

    gain_col = gain_one[:, None]
    w_in = attn_in.reshape(-1, width)
    qkv, scale_one = project(layer_input, gain_col, w_in)
    tiles = bias_tiles(rel_bias)
    position = jnp.arange(SEQ, dtype=jnp.int32)[None, None, :]
    starts = piece_starts[:, :, None]
    inside = (position >= starts) & (position < starts + PIECE)
    last = jnp.max(jnp.where(inside, starts + (PIECE - 1), -1), axis=1)
    limits = jnp.maximum(last, position[0])[:, None, :]

    routes_t = routes.T
    place = jnp.stack([pair_class, half_index]).astype(jnp.int32)
    code = local_codes(place, routes_t, half, groups)
    code_cols = code.T
    dy = grad_out.T

    def own_tokens(array, seq):
        return lax.dynamic_slice_in_dim(array, seq * SEQ + rank * share, share, 1)

    mixed, lse, resid, scale_two, full_h2 = [], [], [], [], []
    for seq in range(seqs):
        mixed_seq, lse_seq, sent = attend(qkv, tiles, limits, attn_out, seq)
        summed = lax.psum_scatter(sent, "tensor", scatter_dimension=0, tiled=True)
        resid_seq = own_tokens(layer_input, seq).T.astype(F32) + summed.astype(F32)
        scale = lax.rsqrt(jnp.sum(resid_seq * resid_seq, axis=1, keepdims=True) / width + EPS)
        normed = (resid_seq * scale * gain_two).astype(BF16)
        mixed.append(mixed_seq)
        lse.append(lse_seq)
        resid.append(resid_seq)
        scale_two.append(scale)
        full_h2.append(lax.all_gather(normed, "tensor", axis=0, tiled=True))

    gates = pair_gates(full_h2[0], full_h2[1], router.T, routes_t)
    slots = groups * half
    rows, row_grads, dy_rows, gate_rows = dispatch(code, gates, full_h2[0], full_h2[1], dy, slots)

    def to_owners(array):
        moved = lax.all_to_all(
            array.reshape(groups, half, width), "expert", split_axis=0, concat_axis=0, tiled=True
        )
        return moved.reshape(slots, width)

    got_rows = to_owners(rows)
    far_rows = lax.ppermute(got_rows, "tensor", along)
    got_grads = to_owners(row_grads)
    far_grads = lax.ppermute(got_grads, "tensor", along)
    (ret, back, own_gate, own_up, own_down, far_gate, far_up, far_down) = run_experts(
        jnp.concatenate([got_rows, far_rows]), jnp.concatenate([got_grads, far_grads]), w_gate, w_up, w_down
    )

    def from_owners(array):
        other = lax.ppermute(array[slots:], "tensor", along)
        return to_owners((array[:slots].astype(F32) + other.astype(F32)).astype(BF16))

    ret = from_owners(ret)
    back = from_owners(back)
    grad_logit, scaled = pair_grads(code, gates, routes_t, dy_rows, ret, gate_rows)
    partial_h2 = spread(code_cols, back, grad_logit.T, router)
    partial_y = spread(code_cols, scaled)
    grad_router = sum(
        mm(grad_logit[:, seq * SEQ : (seq + 1) * SEQ], full_h2[seq].astype(F32))
        for seq in range(seqs)
    )

    grad_gain_two = jnp.zeros((width,), F32)
    grad_resid, full_attn, y_shards = [], [], []
    for seq in range(seqs):
        span = slice(seq * SEQ, (seq + 1) * SEQ)
        grad_h2 = lax.psum_scatter(partial_h2[span], "tensor", scatter_dimension=0, tiled=True).astype(F32)
        own_dy = own_tokens(grad_out, seq).T.astype(F32)
        grad_gain_two = grad_gain_two + jnp.sum(grad_h2 * resid[seq] * scale_two[seq], axis=0)
        scaled_h2 = grad_h2 * gain_two
        inner = jnp.sum(scaled_h2 * resid[seq], axis=1, keepdims=True)
        grad = scale_two[seq] * scaled_h2 - resid[seq] * scale_two[seq] ** 3 * inner / width + own_dy
        grad_resid.append(grad)
        full_attn.append(lax.all_gather(grad.astype(BF16), "tensor", axis=0, tiled=True))
    for seq in range(seqs):
        span = slice(seq * SEQ, (seq + 1) * SEQ)
        y_part = lax.psum_scatter(partial_y[span], "tensor", scatter_dimension=0, tiled=True)
        y_shards.append((resid[seq] + y_part.astype(F32)).astype(BF16).T)
    y_all = [lax.all_gather(shard[None], "tensor", axis=0, tiled=True) for shard in y_shards]
    layer_output = assemble(jnp.concatenate(y_all), BF16)

    grad_attn_out = sum(mm(mixed[seq], full_attn[seq]) for seq in range(seqs))
    w_in_t = w_in.T
    grad_in, near, far, shards = [], [], [], []
    grad_gain_one = jnp.zeros((width,), F32)
    for seq in range(seqs):
        dq, dk, dv, near_seq, far_seq = attend_back(
            qkv, tiles, limits, attn_out, full_attn[seq], lse[seq], seq
        )
        near.append(near_seq)
        far.append(far_seq)
        grads = [g.reshape(-1, SEQ) for g in (dq, dk, dv)]
        update, sent = project_back(layer_input, gain_col, scale_one, w_in_t, grads, seq, ranks)
        grad_in.append(update)
        grad_h1 = lax.psum_scatter(sent, "tensor", scatter_dimension=0, tiled=True)[0].astype(F32)
        own_x = own_tokens(layer_input, seq).astype(F32)
        own_scale = own_tokens(scale_one, seq)
        grad_gain_one = grad_gain_one + jnp.sum(grad_h1 * own_x * own_scale, axis=1)
        scaled_h1 = grad_h1 * gain_col
        inner = jnp.sum(scaled_h1 * own_x, axis=0, keepdims=True)
        grad = own_scale * scaled_h1 - own_x * own_scale**3 * inner / width + grad_resid[seq].T
        shards.append(lax.all_gather(grad.astype(BF16)[None], "tensor", axis=0, tiled=True))
    grad_input = assemble(jnp.concatenate(shards), F32)
    folded = bias_fold(jnp.stack(near), jnp.stack(far))
    grad_rel_bias = folded[:, :, 0].T

    def give(own, other):
        got = lax.ppermute(other, "tensor", across).astype(F32)
        first = jnp.where(pair_class == 0, own, got)
        second = jnp.where(pair_class == 0, got, own)
        return jnp.stack([first, second])

    small = lax.psum(
        jnp.concatenate([grad_gain_one[None], grad_gain_two[None], grad_router]), ("expert", "tensor")
    )
    over_experts = (
        lax.psum((grad_in[0] + grad_in[1]).astype(BF16), "expert").astype(F32),
        lax.psum(grad_rel_bias, "expert"),
        lax.psum(grad_attn_out.astype(BF16), "expert").astype(F32),
    )
    return (
        layer_output,
        grad_input,
        small[0],
        over_experts[0].reshape(attn_in.shape),
        over_experts[1],
        over_experts[2],
        small[1],
        small[2:].T,
        give(own_gate, far_gate),
        give(own_up, far_up),
        give(own_down, far_down),
    )


def allowed_pairs(seq_starts):
    position = jnp.arange(SEQ, dtype=jnp.int32)
    inside = (position[:, None] >= seq_starts[None, :]) & (
        position[:, None] < seq_starts[None, :] + PIECE
    )
    numbers = jnp.arange(seq_starts.shape[0], dtype=jnp.int32) + 1
    piece_label = jnp.sum(inside.astype(jnp.int32) * numbers[None, :], axis=1)
    causal = position[None, :] <= position[:, None]
    shared = (piece_label[:, None] == piece_label[None, :]) & (piece_label[:, None] > 0)
    return causal | shared


def slot_table(routes):
    flat_routes = routes.reshape(-1)
    onehot = (flat_routes[:, None] == jnp.arange(EXPERTS, dtype=jnp.int32)[None, :]).astype(
        jnp.int32
    )
    blocks = onehot.reshape(-1, 128, EXPERTS).astype(F32)
    earlier = jnp.tril(jnp.ones((128, 128), F32), -1)
    inside = jnp.einsum("ij,bje->bie", earlier, blocks)
    count = blocks.shape[0]
    carried = jnp.einsum("ab,be->ae", jnp.tril(jnp.ones((count, count), F32), -1), jnp.sum(blocks, axis=1), precision=HIGH)
    before = (inside + carried[:, None, :]).astype(jnp.int32).reshape(onehot.shape)
    slot_number = jnp.sum(before * onehot, axis=1)
    kept_pairs = slot_number < CAP
    slot_index = jnp.where(kept_pairs, flat_routes * CAP + slot_number, EXPERTS * CAP)
    return (slot_index.reshape(routes.shape), kept_pairs.reshape(routes.shape))


def bucket_onehot():
    offsets = jnp.arange(2 * SEQ - 1, dtype=jnp.int32) - (SEQ - 1)
    return (bucket_of(offsets)[:, None] == jnp.arange(BUCKETS, dtype=jnp.int32)[None, :]).astype(
        jnp.float32
    )


def expand_line(line):
    head_count = line.shape[0]
    padded = jnp.concatenate([line, jnp.zeros((head_count, 1), line.dtype)], axis=1)
    tiled = jnp.tile(padded, (1, SEQ))[:, : SEQ * (2 * SEQ - 1)].reshape(
        head_count, SEQ, 2 * SEQ - 1
    )
    return tiled[:, :, SEQ - 1 :]


def fold_line(full_grid):
    head_count = full_grid.shape[0]
    padded = jnp.pad(full_grid, ((0, 0), (0, 0), (SEQ - 1, 0))).reshape(
        head_count, SEQ * (2 * SEQ - 1)
    )
    padded = jnp.pad(padded, ((0, 0), (0, SEQ))).reshape(head_count, SEQ, 2 * SEQ)
    return jnp.sum(padded, axis=1)[:, : 2 * SEQ - 1]


def reduce_heads(tensor_value):
    return lax.psum(tensor_value, "tensor")


def spread_slots(tensor_value):
    return lax.all_gather(tensor_value, "tensor", axis=2, tiled=True)


def owner_exchange(tensor_value):
    return lax.all_to_all(tensor_value, "expert", split_axis=0, concat_axis=0, tiled=True)


def expert_sums(tensor_value):
    return lax.psum_scatter(tensor_value, "tensor", scatter_dimension=2, tiled=True)


def norm_forward(resid, gain, model_width):
    scale = lax.rsqrt(jnp.sum(resid * resid, axis=1) / model_width + EPS)[:, None]
    return (scale, (resid * scale * gain).astype(jnp.bfloat16))


def norm_backward(resid, scale, gain, grad_normed, model_width):
    grad_gain = jnp.sum(grad_normed * resid * scale, axis=0)
    scaled = grad_normed * gain
    inner = jnp.sum(scaled * resid, axis=1)[:, None]
    return (grad_gain, scale * scaled - resid * scale**3 * inner / model_width)


def attend_scores(bias_full, queries, key_rows, seq_starts):
    scores = (
        jnp.einsum("qhe,khe->hqk", queries, key_rows, preferred_element_type=jnp.float32) * 0.125
        + bias_full
    )
    return jnp.where(allowed_pairs(seq_starts)[None], scores, NEG)


def attend_forward(bias_full, inputs):
    queries, key_rows, value_rows, seq_starts = inputs
    scores = attend_scores(bias_full, queries, key_rows, seq_starts)
    row_max = jnp.max(scores, axis=2, keepdims=True)
    exponent = jnp.exp(scores - row_max)
    row_sum_exp = jnp.sum(exponent, axis=2, keepdims=True)
    weights = (exponent / row_sum_exp).astype(jnp.bfloat16)
    mixed_heads = jnp.einsum(
        "hqk,khe->qhe", weights, value_rows, preferred_element_type=jnp.float32
    )
    return (mixed_heads.astype(jnp.bfloat16), (row_max + jnp.log(row_sum_exp))[:, :, 0])


def attend_backward(bias_full, running, inputs):
    queries, key_rows, value_rows, grad_heads, seq_starts, log_total = inputs
    scores = attend_scores(bias_full, queries, key_rows, seq_starts)
    probabilities = jnp.exp(scores - log_total[:, :, None])
    grad_probs = jnp.einsum(
        "qhe,khe->hqk", grad_heads, value_rows, preferred_element_type=jnp.float32
    )
    inner = jnp.sum(probabilities * grad_probs, axis=2, keepdims=True)
    grad_scores = (probabilities * (grad_probs - inner)).astype(jnp.bfloat16)
    grad_values = jnp.einsum(
        "hqk,qhe->khe",
        probabilities.astype(jnp.bfloat16),
        grad_heads,
        preferred_element_type=jnp.float32,
    )
    grad_queries = (
        jnp.einsum("hqk,khe->qhe", grad_scores, key_rows, preferred_element_type=jnp.float32)
        * 0.125
    )
    grad_keys = (
        jnp.einsum("hqk,qhe->khe", grad_scores, queries, preferred_element_type=jnp.float32) * 0.125
    )
    return (
        running + grad_scores.astype(jnp.float32),
        jnp.stack([grad_queries, grad_keys, grad_values]),
    )


def gelu_product(left, right):
    return jax.nn.gelu(left, approximate=True) * right


def expert_forward(received, weight_gate, weight_up, weight_down):
    gate_part = jnp.einsum(
        "secd,efd->secf", received, weight_gate, preferred_element_type=jnp.float32
    )
    up_part = jnp.einsum("secd,efd->secf", received, weight_up, preferred_element_type=jnp.float32)
    hidden = gelu_product(gate_part, up_part).astype(jnp.bfloat16)
    partial_out = jnp.einsum(
        "secf,efd->secd", hidden, weight_down, preferred_element_type=jnp.float32
    )
    return (gate_part, up_part, hidden, partial_out)


def expert_backward(
    received, gate_part, up_part, hidden, grad_rows_out, weight_gate, weight_up, weight_down
):
    grad_hidden = jnp.einsum(
        "secd,efd->secf", grad_rows_out, weight_down, preferred_element_type=jnp.float32
    )
    product_value, pullback = jax.vjp(gelu_product, gate_part, up_part)
    grad_gate_part, grad_up_part = pullback(grad_hidden)
    grad_gate_part = grad_gate_part.astype(jnp.bfloat16)
    grad_up_part = grad_up_part.astype(jnp.bfloat16)
    grad_down = jnp.einsum(
        "secf,secd->efd", hidden, grad_rows_out, preferred_element_type=jnp.float32
    )
    grad_gate_w = jnp.einsum(
        "secf,secd->efd", grad_gate_part, received, preferred_element_type=jnp.float32
    )
    grad_up_w = jnp.einsum(
        "secf,secd->efd", grad_up_part, received, preferred_element_type=jnp.float32
    )
    grad_rows_in = jnp.einsum(
        "secf,efd->secd", grad_gate_part, weight_gate, preferred_element_type=jnp.float32
    )
    grad_rows_in = grad_rows_in + jnp.einsum(
        "secf,efd->secd", grad_up_part, weight_up, preferred_element_type=jnp.float32
    )
    return (grad_gate_w, grad_up_w, grad_down, grad_rows_in)


def on_device_general(
    layer_input,
    gain_one,
    attn_in,
    rel_bias,
    attn_out,
    gain_two,
    router,
    expert_gate,
    expert_up,
    expert_down,
    routes,
    piece_starts,
    grad_out,
):
    tok_count = layer_input.shape[1]
    model_width = layer_input.shape[0]
    heads_here = rel_bias.shape[1]
    head_width = attn_in.shape[1] // heads_here
    seqs_here = piece_starts.shape[0]
    local_experts = expert_gate.shape[0]
    part_rows = CAP // lax.axis_size("tensor")
    share_start = lax.axis_index("tensor") * part_rows
    tokens = layer_input.T.astype(jnp.float32)
    scale_one, normed = norm_forward(tokens, gain_one, model_width)
    project = jnp.einsum("td,chd->cth", normed, attn_in, preferred_element_type=jnp.float32).astype(
        jnp.bfloat16
    )
    by_seq = project.reshape(3, seqs_here, SEQ, heads_here, head_width)
    onehot_line = bucket_onehot()
    bias_full = expand_line(jnp.dot(onehot_line, rel_bias, precision=HIGH).T)
    mixed_heads, log_total = lax.map(
        partial(attend_forward, bias_full), (by_seq[0], by_seq[1], by_seq[2], piece_starts)
    )
    mixed_heads = mixed_heads.reshape(tok_count, heads_here * head_width)
    resid = tokens + reduce_heads(
        jnp.dot(mixed_heads, attn_out, preferred_element_type=jnp.float32)
    )
    scale_two, normed_two = norm_forward(resid, gain_two, model_width)
    logits = jnp.dot(normed_two, router, preferred_element_type=jnp.float32)
    chosen = (routes[:, :, None] == jnp.arange(EXPERTS, dtype=jnp.int32)[None, None, :]).astype(
        jnp.float32
    )
    picked = jnp.sum(chosen * logits[:, None, :], axis=2)
    gate_weights = jax.nn.softmax(picked, axis=1)
    slot_index, kept_pairs = slot_table(routes)
    keep_float = kept_pairs.astype(jnp.float32)
    mix_weight = gate_weights * keep_float
    safe_index = jnp.minimum(slot_index, EXPERTS * CAP - 1)
    token_rows = jnp.repeat(normed_two, TOP, axis=0)
    buffer = (
        jnp.zeros((EXPERTS * CAP + 1, model_width), jnp.bfloat16)
        .at[slot_index.reshape(-1)]
        .set(token_rows)
    )
    buffer = buffer[: EXPERTS * CAP].reshape(-1, local_experts, CAP, model_width)
    received = lax.all_to_all(buffer, "expert", split_axis=0, concat_axis=0, tiled=True)
    gate_part, up_part, hidden, partial_out = expert_forward(
        received, expert_gate, expert_up, expert_down
    )
    returned = spread_slots(owner_exchange(expert_sums(partial_out).astype(jnp.bfloat16)))
    flat_ret = returned.reshape(EXPERTS * CAP, model_width)
    fetched = flat_ret[safe_index].astype(jnp.float32)
    output = resid + jnp.sum(mix_weight[:, :, None] * fetched, axis=1)
    grad_y = grad_out.T.astype(jnp.float32)
    grad_gates = jnp.sum(grad_y[:, None, :] * fetched, axis=2) * keep_float
    grad_picked = gate_weights * (
        grad_gates - jnp.sum(gate_weights * grad_gates, axis=1, keepdims=True)
    )
    grad_logits = jnp.sum(chosen * grad_picked[:, :, None], axis=1)
    grad_router = jnp.dot(normed_two.astype(jnp.float32).T, grad_logits, precision=HIGH)
    grad_normed_two = jnp.dot(grad_logits, router.astype(jnp.float32).T, precision=HIGH)
    slot_grads = (mix_weight[:, :, None] * grad_y[:, None, :]).astype(jnp.bfloat16)
    grad_ret = (
        jnp.zeros((EXPERTS * CAP + 1, model_width), jnp.bfloat16)
        .at[slot_index.reshape(-1)]
        .set(slot_grads.reshape(-1, model_width))
    )
    grad_ret = grad_ret[: EXPERTS * CAP].reshape(-1, local_experts, CAP, model_width)
    grad_share = lax.dynamic_slice_in_dim(grad_ret, share_start, part_rows, 2)
    grad_rows_out = spread_slots(owner_exchange(grad_share))
    grad_expert_gate, grad_expert_up, grad_expert_down, grad_rows_in = expert_backward(
        received, gate_part, up_part, hidden, grad_rows_out, expert_gate, expert_up, expert_down
    )
    grad_back = spread_slots(owner_exchange(expert_sums(grad_rows_in).astype(jnp.bfloat16)))
    flat_back = grad_back.reshape(EXPERTS * CAP, model_width).astype(jnp.float32)
    grad_normed_two = grad_normed_two + jnp.sum(
        flat_back[safe_index] * keep_float[:, :, None], axis=1
    )
    grad_gain_two, grad_resid = norm_backward(
        resid, scale_two, gain_two, grad_normed_two, model_width
    )
    grad_resid = grad_resid + grad_y
    grad_attn = grad_resid.astype(jnp.bfloat16)
    grad_attn_out = jnp.einsum(
        "th,td->hd", mixed_heads, grad_attn, preferred_element_type=jnp.float32
    )
    grad_mixed = jnp.einsum(
        "td,hd->th", grad_attn, attn_out, preferred_element_type=jnp.float32
    ).astype(jnp.bfloat16)
    grad_by_seq = grad_mixed.reshape(seqs_here, SEQ, heads_here, head_width)
    bias_grad_full, grad_project = lax.scan(
        partial(attend_backward, bias_full),
        jnp.zeros_like(bias_full),
        (by_seq[0], by_seq[1], by_seq[2], grad_by_seq, piece_starts, log_total),
    )
    grad_project = (
        jnp.moveaxis(grad_project, 1, 0)
        .reshape(3, tok_count, heads_here * head_width)
        .astype(jnp.bfloat16)
    )
    grad_attn_in = jnp.einsum(
        "cth,td->chd", grad_project, normed, preferred_element_type=jnp.float32
    )
    grad_normed = reduce_heads(
        jnp.einsum("cth,chd->td", grad_project, attn_in, preferred_element_type=jnp.float32)
    )
    grad_gain_one, grad_tokens = norm_backward(
        tokens, scale_one, gain_one, grad_normed, model_width
    )
    grad_tokens = grad_tokens + grad_resid
    grad_rel_bias = jnp.dot(onehot_line.T, fold_line(bias_grad_full).T, precision=HIGH)
    shared = (
        lax.psum(grad_gain_one.astype(jnp.bfloat16), "expert").astype(jnp.float32),
        lax.psum(grad_attn_in.astype(jnp.bfloat16), "expert").astype(jnp.float32),
        lax.psum(grad_rel_bias.astype(jnp.bfloat16), "expert").astype(jnp.float32),
        lax.psum(grad_attn_out.astype(jnp.bfloat16), "expert").astype(jnp.float32),
        lax.psum(grad_gain_two.astype(jnp.bfloat16), "expert").astype(jnp.float32),
        lax.psum(grad_router.astype(jnp.bfloat16), "expert").astype(jnp.float32),
    )
    return (
        output.astype(jnp.bfloat16).T,
        grad_tokens.T,
        shared[0],
        shared[1],
        shared[2],
        shared[3],
        shared[4],
        shared[5],
        grad_expert_gate,
        grad_expert_up,
        grad_expert_down,
    )


def solution(mesh):
    placed = (
        P(None, "expert"),
        P(),
        P(None, "tensor", None),
        P(None, "tensor"),
        P("tensor", None),
        P(),
        P(),
        P("expert", "tensor", None),
        P("expert", "tensor", None),
        P("expert", "tensor", None),
        P("expert", None),
        P("expert", None),
        P(None, "expert"),
    )
    paired = mesh.shape["tensor"] == 4 and mesh.shape["expert"] * 2 == EXPERTS
    return jax.shard_map(
        on_device if paired else on_device_general,
        mesh=mesh,
        in_specs=placed,
        out_specs=(
            P(None, "expert"),
            P(None, "expert"),
            P(),
            P(None, "tensor", None),
            P(None, "tensor"),
            P("tensor", None),
            P(),
            P(),
            P("expert", "tensor", None),
            P("expert", "tensor", None),
            P("expert", "tensor", None),
        ),
        check_vma=False,
    )
```

```python
from functools import partial

import jax
import jax.numpy as jnp
from jax import lax
from jax.experimental import pallas as pl
from jax.experimental.pallas import tpu as pltpu
from jax.sharding import PartitionSpec as P

EXPERTS = 16
BUCKETS = 32
TOP = 2
PIECE = 256
SEQ = 1024
CAP = 320
BLK = 256


EPS = 1e-06
NEG = -1e30
THRESHOLDS = (12, 16, 23, 32, 46, 64, 91)
HIGH = lax.Precision.HIGHEST
F32 = jnp.float32
BF16 = jnp.bfloat16
NN = (((1,), (0,)), ((), ()))
NT = (((1,), (1,)), ((), ()))
TN = (((0,), (0,)), ((), ()))
MIB = 1 << 20


def mm(left, right, dims=NN):
    return lax.dot_general(left, right, dims, preferred_element_type=F32)


def params(limit=56):
    return pltpu.CompilerParams(vmem_limit_bytes=limit * MIB)


def cost(flops, bytes_accessed, transcendentals=0):
    return pl.CostEstimate(
        flops=int(flops), bytes_accessed=int(bytes_accessed), transcendentals=int(transcendentals)
    )


def bucket_of(offset):
    magnitude = jnp.abs(offset)
    beyond = sum(((magnitude >= threshold).astype(jnp.int32) for threshold in THRESHOLDS))
    lower_part = jnp.where(magnitude < 8, magnitude, 8 + beyond)
    return lower_part + 16 * (offset > 0).astype(jnp.int32)


def project_kernel(x_ref, gain_ref, w_ref, out_ref, scale_ref):
    x = x_ref[...].astype(F32)
    scale = lax.rsqrt(jnp.sum(x * x, axis=0, keepdims=True) / x.shape[0] + EPS)
    normed = (x * scale * gain_ref[...]).astype(BF16)
    out_ref[...] = mm(w_ref[...], normed).astype(BF16)
    scale_ref[...] = scale


def project(x, gain, weights):
    width, tokens = x.shape
    rows = weights.shape[0]
    tile = 512
    return pl.pallas_call(
        project_kernel,
        grid=(tokens // tile,),
        in_specs=[
            pl.BlockSpec((width, tile), lambda i: (0, i)),
            pl.BlockSpec((width, 1), lambda i: (0, 0)),
            pl.BlockSpec((rows, width), lambda i: (0, 0)),
        ],
        out_specs=[
            pl.BlockSpec((rows, tile), lambda i: (0, i)),
            pl.BlockSpec((1, tile), lambda i: (0, i)),
        ],
        out_shape=[
            jax.ShapeDtypeStruct((rows, tokens), BF16),
            jax.ShapeDtypeStruct((1, tokens), F32),
        ],
        compiler_params=params(),
        cost_estimate=cost(2 * width * tokens * rows, 2 * width * tokens * 2),
    )(x, gain, weights)


def bias_tiles_kernel(table_ref, tiles_ref):
    key_at = lax.broadcasted_iota(jnp.int32, (BLK, BLK), 0)
    query_at = lax.broadcasted_iota(jnp.int32, (BLK, BLK), 1)
    for number, shift in enumerate((-1, 0, 1)):
        offset = key_at - query_at + shift * BLK
        bucket = bucket_of(offset)
        low, high = {-1: (0, 16), 0: (0, 32), 1: (16, 32)}[shift]
        for head in range(tiles_ref.shape[0]):
            far = table_ref[15, head]
            value = jnp.zeros((BLK, BLK), F32)
            for index in range(low, high):
                value = jnp.where(bucket == index, table_ref[index, head] - far, value)
            tiles_ref[head, number] = value


def bias_tiles(table):
    heads = table.shape[1]
    return pl.pallas_call(
        bias_tiles_kernel,
        in_specs=[pl.BlockSpec(memory_space=pltpu.SMEM)],
        out_specs=pl.BlockSpec(memory_space=pltpu.VMEM),
        out_shape=jax.ShapeDtypeStruct((heads, 3, BLK, BLK), F32),
        compiler_params=params(),
        cost_estimate=cost(heads * 3 * BLK * BLK * 60, heads * 3 * BLK * BLK * 4),
    )(table)


def bias_fold_kernel(near_ref, far_ref, out_ref):
    heads = near_ref.shape[1]
    key_at = lax.broadcasted_iota(jnp.int32, (BLK, BLK), 0)
    query_at = lax.broadcasted_iota(jnp.int32, (BLK, BLK), 1)
    totals = [[jnp.zeros((8, BLK), F32) for _ in range(BUCKETS)] for _ in range(heads)]
    for number, shift in enumerate((-1, 0, 1)):
        bucket = bucket_of(key_at - query_at + shift * BLK)
        low, high = {-1: (0, 16), 0: (0, 32), 1: (16, 32)}[shift]
        for head in range(heads):
            grads = near_ref[0, head, number] + near_ref[1, head, number]
            for index in range(low, high):
                kept = jnp.where(bucket == index, grads, 0.0)
                totals[head][index] = totals[head][index] + jnp.sum(
                    kept.reshape(BLK // 8, 8, BLK), axis=0
                )
    for head in range(heads):
        totals[head][15] = totals[head][15] + far_ref[0, head] + far_ref[1, head]
        for index in range(BUCKETS):
            line = jnp.sum(totals[head][index], axis=0, keepdims=True)
            out_ref[head, index : index + 1, :] = jnp.broadcast_to(
                jnp.sum(line, axis=1, keepdims=True), (1, 128)
            )


def bias_fold(near, far):
    heads = near.shape[1]
    return pl.pallas_call(
        bias_fold_kernel,
        in_specs=[pl.BlockSpec(memory_space=pltpu.VMEM)] * 2,
        out_specs=pl.BlockSpec(memory_space=pltpu.VMEM),
        out_shape=jax.ShapeDtypeStruct((heads, BUCKETS, 128), F32),
        compiler_params=params(),
        cost_estimate=cost(heads * 3 * BLK * BLK * 60, heads * 6 * BLK * BLK * 4),
    )(near, far)


def key_count(query_block):
    return 2 * BLK if query_block < 2 else 4 * BLK


def block_scores(keys, queries, tiles_ref, limit, block):
    count = key_count(block)
    parts = []
    whole = mm(keys[:, :count], queries, TN)
    for key_block in range(count // BLK):
        part = whole[key_block * BLK : (key_block + 1) * BLK]
        shift = key_block - block
        if -1 <= shift <= 1:
            part = part + tiles_ref[0, shift + 1]
        if shift >= 0:
            key_at = lax.broadcasted_iota(jnp.int32, (BLK, BLK), 0) + key_block * BLK
            part = jnp.where(key_at <= limit, part, NEG)
        parts.append(part)
    return jnp.concatenate(parts, axis=0)


def attend_kernel(q_ref, k_ref, v_ref, tiles_ref, limit_ref, w_ref, out_ref, lse_ref, sent_ref, held):
    head = pl.program_id(0)
    width = q_ref.shape[0]
    queries = q_ref[...] * BF16(0.125)
    keys, values = k_ref[...], v_ref[...]
    for block in range(SEQ // BLK):
        cols = slice(block * BLK, (block + 1) * BLK)
        scores = block_scores(keys, queries[:, cols], tiles_ref, limit_ref[0, :, cols], block)
        top = jnp.max(scores, axis=0, keepdims=True)
        exponent = jnp.exp(scores - top)
        total = jnp.sum(exponent, axis=0, keepdims=True)
        mixed = mm(values[:, : key_count(block)], exponent.astype(BF16)) / total
        mixed = mixed.astype(BF16)
        out_ref[:, cols] = mixed
        held[pl.ds(pl.multiple_of(head * width, width), width), cols] = mixed
        lse_ref[0, :, cols] = top + jnp.log(total)

    @pl.when(head == pl.num_programs(0) - 1)
    def _():
        sent_ref[...] = mm(held[...], w_ref[...], TN).astype(BF16)


def attend(qkv, tiles, limits, attn_out, seq):
    heads = tiles.shape[0]
    width = qkv.shape[0] // (3 * heads)
    model_width = attn_out.shape[1]
    return pl.pallas_call(
        attend_kernel,
        grid=(heads,),
        in_specs=[
            pl.BlockSpec((width, SEQ), lambda h: (h, seq)),
            pl.BlockSpec((width, SEQ), lambda h: (heads + h, seq)),
            pl.BlockSpec((width, SEQ), lambda h: (2 * heads + h, seq)),
            pl.BlockSpec((1, 3, BLK, BLK), lambda h: (h, 0, 0, 0)),
            pl.BlockSpec((1, 1, SEQ), lambda h: (seq, 0, 0)),
            pl.BlockSpec((heads * width, model_width), lambda h: (0, 0)),
        ],
        out_specs=[
            pl.BlockSpec((width, SEQ), lambda h: (h, 0)),
            pl.BlockSpec((1, 1, SEQ), lambda h: (h, 0, 0)),
            pl.BlockSpec((SEQ, model_width), lambda h: (0, 0)),
        ],
        out_shape=[
            jax.ShapeDtypeStruct((heads * width, SEQ), BF16),
            jax.ShapeDtypeStruct((heads, 1, SEQ), F32),
            jax.ShapeDtypeStruct((SEQ, model_width), BF16),
        ],
        scratch_shapes=[pltpu.VMEM((heads * width, SEQ), BF16)],
        compiler_params=params(),
        cost_estimate=cost(heads * SEQ * SEQ * 512, heads * SEQ * 2048, heads * SEQ * SEQ),
    )(qkv, qkv, qkv, tiles, limits, attn_out)


def attend_back_kernel(
    q_ref, k_ref, v_ref, tiles_ref, limit_ref, w_ref, grad_ref, lse_ref,
    dq_ref, dk_ref, dv_ref, near_ref, far_ref, held,
):
    head = pl.program_id(0)
    width = q_ref.shape[0]

    @pl.when(head == 0)
    def _():
        held[...] = mm(w_ref[...], grad_ref[...], NT).astype(BF16)

    queries = q_ref[...] * BF16(0.125)
    keys, values = k_ref[...], v_ref[...]
    grads = held[pl.ds(pl.multiple_of(head * width, width), width), :]
    near_ref[...] = jnp.zeros_like(near_ref)
    far = jnp.zeros((8, BLK), F32)
    grad_keys = jnp.zeros((width, SEQ), F32)
    grad_values = jnp.zeros((width, SEQ), F32)
    for block in range(SEQ // BLK):
        count = key_count(block)
        cols = slice(block * BLK, (block + 1) * BLK)
        scores = block_scores(keys, queries[:, cols], tiles_ref, limit_ref[0, :, cols], block)
        probs = jnp.exp(scores - lse_ref[0, :, cols])
        grad_probs = mm(values[:, :count], grads[:, cols], TN)
        inner = jnp.sum(probs * grad_probs, axis=0, keepdims=True)
        grad_scores = probs * (grad_probs - inner)
        for key_block in range(count // BLK):
            part = grad_scores[key_block * BLK : (key_block + 1) * BLK]
            shift = key_block - block
            if -1 <= shift <= 1:
                near_ref[0, shift + 1] += part
            elif shift < -1:
                far = far + jnp.sum(part.reshape(BLK // 8, 8, BLK), axis=0)
        rounded = grad_scores.astype(BF16)
        add_values = mm(grads[:, cols], probs.astype(BF16), NT)
        add_keys = mm(queries[:, cols], rounded, NT)
        if count == SEQ:
            grad_values = grad_values + add_values
            grad_keys = grad_keys + add_keys
        else:
            filler = jnp.zeros((width, SEQ - count), F32)
            grad_values = grad_values + jnp.concatenate([add_values, filler], axis=1)
            grad_keys = grad_keys + jnp.concatenate([add_keys, filler], axis=1)
        dq_ref[0, :, cols] = (mm(keys[:, :count], rounded) * 0.125).astype(BF16)
    dk_ref[0] = grad_keys.astype(BF16)
    dv_ref[0] = grad_values.astype(BF16)
    far_ref[0] = far


def attend_back(qkv, tiles, limits, attn_out, grad_attn, lse, seq):
    heads = tiles.shape[0]
    width = qkv.shape[0] // (3 * heads)
    model_width = attn_out.shape[1]
    grad_spec = pl.BlockSpec((1, width, SEQ), lambda h: (h, 0, 0))
    return pl.pallas_call(
        attend_back_kernel,
        grid=(heads,),
        in_specs=[
            pl.BlockSpec((width, SEQ), lambda h: (h, seq)),
            pl.BlockSpec((width, SEQ), lambda h: (heads + h, seq)),
            pl.BlockSpec((width, SEQ), lambda h: (2 * heads + h, seq)),
            pl.BlockSpec((1, 3, BLK, BLK), lambda h: (h, 0, 0, 0)),
            pl.BlockSpec((1, 1, SEQ), lambda h: (seq, 0, 0)),
            pl.BlockSpec((heads * width, model_width), lambda h: (0, 0)),
            pl.BlockSpec((SEQ, model_width), lambda h: (0, 0)),
            pl.BlockSpec((1, 1, SEQ), lambda h: (h, 0, 0)),
        ],
        out_specs=[
            grad_spec,
            grad_spec,
            grad_spec,
            pl.BlockSpec((1, 3, BLK, BLK), lambda h: (h, 0, 0, 0)),
            pl.BlockSpec((1, 8, BLK), lambda h: (h, 0, 0)),
        ],
        out_shape=[jax.ShapeDtypeStruct((heads, width, SEQ), BF16)] * 3
        + [
            jax.ShapeDtypeStruct((heads, 3, BLK, BLK), F32),
            jax.ShapeDtypeStruct((heads, 8, BLK), F32),
        ],
        scratch_shapes=[pltpu.VMEM((heads * width, SEQ), BF16)],
        compiler_params=params(),
        cost_estimate=cost(heads * SEQ * SEQ * 1280, heads * SEQ * 4096, heads * SEQ * SEQ),
    )(qkv, qkv, qkv, tiles, limits, attn_out, grad_attn, lse)


def project_back_kernel(
    x_ref, gain_ref, scale_ref, w_ref, *refs
):
    grad_refs, (weight_ref, out_ref) = refs[:3], refs[3:]
    grads = jnp.concatenate([ref[...] for ref in grad_refs], axis=0)
    normed = (x_ref[...].astype(F32) * scale_ref[...] * gain_ref[...]).astype(BF16)
    update = mm(grads, normed, NT)

    @pl.when(pl.program_id(0) == 0)
    def _():
        weight_ref[...] = update

    @pl.when(pl.program_id(0) > 0)
    def _():
        weight_ref[...] += update

    out_ref[0] = mm(w_ref[...], grads).astype(BF16)


def project_back(x, gain, scale, weights_t, grads, seq, ranks):
    width = x.shape[0]
    rows = weights_t.shape[1]
    tile = SEQ // ranks
    return pl.pallas_call(
        project_back_kernel,
        grid=(ranks,),
        in_specs=[
            pl.BlockSpec((width, tile), lambda i: (0, seq * ranks + i)),
            pl.BlockSpec((width, 1), lambda i: (0, 0)),
            pl.BlockSpec((1, tile), lambda i: (0, seq * ranks + i)),
            pl.BlockSpec((width, rows), lambda i: (0, 0)),
        ]
        + [pl.BlockSpec((rows // 3, tile), lambda i: (0, i))] * 3,
        out_specs=[
            pl.BlockSpec((rows, width), lambda i: (0, 0)),
            pl.BlockSpec((1, width, tile), lambda i: (i, 0, 0)),
        ],
        out_shape=[
            jax.ShapeDtypeStruct((rows, width), F32),
            jax.ShapeDtypeStruct((ranks, width, tile), BF16),
        ],
        compiler_params=params(),
        cost_estimate=cost(4 * width * SEQ * rows, 6 * width * SEQ),
    )(x, gain, scale, weights_t, *grads)


def code_kernel(place_ref, routes_ref, code_ref, half, groups):
    pair_class, half_index = place_ref[0], place_ref[1]
    tokens = routes_ref.shape[1]
    expert = lax.broadcasted_iota(jnp.int32, (EXPERTS, BLK), 0)
    earlier = (
        lax.broadcasted_iota(jnp.int32, (BLK, BLK), 0) < lax.broadcasted_iota(jnp.int32, (BLK, BLK), 1)
    ).astype(F32).astype(BF16)
    carry = jnp.zeros((EXPERTS, 1), F32)
    for block in range(tokens // BLK):
        cols = slice(block * BLK, (block + 1) * BLK)
        routes = routes_ref[:, cols]
        hits = [(routes[i : i + 1] == expert) for i in range(TOP)]
        chosen = sum(hit.astype(F32) for hit in hits)
        before = mm(chosen.astype(BF16), earlier) + carry
        carry = carry + jnp.sum(chosen, axis=1, keepdims=True)
        for i in range(TOP):
            slot = jnp.sum(jnp.where(hits[i], before, 0.0), axis=0, keepdims=True).astype(jnp.int32)
            route = routes[i : i + 1]
            owner = route // 2
            local = slot - half_index * half
            mine = (route - 2 * owner == pair_class) & (local >= 0) & (local < half)
            code_ref[i : i + 1, cols] = jnp.where(mine, owner * half + local, -1)


def local_codes(place, routes_t, half, groups):
    return pl.pallas_call(
        partial(code_kernel, half=half, groups=groups),
        in_specs=[
            pl.BlockSpec(memory_space=pltpu.SMEM),
            pl.BlockSpec(memory_space=pltpu.VMEM),
        ],
        out_specs=pl.BlockSpec(memory_space=pltpu.VMEM),
        out_shape=jax.ShapeDtypeStruct(routes_t.shape, jnp.int32),
        compiler_params=params(),
    )(place, routes_t)


def gates_kernel(h0_ref, h1_ref, router_ref, routes_ref, gates_ref):
    expert = lax.broadcasted_iota(jnp.int32, (EXPERTS, SEQ), 0)
    for seq, ref in enumerate((h0_ref, h1_ref)):
        cols = slice(seq * SEQ, (seq + 1) * SEQ)
        logits = mm(router_ref[...], ref[...], NT)
        picked = [
            jnp.sum(jnp.where(routes_ref[i : i + 1, cols] == expert, logits, 0.0), axis=0, keepdims=True)
            for i in range(TOP)
        ]
        top = jnp.maximum(picked[0], picked[1])
        raised = [jnp.exp(value - top) for value in picked]
        total = raised[0] + raised[1]
        for i in range(TOP):
            gates_ref[i : i + 1, cols] = raised[i] / total


def pair_gates(h0, h1, router_t, routes_t):
    return pl.pallas_call(
        gates_kernel,
        in_specs=[pl.BlockSpec(memory_space=pltpu.VMEM)] * 4,
        out_specs=pl.BlockSpec(memory_space=pltpu.VMEM),
        out_shape=jax.ShapeDtypeStruct(routes_t.shape, F32),
        compiler_params=params(),
        cost_estimate=cost(2 * routes_t.shape[1] * EXPERTS * 1024 * 8, 4 * MIB),
    )(h0, h1, router_t, routes_t)


def dispatch_kernel(code_ref, gates_ref, h0_ref, h1_ref, dy_ref, rows_ref, grads_ref, dy_rows_ref, gate_ref):
    count = rows_ref.shape[0]
    slot = lax.broadcasted_iota(jnp.int32, (count, SEQ), 0) + pl.program_id(0) * count
    rows = jnp.zeros(rows_ref.shape, F32)
    dy_rows = jnp.zeros(rows_ref.shape, F32)
    gate = jnp.zeros((count, 1), F32)
    for seq, ref in enumerate((h0_ref, h1_ref)):
        cols = slice(seq * SEQ, (seq + 1) * SEQ)
        hits = [slot == code_ref[i : i + 1, cols] for i in range(TOP)]
        take = jnp.where(hits[0] | hits[1], 1.0, 0.0).astype(BF16)
        weighted = jnp.where(hits[0], gates_ref[0:1, cols], jnp.where(hits[1], gates_ref[1:2, cols], 0.0))
        gate = gate + jnp.sum(weighted, axis=1, keepdims=True)
        rows = rows + mm(take, ref[...])
        dy_rows = dy_rows + mm(take, dy_ref[cols, :])
    rows_ref[...] = rows.astype(BF16)
    dy_rows_ref[...] = dy_rows.astype(BF16)
    grads_ref[...] = (dy_rows * gate).astype(BF16)
    gate_ref[...] = gate


def dispatch(code, gates, h0, h1, dy, slots):
    width = h0.shape[1]
    tile = slots // 4
    row_spec = pl.BlockSpec((tile, width), lambda i: (i, 0))
    whole = lambda shape: pl.BlockSpec(shape, lambda i: (0, 0))
    return pl.pallas_call(
        dispatch_kernel,
        grid=(4,),
        in_specs=[whole(code.shape), whole(gates.shape), whole(h0.shape), whole(h1.shape), whole(dy.shape)],
        out_specs=[row_spec, row_spec, row_spec, pl.BlockSpec((tile, 1), lambda i: (i, 0))],
        out_shape=[jax.ShapeDtypeStruct((slots, width), BF16)] * 3
        + [jax.ShapeDtypeStruct((slots, 1), F32)],
        compiler_params=params(),
        cost_estimate=cost(8 * slots * SEQ * width, 8 * MIB + 6 * slots * width),
    )(code, gates, h0, h1, dy)


def gelu_parts(x):
    inner = 0.7978845608028654 * (x + 0.044715 * (x * x * x))
    bend = jnp.tanh(inner)
    half = 0.5 * (1.0 + bend)
    slope = half + 0.5 * x * (1.0 - bend * bend) * (
        0.7978845608028654 * (1.0 + 3.0 * 0.044715 * (x * x))
    )
    return x * half, slope


def partner_of(index, step):
    found = index
    for bit in (1, 2, 4):
        found = found + ((step // bit) % 2) * (1 - 2 * ((index // bit) % 2)) * bit
    return found


def expert_kernel(
    rows_in, grads_in, gate_in, up_in, down_in,
    ret_out, back_out, own_gate, own_up, own_down, far_gate, far_up, far_down,
    rows, grads, weights, sums, parts, z_send, z_recv, y_send, y_recv, p_send, p_recv, r_send, r_recv, w_send, w_recv, local,
):
    groups, half, width = rows.shape[1:]
    group, rank = lax.axis_index("expert"), lax.axis_index("tensor")
    pair_class, half_index = rank % 2, rank // 2
    across = {"tensor": rank + 1 - 2 * pair_class}
    along = {"tensor": rank + 2 - 4 * half_index}
    mesh_ids = pl.DeviceIdType.MESH
    moved = ((rows_in, rows, ret_out), (grads_in, grads, back_out))

    barrier = pltpu.get_barrier_semaphore()
    for step in range(1, groups):
        pl.semaphore_signal(
            barrier, inc=1, device_id={"expert": partner_of(group, step)}, device_id_type=mesh_ids
        )
    pl.semaphore_signal(barrier, inc=1, device_id=across, device_id_type=mesh_ids)
    pl.semaphore_signal(barrier, inc=1, device_id=along, device_id_type=mesh_ids)
    pl.semaphore_wait(barrier, groups + 1)

    def remote(source, target, send, recv, device):
        return pltpu.make_async_remote_copy(
            src_ref=source, dst_ref=target, send_sem=send, recv_sem=recv,
            device_id=device, device_id_type=mesh_ids,
        )

    def block(ref, number):
        return ref.at[pl.ds(pl.multiple_of(number * half, half), half)]

    def out_of(kind, step):
        source, held, _ = moved[kind]
        other = partner_of(group, step)
        return remote(
            block(source, other), held.at[0, group], z_send.at[kind, step], z_recv.at[kind, step], {"expert": other}
        )

    def forward(kind, step):
        held = moved[kind][1]
        other = partner_of(group, step)
        return remote(held.at[0, other], held.at[1, other], y_send.at[kind, step], y_recv.at[kind, step], along)

    def partial_sum(kind, step):
        held = moved[kind][1]
        other = partner_of(group, step)
        return remote(held.at[1, other], parts.at[kind, other], p_send.at[kind, step], p_recv.at[kind, step], along)

    def result(kind, step):
        other = partner_of(group, step)
        return remote(
            parts.at[kind, other], block(moved[kind][2], group), r_send.at[kind, step], r_recv.at[kind, step], {"expert": other}
        )

    def own_result(kind):
        return pltpu.make_async_copy(parts.at[kind, group], block(moved[kind][2], group), local.at[kind])

    own = [
        pltpu.make_async_copy(block(moved[kind][0], group), moved[kind][1].at[0, group], local.at[kind])
        for kind in range(2)
    ]
    for copy in own:
        copy.start()
    kept, swapped = [], []
    for number, ref in enumerate((gate_in, up_in, down_in)):
        kept.append(pltpu.make_async_copy(ref.at[pair_class], weights.at[number, 0], local.at[2 + number]))
        swapped.append(
            remote(ref.at[1 - pair_class], weights.at[number, 1], w_send.at[number], w_recv.at[number], across)
        )
    for copy in kept + swapped:
        copy.start()
    for step in range(1, groups):
        for kind in range(2):
            out_of(kind, step).start()
    for copy in own:
        copy.wait()
    for kind in range(2):
        forward(kind, 0).start()
    for number in range(3):
        for part in range(2):
            sums[number, part] = jnp.zeros(sums.shape[2:], F32)

    def finish(step):
        other = partner_of(group, step)
        for kind in range(2):
            partial_sum(kind, step).wait()
            held = moved[kind][1]
            parts[kind, other] = (parts[kind, other].astype(F32) + held[0, other].astype(F32)).astype(BF16)

        @pl.when(step == 0)
        def _():
            for kind in range(2):
                own_result(kind).start()

        @pl.when(step > 0)
        def _():
            for kind in range(2):
                result(kind, step).start()

    def body(step, carry):
        @pl.when(step < groups - 1)
        def _():
            for kind in range(2):
                out_of(kind, step + 1).wait()
                forward(kind, step + 1).start()

        @pl.when(step == 0)
        def _():
            for copy in kept + swapped:
                copy.wait()

        for kind in range(2):
            forward(kind, step).wait()
        other = partner_of(group, step)
        tile = jnp.concatenate([rows[0, other], rows[1, other]], axis=0)
        grad = jnp.concatenate([grads[0, other], grads[1, other]], axis=0)
        ret = jnp.zeros(tile.shape, F32)
        back = jnp.zeros(tile.shape, F32)
        for part in range(2):
            w_gate, w_up, w_down = weights[0, part], weights[1, part], weights[2, part]
            gate_part = mm(tile, w_gate, NT)
            up_part = mm(tile, w_up, NT)
            grad_hidden = mm(grad, w_down, NT)
            bent, slope = gelu_parts(gate_part)
            hidden = (bent * up_part).astype(BF16)
            grad_gate = (grad_hidden * up_part * slope).astype(BF16)
            grad_up = (grad_hidden * bent).astype(BF16)
            ret = ret + mm(hidden, w_down)
            back = back + mm(grad_gate, w_gate) + mm(grad_up, w_up)
            sums[0, part] += mm(grad_gate, tile, TN)
            sums[1, part] += mm(grad_up, tile, TN)
            sums[2, part] += mm(hidden, grad, TN)
        for kind, value in enumerate((ret, back)):
            held = moved[kind][1]
            held[0, other] = value[:half].astype(BF16)
            held[1, other] = value[half:].astype(BF16)
            partial_sum(kind, step).start()

        @pl.when(step > 0)
        def _():
            finish(step - 1)

        return carry

    lax.fori_loop(0, groups, body, 0)
    copies = []
    for number, (own_ref, far_ref) in enumerate(((own_gate, far_gate), (own_up, far_up), (own_down, far_down))):
        copies.append(pltpu.make_async_copy(sums.at[number, 0], own_ref, local.at[2 + number]))
        copies[-1].start()
        weights[number, 0] = sums[number, 1].astype(BF16)
        copies.append(pltpu.make_async_copy(weights.at[number, 0], far_ref, local.at[5 + number]))
        copies[-1].start()
    finish(groups - 1)
    for copy in copies:
        copy.wait()
    for kind in range(2):
        own_result(kind).wait()
        for step in range(1, groups):
            result(kind, step).wait()


def run_experts(rows, grads, w_gate, w_up, w_down):
    slots, width = rows.shape
    half = CAP // 2
    groups = slots // half
    units = w_gate.shape[1]
    anywhere = pl.BlockSpec(memory_space=pl.ANY)
    pair = pltpu.SemaphoreType.DMA((2, groups))
    return pl.pallas_call(
        expert_kernel,
        in_specs=[anywhere] * 5,
        out_specs=[anywhere] * 8,
        out_shape=[jax.ShapeDtypeStruct((slots, width), BF16)] * 2
        + [jax.ShapeDtypeStruct((units, width), F32)] * 3
        + [jax.ShapeDtypeStruct((units, width), BF16)] * 3,
        scratch_shapes=[
            pltpu.VMEM((2, groups, half, width), BF16),
            pltpu.VMEM((2, groups, half, width), BF16),
            pltpu.VMEM((3, 2, units, width), BF16),
            pltpu.VMEM((3, 2, units, width), F32),
            pltpu.VMEM((2, groups, half, width), BF16),
        ]
        + [pair] * 8
        + [pltpu.SemaphoreType.DMA((3,))] * 2
        + [pltpu.SemaphoreType.DMA((8,))],
        compiler_params=pltpu.CompilerParams(
            vmem_limit_bytes=60 * MIB, collective_id=1, has_side_effects=True
        ),
        cost_estimate=cost(72 * slots * units * width, 16 * slots * width + 30 * units * width),
    )(rows, grads, w_gate, w_up, w_down)


def pair_grads_kernel(code_ref, gates_ref, routes_ref, dy_rows_ref, ret_ref, gate_ref, logit_ref, scaled_ref):
    slots = ret_ref.shape[0]
    tokens = code_ref.shape[1]
    found = [jnp.zeros((1, tokens), F32) for _ in range(TOP)]
    tile = 320
    for start in range(0, slots, tile):
        span = slice(start, start + tile)
        ret = ret_ref[span, :].astype(F32)
        slot_grad = jnp.sum(dy_rows_ref[span, :].astype(F32) * ret, axis=1, keepdims=True)
        scaled_ref[span, :] = (ret * gate_ref[span, :]).astype(BF16)
        slot = lax.broadcasted_iota(jnp.int32, (tile, tokens), 0) + start
        for i in range(TOP):
            found[i] = found[i] + jnp.sum(
                jnp.where(slot == code_ref[i : i + 1, :], slot_grad, 0.0), axis=0, keepdims=True
            )
    mean = gates_ref[0:1] * found[0] + gates_ref[1:2] * found[1]
    expert = lax.broadcasted_iota(jnp.int32, (EXPERTS, tokens), 0)
    logit_ref[...] = sum(
        jnp.where(routes_ref[i : i + 1] == expert, gates_ref[i : i + 1] * (found[i] - mean), 0.0)
        for i in range(TOP)
    )


def pair_grads(code, gates, routes_t, dy_rows, ret, gate_rows):
    return pl.pallas_call(
        pair_grads_kernel,
        in_specs=[pl.BlockSpec(memory_space=pltpu.VMEM)] * 6,
        out_specs=[pl.BlockSpec(memory_space=pltpu.VMEM)] * 2,
        out_shape=[
            jax.ShapeDtypeStruct((EXPERTS, code.shape[1]), F32),
            jax.ShapeDtypeStruct(ret.shape, BF16),
        ],
        compiler_params=params(),
        cost_estimate=cost(ret.shape[0] * code.shape[1] * 16, 6 * ret.size),
    )(code, gates, routes_t, dy_rows, ret, gate_rows)


def spread_kernel(code_ref, rows_ref, *refs):
    out_ref = refs[-1]
    tile = out_ref.shape[0]
    slot = lax.broadcasted_iota(jnp.int32, (tile, rows_ref.shape[0]), 1)
    code = code_ref[...]
    place = jnp.where((slot == code[:, 0:1]) | (slot == code[:, 1:2]), 1.0, 0.0).astype(BF16)
    value = mm(place, rows_ref[...])
    if len(refs) == 3:
        logit, router = refs[0][...], refs[1][...]
        coarse = logit.astype(BF16)
        fine = (logit - coarse.astype(F32)).astype(BF16)
        value = value + mm(coarse, router, NT) + mm(fine, router, NT)
    out_ref[...] = value.astype(BF16)


def spread(code_cols, rows, logit=None, router=None):
    tokens, width = code_cols.shape[0], rows.shape[1]
    tile = 512
    specs = [
        pl.BlockSpec((tile, TOP), lambda i: (i, 0)),
        pl.BlockSpec(rows.shape, lambda i: (0, 0)),
    ]
    operands = [code_cols, rows]
    if logit is not None:
        specs += [
            pl.BlockSpec((tile, EXPERTS), lambda i: (i, 0)),
            pl.BlockSpec(router.shape, lambda i: (0, 0)),
        ]
        operands += [logit, router]
    return pl.pallas_call(
        spread_kernel,
        grid=(tokens // tile,),
        in_specs=specs,
        out_specs=pl.BlockSpec((tile, width), lambda i: (i, 0)),
        out_shape=jax.ShapeDtypeStruct((tokens, width), BF16),
        compiler_params=params(),
        cost_estimate=cost(2 * tokens * width * rows.shape[0], 2 * rows.size + 2 * tokens * width),
    )(*operands)


def assemble_kernel(in_ref, out_ref):
    out_ref[...] = in_ref[0].astype(out_ref.dtype)


def assemble(shards, kind):
    count, width, tile = shards.shape
    return pl.pallas_call(
        assemble_kernel,
        grid=(count,),
        in_specs=[pl.BlockSpec((1, width, tile), lambda i: (i, 0, 0))],
        out_specs=pl.BlockSpec((width, tile), lambda i: (0, i)),
        out_shape=jax.ShapeDtypeStruct((width, count * tile), kind),
        compiler_params=params(),
        cost_estimate=cost(0, 6 * shards.size),
    )(shards)


def on_device(
    layer_input, gain_one, attn_in, rel_bias, attn_out, gain_two, router,
    expert_gate, expert_up, expert_down, routes, piece_starts, grad_out,
):
    width, tokens = layer_input.shape
    ranks = lax.axis_size("tensor")
    groups = lax.axis_size("expert")
    seqs = piece_starts.shape[0]
    rank = lax.axis_index("tensor")
    pair_class, half_index = rank % 2, rank // 2
    half = CAP // 2
    share = SEQ // ranks
    across = [(r, r ^ 1) for r in range(ranks)]

    gain_col = gain_one[:, None]
    w_in = attn_in.reshape(-1, width)
    qkv, scale_one = project(layer_input, gain_col, w_in)
    tiles = bias_tiles(rel_bias)
    position = jnp.arange(SEQ, dtype=jnp.int32)[None, None, :]
    starts = piece_starts[:, :, None]
    inside = (position >= starts) & (position < starts + PIECE)
    last = jnp.max(jnp.where(inside, starts + (PIECE - 1), -1), axis=1)
    limits = jnp.maximum(last, position[0])[:, None, :]

    routes_t = routes.T
    place = jnp.stack([pair_class, half_index]).astype(jnp.int32)
    code = local_codes(place, routes_t, half, groups)
    code_cols = code.T
    dy = grad_out.T

    def own_tokens(array, seq):
        return lax.dynamic_slice_in_dim(array, seq * SEQ + rank * share, share, 1)

    mixed, lse, resid, scale_two, full_h2 = [], [], [], [], []
    for seq in range(seqs):
        mixed_seq, lse_seq, sent = attend(qkv, tiles, limits, attn_out, seq)
        summed = lax.psum_scatter(sent, "tensor", scatter_dimension=0, tiled=True)
        resid_seq = own_tokens(layer_input, seq).T.astype(F32) + summed.astype(F32)
        scale = lax.rsqrt(jnp.sum(resid_seq * resid_seq, axis=1, keepdims=True) / width + EPS)
        normed = (resid_seq * scale * gain_two).astype(BF16)
        mixed.append(mixed_seq)
        lse.append(lse_seq)
        resid.append(resid_seq)
        scale_two.append(scale)
        full_h2.append(lax.all_gather(normed, "tensor", axis=0, tiled=True))

    gates = pair_gates(full_h2[0], full_h2[1], router.T, routes_t)
    slots = groups * half
    rows, row_grads, dy_rows, gate_rows = dispatch(code, gates, full_h2[0], full_h2[1], dy, slots)

    (ret, back, own_gate, own_up, own_down, far_gate, far_up, far_down) = run_experts(
        rows, row_grads, expert_gate, expert_up, expert_down
    )
    grad_logit, scaled = pair_grads(code, gates, routes_t, dy_rows, ret, gate_rows)
    partial_h2 = spread(code_cols, back, grad_logit.T, router)
    partial_y = spread(code_cols, scaled)
    grad_router = sum(
        mm(grad_logit[:, seq * SEQ : (seq + 1) * SEQ], full_h2[seq].astype(F32))
        for seq in range(seqs)
    )

    grad_gain_two = jnp.zeros((width,), F32)
    grad_resid, full_attn, y_shards = [], [], []
    for seq in range(seqs):
        span = slice(seq * SEQ, (seq + 1) * SEQ)
        grad_h2 = lax.psum_scatter(partial_h2[span], "tensor", scatter_dimension=0, tiled=True).astype(F32)
        own_dy = own_tokens(grad_out, seq).T.astype(F32)
        grad_gain_two = grad_gain_two + jnp.sum(grad_h2 * resid[seq] * scale_two[seq], axis=0)
        scaled_h2 = grad_h2 * gain_two
        inner = jnp.sum(scaled_h2 * resid[seq], axis=1, keepdims=True)
        grad = scale_two[seq] * scaled_h2 - resid[seq] * scale_two[seq] ** 3 * inner / width + own_dy
        grad_resid.append(grad)
        full_attn.append(lax.all_gather(grad.astype(BF16), "tensor", axis=0, tiled=True))
    for seq in range(seqs):
        span = slice(seq * SEQ, (seq + 1) * SEQ)
        y_part = lax.psum_scatter(partial_y[span], "tensor", scatter_dimension=0, tiled=True)
        y_shards.append((resid[seq] + y_part.astype(F32)).astype(BF16).T)
    y_all = [lax.all_gather(shard[None], "tensor", axis=0, tiled=True) for shard in y_shards]
    layer_output = assemble(jnp.concatenate(y_all), BF16)

    grad_attn_out = sum(mm(mixed[seq], full_attn[seq]) for seq in range(seqs))
    w_in_t = w_in.T
    grad_in, near, far, shards = [], [], [], []
    grad_gain_one = jnp.zeros((width,), F32)
    for seq in range(seqs):
        dq, dk, dv, near_seq, far_seq = attend_back(
            qkv, tiles, limits, attn_out, full_attn[seq], lse[seq], seq
        )
        near.append(near_seq)
        far.append(far_seq)
        grads = [g.reshape(-1, SEQ) for g in (dq, dk, dv)]
        update, sent = project_back(layer_input, gain_col, scale_one, w_in_t, grads, seq, ranks)
        grad_in.append(update)
        grad_h1 = lax.psum_scatter(sent, "tensor", scatter_dimension=0, tiled=True)[0].astype(F32)
        own_x = own_tokens(layer_input, seq).astype(F32)
        own_scale = own_tokens(scale_one, seq)
        grad_gain_one = grad_gain_one + jnp.sum(grad_h1 * own_x * own_scale, axis=1)
        scaled_h1 = grad_h1 * gain_col
        inner = jnp.sum(scaled_h1 * own_x, axis=0, keepdims=True)
        grad = own_scale * scaled_h1 - own_x * own_scale**3 * inner / width + grad_resid[seq].T
        shards.append(lax.all_gather(grad.astype(BF16)[None], "tensor", axis=0, tiled=True))
    grad_input = assemble(jnp.concatenate(shards), F32)
    folded = bias_fold(jnp.stack(near), jnp.stack(far))
    grad_rel_bias = folded[:, :, 0].T

    def give(own, other):
        got = lax.ppermute(other, "tensor", across).astype(F32)
        first = jnp.where(pair_class == 0, own, got)
        second = jnp.where(pair_class == 0, got, own)
        return jnp.stack([first, second])

    small = lax.psum(
        jnp.concatenate([grad_gain_one[None], grad_gain_two[None], grad_router]), ("expert", "tensor")
    )
    over_experts = (
        lax.psum((grad_in[0] + grad_in[1]).astype(BF16), "expert").astype(F32),
        lax.psum(grad_rel_bias, "expert"),
        lax.psum(grad_attn_out.astype(BF16), "expert").astype(F32),
    )
    return (
        layer_output,
        grad_input,
        small[0],
        over_experts[0].reshape(attn_in.shape),
        over_experts[1],
        over_experts[2],
        small[1],
        small[2:].T,
        give(own_gate, far_gate),
        give(own_up, far_up),
        give(own_down, far_down),
    )


def allowed_pairs(seq_starts):
    position = jnp.arange(SEQ, dtype=jnp.int32)
    inside = (position[:, None] >= seq_starts[None, :]) & (
        position[:, None] < seq_starts[None, :] + PIECE
    )
    numbers = jnp.arange(seq_starts.shape[0], dtype=jnp.int32) + 1
    piece_label = jnp.sum(inside.astype(jnp.int32) * numbers[None, :], axis=1)
    causal = position[None, :] <= position[:, None]
    shared = (piece_label[:, None] == piece_label[None, :]) & (piece_label[:, None] > 0)
    return causal | shared


def slot_table(routes):
    flat_routes = routes.reshape(-1)
    onehot = (flat_routes[:, None] == jnp.arange(EXPERTS, dtype=jnp.int32)[None, :]).astype(
        jnp.int32
    )
    blocks = onehot.reshape(-1, 128, EXPERTS).astype(F32)
    earlier = jnp.tril(jnp.ones((128, 128), F32), -1)
    inside = jnp.einsum("ij,bje->bie", earlier, blocks)
    count = blocks.shape[0]
    carried = jnp.einsum("ab,be->ae", jnp.tril(jnp.ones((count, count), F32), -1), jnp.sum(blocks, axis=1), precision=HIGH)
    before = (inside + carried[:, None, :]).astype(jnp.int32).reshape(onehot.shape)
    slot_number = jnp.sum(before * onehot, axis=1)
    kept_pairs = slot_number < CAP
    slot_index = jnp.where(kept_pairs, flat_routes * CAP + slot_number, EXPERTS * CAP)
    return (slot_index.reshape(routes.shape), kept_pairs.reshape(routes.shape))


def bucket_onehot():
    offsets = jnp.arange(2 * SEQ - 1, dtype=jnp.int32) - (SEQ - 1)
    return (bucket_of(offsets)[:, None] == jnp.arange(BUCKETS, dtype=jnp.int32)[None, :]).astype(
        jnp.float32
    )


def expand_line(line):
    head_count = line.shape[0]
    padded = jnp.concatenate([line, jnp.zeros((head_count, 1), line.dtype)], axis=1)
    tiled = jnp.tile(padded, (1, SEQ))[:, : SEQ * (2 * SEQ - 1)].reshape(
        head_count, SEQ, 2 * SEQ - 1
    )
    return tiled[:, :, SEQ - 1 :]


def fold_line(full_grid):
    head_count = full_grid.shape[0]
    padded = jnp.pad(full_grid, ((0, 0), (0, 0), (SEQ - 1, 0))).reshape(
        head_count, SEQ * (2 * SEQ - 1)
    )
    padded = jnp.pad(padded, ((0, 0), (0, SEQ))).reshape(head_count, SEQ, 2 * SEQ)
    return jnp.sum(padded, axis=1)[:, : 2 * SEQ - 1]


def reduce_heads(tensor_value):
    return lax.psum(tensor_value, "tensor")


def spread_slots(tensor_value):
    return lax.all_gather(tensor_value, "tensor", axis=2, tiled=True)


def owner_exchange(tensor_value):
    return lax.all_to_all(tensor_value, "expert", split_axis=0, concat_axis=0, tiled=True)


def expert_sums(tensor_value):
    return lax.psum_scatter(tensor_value, "tensor", scatter_dimension=2, tiled=True)


def norm_forward(resid, gain, model_width):
    scale = lax.rsqrt(jnp.sum(resid * resid, axis=1) / model_width + EPS)[:, None]
    return (scale, (resid * scale * gain).astype(jnp.bfloat16))


def norm_backward(resid, scale, gain, grad_normed, model_width):
    grad_gain = jnp.sum(grad_normed * resid * scale, axis=0)
    scaled = grad_normed * gain
    inner = jnp.sum(scaled * resid, axis=1)[:, None]
    return (grad_gain, scale * scaled - resid * scale**3 * inner / model_width)


def attend_scores(bias_full, queries, key_rows, seq_starts):
    scores = (
        jnp.einsum("qhe,khe->hqk", queries, key_rows, preferred_element_type=jnp.float32) * 0.125
        + bias_full
    )
    return jnp.where(allowed_pairs(seq_starts)[None], scores, NEG)


def attend_forward(bias_full, inputs):
    queries, key_rows, value_rows, seq_starts = inputs
    scores = attend_scores(bias_full, queries, key_rows, seq_starts)
    row_max = jnp.max(scores, axis=2, keepdims=True)
    exponent = jnp.exp(scores - row_max)
    row_sum_exp = jnp.sum(exponent, axis=2, keepdims=True)
    weights = (exponent / row_sum_exp).astype(jnp.bfloat16)
    mixed_heads = jnp.einsum(
        "hqk,khe->qhe", weights, value_rows, preferred_element_type=jnp.float32
    )
    return (mixed_heads.astype(jnp.bfloat16), (row_max + jnp.log(row_sum_exp))[:, :, 0])


def attend_backward(bias_full, running, inputs):
    queries, key_rows, value_rows, grad_heads, seq_starts, log_total = inputs
    scores = attend_scores(bias_full, queries, key_rows, seq_starts)
    probabilities = jnp.exp(scores - log_total[:, :, None])
    grad_probs = jnp.einsum(
        "qhe,khe->hqk", grad_heads, value_rows, preferred_element_type=jnp.float32
    )
    inner = jnp.sum(probabilities * grad_probs, axis=2, keepdims=True)
    grad_scores = (probabilities * (grad_probs - inner)).astype(jnp.bfloat16)
    grad_values = jnp.einsum(
        "hqk,qhe->khe",
        probabilities.astype(jnp.bfloat16),
        grad_heads,
        preferred_element_type=jnp.float32,
    )
    grad_queries = (
        jnp.einsum("hqk,khe->qhe", grad_scores, key_rows, preferred_element_type=jnp.float32)
        * 0.125
    )
    grad_keys = (
        jnp.einsum("hqk,qhe->khe", grad_scores, queries, preferred_element_type=jnp.float32) * 0.125
    )
    return (
        running + grad_scores.astype(jnp.float32),
        jnp.stack([grad_queries, grad_keys, grad_values]),
    )


def gelu_product(left, right):
    return jax.nn.gelu(left, approximate=True) * right


def expert_forward(received, weight_gate, weight_up, weight_down):
    gate_part = jnp.einsum(
        "secd,efd->secf", received, weight_gate, preferred_element_type=jnp.float32
    )
    up_part = jnp.einsum("secd,efd->secf", received, weight_up, preferred_element_type=jnp.float32)
    hidden = gelu_product(gate_part, up_part).astype(jnp.bfloat16)
    partial_out = jnp.einsum(
        "secf,efd->secd", hidden, weight_down, preferred_element_type=jnp.float32
    )
    return (gate_part, up_part, hidden, partial_out)


def expert_backward(
    received, gate_part, up_part, hidden, grad_rows_out, weight_gate, weight_up, weight_down
):
    grad_hidden = jnp.einsum(
        "secd,efd->secf", grad_rows_out, weight_down, preferred_element_type=jnp.float32
    )
    product_value, pullback = jax.vjp(gelu_product, gate_part, up_part)
    grad_gate_part, grad_up_part = pullback(grad_hidden)
    grad_gate_part = grad_gate_part.astype(jnp.bfloat16)
    grad_up_part = grad_up_part.astype(jnp.bfloat16)
    grad_down = jnp.einsum(
        "secf,secd->efd", hidden, grad_rows_out, preferred_element_type=jnp.float32
    )
    grad_gate_w = jnp.einsum(
        "secf,secd->efd", grad_gate_part, received, preferred_element_type=jnp.float32
    )
    grad_up_w = jnp.einsum(
        "secf,secd->efd", grad_up_part, received, preferred_element_type=jnp.float32
    )
    grad_rows_in = jnp.einsum(
        "secf,efd->secd", grad_gate_part, weight_gate, preferred_element_type=jnp.float32
    )
    grad_rows_in = grad_rows_in + jnp.einsum(
        "secf,efd->secd", grad_up_part, weight_up, preferred_element_type=jnp.float32
    )
    return (grad_gate_w, grad_up_w, grad_down, grad_rows_in)


def on_device_general(
    layer_input,
    gain_one,
    attn_in,
    rel_bias,
    attn_out,
    gain_two,
    router,
    expert_gate,
    expert_up,
    expert_down,
    routes,
    piece_starts,
    grad_out,
):
    tok_count = layer_input.shape[1]
    model_width = layer_input.shape[0]
    heads_here = rel_bias.shape[1]
    head_width = attn_in.shape[1] // heads_here
    seqs_here = piece_starts.shape[0]
    local_experts = expert_gate.shape[0]
    part_rows = CAP // lax.axis_size("tensor")
    share_start = lax.axis_index("tensor") * part_rows
    tokens = layer_input.T.astype(jnp.float32)
    scale_one, normed = norm_forward(tokens, gain_one, model_width)
    project = jnp.einsum("td,chd->cth", normed, attn_in, preferred_element_type=jnp.float32).astype(
        jnp.bfloat16
    )
    by_seq = project.reshape(3, seqs_here, SEQ, heads_here, head_width)
    onehot_line = bucket_onehot()
    bias_full = expand_line(jnp.dot(onehot_line, rel_bias, precision=HIGH).T)
    mixed_heads, log_total = lax.map(
        partial(attend_forward, bias_full), (by_seq[0], by_seq[1], by_seq[2], piece_starts)
    )
    mixed_heads = mixed_heads.reshape(tok_count, heads_here * head_width)
    resid = tokens + reduce_heads(
        jnp.dot(mixed_heads, attn_out, preferred_element_type=jnp.float32)
    )
    scale_two, normed_two = norm_forward(resid, gain_two, model_width)
    logits = jnp.dot(normed_two, router, preferred_element_type=jnp.float32)
    chosen = (routes[:, :, None] == jnp.arange(EXPERTS, dtype=jnp.int32)[None, None, :]).astype(
        jnp.float32
    )
    picked = jnp.sum(chosen * logits[:, None, :], axis=2)
    gate_weights = jax.nn.softmax(picked, axis=1)
    slot_index, kept_pairs = slot_table(routes)
    keep_float = kept_pairs.astype(jnp.float32)
    mix_weight = gate_weights * keep_float
    safe_index = jnp.minimum(slot_index, EXPERTS * CAP - 1)
    token_rows = jnp.repeat(normed_two, TOP, axis=0)
    buffer = (
        jnp.zeros((EXPERTS * CAP + 1, model_width), jnp.bfloat16)
        .at[slot_index.reshape(-1)]
        .set(token_rows)
    )
    buffer = buffer[: EXPERTS * CAP].reshape(-1, local_experts, CAP, model_width)
    received = lax.all_to_all(buffer, "expert", split_axis=0, concat_axis=0, tiled=True)
    gate_part, up_part, hidden, partial_out = expert_forward(
        received, expert_gate, expert_up, expert_down
    )
    returned = spread_slots(owner_exchange(expert_sums(partial_out).astype(jnp.bfloat16)))
    flat_ret = returned.reshape(EXPERTS * CAP, model_width)
    fetched = flat_ret[safe_index].astype(jnp.float32)
    output = resid + jnp.sum(mix_weight[:, :, None] * fetched, axis=1)
    grad_y = grad_out.T.astype(jnp.float32)
    grad_gates = jnp.sum(grad_y[:, None, :] * fetched, axis=2) * keep_float
    grad_picked = gate_weights * (
        grad_gates - jnp.sum(gate_weights * grad_gates, axis=1, keepdims=True)
    )
    grad_logits = jnp.sum(chosen * grad_picked[:, :, None], axis=1)
    grad_router = jnp.dot(normed_two.astype(jnp.float32).T, grad_logits, precision=HIGH)
    grad_normed_two = jnp.dot(grad_logits, router.astype(jnp.float32).T, precision=HIGH)
    slot_grads = (mix_weight[:, :, None] * grad_y[:, None, :]).astype(jnp.bfloat16)
    grad_ret = (
        jnp.zeros((EXPERTS * CAP + 1, model_width), jnp.bfloat16)
        .at[slot_index.reshape(-1)]
        .set(slot_grads.reshape(-1, model_width))
    )
    grad_ret = grad_ret[: EXPERTS * CAP].reshape(-1, local_experts, CAP, model_width)
    grad_share = lax.dynamic_slice_in_dim(grad_ret, share_start, part_rows, 2)
    grad_rows_out = spread_slots(owner_exchange(grad_share))
    grad_expert_gate, grad_expert_up, grad_expert_down, grad_rows_in = expert_backward(
        received, gate_part, up_part, hidden, grad_rows_out, expert_gate, expert_up, expert_down
    )
    grad_back = spread_slots(owner_exchange(expert_sums(grad_rows_in).astype(jnp.bfloat16)))
    flat_back = grad_back.reshape(EXPERTS * CAP, model_width).astype(jnp.float32)
    grad_normed_two = grad_normed_two + jnp.sum(
        flat_back[safe_index] * keep_float[:, :, None], axis=1
    )
    grad_gain_two, grad_resid = norm_backward(
        resid, scale_two, gain_two, grad_normed_two, model_width
    )
    grad_resid = grad_resid + grad_y
    grad_attn = grad_resid.astype(jnp.bfloat16)
    grad_attn_out = jnp.einsum(
        "th,td->hd", mixed_heads, grad_attn, preferred_element_type=jnp.float32
    )
    grad_mixed = jnp.einsum(
        "td,hd->th", grad_attn, attn_out, preferred_element_type=jnp.float32
    ).astype(jnp.bfloat16)
    grad_by_seq = grad_mixed.reshape(seqs_here, SEQ, heads_here, head_width)
    bias_grad_full, grad_project = lax.scan(
        partial(attend_backward, bias_full),
        jnp.zeros_like(bias_full),
        (by_seq[0], by_seq[1], by_seq[2], grad_by_seq, piece_starts, log_total),
    )
    grad_project = (
        jnp.moveaxis(grad_project, 1, 0)
        .reshape(3, tok_count, heads_here * head_width)
        .astype(jnp.bfloat16)
    )
    grad_attn_in = jnp.einsum(
        "cth,td->chd", grad_project, normed, preferred_element_type=jnp.float32
    )
    grad_normed = reduce_heads(
        jnp.einsum("cth,chd->td", grad_project, attn_in, preferred_element_type=jnp.float32)
    )
    grad_gain_one, grad_tokens = norm_backward(
        tokens, scale_one, gain_one, grad_normed, model_width
    )
    grad_tokens = grad_tokens + grad_resid
    grad_rel_bias = jnp.dot(onehot_line.T, fold_line(bias_grad_full).T, precision=HIGH)
    shared = (
        lax.psum(grad_gain_one.astype(jnp.bfloat16), "expert").astype(jnp.float32),
        lax.psum(grad_attn_in.astype(jnp.bfloat16), "expert").astype(jnp.float32),
        lax.psum(grad_rel_bias.astype(jnp.bfloat16), "expert").astype(jnp.float32),
        lax.psum(grad_attn_out.astype(jnp.bfloat16), "expert").astype(jnp.float32),
        lax.psum(grad_gain_two.astype(jnp.bfloat16), "expert").astype(jnp.float32),
        lax.psum(grad_router.astype(jnp.bfloat16), "expert").astype(jnp.float32),
    )
    return (
        output.astype(jnp.bfloat16).T,
        grad_tokens.T,
        shared[0],
        shared[1],
        shared[2],
        shared[3],
        shared[4],
        shared[5],
        grad_expert_gate,
        grad_expert_up,
        grad_expert_down,
    )


def solution(mesh):
    placed = (
        P(None, "expert"),
        P(),
        P(None, "tensor", None),
        P(None, "tensor"),
        P("tensor", None),
        P(),
        P(),
        P("expert", "tensor", None),
        P("expert", "tensor", None),
        P("expert", "tensor", None),
        P("expert", None),
        P("expert", None),
        P(None, "expert"),
    )
    paired = mesh.shape["tensor"] == 4 and mesh.shape["expert"] * 2 == EXPERTS
    return jax.shard_map(
        on_device if paired else on_device_general,
        mesh=mesh,
        in_specs=placed,
        out_specs=(
            P(None, "expert"),
            P(None, "expert"),
            P(),
            P(None, "tensor", None),
            P(None, "tensor"),
            P("tensor", None),
            P(),
            P(),
            P("expert", "tensor", None),
            P("expert", "tensor", None),
            P("expert", "tensor", None),
        ),
        check_vma=False,
    )
```

```python
from functools import partial

import jax
import jax.numpy as jnp
from jax import lax
from jax.experimental import pallas as pl
from jax.experimental.pallas import tpu as pltpu
from jax.sharding import PartitionSpec as P

EXPERTS = 16
BUCKETS = 32
TOP = 2
PIECE = 256
SEQ = 1024
CAP = 320
BLK = 256


EPS = 1e-06
NEG = -1e30
THRESHOLDS = (12, 16, 23, 32, 46, 64, 91)
HIGH = lax.Precision.HIGHEST
F32 = jnp.float32
BF16 = jnp.bfloat16
NN = (((1,), (0,)), ((), ()))
NT = (((1,), (1,)), ((), ()))
TN = (((0,), (0,)), ((), ()))
MIB = 1 << 20


def mm(left, right, dims=NN):
    return lax.dot_general(left, right, dims, preferred_element_type=F32)


def params(limit=56):
    return pltpu.CompilerParams(vmem_limit_bytes=limit * MIB)


def cost(flops, bytes_accessed, transcendentals=0):
    return pl.CostEstimate(
        flops=int(flops), bytes_accessed=int(bytes_accessed), transcendentals=int(transcendentals)
    )


def bucket_of(offset):
    magnitude = jnp.abs(offset)
    beyond = sum(((magnitude >= threshold).astype(jnp.int32) for threshold in THRESHOLDS))
    lower_part = jnp.where(magnitude < 8, magnitude, 8 + beyond)
    return lower_part + 16 * (offset > 0).astype(jnp.int32)


def project_kernel(x_ref, gain_ref, w_ref, out_ref, scale_ref):
    x = x_ref[...].astype(F32)
    scale = lax.rsqrt(jnp.sum(x * x, axis=0, keepdims=True) / x.shape[0] + EPS)
    normed = (x * scale * gain_ref[...]).astype(BF16)
    out_ref[...] = mm(w_ref[...], normed).astype(BF16)
    scale_ref[...] = scale


def project(x, gain, weights):
    width, tokens = x.shape
    rows = weights.shape[0]
    tile = 512
    return pl.pallas_call(
        project_kernel,
        grid=(tokens // tile,),
        in_specs=[
            pl.BlockSpec((width, tile), lambda i: (0, i)),
            pl.BlockSpec((width, 1), lambda i: (0, 0)),
            pl.BlockSpec((rows, width), lambda i: (0, 0)),
        ],
        out_specs=[
            pl.BlockSpec((rows, tile), lambda i: (0, i)),
            pl.BlockSpec((1, tile), lambda i: (0, i)),
        ],
        out_shape=[
            jax.ShapeDtypeStruct((rows, tokens), BF16),
            jax.ShapeDtypeStruct((1, tokens), F32),
        ],
        compiler_params=params(),
        cost_estimate=cost(2 * width * tokens * rows, 2 * width * tokens * 2),
    )(x, gain, weights)


def bias_tiles_kernel(table_ref, tiles_ref):
    key_at = lax.broadcasted_iota(jnp.int32, (BLK, BLK), 0)
    query_at = lax.broadcasted_iota(jnp.int32, (BLK, BLK), 1)
    for number, shift in enumerate((-1, 0, 1)):
        offset = key_at - query_at + shift * BLK
        bucket = bucket_of(offset)
        low, high = {-1: (0, 16), 0: (0, 32), 1: (16, 32)}[shift]
        for head in range(tiles_ref.shape[0]):
            far = table_ref[15, head]
            value = jnp.zeros((BLK, BLK), F32)
            for index in range(low, high):
                value = jnp.where(bucket == index, table_ref[index, head] - far, value)
            tiles_ref[head, number] = value


def bias_tiles(table):
    heads = table.shape[1]
    return pl.pallas_call(
        bias_tiles_kernel,
        in_specs=[pl.BlockSpec(memory_space=pltpu.SMEM)],
        out_specs=pl.BlockSpec(memory_space=pltpu.VMEM),
        out_shape=jax.ShapeDtypeStruct((heads, 3, BLK, BLK), F32),
        compiler_params=params(),
        cost_estimate=cost(heads * 3 * BLK * BLK * 60, heads * 3 * BLK * BLK * 4),
    )(table)


def bias_fold_kernel(near_ref, far_ref, out_ref):
    heads = out_ref.shape[0]
    key_at = lax.broadcasted_iota(jnp.int32, (BLK, BLK), 0)
    query_at = lax.broadcasted_iota(jnp.int32, (BLK, BLK), 1)
    totals = [[jnp.zeros((8, BLK), F32) for _ in range(BUCKETS)] for _ in range(heads)]
    for number, shift in enumerate((-1, 0, 1)):
        bucket = bucket_of(key_at - query_at + shift * BLK)
        low, high = {-1: (0, 16), 0: (0, 32), 1: (16, 32)}[shift]
        for head in range(heads):
            grads = near_ref[head, number] + near_ref[heads + head, number]
            for index in range(low, high):
                kept = jnp.where(bucket == index, grads, 0.0)
                totals[head][index] = totals[head][index] + jnp.sum(
                    kept.reshape(BLK // 8, 8, BLK), axis=0
                )
    for head in range(heads):
        totals[head][15] = totals[head][15] + far_ref[head] + far_ref[heads + head]
        for index in range(BUCKETS):
            line = jnp.sum(totals[head][index], axis=0, keepdims=True)
            out_ref[head, index : index + 1, :] = jnp.broadcast_to(
                jnp.sum(line, axis=1, keepdims=True), (1, 128)
            )


def bias_fold(near, far):
    heads = near.shape[0] // 2
    return pl.pallas_call(
        bias_fold_kernel,
        in_specs=[pl.BlockSpec(memory_space=pltpu.VMEM)] * 2,
        out_specs=pl.BlockSpec(memory_space=pltpu.VMEM),
        out_shape=jax.ShapeDtypeStruct((heads, BUCKETS, 128), F32),
        compiler_params=params(),
        cost_estimate=cost(heads * 3 * BLK * BLK * 60, heads * 6 * BLK * BLK * 4),
    )(near, far)


def key_count(query_block):
    return 2 * BLK if query_block < 2 else 4 * BLK


def block_scores(keys, queries, tiles_ref, limit, block):
    count = key_count(block)
    parts = []
    whole = mm(keys[:, :count], queries, TN)
    for key_block in range(count // BLK):
        part = whole[key_block * BLK : (key_block + 1) * BLK]
        shift = key_block - block
        if -1 <= shift <= 1:
            part = part + tiles_ref[0, shift + 1]
        if shift >= 0:
            key_at = lax.broadcasted_iota(jnp.int32, (BLK, BLK), 0) + key_block * BLK
            part = jnp.where(key_at <= limit, part, NEG)
        parts.append(part)
    return jnp.concatenate(parts, axis=0)


def attend_kernel(q_ref, k_ref, v_ref, tiles_ref, limit_ref, w_ref, out_ref, lse_ref, sent_ref, held):
    head = pl.program_id(1)
    width = q_ref.shape[0]
    queries = q_ref[...] * BF16(0.125)
    keys, values = k_ref[...], v_ref[...]
    for block in range(SEQ // BLK):
        cols = slice(block * BLK, (block + 1) * BLK)
        scores = block_scores(keys, queries[:, cols], tiles_ref, limit_ref[0, :, cols], block)
        top = jnp.max(scores, axis=0, keepdims=True)
        exponent = jnp.exp(scores - top)
        total = jnp.sum(exponent, axis=0, keepdims=True)
        mixed = mm(values[:, : key_count(block)], exponent.astype(BF16)) / total
        mixed = mixed.astype(BF16)
        out_ref[:, cols] = mixed
        held[pl.ds(pl.multiple_of(head * width, width), width), cols] = mixed
        lse_ref[0, :, cols] = top + jnp.log(total)

    @pl.when(head == pl.num_programs(1) - 1)
    def _():
        sent_ref[...] = mm(held[...], w_ref[...], TN).astype(BF16)


def attend(qkv, tiles, limits, attn_out):
    heads = tiles.shape[0]
    seqs = limits.shape[0]
    width = qkv.shape[0] // (3 * heads)
    model_width = attn_out.shape[1]
    return pl.pallas_call(
        attend_kernel,
        grid=(seqs, heads),
        in_specs=[
            pl.BlockSpec((width, SEQ), lambda s, h: (h, s)),
            pl.BlockSpec((width, SEQ), lambda s, h: (heads + h, s)),
            pl.BlockSpec((width, SEQ), lambda s, h: (2 * heads + h, s)),
            pl.BlockSpec((1, 3, BLK, BLK), lambda s, h: (h, 0, 0, 0)),
            pl.BlockSpec((1, 1, SEQ), lambda s, h: (s, 0, 0)),
            pl.BlockSpec((heads * width, model_width), lambda s, h: (0, 0)),
        ],
        out_specs=[
            pl.BlockSpec((width, SEQ), lambda s, h: (h, s)),
            pl.BlockSpec((1, 1, SEQ), lambda s, h: (s * heads + h, 0, 0)),
            pl.BlockSpec((SEQ, model_width), lambda s, h: (s, 0)),
        ],
        out_shape=[
            jax.ShapeDtypeStruct((heads * width, seqs * SEQ), BF16),
            jax.ShapeDtypeStruct((seqs * heads, 1, SEQ), F32),
            jax.ShapeDtypeStruct((seqs * SEQ, model_width), BF16),
        ],
        scratch_shapes=[pltpu.VMEM((heads * width, SEQ), BF16)],
        compiler_params=params(),
        cost_estimate=cost(seqs * heads * SEQ * SEQ * 512, seqs * heads * SEQ * 2048, seqs * heads * SEQ * SEQ),
    )(qkv, qkv, qkv, tiles, limits, attn_out)


def attend_back_kernel(
    place_ref, q_ref, k_ref, v_ref, tiles_ref, limit_ref, w_ref, grad_ref, lse_ref, *refs
):
    own_refs, got_refs = refs[:3], refs[3:6]
    dq_ref, dk_ref, dv_ref, near_ref, far_ref = refs[6:11]
    placed_refs, held = refs[11:14], refs[14]

    @pl.when(pl.program_id(0) == 0)
    def _():
        for source, target in zip(own_refs, placed_refs):
            target[0] = source[...]

    @pl.when(pl.program_id(0) == 1)
    def _():
        for source, target in zip(got_refs, placed_refs):
            target[0] = source[...].astype(F32)

    head = pl.program_id(1)
    width = q_ref.shape[0]

    @pl.when(head == 0)
    def _():
        held[...] = mm(w_ref[...], grad_ref[...], NT).astype(BF16)

    queries = q_ref[...] * BF16(0.125)
    keys, values = k_ref[...], v_ref[...]
    grads = held[pl.ds(pl.multiple_of(head * width, width), width), :]
    near_ref[...] = jnp.zeros_like(near_ref)
    far = jnp.zeros((8, BLK), F32)
    grad_keys = jnp.zeros((width, SEQ), F32)
    grad_values = jnp.zeros((width, SEQ), F32)
    for block in range(SEQ // BLK):
        count = key_count(block)
        cols = slice(block * BLK, (block + 1) * BLK)
        scores = block_scores(keys, queries[:, cols], tiles_ref, limit_ref[0, :, cols], block)
        probs = jnp.exp(scores - lse_ref[0, :, cols])
        grad_probs = mm(values[:, :count], grads[:, cols], TN)
        inner = jnp.sum(probs * grad_probs, axis=0, keepdims=True)
        grad_scores = probs * (grad_probs - inner)
        for key_block in range(count // BLK):
            part = grad_scores[key_block * BLK : (key_block + 1) * BLK]
            shift = key_block - block
            if -1 <= shift <= 1:
                near_ref[0, shift + 1] += part
            elif shift < -1:
                far = far + jnp.sum(part.reshape(BLK // 8, 8, BLK), axis=0)
        rounded = grad_scores.astype(BF16)
        add_values = mm(grads[:, cols], probs.astype(BF16), NT)
        add_keys = mm(queries[:, cols], rounded, NT)
        if count == SEQ:
            grad_values = grad_values + add_values
            grad_keys = grad_keys + add_keys
        else:
            filler = jnp.zeros((width, SEQ - count), F32)
            grad_values = grad_values + jnp.concatenate([add_values, filler], axis=1)
            grad_keys = grad_keys + jnp.concatenate([add_keys, filler], axis=1)
        dq_ref[:, cols] = (mm(keys[:, :count], rounded) * 0.125).astype(BF16)
    dk_ref[...] = grad_keys.astype(BF16)
    dv_ref[...] = grad_values.astype(BF16)
    far_ref[0] = far


def attend_back(place, qkv, tiles, limits, attn_out, grad_attn, lse, own_grads, got_grads):
    heads = tiles.shape[0]
    seqs = limits.shape[0]
    width = qkv.shape[0] // (3 * heads)
    model_width = attn_out.shape[1]
    units = own_grads[0].shape[0]
    tile = units // heads
    grad_spec = pl.BlockSpec((width, SEQ), lambda s, h, p: (h, s))
    own_spec = pl.BlockSpec((tile, model_width), lambda s, h, p: (jnp.where(s == 0, h, heads - 1), 0))
    got_spec = pl.BlockSpec((tile, model_width), lambda s, h, p: (jnp.where(s == 0, 0, h), 0))
    placed_spec = pl.BlockSpec(
        (1, tile, model_width), lambda s, h, p: (jnp.where(s == 0, p[0], 1 - p[0]), h, 0)
    )
    return pl.pallas_call(
        attend_back_kernel,
        grid_spec=pltpu.PrefetchScalarGridSpec(
            num_scalar_prefetch=1,
            grid=(seqs, heads),
            in_specs=[
                pl.BlockSpec((width, SEQ), lambda s, h, p: (h, s)),
                pl.BlockSpec((width, SEQ), lambda s, h, p: (heads + h, s)),
                pl.BlockSpec((width, SEQ), lambda s, h, p: (2 * heads + h, s)),
                pl.BlockSpec((1, 3, BLK, BLK), lambda s, h, p: (h, 0, 0, 0)),
                pl.BlockSpec((1, 1, SEQ), lambda s, h, p: (s, 0, 0)),
                pl.BlockSpec((heads * width, model_width), lambda s, h, p: (0, 0)),
                pl.BlockSpec((SEQ, model_width), lambda s, h, p: (s, 0)),
                pl.BlockSpec((1, 1, SEQ), lambda s, h, p: (s * heads + h, 0, 0)),
            ]
            + [own_spec] * 3
            + [got_spec] * 3,
            out_specs=[
                grad_spec,
                grad_spec,
                grad_spec,
                pl.BlockSpec((1, 3, BLK, BLK), lambda s, h, p: (s * heads + h, 0, 0, 0)),
                pl.BlockSpec((1, 8, BLK), lambda s, h, p: (s * heads + h, 0, 0)),
            ]
            + [placed_spec] * 3,
            scratch_shapes=[pltpu.VMEM((heads * width, SEQ), BF16)],
        ),
        out_shape=[jax.ShapeDtypeStruct((heads * width, seqs * SEQ), BF16)] * 3
        + [
            jax.ShapeDtypeStruct((seqs * heads, 3, BLK, BLK), F32),
            jax.ShapeDtypeStruct((seqs * heads, 8, BLK), F32),
        ]
        + [jax.ShapeDtypeStruct((2, units, model_width), F32)] * 3,
        compiler_params=params(),
        cost_estimate=cost(seqs * heads * SEQ * SEQ * 1280, seqs * heads * SEQ * 4096, seqs * heads * SEQ * SEQ),
    )(place, qkv, qkv, qkv, tiles, limits, attn_out, grad_attn, lse, *own_grads, *got_grads)


def project_back_kernel(x_ref, gain_ref, scale_ref, w_ref, dq_ref, dk_ref, dv_ref, weight_ref, out_ref, gain_grad_ref):
    grads = jnp.concatenate([dq_ref[...], dk_ref[...], dv_ref[...]], axis=0)
    scaled = x_ref[...].astype(F32) * scale_ref[...]
    update = mm(grads, (scaled * gain_ref[...]).astype(BF16), NT)
    back = mm(w_ref[...], grads, TN)
    gain_update = jnp.sum(back * scaled, axis=1, keepdims=True)

    @pl.when(pl.program_id(0) == 0)
    def _():
        weight_ref[...] = update
        gain_grad_ref[...] = gain_update

    @pl.when(pl.program_id(0) > 0)
    def _():
        weight_ref[...] += update
        gain_grad_ref[...] += gain_update

    out_ref[...] = back.T.astype(BF16)


def project_back(x, gain, scale, weights, grads):
    width, tokens = x.shape
    rows = weights.shape[0]
    tile = 512
    return pl.pallas_call(
        project_back_kernel,
        grid=(tokens // tile,),
        in_specs=[
            pl.BlockSpec((width, tile), lambda i: (0, i)),
            pl.BlockSpec((width, 1), lambda i: (0, 0)),
            pl.BlockSpec((1, tile), lambda i: (0, i)),
            pl.BlockSpec((rows, width), lambda i: (0, 0)),
        ]
        + [pl.BlockSpec((rows // 3, tile), lambda i: (0, i))] * 3,
        out_specs=[
            pl.BlockSpec((rows, width), lambda i: (0, 0)),
            pl.BlockSpec((tile, width), lambda i: (i, 0)),
            pl.BlockSpec((width, 1), lambda i: (0, 0)),
        ],
        out_shape=[
            jax.ShapeDtypeStruct((rows, width), F32),
            jax.ShapeDtypeStruct((tokens, width), BF16),
            jax.ShapeDtypeStruct((width, 1), F32),
        ],
        compiler_params=params(),
        cost_estimate=cost(4 * width * tokens * rows, 6 * width * tokens),
    )(x, gain, scale, weights, *grads)


def exchange(math, rank, source, full, from_across, from_along, to_across, to_along, turn_across, turn_along, sends, recvs, ready=None, ready_full=None):
    pair_class, half_index = rank % 2, rank // 2
    across, along, corner = rank + 1 - 2 * pair_class, rank + 2 - 4 * half_index, 3 - rank
    mesh_ids = pl.DeviceIdType.MESH
    rows, width = source.shape[1:]
    chunks = 4
    size = rows // chunks
    low, high = slice(0, width // 2), slice(width // 2, width)
    barrier = pltpu.get_barrier_semaphore()
    for other in (across, along):
        pl.semaphore_signal(barrier, inc=1, device_id={"tensor": other}, device_id_type=mesh_ids)
    pl.semaphore_wait(barrier, 2)

    def remote(kind, chunk, origin, target, other):
        return pltpu.make_async_remote_copy(
            src_ref=origin, dst_ref=target, send_sem=sends.at[kind, chunk], recv_sem=recvs.at[kind, chunk],
            device_id={"tensor": other}, device_id_type=mesh_ids,
        )

    spans = [slice(chunk * size, (chunk + 1) * size) for chunk in range(chunks)]
    first, second, third, fourth = [], [], [], []
    for chunk, span in enumerate(spans):
        pair = (
            remote(0, chunk, source.at[corner, span, low], turn_across.at[span], across),
            remote(1, chunk, source.at[corner, span, high], turn_along.at[span], along),
        )
        for copy in pair:
            copy.start()
        first.append(pair)
    if ready is not None:
        ready_full[rank] = ready[...]
        extra = [
            remote(8, 0, ready, ready_full.at[rank], across),
            remote(8, 1, ready, ready_full.at[rank], along),
            remote(8, 2, ready_full.at[along, :, high], ready_full.at[along, :, high], across),
            remote(8, 3, ready_full.at[across, :, low], ready_full.at[across, :, low], along),
        ]
    for chunk, span in enumerate(spans):
        first[chunk][0].wait()
        to_along[span, low] = (source[along, span, low].astype(F32) + turn_across[span].astype(F32)).astype(BF16)
        to_along[span, high] = source[along, span, high]
        first[chunk][1].wait()
        to_across[span, low] = source[across, span, low]
        to_across[span, high] = (source[across, span, high].astype(F32) + turn_along[span].astype(F32)).astype(BF16)
        pair = (
            remote(2, chunk, to_across.at[span], from_across.at[span], across),
            remote(3, chunk, to_along.at[span], from_along.at[span], along),
        )
        for copy in pair:
            copy.start()
        second.append(pair)
    if ready is not None:
        for copy in extra[:2]:
            copy.start()

    def pass_on(chunk):
        span = spans[chunk]
        for copy in third[chunk]:
            copy.wait()
        pair = (
            remote(6, chunk, full.at[along, span, high], full.at[along, span, high], across),
            remote(7, chunk, full.at[across, span, low], full.at[across, span, low], along),
        )
        for copy in pair:
            copy.start()
        fourth.append(pair)

    for chunk, span in enumerate(spans):
        for copy in second[chunk]:
            copy.wait()
        total = source[rank, span].astype(F32) + from_across[span].astype(F32) + from_along[span].astype(F32)
        full[rank, span] = math(span, total).astype(BF16)
        pair = (
            remote(4, chunk, full.at[rank, span], full.at[rank, span], across),
            remote(5, chunk, full.at[rank, span], full.at[rank, span], along),
        )
        for copy in pair:
            copy.start()
        third.append(pair)
        if chunk:
            pass_on(chunk - 1)
    pass_on(chunks - 1)
    if ready is not None:
        for copy in extra[:2]:
            copy.wait()
        for copy in extra[2:]:
            copy.start()
        for copy in extra[2:]:
            copy.wait()
    for pair in fourth:
        for copy in pair:
            copy.wait()


def exchange_call(kernel, number, source, operands, extra_shapes):
    tokens, width = source.shape
    ranks = 4
    rows = tokens // ranks
    anywhere = pl.BlockSpec(memory_space=pltpu.VMEM)
    results = pl.pallas_call(
        kernel,
        in_specs=[anywhere] * (1 + len(operands)),
        out_specs=[anywhere] * (1 + len(extra_shapes)),
        out_shape=[jax.ShapeDtypeStruct((ranks, rows, width), BF16)]
        + [jax.ShapeDtypeStruct(shape, kind) for shape, kind in extra_shapes],
        scratch_shapes=[pltpu.VMEM((rows, width), BF16)] * 4
        + [pltpu.VMEM((rows, width // 2), BF16)] * 2
        + [pltpu.SemaphoreType.DMA((9, 4))] * 2,
        compiler_params=pltpu.CompilerParams(
            vmem_limit_bytes=48 * MIB, collective_id=number, has_side_effects=True
        ),
        cost_estimate=cost(40 * MIB, 200 * MIB),
    )(source.reshape(ranks, rows, width), *operands)
    return results[0].reshape(tokens, width), *results[1:]


def norm_two_kernel(source, x_ref, gain_ref, full, resid_ref, scale_ref, *rest):
    def math(span, total):
        resid = x_ref[span, :].astype(F32) + total
        scale = lax.rsqrt(jnp.sum(resid * resid, axis=1, keepdims=True) / resid.shape[1] + EPS)
        resid_ref[span, :] = resid
        scale_ref[span, :] = scale
        return resid * scale * gain_ref[...]

    exchange(math, lax.axis_index("tensor"), source, full, *rest)


def norm_back(grad, value, scale, gain):
    scaled = grad * gain
    inner = jnp.sum(scaled * value, axis=1, keepdims=True)
    return scale * scaled - value * (scale * scale * scale) * (inner / value.shape[1])


def norm_two_back_kernel(source, resid_ref, scale_ref, dy_ref, gain_ref, full, grad_ref, gain_grad_ref, *rest):
    gain_grad_ref[...] = jnp.zeros_like(gain_grad_ref)

    def math(span, total):
        resid, scale = resid_ref[span, :], scale_ref[span, :]
        gain_grad_ref[...] += jnp.sum(total * resid * scale, axis=0, keepdims=True)
        grad = norm_back(total, resid, scale, gain_ref[...]) + dy_ref[span, :].astype(F32)
        grad_ref[span, :] = grad
        return grad

    exchange(math, lax.axis_index("tensor"), source, full, *rest)


def norm_one_back_kernel(source, x_ref, scale_ref, grad_ref, gain_ref, ready, full, ready_full, *rest):
    def math(span, total):
        x = x_ref[span, :].astype(F32)
        return norm_back(total, x, scale_ref[span, :], gain_ref[...]) + grad_ref[span, :]

    exchange(math, lax.axis_index("tensor"), source, full, *rest, ready, ready_full)


def rank_sum_kernel(in_ref, out_ref, held, sends, recvs):
    rank = lax.axis_index("tensor")
    pair_class, half_index = rank % 2, rank // 2
    others = rank + 1 - 2 * pair_class, rank + 2 - 4 * half_index
    mesh_ids = pl.DeviceIdType.MESH
    barrier = pltpu.get_barrier_semaphore()
    for other in others:
        pl.semaphore_signal(barrier, inc=1, device_id={"tensor": other}, device_id_type=mesh_ids)
    pl.semaphore_wait(barrier, 2)
    held[0] = in_ref[...]
    for step, other in enumerate(others):
        copy = pltpu.make_async_remote_copy(
            src_ref=held.at[step], dst_ref=held.at[2 + step], send_sem=sends.at[step], recv_sem=recvs.at[step],
            device_id={"tensor": other}, device_id_type=mesh_ids,
        )
        copy.start()
        copy.wait()
        if step == 0:
            held[1] = held[0] + held[2]
        else:
            out_ref[...] = held[1] + held[3]


def rank_sum(part):
    return pl.pallas_call(
        rank_sum_kernel,
        in_specs=[pl.BlockSpec(memory_space=pltpu.VMEM)],
        out_specs=pl.BlockSpec(memory_space=pltpu.VMEM),
        out_shape=jax.ShapeDtypeStruct(part.shape, F32),
        scratch_shapes=[pltpu.VMEM((4, *part.shape), F32)] + [pltpu.SemaphoreType.DMA((2,))] * 2,
        compiler_params=pltpu.CompilerParams(collective_id=5, has_side_effects=True),
    )(part)


def code_kernel(place_ref, routes_ref, code_ref, half, groups):
    pair_class, half_index = place_ref[0], place_ref[1]
    tokens = routes_ref.shape[1]
    expert = lax.broadcasted_iota(jnp.int32, (EXPERTS, BLK), 0)
    earlier = (
        lax.broadcasted_iota(jnp.int32, (BLK, BLK), 0) < lax.broadcasted_iota(jnp.int32, (BLK, BLK), 1)
    ).astype(F32).astype(BF16)
    carry = jnp.zeros((EXPERTS, 1), F32)
    for block in range(tokens // BLK):
        cols = slice(block * BLK, (block + 1) * BLK)
        routes = routes_ref[:, cols]
        hits = [(routes[i : i + 1] == expert) for i in range(TOP)]
        chosen = sum(hit.astype(F32) for hit in hits)
        before = mm(chosen.astype(BF16), earlier) + carry
        carry = carry + jnp.sum(chosen, axis=1, keepdims=True)
        for i in range(TOP):
            slot = jnp.sum(jnp.where(hits[i], before, 0.0), axis=0, keepdims=True).astype(jnp.int32)
            route = routes[i : i + 1]
            owner = route // 2
            local = slot - half_index * half
            mine = (route - 2 * owner == pair_class) & (local >= 0) & (local < half)
            code_ref[i : i + 1, cols] = jnp.where(mine, owner * half + local, -1)


def local_codes(place, routes_t, half, groups):
    return pl.pallas_call(
        partial(code_kernel, half=half, groups=groups),
        in_specs=[
            pl.BlockSpec(memory_space=pltpu.SMEM),
            pl.BlockSpec(memory_space=pltpu.VMEM),
        ],
        out_specs=pl.BlockSpec(memory_space=pltpu.VMEM),
        out_shape=jax.ShapeDtypeStruct(routes_t.shape, jnp.int32),
        compiler_params=params(),
    )(place, routes_t)


def gates_kernel(h_ref, router_ref, routes_ref, gates_ref):
    expert = lax.broadcasted_iota(jnp.int32, (EXPERTS, h_ref.shape[0]), 0)
    logits = mm(router_ref[...], h_ref[...], NT)
    picked = [
        jnp.sum(jnp.where(routes_ref[i : i + 1] == expert, logits, 0.0), axis=0, keepdims=True)
        for i in range(TOP)
    ]
    top = jnp.maximum(picked[0], picked[1])
    raised = [jnp.exp(value - top) for value in picked]
    total = raised[0] + raised[1]
    for i in range(TOP):
        gates_ref[i : i + 1] = raised[i] / total


def pair_gates(h, router_t, routes_t):
    return pl.pallas_call(
        gates_kernel,
        in_specs=[pl.BlockSpec(memory_space=pltpu.VMEM)] * 3,
        out_specs=pl.BlockSpec(memory_space=pltpu.VMEM),
        out_shape=jax.ShapeDtypeStruct(routes_t.shape, F32),
        compiler_params=params(),
        cost_estimate=cost(2 * routes_t.shape[1] * EXPERTS * 1024 * 8, 4 * MIB),
    )(h, router_t, routes_t)


def dispatch_kernel(code_ref, gates_ref, h_ref, dy_ref, rows_ref, grads_ref, dy_rows_ref, gate_ref):
    count, tokens = rows_ref.shape[0], h_ref.shape[0]
    slot = lax.broadcasted_iota(jnp.int32, (count, tokens), 0) + pl.program_id(0) * count
    hits = [slot == code_ref[i : i + 1, :] for i in range(TOP)]
    take = jnp.where(hits[0] | hits[1], 1.0, 0.0).astype(BF16)
    weighted = jnp.where(hits[0], gates_ref[0:1, :], jnp.where(hits[1], gates_ref[1:2, :], 0.0))
    gate = jnp.sum(weighted, axis=1, keepdims=True)
    rows_ref[...] = mm(take, h_ref[...]).astype(BF16)
    dy_rows = mm(take, dy_ref[...])
    dy_rows_ref[...] = dy_rows.astype(BF16)
    grads_ref[...] = (dy_rows * gate).astype(BF16)
    gate_ref[...] = gate


def dispatch(code, gates, h, dy, slots):
    width = h.shape[1]
    tile = slots // 4
    row_spec = pl.BlockSpec((tile, width), lambda i: (i, 0))
    whole = lambda shape: pl.BlockSpec(shape, lambda i: (0, 0))
    return pl.pallas_call(
        dispatch_kernel,
        grid=(4,),
        in_specs=[whole(code.shape), whole(gates.shape), whole(h.shape), whole(dy.shape)],
        out_specs=[row_spec, row_spec, row_spec, pl.BlockSpec((tile, 1), lambda i: (i, 0))],
        out_shape=[jax.ShapeDtypeStruct((slots, width), BF16)] * 3
        + [jax.ShapeDtypeStruct((slots, 1), F32)],
        compiler_params=params(),
        cost_estimate=cost(8 * slots * SEQ * width, 8 * MIB + 6 * slots * width),
    )(code, gates, h, dy)


def gelu_parts(x):
    inner = 0.7978845608028654 * (x + 0.044715 * (x * x * x))
    bend = jnp.tanh(inner)
    half = 0.5 * (1.0 + bend)
    slope = half + 0.5 * x * (1.0 - bend * bend) * (
        0.7978845608028654 * (1.0 + 3.0 * 0.044715 * (x * x))
    )
    return x * half, slope


def partner_of(index, step):
    found = index
    for bit in (1, 2, 4):
        found = found + ((step // bit) % 2) * (1 - 2 * ((index // bit) % 2)) * bit
    return found


def expert_kernel(
    rows_in, grads_in, gate_in, up_in, down_in, far_gate, far_up,
    ret_out, back_out, own_gate, own_up, own_down, got_gate, got_up, got_down,
    rows, grads, weights, sums, parts, z_send, z_recv, y_send, y_recv, p_send, p_recv, r_send, r_recv, w_send, w_recv, g_send, g_recv, local,
):
    groups, half, width = rows.shape[1:]
    group, rank = lax.axis_index("expert"), lax.axis_index("tensor")
    pair_class, half_index = rank % 2, rank // 2
    across = {"tensor": rank + 1 - 2 * pair_class}
    along = {"tensor": rank + 2 - 4 * half_index}
    mesh_ids = pl.DeviceIdType.MESH
    moved = ((rows_in, rows, ret_out), (grads_in, grads, back_out))

    barrier = pltpu.get_barrier_semaphore()
    for step in range(1, groups):
        pl.semaphore_signal(
            barrier, inc=1, device_id={"expert": partner_of(group, step)}, device_id_type=mesh_ids
        )
    pl.semaphore_signal(barrier, inc=1, device_id=across, device_id_type=mesh_ids)
    pl.semaphore_signal(barrier, inc=1, device_id=along, device_id_type=mesh_ids)
    pl.semaphore_wait(barrier, groups + 1)

    def remote(source, target, send, recv, device):
        return pltpu.make_async_remote_copy(
            src_ref=source, dst_ref=target, send_sem=send, recv_sem=recv,
            device_id=device, device_id_type=mesh_ids,
        )

    def block(ref, number):
        return ref.at[pl.ds(pl.multiple_of(number * half, half), half)]

    def out_of(kind, step):
        source, held, _ = moved[kind]
        other = partner_of(group, step)
        return remote(
            block(source, other), held.at[0, group], z_send.at[kind, step], z_recv.at[kind, step], {"expert": other}
        )

    def forward(kind, step):
        held = moved[kind][1]
        other = partner_of(group, step)
        return remote(held.at[0, other], held.at[1, other], y_send.at[kind, step], y_recv.at[kind, step], along)

    def partial_sum(kind, step):
        held = moved[kind][1]
        other = partner_of(group, step)
        return remote(held.at[1, other], parts.at[kind, other], p_send.at[kind, step], p_recv.at[kind, step], along)

    def result(kind, step):
        other = partner_of(group, step)
        return remote(
            parts.at[kind, other], block(moved[kind][2], group), r_send.at[kind, step], r_recv.at[kind, step], {"expert": other}
        )

    def own_result(kind):
        return pltpu.make_async_copy(parts.at[kind, group], block(moved[kind][2], group), local.at[kind])

    own = [
        pltpu.make_async_copy(block(moved[kind][0], group), moved[kind][1].at[0, group], local.at[kind])
        for kind in range(2)
    ]
    for copy in own:
        copy.start()
    kept = [
        pltpu.make_async_copy(ref.at[pair_class], weights.at[number, 0], local.at[2 + number])
        for number, ref in enumerate((gate_in, up_in, down_in))
    ]
    kept += [
        pltpu.make_async_copy(ref, weights.at[number, 1], local.at[5 + number])
        for number, ref in enumerate((far_gate, far_up))
    ]
    kept.append(remote(down_in.at[1 - pair_class], weights.at[2, 1], w_send.at[0], w_recv.at[0], across))
    for copy in kept:
        copy.start()
    for step in range(1, groups):
        for kind in range(2):
            out_of(kind, step).start()
    def arrive(step):
        for kind in range(2):
            out_of(kind, step).wait()
            forward(kind, step).start()

    near = groups // 2
    for copy in own:
        copy.wait()
    for kind in range(2):
        forward(kind, 0).start()
    for step in range(1, near):
        arrive(step)
    for number in range(3):
        for part in range(2):
            sums[number, part] = jnp.zeros(sums.shape[2:], F32)

    def finish(step):
        other = partner_of(group, step)
        for kind in range(2):
            partial_sum(kind, step).wait()
            held = moved[kind][1]
            parts[kind, other] = (parts[kind, other].astype(F32) + held[0, other].astype(F32)).astype(BF16)

        @pl.when(step == 0)
        def _():
            for kind in range(2):
                own_result(kind).start()

        @pl.when(step > 0)
        def _():
            for kind in range(2):
                result(kind, step).start()

    def body(step, carry):
        @pl.when((step >= near) & (step < groups - 1))
        def _():
            arrive(step + 1)

        @pl.when(step == 0)
        def _():
            for copy in kept:
                copy.wait()

        for kind in range(2):
            forward(kind, step).wait()
        other = partner_of(group, step)
        tile = jnp.concatenate([rows[0, other], rows[1, other]], axis=0)
        grad = jnp.concatenate([grads[0, other], grads[1, other]], axis=0)
        ret = jnp.zeros(tile.shape, F32)
        back = jnp.zeros(tile.shape, F32)
        for part in range(2):
            w_gate, w_up, w_down = weights[0, part], weights[1, part], weights[2, part]
            gate_part = mm(tile, w_gate, NT)
            up_part = mm(tile, w_up, NT)
            grad_hidden = mm(grad, w_down, NT)
            bent, slope = gelu_parts(gate_part)
            hidden = (bent * up_part).astype(BF16)
            grad_gate = (grad_hidden * up_part * slope).astype(BF16)
            grad_up = (grad_hidden * bent).astype(BF16)
            ret = ret + mm(hidden, w_down)
            back = back + mm(grad_gate, w_gate) + mm(grad_up, w_up)
            sums[0, part] += mm(grad_gate, tile, TN)
            sums[1, part] += mm(grad_up, tile, TN)
            sums[2, part] += mm(hidden, grad, TN)
        for kind, value in enumerate((ret, back)):
            held = moved[kind][1]
            held[0, other] = value[:half].astype(BF16)
            held[1, other] = value[half:].astype(BF16)
            partial_sum(kind, step).start()

        @pl.when(step > 0)
        def _():
            finish(step - 1)

        @pl.when(step == near - 1)
        def _():
            arrive(near)

        return carry

    lax.fori_loop(0, groups, body, 0)
    copies = []
    for number, (own_ref, got_ref) in enumerate(((own_gate, got_gate), (own_up, got_up), (own_down, got_down))):
        weights[number, 0] = sums[number, 1].astype(BF16)
        copies.append(remote(weights.at[number, 0], got_ref, g_send.at[number], g_recv.at[number], across))
        copies[-1].start()
        copies.append(pltpu.make_async_copy(sums.at[number, 0], own_ref, local.at[2 + number]))
        copies[-1].start()
    finish(groups - 1)
    for copy in copies:
        copy.wait()
    for kind in range(2):
        own_result(kind).wait()
        for step in range(1, groups):
            result(kind, step).wait()


def run_experts(rows, grads, w_gate, w_up, w_down, far_gate, far_up):
    slots, width = rows.shape
    half = CAP // 2
    groups = slots // half
    units = w_gate.shape[1]
    anywhere = pl.BlockSpec(memory_space=pl.ANY)
    pair = pltpu.SemaphoreType.DMA((2, groups))
    return pl.pallas_call(
        expert_kernel,
        in_specs=[anywhere] * 7,
        out_specs=[anywhere] * 8,
        out_shape=[jax.ShapeDtypeStruct((slots, width), BF16)] * 2
        + [jax.ShapeDtypeStruct((units, width), F32)] * 3
        + [jax.ShapeDtypeStruct((units, width), BF16)] * 3,
        scratch_shapes=[
            pltpu.VMEM((2, groups, half, width), BF16),
            pltpu.VMEM((2, groups, half, width), BF16),
            pltpu.VMEM((3, 2, units, width), BF16),
            pltpu.VMEM((3, 2, units, width), F32),
            pltpu.VMEM((2, groups, half, width), BF16),
        ]
        + [pair] * 8
        + [pltpu.SemaphoreType.DMA((1,))] * 2
        + [pltpu.SemaphoreType.DMA((3,))] * 2
        + [pltpu.SemaphoreType.DMA((7,))],
        compiler_params=pltpu.CompilerParams(
            vmem_limit_bytes=60 * MIB, collective_id=1, has_side_effects=True
        ),
        cost_estimate=cost(72 * slots * units * width, 16 * slots * width + 30 * units * width),
    )(rows, grads, w_gate, w_up, w_down, far_gate, far_up)


def pair_grads_kernel(code_ref, gates_ref, routes_ref, dy_rows_ref, ret_ref, gate_ref, logit_ref, scaled_ref):
    slots = ret_ref.shape[0]
    tokens = code_ref.shape[1]
    found = [jnp.zeros((1, tokens), F32) for _ in range(TOP)]
    tile = 320
    for start in range(0, slots, tile):
        span = slice(start, start + tile)
        ret = ret_ref[span, :].astype(F32)
        slot_grad = jnp.sum(dy_rows_ref[span, :].astype(F32) * ret, axis=1, keepdims=True)
        scaled_ref[span, :] = (ret * gate_ref[span, :]).astype(BF16)
        slot = lax.broadcasted_iota(jnp.int32, (tile, tokens), 0) + start
        for i in range(TOP):
            found[i] = found[i] + jnp.sum(
                jnp.where(slot == code_ref[i : i + 1, :], slot_grad, 0.0), axis=0, keepdims=True
            )
    mean = gates_ref[0:1] * found[0] + gates_ref[1:2] * found[1]
    expert = lax.broadcasted_iota(jnp.int32, (EXPERTS, tokens), 0)
    logit_ref[...] = sum(
        jnp.where(routes_ref[i : i + 1] == expert, gates_ref[i : i + 1] * (found[i] - mean), 0.0)
        for i in range(TOP)
    )


def pair_grads(code, gates, routes_t, dy_rows, ret, gate_rows):
    return pl.pallas_call(
        pair_grads_kernel,
        in_specs=[pl.BlockSpec(memory_space=pltpu.VMEM)] * 6,
        out_specs=[pl.BlockSpec(memory_space=pltpu.VMEM)] * 2,
        out_shape=[
            jax.ShapeDtypeStruct((EXPERTS, code.shape[1]), F32),
            jax.ShapeDtypeStruct(ret.shape, BF16),
        ],
        compiler_params=params(),
        cost_estimate=cost(ret.shape[0] * code.shape[1] * 16, 6 * ret.size),
    )(code, gates, routes_t, dy_rows, ret, gate_rows)


def spread_kernel(code_ref, rows_ref, *refs):
    out_ref = refs[-1]
    tile = out_ref.shape[0]
    slot = lax.broadcasted_iota(jnp.int32, (tile, rows_ref.shape[0]), 1)
    code = code_ref[...]
    place = jnp.where((slot == code[:, 0:1]) | (slot == code[:, 1:2]), 1.0, 0.0).astype(BF16)
    value = mm(place, rows_ref[...])
    if len(refs) == 3:
        logit, router = refs[0][...], refs[1][...]
        coarse = logit.astype(BF16)
        fine = (logit - coarse.astype(F32)).astype(BF16)
        value = value + mm(coarse, router, NT) + mm(fine, router, NT)
    out_ref[...] = value.astype(BF16)


def spread(code_cols, rows, logit=None, router=None):
    tokens, width = code_cols.shape[0], rows.shape[1]
    tile = 512
    specs = [
        pl.BlockSpec((tile, TOP), lambda i: (i, 0)),
        pl.BlockSpec(rows.shape, lambda i: (0, 0)),
    ]
    operands = [code_cols, rows]
    if logit is not None:
        specs += [
            pl.BlockSpec((tile, EXPERTS), lambda i: (i, 0)),
            pl.BlockSpec(router.shape, lambda i: (0, 0)),
        ]
        operands += [logit, router]
    return pl.pallas_call(
        spread_kernel,
        grid=(tokens // tile,),
        in_specs=specs,
        out_specs=pl.BlockSpec((tile, width), lambda i: (i, 0)),
        out_shape=jax.ShapeDtypeStruct((tokens, width), BF16),
        compiler_params=params(),
        cost_estimate=cost(2 * tokens * width * rows.shape[0], 2 * rows.size + 2 * tokens * width),
    )(*operands)


def turn_kernel(in_ref, out_ref):
    out_ref[...] = in_ref[...].astype(F32).T.astype(out_ref.dtype)


def turn(rows, kind):
    tokens, width = rows.shape
    tile = 512
    return pl.pallas_call(
        turn_kernel,
        grid=(tokens // tile,),
        in_specs=[pl.BlockSpec((tile, width), lambda i: (i, 0))],
        out_specs=pl.BlockSpec((width, tile), lambda i: (0, i)),
        out_shape=jax.ShapeDtypeStruct((width, tokens), kind),
        compiler_params=params(),
        cost_estimate=cost(0, 6 * rows.size),
    )(rows)


def on_device(
    layer_input, gain_one, attn_in, rel_bias, attn_out, gain_two, router,
    expert_gate, expert_up, expert_down, routes, piece_starts, grad_out,
):
    width, tokens = layer_input.shape
    ranks = lax.axis_size("tensor")
    groups = lax.axis_size("expert")
    rank = lax.axis_index("tensor")
    pair_class, half_index = rank % 2, rank // 2
    half = CAP // 2

    def trade(weights):
        other = lax.dynamic_index_in_dim(weights, 1 - pair_class, 0, keepdims=False)
        return lax.ppermute(other, "tensor", [(r, r ^ 1) for r in range(ranks)])

    traded = trade(expert_gate), trade(expert_up)
    gain_col = gain_one[:, None]
    w_in = attn_in.reshape(-1, width)
    qkv, scale_one = project(layer_input, gain_col, w_in)
    tiles = bias_tiles(rel_bias)
    position = jnp.arange(SEQ, dtype=jnp.int32)[None, None, :]
    starts = piece_starts[:, :, None]
    inside = (position >= starts) & (position < starts + PIECE)
    last = jnp.max(jnp.where(inside, starts + (PIECE - 1), -1), axis=1)
    limits = jnp.maximum(last, position[0])[:, None, :]

    routes_t = routes.T
    place = jnp.stack([pair_class, half_index]).astype(jnp.int32)
    code = local_codes(place, routes_t, half, groups)
    code_cols = code.T
    dy = grad_out.T

    share = tokens // ranks

    def own(rows, axis=0):
        return lax.dynamic_slice_in_dim(rows, rank * share, share, axis)

    own_x = own(layer_input, 1).T
    own_scale = own(scale_one, 1).T
    mixed, lse, sent = attend(qkv, tiles, limits, attn_out)
    sent, *traded = lax.optimization_barrier((sent, *traded))
    h2, resid, scale_two = exchange_call(
        norm_two_kernel, 2, sent, [own_x, gain_two[None]], [((share, width), F32), ((share, 1), F32)]
    )
    gates = pair_gates(h2, router.T, routes_t)
    slots = groups * half
    rows, row_grads, dy_rows, gate_rows = dispatch(code, gates, h2, dy, slots)
    ret, back, *weight_grads = run_experts(
        rows, row_grads, expert_gate, expert_up, expert_down, *traded
    )
    grad_logit, scaled = pair_grads(code, gates, routes_t, dy_rows, ret, gate_rows)
    partial_h2 = spread(code_cols, back, grad_logit.T, router)
    grad_router = mm(grad_logit.astype(BF16), h2)
    grad_attn, grad_resid, grad_gain_two = exchange_call(
        norm_two_back_kernel, 3, partial_h2, [resid, scale_two, own(dy), gain_two[None]],
        [((share, width), F32), ((1, width), F32)],
    )

    scaled, grad_attn = lax.optimization_barrier((scaled, grad_attn))
    partial_y = spread(code_cols, scaled)
    y_part = lax.psum_scatter(partial_y, "tensor", scatter_dimension=0, tiled=True)
    partial_y, grad_attn = lax.optimization_barrier((partial_y, grad_attn))
    dq, dk, dv, near, far, grad_gate, grad_up, grad_down = attend_back(
        place, qkv, tiles, limits, attn_out, grad_attn, lse, weight_grads[:3], weight_grads[3:]
    )
    grad_attn_out = mm(mixed, grad_attn)
    dq, y_part = lax.optimization_barrier((dq, y_part))
    grad_in, sent, grad_gain_one = project_back(layer_input, gain_col, scale_one, w_in, (dq, dk, dv))
    grad_rel_bias = bias_fold(near, far)[:, :, 0].T

    heads = grad_rel_bias.shape[1]
    small = jnp.concatenate(
        [
            grad_gain_one.T,
            grad_gain_two,
            grad_router,
            jnp.pad(grad_rel_bias.reshape(1, -1), ((0, 0), (0, width - grad_rel_bias.size))),
            jnp.zeros((5, width), F32),
        ]
    )
    sum_in, sum_out, small = lax.psum(
        (grad_in.astype(BF16), grad_attn_out.astype(BF16), small.astype(BF16)), "expert"
    )
    y_own = (resid + y_part.astype(F32)).astype(BF16)
    grad_rows, y_full = exchange_call(
        norm_one_back_kernel, 4, sent, [own_x, own_scale, grad_resid, gain_one[None], y_own],
        [((ranks, share, width), BF16)],
    )
    grad_input = turn(grad_rows, F32)
    layer_output = turn(y_full.reshape(tokens, width), BF16)
    small, layer_output = lax.optimization_barrier((small.astype(F32), layer_output))
    over_ranks = rank_sum(small)
    return (
        layer_output,
        grad_input,
        over_ranks[0],
        sum_in.astype(F32).reshape(attn_in.shape),
        small[2 + EXPERTS, : BUCKETS * heads].reshape(BUCKETS, heads),
        sum_out.astype(F32),
        over_ranks[1],
        over_ranks[2 : 2 + EXPERTS].T,
        grad_gate,
        grad_up,
        grad_down,
    )


def allowed_pairs(seq_starts):
    position = jnp.arange(SEQ, dtype=jnp.int32)
    inside = (position[:, None] >= seq_starts[None, :]) & (
        position[:, None] < seq_starts[None, :] + PIECE
    )
    numbers = jnp.arange(seq_starts.shape[0], dtype=jnp.int32) + 1
    piece_label = jnp.sum(inside.astype(jnp.int32) * numbers[None, :], axis=1)
    causal = position[None, :] <= position[:, None]
    shared = (piece_label[:, None] == piece_label[None, :]) & (piece_label[:, None] > 0)
    return causal | shared


def slot_table(routes):
    flat_routes = routes.reshape(-1)
    onehot = (flat_routes[:, None] == jnp.arange(EXPERTS, dtype=jnp.int32)[None, :]).astype(
        jnp.int32
    )
    blocks = onehot.reshape(-1, 128, EXPERTS).astype(F32)
    earlier = jnp.tril(jnp.ones((128, 128), F32), -1)
    inside = jnp.einsum("ij,bje->bie", earlier, blocks)
    count = blocks.shape[0]
    carried = jnp.einsum("ab,be->ae", jnp.tril(jnp.ones((count, count), F32), -1), jnp.sum(blocks, axis=1), precision=HIGH)
    before = (inside + carried[:, None, :]).astype(jnp.int32).reshape(onehot.shape)
    slot_number = jnp.sum(before * onehot, axis=1)
    kept_pairs = slot_number < CAP
    slot_index = jnp.where(kept_pairs, flat_routes * CAP + slot_number, EXPERTS * CAP)
    return (slot_index.reshape(routes.shape), kept_pairs.reshape(routes.shape))


def bucket_onehot():
    offsets = jnp.arange(2 * SEQ - 1, dtype=jnp.int32) - (SEQ - 1)
    return (bucket_of(offsets)[:, None] == jnp.arange(BUCKETS, dtype=jnp.int32)[None, :]).astype(
        jnp.float32
    )


def expand_line(line):
    head_count = line.shape[0]
    padded = jnp.concatenate([line, jnp.zeros((head_count, 1), line.dtype)], axis=1)
    tiled = jnp.tile(padded, (1, SEQ))[:, : SEQ * (2 * SEQ - 1)].reshape(
        head_count, SEQ, 2 * SEQ - 1
    )
    return tiled[:, :, SEQ - 1 :]


def fold_line(full_grid):
    head_count = full_grid.shape[0]
    padded = jnp.pad(full_grid, ((0, 0), (0, 0), (SEQ - 1, 0))).reshape(
        head_count, SEQ * (2 * SEQ - 1)
    )
    padded = jnp.pad(padded, ((0, 0), (0, SEQ))).reshape(head_count, SEQ, 2 * SEQ)
    return jnp.sum(padded, axis=1)[:, : 2 * SEQ - 1]


def reduce_heads(tensor_value):
    return lax.psum(tensor_value, "tensor")


def spread_slots(tensor_value):
    return lax.all_gather(tensor_value, "tensor", axis=2, tiled=True)


def owner_exchange(tensor_value):
    return lax.all_to_all(tensor_value, "expert", split_axis=0, concat_axis=0, tiled=True)


def expert_sums(tensor_value):
    return lax.psum_scatter(tensor_value, "tensor", scatter_dimension=2, tiled=True)


def norm_forward(resid, gain, model_width):
    scale = lax.rsqrt(jnp.sum(resid * resid, axis=1) / model_width + EPS)[:, None]
    return (scale, (resid * scale * gain).astype(jnp.bfloat16))


def norm_backward(resid, scale, gain, grad_normed, model_width):
    grad_gain = jnp.sum(grad_normed * resid * scale, axis=0)
    scaled = grad_normed * gain
    inner = jnp.sum(scaled * resid, axis=1)[:, None]
    return (grad_gain, scale * scaled - resid * scale**3 * inner / model_width)


def attend_scores(bias_full, queries, key_rows, seq_starts):
    scores = (
        jnp.einsum("qhe,khe->hqk", queries, key_rows, preferred_element_type=jnp.float32) * 0.125
        + bias_full
    )
    return jnp.where(allowed_pairs(seq_starts)[None], scores, NEG)


def attend_forward(bias_full, inputs):
    queries, key_rows, value_rows, seq_starts = inputs
    scores = attend_scores(bias_full, queries, key_rows, seq_starts)
    row_max = jnp.max(scores, axis=2, keepdims=True)
    exponent = jnp.exp(scores - row_max)
    row_sum_exp = jnp.sum(exponent, axis=2, keepdims=True)
    weights = (exponent / row_sum_exp).astype(jnp.bfloat16)
    mixed_heads = jnp.einsum(
        "hqk,khe->qhe", weights, value_rows, preferred_element_type=jnp.float32
    )
    return (mixed_heads.astype(jnp.bfloat16), (row_max + jnp.log(row_sum_exp))[:, :, 0])


def attend_backward(bias_full, running, inputs):
    queries, key_rows, value_rows, grad_heads, seq_starts, log_total = inputs
    scores = attend_scores(bias_full, queries, key_rows, seq_starts)
    probabilities = jnp.exp(scores - log_total[:, :, None])
    grad_probs = jnp.einsum(
        "qhe,khe->hqk", grad_heads, value_rows, preferred_element_type=jnp.float32
    )
    inner = jnp.sum(probabilities * grad_probs, axis=2, keepdims=True)
    grad_scores = (probabilities * (grad_probs - inner)).astype(jnp.bfloat16)
    grad_values = jnp.einsum(
        "hqk,qhe->khe",
        probabilities.astype(jnp.bfloat16),
        grad_heads,
        preferred_element_type=jnp.float32,
    )
    grad_queries = (
        jnp.einsum("hqk,khe->qhe", grad_scores, key_rows, preferred_element_type=jnp.float32)
        * 0.125
    )
    grad_keys = (
        jnp.einsum("hqk,qhe->khe", grad_scores, queries, preferred_element_type=jnp.float32) * 0.125
    )
    return (
        running + grad_scores.astype(jnp.float32),
        jnp.stack([grad_queries, grad_keys, grad_values]),
    )


def gelu_product(left, right):
    return jax.nn.gelu(left, approximate=True) * right


def expert_forward(received, weight_gate, weight_up, weight_down):
    gate_part = jnp.einsum(
        "secd,efd->secf", received, weight_gate, preferred_element_type=jnp.float32
    )
    up_part = jnp.einsum("secd,efd->secf", received, weight_up, preferred_element_type=jnp.float32)
    hidden = gelu_product(gate_part, up_part).astype(jnp.bfloat16)
    partial_out = jnp.einsum(
        "secf,efd->secd", hidden, weight_down, preferred_element_type=jnp.float32
    )
    return (gate_part, up_part, hidden, partial_out)


def expert_backward(
    received, gate_part, up_part, hidden, grad_rows_out, weight_gate, weight_up, weight_down
):
    grad_hidden = jnp.einsum(
        "secd,efd->secf", grad_rows_out, weight_down, preferred_element_type=jnp.float32
    )
    product_value, pullback = jax.vjp(gelu_product, gate_part, up_part)
    grad_gate_part, grad_up_part = pullback(grad_hidden)
    grad_gate_part = grad_gate_part.astype(jnp.bfloat16)
    grad_up_part = grad_up_part.astype(jnp.bfloat16)
    grad_down = jnp.einsum(
        "secf,secd->efd", hidden, grad_rows_out, preferred_element_type=jnp.float32
    )
    grad_gate_w = jnp.einsum(
        "secf,secd->efd", grad_gate_part, received, preferred_element_type=jnp.float32
    )
    grad_up_w = jnp.einsum(
        "secf,secd->efd", grad_up_part, received, preferred_element_type=jnp.float32
    )
    grad_rows_in = jnp.einsum(
        "secf,efd->secd", grad_gate_part, weight_gate, preferred_element_type=jnp.float32
    )
    grad_rows_in = grad_rows_in + jnp.einsum(
        "secf,efd->secd", grad_up_part, weight_up, preferred_element_type=jnp.float32
    )
    return (grad_gate_w, grad_up_w, grad_down, grad_rows_in)


def on_device_general(
    layer_input,
    gain_one,
    attn_in,
    rel_bias,
    attn_out,
    gain_two,
    router,
    expert_gate,
    expert_up,
    expert_down,
    routes,
    piece_starts,
    grad_out,
):
    tok_count = layer_input.shape[1]
    model_width = layer_input.shape[0]
    heads_here = rel_bias.shape[1]
    head_width = attn_in.shape[1] // heads_here
    seqs_here = piece_starts.shape[0]
    local_experts = expert_gate.shape[0]
    part_rows = CAP // lax.axis_size("tensor")
    share_start = lax.axis_index("tensor") * part_rows
    tokens = layer_input.T.astype(jnp.float32)
    scale_one, normed = norm_forward(tokens, gain_one, model_width)
    project = jnp.einsum("td,chd->cth", normed, attn_in, preferred_element_type=jnp.float32).astype(
        jnp.bfloat16
    )
    by_seq = project.reshape(3, seqs_here, SEQ, heads_here, head_width)
    onehot_line = bucket_onehot()
    bias_full = expand_line(jnp.dot(onehot_line, rel_bias, precision=HIGH).T)
    mixed_heads, log_total = lax.map(
        partial(attend_forward, bias_full), (by_seq[0], by_seq[1], by_seq[2], piece_starts)
    )
    mixed_heads = mixed_heads.reshape(tok_count, heads_here * head_width)
    resid = tokens + reduce_heads(
        jnp.dot(mixed_heads, attn_out, preferred_element_type=jnp.float32)
    )
    scale_two, normed_two = norm_forward(resid, gain_two, model_width)
    logits = jnp.dot(normed_two, router, preferred_element_type=jnp.float32)
    chosen = (routes[:, :, None] == jnp.arange(EXPERTS, dtype=jnp.int32)[None, None, :]).astype(
        jnp.float32
    )
    picked = jnp.sum(chosen * logits[:, None, :], axis=2)
    gate_weights = jax.nn.softmax(picked, axis=1)
    slot_index, kept_pairs = slot_table(routes)
    keep_float = kept_pairs.astype(jnp.float32)
    mix_weight = gate_weights * keep_float
    safe_index = jnp.minimum(slot_index, EXPERTS * CAP - 1)
    token_rows = jnp.repeat(normed_two, TOP, axis=0)
    buffer = (
        jnp.zeros((EXPERTS * CAP + 1, model_width), jnp.bfloat16)
        .at[slot_index.reshape(-1)]
        .set(token_rows)
    )
    buffer = buffer[: EXPERTS * CAP].reshape(-1, local_experts, CAP, model_width)
    received = lax.all_to_all(buffer, "expert", split_axis=0, concat_axis=0, tiled=True)
    gate_part, up_part, hidden, partial_out = expert_forward(
        received, expert_gate, expert_up, expert_down
    )
    returned = spread_slots(owner_exchange(expert_sums(partial_out).astype(jnp.bfloat16)))
    flat_ret = returned.reshape(EXPERTS * CAP, model_width)
    fetched = flat_ret[safe_index].astype(jnp.float32)
    output = resid + jnp.sum(mix_weight[:, :, None] * fetched, axis=1)
    grad_y = grad_out.T.astype(jnp.float32)
    grad_gates = jnp.sum(grad_y[:, None, :] * fetched, axis=2) * keep_float
    grad_picked = gate_weights * (
        grad_gates - jnp.sum(gate_weights * grad_gates, axis=1, keepdims=True)
    )
    grad_logits = jnp.sum(chosen * grad_picked[:, :, None], axis=1)
    grad_router = jnp.dot(normed_two.astype(jnp.float32).T, grad_logits, precision=HIGH)
    grad_normed_two = jnp.dot(grad_logits, router.astype(jnp.float32).T, precision=HIGH)
    slot_grads = (mix_weight[:, :, None] * grad_y[:, None, :]).astype(jnp.bfloat16)
    grad_ret = (
        jnp.zeros((EXPERTS * CAP + 1, model_width), jnp.bfloat16)
        .at[slot_index.reshape(-1)]
        .set(slot_grads.reshape(-1, model_width))
    )
    grad_ret = grad_ret[: EXPERTS * CAP].reshape(-1, local_experts, CAP, model_width)
    grad_share = lax.dynamic_slice_in_dim(grad_ret, share_start, part_rows, 2)
    grad_rows_out = spread_slots(owner_exchange(grad_share))
    grad_expert_gate, grad_expert_up, grad_expert_down, grad_rows_in = expert_backward(
        received, gate_part, up_part, hidden, grad_rows_out, expert_gate, expert_up, expert_down
    )
    grad_back = spread_slots(owner_exchange(expert_sums(grad_rows_in).astype(jnp.bfloat16)))
    flat_back = grad_back.reshape(EXPERTS * CAP, model_width).astype(jnp.float32)
    grad_normed_two = grad_normed_two + jnp.sum(
        flat_back[safe_index] * keep_float[:, :, None], axis=1
    )
    grad_gain_two, grad_resid = norm_backward(
        resid, scale_two, gain_two, grad_normed_two, model_width
    )
    grad_resid = grad_resid + grad_y
    grad_attn = grad_resid.astype(jnp.bfloat16)
    grad_attn_out = jnp.einsum(
        "th,td->hd", mixed_heads, grad_attn, preferred_element_type=jnp.float32
    )
    grad_mixed = jnp.einsum(
        "td,hd->th", grad_attn, attn_out, preferred_element_type=jnp.float32
    ).astype(jnp.bfloat16)
    grad_by_seq = grad_mixed.reshape(seqs_here, SEQ, heads_here, head_width)
    bias_grad_full, grad_project = lax.scan(
        partial(attend_backward, bias_full),
        jnp.zeros_like(bias_full),
        (by_seq[0], by_seq[1], by_seq[2], grad_by_seq, piece_starts, log_total),
    )
    grad_project = (
        jnp.moveaxis(grad_project, 1, 0)
        .reshape(3, tok_count, heads_here * head_width)
        .astype(jnp.bfloat16)
    )
    grad_attn_in = jnp.einsum(
        "cth,td->chd", grad_project, normed, preferred_element_type=jnp.float32
    )
    grad_normed = reduce_heads(
        jnp.einsum("cth,chd->td", grad_project, attn_in, preferred_element_type=jnp.float32)
    )
    grad_gain_one, grad_tokens = norm_backward(
        tokens, scale_one, gain_one, grad_normed, model_width
    )
    grad_tokens = grad_tokens + grad_resid
    grad_rel_bias = jnp.dot(onehot_line.T, fold_line(bias_grad_full).T, precision=HIGH)
    shared = (
        lax.psum(grad_gain_one.astype(jnp.bfloat16), "expert").astype(jnp.float32),
        lax.psum(grad_attn_in.astype(jnp.bfloat16), "expert").astype(jnp.float32),
        lax.psum(grad_rel_bias.astype(jnp.bfloat16), "expert").astype(jnp.float32),
        lax.psum(grad_attn_out.astype(jnp.bfloat16), "expert").astype(jnp.float32),
        lax.psum(grad_gain_two.astype(jnp.bfloat16), "expert").astype(jnp.float32),
        lax.psum(grad_router.astype(jnp.bfloat16), "expert").astype(jnp.float32),
    )
    return (
        output.astype(jnp.bfloat16).T,
        grad_tokens.T,
        shared[0],
        shared[1],
        shared[2],
        shared[3],
        shared[4],
        shared[5],
        grad_expert_gate,
        grad_expert_up,
        grad_expert_down,
    )


def solution(mesh):
    placed = (
        P(None, "expert"),
        P(),
        P(None, "tensor", None),
        P(None, "tensor"),
        P("tensor", None),
        P(),
        P(),
        P("expert", "tensor", None),
        P("expert", "tensor", None),
        P("expert", "tensor", None),
        P("expert", None),
        P("expert", None),
        P(None, "expert"),
    )
    paired = mesh.shape["tensor"] == 4 and mesh.shape["expert"] * 2 == EXPERTS
    return jax.shard_map(
        on_device if paired else on_device_general,
        mesh=mesh,
        in_specs=placed,
        out_specs=(
            P(None, "expert"),
            P(None, "expert"),
            P(),
            P(None, "tensor", None),
            P(None, "tensor"),
            P("tensor", None),
            P(),
            P(),
            P("expert", "tensor", None),
            P("expert", "tensor", None),
            P("expert", "tensor", None),
        ),
        check_vma=False,
    )
```

```python
from functools import partial

import jax
import jax.numpy as jnp
from jax import lax
from jax.experimental import pallas as pl
from jax.experimental.pallas import tpu as pltpu
from jax.sharding import PartitionSpec as P

EXPERTS = 16
BUCKETS = 32
TOP = 2
PIECE = 256
SEQ = 1024
CAP = 320
BLK = 256


EPS = 1e-06
NEG = -1e30
THRESHOLDS = (12, 16, 23, 32, 46, 64, 91)
HIGH = lax.Precision.HIGHEST
F32 = jnp.float32
BF16 = jnp.bfloat16
NN = (((1,), (0,)), ((), ()))
NT = (((1,), (1,)), ((), ()))
TN = (((0,), (0,)), ((), ()))
MIB = 1 << 20


def mm(left, right, dims=NN):
    return lax.dot_general(left, right, dims, preferred_element_type=F32)


def params(limit=56):
    return pltpu.CompilerParams(vmem_limit_bytes=limit * MIB)


def cost(flops, bytes_accessed, transcendentals=0):
    return pl.CostEstimate(
        flops=int(flops), bytes_accessed=int(bytes_accessed), transcendentals=int(transcendentals)
    )


def bucket_of(offset):
    magnitude = jnp.abs(offset)
    beyond = sum(((magnitude >= threshold).astype(jnp.int32) for threshold in THRESHOLDS))
    lower_part = jnp.where(magnitude < 8, magnitude, 8 + beyond)
    return lower_part + 16 * (offset > 0).astype(jnp.int32)


def project_kernel(x_ref, gain_ref, w_ref, out_ref, scale_ref):
    x = x_ref[...].astype(F32)
    scale = lax.rsqrt(jnp.sum(x * x, axis=0, keepdims=True) / x.shape[0] + EPS)
    normed = (x * scale * gain_ref[...]).astype(BF16)
    out_ref[...] = mm(w_ref[...], normed).astype(BF16)
    scale_ref[...] = scale


def project(x, gain, weights):
    width, tokens = x.shape
    rows = weights.shape[0]
    tile = 512
    return pl.pallas_call(
        project_kernel,
        grid=(tokens // tile,),
        in_specs=[
            pl.BlockSpec((width, tile), lambda i: (0, i)),
            pl.BlockSpec((width, 1), lambda i: (0, 0)),
            pl.BlockSpec((rows, width), lambda i: (0, 0)),
        ],
        out_specs=[
            pl.BlockSpec((rows, tile), lambda i: (0, i)),
            pl.BlockSpec((1, tile), lambda i: (0, i)),
        ],
        out_shape=[
            jax.ShapeDtypeStruct((rows, tokens), BF16),
            jax.ShapeDtypeStruct((1, tokens), F32),
        ],
        compiler_params=params(),
        cost_estimate=cost(2 * width * tokens * rows, 2 * width * tokens * 2),
    )(x, gain, weights)


def line_offsets(number):
    column = lax.broadcasted_iota(jnp.int32, (8, BLK), 1)
    return (number - 1) * BLK - column


def bias_tiles_kernel(table_ref, tiles_ref):
    row = lax.broadcasted_iota(jnp.int32, (BLK, BLK), 0)
    column = lax.broadcasted_iota(jnp.int32, (BLK, BLK), 1)
    buckets = [bucket_of(line_offsets(number)) for number in range(4)]
    for head in range(tiles_ref.shape[0]):
        far = table_ref[15, head]
        rolled = []
        for number, bucket in enumerate(buckets):
            value = jnp.zeros((8, BLK), F32)
            for index in range(BUCKETS):
                value = jnp.where(bucket == index, table_ref[index, head] - far, value)
            whole = jnp.broadcast_to(value[0:1], (BLK, BLK))
            rolled.append(pltpu.roll(whole, 0, 1, stride=1, stride_axis=0))
        for number in range(3):
            tiles_ref[head, number] = jnp.where(column >= row, rolled[number], rolled[number + 1])


def bias_tiles(table):
    heads = table.shape[1]
    return pl.pallas_call(
        bias_tiles_kernel,
        in_specs=[pl.BlockSpec(memory_space=pltpu.SMEM)],
        out_specs=pl.BlockSpec(memory_space=pltpu.VMEM),
        out_shape=jax.ShapeDtypeStruct((heads, 3, BLK, BLK), F32),
        compiler_params=params(),
        cost_estimate=cost(heads * 3 * BLK * BLK * 60, heads * 3 * BLK * BLK * 4),
    )(table)


def bias_fold(near_ref, far_ref):
    heads = near_ref.shape[0] // 2
    columns = []
    row = lax.broadcasted_iota(jnp.int32, (BLK, BLK), 0)
    column = lax.broadcasted_iota(jnp.int32, (BLK, BLK), 1)
    flip = jnp.where(row + column == BLK - 1, 1.0, 0.0).astype(BF16)
    apart = jnp.where(column == BLK - 1, 0, column + 1)
    ahead = apart <= row
    number_at = lax.broadcasted_iota(jnp.int32, (BUCKETS, BLK), 0)
    for head in range(heads):
        lines = [jnp.zeros((1, BLK), F32) for _ in range(4)]
        for number in range(3):
            grads = near_ref[head, number] + near_ref[heads + head, number]
            coarse = grads.astype(BF16)
            fine = (grads - coarse.astype(F32)).astype(BF16)
            flipped = mm(flip, coarse) + mm(flip, fine)
            rolled = pltpu.roll(flipped, 0, 1, stride=1, stride_axis=0)
            lines[number] += jnp.sum(jnp.where(ahead, rolled, 0.0), axis=0, keepdims=True)
            lines[number + 1] += jnp.sum(jnp.where(ahead, 0.0, rolled), axis=0, keepdims=True)
        total = jnp.zeros((BUCKETS, 1), F32)
        for number, line in enumerate(lines):
            bucket = bucket_of((number - 1) * BLK - apart[:1])
            total += jnp.sum(jnp.where(bucket == number_at, line, 0.0), axis=1, keepdims=True)
        distant = jnp.sum(far_ref[head] + far_ref[heads + head], axis=0, keepdims=True)
        distant = jnp.sum(distant, axis=1, keepdims=True)
        total += jnp.where(number_at[:, :1] == 15, distant, 0.0)
        columns.append(total)
    return columns


def key_count(query_block):
    return 2 * BLK if query_block < 2 else 4 * BLK


def block_scores(keys, queries, tiles_ref, limit, block):
    count = key_count(block)
    parts = []
    whole = mm(keys[:, :count], queries, TN)
    for key_block in range(count // BLK):
        part = whole[key_block * BLK : (key_block + 1) * BLK]
        shift = key_block - block
        if -1 <= shift <= 1:
            part = part + tiles_ref[0, shift + 1]
        if shift >= 0:
            key_at = lax.broadcasted_iota(jnp.int32, (BLK, BLK), 0) + key_block * BLK
            part = jnp.where(key_at <= limit, part, NEG)
        parts.append(part)
    return jnp.concatenate(parts, axis=0)


def attend_kernel(q_ref, k_ref, v_ref, tiles_ref, limit_ref, w_ref, out_ref, lse_ref, sent_ref, held):
    head = pl.program_id(1)
    width = q_ref.shape[0]
    queries = q_ref[...] * BF16(0.125)
    keys, values = k_ref[...], v_ref[...]
    for block in range(SEQ // BLK):
        cols = slice(block * BLK, (block + 1) * BLK)
        scores = block_scores(keys, queries[:, cols], tiles_ref, limit_ref[0, :, cols], block)
        top = jnp.max(scores, axis=0, keepdims=True)
        exponent = jnp.exp(scores - top)
        total = jnp.sum(exponent, axis=0, keepdims=True)
        mixed = mm(values[:, : key_count(block)], exponent.astype(BF16)) / total
        mixed = mixed.astype(BF16)
        out_ref[:, cols] = mixed
        held[pl.ds(pl.multiple_of(head * width, width), width), cols] = mixed
        lse_ref[0, :, cols] = top + jnp.log(total)

    @pl.when(head == pl.num_programs(1) - 1)
    def _():
        sent_ref[...] = mm(held[...], w_ref[...], TN).astype(BF16)


def attend(qkv, tiles, limits, attn_out):
    heads = tiles.shape[0]
    seqs = limits.shape[0]
    width = qkv.shape[0] // (3 * heads)
    model_width = attn_out.shape[1]
    return pl.pallas_call(
        attend_kernel,
        grid=(seqs, heads),
        in_specs=[
            pl.BlockSpec((width, SEQ), lambda s, h: (h, s)),
            pl.BlockSpec((width, SEQ), lambda s, h: (heads + h, s)),
            pl.BlockSpec((width, SEQ), lambda s, h: (2 * heads + h, s)),
            pl.BlockSpec((1, 3, BLK, BLK), lambda s, h: (h, 0, 0, 0)),
            pl.BlockSpec((1, 1, SEQ), lambda s, h: (s, 0, 0)),
            pl.BlockSpec((heads * width, model_width), lambda s, h: (0, 0)),
        ],
        out_specs=[
            pl.BlockSpec((width, SEQ), lambda s, h: (h, s)),
            pl.BlockSpec((1, 1, SEQ), lambda s, h: (s * heads + h, 0, 0)),
            pl.BlockSpec((SEQ, model_width), lambda s, h: (s, 0)),
        ],
        out_shape=[
            jax.ShapeDtypeStruct((heads * width, seqs * SEQ), BF16),
            jax.ShapeDtypeStruct((seqs * heads, 1, SEQ), F32),
            jax.ShapeDtypeStruct((seqs * SEQ, model_width), BF16),
        ],
        scratch_shapes=[pltpu.VMEM((heads * width, SEQ), BF16)],
        compiler_params=params(),
        cost_estimate=cost(seqs * heads * SEQ * SEQ * 512, seqs * heads * SEQ * 2048, seqs * heads * SEQ * SEQ),
    )(qkv, qkv, qkv, tiles, limits, attn_out)


def attend_back_kernel(
    q_ref, k_ref, v_ref, tiles_ref, limit_ref, w_ref, grad_ref, lse_ref, part_ref, resid_ref,
    dq_ref, dk_ref, dv_ref, near_ref, far_ref, y_ref,
    held, parts, turn_across, turn_along, from_across, from_along, sends, recvs, loads,
):
    rank = lax.axis_index("tensor")
    pair_class, half_index = rank % 2, rank // 2
    across, along, corner = rank + 1 - 2 * pair_class, rank + 2 - 4 * half_index, 3 - rank
    step = pl.program_id(0) * pl.num_programs(1) + pl.program_id(1)
    mesh_ids = pl.DeviceIdType.MESH
    middle = parts.shape[2] // 2
    low, high = slice(0, middle), slice(middle, 2 * middle)

    def remote(number, origin, target, other):
        return pltpu.make_async_remote_copy(
            src_ref=origin, dst_ref=target, send_sem=sends.at[number], recv_sem=recvs.at[number],
            device_id={"tensor": other}, device_id_type=mesh_ids,
        )

    first = (
        remote(0, part_ref.at[corner, :, low], turn_across, across),
        remote(1, part_ref.at[corner, :, high], turn_along, along),
    )
    second = remote(2, parts.at[0], from_across, across), remote(3, parts.at[1], from_along, along)
    local = [
        pltpu.make_async_copy(part_ref.at[other], parts.at[number], loads.at[number])
        for number, other in enumerate((across, along, rank))
    ]
    local.append(pltpu.make_async_copy(resid_ref, y_ref, loads.at[3]))

    @pl.when(step == 0)
    def _():
        barrier = pltpu.get_barrier_semaphore()
        for other in (across, along):
            pl.semaphore_signal(barrier, inc=1, device_id={"tensor": other}, device_id_type=mesh_ids)
        pl.semaphore_wait(barrier, 2)
        for copy in first:
            copy.start()
        for copy in local:
            copy.start()

    @pl.when(step == 3)
    def _():
        for copy in (*first, *local):
            copy.wait()
        parts[0, :, high] = (parts[0, :, high].astype(F32) + turn_along[...].astype(F32)).astype(BF16)
        parts[1, :, low] = (parts[1, :, low].astype(F32) + turn_across[...].astype(F32)).astype(BF16)
        for copy in second:
            copy.start()

    head = pl.program_id(1)
    width = q_ref.shape[0]

    @pl.when(head == 0)
    def _():
        held[...] = mm(w_ref[...], grad_ref[...], NT).astype(BF16)

    queries = q_ref[...] * BF16(0.125)
    keys, values = k_ref[...], v_ref[...]
    grads = held[pl.ds(pl.multiple_of(head * width, width), width), :]
    near_ref[...] = jnp.zeros_like(near_ref)
    far = jnp.zeros((8, BLK), F32)
    grad_keys = jnp.zeros((width, SEQ), F32)
    grad_values = jnp.zeros((width, SEQ), F32)
    for block in range(SEQ // BLK):
        count = key_count(block)
        cols = slice(block * BLK, (block + 1) * BLK)
        scores = block_scores(keys, queries[:, cols], tiles_ref, limit_ref[0, :, cols], block)
        probs = jnp.exp(scores - lse_ref[0, :, cols])
        grad_probs = mm(values[:, :count], grads[:, cols], TN)
        inner = jnp.sum(probs * grad_probs, axis=0, keepdims=True)
        grad_scores = probs * (grad_probs - inner)
        for key_block in range(count // BLK):
            part = grad_scores[key_block * BLK : (key_block + 1) * BLK]
            shift = key_block - block
            if -1 <= shift <= 1:
                near_ref[0, shift + 1] += part
            elif shift < -1:
                far = far + jnp.sum(part.reshape(BLK // 8, 8, BLK), axis=0)
        rounded = grad_scores.astype(BF16)
        add_values = mm(grads[:, cols], probs.astype(BF16), NT)
        add_keys = mm(queries[:, cols], rounded, NT)
        if count == SEQ:
            grad_values = grad_values + add_values
            grad_keys = grad_keys + add_keys
        else:
            filler = jnp.zeros((width, SEQ - count), F32)
            grad_values = grad_values + jnp.concatenate([add_values, filler], axis=1)
            grad_keys = grad_keys + jnp.concatenate([add_keys, filler], axis=1)
        dq_ref[:, cols] = (mm(keys[:, :count], rounded) * 0.125).astype(BF16)
    dk_ref[...] = grad_keys.astype(BF16)
    dv_ref[...] = grad_values.astype(BF16)
    far_ref[0] = far

    @pl.when(step == 7)
    def _():
        for copy in second:
            copy.wait()
        y_ref[...] += parts[2].astype(F32) + from_across[...].astype(F32) + from_along[...].astype(F32)


def attend_back(qkv, tiles, limits, attn_out, grad_attn, lse, part, resid):
    heads = tiles.shape[0]
    seqs = limits.shape[0]
    width = qkv.shape[0] // (3 * heads)
    model_width = attn_out.shape[1]
    share = part.shape[1]
    grad_spec = pl.BlockSpec((width, SEQ), lambda s, h: (h, s))
    anywhere = pl.BlockSpec(memory_space=pl.ANY)
    return pl.pallas_call(
        attend_back_kernel,
        grid=(seqs, heads),
        in_specs=[
            pl.BlockSpec((width, SEQ), lambda s, h: (h, s)),
            pl.BlockSpec((width, SEQ), lambda s, h: (heads + h, s)),
            pl.BlockSpec((width, SEQ), lambda s, h: (2 * heads + h, s)),
            pl.BlockSpec((1, 3, BLK, BLK), lambda s, h: (h, 0, 0, 0)),
            pl.BlockSpec((1, 1, SEQ), lambda s, h: (s, 0, 0)),
            pl.BlockSpec((heads * width, model_width), lambda s, h: (0, 0)),
            pl.BlockSpec((SEQ, model_width), lambda s, h: (s, 0)),
            pl.BlockSpec((1, 1, SEQ), lambda s, h: (s * heads + h, 0, 0)),
        ]
        + [anywhere] * 2,
        out_specs=[
            grad_spec,
            grad_spec,
            grad_spec,
            pl.BlockSpec((1, 3, BLK, BLK), lambda s, h: (s * heads + h, 0, 0, 0)),
            pl.BlockSpec((1, 8, BLK), lambda s, h: (s * heads + h, 0, 0)),
            pl.BlockSpec((share, model_width), lambda s, h: (0, 0)),
        ],
        out_shape=[jax.ShapeDtypeStruct((heads * width, seqs * SEQ), BF16)] * 3
        + [
            jax.ShapeDtypeStruct((seqs * heads, 3, BLK, BLK), F32),
            jax.ShapeDtypeStruct((seqs * heads, 8, BLK), F32),
        ]
        + [jax.ShapeDtypeStruct((share, model_width), F32)],
        scratch_shapes=[
            pltpu.VMEM((heads * width, SEQ), BF16),
            pltpu.VMEM((3, share, model_width), BF16),
            pltpu.VMEM((share, model_width // 2), BF16),
            pltpu.VMEM((share, model_width // 2), BF16),
            pltpu.VMEM((share, model_width), BF16),
            pltpu.VMEM((share, model_width), BF16),
            pltpu.SemaphoreType.DMA((4,)),
            pltpu.SemaphoreType.DMA((4,)),
            pltpu.SemaphoreType.DMA((4,)),
        ],
        compiler_params=pltpu.CompilerParams(
            vmem_limit_bytes=60 * MIB, collective_id=5, has_side_effects=True
        ),
        cost_estimate=cost(seqs * heads * SEQ * SEQ * 1280, seqs * heads * SEQ * 4096, seqs * heads * SEQ * SEQ),
    )(qkv, qkv, qkv, tiles, limits, attn_out, grad_attn, lse, part, resid)


def project_back_kernel(
    place_ref, x_ref, gain_ref, scale_ref, w_ref, mixed_ref, attn_ref, dq_ref, dk_ref, dv_ref, *refs
):
    step = pl.program_id(0)
    own_refs, got_refs, (weight_ref, out_ref, gain_grad_ref), placed_refs, total = (
        refs[:2], refs[2:4], refs[4:7], refs[7:9], refs[9]
    )
    for own_ref, got_ref, placed_ref in zip(own_refs, got_refs, placed_refs):
        placed_ref[place_ref[0]] = own_ref[...]
        placed_ref[1 - place_ref[0]] = got_ref[...].astype(F32)
    grads = jnp.concatenate([dq_ref[...], dk_ref[...], dv_ref[...]], axis=0)
    rows = grads.shape[0]
    scaled = x_ref[...].astype(F32) * scale_ref[...]

    @pl.when(step == 0)
    def _():
        total[...] = jnp.zeros_like(total)
        gain_grad_ref[...] = jnp.zeros_like(gain_grad_ref)

    total[:rows] += mm(grads, (scaled * gain_ref[...]).astype(BF16), NT)
    total[rows:] += mm(mixed_ref[...], attn_ref[...])
    back = mm(w_ref[...], grads, TN)
    gain_grad_ref[...] += jnp.sum(back * scaled, axis=1, keepdims=True)
    out_ref[...] = back.T.astype(BF16)

    @pl.when(step == pl.num_programs(0) - 1)
    def _():
        weight_ref[...] = total[...].astype(BF16)


def project_back(place, x, gain, scale, weights, mixed, grad_attn, grads, owns, gots):
    width, tokens = x.shape
    rows = weights.shape[0]
    heads_width = mixed.shape[0]
    units = owns[0].shape[0]
    steps = 4
    tile = tokens // steps
    part = units // steps
    column = lambda count: pl.BlockSpec((count, tile), lambda i: (0, i))
    return pl.pallas_call(
        project_back_kernel,
        grid=(steps,),
        in_specs=[
            pl.BlockSpec(memory_space=pltpu.SMEM),
            column(width),
            pl.BlockSpec((width, 1), lambda i: (0, 0)),
            column(1),
            pl.BlockSpec((rows, width), lambda i: (0, 0)),
            column(heads_width),
            pl.BlockSpec((tile, width), lambda i: (i, 0)),
        ]
        + [column(rows // 3)] * 3
        + [pl.BlockSpec((part, width), lambda i: (i, 0))] * 4,
        out_specs=[
            pl.BlockSpec((rows + heads_width, width), lambda i: (0, 0)),
            pl.BlockSpec((tile, width), lambda i: (i, 0)),
            pl.BlockSpec((width, 1), lambda i: (0, 0)),
        ]
        + [pl.BlockSpec((2, part, width), lambda i: (0, i, 0))] * 2,
        out_shape=[
            jax.ShapeDtypeStruct((rows + heads_width, width), BF16),
            jax.ShapeDtypeStruct((tokens, width), BF16),
            jax.ShapeDtypeStruct((width, 1), F32),
        ]
        + [jax.ShapeDtypeStruct((2, units, width), F32)] * 2,
        scratch_shapes=[pltpu.VMEM((rows + heads_width, width), F32)],
        compiler_params=params(),
        cost_estimate=cost(5 * width * tokens * rows, 6 * width * tokens + 14 * units * width),
    )(place, x, gain, scale, weights, mixed, grad_attn, *grads, *owns, *gots)


def exchange(math, rank, source, full, from_across, from_along, to_across, to_along, turn_across, turn_along, sends, recvs, ready=None, ready_full=None, side=None, peers=(), fill=None, start=None, cut=None):
    pair_class, half_index = rank % 2, rank // 2
    across, along, corner = rank + 1 - 2 * pair_class, rank + 2 - 4 * half_index, 3 - rank
    mesh_ids = pl.DeviceIdType.MESH
    rows, width = source.shape[1:]
    chunks = 4
    size = rows // chunks
    cut = cut or width // 2
    low, high = slice(0, cut), slice(cut, width)
    barrier = pltpu.get_barrier_semaphore()
    for other in (across, along):
        pl.semaphore_signal(barrier, inc=1, device_id={"tensor": other}, device_id_type=mesh_ids)
    for other in peers:
        pl.semaphore_signal(barrier, inc=1, device_id={"expert": other}, device_id_type=mesh_ids)
    pl.semaphore_wait(barrier, 2 + len(peers))

    def remote(kind, chunk, origin, target, other):
        return pltpu.make_async_remote_copy(
            src_ref=origin, dst_ref=target, send_sem=sends.at[kind, chunk], recv_sem=recvs.at[kind, chunk],
            device_id={"tensor": other}, device_id_type=mesh_ids,
        )

    if start:
        start()
    if fill:
        fill(corner)
    spans = [slice(chunk * size, (chunk + 1) * size) for chunk in range(chunks)]
    first, second, third, fourth = [], [], [], []
    for chunk, span in enumerate(spans):
        pair = (
            remote(0, chunk, source.at[corner, span, low], turn_across.at[span, low], across),
            remote(1, chunk, source.at[corner, span, high], turn_along.at[span, high], along),
        )
        for copy in pair:
            copy.start()
        first.append(pair)
    if fill:
        fill(along)
        fill(across)
    if ready is not None:
        ready_full[rank] = ready[...]
        extra = [
            remote(8, 0, ready, ready_full.at[rank], across),
            remote(8, 1, ready, ready_full.at[rank], along),
            remote(8, 2, ready_full.at[along, :, low], ready_full.at[along, :, low], across),
            remote(8, 3, ready_full.at[across, :, high], ready_full.at[across, :, high], along),
        ]
        for copy in extra[:2]:
            copy.start()
    for chunk, span in enumerate(spans):
        if side:
            side(chunk)
        first[chunk][0].wait()
        to_along[span, low] = (source[along, span, low].astype(F32) + turn_across[span, low].astype(F32)).astype(BF16)
        to_along[span, high] = source[along, span, high]
        first[chunk][1].wait()
        to_across[span, low] = source[across, span, low]
        to_across[span, high] = (source[across, span, high].astype(F32) + turn_along[span, high].astype(F32)).astype(BF16)
        pair = (
            remote(2, chunk, to_across.at[span], from_across.at[span], across),
            remote(3, chunk, to_along.at[span], from_along.at[span], along),
        )
        for copy in pair:
            copy.start()
        second.append(pair)
    if ready is not None:
        for copy in extra[:2]:
            copy.wait()
        for copy in extra[2:]:
            copy.start()

    def pass_on(chunk):
        span = spans[chunk]
        for copy in third[chunk]:
            copy.wait()
        pair = (
            remote(6, chunk, full.at[along, span, low], full.at[along, span, low], across),
            remote(7, chunk, full.at[across, span, high], full.at[across, span, high], along),
        )
        for copy in pair:
            copy.start()
        fourth.append(pair)

    if fill:
        fill(rank)
    for chunk, span in enumerate(spans):
        if side:
            side(chunks + chunk)
        for copy in second[chunk]:
            copy.wait()
        total = source[rank, span].astype(F32) + from_across[span].astype(F32) + from_along[span].astype(F32)
        full[rank, span] = math(span, total).astype(BF16)
        pair = (
            remote(4, chunk, full.at[rank, span], full.at[rank, span], across),
            remote(5, chunk, full.at[rank, span], full.at[rank, span], along),
        )
        for copy in pair:
            copy.start()
        third.append(pair)
        if chunk:
            pass_on(chunk - 1)
    pass_on(chunks - 1)
    if ready is not None:
        for copy in extra[2:]:
            copy.wait()
    for pair in fourth:
        for copy in pair:
            copy.wait()
    if side:
        side(2 * chunks)


def exchange_call(kernel, number, shape, operands, extra_shapes, scratch=(), places=None, out_places=None):
    tokens, width = shape
    ranks = 4
    rows = tokens // ranks
    here = pl.BlockSpec(memory_space=pltpu.VMEM)
    results = pl.pallas_call(
        kernel,
        in_specs=places or [here] * len(operands),
        out_specs=out_places or [here] * (1 + len(extra_shapes)),
        out_shape=[jax.ShapeDtypeStruct((ranks, rows, width), BF16)]
        + [jax.ShapeDtypeStruct(shape, kind) for shape, kind in extra_shapes],
        scratch_shapes=[pltpu.VMEM((rows, width), BF16)] * 6
        + [pltpu.SemaphoreType.DMA((9, 4))] * 2
        + list(scratch),
        compiler_params=pltpu.CompilerParams(
            vmem_limit_bytes=60 * MIB, collective_id=number, has_side_effects=True
        ),
        cost_estimate=cost(40 * MIB, 200 * MIB),
    )(*operands)
    return results[0].reshape(tokens, width), *results[1:]


def norm_two_kernel(source, x_ref, gain_ref, grad_out_ref, code_ref, full, resid_ref, scale_ref, dy_ref, dy_rows_ref, *rest):
    def math(span, total):
        resid = x_ref[span, :].astype(F32) + total
        scale = lax.rsqrt(jnp.sum(resid * resid, axis=1, keepdims=True) / resid.shape[1] + EPS)
        resid_ref[span, :] = resid
        scale_ref[span, :] = scale
        return resid * scale * gain_ref[...]

    ranks, rows, width = source.shape
    slots = dy_rows_ref.shape[0] // ranks

    def side(number):
        if number < ranks:
            span = slice(number * rows, (number + 1) * rows)
            dy_ref[span, :] = grad_out_ref[:, span].astype(F32).T.astype(BF16)
        elif number < 2 * ranks:
            start = (number - ranks) * slots
            slot = lax.broadcasted_iota(jnp.int32, (slots, dy_ref.shape[0]), 0) + start
            take = jnp.where((slot == code_ref[0:1]) | (slot == code_ref[1:2]), 1.0, 0.0).astype(BF16)
            dy_rows_ref[start : start + slots, :] = mm(take, dy_ref[...]).astype(BF16)

    exchange(math, lax.axis_index("tensor"), source, full, *rest, side=side)


def norm_back(grad, value, scale, gain):
    scaled = grad * gain
    inner = jnp.sum(scaled * value, axis=1, keepdims=True)
    return scale * scaled - value * (scale * scale * scale) * (inner / value.shape[1])


def norm_two_back_kernel(
    ret_ref, back_ref, code_ref, codes_ref, gates_ref, routes_ref, dy_rows_ref, gate_ref, router_ref, h_ref,
    resid_ref, scale_ref, dy_ref, gain_ref, up_ref, full, grad_ref, gain_grad_ref, router_grad_ref, y_ref, got_ref,
    *rest,
):
    source, scaled, logit_parts, send, recv = rest[-5:]
    rank = lax.axis_index("tensor")
    rows = source.shape[1]
    slots, tokens = ret_ref.shape[0], code_ref.shape[1]
    swap = pltpu.make_async_remote_copy(
        src_ref=up_ref, dst_ref=got_ref, send_sem=send.at[0], recv_sem=recv.at[0],
        device_id={"tensor": rank + 1 - 2 * (rank % 2)}, device_id_type=pl.DeviceIdType.MESH,
    )

    def start():
        swap.start()
        found = [jnp.zeros((1, tokens), F32) for _ in range(TOP)]
        tile = slots // 4
        for begin in range(0, slots, tile):
            span = slice(begin, begin + tile)
            ret = ret_ref[span, :].astype(F32)
            slot_grad = jnp.sum(dy_rows_ref[span, :].astype(F32) * ret, axis=1, keepdims=True)
            scaled[span, :] = (ret * gate_ref[span, :]).astype(BF16)
            slot = lax.broadcasted_iota(jnp.int32, (tile, tokens), 0) + begin
            for i in range(TOP):
                found[i] = found[i] + jnp.sum(
                    jnp.where(slot == code_ref[i : i + 1, :], slot_grad, 0.0), axis=0, keepdims=True
                )
        mean = gates_ref[0:1] * found[0] + gates_ref[1:2] * found[1]
        expert = lax.broadcasted_iota(jnp.int32, (EXPERTS, tokens), 0)
        logit = sum(
            jnp.where(routes_ref[i : i + 1] == expert, gates_ref[i : i + 1] * (found[i] - mean), 0.0)
            for i in range(TOP)
        )
        coarse = logit.astype(BF16)
        fine = (logit - coarse.astype(F32)).astype(BF16)
        for shard in range(tokens // rows):
            span = slice(shard * rows, (shard + 1) * rows)
            logit_parts[shard, :EXPERTS] = coarse[:, span]
            logit_parts[shard, EXPERTS:] = fine[:, span]

    def places(shard):
        slot = lax.broadcasted_iota(jnp.int32, (rows, slots), 1)
        codes = codes_ref[pl.ds(pl.multiple_of(shard * rows, rows), rows), :]
        return jnp.where((slot == codes[:, 0:1]) | (slot == codes[:, 1:2]), 1.0, 0.0).astype(BF16)

    def fill(shard):
        value = mm(places(shard), back_ref[...])
        both = jnp.concatenate([router_ref[...], router_ref[...]], axis=0)
        source[shard] = (value + mm(logit_parts[shard], both, TN)).astype(BF16)

    def side(number):
        shards = tokens // rows
        if number < shards:
            y_ref[number * rows : (number + 1) * rows, :] = mm(places(number), scaled[...]).astype(BF16)
        elif number == shards:
            router_grad_ref[...] = sum(
                mm(logit_parts[shard, :EXPERTS], h_ref[shard * rows : (shard + 1) * rows, :])
                for shard in range(shards)
            )
        elif number == 2 * shards:
            swap.wait()

    gain_grad_ref[...] = jnp.zeros_like(gain_grad_ref)

    def math(span, total):
        resid, scale = resid_ref[span, :], scale_ref[span, :]
        gain_grad_ref[...] += jnp.sum(total * resid * scale, axis=0, keepdims=True)
        own_dy = dy_ref[pl.ds(pl.multiple_of(rank * rows + span.start, 128), span.stop - span.start), :]
        grad = norm_back(total, resid, scale, gain_ref[...]) + own_dy.astype(F32)
        grad_ref[span, :] = grad
        return grad

    exchange(math, rank, source, full, *rest[:-5], side=side, fill=fill, start=start, cut=source.shape[2] // 4)


def norm_one_back_kernel(
    source, x_ref, scale_ref, grad_ref, gain_ref, ready, gain_one_ref, gain_two_ref, router_ref, near_ref, far_ref,
    full, ready_full, small_out, *rest
):
    held, tensor_sends, tensor_recvs, expert_sends, expert_recvs = rest[-5:]
    rank, group = lax.axis_index("tensor"), lax.axis_index("expert")
    pair_class, half_index = rank % 2, rank // 2
    others = rank + 1 - 2 * pair_class, rank + 2 - 4 * half_index
    groups = expert_sends.shape[0]
    mesh_ids = pl.DeviceIdType.MESH
    peers = [partner_of(group, step) for step in range(1, groups)]
    summed = slice(0, small_out.shape[0] - BUCKETS)

    def math(span, total):
        x = x_ref[span, :].astype(F32)
        return norm_back(total, x, scale_ref[span, :], gain_ref[...]) + grad_ref[span, :]

    def to_rank(step):
        return pltpu.make_async_remote_copy(
            src_ref=held.at[groups + step], dst_ref=held.at[groups + 2 + step], send_sem=tensor_sends.at[step],
            recv_sem=tensor_recvs.at[step], device_id={"tensor": others[step]}, device_id_type=mesh_ids,
        )

    def to_group(step):
        return pltpu.make_async_remote_copy(
            src_ref=held.at[group], dst_ref=held.at[group], send_sem=expert_sends.at[step],
            recv_sem=expert_recvs.at[step], device_id={"expert": peers[step - 1]}, device_id_type=mesh_ids,
        )

    def side(number):
        if number == 0:
            held[groups] = jnp.zeros(small_out.shape, F32)
            held[groups, :EXPERTS] = router_ref[...]
            held[groups, EXPERTS : EXPERTS + 1] = gain_two_ref[...]
            held[groups, EXPERTS + 1 : EXPERTS + 2] = jnp.broadcast_to(gain_one_ref[...], (gain_one_ref.shape[0], 128)).T[:1]
            to_rank(0).start()
        elif number == 1:
            to_rank(0).wait()
            held[groups + 1] = held[groups] + held[groups + 2]
            to_rank(1).start()
        elif number == 2:
            to_rank(1).wait()
            for head, column in enumerate(bias_fold(near_ref, far_ref)):
                span = slice(summed.stop, summed.stop + BUCKETS)
                held[group, span, head * 128 : (head + 1) * 128] = jnp.broadcast_to(column, (BUCKETS, 128))
            held[group, summed] = held[groups + 1, summed] + held[groups + 3, summed]
            for step in range(1, groups):
                to_group(step).start()
        elif number == 8:
            for step in range(1, groups):
                to_group(step).wait()
            total = held[0]
            for step in range(1, groups):
                total = total + held[step]
            small_out[...] = total

    exchange(math, rank, source, full, *rest[:-5], ready, ready_full, side=side, peers=peers)


def code_kernel(place_ref, routes_ref, code_ref, half, groups):
    pair_class, half_index = place_ref[0], place_ref[1]
    tokens = routes_ref.shape[1]
    expert = lax.broadcasted_iota(jnp.int32, (EXPERTS, BLK), 0)
    earlier = (
        lax.broadcasted_iota(jnp.int32, (BLK, BLK), 0) < lax.broadcasted_iota(jnp.int32, (BLK, BLK), 1)
    ).astype(F32).astype(BF16)
    carry = jnp.zeros((EXPERTS, 1), F32)
    for block in range(tokens // BLK):
        cols = slice(block * BLK, (block + 1) * BLK)
        routes = routes_ref[:, cols]
        hits = [(routes[i : i + 1] == expert) for i in range(TOP)]
        chosen = sum(hit.astype(F32) for hit in hits)
        before = mm(chosen.astype(BF16), earlier) + carry
        carry = carry + jnp.sum(chosen, axis=1, keepdims=True)
        for i in range(TOP):
            slot = jnp.sum(jnp.where(hits[i], before, 0.0), axis=0, keepdims=True).astype(jnp.int32)
            route = routes[i : i + 1]
            owner = route // 2
            local = slot - half_index * half
            mine = (route - 2 * owner == pair_class) & (local >= 0) & (local < half)
            code_ref[i : i + 1, cols] = jnp.where(mine, owner * half + local, -1)


def local_codes(place, routes_t, half, groups):
    return pl.pallas_call(
        partial(code_kernel, half=half, groups=groups),
        in_specs=[
            pl.BlockSpec(memory_space=pltpu.SMEM),
            pl.BlockSpec(memory_space=pltpu.VMEM),
        ],
        out_specs=pl.BlockSpec(memory_space=pltpu.VMEM),
        out_shape=jax.ShapeDtypeStruct(routes_t.shape, jnp.int32),
        compiler_params=params(),
    )(place, routes_t)


def dispatch_kernel(code_ref, routes_ref, router_ref, h_ref, dy_rows_ref, rows_ref, grads_ref, gate_ref, gates_ref):
    count, tokens = rows_ref.shape[0], h_ref.shape[0]

    @pl.when(pl.program_id(0) == 0)
    def _():
        expert = lax.broadcasted_iota(jnp.int32, (EXPERTS, tokens), 0)
        logits = mm(router_ref[...], h_ref[...], NT)
        picked = [
            jnp.sum(jnp.where(routes_ref[i : i + 1] == expert, logits, 0.0), axis=0, keepdims=True)
            for i in range(TOP)
        ]
        top = jnp.maximum(picked[0], picked[1])
        raised = [jnp.exp(value - top) for value in picked]
        total = raised[0] + raised[1]
        for i in range(TOP):
            gates_ref[i : i + 1] = raised[i] / total

    slot = lax.broadcasted_iota(jnp.int32, (count, tokens), 0) + pl.program_id(0) * count
    hits = [slot == code_ref[i : i + 1, :] for i in range(TOP)]
    take = jnp.where(hits[0] | hits[1], 1.0, 0.0).astype(BF16)
    weighted = jnp.where(hits[0], gates_ref[0:1, :], jnp.where(hits[1], gates_ref[1:2, :], 0.0))
    gate = jnp.sum(weighted, axis=1, keepdims=True)
    rows_ref[...] = mm(take, h_ref[...]).astype(BF16)
    grads_ref[...] = (dy_rows_ref[...].astype(F32) * gate).astype(BF16)
    gate_ref[...] = gate


def dispatch(code, routes_t, router_t, h, dy_rows):
    slots, width = dy_rows.shape
    tile = slots // 4
    row_spec = pl.BlockSpec((tile, width), lambda i: (i, 0))
    whole = lambda shape: pl.BlockSpec(shape, lambda i: (0, 0))
    return pl.pallas_call(
        dispatch_kernel,
        grid=(4,),
        in_specs=[whole(code.shape), whole(code.shape), whole(router_t.shape), whole(h.shape), row_spec],
        out_specs=[row_spec, row_spec, pl.BlockSpec((tile, 1), lambda i: (i, 0)), whole(code.shape)],
        out_shape=[jax.ShapeDtypeStruct((slots, width), BF16)] * 2
        + [jax.ShapeDtypeStruct((slots, 1), F32), jax.ShapeDtypeStruct(code.shape, F32)],
        compiler_params=params(),
        cost_estimate=cost(4 * slots * SEQ * width, 4 * MIB + 6 * slots * width),
    )(code, routes_t, router_t, h, dy_rows)


def gelu_parts(x):
    inner = 0.7978845608028654 * (x + 0.044715 * (x * x * x))
    bend = jnp.tanh(inner)
    half = 0.5 * (1.0 + bend)
    slope = half + 0.5 * x * (1.0 - bend * bend) * (
        0.7978845608028654 * (1.0 + 3.0 * 0.044715 * (x * x))
    )
    return x * half, slope


def partner_of(index, step):
    found = index
    for bit in (1, 2, 4):
        found = found + ((step // bit) % 2) * (1 - 2 * ((index // bit) % 2)) * bit
    return found


def expert_kernel(
    rows_in, grads_in, gate_in, up_in, down_in, far_gate,
    ret_out, back_out, own_gate, own_up, own_down, got_gate, sent_up, sent_down,
    rows, grads, weights, sums, parts, z_send, z_recv, y_send, y_recv, p_send, p_recv, r_send, r_recv, w_send, w_recv, g_send, g_recv, local,
):
    groups, half, width = rows.shape[1:]
    group, rank = lax.axis_index("expert"), lax.axis_index("tensor")
    pair_class, half_index = rank % 2, rank // 2
    across = {"tensor": rank + 1 - 2 * pair_class}
    along = {"tensor": rank + 2 - 4 * half_index}
    mesh_ids = pl.DeviceIdType.MESH
    moved = ((rows_in, rows, ret_out), (grads_in, grads, back_out))

    barrier = pltpu.get_barrier_semaphore()
    for step in range(1, groups):
        pl.semaphore_signal(
            barrier, inc=1, device_id={"expert": partner_of(group, step)}, device_id_type=mesh_ids
        )
    pl.semaphore_signal(barrier, inc=1, device_id=across, device_id_type=mesh_ids)
    pl.semaphore_signal(barrier, inc=1, device_id=along, device_id_type=mesh_ids)
    pl.semaphore_wait(barrier, groups + 1)

    def remote(source, target, send, recv, device):
        return pltpu.make_async_remote_copy(
            src_ref=source, dst_ref=target, send_sem=send, recv_sem=recv,
            device_id=device, device_id_type=mesh_ids,
        )

    def block(ref, number):
        return ref.at[pl.ds(pl.multiple_of(number * half, half), half)]

    def out_of(kind, step):
        source, held, _ = moved[kind]
        other = partner_of(group, step)
        return remote(
            block(source, other), held.at[0, group], z_send.at[kind, step], z_recv.at[kind, step], {"expert": other}
        )

    def forward(kind, step):
        held = moved[kind][1]
        other = partner_of(group, step)
        return remote(held.at[0, other], held.at[1, other], y_send.at[kind, step], y_recv.at[kind, step], along)

    def partial_sum(kind, step):
        held = moved[kind][1]
        other = partner_of(group, step)
        return remote(held.at[1, other], parts.at[kind, other], p_send.at[kind, step], p_recv.at[kind, step], along)

    def result(kind, step):
        other = partner_of(group, step)
        return remote(
            parts.at[kind, other], block(moved[kind][2], group), r_send.at[kind, step], r_recv.at[kind, step], {"expert": other}
        )

    def own_result(kind):
        return pltpu.make_async_copy(parts.at[kind, group], block(moved[kind][2], group), local.at[kind])

    own = [
        pltpu.make_async_copy(block(moved[kind][0], group), moved[kind][1].at[0, group], local.at[kind])
        for kind in range(2)
    ]
    for copy in own:
        copy.start()
    kept = [
        pltpu.make_async_copy(ref.at[pair_class], weights.at[number, 0], local.at[2 + number])
        for number, ref in enumerate((gate_in, up_in, down_in))
    ]
    kept.append(pltpu.make_async_copy(far_gate, weights.at[0, 1], local.at[5]))
    kept += [
        remote(ref.at[1 - pair_class], weights.at[number, 1], w_send.at[number - 1], w_recv.at[number - 1], across)
        for number, ref in ((1, up_in), (2, down_in))
    ]
    for copy in kept:
        copy.start()
    for step in range(1, groups):
        for kind in range(2):
            out_of(kind, step).start()
    def arrive(step):
        for kind in range(2):
            out_of(kind, step).wait()
            forward(kind, step).start()

    near = groups // 2
    for copy in own:
        copy.wait()
    for kind in range(2):
        forward(kind, 0).start()
    for step in range(1, near):
        arrive(step)
    for number in range(3):
        for part in range(2):
            sums[number, part] = jnp.zeros(sums.shape[2:], F32)

    def finish(step):
        other = partner_of(group, step)
        for kind in range(2):
            partial_sum(kind, step).wait()
            held = moved[kind][1]
            parts[kind, other] = (parts[kind, other].astype(F32) + held[0, other].astype(F32)).astype(BF16)

        @pl.when(step == 0)
        def _():
            for kind in range(2):
                own_result(kind).start()

        @pl.when(step > 0)
        def _():
            for kind in range(2):
                result(kind, step).start()

    def body(step, carry):
        @pl.when((step >= near) & (step < groups - 1))
        def _():
            arrive(step + 1)

        @pl.when(step == 0)
        def _():
            for copy in kept:
                copy.wait()

        for kind in range(2):
            forward(kind, step).wait()
        other = partner_of(group, step)
        tile = jnp.concatenate([rows[0, other], rows[1, other]], axis=0)
        grad = jnp.concatenate([grads[0, other], grads[1, other]], axis=0)
        ret = jnp.zeros(tile.shape, F32)
        back = jnp.zeros(tile.shape, F32)
        for part in range(2):
            w_gate, w_up, w_down = weights[0, part], weights[1, part], weights[2, part]
            gate_part = mm(tile, w_gate, NT)
            up_part = mm(tile, w_up, NT)
            grad_hidden = mm(grad, w_down, NT)
            bent, slope = gelu_parts(gate_part)
            hidden = (bent * up_part).astype(BF16)
            grad_gate = (grad_hidden * up_part * slope).astype(BF16)
            grad_up = (grad_hidden * bent).astype(BF16)
            ret = ret + mm(hidden, w_down)
            back = back + mm(grad_gate, w_gate) + mm(grad_up, w_up)
            sums[0, part] += mm(grad_gate, tile, TN)
            sums[1, part] += mm(grad_up, tile, TN)
            sums[2, part] += mm(hidden, grad, TN)
        for kind, value in enumerate((ret, back)):
            held = moved[kind][1]
            held[0, other] = value[:half].astype(BF16)
            held[1, other] = value[half:].astype(BF16)
            partial_sum(kind, step).start()

        @pl.when(step > 0)
        def _():
            finish(step - 1)

        @pl.when(step == near - 1)
        def _():
            arrive(near)

        return carry

    lax.fori_loop(0, groups, body, 0)
    copies = []
    for number, own_ref in enumerate((own_gate, own_up, own_down)):
        weights[number, 0] = sums[number, 1].astype(BF16)
        if number == 0:
            copies.append(remote(weights.at[0, 0], got_gate, g_send.at[0], g_recv.at[0], across))
        else:
            far_ref = (sent_up, sent_down)[number - 1]
            copies.append(pltpu.make_async_copy(weights.at[number, 0], far_ref, local.at[4 + number]))
        copies[-1].start()
        copies.append(pltpu.make_async_copy(sums.at[number, 0], own_ref, local.at[2 + number]))
        copies[-1].start()
    finish(groups - 1)
    for copy in copies:
        copy.wait()
    for kind in range(2):
        own_result(kind).wait()
        for step in range(1, groups):
            result(kind, step).wait()


def run_experts(rows, grads, w_gate, w_up, w_down, far_gate):
    slots, width = rows.shape
    half = CAP // 2
    groups = slots // half
    units = w_gate.shape[1]
    anywhere = pl.BlockSpec(memory_space=pl.ANY)
    pair = pltpu.SemaphoreType.DMA((2, groups))
    return pl.pallas_call(
        expert_kernel,
        in_specs=[anywhere] * 6,
        out_specs=[anywhere] * 8,
        out_shape=[jax.ShapeDtypeStruct((slots, width), BF16)] * 2
        + [jax.ShapeDtypeStruct((units, width), F32)] * 3
        + [jax.ShapeDtypeStruct((units, width), BF16)] * 3,
        scratch_shapes=[
            pltpu.VMEM((2, groups, half, width), BF16),
            pltpu.VMEM((2, groups, half, width), BF16),
            pltpu.VMEM((3, 2, units, width), BF16),
            pltpu.VMEM((3, 2, units, width), F32),
            pltpu.VMEM((2, groups, half, width), BF16),
        ]
        + [pair] * 8
        + [pltpu.SemaphoreType.DMA((2,))] * 2
        + [pltpu.SemaphoreType.DMA((1,))] * 2
        + [pltpu.SemaphoreType.DMA((7,))],
        compiler_params=pltpu.CompilerParams(
            vmem_limit_bytes=60 * MIB, collective_id=1, has_side_effects=True
        ),
        cost_estimate=cost(72 * slots * units * width, 16 * slots * width + 30 * units * width),
    )(rows, grads, w_gate, w_up, w_down, far_gate)


def turn_kernel(in_ref, out_ref):
    out_ref[...] = in_ref[...].astype(F32).T.astype(out_ref.dtype)


def turn(rows, kind):
    tokens, width = rows.shape
    tile = 512
    return pl.pallas_call(
        turn_kernel,
        grid=(tokens // tile,),
        in_specs=[pl.BlockSpec((tile, width), lambda i: (i, 0))],
        out_specs=pl.BlockSpec((width, tile), lambda i: (0, i)),
        out_shape=jax.ShapeDtypeStruct((width, tokens), kind),
        compiler_params=params(),
        cost_estimate=cost(0, 6 * rows.size),
    )(rows)


def turn_and_place_kernel(place_ref, in_ref, own_ref, got_ref, out_ref, placed_ref):
    out_ref[...] = in_ref[...].astype(F32).T.astype(out_ref.dtype)
    placed_ref[place_ref[0]] = own_ref[...]
    placed_ref[1 - place_ref[0]] = got_ref[...].astype(F32)


def turn_and_place(place, rows, kind, own, got):
    tokens, width = rows.shape
    units = own.shape[0]
    steps = 4
    tile, part = tokens // steps, units // steps
    quarter = pl.BlockSpec((part, width), lambda i: (i, 0))
    return pl.pallas_call(
        turn_and_place_kernel,
        grid=(steps,),
        in_specs=[
            pl.BlockSpec(memory_space=pltpu.SMEM),
            pl.BlockSpec((tile, width), lambda i: (i, 0)),
            quarter,
            quarter,
        ],
        out_specs=[
            pl.BlockSpec((width, tile), lambda i: (0, i)),
            pl.BlockSpec((2, part, width), lambda i: (0, i, 0)),
        ],
        out_shape=[
            jax.ShapeDtypeStruct((width, tokens), kind),
            jax.ShapeDtypeStruct((2, units, width), F32),
        ],
        compiler_params=params(),
        cost_estimate=cost(0, 6 * rows.size + 14 * own.size),
    )(place, rows, own, got)


def on_device(
    layer_input, gain_one, attn_in, rel_bias, attn_out, gain_two, router,
    expert_gate, expert_up, expert_down, routes, piece_starts, grad_out,
):
    width, tokens = layer_input.shape
    ranks = lax.axis_size("tensor")
    groups = lax.axis_size("expert")
    rank = lax.axis_index("tensor")
    pair_class, half_index = rank % 2, rank // 2
    half = CAP // 2

    def trade(weights):
        other = lax.dynamic_index_in_dim(weights, 1 - pair_class, 0, keepdims=False)
        return lax.ppermute(other, "tensor", [(r, r ^ 1) for r in range(ranks)])

    traded = trade(expert_gate)
    gain_col = gain_one[:, None]
    w_in = attn_in.reshape(-1, width)
    qkv, scale_one = project(layer_input, gain_col, w_in)
    tiles = bias_tiles(rel_bias)
    position = jnp.arange(SEQ, dtype=jnp.int32)[None, None, :]
    starts = piece_starts[:, :, None]
    inside = (position >= starts) & (position < starts + PIECE)
    last = jnp.max(jnp.where(inside, starts + (PIECE - 1), -1), axis=1)
    limits = jnp.maximum(last, position[0])[:, None, :]

    routes_t = routes.T
    place = jnp.stack([pair_class, half_index]).astype(jnp.int32)
    code = local_codes(place, routes_t, half, groups)
    code_cols = code.T

    share = tokens // ranks

    def own(rows, axis=0):
        return lax.dynamic_slice_in_dim(rows, rank * share, share, axis)

    def by_rank(rows):
        return rows.reshape(ranks, share, width)

    own_x = own(layer_input, 1).T
    own_scale = own(scale_one, 1).T
    mixed, lse, sent = attend(qkv, tiles, limits, attn_out)
    sent, traded = lax.optimization_barrier((sent, traded))
    slots = groups * half
    h2, resid, scale_two, dy, dy_rows = exchange_call(
        norm_two_kernel, 2, sent.shape, [by_rank(sent), own_x, gain_two[None], grad_out, code],
        [((share, width), F32), ((share, 1), F32), ((tokens, width), BF16), ((slots, width), BF16)],
    )
    rows, row_grads, gate_rows, gates = dispatch(code, routes_t, router.T, h2, dy_rows)
    ret, back, own_gate, own_up, own_down, got_gate, sent_up, sent_down = run_experts(
        rows, row_grads, expert_gate, expert_up, expert_down, traded
    )
    here, anywhere = pl.BlockSpec(memory_space=pltpu.VMEM), pl.BlockSpec(memory_space=pl.ANY)
    grad_attn, grad_resid, grad_gain_two, grad_router, partial_y, got_up = exchange_call(
        norm_two_back_kernel, 3, (tokens, width),
        [ret, back, code, code_cols, gates, routes_t, dy_rows, gate_rows, router.T, h2]
        + [resid, scale_two, dy, gain_two[None], sent_up],
        [((share, width), F32), ((1, width), F32), ((EXPERTS, width), F32), ((tokens, width), BF16)]
        + [(sent_up.shape, BF16)],
        [
            pltpu.VMEM((ranks, share, width), BF16),
            pltpu.VMEM((slots, width), BF16),
            pltpu.VMEM((ranks, 2 * EXPERTS, share), BF16),
        ]
        + [pltpu.SemaphoreType.DMA((1,))] * 2,
        [here] * 14 + [anywhere],
        [here] * 5 + [anywhere],
    )

    dq, dk, dv, near, far, y_own = attend_back(
        qkv, tiles, limits, attn_out, grad_attn, lse, by_rank(partial_y), resid
    )
    sent_down, dq, y_own = lax.optimization_barrier((sent_down, dq, y_own))
    got_down = lax.ppermute(sent_down, "tensor", [(r, r ^ 1) for r in range(ranks)])
    weight_rows, sent, grad_gain_one, grad_gate, grad_up = project_back(
        place, layer_input, gain_col, scale_one, w_in, mixed, grad_attn, (dq, dk, dv),
        (own_gate, own_up), (got_gate, got_up),
    )
    sent, got_down = lax.optimization_barrier((sent, got_down))
    summed = lax.psum(weight_rows, "expert")
    y_own = y_own.astype(BF16)
    small_shape = (EXPERTS + 8 + BUCKETS, width)
    grad_rows, y_full, small = exchange_call(
        norm_one_back_kernel, 4, sent.shape,
        [by_rank(sent), own_x, own_scale, grad_resid, gain_one[None], y_own, grad_gain_one, grad_gain_two, grad_router]
        + [near, far],
        [((ranks, share, width), BF16), (small_shape, F32)],
        [pltpu.VMEM((groups + 4, *small_shape), F32)]
        + [pltpu.SemaphoreType.DMA((2,))] * 2
        + [pltpu.SemaphoreType.DMA((groups,))] * 2,
    )
    summed, grad_rows = lax.optimization_barrier((summed, grad_rows))
    grad_input = turn(grad_rows, F32)
    layer_output, grad_down = turn_and_place(place, y_full.reshape(tokens, width), BF16, own_down, got_down)
    in_rows = w_in.shape[0]
    heads = rel_bias.shape[1]
    return (
        layer_output,
        grad_input,
        small[EXPERTS + 1],
        summed[:in_rows].astype(F32).reshape(attn_in.shape),
        small[EXPERTS + 8 :, : heads * 128 : 128],
        summed[in_rows:].astype(F32),
        small[EXPERTS],
        small[:EXPERTS].T,
        grad_gate,
        grad_up,
        grad_down,
    )


def allowed_pairs(seq_starts):
    position = jnp.arange(SEQ, dtype=jnp.int32)
    inside = (position[:, None] >= seq_starts[None, :]) & (
        position[:, None] < seq_starts[None, :] + PIECE
    )
    numbers = jnp.arange(seq_starts.shape[0], dtype=jnp.int32) + 1
    piece_label = jnp.sum(inside.astype(jnp.int32) * numbers[None, :], axis=1)
    causal = position[None, :] <= position[:, None]
    shared = (piece_label[:, None] == piece_label[None, :]) & (piece_label[:, None] > 0)
    return causal | shared


def slot_table(routes):
    flat_routes = routes.reshape(-1)
    onehot = (flat_routes[:, None] == jnp.arange(EXPERTS, dtype=jnp.int32)[None, :]).astype(
        jnp.int32
    )
    blocks = onehot.reshape(-1, 128, EXPERTS).astype(F32)
    earlier = jnp.tril(jnp.ones((128, 128), F32), -1)
    inside = jnp.einsum("ij,bje->bie", earlier, blocks)
    count = blocks.shape[0]
    carried = jnp.einsum("ab,be->ae", jnp.tril(jnp.ones((count, count), F32), -1), jnp.sum(blocks, axis=1), precision=HIGH)
    before = (inside + carried[:, None, :]).astype(jnp.int32).reshape(onehot.shape)
    slot_number = jnp.sum(before * onehot, axis=1)
    kept_pairs = slot_number < CAP
    slot_index = jnp.where(kept_pairs, flat_routes * CAP + slot_number, EXPERTS * CAP)
    return (slot_index.reshape(routes.shape), kept_pairs.reshape(routes.shape))


def bucket_onehot():
    offsets = jnp.arange(2 * SEQ - 1, dtype=jnp.int32) - (SEQ - 1)
    return (bucket_of(offsets)[:, None] == jnp.arange(BUCKETS, dtype=jnp.int32)[None, :]).astype(
        jnp.float32
    )


def expand_line(line):
    head_count = line.shape[0]
    padded = jnp.concatenate([line, jnp.zeros((head_count, 1), line.dtype)], axis=1)
    tiled = jnp.tile(padded, (1, SEQ))[:, : SEQ * (2 * SEQ - 1)].reshape(
        head_count, SEQ, 2 * SEQ - 1
    )
    return tiled[:, :, SEQ - 1 :]


def fold_line(full_grid):
    head_count = full_grid.shape[0]
    padded = jnp.pad(full_grid, ((0, 0), (0, 0), (SEQ - 1, 0))).reshape(
        head_count, SEQ * (2 * SEQ - 1)
    )
    padded = jnp.pad(padded, ((0, 0), (0, SEQ))).reshape(head_count, SEQ, 2 * SEQ)
    return jnp.sum(padded, axis=1)[:, : 2 * SEQ - 1]


def reduce_heads(tensor_value):
    return lax.psum(tensor_value, "tensor")


def spread_slots(tensor_value):
    return lax.all_gather(tensor_value, "tensor", axis=2, tiled=True)


def owner_exchange(tensor_value):
    return lax.all_to_all(tensor_value, "expert", split_axis=0, concat_axis=0, tiled=True)


def expert_sums(tensor_value):
    return lax.psum_scatter(tensor_value, "tensor", scatter_dimension=2, tiled=True)


def norm_forward(resid, gain, model_width):
    scale = lax.rsqrt(jnp.sum(resid * resid, axis=1) / model_width + EPS)[:, None]
    return (scale, (resid * scale * gain).astype(jnp.bfloat16))


def norm_backward(resid, scale, gain, grad_normed, model_width):
    grad_gain = jnp.sum(grad_normed * resid * scale, axis=0)
    scaled = grad_normed * gain
    inner = jnp.sum(scaled * resid, axis=1)[:, None]
    return (grad_gain, scale * scaled - resid * scale**3 * inner / model_width)


def attend_scores(bias_full, queries, key_rows, seq_starts):
    scores = (
        jnp.einsum("qhe,khe->hqk", queries, key_rows, preferred_element_type=jnp.float32) * 0.125
        + bias_full
    )
    return jnp.where(allowed_pairs(seq_starts)[None], scores, NEG)


def attend_forward(bias_full, inputs):
    queries, key_rows, value_rows, seq_starts = inputs
    scores = attend_scores(bias_full, queries, key_rows, seq_starts)
    row_max = jnp.max(scores, axis=2, keepdims=True)
    exponent = jnp.exp(scores - row_max)
    row_sum_exp = jnp.sum(exponent, axis=2, keepdims=True)
    weights = (exponent / row_sum_exp).astype(jnp.bfloat16)
    mixed_heads = jnp.einsum(
        "hqk,khe->qhe", weights, value_rows, preferred_element_type=jnp.float32
    )
    return (mixed_heads.astype(jnp.bfloat16), (row_max + jnp.log(row_sum_exp))[:, :, 0])


def attend_backward(bias_full, running, inputs):
    queries, key_rows, value_rows, grad_heads, seq_starts, log_total = inputs
    scores = attend_scores(bias_full, queries, key_rows, seq_starts)
    probabilities = jnp.exp(scores - log_total[:, :, None])
    grad_probs = jnp.einsum(
        "qhe,khe->hqk", grad_heads, value_rows, preferred_element_type=jnp.float32
    )
    inner = jnp.sum(probabilities * grad_probs, axis=2, keepdims=True)
    grad_scores = (probabilities * (grad_probs - inner)).astype(jnp.bfloat16)
    grad_values = jnp.einsum(
        "hqk,qhe->khe",
        probabilities.astype(jnp.bfloat16),
        grad_heads,
        preferred_element_type=jnp.float32,
    )
    grad_queries = (
        jnp.einsum("hqk,khe->qhe", grad_scores, key_rows, preferred_element_type=jnp.float32)
        * 0.125
    )
    grad_keys = (
        jnp.einsum("hqk,qhe->khe", grad_scores, queries, preferred_element_type=jnp.float32) * 0.125
    )
    return (
        running + grad_scores.astype(jnp.float32),
        jnp.stack([grad_queries, grad_keys, grad_values]),
    )


def gelu_product(left, right):
    return jax.nn.gelu(left, approximate=True) * right


def expert_forward(received, weight_gate, weight_up, weight_down):
    gate_part = jnp.einsum(
        "secd,efd->secf", received, weight_gate, preferred_element_type=jnp.float32
    )
    up_part = jnp.einsum("secd,efd->secf", received, weight_up, preferred_element_type=jnp.float32)
    hidden = gelu_product(gate_part, up_part).astype(jnp.bfloat16)
    partial_out = jnp.einsum(
        "secf,efd->secd", hidden, weight_down, preferred_element_type=jnp.float32
    )
    return (gate_part, up_part, hidden, partial_out)


def expert_backward(
    received, gate_part, up_part, hidden, grad_rows_out, weight_gate, weight_up, weight_down
):
    grad_hidden = jnp.einsum(
        "secd,efd->secf", grad_rows_out, weight_down, preferred_element_type=jnp.float32
    )
    product_value, pullback = jax.vjp(gelu_product, gate_part, up_part)
    grad_gate_part, grad_up_part = pullback(grad_hidden)
    grad_gate_part = grad_gate_part.astype(jnp.bfloat16)
    grad_up_part = grad_up_part.astype(jnp.bfloat16)
    grad_down = jnp.einsum(
        "secf,secd->efd", hidden, grad_rows_out, preferred_element_type=jnp.float32
    )
    grad_gate_w = jnp.einsum(
        "secf,secd->efd", grad_gate_part, received, preferred_element_type=jnp.float32
    )
    grad_up_w = jnp.einsum(
        "secf,secd->efd", grad_up_part, received, preferred_element_type=jnp.float32
    )
    grad_rows_in = jnp.einsum(
        "secf,efd->secd", grad_gate_part, weight_gate, preferred_element_type=jnp.float32
    )
    grad_rows_in = grad_rows_in + jnp.einsum(
        "secf,efd->secd", grad_up_part, weight_up, preferred_element_type=jnp.float32
    )
    return (grad_gate_w, grad_up_w, grad_down, grad_rows_in)


def on_device_general(
    layer_input,
    gain_one,
    attn_in,
    rel_bias,
    attn_out,
    gain_two,
    router,
    expert_gate,
    expert_up,
    expert_down,
    routes,
    piece_starts,
    grad_out,
):
    tok_count = layer_input.shape[1]
    model_width = layer_input.shape[0]
    heads_here = rel_bias.shape[1]
    head_width = attn_in.shape[1] // heads_here
    seqs_here = piece_starts.shape[0]
    local_experts = expert_gate.shape[0]
    part_rows = CAP // lax.axis_size("tensor")
    share_start = lax.axis_index("tensor") * part_rows
    tokens = layer_input.T.astype(jnp.float32)
    scale_one, normed = norm_forward(tokens, gain_one, model_width)
    project = jnp.einsum("td,chd->cth", normed, attn_in, preferred_element_type=jnp.float32).astype(
        jnp.bfloat16
    )
    by_seq = project.reshape(3, seqs_here, SEQ, heads_here, head_width)
    onehot_line = bucket_onehot()
    bias_full = expand_line(jnp.dot(onehot_line, rel_bias, precision=HIGH).T)
    mixed_heads, log_total = lax.map(
        partial(attend_forward, bias_full), (by_seq[0], by_seq[1], by_seq[2], piece_starts)
    )
    mixed_heads = mixed_heads.reshape(tok_count, heads_here * head_width)
    resid = tokens + reduce_heads(
        jnp.dot(mixed_heads, attn_out, preferred_element_type=jnp.float32)
    )
    scale_two, normed_two = norm_forward(resid, gain_two, model_width)
    logits = jnp.dot(normed_two, router, preferred_element_type=jnp.float32)
    chosen = (routes[:, :, None] == jnp.arange(EXPERTS, dtype=jnp.int32)[None, None, :]).astype(
        jnp.float32
    )
    picked = jnp.sum(chosen * logits[:, None, :], axis=2)
    gate_weights = jax.nn.softmax(picked, axis=1)
    slot_index, kept_pairs = slot_table(routes)
    keep_float = kept_pairs.astype(jnp.float32)
    mix_weight = gate_weights * keep_float
    safe_index = jnp.minimum(slot_index, EXPERTS * CAP - 1)
    token_rows = jnp.repeat(normed_two, TOP, axis=0)
    buffer = (
        jnp.zeros((EXPERTS * CAP + 1, model_width), jnp.bfloat16)
        .at[slot_index.reshape(-1)]
        .set(token_rows)
    )
    buffer = buffer[: EXPERTS * CAP].reshape(-1, local_experts, CAP, model_width)
    received = lax.all_to_all(buffer, "expert", split_axis=0, concat_axis=0, tiled=True)
    gate_part, up_part, hidden, partial_out = expert_forward(
        received, expert_gate, expert_up, expert_down
    )
    returned = spread_slots(owner_exchange(expert_sums(partial_out).astype(jnp.bfloat16)))
    flat_ret = returned.reshape(EXPERTS * CAP, model_width)
    fetched = flat_ret[safe_index].astype(jnp.float32)
    output = resid + jnp.sum(mix_weight[:, :, None] * fetched, axis=1)
    grad_y = grad_out.T.astype(jnp.float32)
    grad_gates = jnp.sum(grad_y[:, None, :] * fetched, axis=2) * keep_float
    grad_picked = gate_weights * (
        grad_gates - jnp.sum(gate_weights * grad_gates, axis=1, keepdims=True)
    )
    grad_logits = jnp.sum(chosen * grad_picked[:, :, None], axis=1)
    grad_router = jnp.dot(normed_two.astype(jnp.float32).T, grad_logits, precision=HIGH)
    grad_normed_two = jnp.dot(grad_logits, router.astype(jnp.float32).T, precision=HIGH)
    slot_grads = (mix_weight[:, :, None] * grad_y[:, None, :]).astype(jnp.bfloat16)
    grad_ret = (
        jnp.zeros((EXPERTS * CAP + 1, model_width), jnp.bfloat16)
        .at[slot_index.reshape(-1)]
        .set(slot_grads.reshape(-1, model_width))
    )
    grad_ret = grad_ret[: EXPERTS * CAP].reshape(-1, local_experts, CAP, model_width)
    grad_share = lax.dynamic_slice_in_dim(grad_ret, share_start, part_rows, 2)
    grad_rows_out = spread_slots(owner_exchange(grad_share))
    grad_expert_gate, grad_expert_up, grad_expert_down, grad_rows_in = expert_backward(
        received, gate_part, up_part, hidden, grad_rows_out, expert_gate, expert_up, expert_down
    )
    grad_back = spread_slots(owner_exchange(expert_sums(grad_rows_in).astype(jnp.bfloat16)))
    flat_back = grad_back.reshape(EXPERTS * CAP, model_width).astype(jnp.float32)
    grad_normed_two = grad_normed_two + jnp.sum(
        flat_back[safe_index] * keep_float[:, :, None], axis=1
    )
    grad_gain_two, grad_resid = norm_backward(
        resid, scale_two, gain_two, grad_normed_two, model_width
    )
    grad_resid = grad_resid + grad_y
    grad_attn = grad_resid.astype(jnp.bfloat16)
    grad_attn_out = jnp.einsum(
        "th,td->hd", mixed_heads, grad_attn, preferred_element_type=jnp.float32
    )
    grad_mixed = jnp.einsum(
        "td,hd->th", grad_attn, attn_out, preferred_element_type=jnp.float32
    ).astype(jnp.bfloat16)
    grad_by_seq = grad_mixed.reshape(seqs_here, SEQ, heads_here, head_width)
    bias_grad_full, grad_project = lax.scan(
        partial(attend_backward, bias_full),
        jnp.zeros_like(bias_full),
        (by_seq[0], by_seq[1], by_seq[2], grad_by_seq, piece_starts, log_total),
    )
    grad_project = (
        jnp.moveaxis(grad_project, 1, 0)
        .reshape(3, tok_count, heads_here * head_width)
        .astype(jnp.bfloat16)
    )
    grad_attn_in = jnp.einsum(
        "cth,td->chd", grad_project, normed, preferred_element_type=jnp.float32
    )
    grad_normed = reduce_heads(
        jnp.einsum("cth,chd->td", grad_project, attn_in, preferred_element_type=jnp.float32)
    )
    grad_gain_one, grad_tokens = norm_backward(
        tokens, scale_one, gain_one, grad_normed, model_width
    )
    grad_tokens = grad_tokens + grad_resid
    grad_rel_bias = jnp.dot(onehot_line.T, fold_line(bias_grad_full).T, precision=HIGH)
    shared = (
        lax.psum(grad_gain_one.astype(jnp.bfloat16), "expert").astype(jnp.float32),
        lax.psum(grad_attn_in.astype(jnp.bfloat16), "expert").astype(jnp.float32),
        lax.psum(grad_rel_bias.astype(jnp.bfloat16), "expert").astype(jnp.float32),
        lax.psum(grad_attn_out.astype(jnp.bfloat16), "expert").astype(jnp.float32),
        lax.psum(grad_gain_two.astype(jnp.bfloat16), "expert").astype(jnp.float32),
        lax.psum(grad_router.astype(jnp.bfloat16), "expert").astype(jnp.float32),
    )
    return (
        output.astype(jnp.bfloat16).T,
        grad_tokens.T,
        shared[0],
        shared[1],
        shared[2],
        shared[3],
        shared[4],
        shared[5],
        grad_expert_gate,
        grad_expert_up,
        grad_expert_down,
    )


def solution(mesh):
    placed = (
        P(None, "expert"),
        P(),
        P(None, "tensor", None),
        P(None, "tensor"),
        P("tensor", None),
        P(),
        P(),
        P("expert", "tensor", None),
        P("expert", "tensor", None),
        P("expert", "tensor", None),
        P("expert", None),
        P("expert", None),
        P(None, "expert"),
    )
    paired = mesh.shape["tensor"] == 4 and mesh.shape["expert"] * 2 == EXPERTS
    return jax.shard_map(
        on_device if paired else on_device_general,
        mesh=mesh,
        in_specs=placed,
        out_specs=(
            P(None, "expert"),
            P(None, "expert"),
            P(),
            P(None, "tensor", None),
            P(None, "tensor"),
            P("tensor", None),
            P(),
            P(),
            P("expert", "tensor", None),
            P("expert", "tensor", None),
            P("expert", "tensor", None),
        ),
        check_vma=False,
    )
```

```python
from functools import partial

import jax
import jax.numpy as jnp
from jax import lax
from jax.experimental import pallas as pl
from jax.experimental.pallas import tpu as pltpu
from jax.sharding import PartitionSpec as P

EXPERTS = 16
BUCKETS = 32
TOP = 2
PIECE = 256
SEQ = 1024
CAP = 320
BLK = 256


EPS = 1e-06
NEG = -1e30
THRESHOLDS = (12, 16, 23, 32, 46, 64, 91)
HIGH = lax.Precision.HIGHEST
F32 = jnp.float32
BF16 = jnp.bfloat16
NN = (((1,), (0,)), ((), ()))
NT = (((1,), (1,)), ((), ()))
TN = (((0,), (0,)), ((), ()))
MIB = 1 << 20


def mm(left, right, dims=NN):
    return lax.dot_general(left, right, dims, preferred_element_type=F32)


def params(limit=56):
    return pltpu.CompilerParams(vmem_limit_bytes=limit * MIB)


def cost(flops, bytes_accessed, transcendentals=0):
    return pl.CostEstimate(
        flops=int(flops), bytes_accessed=int(bytes_accessed), transcendentals=int(transcendentals)
    )


def bucket_of(offset):
    magnitude = jnp.abs(offset)
    beyond = sum(((magnitude >= threshold).astype(jnp.int32) for threshold in THRESHOLDS))
    lower_part = jnp.where(magnitude < 8, magnitude, 8 + beyond)
    return lower_part + 16 * (offset > 0).astype(jnp.int32)


def project_kernel(x_ref, gain_ref, w_ref, out_ref, scale_ref):
    x = x_ref[...].astype(F32)
    scale = lax.rsqrt(jnp.sum(x * x, axis=0, keepdims=True) / x.shape[0] + EPS)
    normed = (x * scale * gain_ref[...]).astype(BF16)
    out_ref[...] = mm(w_ref[...], normed).astype(BF16)
    scale_ref[...] = scale


def project(x, gain, weights):
    width, tokens = x.shape
    rows = weights.shape[0]
    tile = 512
    return pl.pallas_call(
        project_kernel,
        grid=(tokens // tile,),
        in_specs=[
            pl.BlockSpec((width, tile), lambda i: (0, i)),
            pl.BlockSpec((width, 1), lambda i: (0, 0)),
            pl.BlockSpec((rows, width), lambda i: (0, 0)),
        ],
        out_specs=[
            pl.BlockSpec((rows, tile), lambda i: (0, i)),
            pl.BlockSpec((1, tile), lambda i: (0, i)),
        ],
        out_shape=[
            jax.ShapeDtypeStruct((rows, tokens), BF16),
            jax.ShapeDtypeStruct((1, tokens), F32),
        ],
        compiler_params=params(),
        cost_estimate=cost(2 * width * tokens * rows, 2 * width * tokens * 2),
    )(x, gain, weights)


def line_offsets(number):
    column = lax.broadcasted_iota(jnp.int32, (8, BLK), 1)
    return (number - 1) * BLK - column


def bias_tiles_kernel(table_ref, tiles_ref):
    row = lax.broadcasted_iota(jnp.int32, (BLK, BLK), 0)
    column = lax.broadcasted_iota(jnp.int32, (BLK, BLK), 1)
    buckets = [bucket_of(line_offsets(number)) for number in range(4)]
    for head in range(tiles_ref.shape[0]):
        far = table_ref[15, head]
        rolled = []
        for number, bucket in enumerate(buckets):
            value = jnp.zeros((8, BLK), F32)
            for index in range(BUCKETS):
                value = jnp.where(bucket == index, table_ref[index, head] - far, value)
            whole = jnp.broadcast_to(value[0:1], (BLK, BLK))
            rolled.append(pltpu.roll(whole, 0, 1, stride=1, stride_axis=0))
        for number in range(3):
            tiles_ref[head, number] = jnp.where(column >= row, rolled[number], rolled[number + 1])


def bias_tiles(table):
    heads = table.shape[1]
    return pl.pallas_call(
        bias_tiles_kernel,
        in_specs=[pl.BlockSpec(memory_space=pltpu.SMEM)],
        out_specs=pl.BlockSpec(memory_space=pltpu.VMEM),
        out_shape=jax.ShapeDtypeStruct((heads, 3, BLK, BLK), F32),
        compiler_params=params(),
        cost_estimate=cost(heads * 3 * BLK * BLK * 60, heads * 3 * BLK * BLK * 4),
    )(table)


def bias_fold(near_ref, far_ref):
    heads = near_ref.shape[0] // 2
    columns = []
    row = lax.broadcasted_iota(jnp.int32, (BLK, BLK), 0)
    column = lax.broadcasted_iota(jnp.int32, (BLK, BLK), 1)
    flip = jnp.where(row + column == BLK - 1, 1.0, 0.0).astype(BF16)
    apart = jnp.where(column == BLK - 1, 0, column + 1)
    ahead = apart <= row
    number_at = lax.broadcasted_iota(jnp.int32, (BUCKETS, BLK), 0)
    for head in range(heads):
        lines = [jnp.zeros((1, BLK), F32) for _ in range(4)]
        for number in range(3):
            grads = near_ref[head, number] + near_ref[heads + head, number]
            coarse = grads.astype(BF16)
            fine = (grads - coarse.astype(F32)).astype(BF16)
            flipped = mm(flip, coarse) + mm(flip, fine)
            rolled = pltpu.roll(flipped, 0, 1, stride=1, stride_axis=0)
            lines[number] += jnp.sum(jnp.where(ahead, rolled, 0.0), axis=0, keepdims=True)
            lines[number + 1] += jnp.sum(jnp.where(ahead, 0.0, rolled), axis=0, keepdims=True)
        total = jnp.zeros((BUCKETS, 1), F32)
        for number, line in enumerate(lines):
            bucket = bucket_of((number - 1) * BLK - apart[:1])
            total += jnp.sum(jnp.where(bucket == number_at, line, 0.0), axis=1, keepdims=True)
        distant = jnp.sum(far_ref[head] + far_ref[heads + head], axis=0, keepdims=True)
        distant = jnp.sum(distant, axis=1, keepdims=True)
        total += jnp.where(number_at[:, :1] == 15, distant, 0.0)
        columns.append(total)
    return columns


def key_count(query_block):
    return 2 * BLK if query_block < 2 else 4 * BLK


def block_scores(keys, queries, tiles_ref, limit, block):
    count = key_count(block)
    parts = []
    whole = mm(keys[:, :count], queries, TN)
    for key_block in range(count // BLK):
        part = whole[key_block * BLK : (key_block + 1) * BLK]
        shift = key_block - block
        if -1 <= shift <= 1:
            part = part + tiles_ref[0, shift + 1]
        if shift >= 0:
            key_at = lax.broadcasted_iota(jnp.int32, (BLK, BLK), 0) + key_block * BLK
            part = jnp.where(key_at <= limit, part, NEG)
        parts.append(part)
    return jnp.concatenate(parts, axis=0)


def attend_kernel(q_ref, k_ref, v_ref, tiles_ref, limit_ref, w_ref, out_ref, lse_ref, sent_ref, held):
    head = pl.program_id(1)
    width = q_ref.shape[0]
    queries = q_ref[...] * BF16(0.125)
    keys, values = k_ref[...], v_ref[...]
    for block in range(SEQ // BLK):
        cols = slice(block * BLK, (block + 1) * BLK)
        scores = block_scores(keys, queries[:, cols], tiles_ref, limit_ref[0, :, cols], block)
        top = jnp.max(scores, axis=0, keepdims=True)
        exponent = jnp.exp(scores - top)
        total = jnp.sum(exponent, axis=0, keepdims=True)
        mixed = mm(values[:, : key_count(block)], exponent.astype(BF16)) / total
        mixed = mixed.astype(BF16)
        out_ref[:, cols] = mixed
        held[pl.ds(pl.multiple_of(head * width, width), width), cols] = mixed
        lse_ref[0, :, cols] = top + jnp.log(total)

    @pl.when(head == pl.num_programs(1) - 1)
    def _():
        sent_ref[...] = mm(held[...], w_ref[...], TN).astype(BF16)


def attend(qkv, tiles, limits, attn_out):
    heads = tiles.shape[0]
    seqs = limits.shape[0]
    width = qkv.shape[0] // (3 * heads)
    model_width = attn_out.shape[1]
    return pl.pallas_call(
        attend_kernel,
        grid=(seqs, heads),
        in_specs=[
            pl.BlockSpec((width, SEQ), lambda s, h: (h, s)),
            pl.BlockSpec((width, SEQ), lambda s, h: (heads + h, s)),
            pl.BlockSpec((width, SEQ), lambda s, h: (2 * heads + h, s)),
            pl.BlockSpec((1, 3, BLK, BLK), lambda s, h: (h, 0, 0, 0)),
            pl.BlockSpec((1, 1, SEQ), lambda s, h: (s, 0, 0)),
            pl.BlockSpec((heads * width, model_width), lambda s, h: (0, 0)),
        ],
        out_specs=[
            pl.BlockSpec((width, SEQ), lambda s, h: (h, s)),
            pl.BlockSpec((1, 1, SEQ), lambda s, h: (s * heads + h, 0, 0)),
            pl.BlockSpec((SEQ, model_width), lambda s, h: (s, 0)),
        ],
        out_shape=[
            jax.ShapeDtypeStruct((heads * width, seqs * SEQ), BF16),
            jax.ShapeDtypeStruct((seqs * heads, 1, SEQ), F32),
            jax.ShapeDtypeStruct((seqs * SEQ, model_width), BF16),
        ],
        scratch_shapes=[pltpu.VMEM((heads * width, SEQ), BF16)],
        compiler_params=params(),
        cost_estimate=cost(seqs * heads * SEQ * SEQ * 512, seqs * heads * SEQ * 2048, seqs * heads * SEQ * SEQ),
    )(qkv, qkv, qkv, tiles, limits, attn_out)


def attend_back_kernel(
    q_ref, k_ref, v_ref, tiles_ref, limit_ref, w_ref, grad_ref, lse_ref, part_ref, resid_ref,
    dq_ref, dk_ref, dv_ref, near_ref, far_ref, y_ref,
    held, parts, turn_across, turn_along, from_across, from_along, sends, recvs, loads,
):
    rank = lax.axis_index("tensor")
    pair_class, half_index = rank % 2, rank // 2
    across, along, corner = rank + 1 - 2 * pair_class, rank + 2 - 4 * half_index, 3 - rank
    step = pl.program_id(0) * pl.num_programs(1) + pl.program_id(1)
    mesh_ids = pl.DeviceIdType.MESH
    middle = parts.shape[2] // 2
    low, high = slice(0, middle), slice(middle, 2 * middle)

    def remote(number, origin, target, other):
        return pltpu.make_async_remote_copy(
            src_ref=origin, dst_ref=target, send_sem=sends.at[number], recv_sem=recvs.at[number],
            device_id={"tensor": other}, device_id_type=mesh_ids,
        )

    first = (
        remote(0, part_ref.at[corner, :, low], turn_across, across),
        remote(1, part_ref.at[corner, :, high], turn_along, along),
    )
    second = remote(2, parts.at[0], from_across, across), remote(3, parts.at[1], from_along, along)
    local = [
        pltpu.make_async_copy(part_ref.at[other], parts.at[number], loads.at[number])
        for number, other in enumerate((across, along, rank))
    ]
    local.append(pltpu.make_async_copy(resid_ref, y_ref, loads.at[3]))

    @pl.when(step == 0)
    def _():
        barrier = pltpu.get_barrier_semaphore()
        for other in (across, along):
            pl.semaphore_signal(barrier, inc=1, device_id={"tensor": other}, device_id_type=mesh_ids)
        pl.semaphore_wait(barrier, 2)
        for copy in first:
            copy.start()
        for copy in local:
            copy.start()

    @pl.when(step == 3)
    def _():
        for copy in (*first, *local):
            copy.wait()
        parts[0, :, high] = (parts[0, :, high].astype(F32) + turn_along[...].astype(F32)).astype(BF16)
        parts[1, :, low] = (parts[1, :, low].astype(F32) + turn_across[...].astype(F32)).astype(BF16)
        for copy in second:
            copy.start()

    head = pl.program_id(1)
    width = q_ref.shape[0]

    @pl.when(head == 0)
    def _():
        held[...] = mm(w_ref[...], grad_ref[...], NT).astype(BF16)

    queries = q_ref[...] * BF16(0.125)
    keys, values = k_ref[...], v_ref[...]
    grads = held[pl.ds(pl.multiple_of(head * width, width), width), :]
    near_ref[...] = jnp.zeros_like(near_ref)
    far = jnp.zeros((8, BLK), F32)
    grad_keys = jnp.zeros((width, SEQ), F32)
    grad_values = jnp.zeros((width, SEQ), F32)
    for block in range(SEQ // BLK):
        count = key_count(block)
        cols = slice(block * BLK, (block + 1) * BLK)
        scores = block_scores(keys, queries[:, cols], tiles_ref, limit_ref[0, :, cols], block)
        probs = jnp.exp(scores - lse_ref[0, :, cols])
        grad_probs = mm(values[:, :count], grads[:, cols], TN)
        inner = jnp.sum(probs * grad_probs, axis=0, keepdims=True)
        grad_scores = probs * (grad_probs - inner)
        for key_block in range(count // BLK):
            part = grad_scores[key_block * BLK : (key_block + 1) * BLK]
            shift = key_block - block
            if -1 <= shift <= 1:
                near_ref[0, shift + 1] += part
            elif shift < -1:
                far = far + jnp.sum(part.reshape(BLK // 8, 8, BLK), axis=0)
        rounded = grad_scores.astype(BF16)
        add_values = mm(grads[:, cols], probs.astype(BF16), NT)
        add_keys = mm(queries[:, cols], rounded, NT)
        if count == SEQ:
            grad_values = grad_values + add_values
            grad_keys = grad_keys + add_keys
        else:
            filler = jnp.zeros((width, SEQ - count), F32)
            grad_values = grad_values + jnp.concatenate([add_values, filler], axis=1)
            grad_keys = grad_keys + jnp.concatenate([add_keys, filler], axis=1)
        dq_ref[:, cols] = (mm(keys[:, :count], rounded) * 0.125).astype(BF16)
    dk_ref[...] = grad_keys.astype(BF16)
    dv_ref[...] = grad_values.astype(BF16)
    far_ref[0] = far

    @pl.when(step == 7)
    def _():
        for copy in second:
            copy.wait()
        y_ref[...] += parts[2].astype(F32) + from_across[...].astype(F32) + from_along[...].astype(F32)


def attend_back(qkv, tiles, limits, attn_out, grad_attn, lse, part, resid):
    heads = tiles.shape[0]
    seqs = limits.shape[0]
    width = qkv.shape[0] // (3 * heads)
    model_width = attn_out.shape[1]
    share = part.shape[1]
    grad_spec = pl.BlockSpec((width, SEQ), lambda s, h: (h, s))
    anywhere = pl.BlockSpec(memory_space=pl.ANY)
    return pl.pallas_call(
        attend_back_kernel,
        grid=(seqs, heads),
        in_specs=[
            pl.BlockSpec((width, SEQ), lambda s, h: (h, s)),
            pl.BlockSpec((width, SEQ), lambda s, h: (heads + h, s)),
            pl.BlockSpec((width, SEQ), lambda s, h: (2 * heads + h, s)),
            pl.BlockSpec((1, 3, BLK, BLK), lambda s, h: (h, 0, 0, 0)),
            pl.BlockSpec((1, 1, SEQ), lambda s, h: (s, 0, 0)),
            pl.BlockSpec((heads * width, model_width), lambda s, h: (0, 0)),
            pl.BlockSpec((SEQ, model_width), lambda s, h: (s, 0)),
            pl.BlockSpec((1, 1, SEQ), lambda s, h: (s * heads + h, 0, 0)),
        ]
        + [anywhere] * 2,
        out_specs=[
            grad_spec,
            grad_spec,
            grad_spec,
            pl.BlockSpec((1, 3, BLK, BLK), lambda s, h: (s * heads + h, 0, 0, 0)),
            pl.BlockSpec((1, 8, BLK), lambda s, h: (s * heads + h, 0, 0)),
            pl.BlockSpec((share, model_width), lambda s, h: (0, 0)),
        ],
        out_shape=[jax.ShapeDtypeStruct((heads * width, seqs * SEQ), BF16)] * 3
        + [
            jax.ShapeDtypeStruct((seqs * heads, 3, BLK, BLK), F32),
            jax.ShapeDtypeStruct((seqs * heads, 8, BLK), F32),
        ]
        + [jax.ShapeDtypeStruct((share, model_width), F32)],
        scratch_shapes=[
            pltpu.VMEM((heads * width, SEQ), BF16),
            pltpu.VMEM((3, share, model_width), BF16),
            pltpu.VMEM((share, model_width // 2), BF16),
            pltpu.VMEM((share, model_width // 2), BF16),
            pltpu.VMEM((share, model_width), BF16),
            pltpu.VMEM((share, model_width), BF16),
            pltpu.SemaphoreType.DMA((4,)),
            pltpu.SemaphoreType.DMA((4,)),
            pltpu.SemaphoreType.DMA((4,)),
        ],
        compiler_params=pltpu.CompilerParams(
            vmem_limit_bytes=60 * MIB, collective_id=5, has_side_effects=True
        ),
        cost_estimate=cost(seqs * heads * SEQ * SEQ * 1280, seqs * heads * SEQ * 4096, seqs * heads * SEQ * SEQ),
    )(qkv, qkv, qkv, tiles, limits, attn_out, grad_attn, lse, part, resid)


def project_back_kernel(
    place_ref, x_ref, gain_ref, scale_ref, w_ref, mixed_ref, attn_ref, dq_ref, dk_ref, dv_ref, *refs
):
    step = pl.program_id(0)
    own_refs, got_refs, (weight_ref, out_ref, gain_grad_ref), placed_refs, total = (
        refs[:2], refs[2:4], refs[4:7], refs[7:9], refs[9]
    )
    for own_ref, got_ref, placed_ref in zip(own_refs, got_refs, placed_refs):
        placed_ref[place_ref[0]] = own_ref[...]
        placed_ref[1 - place_ref[0]] = got_ref[...].astype(F32)
    grads = jnp.concatenate([dq_ref[...], dk_ref[...], dv_ref[...]], axis=0)
    rows = grads.shape[0]
    scaled = x_ref[...].astype(F32) * scale_ref[...]

    @pl.when(step == 0)
    def _():
        total[...] = jnp.zeros_like(total)
        gain_grad_ref[...] = jnp.zeros_like(gain_grad_ref)

    total[:rows] += mm(grads, (scaled * gain_ref[...]).astype(BF16), NT)
    total[rows:] += mm(mixed_ref[...], attn_ref[...])
    back = mm(w_ref[...], grads, TN)
    gain_grad_ref[...] += jnp.sum(back * scaled, axis=1, keepdims=True)
    out_ref[...] = back.T.astype(BF16)

    @pl.when(step == pl.num_programs(0) - 1)
    def _():
        weight_ref[...] = total[...].astype(BF16)


def project_back(place, x, gain, scale, weights, mixed, grad_attn, grads, owns, gots):
    width, tokens = x.shape
    rows = weights.shape[0]
    heads_width = mixed.shape[0]
    units = owns[0].shape[0]
    steps = 4
    tile = tokens // steps
    part = units // steps
    column = lambda count: pl.BlockSpec((count, tile), lambda i: (0, i))
    return pl.pallas_call(
        project_back_kernel,
        grid=(steps,),
        in_specs=[
            pl.BlockSpec(memory_space=pltpu.SMEM),
            column(width),
            pl.BlockSpec((width, 1), lambda i: (0, 0)),
            column(1),
            pl.BlockSpec((rows, width), lambda i: (0, 0)),
            column(heads_width),
            pl.BlockSpec((tile, width), lambda i: (i, 0)),
        ]
        + [column(rows // 3)] * 3
        + [pl.BlockSpec((part, width), lambda i: (i, 0))] * 4,
        out_specs=[
            pl.BlockSpec((rows + heads_width, width), lambda i: (0, 0)),
            pl.BlockSpec((tile, width), lambda i: (i, 0)),
            pl.BlockSpec((width, 1), lambda i: (0, 0)),
        ]
        + [pl.BlockSpec((2, part, width), lambda i: (0, i, 0))] * 2,
        out_shape=[
            jax.ShapeDtypeStruct((rows + heads_width, width), BF16),
            jax.ShapeDtypeStruct((tokens, width), BF16),
            jax.ShapeDtypeStruct((width, 1), F32),
        ]
        + [jax.ShapeDtypeStruct((2, units, width), F32)] * 2,
        scratch_shapes=[pltpu.VMEM((rows + heads_width, width), F32)],
        compiler_params=params(),
        cost_estimate=cost(5 * width * tokens * rows, 6 * width * tokens + 14 * units * width),
    )(place, x, gain, scale, weights, mixed, grad_attn, *grads, *owns, *gots)


def exchange(math, rank, source, full, from_across, from_along, to_across, to_along, turn_across, turn_along, sends, recvs, ready=None, ready_full=None, side=None, peers=(), fill=None, start=None, cut=None):
    pair_class, half_index = rank % 2, rank // 2
    across, along, corner = rank + 1 - 2 * pair_class, rank + 2 - 4 * half_index, 3 - rank
    mesh_ids = pl.DeviceIdType.MESH
    rows, width = source.shape[1:]
    chunks = 4
    size = rows // chunks
    cut = cut or width // 2
    low, high = slice(0, cut), slice(cut, width)
    barrier = pltpu.get_barrier_semaphore()
    for other in (across, along):
        pl.semaphore_signal(barrier, inc=1, device_id={"tensor": other}, device_id_type=mesh_ids)
    for other in peers:
        pl.semaphore_signal(barrier, inc=1, device_id={"expert": other}, device_id_type=mesh_ids)
    pl.semaphore_wait(barrier, 2 + len(peers))

    def remote(kind, chunk, origin, target, other):
        return pltpu.make_async_remote_copy(
            src_ref=origin, dst_ref=target, send_sem=sends.at[kind, chunk], recv_sem=recvs.at[kind, chunk],
            device_id={"tensor": other}, device_id_type=mesh_ids,
        )

    if start:
        start()
    if fill:
        fill(corner)
    spans = [slice(chunk * size, (chunk + 1) * size) for chunk in range(chunks)]
    first, second, third, fourth = [], [], [], []
    for chunk, span in enumerate(spans):
        pair = (
            remote(0, chunk, source.at[corner, span, low], turn_across.at[span, low], across),
            remote(1, chunk, source.at[corner, span, high], turn_along.at[span, high], along),
        )
        for copy in pair:
            copy.start()
        first.append(pair)
    if fill:
        fill(along)
        fill(across)
    if ready is not None:
        ready_full[rank] = ready[...]
        extra = [
            remote(8, 0, ready, ready_full.at[rank], across),
            remote(8, 1, ready, ready_full.at[rank], along),
            remote(8, 2, ready_full.at[along, :, low], ready_full.at[along, :, low], across),
            remote(8, 3, ready_full.at[across, :, high], ready_full.at[across, :, high], along),
        ]
        for copy in extra[:2]:
            copy.start()
    for chunk, span in enumerate(spans):
        if side:
            side(chunk)
        first[chunk][0].wait()
        to_along[span, low] = (source[along, span, low].astype(F32) + turn_across[span, low].astype(F32)).astype(BF16)
        to_along[span, high] = source[along, span, high]
        first[chunk][1].wait()
        to_across[span, low] = source[across, span, low]
        to_across[span, high] = (source[across, span, high].astype(F32) + turn_along[span, high].astype(F32)).astype(BF16)
        pair = (
            remote(2, chunk, to_across.at[span], from_across.at[span], across),
            remote(3, chunk, to_along.at[span], from_along.at[span], along),
        )
        for copy in pair:
            copy.start()
        second.append(pair)
    if ready is not None:
        for copy in extra[:2]:
            copy.wait()
        for copy in extra[2:]:
            copy.start()

    def pass_on(chunk):
        span = spans[chunk]
        for copy in third[chunk]:
            copy.wait()
        pair = (
            remote(6, chunk, full.at[along, span, low], full.at[along, span, low], across),
            remote(7, chunk, full.at[across, span, high], full.at[across, span, high], along),
        )
        for copy in pair:
            copy.start()
        fourth.append(pair)

    if fill:
        fill(rank)
    for chunk, span in enumerate(spans):
        if side:
            side(chunks + chunk)
        for copy in second[chunk]:
            copy.wait()
        total = source[rank, span].astype(F32) + from_across[span].astype(F32) + from_along[span].astype(F32)
        full[rank, span] = math(span, total).astype(BF16)
        pair = (
            remote(4, chunk, full.at[rank, span], full.at[rank, span], across),
            remote(5, chunk, full.at[rank, span], full.at[rank, span], along),
        )
        for copy in pair:
            copy.start()
        third.append(pair)
        if chunk:
            pass_on(chunk - 1)
    pass_on(chunks - 1)
    if ready is not None:
        for copy in extra[2:]:
            copy.wait()
    for pair in fourth:
        for copy in pair:
            copy.wait()
    if side:
        side(2 * chunks)


def exchange_call(kernel, number, shape, operands, extra_shapes, scratch=()):
    tokens, width = shape
    ranks = 4
    rows = tokens // ranks
    here = pl.BlockSpec(memory_space=pltpu.VMEM)
    results = pl.pallas_call(
        kernel,
        in_specs=[here] * len(operands),
        out_specs=[here] * (1 + len(extra_shapes)),
        out_shape=[jax.ShapeDtypeStruct((ranks, rows, width), BF16)]
        + [jax.ShapeDtypeStruct(shape, kind) for shape, kind in extra_shapes],
        scratch_shapes=[pltpu.VMEM((rows, width), BF16)] * 6
        + [pltpu.SemaphoreType.DMA((9, 4))] * 2
        + list(scratch),
        compiler_params=pltpu.CompilerParams(
            vmem_limit_bytes=60 * MIB, collective_id=number, has_side_effects=True
        ),
        cost_estimate=cost(40 * MIB, 200 * MIB),
    )(*operands)
    return results[0].reshape(tokens, width), *results[1:]


def norm_two_kernel(source, x_ref, gain_ref, grad_out_ref, code_ref, full, resid_ref, scale_ref, dy_ref, dy_rows_ref, *rest):
    def math(span, total):
        resid = x_ref[span, :].astype(F32) + total
        scale = lax.rsqrt(jnp.sum(resid * resid, axis=1, keepdims=True) / resid.shape[1] + EPS)
        resid_ref[span, :] = resid
        scale_ref[span, :] = scale
        return resid * scale * gain_ref[...]

    ranks, rows, width = source.shape
    slots = dy_rows_ref.shape[0] // ranks

    def side(number):
        if number < ranks:
            span = slice(number * rows, (number + 1) * rows)
            dy_ref[span, :] = grad_out_ref[:, span].astype(F32).T.astype(BF16)
        elif number < 2 * ranks:
            start = (number - ranks) * slots
            slot = lax.broadcasted_iota(jnp.int32, (slots, dy_ref.shape[0]), 0) + start
            take = jnp.where((slot == code_ref[0:1]) | (slot == code_ref[1:2]), 1.0, 0.0).astype(BF16)
            dy_rows_ref[start : start + slots, :] = mm(take, dy_ref[...]).astype(BF16)

    exchange(math, lax.axis_index("tensor"), source, full, *rest, side=side)


def norm_back(grad, value, scale, gain):
    scaled = grad * gain
    inner = jnp.sum(scaled * value, axis=1, keepdims=True)
    return scale * scaled - value * (scale * scale * scale) * (inner / value.shape[1])


def norm_two_back_kernel(
    ret_ref, back_ref, code_ref, codes_ref, gates_ref, routes_ref, dy_rows_ref, gate_ref, router_ref, h_ref,
    resid_ref, scale_ref, dy_ref, gain_ref, full, grad_ref, gain_grad_ref, router_grad_ref, y_ref, *rest,
):
    source, scaled, logit_parts = rest[-3:]
    rank = lax.axis_index("tensor")
    rows = source.shape[1]
    slots, tokens = ret_ref.shape[0], code_ref.shape[1]
    def start():
        found = [jnp.zeros((1, tokens), F32) for _ in range(TOP)]
        tile = slots // 4
        for begin in range(0, slots, tile):
            span = slice(begin, begin + tile)
            ret = ret_ref[span, :].astype(F32)
            slot_grad = jnp.sum(dy_rows_ref[span, :].astype(F32) * ret, axis=1, keepdims=True)
            scaled[span, :] = (ret * gate_ref[span, :]).astype(BF16)
            slot = lax.broadcasted_iota(jnp.int32, (tile, tokens), 0) + begin
            for i in range(TOP):
                found[i] = found[i] + jnp.sum(
                    jnp.where(slot == code_ref[i : i + 1, :], slot_grad, 0.0), axis=0, keepdims=True
                )
        mean = gates_ref[0:1] * found[0] + gates_ref[1:2] * found[1]
        expert = lax.broadcasted_iota(jnp.int32, (EXPERTS, tokens), 0)
        logit = sum(
            jnp.where(routes_ref[i : i + 1] == expert, gates_ref[i : i + 1] * (found[i] - mean), 0.0)
            for i in range(TOP)
        )
        coarse = logit.astype(BF16)
        fine = (logit - coarse.astype(F32)).astype(BF16)
        for shard in range(tokens // rows):
            span = slice(shard * rows, (shard + 1) * rows)
            logit_parts[shard, :EXPERTS] = coarse[:, span]
            logit_parts[shard, EXPERTS:] = fine[:, span]

    def places(shard):
        slot = lax.broadcasted_iota(jnp.int32, (rows, slots), 1)
        codes = codes_ref[pl.ds(pl.multiple_of(shard * rows, rows), rows), :]
        return jnp.where((slot == codes[:, 0:1]) | (slot == codes[:, 1:2]), 1.0, 0.0).astype(BF16)

    def fill(shard):
        value = mm(places(shard), back_ref[...])
        both = jnp.concatenate([router_ref[...], router_ref[...]], axis=0)
        source[shard] = (value + mm(logit_parts[shard], both, TN)).astype(BF16)

    def side(number):
        shards = tokens // rows
        if number < shards:
            y_ref[number * rows : (number + 1) * rows, :] = mm(places(number), scaled[...]).astype(BF16)
        elif number == shards:
            router_grad_ref[...] = sum(
                mm(logit_parts[shard, :EXPERTS], h_ref[shard * rows : (shard + 1) * rows, :])
                for shard in range(shards)
            )

    gain_grad_ref[...] = jnp.zeros_like(gain_grad_ref)

    def math(span, total):
        resid, scale = resid_ref[span, :], scale_ref[span, :]
        gain_grad_ref[...] += jnp.sum(total * resid * scale, axis=0, keepdims=True)
        own_dy = dy_ref[pl.ds(pl.multiple_of(rank * rows + span.start, 128), span.stop - span.start), :]
        grad = norm_back(total, resid, scale, gain_ref[...]) + own_dy.astype(F32)
        grad_ref[span, :] = grad
        return grad

    exchange(math, rank, source, full, *rest[:-3], side=side, fill=fill, start=start)


def norm_one_back_kernel(
    source, x_ref, scale_ref, grad_ref, gain_ref, ready, gain_one_ref, gain_two_ref, router_ref, near_ref, far_ref,
    full, ready_full, small_out, *rest
):
    held, tensor_sends, tensor_recvs, expert_sends, expert_recvs = rest[-5:]
    rank, group = lax.axis_index("tensor"), lax.axis_index("expert")
    pair_class, half_index = rank % 2, rank // 2
    others = rank + 1 - 2 * pair_class, rank + 2 - 4 * half_index
    groups = expert_sends.shape[0]
    mesh_ids = pl.DeviceIdType.MESH
    peers = [partner_of(group, step) for step in range(1, groups)]
    summed = slice(0, small_out.shape[0] - BUCKETS)

    def math(span, total):
        x = x_ref[span, :].astype(F32)
        return norm_back(total, x, scale_ref[span, :], gain_ref[...]) + grad_ref[span, :]

    def to_rank(step):
        return pltpu.make_async_remote_copy(
            src_ref=held.at[groups + step], dst_ref=held.at[groups + 2 + step], send_sem=tensor_sends.at[step],
            recv_sem=tensor_recvs.at[step], device_id={"tensor": others[step]}, device_id_type=mesh_ids,
        )

    def to_group(step):
        return pltpu.make_async_remote_copy(
            src_ref=held.at[group], dst_ref=held.at[group], send_sem=expert_sends.at[step],
            recv_sem=expert_recvs.at[step], device_id={"expert": peers[step - 1]}, device_id_type=mesh_ids,
        )

    def side(number):
        if number == 0:
            held[groups] = jnp.zeros(small_out.shape, F32)
            held[groups, :EXPERTS] = router_ref[...]
            held[groups, EXPERTS : EXPERTS + 1] = gain_two_ref[...]
            held[groups, EXPERTS + 1 : EXPERTS + 2] = jnp.broadcast_to(gain_one_ref[...], (gain_one_ref.shape[0], 128)).T[:1]
            to_rank(0).start()
        elif number == 1:
            to_rank(0).wait()
            held[groups + 1] = held[groups] + held[groups + 2]
            to_rank(1).start()
        elif number == 2:
            to_rank(1).wait()
            for head, column in enumerate(bias_fold(near_ref, far_ref)):
                span = slice(summed.stop, summed.stop + BUCKETS)
                held[group, span, head * 128 : (head + 1) * 128] = jnp.broadcast_to(column, (BUCKETS, 128))
            held[group, summed] = held[groups + 1, summed] + held[groups + 3, summed]
            for step in range(1, groups):
                to_group(step).start()
        elif number == 8:
            for step in range(1, groups):
                to_group(step).wait()
            total = held[0]
            for step in range(1, groups):
                total = total + held[step]
            small_out[...] = total

    exchange(math, rank, source, full, *rest[:-5], ready, ready_full, side=side, peers=peers)


def code_kernel(place_ref, routes_ref, code_ref, half, groups):
    pair_class, half_index = place_ref[0], place_ref[1]
    tokens = routes_ref.shape[1]
    expert = lax.broadcasted_iota(jnp.int32, (EXPERTS, BLK), 0)
    earlier = (
        lax.broadcasted_iota(jnp.int32, (BLK, BLK), 0) < lax.broadcasted_iota(jnp.int32, (BLK, BLK), 1)
    ).astype(F32).astype(BF16)
    carry = jnp.zeros((EXPERTS, 1), F32)
    for block in range(tokens // BLK):
        cols = slice(block * BLK, (block + 1) * BLK)
        routes = routes_ref[:, cols]
        hits = [(routes[i : i + 1] == expert) for i in range(TOP)]
        chosen = sum(hit.astype(F32) for hit in hits)
        before = mm(chosen.astype(BF16), earlier) + carry
        carry = carry + jnp.sum(chosen, axis=1, keepdims=True)
        for i in range(TOP):
            slot = jnp.sum(jnp.where(hits[i], before, 0.0), axis=0, keepdims=True).astype(jnp.int32)
            route = routes[i : i + 1]
            owner = route // 2
            local = slot - half_index * half
            mine = (route - 2 * owner == pair_class) & (local >= 0) & (local < half)
            code_ref[i : i + 1, cols] = jnp.where(mine, owner * half + local, -1)


def local_codes(place, routes_t, half, groups):
    return pl.pallas_call(
        partial(code_kernel, half=half, groups=groups),
        in_specs=[
            pl.BlockSpec(memory_space=pltpu.SMEM),
            pl.BlockSpec(memory_space=pltpu.VMEM),
        ],
        out_specs=pl.BlockSpec(memory_space=pltpu.VMEM),
        out_shape=jax.ShapeDtypeStruct(routes_t.shape, jnp.int32),
        compiler_params=params(),
    )(place, routes_t)


def dispatch_kernel(code_ref, routes_ref, router_ref, h_ref, dy_rows_ref, rows_ref, grads_ref, gate_ref, gates_ref):
    count, tokens = rows_ref.shape[0], h_ref.shape[0]

    @pl.when(pl.program_id(0) == 0)
    def _():
        expert = lax.broadcasted_iota(jnp.int32, (EXPERTS, tokens), 0)
        logits = mm(router_ref[...], h_ref[...], NT)
        picked = [
            jnp.sum(jnp.where(routes_ref[i : i + 1] == expert, logits, 0.0), axis=0, keepdims=True)
            for i in range(TOP)
        ]
        top = jnp.maximum(picked[0], picked[1])
        raised = [jnp.exp(value - top) for value in picked]
        total = raised[0] + raised[1]
        for i in range(TOP):
            gates_ref[i : i + 1] = raised[i] / total

    slot = lax.broadcasted_iota(jnp.int32, (count, tokens), 0) + pl.program_id(0) * count
    hits = [slot == code_ref[i : i + 1, :] for i in range(TOP)]
    take = jnp.where(hits[0] | hits[1], 1.0, 0.0).astype(BF16)
    weighted = jnp.where(hits[0], gates_ref[0:1, :], jnp.where(hits[1], gates_ref[1:2, :], 0.0))
    gate = jnp.sum(weighted, axis=1, keepdims=True)
    rows_ref[...] = mm(take, h_ref[...]).astype(BF16)
    grads_ref[...] = (dy_rows_ref[...].astype(F32) * gate).astype(BF16)
    gate_ref[...] = gate


def dispatch(code, routes_t, router_t, h, dy_rows):
    slots, width = dy_rows.shape
    tile = slots // 4
    row_spec = pl.BlockSpec((tile, width), lambda i: (i, 0))
    whole = lambda shape: pl.BlockSpec(shape, lambda i: (0, 0))
    return pl.pallas_call(
        dispatch_kernel,
        grid=(4,),
        in_specs=[whole(code.shape), whole(code.shape), whole(router_t.shape), whole(h.shape), row_spec],
        out_specs=[row_spec, row_spec, pl.BlockSpec((tile, 1), lambda i: (i, 0)), whole(code.shape)],
        out_shape=[jax.ShapeDtypeStruct((slots, width), BF16)] * 2
        + [jax.ShapeDtypeStruct((slots, 1), F32), jax.ShapeDtypeStruct(code.shape, F32)],
        compiler_params=params(),
        cost_estimate=cost(4 * slots * SEQ * width, 4 * MIB + 6 * slots * width),
    )(code, routes_t, router_t, h, dy_rows)


def gelu_parts(x):
    inner = 0.7978845608028654 * (x + 0.044715 * (x * x * x))
    bend = jnp.tanh(inner)
    half = 0.5 * (1.0 + bend)
    slope = half + 0.5 * x * (1.0 - bend * bend) * (
        0.7978845608028654 * (1.0 + 3.0 * 0.044715 * (x * x))
    )
    return x * half, slope


def partner_of(index, step):
    found = index
    for bit in (1, 2, 4):
        found = found + ((step // bit) % 2) * (1 - 2 * ((index // bit) % 2)) * bit
    return found


def expert_kernel(
    rows_in, grads_in, gate_in, up_in, down_in, far_gate,
    ret_out, back_out, own_gate, own_up, own_down, got_gate, got_up, got_down,
    rows, grads, weights, sums, parts, z_send, z_recv, y_send, y_recv, p_send, p_recv, r_send, r_recv, w_send, w_recv, g_send, g_recv, local,
):
    groups, half, width = rows.shape[1:]
    group, rank = lax.axis_index("expert"), lax.axis_index("tensor")
    pair_class, half_index = rank % 2, rank // 2
    across = {"tensor": rank + 1 - 2 * pair_class}
    along = {"tensor": rank + 2 - 4 * half_index}
    mesh_ids = pl.DeviceIdType.MESH
    moved = ((rows_in, rows, ret_out), (grads_in, grads, back_out))

    barrier = pltpu.get_barrier_semaphore()
    for step in range(1, groups):
        pl.semaphore_signal(
            barrier, inc=1, device_id={"expert": partner_of(group, step)}, device_id_type=mesh_ids
        )
    pl.semaphore_signal(barrier, inc=1, device_id=across, device_id_type=mesh_ids)
    pl.semaphore_signal(barrier, inc=1, device_id=along, device_id_type=mesh_ids)
    pl.semaphore_wait(barrier, groups + 1)

    def remote(source, target, send, recv, device):
        return pltpu.make_async_remote_copy(
            src_ref=source, dst_ref=target, send_sem=send, recv_sem=recv,
            device_id=device, device_id_type=mesh_ids,
        )

    def block(ref, number):
        return ref.at[pl.ds(pl.multiple_of(number * half, half), half)]

    def out_of(kind, step):
        source, held, _ = moved[kind]
        other = partner_of(group, step)
        return remote(
            block(source, other), held.at[0, group], z_send.at[kind, step], z_recv.at[kind, step], {"expert": other}
        )

    def forward(kind, step):
        held = moved[kind][1]
        other = partner_of(group, step)
        return remote(held.at[0, other], held.at[1, other], y_send.at[kind, step], y_recv.at[kind, step], along)

    def partial_sum(kind, step):
        held = moved[kind][1]
        other = partner_of(group, step)
        return remote(held.at[1, other], parts.at[kind, other], p_send.at[kind, step], p_recv.at[kind, step], along)

    def result(kind, step):
        other = partner_of(group, step)
        return remote(
            parts.at[kind, other], block(moved[kind][2], group), r_send.at[kind, step], r_recv.at[kind, step], {"expert": other}
        )

    def own_result(kind):
        return pltpu.make_async_copy(parts.at[kind, group], block(moved[kind][2], group), local.at[kind])

    own = [
        pltpu.make_async_copy(block(moved[kind][0], group), moved[kind][1].at[0, group], local.at[kind])
        for kind in range(2)
    ]
    for copy in own:
        copy.start()
    kept = [
        pltpu.make_async_copy(ref.at[pair_class], weights.at[number, 0], local.at[2 + number])
        for number, ref in enumerate((gate_in, up_in, down_in))
    ]
    kept.append(pltpu.make_async_copy(far_gate, weights.at[0, 1], local.at[5]))
    kept += [
        remote(ref.at[1 - pair_class], weights.at[number, 1], w_send.at[number - 1], w_recv.at[number - 1], across)
        for number, ref in ((1, up_in), (2, down_in))
    ]
    for copy in kept:
        copy.start()
    for step in range(1, groups):
        for kind in range(2):
            out_of(kind, step).start()

    def arrive(step):
        for kind in range(2):
            out_of(kind, step).wait()
            forward(kind, step).start()

    def give(step):
        for kind in range(2):
            partial_sum(kind, step).start()

    for number in range(3):
        for part in range(2):
            sums[number, part] = jnp.zeros(sums.shape[2:], F32)

    def finish(step):
        other = partner_of(group, step)
        for kind in range(2):
            partial_sum(kind, step).wait()
            held = moved[kind][1]
            parts[kind, other] = (parts[kind, other].astype(F32) + held[0, other].astype(F32)).astype(BF16)

        for kind in range(2):
            if step == 0:
                own_result(kind).start()
            else:
                result(kind, step).start()

    def act(plan):
        for action, step in plan:
            action(step)

    order = (0, 1, 4, 5, 2, 6, 3, 7)
    before = {
        0: [(arrive, 1), (arrive, 2), (arrive, 3), (arrive, 4)],
        1: [(give, 0)],
        2: [(arrive, 5)],
        3: [(give, 4), (finish, 0)],
        4: [(arrive, 6)],
        5: [(give, 5), (finish, 4)],
        6: [(arrive, 7)],
        7: [(give, 6), (finish, 5)],
    }
    ahead = [(give, 7)]
    last = [(give, 2), (finish, 6), (give, 3), (finish, 7), (give, 1), (finish, 2), (finish, 3), (finish, 1)]
    for copy in own:
        copy.wait()
    for kind in range(2):
        forward(kind, 0).start()

    def body(turn, carry):
        for number, plan in before.items():
            pl.when(turn == number)(partial(act, plan))

        @pl.when(turn == 0)
        def _():
            for copy in kept:
                copy.wait()

        step = sum((turn == number).astype(jnp.int32) * which for number, which in enumerate(order))
        for kind in range(2):
            forward(kind, step).wait()
        other = partner_of(group, step)
        tile = jnp.concatenate([rows[0, other], rows[1, other]], axis=0)
        grad = jnp.concatenate([grads[0, other], grads[1, other]], axis=0)
        ret = jnp.zeros(tile.shape, F32)
        back = jnp.zeros(tile.shape, F32)
        for part in range(2):
            w_gate, w_up, w_down = weights[0, part], weights[1, part], weights[2, part]
            gate_part = mm(tile, w_gate, NT)
            up_part = mm(tile, w_up, NT)
            grad_hidden = mm(grad, w_down, NT)
            bent, slope = gelu_parts(gate_part)
            hidden = (bent * up_part).astype(BF16)
            grad_gate = (grad_hidden * up_part * slope).astype(BF16)
            grad_up = (grad_hidden * bent).astype(BF16)
            ret = ret + mm(hidden, w_down)
            back = back + mm(grad_gate, w_gate) + mm(grad_up, w_up)
            sums[0, part] += mm(grad_gate, tile, TN)
            sums[1, part] += mm(grad_up, tile, TN)
            sums[2, part] += mm(hidden, grad, TN)
        for kind, value in enumerate((ret, back)):
            held = moved[kind][1]
            held[0, other] = value[:half].astype(BF16)
            held[1, other] = value[half:].astype(BF16)

        return carry

    lax.fori_loop(0, groups, body, 0)
    act(ahead)
    copies = []
    for number, (own_ref, got_ref) in enumerate(((own_gate, got_gate), (own_up, got_up), (own_down, got_down))):
        weights[number, 0] = sums[number, 1].astype(BF16)
        copies.append(remote(weights.at[number, 0], got_ref, g_send.at[number], g_recv.at[number], across))
        copies[-1].start()
        copies.append(pltpu.make_async_copy(sums.at[number, 0], own_ref, local.at[2 + number]))
        copies[-1].start()
    act(last)
    for copy in copies:
        copy.wait()
    for kind in range(2):
        own_result(kind).wait()
        for step in range(1, groups):
            result(kind, step).wait()


def run_experts(rows, grads, w_gate, w_up, w_down, far_gate):
    slots, width = rows.shape
    half = CAP // 2
    groups = slots // half
    units = w_gate.shape[1]
    anywhere = pl.BlockSpec(memory_space=pl.ANY)
    pair = pltpu.SemaphoreType.DMA((2, groups))
    return pl.pallas_call(
        expert_kernel,
        in_specs=[anywhere] * 6,
        out_specs=[anywhere] * 8,
        out_shape=[jax.ShapeDtypeStruct((slots, width), BF16)] * 2
        + [jax.ShapeDtypeStruct((units, width), F32)] * 3
        + [jax.ShapeDtypeStruct((units, width), BF16)] * 3,
        scratch_shapes=[
            pltpu.VMEM((2, groups, half, width), BF16),
            pltpu.VMEM((2, groups, half, width), BF16),
            pltpu.VMEM((3, 2, units, width), BF16),
            pltpu.VMEM((3, 2, units, width), F32),
            pltpu.VMEM((2, groups, half, width), BF16),
        ]
        + [pair] * 8
        + [pltpu.SemaphoreType.DMA((2,))] * 2
        + [pltpu.SemaphoreType.DMA((3,))] * 2
        + [pltpu.SemaphoreType.DMA((6,))],
        compiler_params=pltpu.CompilerParams(
            vmem_limit_bytes=60 * MIB, collective_id=1, has_side_effects=True
        ),
        cost_estimate=cost(72 * slots * units * width, 16 * slots * width + 30 * units * width),
    )(rows, grads, w_gate, w_up, w_down, far_gate)


def turn_kernel(in_ref, out_ref):
    out_ref[...] = in_ref[...].astype(F32).T.astype(out_ref.dtype)


def turn(rows, kind):
    tokens, width = rows.shape
    tile = 512
    return pl.pallas_call(
        turn_kernel,
        grid=(tokens // tile,),
        in_specs=[pl.BlockSpec((tile, width), lambda i: (i, 0))],
        out_specs=pl.BlockSpec((width, tile), lambda i: (0, i)),
        out_shape=jax.ShapeDtypeStruct((width, tokens), kind),
        compiler_params=params(),
        cost_estimate=cost(0, 6 * rows.size),
    )(rows)


def turn_and_place_kernel(place_ref, in_ref, own_ref, got_ref, out_ref, placed_ref):
    out_ref[...] = in_ref[...].astype(F32).T.astype(out_ref.dtype)
    placed_ref[place_ref[0]] = own_ref[...]
    placed_ref[1 - place_ref[0]] = got_ref[...].astype(F32)


def turn_and_place(place, rows, kind, own, got):
    tokens, width = rows.shape
    units = own.shape[0]
    steps = 4
    tile, part = tokens // steps, units // steps
    quarter = pl.BlockSpec((part, width), lambda i: (i, 0))
    return pl.pallas_call(
        turn_and_place_kernel,
        grid=(steps,),
        in_specs=[
            pl.BlockSpec(memory_space=pltpu.SMEM),
            pl.BlockSpec((tile, width), lambda i: (i, 0)),
            quarter,
            quarter,
        ],
        out_specs=[
            pl.BlockSpec((width, tile), lambda i: (0, i)),
            pl.BlockSpec((2, part, width), lambda i: (0, i, 0)),
        ],
        out_shape=[
            jax.ShapeDtypeStruct((width, tokens), kind),
            jax.ShapeDtypeStruct((2, units, width), F32),
        ],
        compiler_params=params(),
        cost_estimate=cost(0, 6 * rows.size + 14 * own.size),
    )(place, rows, own, got)


def on_device(
    layer_input, gain_one, attn_in, rel_bias, attn_out, gain_two, router,
    expert_gate, expert_up, expert_down, routes, piece_starts, grad_out,
):
    width, tokens = layer_input.shape
    ranks = lax.axis_size("tensor")
    groups = lax.axis_size("expert")
    rank = lax.axis_index("tensor")
    pair_class, half_index = rank % 2, rank // 2
    half = CAP // 2

    def trade(weights):
        other = lax.dynamic_index_in_dim(weights, 1 - pair_class, 0, keepdims=False)
        return lax.ppermute(other, "tensor", [(r, r ^ 1) for r in range(ranks)])

    traded = trade(expert_gate)
    gain_col = gain_one[:, None]
    w_in = attn_in.reshape(-1, width)
    qkv, scale_one = project(layer_input, gain_col, w_in)
    tiles = bias_tiles(rel_bias)
    position = jnp.arange(SEQ, dtype=jnp.int32)[None, None, :]
    starts = piece_starts[:, :, None]
    inside = (position >= starts) & (position < starts + PIECE)
    last = jnp.max(jnp.where(inside, starts + (PIECE - 1), -1), axis=1)
    limits = jnp.maximum(last, position[0])[:, None, :]

    routes_t = routes.T
    place = jnp.stack([pair_class, half_index]).astype(jnp.int32)
    code = local_codes(place, routes_t, half, groups)
    code_cols = code.T

    share = tokens // ranks

    def own(rows, axis=0):
        return lax.dynamic_slice_in_dim(rows, rank * share, share, axis)

    def by_rank(rows):
        return rows.reshape(ranks, share, width)

    own_x = own(layer_input, 1).T
    own_scale = own(scale_one, 1).T
    mixed, lse, sent = attend(qkv, tiles, limits, attn_out)
    sent, traded = lax.optimization_barrier((sent, traded))
    slots = groups * half
    h2, resid, scale_two, dy, dy_rows = exchange_call(
        norm_two_kernel, 2, sent.shape, [by_rank(sent), own_x, gain_two[None], grad_out, code],
        [((share, width), F32), ((share, 1), F32), ((tokens, width), BF16), ((slots, width), BF16)],
    )
    rows, row_grads, gate_rows, gates = dispatch(code, routes_t, router.T, h2, dy_rows)
    ret, back, *weight_grads = run_experts(
        rows, row_grads, expert_gate, expert_up, expert_down, traded
    )
    grad_attn, grad_resid, grad_gain_two, grad_router, partial_y = exchange_call(
        norm_two_back_kernel, 3, (tokens, width),
        [ret, back, code, code_cols, gates, routes_t, dy_rows, gate_rows, router.T, h2]
        + [resid, scale_two, dy, gain_two[None]],
        [((share, width), F32), ((1, width), F32), ((EXPERTS, width), F32), ((tokens, width), BF16)],
        [
            pltpu.VMEM((ranks, share, width), BF16),
            pltpu.VMEM((slots, width), BF16),
            pltpu.VMEM((ranks, 2 * EXPERTS, share), BF16),
        ],
    )

    dq, dk, dv, near, far, y_own = attend_back(
        qkv, tiles, limits, attn_out, grad_attn, lse, by_rank(partial_y), resid
    )
    weight_rows, sent, grad_gain_one, grad_gate, grad_up = project_back(
        place, layer_input, gain_col, scale_one, w_in, mixed, grad_attn, (dq, dk, dv),
        weight_grads[:2], weight_grads[3:5],
    )
    summed = lax.psum(weight_rows, "expert")
    y_own = y_own.astype(BF16)
    small_shape = (EXPERTS + 8 + BUCKETS, width)
    grad_rows, y_full, small = exchange_call(
        norm_one_back_kernel, 4, sent.shape,
        [by_rank(sent), own_x, own_scale, grad_resid, gain_one[None], y_own, grad_gain_one, grad_gain_two, grad_router]
        + [near, far],
        [((ranks, share, width), BF16), (small_shape, F32)],
        [pltpu.VMEM((groups + 4, *small_shape), F32)]
        + [pltpu.SemaphoreType.DMA((2,))] * 2
        + [pltpu.SemaphoreType.DMA((groups,))] * 2,
    )
    summed, grad_rows = lax.optimization_barrier((summed, grad_rows))
    grad_input = turn(grad_rows, F32)
    layer_output, grad_down = turn_and_place(place, y_full.reshape(tokens, width), BF16, weight_grads[2], weight_grads[5])
    in_rows = w_in.shape[0]
    heads = rel_bias.shape[1]
    return (
        layer_output,
        grad_input,
        small[EXPERTS + 1],
        summed[:in_rows].astype(F32).reshape(attn_in.shape),
        small[EXPERTS + 8 :, : heads * 128 : 128],
        summed[in_rows:].astype(F32),
        small[EXPERTS],
        small[:EXPERTS].T,
        grad_gate,
        grad_up,
        grad_down,
    )


def allowed_pairs(seq_starts):
    position = jnp.arange(SEQ, dtype=jnp.int32)
    inside = (position[:, None] >= seq_starts[None, :]) & (
        position[:, None] < seq_starts[None, :] + PIECE
    )
    numbers = jnp.arange(seq_starts.shape[0], dtype=jnp.int32) + 1
    piece_label = jnp.sum(inside.astype(jnp.int32) * numbers[None, :], axis=1)
    causal = position[None, :] <= position[:, None]
    shared = (piece_label[:, None] == piece_label[None, :]) & (piece_label[:, None] > 0)
    return causal | shared


def slot_table(routes):
    flat_routes = routes.reshape(-1)
    onehot = (flat_routes[:, None] == jnp.arange(EXPERTS, dtype=jnp.int32)[None, :]).astype(
        jnp.int32
    )
    blocks = onehot.reshape(-1, 128, EXPERTS).astype(F32)
    earlier = jnp.tril(jnp.ones((128, 128), F32), -1)
    inside = jnp.einsum("ij,bje->bie", earlier, blocks)
    count = blocks.shape[0]
    carried = jnp.einsum("ab,be->ae", jnp.tril(jnp.ones((count, count), F32), -1), jnp.sum(blocks, axis=1), precision=HIGH)
    before = (inside + carried[:, None, :]).astype(jnp.int32).reshape(onehot.shape)
    slot_number = jnp.sum(before * onehot, axis=1)
    kept_pairs = slot_number < CAP
    slot_index = jnp.where(kept_pairs, flat_routes * CAP + slot_number, EXPERTS * CAP)
    return (slot_index.reshape(routes.shape), kept_pairs.reshape(routes.shape))


def bucket_onehot():
    offsets = jnp.arange(2 * SEQ - 1, dtype=jnp.int32) - (SEQ - 1)
    return (bucket_of(offsets)[:, None] == jnp.arange(BUCKETS, dtype=jnp.int32)[None, :]).astype(
        jnp.float32
    )


def expand_line(line):
    head_count = line.shape[0]
    padded = jnp.concatenate([line, jnp.zeros((head_count, 1), line.dtype)], axis=1)
    tiled = jnp.tile(padded, (1, SEQ))[:, : SEQ * (2 * SEQ - 1)].reshape(
        head_count, SEQ, 2 * SEQ - 1
    )
    return tiled[:, :, SEQ - 1 :]


def fold_line(full_grid):
    head_count = full_grid.shape[0]
    padded = jnp.pad(full_grid, ((0, 0), (0, 0), (SEQ - 1, 0))).reshape(
        head_count, SEQ * (2 * SEQ - 1)
    )
    padded = jnp.pad(padded, ((0, 0), (0, SEQ))).reshape(head_count, SEQ, 2 * SEQ)
    return jnp.sum(padded, axis=1)[:, : 2 * SEQ - 1]


def reduce_heads(tensor_value):
    return lax.psum(tensor_value, "tensor")


def spread_slots(tensor_value):
    return lax.all_gather(tensor_value, "tensor", axis=2, tiled=True)


def owner_exchange(tensor_value):
    return lax.all_to_all(tensor_value, "expert", split_axis=0, concat_axis=0, tiled=True)


def expert_sums(tensor_value):
    return lax.psum_scatter(tensor_value, "tensor", scatter_dimension=2, tiled=True)


def norm_forward(resid, gain, model_width):
    scale = lax.rsqrt(jnp.sum(resid * resid, axis=1) / model_width + EPS)[:, None]
    return (scale, (resid * scale * gain).astype(jnp.bfloat16))


def norm_backward(resid, scale, gain, grad_normed, model_width):
    grad_gain = jnp.sum(grad_normed * resid * scale, axis=0)
    scaled = grad_normed * gain
    inner = jnp.sum(scaled * resid, axis=1)[:, None]
    return (grad_gain, scale * scaled - resid * scale**3 * inner / model_width)


def attend_scores(bias_full, queries, key_rows, seq_starts):
    scores = (
        jnp.einsum("qhe,khe->hqk", queries, key_rows, preferred_element_type=jnp.float32) * 0.125
        + bias_full
    )
    return jnp.where(allowed_pairs(seq_starts)[None], scores, NEG)


def attend_forward(bias_full, inputs):
    queries, key_rows, value_rows, seq_starts = inputs
    scores = attend_scores(bias_full, queries, key_rows, seq_starts)
    row_max = jnp.max(scores, axis=2, keepdims=True)
    exponent = jnp.exp(scores - row_max)
    row_sum_exp = jnp.sum(exponent, axis=2, keepdims=True)
    weights = (exponent / row_sum_exp).astype(jnp.bfloat16)
    mixed_heads = jnp.einsum(
        "hqk,khe->qhe", weights, value_rows, preferred_element_type=jnp.float32
    )
    return (mixed_heads.astype(jnp.bfloat16), (row_max + jnp.log(row_sum_exp))[:, :, 0])


def attend_backward(bias_full, running, inputs):
    queries, key_rows, value_rows, grad_heads, seq_starts, log_total = inputs
    scores = attend_scores(bias_full, queries, key_rows, seq_starts)
    probabilities = jnp.exp(scores - log_total[:, :, None])
    grad_probs = jnp.einsum(
        "qhe,khe->hqk", grad_heads, value_rows, preferred_element_type=jnp.float32
    )
    inner = jnp.sum(probabilities * grad_probs, axis=2, keepdims=True)
    grad_scores = (probabilities * (grad_probs - inner)).astype(jnp.bfloat16)
    grad_values = jnp.einsum(
        "hqk,qhe->khe",
        probabilities.astype(jnp.bfloat16),
        grad_heads,
        preferred_element_type=jnp.float32,
    )
    grad_queries = (
        jnp.einsum("hqk,khe->qhe", grad_scores, key_rows, preferred_element_type=jnp.float32)
        * 0.125
    )
    grad_keys = (
        jnp.einsum("hqk,qhe->khe", grad_scores, queries, preferred_element_type=jnp.float32) * 0.125
    )
    return (
        running + grad_scores.astype(jnp.float32),
        jnp.stack([grad_queries, grad_keys, grad_values]),
    )


def gelu_product(left, right):
    return jax.nn.gelu(left, approximate=True) * right


def expert_forward(received, weight_gate, weight_up, weight_down):
    gate_part = jnp.einsum(
        "secd,efd->secf", received, weight_gate, preferred_element_type=jnp.float32
    )
    up_part = jnp.einsum("secd,efd->secf", received, weight_up, preferred_element_type=jnp.float32)
    hidden = gelu_product(gate_part, up_part).astype(jnp.bfloat16)
    partial_out = jnp.einsum(
        "secf,efd->secd", hidden, weight_down, preferred_element_type=jnp.float32
    )
    return (gate_part, up_part, hidden, partial_out)


def expert_backward(
    received, gate_part, up_part, hidden, grad_rows_out, weight_gate, weight_up, weight_down
):
    grad_hidden = jnp.einsum(
        "secd,efd->secf", grad_rows_out, weight_down, preferred_element_type=jnp.float32
    )
    product_value, pullback = jax.vjp(gelu_product, gate_part, up_part)
    grad_gate_part, grad_up_part = pullback(grad_hidden)
    grad_gate_part = grad_gate_part.astype(jnp.bfloat16)
    grad_up_part = grad_up_part.astype(jnp.bfloat16)
    grad_down = jnp.einsum(
        "secf,secd->efd", hidden, grad_rows_out, preferred_element_type=jnp.float32
    )
    grad_gate_w = jnp.einsum(
        "secf,secd->efd", grad_gate_part, received, preferred_element_type=jnp.float32
    )
    grad_up_w = jnp.einsum(
        "secf,secd->efd", grad_up_part, received, preferred_element_type=jnp.float32
    )
    grad_rows_in = jnp.einsum(
        "secf,efd->secd", grad_gate_part, weight_gate, preferred_element_type=jnp.float32
    )
    grad_rows_in = grad_rows_in + jnp.einsum(
        "secf,efd->secd", grad_up_part, weight_up, preferred_element_type=jnp.float32
    )
    return (grad_gate_w, grad_up_w, grad_down, grad_rows_in)


def on_device_general(
    layer_input,
    gain_one,
    attn_in,
    rel_bias,
    attn_out,
    gain_two,
    router,
    expert_gate,
    expert_up,
    expert_down,
    routes,
    piece_starts,
    grad_out,
):
    tok_count = layer_input.shape[1]
    model_width = layer_input.shape[0]
    heads_here = rel_bias.shape[1]
    head_width = attn_in.shape[1] // heads_here
    seqs_here = piece_starts.shape[0]
    local_experts = expert_gate.shape[0]
    part_rows = CAP // lax.axis_size("tensor")
    share_start = lax.axis_index("tensor") * part_rows
    tokens = layer_input.T.astype(jnp.float32)
    scale_one, normed = norm_forward(tokens, gain_one, model_width)
    project = jnp.einsum("td,chd->cth", normed, attn_in, preferred_element_type=jnp.float32).astype(
        jnp.bfloat16
    )
    by_seq = project.reshape(3, seqs_here, SEQ, heads_here, head_width)
    onehot_line = bucket_onehot()
    bias_full = expand_line(jnp.dot(onehot_line, rel_bias, precision=HIGH).T)
    mixed_heads, log_total = lax.map(
        partial(attend_forward, bias_full), (by_seq[0], by_seq[1], by_seq[2], piece_starts)
    )
    mixed_heads = mixed_heads.reshape(tok_count, heads_here * head_width)
    resid = tokens + reduce_heads(
        jnp.dot(mixed_heads, attn_out, preferred_element_type=jnp.float32)
    )
    scale_two, normed_two = norm_forward(resid, gain_two, model_width)
    logits = jnp.dot(normed_two, router, preferred_element_type=jnp.float32)
    chosen = (routes[:, :, None] == jnp.arange(EXPERTS, dtype=jnp.int32)[None, None, :]).astype(
        jnp.float32
    )
    picked = jnp.sum(chosen * logits[:, None, :], axis=2)
    gate_weights = jax.nn.softmax(picked, axis=1)
    slot_index, kept_pairs = slot_table(routes)
    keep_float = kept_pairs.astype(jnp.float32)
    mix_weight = gate_weights * keep_float
    safe_index = jnp.minimum(slot_index, EXPERTS * CAP - 1)
    token_rows = jnp.repeat(normed_two, TOP, axis=0)
    buffer = (
        jnp.zeros((EXPERTS * CAP + 1, model_width), jnp.bfloat16)
        .at[slot_index.reshape(-1)]
        .set(token_rows)
    )
    buffer = buffer[: EXPERTS * CAP].reshape(-1, local_experts, CAP, model_width)
    received = lax.all_to_all(buffer, "expert", split_axis=0, concat_axis=0, tiled=True)
    gate_part, up_part, hidden, partial_out = expert_forward(
        received, expert_gate, expert_up, expert_down
    )
    returned = spread_slots(owner_exchange(expert_sums(partial_out).astype(jnp.bfloat16)))
    flat_ret = returned.reshape(EXPERTS * CAP, model_width)
    fetched = flat_ret[safe_index].astype(jnp.float32)
    output = resid + jnp.sum(mix_weight[:, :, None] * fetched, axis=1)
    grad_y = grad_out.T.astype(jnp.float32)
    grad_gates = jnp.sum(grad_y[:, None, :] * fetched, axis=2) * keep_float
    grad_picked = gate_weights * (
        grad_gates - jnp.sum(gate_weights * grad_gates, axis=1, keepdims=True)
    )
    grad_logits = jnp.sum(chosen * grad_picked[:, :, None], axis=1)
    grad_router = jnp.dot(normed_two.astype(jnp.float32).T, grad_logits, precision=HIGH)
    grad_normed_two = jnp.dot(grad_logits, router.astype(jnp.float32).T, precision=HIGH)
    slot_grads = (mix_weight[:, :, None] * grad_y[:, None, :]).astype(jnp.bfloat16)
    grad_ret = (
        jnp.zeros((EXPERTS * CAP + 1, model_width), jnp.bfloat16)
        .at[slot_index.reshape(-1)]
        .set(slot_grads.reshape(-1, model_width))
    )
    grad_ret = grad_ret[: EXPERTS * CAP].reshape(-1, local_experts, CAP, model_width)
    grad_share = lax.dynamic_slice_in_dim(grad_ret, share_start, part_rows, 2)
    grad_rows_out = spread_slots(owner_exchange(grad_share))
    grad_expert_gate, grad_expert_up, grad_expert_down, grad_rows_in = expert_backward(
        received, gate_part, up_part, hidden, grad_rows_out, expert_gate, expert_up, expert_down
    )
    grad_back = spread_slots(owner_exchange(expert_sums(grad_rows_in).astype(jnp.bfloat16)))
    flat_back = grad_back.reshape(EXPERTS * CAP, model_width).astype(jnp.float32)
    grad_normed_two = grad_normed_two + jnp.sum(
        flat_back[safe_index] * keep_float[:, :, None], axis=1
    )
    grad_gain_two, grad_resid = norm_backward(
        resid, scale_two, gain_two, grad_normed_two, model_width
    )
    grad_resid = grad_resid + grad_y
    grad_attn = grad_resid.astype(jnp.bfloat16)
    grad_attn_out = jnp.einsum(
        "th,td->hd", mixed_heads, grad_attn, preferred_element_type=jnp.float32
    )
    grad_mixed = jnp.einsum(
        "td,hd->th", grad_attn, attn_out, preferred_element_type=jnp.float32
    ).astype(jnp.bfloat16)
    grad_by_seq = grad_mixed.reshape(seqs_here, SEQ, heads_here, head_width)
    bias_grad_full, grad_project = lax.scan(
        partial(attend_backward, bias_full),
        jnp.zeros_like(bias_full),
        (by_seq[0], by_seq[1], by_seq[2], grad_by_seq, piece_starts, log_total),
    )
    grad_project = (
        jnp.moveaxis(grad_project, 1, 0)
        .reshape(3, tok_count, heads_here * head_width)
        .astype(jnp.bfloat16)
    )
    grad_attn_in = jnp.einsum(
        "cth,td->chd", grad_project, normed, preferred_element_type=jnp.float32
    )
    grad_normed = reduce_heads(
        jnp.einsum("cth,chd->td", grad_project, attn_in, preferred_element_type=jnp.float32)
    )
    grad_gain_one, grad_tokens = norm_backward(
        tokens, scale_one, gain_one, grad_normed, model_width
    )
    grad_tokens = grad_tokens + grad_resid
    grad_rel_bias = jnp.dot(onehot_line.T, fold_line(bias_grad_full).T, precision=HIGH)
    shared = (
        lax.psum(grad_gain_one.astype(jnp.bfloat16), "expert").astype(jnp.float32),
        lax.psum(grad_attn_in.astype(jnp.bfloat16), "expert").astype(jnp.float32),
        lax.psum(grad_rel_bias.astype(jnp.bfloat16), "expert").astype(jnp.float32),
        lax.psum(grad_attn_out.astype(jnp.bfloat16), "expert").astype(jnp.float32),
        lax.psum(grad_gain_two.astype(jnp.bfloat16), "expert").astype(jnp.float32),
        lax.psum(grad_router.astype(jnp.bfloat16), "expert").astype(jnp.float32),
    )
    return (
        output.astype(jnp.bfloat16).T,
        grad_tokens.T,
        shared[0],
        shared[1],
        shared[2],
        shared[3],
        shared[4],
        shared[5],
        grad_expert_gate,
        grad_expert_up,
        grad_expert_down,
    )


def solution(mesh):
    placed = (
        P(None, "expert"),
        P(),
        P(None, "tensor", None),
        P(None, "tensor"),
        P("tensor", None),
        P(),
        P(),
        P("expert", "tensor", None),
        P("expert", "tensor", None),
        P("expert", "tensor", None),
        P("expert", None),
        P("expert", None),
        P(None, "expert"),
    )
    paired = mesh.shape["tensor"] == 4 and mesh.shape["expert"] * 2 == EXPERTS
    return jax.shard_map(
        on_device if paired else on_device_general,
        mesh=mesh,
        in_specs=placed,
        out_specs=(
            P(None, "expert"),
            P(None, "expert"),
            P(),
            P(None, "tensor", None),
            P(None, "tensor"),
            P("tensor", None),
            P(),
            P(),
            P("expert", "tensor", None),
            P("expert", "tensor", None),
            P("expert", "tensor", None),
        ),
        check_vma=False,
    )
```

```python
from functools import partial

import jax
import jax.numpy as jnp
from jax import lax
from jax.experimental import pallas as pl
from jax.experimental.pallas import tpu as pltpu
from jax.sharding import PartitionSpec as P

EXPERTS = 16
BUCKETS = 32
TOP = 2
PIECE = 256
SEQ = 1024
CAP = 320
BLK = 256


EPS = 1e-06
NEG = -1e30
THRESHOLDS = (12, 16, 23, 32, 46, 64, 91)
HIGH = lax.Precision.HIGHEST
F32 = jnp.float32
BF16 = jnp.bfloat16
NN = (((1,), (0,)), ((), ()))
NT = (((1,), (1,)), ((), ()))
TN = (((0,), (0,)), ((), ()))
MIB = 1 << 20


def mm(left, right, dims=NN):
    return lax.dot_general(left, right, dims, preferred_element_type=F32)


def params(limit=56):
    return pltpu.CompilerParams(vmem_limit_bytes=limit * MIB)


def cost(flops, bytes_accessed, transcendentals=0):
    return pl.CostEstimate(
        flops=int(flops), bytes_accessed=int(bytes_accessed), transcendentals=int(transcendentals)
    )


def bucket_of(offset):
    magnitude = jnp.abs(offset)
    beyond = sum(((magnitude >= threshold).astype(jnp.int32) for threshold in THRESHOLDS))
    lower_part = jnp.where(magnitude < 8, magnitude, 8 + beyond)
    return lower_part + 16 * (offset > 0).astype(jnp.int32)


def project_kernel(x_ref, gain_ref, w_ref, out_ref, scale_ref):
    x = x_ref[...].astype(F32)
    scale = lax.rsqrt(jnp.sum(x * x, axis=0, keepdims=True) / x.shape[0] + EPS)
    normed = (x * scale * gain_ref[...]).astype(BF16)
    out_ref[...] = mm(w_ref[...], normed).astype(BF16)
    scale_ref[...] = scale


def project(x, gain, weights):
    width, tokens = x.shape
    rows = weights.shape[0]
    tile = 512
    return pl.pallas_call(
        project_kernel,
        grid=(tokens // tile,),
        in_specs=[
            pl.BlockSpec((width, tile), lambda i: (0, i)),
            pl.BlockSpec((width, 1), lambda i: (0, 0)),
            pl.BlockSpec((rows, width), lambda i: (0, 0)),
        ],
        out_specs=[
            pl.BlockSpec((rows, tile), lambda i: (0, i)),
            pl.BlockSpec((1, tile), lambda i: (0, i)),
        ],
        out_shape=[
            jax.ShapeDtypeStruct((rows, tokens), BF16),
            jax.ShapeDtypeStruct((1, tokens), F32),
        ],
        compiler_params=params(),
        cost_estimate=cost(2 * width * tokens * rows, 2 * width * tokens * 2),
    )(x, gain, weights)


def line_offsets(number):
    column = lax.broadcasted_iota(jnp.int32, (8, BLK), 1)
    return (number - 1) * BLK - column


def bias_tiles_kernel(table_ref, tiles_ref):
    row = lax.broadcasted_iota(jnp.int32, (BLK, BLK), 0)
    column = lax.broadcasted_iota(jnp.int32, (BLK, BLK), 1)
    buckets = [bucket_of(line_offsets(number)) for number in range(4)]
    for head in range(tiles_ref.shape[0]):
        far = table_ref[15, head]
        rolled = []
        for number, bucket in enumerate(buckets):
            value = jnp.zeros((8, BLK), F32)
            for index in range(BUCKETS):
                value = jnp.where(bucket == index, table_ref[index, head] - far, value)
            whole = jnp.broadcast_to(value[0:1], (BLK, BLK))
            rolled.append(pltpu.roll(whole, 0, 1, stride=1, stride_axis=0))
        for number in range(3):
            tiles_ref[head, number] = jnp.where(column >= row, rolled[number], rolled[number + 1])


def bias_tiles(table):
    heads = table.shape[1]
    return pl.pallas_call(
        bias_tiles_kernel,
        in_specs=[pl.BlockSpec(memory_space=pltpu.SMEM)],
        out_specs=pl.BlockSpec(memory_space=pltpu.VMEM),
        out_shape=jax.ShapeDtypeStruct((heads, 3, BLK, BLK), F32),
        compiler_params=params(),
        cost_estimate=cost(heads * 3 * BLK * BLK * 60, heads * 3 * BLK * BLK * 4),
    )(table)


def bias_fold(near_ref, far_ref):
    heads = near_ref.shape[0] // 2
    sums = jnp.zeros((BUCKETS, 128), F32)
    lane = lax.broadcasted_iota(jnp.int32, (BUCKETS, 128), 1)
    row = lax.broadcasted_iota(jnp.int32, (BLK, BLK), 0)
    column = lax.broadcasted_iota(jnp.int32, (BLK, BLK), 1)
    flip = jnp.where(row + column == BLK - 1, 1.0, 0.0).astype(BF16)
    apart = jnp.where(column == BLK - 1, 0, column + 1)
    ahead = apart <= row
    number_at = lax.broadcasted_iota(jnp.int32, (BUCKETS, BLK), 0)
    for head in range(heads):
        lines = [jnp.zeros((1, BLK), F32) for _ in range(4)]
        for number in range(3):
            grads = near_ref[head, number] + near_ref[heads + head, number]
            coarse = grads.astype(BF16)
            fine = (grads - coarse.astype(F32)).astype(BF16)
            flipped = mm(flip, coarse) + mm(flip, fine)
            rolled = pltpu.roll(flipped, 0, 1, stride=1, stride_axis=0)
            lines[number] += jnp.sum(jnp.where(ahead, rolled, 0.0), axis=0, keepdims=True)
            lines[number + 1] += jnp.sum(jnp.where(ahead, 0.0, rolled), axis=0, keepdims=True)
        total = jnp.zeros((BUCKETS, 1), F32)
        for number, line in enumerate(lines):
            bucket = bucket_of((number - 1) * BLK - apart[:1])
            total += jnp.sum(jnp.where(bucket == number_at, line, 0.0), axis=1, keepdims=True)
        distant = jnp.sum(far_ref[head] + far_ref[heads + head], axis=0, keepdims=True)
        distant = jnp.sum(distant, axis=1, keepdims=True)
        total += jnp.where(number_at[:, :1] == 15, distant, 0.0)
        sums = jnp.where(lane == head, total, sums)
    return sums


def key_count(query_block):
    return 2 * BLK if query_block < 2 else 4 * BLK


def block_scores(keys, queries, tiles_ref, limit, block):
    count = key_count(block)
    parts = []
    whole = mm(keys[:, :count], queries, TN)
    for key_block in range(count // BLK):
        part = whole[key_block * BLK : (key_block + 1) * BLK]
        shift = key_block - block
        if -1 <= shift <= 1:
            part = part + tiles_ref[0, shift + 1]
        if shift >= 0:
            key_at = lax.broadcasted_iota(jnp.int32, (BLK, BLK), 0) + key_block * BLK
            part = jnp.where(key_at <= limit, part, NEG)
        parts.append(part)
    return jnp.concatenate(parts, axis=0)


def attend_kernel(q_ref, k_ref, v_ref, tiles_ref, limit_ref, w_ref, out_ref, lse_ref, sent_ref, held):
    head = pl.program_id(1)
    width = q_ref.shape[0]
    queries = q_ref[...] * BF16(0.125)
    keys, values = k_ref[...], v_ref[...]
    for block in range(SEQ // BLK):
        cols = slice(block * BLK, (block + 1) * BLK)
        scores = block_scores(keys, queries[:, cols], tiles_ref, limit_ref[0, :, cols], block)
        top = jnp.max(scores, axis=0, keepdims=True)
        exponent = jnp.exp(scores - top)
        total = jnp.sum(exponent, axis=0, keepdims=True)
        mixed = mm(values[:, : key_count(block)], exponent.astype(BF16)) / total
        mixed = mixed.astype(BF16)
        out_ref[:, cols] = mixed
        held[pl.ds(pl.multiple_of(head * width, width), width), cols] = mixed
        lse_ref[0, :, cols] = top + jnp.log(total)

    @pl.when(head == pl.num_programs(1) - 1)
    def _():
        sent_ref[...] = mm(held[...], w_ref[...], TN).astype(BF16)


def attend(qkv, tiles, limits, attn_out):
    heads = tiles.shape[0]
    seqs = limits.shape[0]
    width = qkv.shape[0] // (3 * heads)
    model_width = attn_out.shape[1]
    return pl.pallas_call(
        attend_kernel,
        grid=(seqs, heads),
        in_specs=[
            pl.BlockSpec((width, SEQ), lambda s, h: (h, s)),
            pl.BlockSpec((width, SEQ), lambda s, h: (heads + h, s)),
            pl.BlockSpec((width, SEQ), lambda s, h: (2 * heads + h, s)),
            pl.BlockSpec((1, 3, BLK, BLK), lambda s, h: (h, 0, 0, 0)),
            pl.BlockSpec((1, 1, SEQ), lambda s, h: (s, 0, 0)),
            pl.BlockSpec((heads * width, model_width), lambda s, h: (0, 0)),
        ],
        out_specs=[
            pl.BlockSpec((width, SEQ), lambda s, h: (h, s)),
            pl.BlockSpec((1, 1, SEQ), lambda s, h: (s * heads + h, 0, 0)),
            pl.BlockSpec((SEQ, model_width), lambda s, h: (s, 0)),
        ],
        out_shape=[
            jax.ShapeDtypeStruct((heads * width, seqs * SEQ), BF16),
            jax.ShapeDtypeStruct((seqs * heads, 1, SEQ), F32),
            jax.ShapeDtypeStruct((seqs * SEQ, model_width), BF16),
        ],
        scratch_shapes=[pltpu.VMEM((heads * width, SEQ), BF16)],
        compiler_params=params(),
        cost_estimate=cost(seqs * heads * SEQ * SEQ * 512, seqs * heads * SEQ * 2048, seqs * heads * SEQ * SEQ),
    )(qkv, qkv, qkv, tiles, limits, attn_out)


def attend_back_kernel(
    q_ref, k_ref, v_ref, tiles_ref, limit_ref, w_ref, grad_ref, lse_ref, part_ref, resid_ref,
    dq_ref, dk_ref, dv_ref, near_ref, far_ref, y_ref,
    held, parts, total, turn_across, turn_along, from_across, from_along, sends, recvs, loads,
):
    rank = lax.axis_index("tensor")
    pair_class, half_index = rank % 2, rank // 2
    across, along, corner = rank + 1 - 2 * pair_class, rank + 2 - 4 * half_index, 3 - rank
    step = pl.program_id(0) * pl.num_programs(1) + pl.program_id(1)
    mesh_ids = pl.DeviceIdType.MESH
    middle = parts.shape[2] // 2
    low, high = slice(0, middle), slice(middle, 2 * middle)

    def remote(number, origin, target, other):
        return pltpu.make_async_remote_copy(
            src_ref=origin, dst_ref=target, send_sem=sends.at[number], recv_sem=recvs.at[number],
            device_id={"tensor": other}, device_id_type=mesh_ids,
        )

    first = (
        remote(0, part_ref.at[corner, :, low], turn_across, across),
        remote(1, part_ref.at[corner, :, high], turn_along, along),
    )
    second = remote(2, parts.at[0], from_across, across), remote(3, parts.at[1], from_along, along)
    local = [
        pltpu.make_async_copy(part_ref.at[other], parts.at[number], loads.at[number])
        for number, other in enumerate((across, along, rank))
    ]
    local.append(pltpu.make_async_copy(resid_ref, total, loads.at[3]))

    @pl.when(step == 0)
    def _():
        barrier = pltpu.get_barrier_semaphore()
        for other in (across, along):
            pl.semaphore_signal(barrier, inc=1, device_id={"tensor": other}, device_id_type=mesh_ids)
        pl.semaphore_wait(barrier, 2)
        for copy in first:
            copy.start()
        for copy in local:
            copy.start()

    @pl.when(step == 3)
    def _():
        for copy in (*first, *local):
            copy.wait()
        parts[0, :, high] = (parts[0, :, high].astype(F32) + turn_along[...].astype(F32)).astype(BF16)
        parts[1, :, low] = (parts[1, :, low].astype(F32) + turn_across[...].astype(F32)).astype(BF16)
        for copy in second:
            copy.start()

    head = pl.program_id(1)
    width = q_ref.shape[0]

    @pl.when(head == 0)
    def _():
        held[...] = mm(w_ref[...], grad_ref[...], NT).astype(BF16)

    queries = q_ref[...] * BF16(0.125)
    keys, values = k_ref[...], v_ref[...]
    grads = held[pl.ds(pl.multiple_of(head * width, width), width), :]
    near_ref[...] = jnp.zeros_like(near_ref)
    far = jnp.zeros((8, BLK), F32)
    grad_keys = jnp.zeros((width, SEQ), F32)
    grad_values = jnp.zeros((width, SEQ), F32)
    for block in range(SEQ // BLK):
        count = key_count(block)
        cols = slice(block * BLK, (block + 1) * BLK)
        scores = block_scores(keys, queries[:, cols], tiles_ref, limit_ref[0, :, cols], block)
        probs = jnp.exp(scores - lse_ref[0, :, cols])
        grad_probs = mm(values[:, :count], grads[:, cols], TN)
        inner = jnp.sum(probs * grad_probs, axis=0, keepdims=True)
        grad_scores = probs * (grad_probs - inner)
        for key_block in range(count // BLK):
            part = grad_scores[key_block * BLK : (key_block + 1) * BLK]
            shift = key_block - block
            if -1 <= shift <= 1:
                near_ref[0, shift + 1] += part
            elif shift < -1:
                far = far + jnp.sum(part.reshape(BLK // 8, 8, BLK), axis=0)
        rounded = grad_scores.astype(BF16)
        add_values = mm(grads[:, cols], probs.astype(BF16), NT)
        add_keys = mm(queries[:, cols], rounded, NT)
        if count == SEQ:
            grad_values = grad_values + add_values
            grad_keys = grad_keys + add_keys
        else:
            filler = jnp.zeros((width, SEQ - count), F32)
            grad_values = grad_values + jnp.concatenate([add_values, filler], axis=1)
            grad_keys = grad_keys + jnp.concatenate([add_keys, filler], axis=1)
        dq_ref[:, cols] = (mm(keys[:, :count], rounded) * 0.125).astype(BF16)
    dk_ref[...] = grad_keys.astype(BF16)
    dv_ref[...] = grad_values.astype(BF16)
    far_ref[0] = far

    @pl.when(step == 7)
    def _():
        for copy in second:
            copy.wait()
        summed = parts[2].astype(F32) + from_across[...].astype(F32) + from_along[...].astype(F32)
        y_ref[...] = (total[...] + summed).astype(BF16)


def attend_back(qkv, tiles, limits, attn_out, grad_attn, lse, part, resid):
    heads = tiles.shape[0]
    seqs = limits.shape[0]
    width = qkv.shape[0] // (3 * heads)
    model_width = attn_out.shape[1]
    share = part.shape[1]
    grad_spec = pl.BlockSpec((width, SEQ), lambda s, h: (h, s))
    anywhere = pl.BlockSpec(memory_space=pl.ANY)
    return pl.pallas_call(
        attend_back_kernel,
        grid=(seqs, heads),
        in_specs=[
            pl.BlockSpec((width, SEQ), lambda s, h: (h, s)),
            pl.BlockSpec((width, SEQ), lambda s, h: (heads + h, s)),
            pl.BlockSpec((width, SEQ), lambda s, h: (2 * heads + h, s)),
            pl.BlockSpec((1, 3, BLK, BLK), lambda s, h: (h, 0, 0, 0)),
            pl.BlockSpec((1, 1, SEQ), lambda s, h: (s, 0, 0)),
            pl.BlockSpec((heads * width, model_width), lambda s, h: (0, 0)),
            pl.BlockSpec((SEQ, model_width), lambda s, h: (s, 0)),
            pl.BlockSpec((1, 1, SEQ), lambda s, h: (s * heads + h, 0, 0)),
        ]
        + [anywhere] * 2,
        out_specs=[
            grad_spec,
            grad_spec,
            grad_spec,
            pl.BlockSpec((1, 3, BLK, BLK), lambda s, h: (s * heads + h, 0, 0, 0)),
            pl.BlockSpec((1, 8, BLK), lambda s, h: (s * heads + h, 0, 0)),
            pl.BlockSpec((share, model_width), lambda s, h: (0, 0)),
        ],
        out_shape=[jax.ShapeDtypeStruct((heads * width, seqs * SEQ), BF16)] * 3
        + [
            jax.ShapeDtypeStruct((seqs * heads, 3, BLK, BLK), F32),
            jax.ShapeDtypeStruct((seqs * heads, 8, BLK), F32),
        ]
        + [jax.ShapeDtypeStruct((share, model_width), BF16)],
        scratch_shapes=[
            pltpu.VMEM((heads * width, SEQ), BF16),
            pltpu.VMEM((3, share, model_width), BF16),
            pltpu.VMEM((share, model_width), F32),
            pltpu.VMEM((share, model_width // 2), BF16),
            pltpu.VMEM((share, model_width // 2), BF16),
            pltpu.VMEM((share, model_width), BF16),
            pltpu.VMEM((share, model_width), BF16),
            pltpu.SemaphoreType.DMA((4,)),
            pltpu.SemaphoreType.DMA((4,)),
            pltpu.SemaphoreType.DMA((4,)),
        ],
        compiler_params=pltpu.CompilerParams(
            vmem_limit_bytes=60 * MIB, collective_id=5, has_side_effects=True
        ),
        cost_estimate=cost(seqs * heads * SEQ * SEQ * 1280, seqs * heads * SEQ * 4096, seqs * heads * SEQ * SEQ),
    )(qkv, qkv, qkv, tiles, limits, attn_out, grad_attn, lse, part, resid)


def project_back_kernel(
    place_ref, x_ref, gain_ref, scale_ref, w_ref, mixed_ref, attn_ref, dq_ref, dk_ref, dv_ref, *refs
):
    step = pl.program_id(0)
    own_refs, got_refs, (weight_ref, out_ref, gain_grad_ref), placed_refs, total = (
        refs[:2], refs[2:4], refs[4:7], refs[7:9], refs[9]
    )
    for own_ref, got_ref, placed_ref in zip(own_refs, got_refs, placed_refs):
        placed_ref[place_ref[0]] = own_ref[...]
        placed_ref[1 - place_ref[0]] = got_ref[...].astype(F32)
    grads = jnp.concatenate([dq_ref[...], dk_ref[...], dv_ref[...]], axis=0)
    rows = grads.shape[0]
    scaled = x_ref[...].astype(F32) * scale_ref[...]

    @pl.when(step == 0)
    def _():
        total[...] = jnp.zeros_like(total)
        gain_grad_ref[...] = jnp.zeros_like(gain_grad_ref)

    total[:rows] += mm(grads, (scaled * gain_ref[...]).astype(BF16), NT)
    total[rows:] += mm(mixed_ref[...], attn_ref[...])
    back = mm(w_ref[...], grads, TN)
    gain_grad_ref[...] += jnp.sum(back * scaled, axis=1, keepdims=True)
    out_ref[...] = back.T.astype(BF16)

    @pl.when(step == pl.num_programs(0) - 1)
    def _():
        weight_ref[...] = total[...].astype(BF16)


def project_back(place, x, gain, scale, weights, mixed, grad_attn, grads, owns, gots):
    width, tokens = x.shape
    rows = weights.shape[0]
    heads_width = mixed.shape[0]
    units = owns[0].shape[0]
    steps = 4
    tile = tokens // steps
    part = units // steps
    column = lambda count: pl.BlockSpec((count, tile), lambda i: (0, i))
    return pl.pallas_call(
        project_back_kernel,
        grid=(steps,),
        in_specs=[
            pl.BlockSpec(memory_space=pltpu.SMEM),
            column(width),
            pl.BlockSpec((width, 1), lambda i: (0, 0)),
            column(1),
            pl.BlockSpec((rows, width), lambda i: (0, 0)),
            column(heads_width),
            pl.BlockSpec((tile, width), lambda i: (i, 0)),
        ]
        + [column(rows // 3)] * 3
        + [pl.BlockSpec((part, width), lambda i: (i, 0))] * 4,
        out_specs=[
            pl.BlockSpec((rows + heads_width, width), lambda i: (0, 0)),
            pl.BlockSpec((tile, width), lambda i: (i, 0)),
            pl.BlockSpec((width, 1), lambda i: (0, 0)),
        ]
        + [pl.BlockSpec((2, part, width), lambda i: (0, i, 0))] * 2,
        out_shape=[
            jax.ShapeDtypeStruct((rows + heads_width, width), BF16),
            jax.ShapeDtypeStruct((tokens, width), BF16),
            jax.ShapeDtypeStruct((width, 1), F32),
        ]
        + [jax.ShapeDtypeStruct((2, units, width), F32)] * 2,
        scratch_shapes=[pltpu.VMEM((rows + heads_width, width), F32)],
        compiler_params=params(),
        cost_estimate=cost(5 * width * tokens * rows, 6 * width * tokens + 14 * units * width),
    )(place, x, gain, scale, weights, mixed, grad_attn, *grads, *owns, *gots)


def exchange(math, rank, source, full, from_across, from_along, to_across, to_along, turn_across, turn_along, sends, recvs, ready=None, ready_full=None, side=None, peers=(), fill=None, start=None, cut=None):
    pair_class, half_index = rank % 2, rank // 2
    across, along, corner = rank + 1 - 2 * pair_class, rank + 2 - 4 * half_index, 3 - rank
    mesh_ids = pl.DeviceIdType.MESH
    rows, width = source.shape[1:]
    chunks = 4
    size = rows // chunks
    cut = cut or width // 2
    low, high = slice(0, cut), slice(cut, width)
    barrier = pltpu.get_barrier_semaphore()
    for other in (across, along):
        pl.semaphore_signal(barrier, inc=1, device_id={"tensor": other}, device_id_type=mesh_ids)
    for other in peers:
        pl.semaphore_signal(barrier, inc=1, device_id={"expert": other}, device_id_type=mesh_ids)
    pl.semaphore_wait(barrier, 2 + len(peers))

    def remote(kind, chunk, origin, target, other):
        return pltpu.make_async_remote_copy(
            src_ref=origin, dst_ref=target, send_sem=sends.at[kind, chunk], recv_sem=recvs.at[kind, chunk],
            device_id={"tensor": other}, device_id_type=mesh_ids,
        )

    if start:
        start()
    if fill:
        fill(corner)
    spans = [slice(chunk * size, (chunk + 1) * size) for chunk in range(chunks)]
    first, second, third, fourth = [], [], [], []
    for chunk, span in enumerate(spans):
        pair = (
            remote(0, chunk, source.at[corner, span, low], turn_across.at[span, low], across),
            remote(1, chunk, source.at[corner, span, high], turn_along.at[span, high], along),
        )
        for copy in pair:
            copy.start()
        first.append(pair)
    if fill:
        fill(along)
        fill(across)
    if ready is not None:
        _, near_across, near_along = ready
        extra = [
            remote(8, 0, near_along.at[:, low], ready_full.at[along, :, low], across),
            remote(8, 1, near_across.at[:, high], ready_full.at[across, :, high], along),
        ]
        for copy in extra:
            copy.start()
    for chunk, span in enumerate(spans):
        if side:
            side(chunk)
        first[chunk][0].wait()
        to_along[span, low] = (source[along, span, low].astype(F32) + turn_across[span, low].astype(F32)).astype(BF16)
        to_along[span, high] = source[along, span, high]
        first[chunk][1].wait()
        to_across[span, low] = source[across, span, low]
        to_across[span, high] = (source[across, span, high].astype(F32) + turn_along[span, high].astype(F32)).astype(BF16)
        pair = (
            remote(2, chunk, to_across.at[span], from_across.at[span], across),
            remote(3, chunk, to_along.at[span], from_along.at[span], along),
        )
        for copy in pair:
            copy.start()
        second.append(pair)
    if ready is not None:
        for other, piece in zip((rank, across, along), ready):
            ready_full[other] = piece[...]

    def pass_on(chunk):
        span = spans[chunk]
        for copy in third[chunk]:
            copy.wait()
        pair = (
            remote(6, chunk, full.at[along, span, low], full.at[along, span, low], across),
            remote(7, chunk, full.at[across, span, high], full.at[across, span, high], along),
        )
        for copy in pair:
            copy.start()
        fourth.append(pair)

    if fill:
        fill(rank)
    for chunk, span in enumerate(spans):
        if side:
            side(chunks + chunk)
        for copy in second[chunk]:
            copy.wait()
        total = source[rank, span].astype(F32) + from_across[span].astype(F32) + from_along[span].astype(F32)
        full[rank, span] = math(span, total).astype(BF16)
        pair = (
            remote(4, chunk, full.at[rank, span], full.at[rank, span], across),
            remote(5, chunk, full.at[rank, span], full.at[rank, span], along),
        )
        for copy in pair:
            copy.start()
        third.append(pair)
        if chunk:
            pass_on(chunk - 1)
    pass_on(chunks - 1)
    if ready is not None:
        for copy in extra:
            copy.wait()
    for pair in fourth:
        for copy in pair:
            copy.wait()
    if side:
        side(2 * chunks)


def exchange_call(kernel, number, shape, operands, extra_shapes, scratch=(), in_hbm=()):
    tokens, width = shape
    ranks = 4
    rows = tokens // ranks
    here = pl.BlockSpec(memory_space=pltpu.VMEM)
    results = pl.pallas_call(
        kernel,
        in_specs=[pl.BlockSpec(memory_space=pl.ANY) if k in in_hbm else here for k in range(len(operands))],
        out_specs=[here] * (1 + len(extra_shapes)),
        out_shape=[jax.ShapeDtypeStruct((ranks, rows, width), BF16)]
        + [jax.ShapeDtypeStruct(shape, kind) for shape, kind in extra_shapes],
        scratch_shapes=[pltpu.VMEM((rows, width), BF16)] * 6
        + [pltpu.SemaphoreType.DMA((9, 4))] * 2
        + list(scratch),
        compiler_params=pltpu.CompilerParams(
            vmem_limit_bytes=60 * MIB, collective_id=number, has_side_effects=True
        ),
        cost_estimate=cost(40 * MIB, 200 * MIB),
    )(*operands)
    return results[0].reshape(tokens, width), *results[1:]


def norm_two_kernel(
    source, x_ref, gain_ref, grad_out_ref, routes_ref,
    full, resid_ref, scale_ref, dy_ref, dy_rows_ref, code_ref, codes_ref, own_ref, *rest,
):
    held, load = rest[-2:]
    rank = lax.axis_index("tensor")
    ranks, rows, width = source.shape
    slots = dy_rows_ref.shape[0] // ranks
    own = pltpu.make_async_copy(x_ref.at[:, pl.ds(pl.multiple_of(rank * rows, rows), rows)], held, load.at[0])

    def math(span, total):
        resid = own_ref[span, :].astype(F32) + total
        scale = lax.rsqrt(jnp.sum(resid * resid, axis=1, keepdims=True) / resid.shape[1] + EPS)
        resid_ref[span, :] = resid
        scale_ref[span, :] = scale
        return resid * scale * gain_ref[...]

    def side(number):
        if number == 0:
            own.wait()
            own_ref[...] = held[...].astype(F32).T.astype(BF16)
            local_codes(routes_ref, code_ref, rank % 2, rank // 2, CAP // 2)
            codes_ref[...] = jnp.concatenate([code_ref[...].astype(F32)] * 4, axis=0).T[:, :TOP].astype(jnp.int32)
        if number < ranks:
            span = slice(number * rows, (number + 1) * rows)
            dy_ref[span, :] = grad_out_ref[:, span].astype(F32).T.astype(BF16)
        elif number < 2 * ranks:
            start = (number - ranks) * slots
            slot = lax.broadcasted_iota(jnp.int32, (slots, dy_ref.shape[0]), 0) + start
            take = jnp.where((slot == code_ref[0:1]) | (slot == code_ref[1:2]), 1.0, 0.0).astype(BF16)
            dy_rows_ref[start : start + slots, :] = mm(take, dy_ref[...]).astype(BF16)

    exchange(math, rank, source, full, *rest[:-2], side=side, start=own.start)


def norm_back(grad, value, scale, gain):
    scaled = grad * gain
    inner = jnp.sum(scaled * value, axis=1, keepdims=True)
    return scale * scaled - value * (scale * scale * scale) * (inner / value.shape[1])


def norm_two_back_kernel(
    ret_ref, back_ref, code_ref, codes_ref, gates_ref, routes_ref, dy_rows_ref, gate_ref, router_ref, h_ref,
    resid_ref, scale_ref, dy_ref, gain_ref, full, grad_ref, gain_grad_ref, router_grad_ref, y_ref, *rest,
):
    source, scaled, logit_parts = rest[-3:]
    rank = lax.axis_index("tensor")
    rows = source.shape[1]
    slots, tokens = ret_ref.shape[0], code_ref.shape[1]
    def start():
        found = [jnp.zeros((1, tokens), F32) for _ in range(TOP)]
        tile = slots // 4
        for begin in range(0, slots, tile):
            span = slice(begin, begin + tile)
            ret = ret_ref[span, :].astype(F32)
            slot_grad = jnp.sum(dy_rows_ref[span, :].astype(F32) * ret, axis=1, keepdims=True)
            scaled[span, :] = (ret * gate_ref[span, :]).astype(BF16)
            slot = lax.broadcasted_iota(jnp.int32, (tile, tokens), 0) + begin
            for i in range(TOP):
                found[i] = found[i] + jnp.sum(
                    jnp.where(slot == code_ref[i : i + 1, :], slot_grad, 0.0), axis=0, keepdims=True
                )
        mean = gates_ref[0:1] * found[0] + gates_ref[1:2] * found[1]
        expert = lax.broadcasted_iota(jnp.int32, (EXPERTS, tokens), 0)
        logit = sum(
            jnp.where(routes_ref[i : i + 1] == expert, gates_ref[i : i + 1] * (found[i] - mean), 0.0)
            for i in range(TOP)
        )
        coarse = logit.astype(BF16)
        fine = (logit - coarse.astype(F32)).astype(BF16)
        for shard in range(tokens // rows):
            span = slice(shard * rows, (shard + 1) * rows)
            logit_parts[shard, :EXPERTS] = coarse[:, span]
            logit_parts[shard, EXPERTS:] = fine[:, span]

    def places(shard):
        slot = lax.broadcasted_iota(jnp.int32, (rows, slots), 1)
        codes = codes_ref[pl.ds(pl.multiple_of(shard * rows, rows), rows), :]
        return jnp.where((slot == codes[:, 0:1]) | (slot == codes[:, 1:2]), 1.0, 0.0).astype(BF16)

    def fill(shard):
        value = mm(places(shard), back_ref[...])
        both = jnp.concatenate([router_ref[...], router_ref[...]], axis=0)
        source[shard] = (value + mm(logit_parts[shard], both, TN)).astype(BF16)

    def side(number):
        shards = tokens // rows
        if number < shards:
            y_ref[number * rows : (number + 1) * rows, :] = mm(places(number), scaled[...]).astype(BF16)
        elif number == shards:
            router_grad_ref[...] = sum(
                mm(logit_parts[shard, :EXPERTS], h_ref[shard * rows : (shard + 1) * rows, :])
                for shard in range(shards)
            )

    gain_grad_ref[...] = jnp.zeros_like(gain_grad_ref)

    def math(span, total):
        resid, scale = resid_ref[span, :], scale_ref[span, :]
        gain_grad_ref[...] += jnp.sum(total * resid * scale, axis=0, keepdims=True)
        own_dy = dy_ref[pl.ds(pl.multiple_of(rank * rows + span.start, 128), span.stop - span.start), :]
        grad = norm_back(total, resid, scale, gain_ref[...]) + own_dy.astype(F32)
        grad_ref[span, :] = grad
        return grad

    exchange(math, rank, source, full, *rest[:-3], side=side, fill=fill, start=start)


def norm_one_back_kernel(
    source, x_ref, scale_ref, grad_ref, gain_ref, y_own, y_across, y_along, gain_one_ref, gain_two_ref, router_ref,
    near_ref, far_ref, full, ready_full, small_out, *rest,
):
    held, near, scale, load, tensor_sends, tensor_recvs, expert_sends, expert_recvs = rest[-8:]
    rank, group = lax.axis_index("tensor"), lax.axis_index("expert")
    pair_class, half_index = rank % 2, rank // 2
    others = rank + 1 - 2 * pair_class, rank + 2 - 4 * half_index
    groups = expert_sends.shape[0]
    mesh_ids = pl.DeviceIdType.MESH
    peers = [partner_of(group, step) for step in range(1, groups)]
    summed = slice(0, small_out.shape[0] - BUCKETS)
    rows = source.shape[1]
    loading = pltpu.make_async_copy(near_ref, near, load.at[0])

    def math(span, total):
        x = x_ref[span, :].astype(F32)
        return norm_back(total, x, scale[span, :], gain_ref[...]) + grad_ref[span, :]

    def to_rank(step):
        return pltpu.make_async_remote_copy(
            src_ref=held.at[groups + step], dst_ref=held.at[groups + 2 + step], send_sem=tensor_sends.at[step],
            recv_sem=tensor_recvs.at[step], device_id={"tensor": others[step]}, device_id_type=mesh_ids,
        )

    def to_group(step):
        return pltpu.make_async_remote_copy(
            src_ref=held.at[group], dst_ref=held.at[group], send_sem=expert_sends.at[step],
            recv_sem=expert_recvs.at[step], device_id={"expert": peers[step - 1]}, device_id_type=mesh_ids,
        )

    def start():
        loading.start()
        held[groups] = jnp.zeros(small_out.shape, F32)
        held[groups, :EXPERTS] = router_ref[...]
        held[groups, EXPERTS : EXPERTS + 1] = gain_two_ref[...]
        held[groups, EXPERTS + 1 : EXPERTS + 2] = jnp.broadcast_to(gain_one_ref[...], (gain_one_ref.shape[0], 128)).T[:1]
        to_rank(0).start()

    def side(number):
        if number == 0:
            own_scale = scale_ref[:, pl.ds(pl.multiple_of(rank * rows, rows), rows)]
            scale[...] = jnp.broadcast_to(own_scale, (8, rows)).T[:, :1]
            loading.wait()
            held[group] = jnp.zeros(small_out.shape, F32)
            held[group, summed.stop :, :128] = bias_fold(near, far_ref)
        elif number == 1:
            to_rank(0).wait()
            held[groups + 1] = held[groups] + held[groups + 2]
            to_rank(1).start()
        elif number == 5:
            to_rank(1).wait()
            held[group, summed] = held[groups + 1, summed] + held[groups + 3, summed]
            for step in range(1, groups):
                to_group(step).start()
        elif number == 8:
            for step in range(1, groups):
                to_group(step).wait()
            total = held[0]
            for step in range(1, groups):
                total = total + held[step]
            small_out[...] = total

    exchange(
        math, rank, source, full, *rest[:-8], (y_own, y_across, y_along), ready_full, side=side, peers=peers, start=start
    )


def local_codes(routes_ref, code_ref, pair_class, half_index, half):
    tokens = routes_ref.shape[1]
    expert = lax.broadcasted_iota(jnp.int32, (EXPERTS, BLK), 0)
    earlier = (
        lax.broadcasted_iota(jnp.int32, (BLK, BLK), 0) < lax.broadcasted_iota(jnp.int32, (BLK, BLK), 1)
    ).astype(F32).astype(BF16)
    carry = jnp.zeros((EXPERTS, 1), F32)
    for block in range(tokens // BLK):
        cols = slice(block * BLK, (block + 1) * BLK)
        routes = routes_ref[:, cols]
        hits = [(routes[i : i + 1] == expert) for i in range(TOP)]
        chosen = sum(hit.astype(F32) for hit in hits)
        before = mm(chosen.astype(BF16), earlier) + carry
        carry = carry + jnp.sum(chosen, axis=1, keepdims=True)
        for i in range(TOP):
            slot = jnp.sum(jnp.where(hits[i], before, 0.0), axis=0, keepdims=True).astype(jnp.int32)
            route = routes[i : i + 1]
            owner = route // 2
            local = slot - half_index * half
            mine = (route - 2 * owner == pair_class) & (local >= 0) & (local < half)
            code_ref[i : i + 1, cols] = jnp.where(mine, owner * half + local, -1)


def dispatch_kernel(code_ref, routes_ref, router_ref, h_ref, dy_rows_ref, rows_ref, grads_ref, gate_ref, gates_ref):
    count, tokens = rows_ref.shape[0], h_ref.shape[0]

    @pl.when(pl.program_id(0) == 0)
    def _():
        expert = lax.broadcasted_iota(jnp.int32, (EXPERTS, tokens), 0)
        logits = mm(router_ref[...], h_ref[...], NT)
        picked = [
            jnp.sum(jnp.where(routes_ref[i : i + 1] == expert, logits, 0.0), axis=0, keepdims=True)
            for i in range(TOP)
        ]
        top = jnp.maximum(picked[0], picked[1])
        raised = [jnp.exp(value - top) for value in picked]
        total = raised[0] + raised[1]
        for i in range(TOP):
            gates_ref[i : i + 1] = raised[i] / total

    slot = lax.broadcasted_iota(jnp.int32, (count, tokens), 0) + pl.program_id(0) * count
    hits = [slot == code_ref[i : i + 1, :] for i in range(TOP)]
    take = jnp.where(hits[0] | hits[1], 1.0, 0.0).astype(BF16)
    weighted = jnp.where(hits[0], gates_ref[0:1, :], jnp.where(hits[1], gates_ref[1:2, :], 0.0))
    gate = jnp.sum(weighted, axis=1, keepdims=True)
    rows_ref[...] = mm(take, h_ref[...]).astype(BF16)
    grads_ref[...] = (dy_rows_ref[...].astype(F32) * gate).astype(BF16)
    gate_ref[...] = gate


def dispatch(code, routes_t, router_t, h, dy_rows):
    slots, width = dy_rows.shape
    tile = slots // 4
    row_spec = pl.BlockSpec((tile, width), lambda i: (i, 0))
    whole = lambda shape: pl.BlockSpec(shape, lambda i: (0, 0))
    return pl.pallas_call(
        dispatch_kernel,
        grid=(4,),
        in_specs=[whole(code.shape), whole(code.shape), whole(router_t.shape), whole(h.shape), row_spec],
        out_specs=[row_spec, row_spec, pl.BlockSpec((tile, 1), lambda i: (i, 0)), whole(code.shape)],
        out_shape=[jax.ShapeDtypeStruct((slots, width), BF16)] * 2
        + [jax.ShapeDtypeStruct((slots, 1), F32), jax.ShapeDtypeStruct(code.shape, F32)],
        compiler_params=params(),
        cost_estimate=cost(4 * slots * SEQ * width, 4 * MIB + 6 * slots * width),
    )(code, routes_t, router_t, h, dy_rows)


def gelu_parts(x):
    inner = 0.7978845608028654 * (x + 0.044715 * (x * x * x))
    bend = jnp.tanh(inner)
    half = 0.5 * (1.0 + bend)
    slope = half + 0.5 * x * (1.0 - bend * bend) * (
        0.7978845608028654 * (1.0 + 3.0 * 0.044715 * (x * x))
    )
    return x * half, slope


def partner_of(index, step):
    found = index
    for bit in (1, 2, 4):
        found = found + ((step // bit) % 2) * (1 - 2 * ((index // bit) % 2)) * bit
    return found


def expert_kernel(
    rows_in, grads_in, gate_in, up_in, down_in, far_gate,
    ret_out, back_out, own_gate, own_up, own_down, got_gate, got_up, got_down,
    rows, grads, weights, sums, parts, z_send, z_recv, y_send, y_recv, p_send, p_recv, r_send, r_recv, w_send, w_recv, g_send, g_recv, local,
):
    groups, half, width = rows.shape[1:]
    group, rank = lax.axis_index("expert"), lax.axis_index("tensor")
    pair_class, half_index = rank % 2, rank // 2
    across = {"tensor": rank + 1 - 2 * pair_class}
    along = {"tensor": rank + 2 - 4 * half_index}
    mesh_ids = pl.DeviceIdType.MESH
    moved = ((rows_in, rows, ret_out), (grads_in, grads, back_out))

    barrier = pltpu.get_barrier_semaphore()
    for step in range(1, groups):
        pl.semaphore_signal(
            barrier, inc=1, device_id={"expert": partner_of(group, step)}, device_id_type=mesh_ids
        )
    pl.semaphore_signal(barrier, inc=1, device_id=across, device_id_type=mesh_ids)
    pl.semaphore_signal(barrier, inc=1, device_id=along, device_id_type=mesh_ids)
    pl.semaphore_wait(barrier, groups + 1)

    def remote(source, target, send, recv, device):
        return pltpu.make_async_remote_copy(
            src_ref=source, dst_ref=target, send_sem=send, recv_sem=recv,
            device_id=device, device_id_type=mesh_ids,
        )

    def block(ref, number):
        return ref.at[pl.ds(pl.multiple_of(number * half, half), half)]

    def out_of(kind, step):
        source, held, _ = moved[kind]
        other = partner_of(group, step)
        return remote(
            block(source, other), held.at[0, group], z_send.at[kind, step], z_recv.at[kind, step], {"expert": other}
        )

    def forward(kind, step):
        held = moved[kind][1]
        other = partner_of(group, step)
        return remote(held.at[0, other], held.at[1, other], y_send.at[kind, step], y_recv.at[kind, step], along)

    def partial_sum(kind, step):
        held = moved[kind][1]
        other = partner_of(group, step)
        return remote(held.at[1, other], parts.at[kind, other], p_send.at[kind, step], p_recv.at[kind, step], along)

    def result(kind, step):
        other = partner_of(group, step)
        return remote(
            parts.at[kind, other], block(moved[kind][2], group), r_send.at[kind, step], r_recv.at[kind, step], {"expert": other}
        )

    def own_result(kind):
        return pltpu.make_async_copy(parts.at[kind, group], block(moved[kind][2], group), local.at[kind])

    own = [
        pltpu.make_async_copy(block(moved[kind][0], group), moved[kind][1].at[0, group], local.at[kind])
        for kind in range(2)
    ]
    for copy in own:
        copy.start()
    kept = [
        pltpu.make_async_copy(ref.at[pair_class], weights.at[number, 0], local.at[2 + number])
        for number, ref in enumerate((gate_in, up_in, down_in))
    ]
    kept.append(pltpu.make_async_copy(far_gate, weights.at[0, 1], local.at[5]))
    kept += [
        remote(ref.at[1 - pair_class], weights.at[number, 1], w_send.at[number - 1], w_recv.at[number - 1], across)
        for number, ref in ((1, up_in), (2, down_in))
    ]
    for copy in kept:
        copy.start()
    for step in range(1, groups):
        for kind in range(2):
            out_of(kind, step).start()

    def arrive(step):
        for kind in range(2):
            out_of(kind, step).wait()
            forward(kind, step).start()

    def give(step):
        for kind in range(2):
            partial_sum(kind, step).start()

    for number in range(3):
        for part in range(2):
            sums[number, part] = jnp.zeros(sums.shape[2:], F32)

    def finish(step):
        other = partner_of(group, step)
        for kind in range(2):
            partial_sum(kind, step).wait()
            held = moved[kind][1]
            parts[kind, other] = (parts[kind, other].astype(F32) + held[0, other].astype(F32)).astype(BF16)

        for kind in range(2):
            if step == 0:
                own_result(kind).start()
            else:
                result(kind, step).start()

    def act(plan):
        for action, step in plan:
            action(step)

    order = (0, 1, 4, 5, 2, 6, 3, 7)
    before = {
        0: [(arrive, 1), (arrive, 2), (arrive, 3), (arrive, 4)],
        1: [(give, 0)],
        2: [(arrive, 5)],
        3: [(give, 4), (finish, 0)],
        4: [(arrive, 6)],
        5: [(give, 5), (finish, 4)],
        6: [(arrive, 7)],
        7: [(give, 6), (finish, 5)],
    }
    ahead = [(give, 7)]
    last = [(give, 2), (finish, 6), (give, 3), (finish, 7), (give, 1), (finish, 2), (finish, 3), (finish, 1)]
    for copy in own:
        copy.wait()
    for kind in range(2):
        forward(kind, 0).start()

    def body(turn, carry):
        for number, plan in before.items():
            pl.when(turn == number)(partial(act, plan))

        @pl.when(turn == 0)
        def _():
            for copy in kept:
                copy.wait()

        step = sum((turn == number).astype(jnp.int32) * which for number, which in enumerate(order))
        for kind in range(2):
            forward(kind, step).wait()
        other = partner_of(group, step)
        tile = jnp.concatenate([rows[0, other], rows[1, other]], axis=0)
        grad = jnp.concatenate([grads[0, other], grads[1, other]], axis=0)
        ret = jnp.zeros(tile.shape, F32)
        back = jnp.zeros(tile.shape, F32)
        for part in range(2):
            w_gate, w_up, w_down = weights[0, part], weights[1, part], weights[2, part]
            gate_part = mm(tile, w_gate, NT)
            up_part = mm(tile, w_up, NT)
            grad_hidden = mm(grad, w_down, NT)
            bent, slope = gelu_parts(gate_part)
            hidden = (bent * up_part).astype(BF16)
            grad_gate = (grad_hidden * up_part * slope).astype(BF16)
            grad_up = (grad_hidden * bent).astype(BF16)
            ret = ret + mm(hidden, w_down)
            back = back + mm(grad_gate, w_gate) + mm(grad_up, w_up)
            sums[0, part] += mm(grad_gate, tile, TN)
            sums[1, part] += mm(grad_up, tile, TN)
            sums[2, part] += mm(hidden, grad, TN)
        for kind, value in enumerate((ret, back)):
            held = moved[kind][1]
            held[0, other] = value[:half].astype(BF16)
            held[1, other] = value[half:].astype(BF16)

        return carry

    lax.fori_loop(0, groups, body, 0)
    act(ahead)
    copies = []
    for number, (own_ref, got_ref) in enumerate(((own_gate, got_gate), (own_up, got_up), (own_down, got_down))):
        weights[number, 0] = sums[number, 1].astype(BF16)
        copies.append(remote(weights.at[number, 0], got_ref, g_send.at[number], g_recv.at[number], across))
        copies[-1].start()
        copies.append(pltpu.make_async_copy(sums.at[number, 0], own_ref, local.at[2 + number]))
        copies[-1].start()
    act(last)
    for copy in copies:
        copy.wait()
    for kind in range(2):
        own_result(kind).wait()
        for step in range(1, groups):
            result(kind, step).wait()


def run_experts(rows, grads, w_gate, w_up, w_down, far_gate):
    slots, width = rows.shape
    half = CAP // 2
    groups = slots // half
    units = w_gate.shape[1]
    anywhere = pl.BlockSpec(memory_space=pl.ANY)
    pair = pltpu.SemaphoreType.DMA((2, groups))
    return pl.pallas_call(
        expert_kernel,
        in_specs=[anywhere] * 6,
        out_specs=[anywhere] * 8,
        out_shape=[jax.ShapeDtypeStruct((slots, width), BF16)] * 2
        + [jax.ShapeDtypeStruct((units, width), F32)] * 3
        + [jax.ShapeDtypeStruct((units, width), BF16)] * 3,
        scratch_shapes=[
            pltpu.VMEM((2, groups, half, width), BF16),
            pltpu.VMEM((2, groups, half, width), BF16),
            pltpu.VMEM((3, 2, units, width), BF16),
            pltpu.VMEM((3, 2, units, width), F32),
            pltpu.VMEM((2, groups, half, width), BF16),
        ]
        + [pair] * 8
        + [pltpu.SemaphoreType.DMA((2,))] * 2
        + [pltpu.SemaphoreType.DMA((3,))] * 2
        + [pltpu.SemaphoreType.DMA((6,))],
        compiler_params=pltpu.CompilerParams(
            vmem_limit_bytes=60 * MIB, collective_id=1, has_side_effects=True
        ),
        cost_estimate=cost(72 * slots * units * width, 16 * slots * width + 30 * units * width),
    )(rows, grads, w_gate, w_up, w_down, far_gate)


def finish_kernel(
    place_ref, rows_ref, y_ref, own_ref, got_ref, summed_ref, small_ref,
    output_ref, grad_ref, placed_ref, in_ref, out_ref, one_ref, two_ref, router_ref, bias_ref,
):
    step = pl.program_id(0)
    output_ref[...] = y_ref[...].astype(F32).T.astype(BF16)
    grad_ref[...] = rows_ref[...].astype(F32).T
    placed_ref[place_ref[0]] = own_ref[...]
    placed_ref[1 - place_ref[0]] = got_ref[...].astype(F32)

    @pl.when(step < 3)
    def _():
        in_ref[...] = summed_ref[...].astype(F32)

    @pl.when(step == 3)
    def _():
        out_ref[...] = summed_ref[...].astype(F32)
        router_ref[...] = small_ref[:EXPERTS]
        two_ref[...] = small_ref[EXPERTS : EXPERTS + 1]
        one_ref[...] = small_ref[EXPERTS + 1 : EXPERTS + 2]
        bias_ref[...] = small_ref[EXPERTS + 8 :, :128].T[: bias_ref.shape[0]]


def finish_outputs(place, rows, y_rows, own, got, summed, small, heads):
    tokens, width = rows.shape
    units = own.shape[0]
    steps = 4
    tile, part, block = tokens // steps, units // steps, summed.shape[0] // steps
    quarter = pl.BlockSpec((part, width), lambda i: (i, 0))
    token_spec = pl.BlockSpec((tile, width), lambda i: (i, 0))
    feature_spec = pl.BlockSpec((width, tile), lambda i: (0, i))
    whole = lambda *shape: pl.BlockSpec(shape, lambda i: (0, 0))
    return pl.pallas_call(
        finish_kernel,
        grid=(steps,),
        in_specs=[
            pl.BlockSpec(memory_space=pltpu.SMEM),
            token_spec,
            token_spec,
            quarter,
            quarter,
            pl.BlockSpec((block, width), lambda i: (i, 0)),
            whole(*small.shape),
        ],
        out_specs=[
            feature_spec,
            feature_spec,
            pl.BlockSpec((2, part, width), lambda i: (0, i, 0)),
            pl.BlockSpec((block, width), lambda i: (jnp.minimum(i, 2), 0)),
            whole(block, width),
            whole(1, width),
            whole(1, width),
            whole(EXPERTS, width),
            whole(heads, BUCKETS),
        ],
        out_shape=[
            jax.ShapeDtypeStruct((width, tokens), BF16),
            jax.ShapeDtypeStruct((width, tokens), F32),
            jax.ShapeDtypeStruct((2, units, width), F32),
            jax.ShapeDtypeStruct((3 * block, width), F32),
            jax.ShapeDtypeStruct((block, width), F32),
            jax.ShapeDtypeStruct((1, width), F32),
            jax.ShapeDtypeStruct((1, width), F32),
            jax.ShapeDtypeStruct((EXPERTS, width), F32),
            jax.ShapeDtypeStruct((heads, BUCKETS), F32),
        ],
        compiler_params=params(),
        cost_estimate=cost(0, 10 * rows.size + 14 * own.size + 6 * summed.size),
    )(place, rows, y_rows, own, got, summed, small)


def on_device(
    layer_input, gain_one, attn_in, rel_bias, attn_out, gain_two, router,
    expert_gate, expert_up, expert_down, routes, piece_starts, grad_out,
):
    width, tokens = layer_input.shape
    ranks = lax.axis_size("tensor")
    groups = lax.axis_size("expert")
    rank = lax.axis_index("tensor")
    pair_class, half_index = rank % 2, rank // 2
    half = CAP // 2

    def trade(weights):
        other = lax.dynamic_index_in_dim(weights, 1 - pair_class, 0, keepdims=False)
        return lax.ppermute(other, "tensor", [(r, r ^ 1) for r in range(ranks)])

    traded = trade(expert_gate)
    gain_col = gain_one[:, None]
    w_in = attn_in.reshape(-1, width)
    qkv, scale_one = project(layer_input, gain_col, w_in)
    tiles = bias_tiles(rel_bias)
    position = jnp.arange(SEQ, dtype=jnp.int32)[None, None, :]
    starts = piece_starts[:, :, None]
    inside = (position >= starts) & (position < starts + PIECE)
    last = jnp.max(jnp.where(inside, starts + (PIECE - 1), -1), axis=1)
    limits = jnp.maximum(last, position[0])[:, None, :]

    routes_t = routes.T
    place = jnp.stack([pair_class, half_index]).astype(jnp.int32)
    share = tokens // ranks

    def by_rank(rows):
        return rows.reshape(ranks, share, width)

    mixed, lse, sent = attend(qkv, tiles, limits, attn_out)
    sent, traded = lax.optimization_barrier((sent, traded))
    slots = groups * half
    h2, resid, scale_two, dy, dy_rows, code, code_cols, own_x = exchange_call(
        norm_two_kernel, 2, sent.shape, [by_rank(sent), layer_input, gain_two[None], grad_out, routes_t],
        [((share, width), F32), ((share, 1), F32), ((tokens, width), BF16), ((slots, width), BF16)]
        + [((TOP, tokens), jnp.int32), ((tokens, TOP), jnp.int32), ((share, width), BF16)],
        [pltpu.VMEM((width, share), BF16), pltpu.SemaphoreType.DMA((1,))],
        (1,),
    )
    rows, row_grads, gate_rows, gates = dispatch(code, routes_t, router.T, h2, dy_rows)
    ret, back, *weight_grads = run_experts(
        rows, row_grads, expert_gate, expert_up, expert_down, traded
    )
    grad_attn, grad_resid, grad_gain_two, grad_router, partial_y = exchange_call(
        norm_two_back_kernel, 3, (tokens, width),
        [ret, back, code, code_cols, gates, routes_t, dy_rows, gate_rows, router.T, h2]
        + [resid, scale_two, dy, gain_two[None]],
        [((share, width), F32), ((1, width), F32), ((EXPERTS, width), F32), ((tokens, width), BF16)],
        [
            pltpu.VMEM((ranks, share, width), BF16),
            pltpu.VMEM((slots, width), BF16),
            pltpu.VMEM((ranks, 2 * EXPERTS, share), BF16),
        ],
    )

    dq, dk, dv, near, far, y_own = attend_back(
        qkv, tiles, limits, attn_out, grad_attn, lse, by_rank(partial_y), resid
    )
    dq, y_own = lax.optimization_barrier((dq, y_own))
    y_across = lax.ppermute(y_own, "tensor", [(r, r ^ 1) for r in range(ranks)])
    y_along = lax.ppermute(y_own, "tensor", [(r, r ^ 2) for r in range(ranks)])
    weight_rows, sent, grad_gain_one, grad_gate, grad_up = project_back(
        place, layer_input, gain_col, scale_one, w_in, mixed, grad_attn, (dq, dk, dv),
        weight_grads[:2], weight_grads[3:5],
    )
    sent, y_across, y_along = lax.optimization_barrier((sent, y_across, y_along))
    summed = lax.psum(weight_rows, "expert")
    small_shape = (EXPERTS + 8 + BUCKETS, width)
    grad_rows, y_full, small = exchange_call(
        norm_one_back_kernel, 4, sent.shape,
        [by_rank(sent), own_x, scale_one, grad_resid, gain_one[None], y_own, y_across, y_along]
        + [grad_gain_one, grad_gain_two, grad_router, near, far],
        [((ranks, share, width), BF16), (small_shape, F32)],
        [pltpu.VMEM((groups + 4, *small_shape), F32), pltpu.VMEM(near.shape, F32), pltpu.VMEM((share, 1), F32)]
        + [pltpu.SemaphoreType.DMA((1,))]
        + [pltpu.SemaphoreType.DMA((2,))] * 2
        + [pltpu.SemaphoreType.DMA((groups,))] * 2,
        (11,),
    )
    summed, grad_rows = lax.optimization_barrier((summed, grad_rows))
    layer_output, grad_input, grad_down, grad_in, grad_attn_out, grad_one, grad_two, grad_router, grad_bias = finish_outputs(
        place, grad_rows, y_full.reshape(tokens, width), weight_grads[2], weight_grads[5], summed, small, rel_bias.shape[1]
    )
    return (
        layer_output,
        grad_input,
        grad_one[0],
        grad_in.reshape(attn_in.shape),
        grad_bias.T,
        grad_attn_out,
        grad_two[0],
        grad_router.T,
        grad_gate,
        grad_up,
        grad_down,
    )


def allowed_pairs(seq_starts):
    position = jnp.arange(SEQ, dtype=jnp.int32)
    inside = (position[:, None] >= seq_starts[None, :]) & (
        position[:, None] < seq_starts[None, :] + PIECE
    )
    numbers = jnp.arange(seq_starts.shape[0], dtype=jnp.int32) + 1
    piece_label = jnp.sum(inside.astype(jnp.int32) * numbers[None, :], axis=1)
    causal = position[None, :] <= position[:, None]
    shared = (piece_label[:, None] == piece_label[None, :]) & (piece_label[:, None] > 0)
    return causal | shared


def slot_table(routes):
    flat_routes = routes.reshape(-1)
    onehot = (flat_routes[:, None] == jnp.arange(EXPERTS, dtype=jnp.int32)[None, :]).astype(
        jnp.int32
    )
    blocks = onehot.reshape(-1, 128, EXPERTS).astype(F32)
    earlier = jnp.tril(jnp.ones((128, 128), F32), -1)
    inside = jnp.einsum("ij,bje->bie", earlier, blocks)
    count = blocks.shape[0]
    carried = jnp.einsum("ab,be->ae", jnp.tril(jnp.ones((count, count), F32), -1), jnp.sum(blocks, axis=1), precision=HIGH)
    before = (inside + carried[:, None, :]).astype(jnp.int32).reshape(onehot.shape)
    slot_number = jnp.sum(before * onehot, axis=1)
    kept_pairs = slot_number < CAP
    slot_index = jnp.where(kept_pairs, flat_routes * CAP + slot_number, EXPERTS * CAP)
    return (slot_index.reshape(routes.shape), kept_pairs.reshape(routes.shape))


def bucket_onehot():
    offsets = jnp.arange(2 * SEQ - 1, dtype=jnp.int32) - (SEQ - 1)
    return (bucket_of(offsets)[:, None] == jnp.arange(BUCKETS, dtype=jnp.int32)[None, :]).astype(
        jnp.float32
    )


def expand_line(line):
    head_count = line.shape[0]
    padded = jnp.concatenate([line, jnp.zeros((head_count, 1), line.dtype)], axis=1)
    tiled = jnp.tile(padded, (1, SEQ))[:, : SEQ * (2 * SEQ - 1)].reshape(
        head_count, SEQ, 2 * SEQ - 1
    )
    return tiled[:, :, SEQ - 1 :]


def fold_line(full_grid):
    head_count = full_grid.shape[0]
    padded = jnp.pad(full_grid, ((0, 0), (0, 0), (SEQ - 1, 0))).reshape(
        head_count, SEQ * (2 * SEQ - 1)
    )
    padded = jnp.pad(padded, ((0, 0), (0, SEQ))).reshape(head_count, SEQ, 2 * SEQ)
    return jnp.sum(padded, axis=1)[:, : 2 * SEQ - 1]


def reduce_heads(tensor_value):
    return lax.psum(tensor_value, "tensor")


def spread_slots(tensor_value):
    return lax.all_gather(tensor_value, "tensor", axis=2, tiled=True)


def owner_exchange(tensor_value):
    return lax.all_to_all(tensor_value, "expert", split_axis=0, concat_axis=0, tiled=True)


def expert_sums(tensor_value):
    return lax.psum_scatter(tensor_value, "tensor", scatter_dimension=2, tiled=True)


def norm_forward(resid, gain, model_width):
    scale = lax.rsqrt(jnp.sum(resid * resid, axis=1) / model_width + EPS)[:, None]
    return (scale, (resid * scale * gain).astype(jnp.bfloat16))


def norm_backward(resid, scale, gain, grad_normed, model_width):
    grad_gain = jnp.sum(grad_normed * resid * scale, axis=0)
    scaled = grad_normed * gain
    inner = jnp.sum(scaled * resid, axis=1)[:, None]
    return (grad_gain, scale * scaled - resid * scale**3 * inner / model_width)


def attend_scores(bias_full, queries, key_rows, seq_starts):
    scores = (
        jnp.einsum("qhe,khe->hqk", queries, key_rows, preferred_element_type=jnp.float32) * 0.125
        + bias_full
    )
    return jnp.where(allowed_pairs(seq_starts)[None], scores, NEG)


def attend_forward(bias_full, inputs):
    queries, key_rows, value_rows, seq_starts = inputs
    scores = attend_scores(bias_full, queries, key_rows, seq_starts)
    row_max = jnp.max(scores, axis=2, keepdims=True)
    exponent = jnp.exp(scores - row_max)
    row_sum_exp = jnp.sum(exponent, axis=2, keepdims=True)
    weights = (exponent / row_sum_exp).astype(jnp.bfloat16)
    mixed_heads = jnp.einsum(
        "hqk,khe->qhe", weights, value_rows, preferred_element_type=jnp.float32
    )
    return (mixed_heads.astype(jnp.bfloat16), (row_max + jnp.log(row_sum_exp))[:, :, 0])


def attend_backward(bias_full, running, inputs):
    queries, key_rows, value_rows, grad_heads, seq_starts, log_total = inputs
    scores = attend_scores(bias_full, queries, key_rows, seq_starts)
    probabilities = jnp.exp(scores - log_total[:, :, None])
    grad_probs = jnp.einsum(
        "qhe,khe->hqk", grad_heads, value_rows, preferred_element_type=jnp.float32
    )
    inner = jnp.sum(probabilities * grad_probs, axis=2, keepdims=True)
    grad_scores = (probabilities * (grad_probs - inner)).astype(jnp.bfloat16)
    grad_values = jnp.einsum(
        "hqk,qhe->khe",
        probabilities.astype(jnp.bfloat16),
        grad_heads,
        preferred_element_type=jnp.float32,
    )
    grad_queries = (
        jnp.einsum("hqk,khe->qhe", grad_scores, key_rows, preferred_element_type=jnp.float32)
        * 0.125
    )
    grad_keys = (
        jnp.einsum("hqk,qhe->khe", grad_scores, queries, preferred_element_type=jnp.float32) * 0.125
    )
    return (
        running + grad_scores.astype(jnp.float32),
        jnp.stack([grad_queries, grad_keys, grad_values]),
    )


def gelu_product(left, right):
    return jax.nn.gelu(left, approximate=True) * right


def expert_forward(received, weight_gate, weight_up, weight_down):
    gate_part = jnp.einsum(
        "secd,efd->secf", received, weight_gate, preferred_element_type=jnp.float32
    )
    up_part = jnp.einsum("secd,efd->secf", received, weight_up, preferred_element_type=jnp.float32)
    hidden = gelu_product(gate_part, up_part).astype(jnp.bfloat16)
    partial_out = jnp.einsum(
        "secf,efd->secd", hidden, weight_down, preferred_element_type=jnp.float32
    )
    return (gate_part, up_part, hidden, partial_out)


def expert_backward(
    received, gate_part, up_part, hidden, grad_rows_out, weight_gate, weight_up, weight_down
):
    grad_hidden = jnp.einsum(
        "secd,efd->secf", grad_rows_out, weight_down, preferred_element_type=jnp.float32
    )
    product_value, pullback = jax.vjp(gelu_product, gate_part, up_part)
    grad_gate_part, grad_up_part = pullback(grad_hidden)
    grad_gate_part = grad_gate_part.astype(jnp.bfloat16)
    grad_up_part = grad_up_part.astype(jnp.bfloat16)
    grad_down = jnp.einsum(
        "secf,secd->efd", hidden, grad_rows_out, preferred_element_type=jnp.float32
    )
    grad_gate_w = jnp.einsum(
        "secf,secd->efd", grad_gate_part, received, preferred_element_type=jnp.float32
    )
    grad_up_w = jnp.einsum(
        "secf,secd->efd", grad_up_part, received, preferred_element_type=jnp.float32
    )
    grad_rows_in = jnp.einsum(
        "secf,efd->secd", grad_gate_part, weight_gate, preferred_element_type=jnp.float32
    )
    grad_rows_in = grad_rows_in + jnp.einsum(
        "secf,efd->secd", grad_up_part, weight_up, preferred_element_type=jnp.float32
    )
    return (grad_gate_w, grad_up_w, grad_down, grad_rows_in)


def on_device_general(
    layer_input,
    gain_one,
    attn_in,
    rel_bias,
    attn_out,
    gain_two,
    router,
    expert_gate,
    expert_up,
    expert_down,
    routes,
    piece_starts,
    grad_out,
):
    tok_count = layer_input.shape[1]
    model_width = layer_input.shape[0]
    heads_here = rel_bias.shape[1]
    head_width = attn_in.shape[1] // heads_here
    seqs_here = piece_starts.shape[0]
    local_experts = expert_gate.shape[0]
    part_rows = CAP // lax.axis_size("tensor")
    share_start = lax.axis_index("tensor") * part_rows
    tokens = layer_input.T.astype(jnp.float32)
    scale_one, normed = norm_forward(tokens, gain_one, model_width)
    project = jnp.einsum("td,chd->cth", normed, attn_in, preferred_element_type=jnp.float32).astype(
        jnp.bfloat16
    )
    by_seq = project.reshape(3, seqs_here, SEQ, heads_here, head_width)
    onehot_line = bucket_onehot()
    bias_full = expand_line(jnp.dot(onehot_line, rel_bias, precision=HIGH).T)
    mixed_heads, log_total = lax.map(
        partial(attend_forward, bias_full), (by_seq[0], by_seq[1], by_seq[2], piece_starts)
    )
    mixed_heads = mixed_heads.reshape(tok_count, heads_here * head_width)
    resid = tokens + reduce_heads(
        jnp.dot(mixed_heads, attn_out, preferred_element_type=jnp.float32)
    )
    scale_two, normed_two = norm_forward(resid, gain_two, model_width)
    logits = jnp.dot(normed_two, router, preferred_element_type=jnp.float32)
    chosen = (routes[:, :, None] == jnp.arange(EXPERTS, dtype=jnp.int32)[None, None, :]).astype(
        jnp.float32
    )
    picked = jnp.sum(chosen * logits[:, None, :], axis=2)
    gate_weights = jax.nn.softmax(picked, axis=1)
    slot_index, kept_pairs = slot_table(routes)
    keep_float = kept_pairs.astype(jnp.float32)
    mix_weight = gate_weights * keep_float
    safe_index = jnp.minimum(slot_index, EXPERTS * CAP - 1)
    token_rows = jnp.repeat(normed_two, TOP, axis=0)
    buffer = (
        jnp.zeros((EXPERTS * CAP + 1, model_width), jnp.bfloat16)
        .at[slot_index.reshape(-1)]
        .set(token_rows)
    )
    buffer = buffer[: EXPERTS * CAP].reshape(-1, local_experts, CAP, model_width)
    received = lax.all_to_all(buffer, "expert", split_axis=0, concat_axis=0, tiled=True)
    gate_part, up_part, hidden, partial_out = expert_forward(
        received, expert_gate, expert_up, expert_down
    )
    returned = spread_slots(owner_exchange(expert_sums(partial_out).astype(jnp.bfloat16)))
    flat_ret = returned.reshape(EXPERTS * CAP, model_width)
    fetched = flat_ret[safe_index].astype(jnp.float32)
    output = resid + jnp.sum(mix_weight[:, :, None] * fetched, axis=1)
    grad_y = grad_out.T.astype(jnp.float32)
    grad_gates = jnp.sum(grad_y[:, None, :] * fetched, axis=2) * keep_float
    grad_picked = gate_weights * (
        grad_gates - jnp.sum(gate_weights * grad_gates, axis=1, keepdims=True)
    )
    grad_logits = jnp.sum(chosen * grad_picked[:, :, None], axis=1)
    grad_router = jnp.dot(normed_two.astype(jnp.float32).T, grad_logits, precision=HIGH)
    grad_normed_two = jnp.dot(grad_logits, router.astype(jnp.float32).T, precision=HIGH)
    slot_grads = (mix_weight[:, :, None] * grad_y[:, None, :]).astype(jnp.bfloat16)
    grad_ret = (
        jnp.zeros((EXPERTS * CAP + 1, model_width), jnp.bfloat16)
        .at[slot_index.reshape(-1)]
        .set(slot_grads.reshape(-1, model_width))
    )
    grad_ret = grad_ret[: EXPERTS * CAP].reshape(-1, local_experts, CAP, model_width)
    grad_share = lax.dynamic_slice_in_dim(grad_ret, share_start, part_rows, 2)
    grad_rows_out = spread_slots(owner_exchange(grad_share))
    grad_expert_gate, grad_expert_up, grad_expert_down, grad_rows_in = expert_backward(
        received, gate_part, up_part, hidden, grad_rows_out, expert_gate, expert_up, expert_down
    )
    grad_back = spread_slots(owner_exchange(expert_sums(grad_rows_in).astype(jnp.bfloat16)))
    flat_back = grad_back.reshape(EXPERTS * CAP, model_width).astype(jnp.float32)
    grad_normed_two = grad_normed_two + jnp.sum(
        flat_back[safe_index] * keep_float[:, :, None], axis=1
    )
    grad_gain_two, grad_resid = norm_backward(
        resid, scale_two, gain_two, grad_normed_two, model_width
    )
    grad_resid = grad_resid + grad_y
    grad_attn = grad_resid.astype(jnp.bfloat16)
    grad_attn_out = jnp.einsum(
        "th,td->hd", mixed_heads, grad_attn, preferred_element_type=jnp.float32
    )
    grad_mixed = jnp.einsum(
        "td,hd->th", grad_attn, attn_out, preferred_element_type=jnp.float32
    ).astype(jnp.bfloat16)
    grad_by_seq = grad_mixed.reshape(seqs_here, SEQ, heads_here, head_width)
    bias_grad_full, grad_project = lax.scan(
        partial(attend_backward, bias_full),
        jnp.zeros_like(bias_full),
        (by_seq[0], by_seq[1], by_seq[2], grad_by_seq, piece_starts, log_total),
    )
    grad_project = (
        jnp.moveaxis(grad_project, 1, 0)
        .reshape(3, tok_count, heads_here * head_width)
        .astype(jnp.bfloat16)
    )
    grad_attn_in = jnp.einsum(
        "cth,td->chd", grad_project, normed, preferred_element_type=jnp.float32
    )
    grad_normed = reduce_heads(
        jnp.einsum("cth,chd->td", grad_project, attn_in, preferred_element_type=jnp.float32)
    )
    grad_gain_one, grad_tokens = norm_backward(
        tokens, scale_one, gain_one, grad_normed, model_width
    )
    grad_tokens = grad_tokens + grad_resid
    grad_rel_bias = jnp.dot(onehot_line.T, fold_line(bias_grad_full).T, precision=HIGH)
    shared = (
        lax.psum(grad_gain_one.astype(jnp.bfloat16), "expert").astype(jnp.float32),
        lax.psum(grad_attn_in.astype(jnp.bfloat16), "expert").astype(jnp.float32),
        lax.psum(grad_rel_bias.astype(jnp.bfloat16), "expert").astype(jnp.float32),
        lax.psum(grad_attn_out.astype(jnp.bfloat16), "expert").astype(jnp.float32),
        lax.psum(grad_gain_two.astype(jnp.bfloat16), "expert").astype(jnp.float32),
        lax.psum(grad_router.astype(jnp.bfloat16), "expert").astype(jnp.float32),
    )
    return (
        output.astype(jnp.bfloat16).T,
        grad_tokens.T,
        shared[0],
        shared[1],
        shared[2],
        shared[3],
        shared[4],
        shared[5],
        grad_expert_gate,
        grad_expert_up,
        grad_expert_down,
    )


def solution(mesh):
    placed = (
        P(None, "expert"),
        P(),
        P(None, "tensor", None),
        P(None, "tensor"),
        P("tensor", None),
        P(),
        P(),
        P("expert", "tensor", None),
        P("expert", "tensor", None),
        P("expert", "tensor", None),
        P("expert", None),
        P("expert", None),
        P(None, "expert"),
    )
    paired = mesh.shape["tensor"] == 4 and mesh.shape["expert"] * 2 == EXPERTS
    return jax.shard_map(
        on_device if paired else on_device_general,
        mesh=mesh,
        in_specs=placed,
        out_specs=(
            P(None, "expert"),
            P(None, "expert"),
            P(),
            P(None, "tensor", None),
            P(None, "tensor"),
            P("tensor", None),
            P(),
            P(),
            P("expert", "tensor", None),
            P("expert", "tensor", None),
            P("expert", "tensor", None),
        ),
        check_vma=False,
    )
```

```python
from functools import partial

import jax
import jax.numpy as jnp
from jax import lax
from jax.experimental import pallas as pl
from jax.experimental.pallas import tpu as pltpu
from jax.sharding import PartitionSpec as P

EXPERTS = 16
BUCKETS = 32
TOP = 2
PIECE = 256
SEQ = 1024
CAP = 320
BLK = 256


EPS = 1e-06
NEG = -1e30
THRESHOLDS = (12, 16, 23, 32, 46, 64, 91)
HIGH = lax.Precision.HIGHEST
F32 = jnp.float32
BF16 = jnp.bfloat16
NN = (((1,), (0,)), ((), ()))
NT = (((1,), (1,)), ((), ()))
TN = (((0,), (0,)), ((), ()))
MIB = 1 << 20


def mm(left, right, dims=NN):
    return lax.dot_general(left, right, dims, preferred_element_type=F32)


def params(limit=56):
    return pltpu.CompilerParams(vmem_limit_bytes=limit * MIB)


def cost(flops, bytes_accessed, transcendentals=0):
    return pl.CostEstimate(
        flops=int(flops), bytes_accessed=int(bytes_accessed), transcendentals=int(transcendentals)
    )


def bucket_of(offset):
    magnitude = jnp.abs(offset)
    beyond = sum(((magnitude >= threshold).astype(jnp.int32) for threshold in THRESHOLDS))
    lower_part = jnp.where(magnitude < 8, magnitude, 8 + beyond)
    return lower_part + 16 * (offset > 0).astype(jnp.int32)


def project_kernel(x_ref, gain_ref, w_ref, out_ref, scale_ref):
    x = x_ref[...].astype(F32)
    scale = lax.rsqrt(jnp.sum(x * x, axis=0, keepdims=True) / x.shape[0] + EPS)
    normed = (x * scale * gain_ref[...]).astype(BF16)
    out_ref[...] = mm(w_ref[...], normed).astype(BF16)
    scale_ref[...] = scale


def project(x, gain, weights):
    width, tokens = x.shape
    rows = weights.shape[0]
    tile = 512
    return pl.pallas_call(
        project_kernel,
        grid=(tokens // tile,),
        in_specs=[
            pl.BlockSpec((width, tile), lambda i: (0, i)),
            pl.BlockSpec((width, 1), lambda i: (0, 0)),
            pl.BlockSpec((rows, width), lambda i: (0, 0)),
        ],
        out_specs=[
            pl.BlockSpec((rows, tile), lambda i: (0, i)),
            pl.BlockSpec((1, tile), lambda i: (0, i)),
        ],
        out_shape=[
            jax.ShapeDtypeStruct((rows, tokens), BF16),
            jax.ShapeDtypeStruct((1, tokens), F32),
        ],
        compiler_params=params(),
        cost_estimate=cost(2 * width * tokens * rows, 2 * width * tokens * 2),
    )(x, gain, weights)


def line_offsets(number):
    column = lax.broadcasted_iota(jnp.int32, (8, BLK), 1)
    return (number - 1) * BLK - column


def bias_tiles_kernel(table_ref, tiles_ref):
    row = lax.broadcasted_iota(jnp.int32, (BLK, BLK), 0)
    column = lax.broadcasted_iota(jnp.int32, (BLK, BLK), 1)
    buckets = [bucket_of(line_offsets(number)) for number in range(4)]
    for head in range(tiles_ref.shape[0]):
        far = table_ref[15, head]
        rolled = []
        for number, bucket in enumerate(buckets):
            value = jnp.zeros((8, BLK), F32)
            for index in range(BUCKETS):
                value = jnp.where(bucket == index, table_ref[index, head] - far, value)
            whole = jnp.broadcast_to(value[0:1], (BLK, BLK))
            rolled.append(pltpu.roll(whole, 0, 1, stride=1, stride_axis=0))
        for number in range(3):
            tiles_ref[head, number] = jnp.where(column >= row, rolled[number], rolled[number + 1])


def bias_tiles(table):
    heads = table.shape[1]
    return pl.pallas_call(
        bias_tiles_kernel,
        in_specs=[pl.BlockSpec(memory_space=pltpu.SMEM)],
        out_specs=pl.BlockSpec(memory_space=pltpu.VMEM),
        out_shape=jax.ShapeDtypeStruct((heads, 3, BLK, BLK), F32),
        compiler_params=params(),
        cost_estimate=cost(heads * 3 * BLK * BLK * 60, heads * 3 * BLK * BLK * 4),
    )(table)


def bias_fold(near_ref, far_ref):
    heads = near_ref.shape[0] // 2
    sums = jnp.zeros((BUCKETS, 128), F32)
    lane = lax.broadcasted_iota(jnp.int32, (BUCKETS, 128), 1)
    row = lax.broadcasted_iota(jnp.int32, (BLK, BLK), 0)
    column = lax.broadcasted_iota(jnp.int32, (BLK, BLK), 1)
    flip = jnp.where(row + column == BLK - 1, 1.0, 0.0).astype(BF16)
    apart = jnp.where(column == BLK - 1, 0, column + 1)
    ahead = apart <= row
    number_at = lax.broadcasted_iota(jnp.int32, (BUCKETS, BLK), 0)
    for head in range(heads):
        lines = [jnp.zeros((1, BLK), F32) for _ in range(4)]
        for number in range(3):
            grads = near_ref[head, number] + near_ref[heads + head, number]
            coarse = grads.astype(BF16)
            fine = (grads - coarse.astype(F32)).astype(BF16)
            flipped = mm(flip, coarse) + mm(flip, fine)
            rolled = pltpu.roll(flipped, 0, 1, stride=1, stride_axis=0)
            lines[number] += jnp.sum(jnp.where(ahead, rolled, 0.0), axis=0, keepdims=True)
            lines[number + 1] += jnp.sum(jnp.where(ahead, 0.0, rolled), axis=0, keepdims=True)
        total = jnp.zeros((BUCKETS, 1), F32)
        for number, line in enumerate(lines):
            bucket = bucket_of((number - 1) * BLK - apart[:1])
            total += jnp.sum(jnp.where(bucket == number_at, line, 0.0), axis=1, keepdims=True)
        distant = jnp.sum(far_ref[head] + far_ref[heads + head], axis=0, keepdims=True)
        distant = jnp.sum(distant, axis=1, keepdims=True)
        total += jnp.where(number_at[:, :1] == 15, distant, 0.0)
        sums = jnp.where(lane == head, total, sums)
    return sums


def key_count(query_block):
    return 2 * BLK if query_block < 2 else 4 * BLK


def block_scores(keys, queries, tiles_ref, limit, block):
    count = key_count(block)
    parts = []
    whole = mm(keys[:, :count], queries, TN)
    for key_block in range(count // BLK):
        part = whole[key_block * BLK : (key_block + 1) * BLK]
        shift = key_block - block
        if -1 <= shift <= 1:
            part = part + tiles_ref[0, shift + 1]
        if shift >= 0:
            key_at = lax.broadcasted_iota(jnp.int32, (BLK, BLK), 0) + key_block * BLK
            part = jnp.where(key_at <= limit, part, NEG)
        parts.append(part)
    return jnp.concatenate(parts, axis=0)


def attend_kernel(q_ref, k_ref, v_ref, tiles_ref, limit_ref, w_ref, out_ref, lse_ref, sent_ref, held):
    head = pl.program_id(1)
    width = q_ref.shape[0]
    queries = q_ref[...] * BF16(0.125)
    keys, values = k_ref[...], v_ref[...]
    for block in range(SEQ // BLK):
        cols = slice(block * BLK, (block + 1) * BLK)
        scores = block_scores(keys, queries[:, cols], tiles_ref, limit_ref[0, :, cols], block)
        top = jnp.max(scores, axis=0, keepdims=True)
        exponent = jnp.exp(scores - top)
        total = jnp.sum(exponent, axis=0, keepdims=True)
        mixed = mm(values[:, : key_count(block)], exponent.astype(BF16)) / total
        mixed = mixed.astype(BF16)
        out_ref[:, cols] = mixed
        held[pl.ds(pl.multiple_of(head * width, width), width), cols] = mixed
        lse_ref[0, :, cols] = top + jnp.log(total)

    @pl.when(head == pl.num_programs(1) - 1)
    def _():
        sent_ref[...] = mm(held[...], w_ref[...], TN).astype(BF16)


def attend(qkv, tiles, limits, attn_out):
    heads = tiles.shape[0]
    seqs = limits.shape[0]
    width = qkv.shape[0] // (3 * heads)
    model_width = attn_out.shape[1]
    return pl.pallas_call(
        attend_kernel,
        grid=(seqs, heads),
        in_specs=[
            pl.BlockSpec((width, SEQ), lambda s, h: (h, s)),
            pl.BlockSpec((width, SEQ), lambda s, h: (heads + h, s)),
            pl.BlockSpec((width, SEQ), lambda s, h: (2 * heads + h, s)),
            pl.BlockSpec((1, 3, BLK, BLK), lambda s, h: (h, 0, 0, 0)),
            pl.BlockSpec((1, 1, SEQ), lambda s, h: (s, 0, 0)),
            pl.BlockSpec((heads * width, model_width), lambda s, h: (0, 0)),
        ],
        out_specs=[
            pl.BlockSpec((width, SEQ), lambda s, h: (h, s)),
            pl.BlockSpec((1, 1, SEQ), lambda s, h: (s * heads + h, 0, 0)),
            pl.BlockSpec((SEQ, model_width), lambda s, h: (s, 0)),
        ],
        out_shape=[
            jax.ShapeDtypeStruct((heads * width, seqs * SEQ), BF16),
            jax.ShapeDtypeStruct((seqs * heads, 1, SEQ), F32),
            jax.ShapeDtypeStruct((seqs * SEQ, model_width), BF16),
        ],
        scratch_shapes=[pltpu.VMEM((heads * width, SEQ), BF16)],
        compiler_params=params(),
        cost_estimate=cost(seqs * heads * SEQ * SEQ * 512, seqs * heads * SEQ * 2048, seqs * heads * SEQ * SEQ),
    )(qkv, qkv, qkv, tiles, limits, attn_out)


def attend_back_kernel(
    q_ref, k_ref, v_ref, tiles_ref, limit_ref, w_ref, grad_ref, lse_ref, part_ref, resid_ref,
    dq_ref, dk_ref, dv_ref, near_ref, far_ref, y_ref,
    held, parts, total, turn_across, turn_along, from_across, from_along, sends, recvs, loads,
):
    rank = lax.axis_index("tensor")
    pair_class, half_index = rank % 2, rank // 2
    across, along, corner = rank + 1 - 2 * pair_class, rank + 2 - 4 * half_index, 3 - rank
    step = pl.program_id(0) * pl.num_programs(1) + pl.program_id(1)
    mesh_ids = pl.DeviceIdType.MESH
    middle = parts.shape[2] // 2
    low, high = slice(0, middle), slice(middle, 2 * middle)

    def remote(number, origin, target, other):
        return pltpu.make_async_remote_copy(
            src_ref=origin, dst_ref=target, send_sem=sends.at[number], recv_sem=recvs.at[number],
            device_id={"tensor": other}, device_id_type=mesh_ids,
        )

    first = (
        remote(0, part_ref.at[corner, :, low], turn_across, across),
        remote(1, part_ref.at[corner, :, high], turn_along, along),
    )
    second = remote(2, parts.at[0], from_across, across), remote(3, parts.at[1], from_along, along)
    local = [
        pltpu.make_async_copy(part_ref.at[other], parts.at[number], loads.at[number])
        for number, other in enumerate((across, along, rank))
    ]
    local.append(pltpu.make_async_copy(resid_ref, total, loads.at[3]))

    @pl.when(step == 0)
    def _():
        barrier = pltpu.get_barrier_semaphore()
        for other in (across, along):
            pl.semaphore_signal(barrier, inc=1, device_id={"tensor": other}, device_id_type=mesh_ids)
        pl.semaphore_wait(barrier, 2)
        for copy in first:
            copy.start()
        for copy in local:
            copy.start()

    @pl.when(step == 3)
    def _():
        for copy in (*first, *local):
            copy.wait()
        parts[0, :, high] = (parts[0, :, high].astype(F32) + turn_along[...].astype(F32)).astype(BF16)
        parts[1, :, low] = (parts[1, :, low].astype(F32) + turn_across[...].astype(F32)).astype(BF16)
        for copy in second:
            copy.start()

    head = pl.program_id(1)
    width = q_ref.shape[0]

    @pl.when(head == 0)
    def _():
        held[...] = mm(w_ref[...], grad_ref[...], NT).astype(BF16)

    queries = q_ref[...] * BF16(0.125)
    keys, values = k_ref[...], v_ref[...]
    grads = held[pl.ds(pl.multiple_of(head * width, width), width), :]
    near_ref[...] = jnp.zeros_like(near_ref)
    far = jnp.zeros((8, BLK), F32)
    grad_keys = jnp.zeros((width, SEQ), F32)
    grad_values = jnp.zeros((width, SEQ), F32)
    for block in range(SEQ // BLK):
        count = key_count(block)
        cols = slice(block * BLK, (block + 1) * BLK)
        scores = block_scores(keys, queries[:, cols], tiles_ref, limit_ref[0, :, cols], block)
        probs = jnp.exp(scores - lse_ref[0, :, cols])
        grad_probs = mm(values[:, :count], grads[:, cols], TN)
        inner = jnp.sum(probs * grad_probs, axis=0, keepdims=True)
        grad_scores = probs * (grad_probs - inner)
        for key_block in range(count // BLK):
            part = grad_scores[key_block * BLK : (key_block + 1) * BLK]
            shift = key_block - block
            if -1 <= shift <= 1:
                near_ref[0, shift + 1] += part
            elif shift < -1:
                far = far + jnp.sum(part.reshape(BLK // 8, 8, BLK), axis=0)
        rounded = grad_scores.astype(BF16)
        add_values = mm(grads[:, cols], probs.astype(BF16), NT)
        add_keys = mm(queries[:, cols], rounded, NT)
        if count == SEQ:
            grad_values = grad_values + add_values
            grad_keys = grad_keys + add_keys
        else:
            filler = jnp.zeros((width, SEQ - count), F32)
            grad_values = grad_values + jnp.concatenate([add_values, filler], axis=1)
            grad_keys = grad_keys + jnp.concatenate([add_keys, filler], axis=1)
        dq_ref[:, cols] = (mm(keys[:, :count], rounded) * 0.125).astype(BF16)
    dk_ref[...] = grad_keys.astype(BF16)
    dv_ref[...] = grad_values.astype(BF16)
    far_ref[0] = far

    @pl.when(step == 7)
    def _():
        for copy in second:
            copy.wait()
        summed = parts[2].astype(F32) + from_across[...].astype(F32) + from_along[...].astype(F32)
        y_ref[...] = (total[...] + summed).astype(BF16)


def attend_back(qkv, tiles, limits, attn_out, grad_attn, lse, part, resid):
    heads = tiles.shape[0]
    seqs = limits.shape[0]
    width = qkv.shape[0] // (3 * heads)
    model_width = attn_out.shape[1]
    share = part.shape[1]
    grad_spec = pl.BlockSpec((width, SEQ), lambda s, h: (h, s))
    anywhere = pl.BlockSpec(memory_space=pl.ANY)
    return pl.pallas_call(
        attend_back_kernel,
        grid=(seqs, heads),
        in_specs=[
            pl.BlockSpec((width, SEQ), lambda s, h: (h, s)),
            pl.BlockSpec((width, SEQ), lambda s, h: (heads + h, s)),
            pl.BlockSpec((width, SEQ), lambda s, h: (2 * heads + h, s)),
            pl.BlockSpec((1, 3, BLK, BLK), lambda s, h: (h, 0, 0, 0)),
            pl.BlockSpec((1, 1, SEQ), lambda s, h: (s, 0, 0)),
            pl.BlockSpec((heads * width, model_width), lambda s, h: (0, 0)),
            pl.BlockSpec((SEQ, model_width), lambda s, h: (s, 0)),
            pl.BlockSpec((1, 1, SEQ), lambda s, h: (s * heads + h, 0, 0)),
        ]
        + [anywhere] * 2,
        out_specs=[
            grad_spec,
            grad_spec,
            grad_spec,
            pl.BlockSpec((1, 3, BLK, BLK), lambda s, h: (s * heads + h, 0, 0, 0)),
            pl.BlockSpec((1, 8, BLK), lambda s, h: (s * heads + h, 0, 0)),
            pl.BlockSpec((share, model_width), lambda s, h: (0, 0)),
        ],
        out_shape=[jax.ShapeDtypeStruct((heads * width, seqs * SEQ), BF16)] * 3
        + [
            jax.ShapeDtypeStruct((seqs * heads, 3, BLK, BLK), F32),
            jax.ShapeDtypeStruct((seqs * heads, 8, BLK), F32),
        ]
        + [jax.ShapeDtypeStruct((share, model_width), BF16)],
        scratch_shapes=[
            pltpu.VMEM((heads * width, SEQ), BF16),
            pltpu.VMEM((3, share, model_width), BF16),
            pltpu.VMEM((share, model_width), F32),
            pltpu.VMEM((share, model_width // 2), BF16),
            pltpu.VMEM((share, model_width // 2), BF16),
            pltpu.VMEM((share, model_width), BF16),
            pltpu.VMEM((share, model_width), BF16),
            pltpu.SemaphoreType.DMA((4,)),
            pltpu.SemaphoreType.DMA((4,)),
            pltpu.SemaphoreType.DMA((4,)),
        ],
        compiler_params=pltpu.CompilerParams(
            vmem_limit_bytes=60 * MIB, collective_id=5, has_side_effects=True
        ),
        cost_estimate=cost(seqs * heads * SEQ * SEQ * 1280, seqs * heads * SEQ * 4096, seqs * heads * SEQ * SEQ),
    )(qkv, qkv, qkv, tiles, limits, attn_out, grad_attn, lse, part, resid)


def project_back_kernel(
    place_ref, x_ref, gain_ref, gain_row_ref, scale_ref, w_ref, mixed_ref, attn_ref, dq_ref, dk_ref, dv_ref, *refs
):
    step = pl.program_id(0)
    own_refs, got_refs, (weight_ref, out_ref, gain_grad_ref), placed_refs, total = (
        refs[:2], refs[2:4], refs[4:7], refs[7:9], refs[9]
    )
    for own_ref, got_ref, placed_ref in zip(own_refs, got_refs, placed_refs):
        placed_ref[place_ref[0]] = own_ref[...]
        placed_ref[1 - place_ref[0]] = got_ref[...].astype(F32)
    grads = jnp.concatenate([dq_ref[...], dk_ref[...], dv_ref[...]], axis=0)
    rows = grads.shape[0]
    normed = (x_ref[...].astype(F32) * scale_ref[...] * gain_ref[...]).astype(BF16)

    @pl.when(step == 0)
    def _():
        total[...] = jnp.zeros_like(total)

    total[:rows] += mm(grads, normed, NT)
    total[rows:] += mm(mixed_ref[...], attn_ref[...])
    out_ref[...] = mm(grads, w_ref[...], TN).astype(BF16)

    @pl.when(step == pl.num_programs(0) - 1)
    def _():
        weight_ref[...] = total[...].astype(BF16)
        through = jnp.sum(total[:rows] * w_ref[...].astype(F32), axis=0, keepdims=True)
        gain_grad_ref[...] = through / gain_row_ref[...]


def project_back(place, x, gain, gain_row, scale, weights, mixed, grad_attn, grads, owns, gots):
    width, tokens = x.shape
    rows = weights.shape[0]
    heads_width = mixed.shape[0]
    units = owns[0].shape[0]
    steps = 4
    tile = tokens // steps
    part = units // steps
    column = lambda count: pl.BlockSpec((count, tile), lambda i: (0, i))
    return pl.pallas_call(
        project_back_kernel,
        grid=(steps,),
        in_specs=[
            pl.BlockSpec(memory_space=pltpu.SMEM),
            column(width),
            pl.BlockSpec((width, 1), lambda i: (0, 0)),
            pl.BlockSpec((1, width), lambda i: (0, 0)),
            column(1),
            pl.BlockSpec((rows, width), lambda i: (0, 0)),
            column(heads_width),
            pl.BlockSpec((tile, width), lambda i: (i, 0)),
        ]
        + [column(rows // 3)] * 3
        + [pl.BlockSpec((part, width), lambda i: (i, 0))] * 4,
        out_specs=[
            pl.BlockSpec((rows + heads_width, width), lambda i: (0, 0)),
            pl.BlockSpec((tile, width), lambda i: (i, 0)),
            pl.BlockSpec((1, width), lambda i: (0, 0)),
        ]
        + [pl.BlockSpec((2, part, width), lambda i: (0, i, 0))] * 2,
        out_shape=[
            jax.ShapeDtypeStruct((rows + heads_width, width), BF16),
            jax.ShapeDtypeStruct((tokens, width), BF16),
            jax.ShapeDtypeStruct((1, width), F32),
        ]
        + [jax.ShapeDtypeStruct((2, units, width), F32)] * 2,
        scratch_shapes=[pltpu.VMEM((rows + heads_width, width), F32)],
        compiler_params=params(),
        cost_estimate=cost(5 * width * tokens * rows, 6 * width * tokens + 14 * units * width),
    )(place, x, gain, gain_row, scale, weights, mixed, grad_attn, *grads, *owns, *gots)


def exchange(math, rank, source, full, from_across, from_along, to_across, to_along, turn_across, turn_along, sends, recvs, ready=None, ready_full=None, side=None, peers=(), fill=None, start=None, cut=None, later=None):
    pair_class, half_index = rank % 2, rank // 2
    across, along, corner = rank + 1 - 2 * pair_class, rank + 2 - 4 * half_index, 3 - rank
    mesh_ids = pl.DeviceIdType.MESH
    rows, width = source.shape[1:]
    chunks = 4
    size = rows // chunks
    cut = cut or width // 2
    low, high = slice(0, cut), slice(cut, width)
    barrier = pltpu.get_barrier_semaphore()
    near = (across, along, corner) if later else (across, along)
    for other in near:
        pl.semaphore_signal(barrier, inc=1, device_id={"tensor": other}, device_id_type=mesh_ids)
    for other in peers:
        pl.semaphore_signal(barrier, inc=1, device_id={"expert": other}, device_id_type=mesh_ids)
    pl.semaphore_wait(barrier, len(near) + len(peers))

    def remote(kind, chunk, origin, target, other):
        return pltpu.make_async_remote_copy(
            src_ref=origin, dst_ref=target, send_sem=sends.at[kind, chunk], recv_sem=recvs.at[kind, chunk],
            device_id={"tensor": other}, device_id_type=mesh_ids,
        )

    if start:
        start()
    if fill:
        fill(corner)
    spans = [slice(chunk * size, (chunk + 1) * size) for chunk in range(chunks)]
    first, second, third, fourth = [], [], [], []
    for chunk, span in enumerate(spans):
        pair = (
            remote(0, chunk, source.at[corner, span, low], turn_across.at[span, low], across),
            remote(1, chunk, source.at[corner, span, high], turn_along.at[span, high], along),
        )
        for copy in pair:
            copy.start()
        first.append(pair)
    if fill:
        fill(along)
        fill(across)
    if ready is not None:
        _, near_across, near_along = ready
        extra = [
            remote(8, 0, near_along.at[:, low], ready_full.at[along, :, low], across),
            remote(8, 1, near_across.at[:, high], ready_full.at[across, :, high], along),
        ]
        for copy in extra:
            copy.start()
    for chunk, span in enumerate(spans):
        if side:
            side(chunk)
        first[chunk][0].wait()
        to_along[span, low] = (source[along, span, low].astype(F32) + turn_across[span, low].astype(F32)).astype(BF16)
        to_along[span, high] = source[along, span, high]
        first[chunk][1].wait()
        to_across[span, low] = source[across, span, low]
        to_across[span, high] = (source[across, span, high].astype(F32) + turn_along[span, high].astype(F32)).astype(BF16)
        pair = (
            remote(2, chunk, to_across.at[span], from_across.at[span], across),
            remote(3, chunk, to_along.at[span], from_along.at[span], along),
        )
        for copy in pair:
            copy.start()
        second.append(pair)
    if ready is not None:
        for other, piece in zip((rank, across, along), ready):
            ready_full[other] = piece[...]

    def pass_on(chunk):
        span = spans[chunk]
        for copy in third[chunk]:
            copy.wait()
        pair = (
            remote(6, chunk, full.at[along, span, low], full.at[along, span, low], across),
            remote(7, chunk, full.at[across, span, high], full.at[across, span, high], along),
        )
        for copy in pair:
            copy.start()
        fourth.append(pair)

    if fill:
        fill(rank)
    if later:
        later((across, along, corner))
    for chunk, span in enumerate(spans):
        if side:
            side(chunks + chunk)
        for copy in second[chunk]:
            copy.wait()
        total = source[rank, span].astype(F32) + from_across[span].astype(F32) + from_along[span].astype(F32)
        full[rank, span] = math(span, total).astype(BF16)
        pair = (
            remote(4, chunk, full.at[rank, span], full.at[rank, span], across),
            remote(5, chunk, full.at[rank, span], full.at[rank, span], along),
        )
        for copy in pair:
            copy.start()
        third.append(pair)
        if chunk:
            pass_on(chunk - 1)
    pass_on(chunks - 1)
    if ready is not None:
        for copy in extra:
            copy.wait()
    if side and later:
        side(2 * chunks)
    for pair in fourth:
        for copy in pair:
            copy.wait()
    if side and not later:
        side(2 * chunks)


def exchange_call(kernel, number, shape, operands, extra_shapes, scratch=(), in_hbm=()):
    tokens, width = shape
    ranks = 4
    rows = tokens // ranks
    here = pl.BlockSpec(memory_space=pltpu.VMEM)
    results = pl.pallas_call(
        kernel,
        in_specs=[pl.BlockSpec(memory_space=pl.ANY) if k in in_hbm else here for k in range(len(operands))],
        out_specs=[here] * (1 + len(extra_shapes)),
        out_shape=[jax.ShapeDtypeStruct((ranks, rows, width), BF16)]
        + [jax.ShapeDtypeStruct(shape, kind) for shape, kind in extra_shapes],
        scratch_shapes=[pltpu.VMEM((rows, width), BF16)] * 6
        + [pltpu.SemaphoreType.DMA((9, 4))] * 2
        + list(scratch),
        compiler_params=pltpu.CompilerParams(
            vmem_limit_bytes=60 * MIB, collective_id=number, has_side_effects=True
        ),
        cost_estimate=cost(40 * MIB, 200 * MIB),
    )(*operands)
    return results[0].reshape(tokens, width), *results[1:]


def norm_two_kernel(
    source, x_ref, gain_ref, grad_out_ref, routes_ref,
    full, resid_ref, scale_ref, dy_ref, dy_rows_ref, code_ref, codes_ref, own_ref, *rest,
):
    held, load = rest[-2:]
    rank = lax.axis_index("tensor")
    ranks, rows, width = source.shape
    slots = dy_rows_ref.shape[0] // ranks
    own = pltpu.make_async_copy(x_ref.at[:, pl.ds(pl.multiple_of(rank * rows, rows), rows)], held, load.at[0])

    def math(span, total):
        resid = own_ref[span, :].astype(F32) + total
        scale = lax.rsqrt(jnp.sum(resid * resid, axis=1, keepdims=True) / resid.shape[1] + EPS)
        resid_ref[span, :] = resid
        scale_ref[span, :] = scale
        return resid * scale * gain_ref[...]

    def side(number):
        if number == 0:
            own.wait()
            own_ref[...] = held[...].astype(F32).T.astype(BF16)
            local_codes(routes_ref, code_ref, rank % 2, rank // 2, CAP // 2)
            codes_ref[...] = jnp.concatenate([code_ref[...].astype(F32)] * 4, axis=0).T[:, :TOP].astype(jnp.int32)
        if number < ranks:
            span = slice(number * rows, (number + 1) * rows)
            dy_ref[span, :] = grad_out_ref[:, span].astype(F32).T.astype(BF16)
        elif number < 2 * ranks:
            start = (number - ranks) * slots
            slot = lax.broadcasted_iota(jnp.int32, (slots, dy_ref.shape[0]), 0) + start
            take = jnp.where((slot == code_ref[0:1]) | (slot == code_ref[1:2]), 1.0, 0.0).astype(BF16)
            dy_rows_ref[start : start + slots, :] = mm(take, dy_ref[...]).astype(BF16)

    exchange(math, rank, source, full, *rest[:-2], side=side, start=own.start)


def norm_back(grad, value, scale, gain):
    scaled = grad * gain
    inner = jnp.sum(scaled * value, axis=1, keepdims=True)
    return scale * scaled - value * (scale * scale * scale) * (inner / value.shape[1])


def norm_two_back_kernel(
    ret_ref, back_ref, code_ref, codes_ref, gates_ref, routes_ref, dy_rows_ref, gate_ref, router_ref, h_ref,
    resid_ref, scale_ref, dy_ref, gain_ref, full, grad_ref, gain_grad_ref, router_grad_ref, y_ref, *rest,
):
    source, scaled, logit_parts, logit_own, send, recv = rest[-6:]
    rank = lax.axis_index("tensor")
    rows = source.shape[1]
    slots, tokens = ret_ref.shape[0], code_ref.shape[1]
    ranks = tokens // rows
    copies = []

    def later(others):
        found = [jnp.zeros((1, tokens), F32) for _ in range(TOP)]
        tile = slots // 4
        for begin in range(0, slots, tile):
            span = slice(begin, begin + tile)
            ret = ret_ref[span, :].astype(F32)
            slot_grad = jnp.sum(dy_rows_ref[span, :].astype(F32) * ret, axis=1, keepdims=True)
            scaled[span, :] = (ret * gate_ref[span, :]).astype(BF16)
            slot = lax.broadcasted_iota(jnp.int32, (tile, tokens), 0) + begin
            for i in range(TOP):
                found[i] = found[i] + jnp.sum(
                    jnp.where(slot == code_ref[i : i + 1, :], slot_grad, 0.0), axis=0, keepdims=True
                )
        mean = gates_ref[0:1] * found[0] + gates_ref[1:2] * found[1]
        expert = lax.broadcasted_iota(jnp.int32, (EXPERTS, tokens), 0)
        logit = sum(
            jnp.where(routes_ref[i : i + 1] == expert, gates_ref[i : i + 1] * (found[i] - mean), 0.0)
            for i in range(TOP)
        )
        for shard in range(ranks):
            logit_parts[shard] = logit[:, shard * rows : (shard + 1) * rows]
        for number, other in enumerate(others):
            copies.append(
                pltpu.make_async_remote_copy(
                    src_ref=logit_parts.at[other], dst_ref=logit_parts.at[ranks + number], send_sem=send.at[number],
                    recv_sem=recv.at[number], device_id={"tensor": other}, device_id_type=pl.DeviceIdType.MESH,
                )
            )
            copies[-1].start()

    def places(shard):
        slot = lax.broadcasted_iota(jnp.int32, (rows, slots), 1)
        codes = codes_ref[pl.ds(pl.multiple_of(shard * rows, rows), rows), :]
        return jnp.where((slot == codes[:, 0:1]) | (slot == codes[:, 1:2]), 1.0, 0.0).astype(BF16)

    def fill(shard):
        source[shard] = mm(places(shard), back_ref[...]).astype(BF16)

    def side(number):
        if number == ranks:
            router_grad_ref[...] = sum(
                mm(logit_parts[shard].astype(BF16), h_ref[shard * rows : (shard + 1) * rows, :])
                for shard in range(ranks)
            )
            for copy in copies:
                copy.wait()
            logit = logit_parts[rank] + logit_parts[ranks] + logit_parts[ranks + 1] + logit_parts[ranks + 2]
            coarse = logit.astype(BF16)
            logit_own[:EXPERTS] = coarse
            logit_own[EXPERTS:] = (logit - coarse.astype(F32)).astype(BF16)
        elif number > ranks:
            shard = number - ranks - 1
            y_ref[shard * rows : (shard + 1) * rows, :] = mm(places(shard), scaled[...]).astype(BF16)

    gain_grad_ref[...] = jnp.zeros_like(gain_grad_ref)

    def math(span, total):
        resid, scale = resid_ref[span, :], scale_ref[span, :]
        both = jnp.concatenate([router_ref[...], router_ref[...]], axis=0)
        total = total + mm(logit_own[:, span], both, TN)
        gain_grad_ref[...] += jnp.sum(total * resid * scale, axis=0, keepdims=True)
        own_dy = dy_ref[pl.ds(pl.multiple_of(rank * rows + span.start, 128), span.stop - span.start), :]
        grad = norm_back(total, resid, scale, gain_ref[...]) + own_dy.astype(F32)
        grad_ref[span, :] = grad
        return grad

    exchange(math, rank, source, full, *rest[:-6], side=side, fill=fill, later=later)


def norm_one_back_kernel(
    source, x_ref, scale_ref, grad_ref, gain_ref, y_own, y_across, y_along, gain_one_ref, gain_two_ref, router_ref,
    near_ref, far_ref, full, ready_full, small_out, *rest,
):
    held, gathered, near, scale, load, tensor_sends, tensor_recvs, expert_sends, expert_recvs = rest[-9:]
    rank, group = lax.axis_index("tensor"), lax.axis_index("expert")
    pair_class, half_index = rank % 2, rank // 2
    others = rank + 1 - 2 * pair_class, rank + 2 - 4 * half_index
    groups = expert_sends.shape[0]
    mesh_ids = pl.DeviceIdType.MESH
    peers = [partner_of(group, step) for step in range(1, groups)]
    heads = near_ref.shape[0] // 2
    rows = source.shape[1]
    loading = pltpu.make_async_copy(near_ref, near, load.at[0])

    def math(span, total):
        x = x_ref[span, :].astype(F32)
        return norm_back(total, x, scale[span, :], gain_ref[...]) + grad_ref[span, :]

    def to_rank(step):
        return pltpu.make_async_remote_copy(
            src_ref=held.at[step], dst_ref=held.at[2 + step], send_sem=tensor_sends.at[step],
            recv_sem=tensor_recvs.at[step], device_id={"tensor": others[step]}, device_id_type=mesh_ids,
        )

    def to_group(step):
        return pltpu.make_async_remote_copy(
            src_ref=gathered.at[group], dst_ref=gathered.at[group], send_sem=expert_sends.at[step],
            recv_sem=expert_recvs.at[step], device_id={"expert": peers[step - 1]}, device_id_type=mesh_ids,
        )

    def start():
        loading.start()
        held[0] = jnp.zeros(small_out.shape, F32)
        held[0, :EXPERTS] = router_ref[...]
        held[0, EXPERTS : EXPERTS + 1] = gain_two_ref[...]
        held[0, EXPERTS + 1 : EXPERTS + 2] = gain_one_ref[...]
        to_rank(0).start()

    def side(number):
        if number == 0:
            own_scale = scale_ref[:, pl.ds(pl.multiple_of(rank * rows, rows), rows)]
            scale[...] = jnp.broadcast_to(own_scale, (8, rows)).T[:, :1]
            loading.wait()
            small_out[:BUCKETS, :128] = bias_fold(near, far_ref)
        elif number == 1:
            to_rank(0).wait()
            held[1] = held[0] + held[2]
            to_rank(1).start()
        elif number == 5:
            to_rank(1).wait()
            turned = small_out[:BUCKETS, :128].T
            held[0] = held[1] + held[3]
            held[0, EXPERTS + 2 : EXPERTS + 2 + heads, :BUCKETS] = turned[:heads]
            gathered[group] = held[0].astype(BF16)
            for step in range(1, groups):
                to_group(step).start()
        elif number == 8:
            for step in range(1, groups):
                to_group(step).wait()
            total = gathered[0].astype(F32)
            for step in range(1, groups):
                total = total + gathered[step].astype(F32)
            small_out[...] = total

    exchange(
        math, rank, source, full, *rest[:-9], (y_own, y_across, y_along), ready_full, side=side, peers=peers, start=start
    )


def local_codes(routes_ref, code_ref, pair_class, half_index, half):
    tokens = routes_ref.shape[1]
    expert = lax.broadcasted_iota(jnp.int32, (EXPERTS, BLK), 0)
    earlier = (
        lax.broadcasted_iota(jnp.int32, (BLK, BLK), 0) < lax.broadcasted_iota(jnp.int32, (BLK, BLK), 1)
    ).astype(F32).astype(BF16)
    carry = jnp.zeros((EXPERTS, 1), F32)
    for block in range(tokens // BLK):
        cols = slice(block * BLK, (block + 1) * BLK)
        routes = routes_ref[:, cols]
        hits = [(routes[i : i + 1] == expert) for i in range(TOP)]
        chosen = sum(hit.astype(F32) for hit in hits)
        before = mm(chosen.astype(BF16), earlier) + carry
        carry = carry + jnp.sum(chosen, axis=1, keepdims=True)
        for i in range(TOP):
            slot = jnp.sum(jnp.where(hits[i], before, 0.0), axis=0, keepdims=True).astype(jnp.int32)
            route = routes[i : i + 1]
            owner = route // 2
            local = slot - half_index * half
            mine = (route - 2 * owner == pair_class) & (local >= 0) & (local < half)
            code_ref[i : i + 1, cols] = jnp.where(mine, owner * half + local, -1)


def dispatch_kernel(code_ref, routes_ref, router_ref, h_ref, dy_rows_ref, rows_ref, grads_ref, gate_ref, gates_ref):
    count, tokens = rows_ref.shape[0], h_ref.shape[0]

    @pl.when(pl.program_id(0) == 0)
    def _():
        expert = lax.broadcasted_iota(jnp.int32, (EXPERTS, tokens), 0)
        logits = mm(router_ref[...], h_ref[...], NT)
        picked = [
            jnp.sum(jnp.where(routes_ref[i : i + 1] == expert, logits, 0.0), axis=0, keepdims=True)
            for i in range(TOP)
        ]
        top = jnp.maximum(picked[0], picked[1])
        raised = [jnp.exp(value - top) for value in picked]
        total = raised[0] + raised[1]
        for i in range(TOP):
            gates_ref[i : i + 1] = raised[i] / total

    slot = lax.broadcasted_iota(jnp.int32, (count, tokens), 0) + pl.program_id(0) * count
    hits = [slot == code_ref[i : i + 1, :] for i in range(TOP)]
    take = jnp.where(hits[0] | hits[1], 1.0, 0.0).astype(BF16)
    weighted = jnp.where(hits[0], gates_ref[0:1, :], jnp.where(hits[1], gates_ref[1:2, :], 0.0))
    gate = jnp.sum(weighted, axis=1, keepdims=True)
    rows_ref[...] = mm(take, h_ref[...]).astype(BF16)
    grads_ref[...] = (dy_rows_ref[...].astype(F32) * gate).astype(BF16)
    gate_ref[...] = gate


def dispatch(code, routes_t, router_t, h, dy_rows):
    slots, width = dy_rows.shape
    tile = slots // 4
    row_spec = pl.BlockSpec((tile, width), lambda i: (i, 0))
    whole = lambda shape: pl.BlockSpec(shape, lambda i: (0, 0))
    return pl.pallas_call(
        dispatch_kernel,
        grid=(4,),
        in_specs=[whole(code.shape), whole(code.shape), whole(router_t.shape), whole(h.shape), row_spec],
        out_specs=[row_spec, row_spec, pl.BlockSpec((tile, 1), lambda i: (i, 0)), whole(code.shape)],
        out_shape=[jax.ShapeDtypeStruct((slots, width), BF16)] * 2
        + [jax.ShapeDtypeStruct((slots, 1), F32), jax.ShapeDtypeStruct(code.shape, F32)],
        compiler_params=params(),
        cost_estimate=cost(4 * slots * SEQ * width, 4 * MIB + 6 * slots * width),
    )(code, routes_t, router_t, h, dy_rows)


def gelu_parts(x):
    inner = 0.7978845608028654 * (x + 0.044715 * (x * x * x))
    bend = jnp.tanh(inner)
    half = 0.5 * (1.0 + bend)
    slope = half + 0.5 * x * (1.0 - bend * bend) * (
        0.7978845608028654 * (1.0 + 3.0 * 0.044715 * (x * x))
    )
    return x * half, slope


def partner_of(index, step):
    found = index
    for bit in (1, 2, 4):
        found = found + ((step // bit) % 2) * (1 - 2 * ((index // bit) % 2)) * bit
    return found


def expert_kernel(
    rows_in, grads_in, gate_in, up_in, down_in, far_gate,
    ret_out, back_out, own_gate, own_up, own_down, got_gate, got_up, got_down,
    rows, grads, weights, sums, parts, z_send, z_recv, y_send, y_recv, p_send, p_recv, r_send, r_recv, w_send, w_recv, g_send, g_recv, local,
):
    groups, half, width = rows.shape[1:]
    group, rank = lax.axis_index("expert"), lax.axis_index("tensor")
    pair_class, half_index = rank % 2, rank // 2
    across = {"tensor": rank + 1 - 2 * pair_class}
    along = {"tensor": rank + 2 - 4 * half_index}
    mesh_ids = pl.DeviceIdType.MESH
    moved = ((rows_in, rows, ret_out), (grads_in, grads, back_out))

    barrier = pltpu.get_barrier_semaphore()
    for step in range(1, groups):
        pl.semaphore_signal(
            barrier, inc=1, device_id={"expert": partner_of(group, step)}, device_id_type=mesh_ids
        )
    pl.semaphore_signal(barrier, inc=1, device_id=across, device_id_type=mesh_ids)
    pl.semaphore_signal(barrier, inc=1, device_id=along, device_id_type=mesh_ids)
    pl.semaphore_wait(barrier, groups + 1)

    def remote(source, target, send, recv, device):
        return pltpu.make_async_remote_copy(
            src_ref=source, dst_ref=target, send_sem=send, recv_sem=recv,
            device_id=device, device_id_type=mesh_ids,
        )

    def block(ref, number):
        return ref.at[pl.ds(pl.multiple_of(number * half, half), half)]

    def out_of(kind, step):
        source, held, _ = moved[kind]
        other = partner_of(group, step)
        return remote(
            block(source, other), held.at[0, group], z_send.at[kind, step], z_recv.at[kind, step], {"expert": other}
        )

    def forward(kind, step):
        held = moved[kind][1]
        other = partner_of(group, step)
        return remote(held.at[0, other], held.at[1, other], y_send.at[kind, step], y_recv.at[kind, step], along)

    def partial_sum(kind, step):
        held = moved[kind][1]
        other = partner_of(group, step)
        return remote(held.at[1, other], parts.at[kind, other], p_send.at[kind, step], p_recv.at[kind, step], along)

    def result(kind, step):
        other = partner_of(group, step)
        return remote(
            parts.at[kind, other], block(moved[kind][2], group), r_send.at[kind, step], r_recv.at[kind, step], {"expert": other}
        )

    def own_result(kind):
        return pltpu.make_async_copy(parts.at[kind, group], block(moved[kind][2], group), local.at[kind])

    own = [
        pltpu.make_async_copy(block(moved[kind][0], group), moved[kind][1].at[0, group], local.at[kind])
        for kind in range(2)
    ]
    for copy in own:
        copy.start()
    kept = [
        pltpu.make_async_copy(ref.at[pair_class], weights.at[number, 0], local.at[2 + number])
        for number, ref in enumerate((gate_in, up_in, down_in))
    ]
    kept.append(pltpu.make_async_copy(far_gate, weights.at[0, 1], local.at[5]))
    kept += [
        remote(ref.at[1 - pair_class], weights.at[number, 1], w_send.at[number - 1], w_recv.at[number - 1], across)
        for number, ref in ((1, up_in), (2, down_in))
    ]
    for copy in kept:
        copy.start()
    for step in range(1, groups):
        for kind in range(2):
            out_of(kind, step).start()

    def arrive(step):
        for kind in range(2):
            out_of(kind, step).wait()
            forward(kind, step).start()

    def give(step):
        for kind in range(2):
            partial_sum(kind, step).start()

    for number in range(3):
        for part in range(2):
            sums[number, part] = jnp.zeros(sums.shape[2:], F32)

    def finish(step):
        other = partner_of(group, step)
        for kind in range(2):
            partial_sum(kind, step).wait()
            held = moved[kind][1]
            parts[kind, other] = (parts[kind, other].astype(F32) + held[0, other].astype(F32)).astype(BF16)

        for kind in range(2):
            if step == 0:
                own_result(kind).start()
            else:
                result(kind, step).start()

    def act(plan):
        for action, step in plan:
            action(step)

    order = (0, 1, 4, 5, 2, 6, 3, 7)
    before = {
        0: [(arrive, 1), (arrive, 2), (arrive, 3), (arrive, 4)],
        1: [(give, 0)],
        2: [(arrive, 5)],
        3: [(give, 4), (finish, 0)],
        4: [(arrive, 6)],
        5: [(give, 5), (finish, 4)],
        6: [(arrive, 7)],
        7: [(give, 6), (finish, 5)],
    }
    ahead = [(give, 7)]
    last = [(give, 2), (finish, 6), (give, 3), (finish, 7), (give, 1), (finish, 2), (finish, 3), (finish, 1)]
    for copy in own:
        copy.wait()
    for kind in range(2):
        forward(kind, 0).start()

    def body(turn, carry):
        for number, plan in before.items():
            pl.when(turn == number)(partial(act, plan))

        @pl.when(turn == 0)
        def _():
            for copy in kept:
                copy.wait()

        step = sum((turn == number).astype(jnp.int32) * which for number, which in enumerate(order))
        for kind in range(2):
            forward(kind, step).wait()
        other = partner_of(group, step)
        tile = jnp.concatenate([rows[0, other], rows[1, other]], axis=0)
        grad = jnp.concatenate([grads[0, other], grads[1, other]], axis=0)
        ret = jnp.zeros(tile.shape, F32)
        back = jnp.zeros(tile.shape, F32)
        for part in range(2):
            w_gate, w_up, w_down = weights[0, part], weights[1, part], weights[2, part]
            gate_part = mm(tile, w_gate, NT)
            up_part = mm(tile, w_up, NT)
            grad_hidden = mm(grad, w_down, NT)
            bent, slope = gelu_parts(gate_part)
            hidden = (bent * up_part).astype(BF16)
            grad_gate = (grad_hidden * up_part * slope).astype(BF16)
            grad_up = (grad_hidden * bent).astype(BF16)
            ret = ret + mm(hidden, w_down)
            back = back + mm(grad_gate, w_gate) + mm(grad_up, w_up)
            sums[0, part] += mm(grad_gate, tile, TN)
            sums[1, part] += mm(grad_up, tile, TN)
            sums[2, part] += mm(hidden, grad, TN)
        for kind, value in enumerate((ret, back)):
            held = moved[kind][1]
            held[0, other] = value[:half].astype(BF16)
            held[1, other] = value[half:].astype(BF16)

        return carry

    lax.fori_loop(0, groups, body, 0)
    act(ahead)
    copies = []
    for number, (own_ref, got_ref) in enumerate(((own_gate, got_gate), (own_up, got_up), (own_down, got_down))):
        weights[number, 0] = sums[number, 1].astype(BF16)
        copies.append(remote(weights.at[number, 0], got_ref, g_send.at[number], g_recv.at[number], across))
        copies[-1].start()
        copies.append(pltpu.make_async_copy(sums.at[number, 0], own_ref, local.at[2 + number]))
        copies[-1].start()
    act(last)
    for copy in copies:
        copy.wait()
    for kind in range(2):
        own_result(kind).wait()
        for step in range(1, groups):
            result(kind, step).wait()


def run_experts(rows, grads, w_gate, w_up, w_down, far_gate):
    slots, width = rows.shape
    half = CAP // 2
    groups = slots // half
    units = w_gate.shape[1]
    anywhere = pl.BlockSpec(memory_space=pl.ANY)
    pair = pltpu.SemaphoreType.DMA((2, groups))
    return pl.pallas_call(
        expert_kernel,
        in_specs=[anywhere] * 6,
        out_specs=[anywhere] * 8,
        out_shape=[jax.ShapeDtypeStruct((slots, width), BF16)] * 2
        + [jax.ShapeDtypeStruct((units, width), F32)] * 3
        + [jax.ShapeDtypeStruct((units, width), BF16)] * 3,
        scratch_shapes=[
            pltpu.VMEM((2, groups, half, width), BF16),
            pltpu.VMEM((2, groups, half, width), BF16),
            pltpu.VMEM((3, 2, units, width), BF16),
            pltpu.VMEM((3, 2, units, width), F32),
            pltpu.VMEM((2, groups, half, width), BF16),
        ]
        + [pair] * 8
        + [pltpu.SemaphoreType.DMA((2,))] * 2
        + [pltpu.SemaphoreType.DMA((3,))] * 2
        + [pltpu.SemaphoreType.DMA((6,))],
        compiler_params=pltpu.CompilerParams(
            vmem_limit_bytes=60 * MIB, collective_id=1, has_side_effects=True
        ),
        cost_estimate=cost(72 * slots * units * width, 16 * slots * width + 30 * units * width),
    )(rows, grads, w_gate, w_up, w_down, far_gate)


def finish_kernel(
    place_ref, rows_ref, y_ref, own_ref, got_ref, summed_ref, small_ref,
    output_ref, grad_ref, placed_ref, in_ref, out_ref, one_ref, two_ref, router_ref, bias_ref,
):
    step = pl.program_id(0)
    output_ref[...] = y_ref[...].astype(F32).T.astype(BF16)
    grad_ref[...] = rows_ref[...].astype(F32).T
    placed_ref[place_ref[0]] = own_ref[...]
    placed_ref[1 - place_ref[0]] = got_ref[...].astype(F32)

    @pl.when(step < 3)
    def _():
        in_ref[...] = summed_ref[...].astype(F32)

    @pl.when(step == 3)
    def _():
        out_ref[...] = summed_ref[...].astype(F32)
        router_ref[...] = small_ref[:EXPERTS]
        two_ref[...] = small_ref[EXPERTS : EXPERTS + 1]
        one_ref[...] = small_ref[EXPERTS + 1 : EXPERTS + 2]
        bias_ref[...] = small_ref[EXPERTS + 2 : EXPERTS + 2 + bias_ref.shape[0], :BUCKETS]


def finish_outputs(place, rows, y_rows, own, got, summed, small, heads):
    tokens, width = rows.shape
    units = own.shape[0]
    steps = 4
    tile, part, block = tokens // steps, units // steps, summed.shape[0] // steps
    quarter = pl.BlockSpec((part, width), lambda i: (i, 0))
    token_spec = pl.BlockSpec((tile, width), lambda i: (i, 0))
    feature_spec = pl.BlockSpec((width, tile), lambda i: (0, i))
    whole = lambda *shape: pl.BlockSpec(shape, lambda i: (0, 0))
    return pl.pallas_call(
        finish_kernel,
        grid=(steps,),
        in_specs=[
            pl.BlockSpec(memory_space=pltpu.SMEM),
            token_spec,
            token_spec,
            quarter,
            quarter,
            pl.BlockSpec((block, width), lambda i: (i, 0)),
            whole(*small.shape),
        ],
        out_specs=[
            feature_spec,
            feature_spec,
            pl.BlockSpec((2, part, width), lambda i: (0, i, 0)),
            pl.BlockSpec((block, width), lambda i: (jnp.minimum(i, 2), 0)),
            whole(block, width),
            whole(1, width),
            whole(1, width),
            whole(EXPERTS, width),
            whole(heads, BUCKETS),
        ],
        out_shape=[
            jax.ShapeDtypeStruct((width, tokens), BF16),
            jax.ShapeDtypeStruct((width, tokens), F32),
            jax.ShapeDtypeStruct((2, units, width), F32),
            jax.ShapeDtypeStruct((3 * block, width), F32),
            jax.ShapeDtypeStruct((block, width), F32),
            jax.ShapeDtypeStruct((1, width), F32),
            jax.ShapeDtypeStruct((1, width), F32),
            jax.ShapeDtypeStruct((EXPERTS, width), F32),
            jax.ShapeDtypeStruct((heads, BUCKETS), F32),
        ],
        compiler_params=params(),
        cost_estimate=cost(0, 10 * rows.size + 14 * own.size + 6 * summed.size),
    )(place, rows, y_rows, own, got, summed, small)


def on_device(
    layer_input, gain_one, attn_in, rel_bias, attn_out, gain_two, router,
    expert_gate, expert_up, expert_down, routes, piece_starts, grad_out,
):
    width, tokens = layer_input.shape
    ranks = lax.axis_size("tensor")
    groups = lax.axis_size("expert")
    rank = lax.axis_index("tensor")
    pair_class, half_index = rank % 2, rank // 2
    half = CAP // 2

    def trade(weights):
        other = lax.dynamic_index_in_dim(weights, 1 - pair_class, 0, keepdims=False)
        return lax.ppermute(other, "tensor", [(r, r ^ 1) for r in range(ranks)])

    traded = trade(expert_gate)
    gain_col = gain_one[:, None]
    w_in = attn_in.reshape(-1, width)
    qkv, scale_one = project(layer_input, gain_col, w_in)
    tiles = bias_tiles(rel_bias)
    position = jnp.arange(SEQ, dtype=jnp.int32)[None, None, :]
    starts = piece_starts[:, :, None]
    inside = (position >= starts) & (position < starts + PIECE)
    last = jnp.max(jnp.where(inside, starts + (PIECE - 1), -1), axis=1)
    limits = jnp.maximum(last, position[0])[:, None, :]

    routes_t = routes.T
    place = jnp.stack([pair_class, half_index]).astype(jnp.int32)
    share = tokens // ranks

    def by_rank(rows):
        return rows.reshape(ranks, share, width)

    mixed, lse, sent = attend(qkv, tiles, limits, attn_out)
    sent, traded = lax.optimization_barrier((sent, traded))
    slots = groups * half
    h2, resid, scale_two, dy, dy_rows, code, code_cols, own_x = exchange_call(
        norm_two_kernel, 2, sent.shape, [by_rank(sent), layer_input, gain_two[None], grad_out, routes_t],
        [((share, width), F32), ((share, 1), F32), ((tokens, width), BF16), ((slots, width), BF16)]
        + [((TOP, tokens), jnp.int32), ((tokens, TOP), jnp.int32), ((share, width), BF16)],
        [pltpu.VMEM((width, share), BF16), pltpu.SemaphoreType.DMA((1,))],
        (1,),
    )
    rows, row_grads, gate_rows, gates = dispatch(code, routes_t, router.T, h2, dy_rows)
    ret, back, *weight_grads = run_experts(
        rows, row_grads, expert_gate, expert_up, expert_down, traded
    )
    grad_attn, grad_resid, grad_gain_two, grad_router, partial_y = exchange_call(
        norm_two_back_kernel, 3, (tokens, width),
        [ret, back, code, code_cols, gates, routes_t, dy_rows, gate_rows, router.T, h2]
        + [resid, scale_two, dy, gain_two[None]],
        [((share, width), F32), ((1, width), F32), ((EXPERTS, width), F32), ((tokens, width), BF16)],
        [
            pltpu.VMEM((ranks, share, width), BF16),
            pltpu.VMEM((slots, width), BF16),
            pltpu.VMEM((ranks + 3, EXPERTS, share), F32),
            pltpu.VMEM((2 * EXPERTS, share), BF16),
        ]
        + [pltpu.SemaphoreType.DMA((3,))] * 2,
    )

    dq, dk, dv, near, far, y_own = attend_back(
        qkv, tiles, limits, attn_out, grad_attn, lse, by_rank(partial_y), resid
    )
    dq, y_own = lax.optimization_barrier((dq, y_own))
    y_across = lax.ppermute(y_own, "tensor", [(r, r ^ 1) for r in range(ranks)])
    y_along = lax.ppermute(y_own, "tensor", [(r, r ^ 2) for r in range(ranks)])
    weight_rows, sent, grad_gain_one, grad_gate, grad_up = project_back(
        place, layer_input, gain_col, gain_one[None], scale_one, w_in, mixed, grad_attn, (dq, dk, dv),
        weight_grads[:2], weight_grads[3:5],
    )
    sent, y_across, y_along = lax.optimization_barrier((sent, y_across, y_along))
    summed = lax.psum(weight_rows, "expert")
    small_shape = (BUCKETS, width)
    grad_rows, y_full, small = exchange_call(
        norm_one_back_kernel, 4, sent.shape,
        [by_rank(sent), own_x, scale_one, grad_resid, gain_one[None], y_own, y_across, y_along]
        + [grad_gain_one, grad_gain_two, grad_router, near, far],
        [((ranks, share, width), BF16), (small_shape, F32)],
        [pltpu.VMEM((4, *small_shape), F32), pltpu.VMEM((groups, *small_shape), BF16), pltpu.VMEM(near.shape, F32), pltpu.VMEM((share, 1), F32)]
        + [pltpu.SemaphoreType.DMA((1,))]
        + [pltpu.SemaphoreType.DMA((2,))] * 2
        + [pltpu.SemaphoreType.DMA((groups,))] * 2,
        (11,),
    )
    summed, grad_rows = lax.optimization_barrier((summed, grad_rows))
    layer_output, grad_input, grad_down, grad_in, grad_attn_out, grad_one, grad_two, grad_router, grad_bias = finish_outputs(
        place, grad_rows, y_full.reshape(tokens, width), weight_grads[2], weight_grads[5], summed, small, rel_bias.shape[1]
    )
    return (
        layer_output,
        grad_input,
        grad_one[0],
        grad_in.reshape(attn_in.shape),
        grad_bias.T,
        grad_attn_out,
        grad_two[0],
        grad_router.T,
        grad_gate,
        grad_up,
        grad_down,
    )


def allowed_pairs(seq_starts):
    position = jnp.arange(SEQ, dtype=jnp.int32)
    inside = (position[:, None] >= seq_starts[None, :]) & (
        position[:, None] < seq_starts[None, :] + PIECE
    )
    numbers = jnp.arange(seq_starts.shape[0], dtype=jnp.int32) + 1
    piece_label = jnp.sum(inside.astype(jnp.int32) * numbers[None, :], axis=1)
    causal = position[None, :] <= position[:, None]
    shared = (piece_label[:, None] == piece_label[None, :]) & (piece_label[:, None] > 0)
    return causal | shared


def slot_table(routes):
    flat_routes = routes.reshape(-1)
    onehot = (flat_routes[:, None] == jnp.arange(EXPERTS, dtype=jnp.int32)[None, :]).astype(
        jnp.int32
    )
    blocks = onehot.reshape(-1, 128, EXPERTS).astype(F32)
    earlier = jnp.tril(jnp.ones((128, 128), F32), -1)
    inside = jnp.einsum("ij,bje->bie", earlier, blocks)
    count = blocks.shape[0]
    carried = jnp.einsum("ab,be->ae", jnp.tril(jnp.ones((count, count), F32), -1), jnp.sum(blocks, axis=1), precision=HIGH)
    before = (inside + carried[:, None, :]).astype(jnp.int32).reshape(onehot.shape)
    slot_number = jnp.sum(before * onehot, axis=1)
    kept_pairs = slot_number < CAP
    slot_index = jnp.where(kept_pairs, flat_routes * CAP + slot_number, EXPERTS * CAP)
    return (slot_index.reshape(routes.shape), kept_pairs.reshape(routes.shape))


def bucket_onehot():
    offsets = jnp.arange(2 * SEQ - 1, dtype=jnp.int32) - (SEQ - 1)
    return (bucket_of(offsets)[:, None] == jnp.arange(BUCKETS, dtype=jnp.int32)[None, :]).astype(
        jnp.float32
    )


def expand_line(line):
    head_count = line.shape[0]
    padded = jnp.concatenate([line, jnp.zeros((head_count, 1), line.dtype)], axis=1)
    tiled = jnp.tile(padded, (1, SEQ))[:, : SEQ * (2 * SEQ - 1)].reshape(
        head_count, SEQ, 2 * SEQ - 1
    )
    return tiled[:, :, SEQ - 1 :]


def fold_line(full_grid):
    head_count = full_grid.shape[0]
    padded = jnp.pad(full_grid, ((0, 0), (0, 0), (SEQ - 1, 0))).reshape(
        head_count, SEQ * (2 * SEQ - 1)
    )
    padded = jnp.pad(padded, ((0, 0), (0, SEQ))).reshape(head_count, SEQ, 2 * SEQ)
    return jnp.sum(padded, axis=1)[:, : 2 * SEQ - 1]


def reduce_heads(tensor_value):
    return lax.psum(tensor_value, "tensor")


def spread_slots(tensor_value):
    return lax.all_gather(tensor_value, "tensor", axis=2, tiled=True)


def owner_exchange(tensor_value):
    return lax.all_to_all(tensor_value, "expert", split_axis=0, concat_axis=0, tiled=True)


def expert_sums(tensor_value):
    return lax.psum_scatter(tensor_value, "tensor", scatter_dimension=2, tiled=True)


def norm_forward(resid, gain, model_width):
    scale = lax.rsqrt(jnp.sum(resid * resid, axis=1) / model_width + EPS)[:, None]
    return (scale, (resid * scale * gain).astype(jnp.bfloat16))


def norm_backward(resid, scale, gain, grad_normed, model_width):
    grad_gain = jnp.sum(grad_normed * resid * scale, axis=0)
    scaled = grad_normed * gain
    inner = jnp.sum(scaled * resid, axis=1)[:, None]
    return (grad_gain, scale * scaled - resid * scale**3 * inner / model_width)


def attend_scores(bias_full, queries, key_rows, seq_starts):
    scores = (
        jnp.einsum("qhe,khe->hqk", queries, key_rows, preferred_element_type=jnp.float32) * 0.125
        + bias_full
    )
    return jnp.where(allowed_pairs(seq_starts)[None], scores, NEG)


def attend_forward(bias_full, inputs):
    queries, key_rows, value_rows, seq_starts = inputs
    scores = attend_scores(bias_full, queries, key_rows, seq_starts)
    row_max = jnp.max(scores, axis=2, keepdims=True)
    exponent = jnp.exp(scores - row_max)
    row_sum_exp = jnp.sum(exponent, axis=2, keepdims=True)
    weights = (exponent / row_sum_exp).astype(jnp.bfloat16)
    mixed_heads = jnp.einsum(
        "hqk,khe->qhe", weights, value_rows, preferred_element_type=jnp.float32
    )
    return (mixed_heads.astype(jnp.bfloat16), (row_max + jnp.log(row_sum_exp))[:, :, 0])


def attend_backward(bias_full, running, inputs):
    queries, key_rows, value_rows, grad_heads, seq_starts, log_total = inputs
    scores = attend_scores(bias_full, queries, key_rows, seq_starts)
    probabilities = jnp.exp(scores - log_total[:, :, None])
    grad_probs = jnp.einsum(
        "qhe,khe->hqk", grad_heads, value_rows, preferred_element_type=jnp.float32
    )
    inner = jnp.sum(probabilities * grad_probs, axis=2, keepdims=True)
    grad_scores = (probabilities * (grad_probs - inner)).astype(jnp.bfloat16)
    grad_values = jnp.einsum(
        "hqk,qhe->khe",
        probabilities.astype(jnp.bfloat16),
        grad_heads,
        preferred_element_type=jnp.float32,
    )
    grad_queries = (
        jnp.einsum("hqk,khe->qhe", grad_scores, key_rows, preferred_element_type=jnp.float32)
        * 0.125
    )
    grad_keys = (
        jnp.einsum("hqk,qhe->khe", grad_scores, queries, preferred_element_type=jnp.float32) * 0.125
    )
    return (
        running + grad_scores.astype(jnp.float32),
        jnp.stack([grad_queries, grad_keys, grad_values]),
    )


def gelu_product(left, right):
    return jax.nn.gelu(left, approximate=True) * right


def expert_forward(received, weight_gate, weight_up, weight_down):
    gate_part = jnp.einsum(
        "secd,efd->secf", received, weight_gate, preferred_element_type=jnp.float32
    )
    up_part = jnp.einsum("secd,efd->secf", received, weight_up, preferred_element_type=jnp.float32)
    hidden = gelu_product(gate_part, up_part).astype(jnp.bfloat16)
    partial_out = jnp.einsum(
        "secf,efd->secd", hidden, weight_down, preferred_element_type=jnp.float32
    )
    return (gate_part, up_part, hidden, partial_out)


def expert_backward(
    received, gate_part, up_part, hidden, grad_rows_out, weight_gate, weight_up, weight_down
):
    grad_hidden = jnp.einsum(
        "secd,efd->secf", grad_rows_out, weight_down, preferred_element_type=jnp.float32
    )
    product_value, pullback = jax.vjp(gelu_product, gate_part, up_part)
    grad_gate_part, grad_up_part = pullback(grad_hidden)
    grad_gate_part = grad_gate_part.astype(jnp.bfloat16)
    grad_up_part = grad_up_part.astype(jnp.bfloat16)
    grad_down = jnp.einsum(
        "secf,secd->efd", hidden, grad_rows_out, preferred_element_type=jnp.float32
    )
    grad_gate_w = jnp.einsum(
        "secf,secd->efd", grad_gate_part, received, preferred_element_type=jnp.float32
    )
    grad_up_w = jnp.einsum(
        "secf,secd->efd", grad_up_part, received, preferred_element_type=jnp.float32
    )
    grad_rows_in = jnp.einsum(
        "secf,efd->secd", grad_gate_part, weight_gate, preferred_element_type=jnp.float32
    )
    grad_rows_in = grad_rows_in + jnp.einsum(
        "secf,efd->secd", grad_up_part, weight_up, preferred_element_type=jnp.float32
    )
    return (grad_gate_w, grad_up_w, grad_down, grad_rows_in)


def on_device_general(
    layer_input,
    gain_one,
    attn_in,
    rel_bias,
    attn_out,
    gain_two,
    router,
    expert_gate,
    expert_up,
    expert_down,
    routes,
    piece_starts,
    grad_out,
):
    tok_count = layer_input.shape[1]
    model_width = layer_input.shape[0]
    heads_here = rel_bias.shape[1]
    head_width = attn_in.shape[1] // heads_here
    seqs_here = piece_starts.shape[0]
    local_experts = expert_gate.shape[0]
    part_rows = CAP // lax.axis_size("tensor")
    share_start = lax.axis_index("tensor") * part_rows
    tokens = layer_input.T.astype(jnp.float32)
    scale_one, normed = norm_forward(tokens, gain_one, model_width)
    project = jnp.einsum("td,chd->cth", normed, attn_in, preferred_element_type=jnp.float32).astype(
        jnp.bfloat16
    )
    by_seq = project.reshape(3, seqs_here, SEQ, heads_here, head_width)
    onehot_line = bucket_onehot()
    bias_full = expand_line(jnp.dot(onehot_line, rel_bias, precision=HIGH).T)
    mixed_heads, log_total = lax.map(
        partial(attend_forward, bias_full), (by_seq[0], by_seq[1], by_seq[2], piece_starts)
    )
    mixed_heads = mixed_heads.reshape(tok_count, heads_here * head_width)
    resid = tokens + reduce_heads(
        jnp.dot(mixed_heads, attn_out, preferred_element_type=jnp.float32)
    )
    scale_two, normed_two = norm_forward(resid, gain_two, model_width)
    logits = jnp.dot(normed_two, router, preferred_element_type=jnp.float32)
    chosen = (routes[:, :, None] == jnp.arange(EXPERTS, dtype=jnp.int32)[None, None, :]).astype(
        jnp.float32
    )
    picked = jnp.sum(chosen * logits[:, None, :], axis=2)
    gate_weights = jax.nn.softmax(picked, axis=1)
    slot_index, kept_pairs = slot_table(routes)
    keep_float = kept_pairs.astype(jnp.float32)
    mix_weight = gate_weights * keep_float
    safe_index = jnp.minimum(slot_index, EXPERTS * CAP - 1)
    token_rows = jnp.repeat(normed_two, TOP, axis=0)
    buffer = (
        jnp.zeros((EXPERTS * CAP + 1, model_width), jnp.bfloat16)
        .at[slot_index.reshape(-1)]
        .set(token_rows)
    )
    buffer = buffer[: EXPERTS * CAP].reshape(-1, local_experts, CAP, model_width)
    received = lax.all_to_all(buffer, "expert", split_axis=0, concat_axis=0, tiled=True)
    gate_part, up_part, hidden, partial_out = expert_forward(
        received, expert_gate, expert_up, expert_down
    )
    returned = spread_slots(owner_exchange(expert_sums(partial_out).astype(jnp.bfloat16)))
    flat_ret = returned.reshape(EXPERTS * CAP, model_width)
    fetched = flat_ret[safe_index].astype(jnp.float32)
    output = resid + jnp.sum(mix_weight[:, :, None] * fetched, axis=1)
    grad_y = grad_out.T.astype(jnp.float32)
    grad_gates = jnp.sum(grad_y[:, None, :] * fetched, axis=2) * keep_float
    grad_picked = gate_weights * (
        grad_gates - jnp.sum(gate_weights * grad_gates, axis=1, keepdims=True)
    )
    grad_logits = jnp.sum(chosen * grad_picked[:, :, None], axis=1)
    grad_router = jnp.dot(normed_two.astype(jnp.float32).T, grad_logits, precision=HIGH)
    grad_normed_two = jnp.dot(grad_logits, router.astype(jnp.float32).T, precision=HIGH)
    slot_grads = (mix_weight[:, :, None] * grad_y[:, None, :]).astype(jnp.bfloat16)
    grad_ret = (
        jnp.zeros((EXPERTS * CAP + 1, model_width), jnp.bfloat16)
        .at[slot_index.reshape(-1)]
        .set(slot_grads.reshape(-1, model_width))
    )
    grad_ret = grad_ret[: EXPERTS * CAP].reshape(-1, local_experts, CAP, model_width)
    grad_share = lax.dynamic_slice_in_dim(grad_ret, share_start, part_rows, 2)
    grad_rows_out = spread_slots(owner_exchange(grad_share))
    grad_expert_gate, grad_expert_up, grad_expert_down, grad_rows_in = expert_backward(
        received, gate_part, up_part, hidden, grad_rows_out, expert_gate, expert_up, expert_down
    )
    grad_back = spread_slots(owner_exchange(expert_sums(grad_rows_in).astype(jnp.bfloat16)))
    flat_back = grad_back.reshape(EXPERTS * CAP, model_width).astype(jnp.float32)
    grad_normed_two = grad_normed_two + jnp.sum(
        flat_back[safe_index] * keep_float[:, :, None], axis=1
    )
    grad_gain_two, grad_resid = norm_backward(
        resid, scale_two, gain_two, grad_normed_two, model_width
    )
    grad_resid = grad_resid + grad_y
    grad_attn = grad_resid.astype(jnp.bfloat16)
    grad_attn_out = jnp.einsum(
        "th,td->hd", mixed_heads, grad_attn, preferred_element_type=jnp.float32
    )
    grad_mixed = jnp.einsum(
        "td,hd->th", grad_attn, attn_out, preferred_element_type=jnp.float32
    ).astype(jnp.bfloat16)
    grad_by_seq = grad_mixed.reshape(seqs_here, SEQ, heads_here, head_width)
    bias_grad_full, grad_project = lax.scan(
        partial(attend_backward, bias_full),
        jnp.zeros_like(bias_full),
        (by_seq[0], by_seq[1], by_seq[2], grad_by_seq, piece_starts, log_total),
    )
    grad_project = (
        jnp.moveaxis(grad_project, 1, 0)
        .reshape(3, tok_count, heads_here * head_width)
        .astype(jnp.bfloat16)
    )
    grad_attn_in = jnp.einsum(
        "cth,td->chd", grad_project, normed, preferred_element_type=jnp.float32
    )
    grad_normed = reduce_heads(
        jnp.einsum("cth,chd->td", grad_project, attn_in, preferred_element_type=jnp.float32)
    )
    grad_gain_one, grad_tokens = norm_backward(
        tokens, scale_one, gain_one, grad_normed, model_width
    )
    grad_tokens = grad_tokens + grad_resid
    grad_rel_bias = jnp.dot(onehot_line.T, fold_line(bias_grad_full).T, precision=HIGH)
    shared = (
        lax.psum(grad_gain_one.astype(jnp.bfloat16), "expert").astype(jnp.float32),
        lax.psum(grad_attn_in.astype(jnp.bfloat16), "expert").astype(jnp.float32),
        lax.psum(grad_rel_bias.astype(jnp.bfloat16), "expert").astype(jnp.float32),
        lax.psum(grad_attn_out.astype(jnp.bfloat16), "expert").astype(jnp.float32),
        lax.psum(grad_gain_two.astype(jnp.bfloat16), "expert").astype(jnp.float32),
        lax.psum(grad_router.astype(jnp.bfloat16), "expert").astype(jnp.float32),
    )
    return (
        output.astype(jnp.bfloat16).T,
        grad_tokens.T,
        shared[0],
        shared[1],
        shared[2],
        shared[3],
        shared[4],
        shared[5],
        grad_expert_gate,
        grad_expert_up,
        grad_expert_down,
    )


def solution(mesh):
    placed = (
        P(None, "expert"),
        P(),
        P(None, "tensor", None),
        P(None, "tensor"),
        P("tensor", None),
        P(),
        P(),
        P("expert", "tensor", None),
        P("expert", "tensor", None),
        P("expert", "tensor", None),
        P("expert", None),
        P("expert", None),
        P(None, "expert"),
    )
    paired = mesh.shape["tensor"] == 4 and mesh.shape["expert"] * 2 == EXPERTS
    return jax.shard_map(
        on_device if paired else on_device_general,
        mesh=mesh,
        in_specs=placed,
        out_specs=(
            P(None, "expert"),
            P(None, "expert"),
            P(),
            P(None, "tensor", None),
            P(None, "tensor"),
            P("tensor", None),
            P(),
            P(),
            P("expert", "tensor", None),
            P("expert", "tensor", None),
            P("expert", "tensor", None),
        ),
        check_vma=False,
    )
```

```python
from functools import partial

import jax
import jax.numpy as jnp
from jax import lax
from jax.experimental import pallas as pl
from jax.experimental.pallas import tpu as pltpu
from jax.sharding import PartitionSpec as P

EXPERTS = 16
BUCKETS = 32
TOP = 2
PIECE = 256
SEQ = 1024
CAP = 320
BLK = 256


EPS = 1e-06
NEG = -1e30
THRESHOLDS = (12, 16, 23, 32, 46, 64, 91)
HIGH = lax.Precision.HIGHEST
F32 = jnp.float32
BF16 = jnp.bfloat16
NN = (((1,), (0,)), ((), ()))
NT = (((1,), (1,)), ((), ()))
TN = (((0,), (0,)), ((), ()))
MIB = 1 << 20


def mm(left, right, dims=NN):
    return lax.dot_general(left, right, dims, preferred_element_type=F32)


def params(limit=56):
    return pltpu.CompilerParams(vmem_limit_bytes=limit * MIB)


def cost(flops, bytes_accessed, transcendentals=0):
    return pl.CostEstimate(
        flops=int(flops), bytes_accessed=int(bytes_accessed), transcendentals=int(transcendentals)
    )


def bucket_of(offset):
    magnitude = jnp.abs(offset)
    beyond = sum(((magnitude >= threshold).astype(jnp.int32) for threshold in THRESHOLDS))
    lower_part = jnp.where(magnitude < 8, magnitude, 8 + beyond)
    return lower_part + 16 * (offset > 0).astype(jnp.int32)


def project_kernel(x_ref, gain_ref, w_ref, out_ref, scale_ref):
    x = x_ref[...].astype(F32)
    scale = lax.rsqrt(jnp.sum(x * x, axis=0, keepdims=True) / x.shape[0] + EPS)
    normed = (x * scale * gain_ref[...]).astype(BF16)
    out_ref[...] = mm(w_ref[...], normed).astype(BF16)
    scale_ref[...] = scale


def project(x, gain, weights):
    width, tokens = x.shape
    rows = weights.shape[0]
    tile = 512
    return pl.pallas_call(
        project_kernel,
        grid=(tokens // tile,),
        in_specs=[
            pl.BlockSpec((width, tile), lambda i: (0, i)),
            pl.BlockSpec((width, 1), lambda i: (0, 0)),
            pl.BlockSpec((rows, width), lambda i: (0, 0)),
        ],
        out_specs=[
            pl.BlockSpec((rows, tile), lambda i: (0, i)),
            pl.BlockSpec((1, tile), lambda i: (0, i)),
        ],
        out_shape=[
            jax.ShapeDtypeStruct((rows, tokens), BF16),
            jax.ShapeDtypeStruct((1, tokens), F32),
        ],
        compiler_params=params(),
        cost_estimate=cost(2 * width * tokens * rows, 2 * width * tokens * 2),
    )(x, gain, weights)


def line_offsets(number):
    column = lax.broadcasted_iota(jnp.int32, (8, BLK), 1)
    return (number - 1) * BLK - column


def bias_tiles_kernel(table_ref, tiles_ref):
    row = lax.broadcasted_iota(jnp.int32, (BLK, BLK), 0)
    column = lax.broadcasted_iota(jnp.int32, (BLK, BLK), 1)
    buckets = [bucket_of(line_offsets(number)) for number in range(4)]
    for head in range(tiles_ref.shape[0]):
        far = table_ref[15, head]
        rolled = []
        for number, bucket in enumerate(buckets):
            value = jnp.zeros((8, BLK), F32)
            for index in range(BUCKETS):
                value = jnp.where(bucket == index, table_ref[index, head] - far, value)
            whole = jnp.broadcast_to(value[0:1], (BLK, BLK))
            rolled.append(pltpu.roll(whole, 0, 1, stride=1, stride_axis=0))
        for number in range(3):
            tiles_ref[head, number] = jnp.where(column >= row, rolled[number], rolled[number + 1])


def bias_tiles(table):
    heads = table.shape[1]
    return pl.pallas_call(
        bias_tiles_kernel,
        in_specs=[pl.BlockSpec(memory_space=pltpu.SMEM)],
        out_specs=pl.BlockSpec(memory_space=pltpu.VMEM),
        out_shape=jax.ShapeDtypeStruct((heads, 3, BLK, BLK), F32),
        compiler_params=params(),
        cost_estimate=cost(heads * 3 * BLK * BLK * 60, heads * 3 * BLK * BLK * 4),
    )(table)


def bias_fold(near_ref, far_ref):
    heads = near_ref.shape[0] // 2
    sums = jnp.zeros((BUCKETS, 128), F32)
    lane = lax.broadcasted_iota(jnp.int32, (BUCKETS, 128), 1)
    row = lax.broadcasted_iota(jnp.int32, (BLK, BLK), 0)
    column = lax.broadcasted_iota(jnp.int32, (BLK, BLK), 1)
    flip = jnp.where(row + column == BLK - 1, 1.0, 0.0).astype(BF16)
    apart = jnp.where(column == BLK - 1, 0, column + 1)
    ahead = apart <= row
    number_at = lax.broadcasted_iota(jnp.int32, (BUCKETS, BLK), 0)
    for head in range(heads):
        lines = [jnp.zeros((1, BLK), F32) for _ in range(4)]
        for number in range(3):
            grads = near_ref[head, number] + near_ref[heads + head, number]
            coarse = grads.astype(BF16)
            fine = (grads - coarse.astype(F32)).astype(BF16)
            flipped = mm(flip, coarse) + mm(flip, fine)
            rolled = pltpu.roll(flipped, 0, 1, stride=1, stride_axis=0)
            lines[number] += jnp.sum(jnp.where(ahead, rolled, 0.0), axis=0, keepdims=True)
            lines[number + 1] += jnp.sum(jnp.where(ahead, 0.0, rolled), axis=0, keepdims=True)
        total = jnp.zeros((BUCKETS, 1), F32)
        for number, line in enumerate(lines):
            bucket = bucket_of((number - 1) * BLK - apart[:1])
            total += jnp.sum(jnp.where(bucket == number_at, line, 0.0), axis=1, keepdims=True)
        distant = jnp.sum(far_ref[head] + far_ref[heads + head], axis=0, keepdims=True)
        distant = jnp.sum(distant, axis=1, keepdims=True)
        total += jnp.where(number_at[:, :1] == 15, distant, 0.0)
        sums = jnp.where(lane == head, total, sums)
    return sums


def key_count(query_block):
    return 2 * BLK if query_block < 2 else 4 * BLK


def block_scores(keys, queries, tiles_ref, limit, block):
    count = key_count(block)
    parts = []
    whole = mm(keys[:, :count], queries, TN)
    for key_block in range(count // BLK):
        part = whole[key_block * BLK : (key_block + 1) * BLK]
        shift = key_block - block
        if -1 <= shift <= 1:
            part = part + tiles_ref[0, shift + 1]
        if shift >= 0:
            key_at = lax.broadcasted_iota(jnp.int32, (BLK, BLK), 0) + key_block * BLK
            part = jnp.where(key_at <= limit, part, NEG)
        parts.append(part)
    return jnp.concatenate(parts, axis=0)


def attend_kernel(q_ref, k_ref, v_ref, tiles_ref, limit_ref, w_ref, out_ref, lse_ref, sent_ref, held):
    head = pl.program_id(1)
    width = q_ref.shape[0]
    queries = q_ref[...] * BF16(0.125)
    keys, values = k_ref[...], v_ref[...]
    for block in range(SEQ // BLK):
        cols = slice(block * BLK, (block + 1) * BLK)
        scores = block_scores(keys, queries[:, cols], tiles_ref, limit_ref[0, :, cols], block)
        top = jnp.max(scores, axis=0, keepdims=True)
        exponent = jnp.exp(scores - top)
        total = jnp.sum(exponent, axis=0, keepdims=True)
        mixed = mm(values[:, : key_count(block)], exponent.astype(BF16)) / total
        mixed = mixed.astype(BF16)
        out_ref[:, cols] = mixed
        held[pl.ds(pl.multiple_of(head * width, width), width), cols] = mixed
        lse_ref[0, :, cols] = top + jnp.log(total)

    @pl.when(head == pl.num_programs(1) - 1)
    def _():
        sent_ref[...] = mm(held[...], w_ref[...], TN).astype(BF16)


def attend(qkv, tiles, limits, attn_out):
    heads = tiles.shape[0]
    seqs = limits.shape[0]
    width = qkv.shape[0] // (3 * heads)
    model_width = attn_out.shape[1]
    return pl.pallas_call(
        attend_kernel,
        grid=(seqs, heads),
        in_specs=[
            pl.BlockSpec((width, SEQ), lambda s, h: (h, s)),
            pl.BlockSpec((width, SEQ), lambda s, h: (heads + h, s)),
            pl.BlockSpec((width, SEQ), lambda s, h: (2 * heads + h, s)),
            pl.BlockSpec((1, 3, BLK, BLK), lambda s, h: (h, 0, 0, 0)),
            pl.BlockSpec((1, 1, SEQ), lambda s, h: (s, 0, 0)),
            pl.BlockSpec((heads * width, model_width), lambda s, h: (0, 0)),
        ],
        out_specs=[
            pl.BlockSpec((width, SEQ), lambda s, h: (h, s)),
            pl.BlockSpec((1, 1, SEQ), lambda s, h: (s * heads + h, 0, 0)),
            pl.BlockSpec((SEQ, model_width), lambda s, h: (s, 0)),
        ],
        out_shape=[
            jax.ShapeDtypeStruct((heads * width, seqs * SEQ), BF16),
            jax.ShapeDtypeStruct((seqs * heads, 1, SEQ), F32),
            jax.ShapeDtypeStruct((seqs * SEQ, model_width), BF16),
        ],
        scratch_shapes=[pltpu.VMEM((heads * width, SEQ), BF16)],
        compiler_params=params(),
        cost_estimate=cost(seqs * heads * SEQ * SEQ * 512, seqs * heads * SEQ * 2048, seqs * heads * SEQ * SEQ),
    )(qkv, qkv, qkv, tiles, limits, attn_out)


def attend_back_kernel(
    q_ref, k_ref, v_ref, tiles_ref, limit_ref, w_ref, grad_ref, lse_ref, part_ref, resid_ref,
    dq_ref, dk_ref, dv_ref, near_ref, far_ref, y_ref,
    held, parts, total, turn_across, turn_along, from_across, from_along, sends, recvs, loads,
):
    rank = lax.axis_index("tensor")
    pair_class, half_index = rank % 2, rank // 2
    across, along, corner = rank + 1 - 2 * pair_class, rank + 2 - 4 * half_index, 3 - rank
    step = pl.program_id(0) * pl.num_programs(1) + pl.program_id(1)
    mesh_ids = pl.DeviceIdType.MESH
    middle = parts.shape[2] // 2
    low, high = slice(0, middle), slice(middle, 2 * middle)

    def remote(number, origin, target, other):
        return pltpu.make_async_remote_copy(
            src_ref=origin, dst_ref=target, send_sem=sends.at[number], recv_sem=recvs.at[number],
            device_id={"tensor": other}, device_id_type=mesh_ids,
        )

    first = (
        remote(0, part_ref.at[corner, :, low], turn_across, across),
        remote(1, part_ref.at[corner, :, high], turn_along, along),
    )
    second = remote(2, parts.at[0], from_across, across), remote(3, parts.at[1], from_along, along)
    local = [
        pltpu.make_async_copy(part_ref.at[other], parts.at[number], loads.at[number])
        for number, other in enumerate((across, along, rank))
    ]
    local.append(pltpu.make_async_copy(resid_ref, total, loads.at[3]))

    @pl.when(step == 0)
    def _():
        barrier = pltpu.get_barrier_semaphore()
        for other in (across, along):
            pl.semaphore_signal(barrier, inc=1, device_id={"tensor": other}, device_id_type=mesh_ids)
        pl.semaphore_wait(barrier, 2)
        for copy in first:
            copy.start()
        for copy in local:
            copy.start()

    @pl.when(step == 3)
    def _():
        for copy in (*first, *local):
            copy.wait()
        parts[0, :, high] = (parts[0, :, high].astype(F32) + turn_along[...].astype(F32)).astype(BF16)
        parts[1, :, low] = (parts[1, :, low].astype(F32) + turn_across[...].astype(F32)).astype(BF16)
        for copy in second:
            copy.start()

    head = pl.program_id(1)
    width = q_ref.shape[0]

    @pl.when(head == 0)
    def _():
        held[...] = mm(w_ref[...], grad_ref[...], NT).astype(BF16)

    queries = q_ref[...] * BF16(0.125)
    keys, values = k_ref[...], v_ref[...]
    grads = held[pl.ds(pl.multiple_of(head * width, width), width), :]
    near_ref[...] = jnp.zeros_like(near_ref)
    far = jnp.zeros((8, BLK), F32)
    grad_keys = jnp.zeros((width, SEQ), F32)
    grad_values = jnp.zeros((width, SEQ), F32)
    for block in range(SEQ // BLK):
        count = key_count(block)
        cols = slice(block * BLK, (block + 1) * BLK)
        scores = block_scores(keys, queries[:, cols], tiles_ref, limit_ref[0, :, cols], block)
        probs = jnp.exp(scores - lse_ref[0, :, cols])
        grad_probs = mm(values[:, :count], grads[:, cols], TN)
        inner = jnp.sum(probs * grad_probs, axis=0, keepdims=True)
        grad_scores = probs * (grad_probs - inner)
        for key_block in range(count // BLK):
            part = grad_scores[key_block * BLK : (key_block + 1) * BLK]
            shift = key_block - block
            if -1 <= shift <= 1:
                near_ref[0, shift + 1] += part
            elif shift < -1:
                far = far + jnp.sum(part.reshape(BLK // 8, 8, BLK), axis=0)
        rounded = grad_scores.astype(BF16)
        add_values = mm(grads[:, cols], probs.astype(BF16), NT)
        add_keys = mm(queries[:, cols], rounded, NT)
        if count == SEQ:
            grad_values = grad_values + add_values
            grad_keys = grad_keys + add_keys
        else:
            filler = jnp.zeros((width, SEQ - count), F32)
            grad_values = grad_values + jnp.concatenate([add_values, filler], axis=1)
            grad_keys = grad_keys + jnp.concatenate([add_keys, filler], axis=1)
        dq_ref[:, cols] = (mm(keys[:, :count], rounded) * 0.125).astype(BF16)
    dk_ref[...] = grad_keys.astype(BF16)
    dv_ref[...] = grad_values.astype(BF16)
    far_ref[0] = far

    @pl.when(step == 7)
    def _():
        for copy in second:
            copy.wait()
        summed = parts[2].astype(F32) + from_across[...].astype(F32) + from_along[...].astype(F32)
        y_ref[...] = (total[...] + summed).astype(BF16)


def attend_back(qkv, tiles, limits, attn_out, grad_attn, lse, part, resid):
    heads = tiles.shape[0]
    seqs = limits.shape[0]
    width = qkv.shape[0] // (3 * heads)
    model_width = attn_out.shape[1]
    share = part.shape[1]
    grad_spec = pl.BlockSpec((width, SEQ), lambda s, h: (h, s))
    anywhere = pl.BlockSpec(memory_space=pl.ANY)
    return pl.pallas_call(
        attend_back_kernel,
        grid=(seqs, heads),
        in_specs=[
            pl.BlockSpec((width, SEQ), lambda s, h: (h, s)),
            pl.BlockSpec((width, SEQ), lambda s, h: (heads + h, s)),
            pl.BlockSpec((width, SEQ), lambda s, h: (2 * heads + h, s)),
            pl.BlockSpec((1, 3, BLK, BLK), lambda s, h: (h, 0, 0, 0)),
            pl.BlockSpec((1, 1, SEQ), lambda s, h: (s, 0, 0)),
            pl.BlockSpec((heads * width, model_width), lambda s, h: (0, 0)),
            pl.BlockSpec((SEQ, model_width), lambda s, h: (s, 0)),
            pl.BlockSpec((1, 1, SEQ), lambda s, h: (s * heads + h, 0, 0)),
        ]
        + [anywhere] * 2,
        out_specs=[
            grad_spec,
            grad_spec,
            grad_spec,
            pl.BlockSpec((1, 3, BLK, BLK), lambda s, h: (s * heads + h, 0, 0, 0)),
            pl.BlockSpec((1, 8, BLK), lambda s, h: (s * heads + h, 0, 0)),
            pl.BlockSpec((share, model_width), lambda s, h: (0, 0)),
        ],
        out_shape=[jax.ShapeDtypeStruct((heads * width, seqs * SEQ), BF16)] * 3
        + [
            jax.ShapeDtypeStruct((seqs * heads, 3, BLK, BLK), F32),
            jax.ShapeDtypeStruct((seqs * heads, 8, BLK), F32),
        ]
        + [jax.ShapeDtypeStruct((share, model_width), BF16)],
        scratch_shapes=[
            pltpu.VMEM((heads * width, SEQ), BF16),
            pltpu.VMEM((3, share, model_width), BF16),
            pltpu.VMEM((share, model_width), F32),
            pltpu.VMEM((share, model_width // 2), BF16),
            pltpu.VMEM((share, model_width // 2), BF16),
            pltpu.VMEM((share, model_width), BF16),
            pltpu.VMEM((share, model_width), BF16),
            pltpu.SemaphoreType.DMA((4,)),
            pltpu.SemaphoreType.DMA((4,)),
            pltpu.SemaphoreType.DMA((4,)),
        ],
        compiler_params=pltpu.CompilerParams(
            vmem_limit_bytes=60 * MIB, collective_id=5, has_side_effects=True
        ),
        cost_estimate=cost(seqs * heads * SEQ * SEQ * 1280, seqs * heads * SEQ * 4096, seqs * heads * SEQ * SEQ),
    )(qkv, qkv, qkv, tiles, limits, attn_out, grad_attn, lse, part, resid)


def project_back_kernel(
    place_ref, x_ref, gain_ref, gain_row_ref, scale_ref, w_ref, mixed_ref, attn_ref, dq_ref, dk_ref, dv_ref, *refs
):
    step = pl.program_id(0)
    own_refs, got_refs, (weight_ref, out_ref, gain_grad_ref), placed_refs, total = (
        refs[:2], refs[2:4], refs[4:7], refs[7:9], refs[9]
    )
    for own_ref, got_ref, placed_ref in zip(own_refs, got_refs, placed_refs):
        placed_ref[place_ref[0]] = own_ref[...]
        placed_ref[1 - place_ref[0]] = got_ref[...].astype(F32)
    grads = jnp.concatenate([dq_ref[...], dk_ref[...], dv_ref[...]], axis=0)
    rows = grads.shape[0]
    normed = (x_ref[...].astype(F32) * scale_ref[...] * gain_ref[...]).astype(BF16)

    @pl.when(step == 0)
    def _():
        total[...] = jnp.zeros_like(total)

    total[:rows] += mm(grads, normed, NT)
    total[rows:] += mm(mixed_ref[...], attn_ref[...])
    out_ref[...] = mm(grads, w_ref[...], TN).astype(BF16)

    @pl.when(step == pl.num_programs(0) - 1)
    def _():
        weight_ref[...] = total[...].astype(BF16)
        through = jnp.sum(total[:rows] * w_ref[...].astype(F32), axis=0, keepdims=True)
        gain_grad_ref[...] = through / gain_row_ref[...]


def project_back(place, x, gain, gain_row, scale, weights, mixed, grad_attn, grads, owns, gots):
    width, tokens = x.shape
    rows = weights.shape[0]
    heads_width = mixed.shape[0]
    units = owns[0].shape[0]
    steps = 4
    tile = tokens // steps
    part = units // steps
    column = lambda count: pl.BlockSpec((count, tile), lambda i: (0, i))
    return pl.pallas_call(
        project_back_kernel,
        grid=(steps,),
        in_specs=[
            pl.BlockSpec(memory_space=pltpu.SMEM),
            column(width),
            pl.BlockSpec((width, 1), lambda i: (0, 0)),
            pl.BlockSpec((1, width), lambda i: (0, 0)),
            column(1),
            pl.BlockSpec((rows, width), lambda i: (0, 0)),
            column(heads_width),
            pl.BlockSpec((tile, width), lambda i: (i, 0)),
        ]
        + [column(rows // 3)] * 3
        + [pl.BlockSpec((part, width), lambda i: (i, 0))] * 4,
        out_specs=[
            pl.BlockSpec((rows + heads_width, width), lambda i: (0, 0)),
            pl.BlockSpec((tile, width), lambda i: (i, 0)),
            pl.BlockSpec((1, width), lambda i: (0, 0)),
        ]
        + [pl.BlockSpec((2, part, width), lambda i: (0, i, 0))] * 2,
        out_shape=[
            jax.ShapeDtypeStruct((rows + heads_width, width), BF16),
            jax.ShapeDtypeStruct((tokens, width), BF16),
            jax.ShapeDtypeStruct((1, width), F32),
        ]
        + [jax.ShapeDtypeStruct((2, units, width), F32)] * 2,
        scratch_shapes=[pltpu.VMEM((rows + heads_width, width), F32)],
        compiler_params=params(),
        cost_estimate=cost(5 * width * tokens * rows, 6 * width * tokens + 14 * units * width),
    )(place, x, gain, gain_row, scale, weights, mixed, grad_attn, *grads, *owns, *gots)


def exchange(
    math, rank, source, full_out, full, from_across, from_along, to_across, to_along, turn_across, turn_along, sends, recvs, outs, ready=None, ready_full=None, side=None, peers=(), fill=None, start=None, cut=None, later=None):
    pair_class, half_index = rank % 2, rank // 2
    across, along, corner = rank + 1 - 2 * pair_class, rank + 2 - 4 * half_index, 3 - rank
    mesh_ids = pl.DeviceIdType.MESH
    rows, width = source.shape[1:]
    chunks = 4
    size = rows // chunks
    cut = cut or width // 2
    low, high = slice(0, cut), slice(cut, width)
    barrier = pltpu.get_barrier_semaphore()
    near = (across, along, corner) if later else (across, along)
    for other in near:
        pl.semaphore_signal(barrier, inc=1, device_id={"tensor": other}, device_id_type=mesh_ids)
    for other in peers:
        pl.semaphore_signal(barrier, inc=1, device_id={"expert": other}, device_id_type=mesh_ids)
    pl.semaphore_wait(barrier, len(near) + len(peers))

    def remote(kind, chunk, origin, target, other):
        return pltpu.make_async_remote_copy(
            src_ref=origin, dst_ref=target, send_sem=sends.at[kind, chunk], recv_sem=recvs.at[kind, chunk],
            device_id={"tensor": other}, device_id_type=mesh_ids,
        )

    if start:
        start()
    if fill:
        fill(corner)
    spans = [slice(chunk * size, (chunk + 1) * size) for chunk in range(chunks)]
    first, second, third, fourth = [], [], [], []
    for chunk, span in enumerate(spans):
        pair = (
            remote(0, chunk, source.at[corner, span, low], turn_across.at[span, low], across),
            remote(1, chunk, source.at[corner, span, high], turn_along.at[span, high], along),
        )
        for copy in pair:
            copy.start()
        first.append(pair)
    if fill:
        fill(along)
        fill(across)
    leaving = []

    def leave(number, other):
        leaving.append(pltpu.make_async_copy(full.at[other], full_out.at[other], outs.at[number]))
        leaving[-1].start()

    if ready is not None:
        _, near_across, near_along = ready
        extra = [
            remote(8, 0, near_along.at[:, low], ready_full.at[along, :, low], across),
            remote(8, 1, near_across.at[:, high], ready_full.at[across, :, high], along),
        ]
        extra += [
            pltpu.make_async_copy(piece, ready_full.at[other], outs.at[4 + number])
            for number, (other, piece) in enumerate(zip((rank, across, along), ready))
        ]
        for copy in extra:
            copy.start()
    for chunk, span in enumerate(spans):
        if side:
            side(chunk)
        first[chunk][0].wait()
        to_along[span, low] = (source[along, span, low].astype(F32) + turn_across[span, low].astype(F32)).astype(BF16)
        to_along[span, high] = source[along, span, high]
        first[chunk][1].wait()
        to_across[span, low] = source[across, span, low]
        to_across[span, high] = (source[across, span, high].astype(F32) + turn_along[span, high].astype(F32)).astype(BF16)
        pair = (
            remote(2, chunk, to_across.at[span], from_across.at[span], across),
            remote(3, chunk, to_along.at[span], from_along.at[span], along),
        )
        for copy in pair:
            copy.start()
        second.append(pair)
    def pass_on(chunk):
        span = spans[chunk]
        for copy in third[chunk]:
            copy.wait()
        pair = (
            remote(6, chunk, full.at[along, span, low], full.at[along, span, low], across),
            remote(7, chunk, full.at[across, span, high], full.at[across, span, high], along),
        )
        for copy in pair:
            copy.start()
        fourth.append(pair)

    if fill:
        fill(rank)
    if later:
        later((across, along, corner))
    for chunk, span in enumerate(spans):
        if side:
            side(chunks + chunk)
        for copy in second[chunk]:
            copy.wait()
        total = source[rank, span].astype(F32) + from_across[span].astype(F32) + from_along[span].astype(F32)
        full[rank, span] = math(span, total).astype(BF16)
        pair = (
            remote(4, chunk, full.at[rank, span], full.at[rank, span], across),
            remote(5, chunk, full.at[rank, span], full.at[rank, span], along),
        )
        for copy in pair:
            copy.start()
        third.append(pair)
        if chunk:
            pass_on(chunk - 1)
    leave(0, rank)
    pass_on(chunks - 1)
    leave(1, across)
    leave(2, along)
    if ready is not None:
        for copy in extra:
            copy.wait()
    if side and later:
        side(2 * chunks)
    for pair in fourth:
        for copy in pair:
            copy.wait()
    leave(3, corner)
    if side and not later:
        side(2 * chunks)
    for copy in leaving:
        copy.wait()


def exchange_call(kernel, number, shape, operands, extra_shapes, scratch=(), in_hbm=(), out_hbm=()):
    tokens, width = shape
    ranks = 4
    rows = tokens // ranks
    here = pl.BlockSpec(memory_space=pltpu.VMEM)
    results = pl.pallas_call(
        kernel,
        in_specs=[pl.BlockSpec(memory_space=pl.ANY) if k in in_hbm else here for k in range(len(operands))],
        out_specs=[pl.BlockSpec(memory_space=pl.ANY)]
        + [pl.BlockSpec(memory_space=pl.ANY) if k in out_hbm else here for k in range(len(extra_shapes))],
        out_shape=[jax.ShapeDtypeStruct((ranks, rows, width), BF16)]
        + [jax.ShapeDtypeStruct(shape, kind) for shape, kind in extra_shapes],
        scratch_shapes=[pltpu.VMEM((ranks, rows, width), BF16)]
        + [pltpu.VMEM((rows, width), BF16)] * 6
        + [pltpu.SemaphoreType.DMA((9, 4))] * 2
        + [pltpu.SemaphoreType.DMA((7,))]
        + list(scratch),
        compiler_params=pltpu.CompilerParams(
            vmem_limit_bytes=60 * MIB, collective_id=number, has_side_effects=True
        ),
        cost_estimate=cost(40 * MIB, 200 * MIB),
    )(*operands)
    return results[0].reshape(tokens, width), *results[1:]


def norm_two_kernel(
    source, x_ref, gain_ref, grad_out_ref, routes_ref,
    full, resid_ref, scale_ref, dy_out, dy_rows_out, code_ref, codes_ref, own_ref, *rest,
):
    held, grad_out, dy_ref, dy_rows_ref, load = rest[-5:]
    rank = lax.axis_index("tensor")
    ranks, rows, width = source.shape
    loading = pltpu.make_async_copy(grad_out_ref, grad_out, load.at[1])
    storing = [
        pltpu.make_async_copy(dy_ref, dy_out, load.at[2]),
        pltpu.make_async_copy(dy_rows_ref, dy_rows_out, load.at[3]),
    ]

    def start():
        own.start()
        loading.start()

    slots = dy_rows_ref.shape[0] // ranks
    own = pltpu.make_async_copy(x_ref.at[:, pl.ds(pl.multiple_of(rank * rows, rows), rows)], held, load.at[0])

    def math(span, total):
        resid = own_ref[span, :].astype(F32) + total
        scale = lax.rsqrt(jnp.sum(resid * resid, axis=1, keepdims=True) / resid.shape[1] + EPS)
        resid_ref[span, :] = resid
        scale_ref[span, :] = scale
        return resid * scale * gain_ref[...]

    def side(number):
        if number == 0:
            own.wait()
            own_ref[...] = held[...].astype(F32).T.astype(BF16)
            local_codes(routes_ref, code_ref, rank % 2, rank // 2, CAP // 2)
            codes_ref[...] = jnp.concatenate([code_ref[...].astype(F32)] * 4, axis=0).T[:, :TOP].astype(jnp.int32)
            loading.wait()
        if number < ranks:
            span = slice(number * rows, (number + 1) * rows)
            dy_ref[span, :] = grad_out[:, span].astype(F32).T.astype(BF16)
        elif number < 2 * ranks:
            start = (number - ranks) * slots
            slot = lax.broadcasted_iota(jnp.int32, (slots, dy_ref.shape[0]), 0) + start
            take = jnp.where((slot == code_ref[0:1]) | (slot == code_ref[1:2]), 1.0, 0.0).astype(BF16)
            dy_rows_ref[start : start + slots, :] = mm(take, dy_ref[...]).astype(BF16)
        if number == ranks - 1:
            storing[0].start()
        elif number == 2 * ranks - 1:
            storing[1].start()
        elif number == 2 * ranks:
            for copy in storing:
                copy.wait()

    exchange(math, rank, source, full, *rest[:-5], side=side, start=start)


def norm_back(grad, value, scale, gain):
    scaled = grad * gain
    inner = jnp.sum(scaled * value, axis=1, keepdims=True)
    return scale * scaled - value * (scale * scale * scale) * (inner / value.shape[1])


def norm_two_back_kernel(
    ret_in, back_ref, code_ref, codes_ref, gates_ref, routes_ref, dy_rows_in, gate_ref, router_ref, h_in,
    resid_in, scale_ref, dy_in, gain_ref, full, grad_ref, gain_grad_ref, router_grad_ref, y_out, *rest,
):
    source, scaled, logit_parts, logit_own, send, recv, ret_ref, dy_rows_ref, h_ref, resid_ref, dy_ref, y_ref, load = rest[-13:]
    rank = lax.axis_index("tensor")
    rows = source.shape[1]
    slots, tokens = ret_ref.shape[0], code_ref.shape[1]
    ranks = tokens // rows
    copies = []
    own_dy = dy_in.at[pl.ds(pl.multiple_of(rank * rows, rows), rows)]
    pairs = ((ret_in, ret_ref), (dy_rows_in, dy_rows_ref), (resid_in, resid_ref), (own_dy, dy_ref), (h_in, h_ref))
    loading = [pltpu.make_async_copy(*pair, load.at[number]) for number, pair in enumerate(pairs)]
    storing = [
        pltpu.make_async_copy(y_ref.at[shard], y_out.at[pl.ds(shard * rows, rows)], load.at[5 + shard])
        for shard in range(ranks)
    ]

    def start():
        for copy in loading:
            copy.start()

    def later(others):
        for copy in loading:
            copy.wait()
        found = [jnp.zeros((1, tokens), F32) for _ in range(TOP)]
        tile = slots // 4
        for begin in range(0, slots, tile):
            span = slice(begin, begin + tile)
            ret = ret_ref[span, :].astype(F32)
            slot_grad = jnp.sum(dy_rows_ref[span, :].astype(F32) * ret, axis=1, keepdims=True)
            scaled[span, :] = (ret * gate_ref[span, :]).astype(BF16)
            slot = lax.broadcasted_iota(jnp.int32, (tile, tokens), 0) + begin
            for i in range(TOP):
                found[i] = found[i] + jnp.sum(
                    jnp.where(slot == code_ref[i : i + 1, :], slot_grad, 0.0), axis=0, keepdims=True
                )
        mean = gates_ref[0:1] * found[0] + gates_ref[1:2] * found[1]
        expert = lax.broadcasted_iota(jnp.int32, (EXPERTS, tokens), 0)
        logit = sum(
            jnp.where(routes_ref[i : i + 1] == expert, gates_ref[i : i + 1] * (found[i] - mean), 0.0)
            for i in range(TOP)
        )
        for shard in range(ranks):
            logit_parts[shard] = logit[:, shard * rows : (shard + 1) * rows]
        for number, other in enumerate(others):
            copies.append(
                pltpu.make_async_remote_copy(
                    src_ref=logit_parts.at[other], dst_ref=logit_parts.at[ranks + number], send_sem=send.at[number],
                    recv_sem=recv.at[number], device_id={"tensor": other}, device_id_type=pl.DeviceIdType.MESH,
                )
            )
            copies[-1].start()

    def places(shard):
        slot = lax.broadcasted_iota(jnp.int32, (rows, slots), 1)
        codes = codes_ref[pl.ds(pl.multiple_of(shard * rows, rows), rows), :]
        return jnp.where((slot == codes[:, 0:1]) | (slot == codes[:, 1:2]), 1.0, 0.0).astype(BF16)

    def fill(shard):
        source[shard] = mm(places(shard), back_ref[...]).astype(BF16)

    def side(number):
        if number == ranks:
            router_grad_ref[...] = sum(
                mm(logit_parts[shard].astype(BF16), h_ref[shard * rows : (shard + 1) * rows, :])
                for shard in range(ranks)
            )
            for copy in copies:
                copy.wait()
            logit = logit_parts[rank] + logit_parts[ranks] + logit_parts[ranks + 1] + logit_parts[ranks + 2]
            coarse = logit.astype(BF16)
            logit_own[:EXPERTS] = coarse
            logit_own[EXPERTS:] = (logit - coarse.astype(F32)).astype(BF16)
        elif number > ranks:
            shard = number - ranks - 1
            y_ref[shard] = mm(places(shard), scaled[...]).astype(BF16)
            storing[shard].start()
            if shard == ranks - 1:
                for copy in storing:
                    copy.wait()

    gain_grad_ref[...] = jnp.zeros_like(gain_grad_ref)

    def math(span, total):
        resid, scale = resid_ref[span, :], scale_ref[span, :]
        both = jnp.concatenate([router_ref[...], router_ref[...]], axis=0)
        total = total + mm(logit_own[:, span], both, TN)
        gain_grad_ref[...] += jnp.sum(total * resid * scale, axis=0, keepdims=True)
        grad = norm_back(total, resid, scale, gain_ref[...]) + dy_ref[span, :].astype(F32)
        grad_ref[span, :] = grad
        return grad

    exchange(math, rank, source, full, *rest[:-13], side=side, fill=fill, start=start, later=later)


def norm_one_back_kernel(
    source, x_in, scale_ref, grad_in, gain_ref, y_own, y_across, y_along, gain_one_ref, gain_two_ref, router_ref,
    near_ref, far_ref, full, ready_full, small_out, *rest,
):
    x_ref, grad_ref, held, gathered, near, scale, load, tensor_sends, tensor_recvs, expert_sends, expert_recvs = rest[-11:]
    rank, group = lax.axis_index("tensor"), lax.axis_index("expert")
    pair_class, half_index = rank % 2, rank // 2
    others = rank + 1 - 2 * pair_class, rank + 2 - 4 * half_index
    groups = expert_sends.shape[0]
    mesh_ids = pl.DeviceIdType.MESH
    peers = [partner_of(group, step) for step in range(1, groups)]
    heads = near_ref.shape[0] // 2
    rows = source.shape[1]
    pairs = ((near_ref, near), (x_in, x_ref), (grad_in, grad_ref))
    loading = [pltpu.make_async_copy(*pair, load.at[number]) for number, pair in enumerate(pairs)]

    def math(span, total):
        x = x_ref[span, :].astype(F32)
        return norm_back(total, x, scale[span, :], gain_ref[...]) + grad_ref[span, :]

    def to_rank(step):
        return pltpu.make_async_remote_copy(
            src_ref=held.at[step], dst_ref=held.at[2 + step], send_sem=tensor_sends.at[step],
            recv_sem=tensor_recvs.at[step], device_id={"tensor": others[step]}, device_id_type=mesh_ids,
        )

    def to_group(step):
        return pltpu.make_async_remote_copy(
            src_ref=gathered.at[group], dst_ref=gathered.at[group], send_sem=expert_sends.at[step],
            recv_sem=expert_recvs.at[step], device_id={"expert": peers[step - 1]}, device_id_type=mesh_ids,
        )

    def start():
        for copy in loading:
            copy.start()
        held[0] = jnp.zeros(small_out.shape, F32)
        held[0, :EXPERTS] = router_ref[...]
        held[0, EXPERTS : EXPERTS + 1] = gain_two_ref[...]
        held[0, EXPERTS + 1 : EXPERTS + 2] = gain_one_ref[...]
        to_rank(0).start()

    def side(number):
        if number == 0:
            own_scale = scale_ref[:, pl.ds(pl.multiple_of(rank * rows, rows), rows)]
            scale[...] = jnp.broadcast_to(own_scale, (8, rows)).T[:, :1]
            for copy in loading:
                copy.wait()
            small_out[:BUCKETS, :128] = bias_fold(near, far_ref)
        elif number == 1:
            to_rank(0).wait()
            held[1] = held[0] + held[2]
            to_rank(1).start()
        elif number == 5:
            to_rank(1).wait()
            turned = small_out[:BUCKETS, :128].T
            held[0] = held[1] + held[3]
            held[0, EXPERTS + 2 : EXPERTS + 2 + heads, :BUCKETS] = turned[:heads]
            gathered[group] = held[0].astype(BF16)
            for step in range(1, groups):
                to_group(step).start()
        elif number == 8:
            for step in range(1, groups):
                to_group(step).wait()
            total = gathered[0].astype(F32)
            for step in range(1, groups):
                total = total + gathered[step].astype(F32)
            small_out[...] = total

    exchange(
        math, rank, source, full, *rest[:-11], (y_own, y_across, y_along), ready_full, side=side, peers=peers, start=start
    )


def local_codes(routes_ref, code_ref, pair_class, half_index, half):
    tokens = routes_ref.shape[1]
    expert = lax.broadcasted_iota(jnp.int32, (EXPERTS, BLK), 0)
    earlier = (
        lax.broadcasted_iota(jnp.int32, (BLK, BLK), 0) < lax.broadcasted_iota(jnp.int32, (BLK, BLK), 1)
    ).astype(F32).astype(BF16)
    carry = jnp.zeros((EXPERTS, 1), F32)
    for block in range(tokens // BLK):
        cols = slice(block * BLK, (block + 1) * BLK)
        routes = routes_ref[:, cols]
        hits = [(routes[i : i + 1] == expert) for i in range(TOP)]
        chosen = sum(hit.astype(F32) for hit in hits)
        before = mm(chosen.astype(BF16), earlier) + carry
        carry = carry + jnp.sum(chosen, axis=1, keepdims=True)
        for i in range(TOP):
            slot = jnp.sum(jnp.where(hits[i], before, 0.0), axis=0, keepdims=True).astype(jnp.int32)
            route = routes[i : i + 1]
            owner = route // 2
            local = slot - half_index * half
            mine = (route - 2 * owner == pair_class) & (local >= 0) & (local < half)
            code_ref[i : i + 1, cols] = jnp.where(mine, owner * half + local, -1)


def dispatch_kernel(code_ref, routes_ref, router_ref, h_ref, dy_rows_ref, rows_ref, grads_ref, gate_ref, gates_ref):
    count, tokens = rows_ref.shape[0], h_ref.shape[0]

    @pl.when(pl.program_id(0) == 0)
    def _():
        expert = lax.broadcasted_iota(jnp.int32, (EXPERTS, tokens), 0)
        logits = mm(router_ref[...], h_ref[...], NT)
        picked = [
            jnp.sum(jnp.where(routes_ref[i : i + 1] == expert, logits, 0.0), axis=0, keepdims=True)
            for i in range(TOP)
        ]
        top = jnp.maximum(picked[0], picked[1])
        raised = [jnp.exp(value - top) for value in picked]
        total = raised[0] + raised[1]
        for i in range(TOP):
            gates_ref[i : i + 1] = raised[i] / total

    slot = lax.broadcasted_iota(jnp.int32, (count, tokens), 0) + pl.program_id(0) * count
    hits = [slot == code_ref[i : i + 1, :] for i in range(TOP)]
    take = jnp.where(hits[0] | hits[1], 1.0, 0.0).astype(BF16)
    weighted = jnp.where(hits[0], gates_ref[0:1, :], jnp.where(hits[1], gates_ref[1:2, :], 0.0))
    gate = jnp.sum(weighted, axis=1, keepdims=True)
    rows_ref[...] = mm(take, h_ref[...]).astype(BF16)
    grads_ref[...] = (dy_rows_ref[...].astype(F32) * gate).astype(BF16)
    gate_ref[...] = gate


def dispatch(code, routes_t, router_t, h, dy_rows):
    slots, width = dy_rows.shape
    tile = slots // 4
    row_spec = pl.BlockSpec((tile, width), lambda i: (i, 0))
    whole = lambda shape: pl.BlockSpec(shape, lambda i: (0, 0))
    return pl.pallas_call(
        dispatch_kernel,
        grid=(4,),
        in_specs=[whole(code.shape), whole(code.shape), whole(router_t.shape), whole(h.shape), row_spec],
        out_specs=[row_spec, row_spec, pl.BlockSpec((tile, 1), lambda i: (i, 0)), whole(code.shape)],
        out_shape=[jax.ShapeDtypeStruct((slots, width), BF16)] * 2
        + [jax.ShapeDtypeStruct((slots, 1), F32), jax.ShapeDtypeStruct(code.shape, F32)],
        compiler_params=params(),
        cost_estimate=cost(4 * slots * SEQ * width, 4 * MIB + 6 * slots * width),
    )(code, routes_t, router_t, h, dy_rows)


def gelu_parts(x):
    inner = 0.7978845608028654 * (x + 0.044715 * (x * x * x))
    bend = jnp.tanh(inner)
    half = 0.5 * (1.0 + bend)
    slope = half + 0.5 * x * (1.0 - bend * bend) * (
        0.7978845608028654 * (1.0 + 3.0 * 0.044715 * (x * x))
    )
    return x * half, slope


def partner_of(index, step):
    found = index
    for bit in (1, 2, 4):
        found = found + ((step // bit) % 2) * (1 - 2 * ((index // bit) % 2)) * bit
    return found


def expert_kernel(
    rows_in, grads_in, gate_in, up_in, down_in, far_gate,
    ret_out, back_out, own_gate, own_up, own_down, got_gate, got_up, got_down,
    rows, grads, weights, sums, parts, z_send, z_recv, y_send, y_recv, p_send, p_recv, r_send, r_recv, w_send, w_recv, g_send, g_recv, local,
):
    groups, half, width = rows.shape[1:]
    group, rank = lax.axis_index("expert"), lax.axis_index("tensor")
    pair_class, half_index = rank % 2, rank // 2
    across = {"tensor": rank + 1 - 2 * pair_class}
    along = {"tensor": rank + 2 - 4 * half_index}
    mesh_ids = pl.DeviceIdType.MESH
    moved = ((rows_in, rows, ret_out), (grads_in, grads, back_out))

    barrier = pltpu.get_barrier_semaphore()
    for step in range(1, groups):
        pl.semaphore_signal(
            barrier, inc=1, device_id={"expert": partner_of(group, step)}, device_id_type=mesh_ids
        )
    pl.semaphore_signal(barrier, inc=1, device_id=across, device_id_type=mesh_ids)
    pl.semaphore_signal(barrier, inc=1, device_id=along, device_id_type=mesh_ids)
    pl.semaphore_wait(barrier, groups + 1)

    def remote(source, target, send, recv, device):
        return pltpu.make_async_remote_copy(
            src_ref=source, dst_ref=target, send_sem=send, recv_sem=recv,
            device_id=device, device_id_type=mesh_ids,
        )

    def block(ref, number):
        return ref.at[pl.ds(pl.multiple_of(number * half, half), half)]

    def out_of(kind, step):
        source, held, _ = moved[kind]
        other = partner_of(group, step)
        return remote(
            block(source, other), held.at[0, group], z_send.at[kind, step], z_recv.at[kind, step], {"expert": other}
        )

    def forward(kind, step):
        held = moved[kind][1]
        other = partner_of(group, step)
        return remote(held.at[0, other], held.at[1, other], y_send.at[kind, step], y_recv.at[kind, step], along)

    def partial_sum(kind, step):
        held = moved[kind][1]
        other = partner_of(group, step)
        return remote(held.at[1, other], parts.at[kind, other], p_send.at[kind, step], p_recv.at[kind, step], along)

    def result(kind, step):
        other = partner_of(group, step)
        return remote(
            parts.at[kind, other], block(moved[kind][2], group), r_send.at[kind, step], r_recv.at[kind, step], {"expert": other}
        )

    def own_result(kind):
        return pltpu.make_async_copy(parts.at[kind, group], block(moved[kind][2], group), local.at[kind])

    own = [
        pltpu.make_async_copy(block(moved[kind][0], group), moved[kind][1].at[0, group], local.at[kind])
        for kind in range(2)
    ]
    for copy in own:
        copy.start()
    kept = [
        pltpu.make_async_copy(ref.at[pair_class], weights.at[number, 0], local.at[2 + number])
        for number, ref in enumerate((gate_in, up_in, down_in))
    ]
    kept.append(pltpu.make_async_copy(far_gate, weights.at[0, 1], local.at[5]))
    kept += [
        remote(ref.at[1 - pair_class], weights.at[number, 1], w_send.at[number - 1], w_recv.at[number - 1], across)
        for number, ref in ((1, up_in), (2, down_in))
    ]
    for copy in kept:
        copy.start()
    for step in range(1, groups):
        for kind in range(2):
            out_of(kind, step).start()

    def arrive(step):
        for kind in range(2):
            out_of(kind, step).wait()
            forward(kind, step).start()

    def give(step):
        for kind in range(2):
            partial_sum(kind, step).start()

    for number in range(3):
        for part in range(2):
            sums[number, part] = jnp.zeros(sums.shape[2:], F32)

    def finish(step):
        other = partner_of(group, step)
        for kind in range(2):
            partial_sum(kind, step).wait()
            held = moved[kind][1]
            parts[kind, other] = (parts[kind, other].astype(F32) + held[0, other].astype(F32)).astype(BF16)

        for kind in range(2):
            if step == 0:
                own_result(kind).start()
            else:
                result(kind, step).start()

    def act(plan):
        for action, step in plan:
            action(step)

    order = (0, 1, 4, 5, 2, 6, 3, 7)
    before = {
        0: [(arrive, 1), (arrive, 2), (arrive, 3), (arrive, 4)],
        1: [(give, 0)],
        2: [(arrive, 5)],
        3: [(give, 4), (finish, 0)],
        4: [(arrive, 6)],
        5: [(give, 5), (finish, 4)],
        6: [(arrive, 7)],
        7: [(give, 6), (finish, 5)],
    }
    ahead = [(give, 7)]
    last = [(give, 2), (finish, 6), (give, 3), (finish, 7), (give, 1), (finish, 2), (finish, 3), (finish, 1)]
    for copy in own:
        copy.wait()
    for kind in range(2):
        forward(kind, 0).start()

    def body(turn, carry):
        for number, plan in before.items():
            pl.when(turn == number)(partial(act, plan))

        @pl.when(turn == 0)
        def _():
            for copy in kept:
                copy.wait()

        step = sum((turn == number).astype(jnp.int32) * which for number, which in enumerate(order))
        for kind in range(2):
            forward(kind, step).wait()
        other = partner_of(group, step)
        tile = jnp.concatenate([rows[0, other], rows[1, other]], axis=0)
        grad = jnp.concatenate([grads[0, other], grads[1, other]], axis=0)
        ret = jnp.zeros(tile.shape, F32)
        back = jnp.zeros(tile.shape, F32)
        for part in range(2):
            w_gate, w_up, w_down = weights[0, part], weights[1, part], weights[2, part]
            gate_part = mm(tile, w_gate, NT)
            up_part = mm(tile, w_up, NT)
            grad_hidden = mm(grad, w_down, NT)
            bent, slope = gelu_parts(gate_part)
            hidden = (bent * up_part).astype(BF16)
            grad_gate = (grad_hidden * up_part * slope).astype(BF16)
            grad_up = (grad_hidden * bent).astype(BF16)
            ret = ret + mm(hidden, w_down)
            back = back + mm(grad_gate, w_gate) + mm(grad_up, w_up)
            sums[0, part] += mm(grad_gate, tile, TN)
            sums[1, part] += mm(grad_up, tile, TN)
            sums[2, part] += mm(hidden, grad, TN)
        for kind, value in enumerate((ret, back)):
            held = moved[kind][1]
            held[0, other] = value[:half].astype(BF16)
            held[1, other] = value[half:].astype(BF16)

        return carry

    lax.fori_loop(0, groups, body, 0)
    act(ahead)
    copies = []
    for number, (own_ref, got_ref) in enumerate(((own_gate, got_gate), (own_up, got_up), (own_down, got_down))):
        weights[number, 0] = sums[number, 1].astype(BF16)
        copies.append(remote(weights.at[number, 0], got_ref, g_send.at[number], g_recv.at[number], across))
        copies[-1].start()
        copies.append(pltpu.make_async_copy(sums.at[number, 0], own_ref, local.at[2 + number]))
        copies[-1].start()
    act(last)
    for copy in copies:
        copy.wait()
    for kind in range(2):
        own_result(kind).wait()
        for step in range(1, groups):
            result(kind, step).wait()


def run_experts(rows, grads, w_gate, w_up, w_down, far_gate):
    slots, width = rows.shape
    half = CAP // 2
    groups = slots // half
    units = w_gate.shape[1]
    anywhere = pl.BlockSpec(memory_space=pl.ANY)
    pair = pltpu.SemaphoreType.DMA((2, groups))
    return pl.pallas_call(
        expert_kernel,
        in_specs=[anywhere] * 6,
        out_specs=[anywhere] * 8,
        out_shape=[jax.ShapeDtypeStruct((slots, width), BF16)] * 2
        + [jax.ShapeDtypeStruct((units, width), F32)] * 3
        + [jax.ShapeDtypeStruct((units, width), BF16)] * 3,
        scratch_shapes=[
            pltpu.VMEM((2, groups, half, width), BF16),
            pltpu.VMEM((2, groups, half, width), BF16),
            pltpu.VMEM((3, 2, units, width), BF16),
            pltpu.VMEM((3, 2, units, width), F32),
            pltpu.VMEM((2, groups, half, width), BF16),
        ]
        + [pair] * 8
        + [pltpu.SemaphoreType.DMA((2,))] * 2
        + [pltpu.SemaphoreType.DMA((3,))] * 2
        + [pltpu.SemaphoreType.DMA((6,))],
        compiler_params=pltpu.CompilerParams(
            vmem_limit_bytes=60 * MIB, collective_id=1, has_side_effects=True
        ),
        cost_estimate=cost(72 * slots * units * width, 16 * slots * width + 30 * units * width),
    )(rows, grads, w_gate, w_up, w_down, far_gate)


def finish_kernel(
    place_ref, rows_ref, y_ref, own_ref, got_ref, summed_ref, small_ref,
    output_ref, grad_ref, placed_ref, in_ref, out_ref, one_ref, two_ref, router_ref, bias_ref,
):
    step = pl.program_id(0)
    output_ref[...] = y_ref[...].astype(F32).T.astype(BF16)
    grad_ref[...] = rows_ref[...].astype(F32).T
    placed_ref[place_ref[0]] = own_ref[...]
    placed_ref[1 - place_ref[0]] = got_ref[...].astype(F32)

    @pl.when(step < 3)
    def _():
        in_ref[...] = summed_ref[...].astype(F32)

    @pl.when(step == 3)
    def _():
        out_ref[...] = summed_ref[...].astype(F32)
        router_ref[...] = small_ref[:EXPERTS]
        two_ref[...] = small_ref[EXPERTS : EXPERTS + 1]
        one_ref[...] = small_ref[EXPERTS + 1 : EXPERTS + 2]
        bias_ref[...] = small_ref[EXPERTS + 2 : EXPERTS + 2 + bias_ref.shape[0], :BUCKETS]


def finish_outputs(place, rows, y_rows, own, got, summed, small, heads):
    tokens, width = rows.shape
    units = own.shape[0]
    steps = 4
    tile, part, block = tokens // steps, units // steps, summed.shape[0] // steps
    quarter = pl.BlockSpec((part, width), lambda i: (i, 0))
    token_spec = pl.BlockSpec((tile, width), lambda i: (i, 0))
    feature_spec = pl.BlockSpec((width, tile), lambda i: (0, i))
    whole = lambda *shape: pl.BlockSpec(shape, lambda i: (0, 0))
    return pl.pallas_call(
        finish_kernel,
        grid=(steps,),
        in_specs=[
            pl.BlockSpec(memory_space=pltpu.SMEM),
            token_spec,
            token_spec,
            quarter,
            quarter,
            pl.BlockSpec((block, width), lambda i: (i, 0)),
            whole(*small.shape),
        ],
        out_specs=[
            feature_spec,
            feature_spec,
            pl.BlockSpec((2, part, width), lambda i: (0, i, 0)),
            pl.BlockSpec((block, width), lambda i: (jnp.minimum(i, 2), 0)),
            whole(block, width),
            whole(1, width),
            whole(1, width),
            whole(EXPERTS, width),
            whole(heads, BUCKETS),
        ],
        out_shape=[
            jax.ShapeDtypeStruct((width, tokens), BF16),
            jax.ShapeDtypeStruct((width, tokens), F32),
            jax.ShapeDtypeStruct((2, units, width), F32),
            jax.ShapeDtypeStruct((3 * block, width), F32),
            jax.ShapeDtypeStruct((block, width), F32),
            jax.ShapeDtypeStruct((1, width), F32),
            jax.ShapeDtypeStruct((1, width), F32),
            jax.ShapeDtypeStruct((EXPERTS, width), F32),
            jax.ShapeDtypeStruct((heads, BUCKETS), F32),
        ],
        compiler_params=params(),
        cost_estimate=cost(0, 10 * rows.size + 14 * own.size + 6 * summed.size),
    )(place, rows, y_rows, own, got, summed, small)


def on_device(
    layer_input, gain_one, attn_in, rel_bias, attn_out, gain_two, router,
    expert_gate, expert_up, expert_down, routes, piece_starts, grad_out,
):
    width, tokens = layer_input.shape
    ranks = lax.axis_size("tensor")
    groups = lax.axis_size("expert")
    rank = lax.axis_index("tensor")
    pair_class, half_index = rank % 2, rank // 2
    half = CAP // 2

    def trade(weights):
        other = lax.dynamic_index_in_dim(weights, 1 - pair_class, 0, keepdims=False)
        return lax.ppermute(other, "tensor", [(r, r ^ 1) for r in range(ranks)])

    traded = trade(expert_gate)
    gain_col = gain_one[:, None]
    w_in = attn_in.reshape(-1, width)
    qkv, scale_one = project(layer_input, gain_col, w_in)
    tiles = bias_tiles(rel_bias)
    position = jnp.arange(SEQ, dtype=jnp.int32)[None, None, :]
    starts = piece_starts[:, :, None]
    inside = (position >= starts) & (position < starts + PIECE)
    last = jnp.max(jnp.where(inside, starts + (PIECE - 1), -1), axis=1)
    limits = jnp.maximum(last, position[0])[:, None, :]

    routes_t = routes.T
    place = jnp.stack([pair_class, half_index]).astype(jnp.int32)
    share = tokens // ranks

    def by_rank(rows):
        return rows.reshape(ranks, share, width)

    mixed, lse, sent = attend(qkv, tiles, limits, attn_out)
    sent, traded = lax.optimization_barrier((sent, traded))
    slots = groups * half
    h2, resid, scale_two, dy, dy_rows, code, code_cols, own_x = exchange_call(
        norm_two_kernel, 2, sent.shape, [by_rank(sent), layer_input, gain_two[None], grad_out, routes_t],
        [((share, width), F32), ((share, 1), F32), ((tokens, width), BF16), ((slots, width), BF16)]
        + [((TOP, tokens), jnp.int32), ((tokens, TOP), jnp.int32), ((share, width), BF16)],
        [pltpu.VMEM((width, share), BF16), pltpu.VMEM((width, tokens), BF16), pltpu.VMEM((tokens, width), BF16)]
        + [pltpu.VMEM((slots, width), BF16), pltpu.SemaphoreType.DMA((4,))],
        (1, 3),
        (2, 3),
    )
    rows, row_grads, gate_rows, gates = dispatch(code, routes_t, router.T, h2, dy_rows)
    ret, back, *weight_grads = run_experts(
        rows, row_grads, expert_gate, expert_up, expert_down, traded
    )
    grad_attn, grad_resid, grad_gain_two, grad_router, partial_y = exchange_call(
        norm_two_back_kernel, 3, (tokens, width),
        [ret, back, code, code_cols, gates, routes_t, dy_rows, gate_rows, router.T, h2]
        + [resid, scale_two, dy, gain_two[None]],
        [((share, width), F32), ((1, width), F32), ((EXPERTS, width), F32), ((tokens, width), BF16)],
        [
            pltpu.VMEM((ranks, share, width), BF16),
            pltpu.VMEM((slots, width), BF16),
            pltpu.VMEM((ranks + 3, EXPERTS, share), F32),
            pltpu.VMEM((2 * EXPERTS, share), BF16),
        ]
        + [pltpu.SemaphoreType.DMA((3,))] * 2
        + [pltpu.VMEM((slots, width), BF16)] * 2
        + [pltpu.VMEM((tokens, width), BF16), pltpu.VMEM((share, width), F32), pltpu.VMEM((share, width), BF16)]
        + [pltpu.VMEM((ranks, share, width), BF16), pltpu.SemaphoreType.DMA((9,))],
        (0, 6, 9, 10, 12),
        (3,),
    )

    dq, dk, dv, near, far, y_own = attend_back(
        qkv, tiles, limits, attn_out, grad_attn, lse, by_rank(partial_y), resid
    )
    dq, y_own = lax.optimization_barrier((dq, y_own))
    y_across = lax.ppermute(y_own, "tensor", [(r, r ^ 1) for r in range(ranks)])
    y_along = lax.ppermute(y_own, "tensor", [(r, r ^ 2) for r in range(ranks)])
    weight_rows, sent, grad_gain_one, grad_gate, grad_up = project_back(
        place, layer_input, gain_col, gain_one[None], scale_one, w_in, mixed, grad_attn, (dq, dk, dv),
        weight_grads[:2], weight_grads[3:5],
    )
    sent, y_across, y_along = lax.optimization_barrier((sent, y_across, y_along))
    summed = lax.psum(weight_rows, "expert")
    small_shape = (BUCKETS, width)
    grad_rows, y_full, small = exchange_call(
        norm_one_back_kernel, 4, sent.shape,
        [by_rank(sent), own_x, scale_one, grad_resid, gain_one[None], y_own, y_across, y_along]
        + [grad_gain_one, grad_gain_two, grad_router, near, far],
        [((ranks, share, width), BF16), (small_shape, F32)],
        [pltpu.VMEM((share, width), BF16), pltpu.VMEM((share, width), F32)]
        + [pltpu.VMEM((4, *small_shape), F32), pltpu.VMEM((groups, *small_shape), BF16), pltpu.VMEM(near.shape, F32), pltpu.VMEM((share, 1), F32)]
        + [pltpu.SemaphoreType.DMA((3,))]
        + [pltpu.SemaphoreType.DMA((2,))] * 2
        + [pltpu.SemaphoreType.DMA((groups,))] * 2,
        (1, 3, 5, 6, 7, 11),
        (0,),
    )
    summed, grad_rows = lax.optimization_barrier((summed, grad_rows))
    layer_output, grad_input, grad_down, grad_in, grad_attn_out, grad_one, grad_two, grad_router, grad_bias = finish_outputs(
        place, grad_rows, y_full.reshape(tokens, width), weight_grads[2], weight_grads[5], summed, small, rel_bias.shape[1]
    )
    return (
        layer_output,
        grad_input,
        grad_one[0],
        grad_in.reshape(attn_in.shape),
        grad_bias.T,
        grad_attn_out,
        grad_two[0],
        grad_router.T,
        grad_gate,
        grad_up,
        grad_down,
    )


def allowed_pairs(seq_starts):
    position = jnp.arange(SEQ, dtype=jnp.int32)
    inside = (position[:, None] >= seq_starts[None, :]) & (
        position[:, None] < seq_starts[None, :] + PIECE
    )
    numbers = jnp.arange(seq_starts.shape[0], dtype=jnp.int32) + 1
    piece_label = jnp.sum(inside.astype(jnp.int32) * numbers[None, :], axis=1)
    causal = position[None, :] <= position[:, None]
    shared = (piece_label[:, None] == piece_label[None, :]) & (piece_label[:, None] > 0)
    return causal | shared


def slot_table(routes):
    flat_routes = routes.reshape(-1)
    onehot = (flat_routes[:, None] == jnp.arange(EXPERTS, dtype=jnp.int32)[None, :]).astype(
        jnp.int32
    )
    blocks = onehot.reshape(-1, 128, EXPERTS).astype(F32)
    earlier = jnp.tril(jnp.ones((128, 128), F32), -1)
    inside = jnp.einsum("ij,bje->bie", earlier, blocks)
    count = blocks.shape[0]
    carried = jnp.einsum("ab,be->ae", jnp.tril(jnp.ones((count, count), F32), -1), jnp.sum(blocks, axis=1), precision=HIGH)
    before = (inside + carried[:, None, :]).astype(jnp.int32).reshape(onehot.shape)
    slot_number = jnp.sum(before * onehot, axis=1)
    kept_pairs = slot_number < CAP
    slot_index = jnp.where(kept_pairs, flat_routes * CAP + slot_number, EXPERTS * CAP)
    return (slot_index.reshape(routes.shape), kept_pairs.reshape(routes.shape))


def bucket_onehot():
    offsets = jnp.arange(2 * SEQ - 1, dtype=jnp.int32) - (SEQ - 1)
    return (bucket_of(offsets)[:, None] == jnp.arange(BUCKETS, dtype=jnp.int32)[None, :]).astype(
        jnp.float32
    )


def expand_line(line):
    head_count = line.shape[0]
    padded = jnp.concatenate([line, jnp.zeros((head_count, 1), line.dtype)], axis=1)
    tiled = jnp.tile(padded, (1, SEQ))[:, : SEQ * (2 * SEQ - 1)].reshape(
        head_count, SEQ, 2 * SEQ - 1
    )
    return tiled[:, :, SEQ - 1 :]


def fold_line(full_grid):
    head_count = full_grid.shape[0]
    padded = jnp.pad(full_grid, ((0, 0), (0, 0), (SEQ - 1, 0))).reshape(
        head_count, SEQ * (2 * SEQ - 1)
    )
    padded = jnp.pad(padded, ((0, 0), (0, SEQ))).reshape(head_count, SEQ, 2 * SEQ)
    return jnp.sum(padded, axis=1)[:, : 2 * SEQ - 1]


def reduce_heads(tensor_value):
    return lax.psum(tensor_value, "tensor")


def spread_slots(tensor_value):
    return lax.all_gather(tensor_value, "tensor", axis=2, tiled=True)


def owner_exchange(tensor_value):
    return lax.all_to_all(tensor_value, "expert", split_axis=0, concat_axis=0, tiled=True)


def expert_sums(tensor_value):
    return lax.psum_scatter(tensor_value, "tensor", scatter_dimension=2, tiled=True)


def norm_forward(resid, gain, model_width):
    scale = lax.rsqrt(jnp.sum(resid * resid, axis=1) / model_width + EPS)[:, None]
    return (scale, (resid * scale * gain).astype(jnp.bfloat16))


def norm_backward(resid, scale, gain, grad_normed, model_width):
    grad_gain = jnp.sum(grad_normed * resid * scale, axis=0)
    scaled = grad_normed * gain
    inner = jnp.sum(scaled * resid, axis=1)[:, None]
    return (grad_gain, scale * scaled - resid * scale**3 * inner / model_width)


def attend_scores(bias_full, queries, key_rows, seq_starts):
    scores = (
        jnp.einsum("qhe,khe->hqk", queries, key_rows, preferred_element_type=jnp.float32) * 0.125
        + bias_full
    )
    return jnp.where(allowed_pairs(seq_starts)[None], scores, NEG)


def attend_forward(bias_full, inputs):
    queries, key_rows, value_rows, seq_starts = inputs
    scores = attend_scores(bias_full, queries, key_rows, seq_starts)
    row_max = jnp.max(scores, axis=2, keepdims=True)
    exponent = jnp.exp(scores - row_max)
    row_sum_exp = jnp.sum(exponent, axis=2, keepdims=True)
    weights = (exponent / row_sum_exp).astype(jnp.bfloat16)
    mixed_heads = jnp.einsum(
        "hqk,khe->qhe", weights, value_rows, preferred_element_type=jnp.float32
    )
    return (mixed_heads.astype(jnp.bfloat16), (row_max + jnp.log(row_sum_exp))[:, :, 0])


def attend_backward(bias_full, running, inputs):
    queries, key_rows, value_rows, grad_heads, seq_starts, log_total = inputs
    scores = attend_scores(bias_full, queries, key_rows, seq_starts)
    probabilities = jnp.exp(scores - log_total[:, :, None])
    grad_probs = jnp.einsum(
        "qhe,khe->hqk", grad_heads, value_rows, preferred_element_type=jnp.float32
    )
    inner = jnp.sum(probabilities * grad_probs, axis=2, keepdims=True)
    grad_scores = (probabilities * (grad_probs - inner)).astype(jnp.bfloat16)
    grad_values = jnp.einsum(
        "hqk,qhe->khe",
        probabilities.astype(jnp.bfloat16),
        grad_heads,
        preferred_element_type=jnp.float32,
    )
    grad_queries = (
        jnp.einsum("hqk,khe->qhe", grad_scores, key_rows, preferred_element_type=jnp.float32)
        * 0.125
    )
    grad_keys = (
        jnp.einsum("hqk,qhe->khe", grad_scores, queries, preferred_element_type=jnp.float32) * 0.125
    )
    return (
        running + grad_scores.astype(jnp.float32),
        jnp.stack([grad_queries, grad_keys, grad_values]),
    )


def gelu_product(left, right):
    return jax.nn.gelu(left, approximate=True) * right


def expert_forward(received, weight_gate, weight_up, weight_down):
    gate_part = jnp.einsum(
        "secd,efd->secf", received, weight_gate, preferred_element_type=jnp.float32
    )
    up_part = jnp.einsum("secd,efd->secf", received, weight_up, preferred_element_type=jnp.float32)
    hidden = gelu_product(gate_part, up_part).astype(jnp.bfloat16)
    partial_out = jnp.einsum(
        "secf,efd->secd", hidden, weight_down, preferred_element_type=jnp.float32
    )
    return (gate_part, up_part, hidden, partial_out)


def expert_backward(
    received, gate_part, up_part, hidden, grad_rows_out, weight_gate, weight_up, weight_down
):
    grad_hidden = jnp.einsum(
        "secd,efd->secf", grad_rows_out, weight_down, preferred_element_type=jnp.float32
    )
    product_value, pullback = jax.vjp(gelu_product, gate_part, up_part)
    grad_gate_part, grad_up_part = pullback(grad_hidden)
    grad_gate_part = grad_gate_part.astype(jnp.bfloat16)
    grad_up_part = grad_up_part.astype(jnp.bfloat16)
    grad_down = jnp.einsum(
        "secf,secd->efd", hidden, grad_rows_out, preferred_element_type=jnp.float32
    )
    grad_gate_w = jnp.einsum(
        "secf,secd->efd", grad_gate_part, received, preferred_element_type=jnp.float32
    )
    grad_up_w = jnp.einsum(
        "secf,secd->efd", grad_up_part, received, preferred_element_type=jnp.float32
    )
    grad_rows_in = jnp.einsum(
        "secf,efd->secd", grad_gate_part, weight_gate, preferred_element_type=jnp.float32
    )
    grad_rows_in = grad_rows_in + jnp.einsum(
        "secf,efd->secd", grad_up_part, weight_up, preferred_element_type=jnp.float32
    )
    return (grad_gate_w, grad_up_w, grad_down, grad_rows_in)


def on_device_general(
    layer_input,
    gain_one,
    attn_in,
    rel_bias,
    attn_out,
    gain_two,
    router,
    expert_gate,
    expert_up,
    expert_down,
    routes,
    piece_starts,
    grad_out,
):
    tok_count = layer_input.shape[1]
    model_width = layer_input.shape[0]
    heads_here = rel_bias.shape[1]
    head_width = attn_in.shape[1] // heads_here
    seqs_here = piece_starts.shape[0]
    local_experts = expert_gate.shape[0]
    part_rows = CAP // lax.axis_size("tensor")
    share_start = lax.axis_index("tensor") * part_rows
    tokens = layer_input.T.astype(jnp.float32)
    scale_one, normed = norm_forward(tokens, gain_one, model_width)
    project = jnp.einsum("td,chd->cth", normed, attn_in, preferred_element_type=jnp.float32).astype(
        jnp.bfloat16
    )
    by_seq = project.reshape(3, seqs_here, SEQ, heads_here, head_width)
    onehot_line = bucket_onehot()
    bias_full = expand_line(jnp.dot(onehot_line, rel_bias, precision=HIGH).T)
    mixed_heads, log_total = lax.map(
        partial(attend_forward, bias_full), (by_seq[0], by_seq[1], by_seq[2], piece_starts)
    )
    mixed_heads = mixed_heads.reshape(tok_count, heads_here * head_width)
    resid = tokens + reduce_heads(
        jnp.dot(mixed_heads, attn_out, preferred_element_type=jnp.float32)
    )
    scale_two, normed_two = norm_forward(resid, gain_two, model_width)
    logits = jnp.dot(normed_two, router, preferred_element_type=jnp.float32)
    chosen = (routes[:, :, None] == jnp.arange(EXPERTS, dtype=jnp.int32)[None, None, :]).astype(
        jnp.float32
    )
    picked = jnp.sum(chosen * logits[:, None, :], axis=2)
    gate_weights = jax.nn.softmax(picked, axis=1)
    slot_index, kept_pairs = slot_table(routes)
    keep_float = kept_pairs.astype(jnp.float32)
    mix_weight = gate_weights * keep_float
    safe_index = jnp.minimum(slot_index, EXPERTS * CAP - 1)
    token_rows = jnp.repeat(normed_two, TOP, axis=0)
    buffer = (
        jnp.zeros((EXPERTS * CAP + 1, model_width), jnp.bfloat16)
        .at[slot_index.reshape(-1)]
        .set(token_rows)
    )
    buffer = buffer[: EXPERTS * CAP].reshape(-1, local_experts, CAP, model_width)
    received = lax.all_to_all(buffer, "expert", split_axis=0, concat_axis=0, tiled=True)
    gate_part, up_part, hidden, partial_out = expert_forward(
        received, expert_gate, expert_up, expert_down
    )
    returned = spread_slots(owner_exchange(expert_sums(partial_out).astype(jnp.bfloat16)))
    flat_ret = returned.reshape(EXPERTS * CAP, model_width)
    fetched = flat_ret[safe_index].astype(jnp.float32)
    output = resid + jnp.sum(mix_weight[:, :, None] * fetched, axis=1)
    grad_y = grad_out.T.astype(jnp.float32)
    grad_gates = jnp.sum(grad_y[:, None, :] * fetched, axis=2) * keep_float
    grad_picked = gate_weights * (
        grad_gates - jnp.sum(gate_weights * grad_gates, axis=1, keepdims=True)
    )
    grad_logits = jnp.sum(chosen * grad_picked[:, :, None], axis=1)
    grad_router = jnp.dot(normed_two.astype(jnp.float32).T, grad_logits, precision=HIGH)
    grad_normed_two = jnp.dot(grad_logits, router.astype(jnp.float32).T, precision=HIGH)
    slot_grads = (mix_weight[:, :, None] * grad_y[:, None, :]).astype(jnp.bfloat16)
    grad_ret = (
        jnp.zeros((EXPERTS * CAP + 1, model_width), jnp.bfloat16)
        .at[slot_index.reshape(-1)]
        .set(slot_grads.reshape(-1, model_width))
    )
    grad_ret = grad_ret[: EXPERTS * CAP].reshape(-1, local_experts, CAP, model_width)
    grad_share = lax.dynamic_slice_in_dim(grad_ret, share_start, part_rows, 2)
    grad_rows_out = spread_slots(owner_exchange(grad_share))
    grad_expert_gate, grad_expert_up, grad_expert_down, grad_rows_in = expert_backward(
        received, gate_part, up_part, hidden, grad_rows_out, expert_gate, expert_up, expert_down
    )
    grad_back = spread_slots(owner_exchange(expert_sums(grad_rows_in).astype(jnp.bfloat16)))
    flat_back = grad_back.reshape(EXPERTS * CAP, model_width).astype(jnp.float32)
    grad_normed_two = grad_normed_two + jnp.sum(
        flat_back[safe_index] * keep_float[:, :, None], axis=1
    )
    grad_gain_two, grad_resid = norm_backward(
        resid, scale_two, gain_two, grad_normed_two, model_width
    )
    grad_resid = grad_resid + grad_y
    grad_attn = grad_resid.astype(jnp.bfloat16)
    grad_attn_out = jnp.einsum(
        "th,td->hd", mixed_heads, grad_attn, preferred_element_type=jnp.float32
    )
    grad_mixed = jnp.einsum(
        "td,hd->th", grad_attn, attn_out, preferred_element_type=jnp.float32
    ).astype(jnp.bfloat16)
    grad_by_seq = grad_mixed.reshape(seqs_here, SEQ, heads_here, head_width)
    bias_grad_full, grad_project = lax.scan(
        partial(attend_backward, bias_full),
        jnp.zeros_like(bias_full),
        (by_seq[0], by_seq[1], by_seq[2], grad_by_seq, piece_starts, log_total),
    )
    grad_project = (
        jnp.moveaxis(grad_project, 1, 0)
        .reshape(3, tok_count, heads_here * head_width)
        .astype(jnp.bfloat16)
    )
    grad_attn_in = jnp.einsum(
        "cth,td->chd", grad_project, normed, preferred_element_type=jnp.float32
    )
    grad_normed = reduce_heads(
        jnp.einsum("cth,chd->td", grad_project, attn_in, preferred_element_type=jnp.float32)
    )
    grad_gain_one, grad_tokens = norm_backward(
        tokens, scale_one, gain_one, grad_normed, model_width
    )
    grad_tokens = grad_tokens + grad_resid
    grad_rel_bias = jnp.dot(onehot_line.T, fold_line(bias_grad_full).T, precision=HIGH)
    shared = (
        lax.psum(grad_gain_one.astype(jnp.bfloat16), "expert").astype(jnp.float32),
        lax.psum(grad_attn_in.astype(jnp.bfloat16), "expert").astype(jnp.float32),
        lax.psum(grad_rel_bias.astype(jnp.bfloat16), "expert").astype(jnp.float32),
        lax.psum(grad_attn_out.astype(jnp.bfloat16), "expert").astype(jnp.float32),
        lax.psum(grad_gain_two.astype(jnp.bfloat16), "expert").astype(jnp.float32),
        lax.psum(grad_router.astype(jnp.bfloat16), "expert").astype(jnp.float32),
    )
    return (
        output.astype(jnp.bfloat16).T,
        grad_tokens.T,
        shared[0],
        shared[1],
        shared[2],
        shared[3],
        shared[4],
        shared[5],
        grad_expert_gate,
        grad_expert_up,
        grad_expert_down,
    )


def solution(mesh):
    placed = (
        P(None, "expert"),
        P(),
        P(None, "tensor", None),
        P(None, "tensor"),
        P("tensor", None),
        P(),
        P(),
        P("expert", "tensor", None),
        P("expert", "tensor", None),
        P("expert", "tensor", None),
        P("expert", None),
        P("expert", None),
        P(None, "expert"),
    )
    paired = mesh.shape["tensor"] == 4 and mesh.shape["expert"] * 2 == EXPERTS
    return jax.shard_map(
        on_device if paired else on_device_general,
        mesh=mesh,
        in_specs=placed,
        out_specs=(
            P(None, "expert"),
            P(None, "expert"),
            P(),
            P(None, "tensor", None),
            P(None, "tensor"),
            P("tensor", None),
            P(),
            P(),
            P("expert", "tensor", None),
            P("expert", "tensor", None),
            P("expert", "tensor", None),
        ),
        check_vma=False,
    )
```

```python
from functools import partial

import jax
import jax.numpy as jnp
from jax import lax
from jax.experimental import pallas as pl
from jax.experimental.pallas import tpu as pltpu
from jax.sharding import PartitionSpec as P

EXPERTS = 16
BUCKETS = 32
TOP = 2
PIECE = 256
SEQ = 1024
CAP = 320
BLK = 256


EPS = 1e-06
NEG = -1e30
THRESHOLDS = (12, 16, 23, 32, 46, 64, 91)
HIGH = lax.Precision.HIGHEST
F32 = jnp.float32
BF16 = jnp.bfloat16
NN = (((1,), (0,)), ((), ()))
NT = (((1,), (1,)), ((), ()))
TN = (((0,), (0,)), ((), ()))
MIB = 1 << 20


def mm(left, right, dims=NN):
    return lax.dot_general(left, right, dims, preferred_element_type=F32)


def params(limit=56):
    return pltpu.CompilerParams(vmem_limit_bytes=limit * MIB)


def cost(flops, bytes_accessed, transcendentals=0):
    return pl.CostEstimate(
        flops=int(flops), bytes_accessed=int(bytes_accessed), transcendentals=int(transcendentals)
    )


def bucket_of(offset):
    magnitude = jnp.abs(offset)
    beyond = sum(((magnitude >= threshold).astype(jnp.int32) for threshold in THRESHOLDS))
    lower_part = jnp.where(magnitude < 8, magnitude, 8 + beyond)
    return lower_part + 16 * (offset > 0).astype(jnp.int32)


def project_kernel(x_ref, gain_ref, w_ref, out_ref, scale_ref):
    x = x_ref[...].astype(F32)
    scale = lax.rsqrt(jnp.sum(x * x, axis=0, keepdims=True) / x.shape[0] + EPS)
    normed = (x * scale * gain_ref[...]).astype(BF16)
    out_ref[...] = mm(w_ref[...], normed).astype(BF16)
    scale_ref[...] = scale


def project(x, gain, weights):
    width, tokens = x.shape
    rows = weights.shape[0]
    tile = 512
    return pl.pallas_call(
        project_kernel,
        grid=(tokens // tile,),
        in_specs=[
            pl.BlockSpec((width, tile), lambda i: (0, i)),
            pl.BlockSpec((width, 1), lambda i: (0, 0)),
            pl.BlockSpec((rows, width), lambda i: (0, 0)),
        ],
        out_specs=[
            pl.BlockSpec((rows, tile), lambda i: (0, i)),
            pl.BlockSpec((1, tile), lambda i: (0, i)),
        ],
        out_shape=[
            jax.ShapeDtypeStruct((rows, tokens), BF16),
            jax.ShapeDtypeStruct((1, tokens), F32),
        ],
        compiler_params=params(),
        cost_estimate=cost(2 * width * tokens * rows, 2 * width * tokens * 2),
    )(x, gain, weights)


def line_offsets(number):
    column = lax.broadcasted_iota(jnp.int32, (8, BLK), 1)
    return (number - 1) * BLK - column


def bias_tiles_kernel(table_ref, tiles_ref):
    row = lax.broadcasted_iota(jnp.int32, (BLK, BLK), 0)
    column = lax.broadcasted_iota(jnp.int32, (BLK, BLK), 1)
    buckets = [bucket_of(line_offsets(number)) for number in range(4)]
    for head in range(tiles_ref.shape[0]):
        far = table_ref[15, head]
        rolled = []
        for number, bucket in enumerate(buckets):
            value = jnp.zeros((8, BLK), F32)
            for index in range(BUCKETS):
                value = jnp.where(bucket == index, table_ref[index, head] - far, value)
            whole = jnp.broadcast_to(value[0:1], (BLK, BLK))
            rolled.append(pltpu.roll(whole, 0, 1, stride=1, stride_axis=0))
        for number in range(3):
            tiles_ref[head, number] = jnp.where(column >= row, rolled[number], rolled[number + 1])


def bias_tiles(table):
    heads = table.shape[1]
    return pl.pallas_call(
        bias_tiles_kernel,
        in_specs=[pl.BlockSpec(memory_space=pltpu.SMEM)],
        out_specs=pl.BlockSpec(memory_space=pltpu.VMEM),
        out_shape=jax.ShapeDtypeStruct((heads, 3, BLK, BLK), F32),
        compiler_params=params(),
        cost_estimate=cost(heads * 3 * BLK * BLK * 60, heads * 3 * BLK * BLK * 4),
    )(table)


def bias_fold(near_ref, far_ref):
    heads = near_ref.shape[0] // 2
    sums = jnp.zeros((BUCKETS, 128), F32)
    lane = lax.broadcasted_iota(jnp.int32, (BUCKETS, 128), 1)
    row = lax.broadcasted_iota(jnp.int32, (BLK, BLK), 0)
    column = lax.broadcasted_iota(jnp.int32, (BLK, BLK), 1)
    flip = jnp.where(row + column == BLK - 1, 1.0, 0.0).astype(BF16)
    apart = jnp.where(column == BLK - 1, 0, column + 1)
    ahead = apart <= row
    number_at = lax.broadcasted_iota(jnp.int32, (BUCKETS, BLK), 0)
    for head in range(heads):
        lines = [jnp.zeros((1, BLK), F32) for _ in range(4)]
        for number in range(3):
            grads = near_ref[head, number] + near_ref[heads + head, number]
            coarse = grads.astype(BF16)
            fine = (grads - coarse.astype(F32)).astype(BF16)
            flipped = mm(flip, coarse) + mm(flip, fine)
            rolled = pltpu.roll(flipped, 0, 1, stride=1, stride_axis=0)
            lines[number] += jnp.sum(jnp.where(ahead, rolled, 0.0), axis=0, keepdims=True)
            lines[number + 1] += jnp.sum(jnp.where(ahead, 0.0, rolled), axis=0, keepdims=True)
        total = jnp.zeros((BUCKETS, 1), F32)
        for number, line in enumerate(lines):
            bucket = bucket_of((number - 1) * BLK - apart[:1])
            total += jnp.sum(jnp.where(bucket == number_at, line, 0.0), axis=1, keepdims=True)
        distant = jnp.sum(far_ref[head] + far_ref[heads + head], axis=0, keepdims=True)
        distant = jnp.sum(distant, axis=1, keepdims=True)
        total += jnp.where(number_at[:, :1] == 15, distant, 0.0)
        sums = jnp.where(lane == head, total, sums)
    return sums


def key_count(query_block):
    return 2 * BLK if query_block < 2 else 4 * BLK


def block_scores(keys, queries, tiles_ref, limit, block):
    count = key_count(block)
    parts = []
    whole = mm(keys[:, :count], queries, TN)
    for key_block in range(count // BLK):
        part = whole[key_block * BLK : (key_block + 1) * BLK]
        shift = key_block - block
        if -1 <= shift <= 1:
            part = part + tiles_ref[0, shift + 1]
        if shift >= 0:
            key_at = lax.broadcasted_iota(jnp.int32, (BLK, BLK), 0) + key_block * BLK
            part = jnp.where(key_at <= limit, part, NEG)
        parts.append(part)
    return jnp.concatenate(parts, axis=0)


def attend_kernel(q_ref, k_ref, v_ref, tiles_ref, limit_ref, w_ref, out_ref, lse_ref, sent_ref, held):
    head = pl.program_id(1)
    width = q_ref.shape[0]
    queries = q_ref[...] * BF16(0.125)
    keys, values = k_ref[...], v_ref[...]
    for block in range(SEQ // BLK):
        cols = slice(block * BLK, (block + 1) * BLK)
        scores = block_scores(keys, queries[:, cols], tiles_ref, limit_ref[0, :, cols], block)
        top = jnp.max(scores, axis=0, keepdims=True)
        exponent = jnp.exp(scores - top)
        total = jnp.sum(exponent, axis=0, keepdims=True)
        mixed = mm(values[:, : key_count(block)], exponent.astype(BF16)) / total
        mixed = mixed.astype(BF16)
        out_ref[:, cols] = mixed
        held[pl.ds(pl.multiple_of(head * width, width), width), cols] = mixed
        lse_ref[0, :, cols] = top + jnp.log(total)

    @pl.when(head == pl.num_programs(1) - 1)
    def _():
        sent_ref[...] = mm(held[...], w_ref[...], TN).astype(BF16)


def attend(qkv, tiles, limits, attn_out):
    heads = tiles.shape[0]
    seqs = limits.shape[0]
    width = qkv.shape[0] // (3 * heads)
    model_width = attn_out.shape[1]
    return pl.pallas_call(
        attend_kernel,
        grid=(seqs, heads),
        in_specs=[
            pl.BlockSpec((width, SEQ), lambda s, h: (h, s)),
            pl.BlockSpec((width, SEQ), lambda s, h: (heads + h, s)),
            pl.BlockSpec((width, SEQ), lambda s, h: (2 * heads + h, s)),
            pl.BlockSpec((1, 3, BLK, BLK), lambda s, h: (h, 0, 0, 0)),
            pl.BlockSpec((1, 1, SEQ), lambda s, h: (s, 0, 0)),
            pl.BlockSpec((heads * width, model_width), lambda s, h: (0, 0)),
        ],
        out_specs=[
            pl.BlockSpec((width, SEQ), lambda s, h: (h, s)),
            pl.BlockSpec((1, 1, SEQ), lambda s, h: (s * heads + h, 0, 0)),
            pl.BlockSpec((SEQ, model_width), lambda s, h: (s, 0)),
        ],
        out_shape=[
            jax.ShapeDtypeStruct((heads * width, seqs * SEQ), BF16),
            jax.ShapeDtypeStruct((seqs * heads, 1, SEQ), F32),
            jax.ShapeDtypeStruct((seqs * SEQ, model_width), BF16),
        ],
        scratch_shapes=[pltpu.VMEM((heads * width, SEQ), BF16)],
        compiler_params=params(),
        cost_estimate=cost(seqs * heads * SEQ * SEQ * 512, seqs * heads * SEQ * 2048, seqs * heads * SEQ * SEQ),
    )(qkv, qkv, qkv, tiles, limits, attn_out)


def attend_back_kernel(
    q_ref, k_ref, v_ref, tiles_ref, limit_ref, w_ref, grad_ref, lse_ref, part_ref, resid_ref,
    dq_ref, dk_ref, dv_ref, near_ref, far_ref, y_ref,
    held, parts, total, turn_across, turn_along, from_across, from_along, sends, recvs, loads,
):
    rank = lax.axis_index("tensor")
    pair_class, half_index = rank % 2, rank // 2
    across, along, corner = rank + 1 - 2 * pair_class, rank + 2 - 4 * half_index, 3 - rank
    step = pl.program_id(0) * pl.num_programs(1) + pl.program_id(1)
    mesh_ids = pl.DeviceIdType.MESH
    middle = parts.shape[2] // 2
    low, high = slice(0, middle), slice(middle, 2 * middle)

    def remote(number, origin, target, other):
        return pltpu.make_async_remote_copy(
            src_ref=origin, dst_ref=target, send_sem=sends.at[number], recv_sem=recvs.at[number],
            device_id={"tensor": other}, device_id_type=mesh_ids,
        )

    first = (
        remote(0, part_ref.at[corner, :, low], turn_across, across),
        remote(1, part_ref.at[corner, :, high], turn_along, along),
    )
    second = remote(2, parts.at[0], from_across, across), remote(3, parts.at[1], from_along, along)
    local = [
        pltpu.make_async_copy(part_ref.at[other], parts.at[number], loads.at[number])
        for number, other in enumerate((across, along, rank))
    ]
    local.append(pltpu.make_async_copy(resid_ref, total, loads.at[3]))

    @pl.when(step == 0)
    def _():
        barrier = pltpu.get_barrier_semaphore()
        for other in (across, along):
            pl.semaphore_signal(barrier, inc=1, device_id={"tensor": other}, device_id_type=mesh_ids)
        pl.semaphore_wait(barrier, 2)
        for copy in first:
            copy.start()
        for copy in local:
            copy.start()

    @pl.when(step == 3)
    def _():
        for copy in (*first, *local):
            copy.wait()
        parts[0, :, high] = (parts[0, :, high].astype(F32) + turn_along[...].astype(F32)).astype(BF16)
        parts[1, :, low] = (parts[1, :, low].astype(F32) + turn_across[...].astype(F32)).astype(BF16)
        for copy in second:
            copy.start()

    head = pl.program_id(1)
    width = q_ref.shape[0]

    @pl.when(head == 0)
    def _():
        held[...] = mm(w_ref[...], grad_ref[...], NT).astype(BF16)

    queries = q_ref[...] * BF16(0.125)
    keys, values = k_ref[...], v_ref[...]
    grads = held[pl.ds(pl.multiple_of(head * width, width), width), :]
    near_ref[...] = jnp.zeros_like(near_ref)
    far = jnp.zeros((8, BLK), F32)
    grad_keys = jnp.zeros((width, SEQ), F32)
    grad_values = jnp.zeros((width, SEQ), F32)
    for block in range(SEQ // BLK):
        count = key_count(block)
        cols = slice(block * BLK, (block + 1) * BLK)
        scores = block_scores(keys, queries[:, cols], tiles_ref, limit_ref[0, :, cols], block)
        probs = jnp.exp(scores - lse_ref[0, :, cols])
        grad_probs = mm(values[:, :count], grads[:, cols], TN)
        inner = jnp.sum(probs * grad_probs, axis=0, keepdims=True)
        grad_scores = probs * (grad_probs - inner)
        for key_block in range(count // BLK):
            part = grad_scores[key_block * BLK : (key_block + 1) * BLK]
            shift = key_block - block
            if -1 <= shift <= 1:
                near_ref[0, shift + 1] += part
            elif shift < -1:
                far = far + jnp.sum(part.reshape(BLK // 8, 8, BLK), axis=0)
        rounded = grad_scores.astype(BF16)
        add_values = mm(grads[:, cols], probs.astype(BF16), NT)
        add_keys = mm(queries[:, cols], rounded, NT)
        if count == SEQ:
            grad_values = grad_values + add_values
            grad_keys = grad_keys + add_keys
        else:
            filler = jnp.zeros((width, SEQ - count), F32)
            grad_values = grad_values + jnp.concatenate([add_values, filler], axis=1)
            grad_keys = grad_keys + jnp.concatenate([add_keys, filler], axis=1)
        dq_ref[:, cols] = (mm(keys[:, :count], rounded) * 0.125).astype(BF16)
    dk_ref[...] = grad_keys.astype(BF16)
    dv_ref[...] = grad_values.astype(BF16)
    far_ref[0] = far

    @pl.when(step == 7)
    def _():
        for copy in second:
            copy.wait()
        summed = parts[2].astype(F32) + from_across[...].astype(F32) + from_along[...].astype(F32)
        y_ref[...] = (total[...] + summed).astype(BF16)


def attend_back(qkv, tiles, limits, attn_out, grad_attn, lse, part, resid):
    heads = tiles.shape[0]
    seqs = limits.shape[0]
    width = qkv.shape[0] // (3 * heads)
    model_width = attn_out.shape[1]
    share = part.shape[1]
    grad_spec = pl.BlockSpec((width, SEQ), lambda s, h: (h, s))
    anywhere = pl.BlockSpec(memory_space=pl.ANY)
    return pl.pallas_call(
        attend_back_kernel,
        grid=(seqs, heads),
        in_specs=[
            pl.BlockSpec((width, SEQ), lambda s, h: (h, s)),
            pl.BlockSpec((width, SEQ), lambda s, h: (heads + h, s)),
            pl.BlockSpec((width, SEQ), lambda s, h: (2 * heads + h, s)),
            pl.BlockSpec((1, 3, BLK, BLK), lambda s, h: (h, 0, 0, 0)),
            pl.BlockSpec((1, 1, SEQ), lambda s, h: (s, 0, 0)),
            pl.BlockSpec((heads * width, model_width), lambda s, h: (0, 0)),
            pl.BlockSpec((SEQ, model_width), lambda s, h: (s, 0)),
            pl.BlockSpec((1, 1, SEQ), lambda s, h: (s * heads + h, 0, 0)),
        ]
        + [anywhere] * 2,
        out_specs=[
            grad_spec,
            grad_spec,
            grad_spec,
            pl.BlockSpec((1, 3, BLK, BLK), lambda s, h: (s * heads + h, 0, 0, 0)),
            pl.BlockSpec((1, 8, BLK), lambda s, h: (s * heads + h, 0, 0)),
            pl.BlockSpec((share, model_width), lambda s, h: (0, 0)),
        ],
        out_shape=[jax.ShapeDtypeStruct((heads * width, seqs * SEQ), BF16)] * 3
        + [
            jax.ShapeDtypeStruct((seqs * heads, 3, BLK, BLK), F32),
            jax.ShapeDtypeStruct((seqs * heads, 8, BLK), F32),
        ]
        + [jax.ShapeDtypeStruct((share, model_width), BF16)],
        scratch_shapes=[
            pltpu.VMEM((heads * width, SEQ), BF16),
            pltpu.VMEM((3, share, model_width), BF16),
            pltpu.VMEM((share, model_width), F32),
            pltpu.VMEM((share, model_width // 2), BF16),
            pltpu.VMEM((share, model_width // 2), BF16),
            pltpu.VMEM((share, model_width), BF16),
            pltpu.VMEM((share, model_width), BF16),
            pltpu.SemaphoreType.DMA((4,)),
            pltpu.SemaphoreType.DMA((4,)),
            pltpu.SemaphoreType.DMA((4,)),
        ],
        compiler_params=pltpu.CompilerParams(
            vmem_limit_bytes=60 * MIB, collective_id=5, has_side_effects=True
        ),
        cost_estimate=cost(seqs * heads * SEQ * SEQ * 1280, seqs * heads * SEQ * 4096, seqs * heads * SEQ * SEQ),
    )(qkv, qkv, qkv, tiles, limits, attn_out, grad_attn, lse, part, resid)


def project_back_kernel(
    place_ref, x_ref, gain_ref, gain_row_ref, scale_ref, w_ref, mixed_ref, attn_ref, dq_ref, dk_ref, dv_ref, *refs
):
    step = pl.program_id(0)
    own_refs, got_refs, (weight_ref, out_ref, gain_grad_ref), placed_refs, total = (
        refs[:3], refs[3:6], refs[6:9], refs[9:12], refs[12]
    )
    for own_ref, got_ref, placed_ref in zip(own_refs, got_refs, placed_refs):
        placed_ref[place_ref[0]] = own_ref[...]
        placed_ref[1 - place_ref[0]] = got_ref[...].astype(F32)
    grads = jnp.concatenate([dq_ref[...], dk_ref[...], dv_ref[...]], axis=0)
    rows = grads.shape[0]
    normed = (x_ref[...].astype(F32) * scale_ref[...] * gain_ref[...]).astype(BF16)

    @pl.when(step == 0)
    def _():
        total[...] = jnp.zeros_like(total)

    total[:rows] += mm(grads, normed, NT)
    total[rows:] += mm(mixed_ref[...], attn_ref[...])
    out_ref[...] = mm(grads, w_ref[...], TN).astype(BF16)

    @pl.when(step == pl.num_programs(0) - 1)
    def _():
        weight_ref[...] = total[...].astype(BF16)
        through = jnp.sum(total[:rows] * w_ref[...].astype(F32), axis=0, keepdims=True)
        gain_grad_ref[...] = through / gain_row_ref[...]


def project_back(place, x, gain, gain_row, scale, weights, mixed, grad_attn, grads, owns, gots):
    width, tokens = x.shape
    rows = weights.shape[0]
    heads_width = mixed.shape[0]
    units = owns[0].shape[0]
    steps = 4
    tile = tokens // steps
    part = units // steps
    column = lambda count: pl.BlockSpec((count, tile), lambda i: (0, i))
    return pl.pallas_call(
        project_back_kernel,
        grid=(steps,),
        in_specs=[
            pl.BlockSpec(memory_space=pltpu.SMEM),
            column(width),
            pl.BlockSpec((width, 1), lambda i: (0, 0)),
            pl.BlockSpec((1, width), lambda i: (0, 0)),
            column(1),
            pl.BlockSpec((rows, width), lambda i: (0, 0)),
            column(heads_width),
            pl.BlockSpec((tile, width), lambda i: (i, 0)),
        ]
        + [column(rows // 3)] * 3
        + [pl.BlockSpec((part, width), lambda i: (i, 0))] * 6,
        out_specs=[
            pl.BlockSpec((rows + heads_width, width), lambda i: (0, 0)),
            pl.BlockSpec((tile, width), lambda i: (i, 0)),
            pl.BlockSpec((1, width), lambda i: (0, 0)),
        ]
        + [pl.BlockSpec((2, part, width), lambda i: (0, i, 0))] * 3,
        out_shape=[
            jax.ShapeDtypeStruct((rows + heads_width, width), BF16),
            jax.ShapeDtypeStruct((tokens, width), BF16),
            jax.ShapeDtypeStruct((1, width), F32),
        ]
        + [jax.ShapeDtypeStruct((2, units, width), F32)] * 3,
        scratch_shapes=[pltpu.VMEM((rows + heads_width, width), F32)],
        compiler_params=params(),
        cost_estimate=cost(5 * width * tokens * rows, 6 * width * tokens + 14 * units * width),
    )(place, x, gain, gain_row, scale, weights, mixed, grad_attn, *grads, *owns, *gots)


def exchange(
    math, rank, source, full_out, full, from_across, from_along, to_across, to_along, turn_across, turn_along, sends, recvs, outs, ready=None, ready_full=None, side=None, peers=(), fill=None, start=None, cut=None, later=None):
    pair_class, half_index = rank % 2, rank // 2
    across, along, corner = rank + 1 - 2 * pair_class, rank + 2 - 4 * half_index, 3 - rank
    mesh_ids = pl.DeviceIdType.MESH
    rows, width = source.shape[1:]
    chunks = 4
    size = rows // chunks
    cut = cut or width // 2
    low, high = slice(0, cut), slice(cut, width)
    barrier = pltpu.get_barrier_semaphore()
    near = (across, along, corner) if later else (across, along)
    for other in near:
        pl.semaphore_signal(barrier, inc=1, device_id={"tensor": other}, device_id_type=mesh_ids)
    for other in peers:
        pl.semaphore_signal(barrier, inc=1, device_id={"expert": other}, device_id_type=mesh_ids)
    pl.semaphore_wait(barrier, len(near) + len(peers))

    def remote(kind, chunk, origin, target, other):
        return pltpu.make_async_remote_copy(
            src_ref=origin, dst_ref=target, send_sem=sends.at[kind, chunk], recv_sem=recvs.at[kind, chunk],
            device_id={"tensor": other}, device_id_type=mesh_ids,
        )

    if start:
        start()
    if fill:
        fill(corner)
    spans = [slice(chunk * size, (chunk + 1) * size) for chunk in range(chunks)]
    first, second, third, fourth = [], [], [], []
    for chunk, span in enumerate(spans):
        pair = (
            remote(0, chunk, source.at[corner, span, low], turn_across.at[span, low], across),
            remote(1, chunk, source.at[corner, span, high], turn_along.at[span, high], along),
        )
        for copy in pair:
            copy.start()
        first.append(pair)
    if fill:
        fill(along)
        fill(across)
    leaving = []

    def leave(number, other):
        leaving.append(pltpu.make_async_copy(full.at[other], full_out.at[other], outs.at[number]))
        leaving[-1].start()

    if ready is not None:
        _, near_across, near_along = ready
        extra = [
            remote(8, 0, near_along.at[:, low], ready_full.at[along, :, low], across),
            remote(8, 1, near_across.at[:, high], ready_full.at[across, :, high], along),
        ]
        extra += [
            pltpu.make_async_copy(piece, ready_full.at[other], outs.at[4 + number])
            for number, (other, piece) in enumerate(zip((rank, across, along), ready))
        ]
        for copy in extra:
            copy.start()
    for chunk, span in enumerate(spans):
        if side:
            side(chunk)
        first[chunk][0].wait()
        to_along[span, low] = (source[along, span, low].astype(F32) + turn_across[span, low].astype(F32)).astype(BF16)
        to_along[span, high] = source[along, span, high]
        first[chunk][1].wait()
        to_across[span, low] = source[across, span, low]
        to_across[span, high] = (source[across, span, high].astype(F32) + turn_along[span, high].astype(F32)).astype(BF16)
        pair = (
            remote(2, chunk, to_across.at[span], from_across.at[span], across),
            remote(3, chunk, to_along.at[span], from_along.at[span], along),
        )
        for copy in pair:
            copy.start()
        second.append(pair)
    def pass_on(chunk):
        span = spans[chunk]
        for copy in third[chunk]:
            copy.wait()
        pair = (
            remote(6, chunk, full.at[along, span, low], full.at[along, span, low], across),
            remote(7, chunk, full.at[across, span, high], full.at[across, span, high], along),
        )
        for copy in pair:
            copy.start()
        fourth.append(pair)

    if fill:
        fill(rank)
    if later:
        later((across, along, corner))
    for chunk, span in enumerate(spans):
        if side:
            side(chunks + chunk)
        for copy in second[chunk]:
            copy.wait()
        total = source[rank, span].astype(F32) + from_across[span].astype(F32) + from_along[span].astype(F32)
        full[rank, span] = math(span, total).astype(BF16)
        pair = (
            remote(4, chunk, full.at[rank, span], full.at[rank, span], across),
            remote(5, chunk, full.at[rank, span], full.at[rank, span], along),
        )
        for copy in pair:
            copy.start()
        third.append(pair)
        if chunk:
            pass_on(chunk - 1)
    leave(0, rank)
    pass_on(chunks - 1)
    leave(1, across)
    leave(2, along)
    if ready is not None:
        for copy in extra:
            copy.wait()
    if side and later:
        side(2 * chunks)
    for pair in fourth:
        for copy in pair:
            copy.wait()
    leave(3, corner)
    if side and not later:
        side(2 * chunks)
    for copy in leaving:
        copy.wait()


def exchange_call(kernel, number, shape, operands, extra_shapes, scratch=(), in_hbm=(), out_hbm=()):
    tokens, width = shape
    ranks = 4
    rows = tokens // ranks
    here = pl.BlockSpec(memory_space=pltpu.VMEM)
    results = pl.pallas_call(
        kernel,
        in_specs=[pl.BlockSpec(memory_space=pl.ANY) if k in in_hbm else here for k in range(len(operands))],
        out_specs=[pl.BlockSpec(memory_space=pl.ANY)]
        + [pl.BlockSpec(memory_space=pl.ANY) if k in out_hbm else here for k in range(len(extra_shapes))],
        out_shape=[jax.ShapeDtypeStruct((ranks, rows, width), BF16)]
        + [jax.ShapeDtypeStruct(shape, kind) for shape, kind in extra_shapes],
        scratch_shapes=[pltpu.VMEM((ranks, rows, width), BF16)]
        + [pltpu.VMEM((rows, width), BF16)] * 6
        + [pltpu.SemaphoreType.DMA((9, 4))] * 2
        + [pltpu.SemaphoreType.DMA((7,))]
        + list(scratch),
        compiler_params=pltpu.CompilerParams(
            vmem_limit_bytes=60 * MIB, collective_id=number, has_side_effects=True
        ),
        cost_estimate=cost(40 * MIB, 200 * MIB),
    )(*operands)
    return results[0].reshape(tokens, width), *results[1:]


def norm_two_kernel(
    source, x_ref, gain_ref, grad_out_ref, routes_ref,
    full, resid_ref, scale_ref, dy_out, dy_rows_out, code_ref, codes_ref, own_ref, *rest,
):
    held, grad_out, dy_ref, dy_rows_ref, load = rest[-5:]
    rank = lax.axis_index("tensor")
    ranks, rows, width = source.shape
    loading = pltpu.make_async_copy(grad_out_ref, grad_out, load.at[1])
    storing = [
        pltpu.make_async_copy(dy_ref, dy_out, load.at[2]),
        pltpu.make_async_copy(dy_rows_ref, dy_rows_out, load.at[3]),
    ]

    def start():
        own.start()
        loading.start()

    slots = dy_rows_ref.shape[0] // ranks
    own = pltpu.make_async_copy(x_ref.at[:, pl.ds(pl.multiple_of(rank * rows, rows), rows)], held, load.at[0])

    def math(span, total):
        resid = own_ref[span, :].astype(F32) + total
        scale = lax.rsqrt(jnp.sum(resid * resid, axis=1, keepdims=True) / resid.shape[1] + EPS)
        resid_ref[span, :] = resid
        scale_ref[span, :] = scale
        return resid * scale * gain_ref[...]

    def side(number):
        if number == 0:
            own.wait()
            own_ref[...] = held[...].astype(F32).T.astype(BF16)
            local_codes(routes_ref, code_ref, rank % 2, rank // 2, CAP // 2)
            codes_ref[...] = jnp.concatenate([code_ref[...].astype(F32)] * 4, axis=0).T[:, :TOP].astype(jnp.int32)
            loading.wait()
        if number < ranks:
            span = slice(number * rows, (number + 1) * rows)
            dy_ref[span, :] = grad_out[:, span].astype(F32).T.astype(BF16)
        elif number < 2 * ranks:
            start = (number - ranks) * slots
            slot = lax.broadcasted_iota(jnp.int32, (slots, dy_ref.shape[0]), 0) + start
            take = jnp.where((slot == code_ref[0:1]) | (slot == code_ref[1:2]), 1.0, 0.0).astype(BF16)
            dy_rows_ref[start : start + slots, :] = mm(take, dy_ref[...]).astype(BF16)
        if number == ranks - 1:
            storing[0].start()
        elif number == 2 * ranks - 1:
            storing[1].start()
        elif number == 2 * ranks:
            for copy in storing:
                copy.wait()

    exchange(math, rank, source, full, *rest[:-5], side=side, start=start)


def norm_back(grad, value, scale, gain):
    scaled = grad * gain
    inner = jnp.sum(scaled * value, axis=1, keepdims=True)
    return scale * scaled - value * (scale * scale * scale) * (inner / value.shape[1])


def norm_two_back_kernel(
    ret_in, back_ref, code_ref, codes_ref, gates_ref, routes_ref, dy_rows_in, gate_ref, router_ref, h_in,
    resid_in, scale_ref, dy_in, gain_ref, full, grad_ref, gain_grad_ref, router_grad_ref, y_out, *rest,
):
    source, scaled, logit_parts, logit_own, send, recv, ret_ref, dy_rows_ref, h_ref, resid_ref, dy_ref, y_ref, load = rest[-13:]
    rank = lax.axis_index("tensor")
    rows = source.shape[1]
    slots, tokens = ret_ref.shape[0], code_ref.shape[1]
    ranks = tokens // rows
    copies = []
    own_dy = dy_in.at[pl.ds(pl.multiple_of(rank * rows, rows), rows)]
    pairs = ((ret_in, ret_ref), (dy_rows_in, dy_rows_ref), (resid_in, resid_ref), (own_dy, dy_ref), (h_in, h_ref))
    loading = [pltpu.make_async_copy(*pair, load.at[number]) for number, pair in enumerate(pairs)]
    storing = [
        pltpu.make_async_copy(y_ref.at[shard], y_out.at[pl.ds(shard * rows, rows)], load.at[5 + shard])
        for shard in range(ranks)
    ]

    def start():
        for copy in loading:
            copy.start()

    def later(others):
        for copy in loading:
            copy.wait()
        found = [jnp.zeros((1, tokens), F32) for _ in range(TOP)]
        tile = slots // 4
        for begin in range(0, slots, tile):
            span = slice(begin, begin + tile)
            ret = ret_ref[span, :].astype(F32)
            slot_grad = jnp.sum(dy_rows_ref[span, :].astype(F32) * ret, axis=1, keepdims=True)
            scaled[span, :] = (ret * gate_ref[span, :]).astype(BF16)
            slot = lax.broadcasted_iota(jnp.int32, (tile, tokens), 0) + begin
            for i in range(TOP):
                found[i] = found[i] + jnp.sum(
                    jnp.where(slot == code_ref[i : i + 1, :], slot_grad, 0.0), axis=0, keepdims=True
                )
        mean = gates_ref[0:1] * found[0] + gates_ref[1:2] * found[1]
        expert = lax.broadcasted_iota(jnp.int32, (EXPERTS, tokens), 0)
        logit = sum(
            jnp.where(routes_ref[i : i + 1] == expert, gates_ref[i : i + 1] * (found[i] - mean), 0.0)
            for i in range(TOP)
        )
        for shard in range(ranks):
            logit_parts[shard] = logit[:, shard * rows : (shard + 1) * rows]
        for number, other in enumerate(others):
            copies.append(
                pltpu.make_async_remote_copy(
                    src_ref=logit_parts.at[other], dst_ref=logit_parts.at[ranks + number], send_sem=send.at[number],
                    recv_sem=recv.at[number], device_id={"tensor": other}, device_id_type=pl.DeviceIdType.MESH,
                )
            )
            copies[-1].start()

    def places(shard):
        slot = lax.broadcasted_iota(jnp.int32, (rows, slots), 1)
        codes = codes_ref[pl.ds(pl.multiple_of(shard * rows, rows), rows), :]
        return jnp.where((slot == codes[:, 0:1]) | (slot == codes[:, 1:2]), 1.0, 0.0).astype(BF16)

    def fill(shard):
        source[shard] = mm(places(shard), back_ref[...]).astype(BF16)

    def side(number):
        if number == ranks:
            router_grad_ref[...] = sum(
                mm(logit_parts[shard].astype(BF16), h_ref[shard * rows : (shard + 1) * rows, :])
                for shard in range(ranks)
            )
            for copy in copies:
                copy.wait()
            logit = logit_parts[rank] + logit_parts[ranks] + logit_parts[ranks + 1] + logit_parts[ranks + 2]
            coarse = logit.astype(BF16)
            logit_own[:EXPERTS] = coarse
            logit_own[EXPERTS:] = (logit - coarse.astype(F32)).astype(BF16)
        elif number > ranks:
            shard = number - ranks - 1
            y_ref[shard] = mm(places(shard), scaled[...]).astype(BF16)
            storing[shard].start()
            if shard == ranks - 1:
                for copy in storing:
                    copy.wait()

    gain_grad_ref[...] = jnp.zeros_like(gain_grad_ref)

    def math(span, total):
        resid, scale = resid_ref[span, :], scale_ref[span, :]
        both = jnp.concatenate([router_ref[...], router_ref[...]], axis=0)
        total = total + mm(logit_own[:, span], both, TN)
        gain_grad_ref[...] += jnp.sum(total * resid * scale, axis=0, keepdims=True)
        grad = norm_back(total, resid, scale, gain_ref[...]) + dy_ref[span, :].astype(F32)
        grad_ref[span, :] = grad
        return grad

    exchange(math, rank, source, full, *rest[:-13], side=side, fill=fill, start=start, later=later)


def norm_one_back_kernel(
    source, x_in, scale_ref, grad_in, gain_ref, y_own, y_across, y_along, gain_one_ref, gain_two_ref, router_ref,
    near_ref, far_ref, full, ready_full, small_out, *rest,
):
    x_ref, grad_ref, held, gathered, near, scale, load, tensor_sends, tensor_recvs, expert_sends, expert_recvs = rest[-11:]
    rank, group = lax.axis_index("tensor"), lax.axis_index("expert")
    pair_class, half_index = rank % 2, rank // 2
    others = rank + 1 - 2 * pair_class, rank + 2 - 4 * half_index
    groups = expert_sends.shape[0]
    mesh_ids = pl.DeviceIdType.MESH
    peers = [partner_of(group, step) for step in range(1, groups)]
    heads = near_ref.shape[0] // 2
    rows = source.shape[1]
    pairs = ((near_ref, near), (x_in, x_ref), (grad_in, grad_ref))
    loading = [pltpu.make_async_copy(*pair, load.at[number]) for number, pair in enumerate(pairs)]

    def math(span, total):
        x = x_ref[span, :].astype(F32)
        return norm_back(total, x, scale[span, :], gain_ref[...]) + grad_ref[span, :]

    def to_rank(step):
        return pltpu.make_async_remote_copy(
            src_ref=held.at[step], dst_ref=held.at[2 + step], send_sem=tensor_sends.at[step],
            recv_sem=tensor_recvs.at[step], device_id={"tensor": others[step]}, device_id_type=mesh_ids,
        )

    def to_group(step):
        return pltpu.make_async_remote_copy(
            src_ref=gathered.at[group], dst_ref=gathered.at[group], send_sem=expert_sends.at[step],
            recv_sem=expert_recvs.at[step], device_id={"expert": peers[step - 1]}, device_id_type=mesh_ids,
        )

    def start():
        for copy in loading:
            copy.start()
        held[0] = jnp.zeros(small_out.shape, F32)
        held[0, :EXPERTS] = router_ref[...]
        held[0, EXPERTS : EXPERTS + 1] = gain_two_ref[...]
        held[0, EXPERTS + 1 : EXPERTS + 2] = gain_one_ref[...]
        to_rank(0).start()

    def side(number):
        if number == 0:
            own_scale = scale_ref[:, pl.ds(pl.multiple_of(rank * rows, rows), rows)]
            scale[...] = jnp.broadcast_to(own_scale, (8, rows)).T[:, :1]
            for copy in loading:
                copy.wait()
            small_out[:BUCKETS, :128] = bias_fold(near, far_ref)
        elif number == 1:
            to_rank(0).wait()
            held[1] = held[0] + held[2]
            to_rank(1).start()
        elif number == 5:
            to_rank(1).wait()
            turned = small_out[:BUCKETS, :128].T
            held[0] = held[1] + held[3]
            held[0, EXPERTS + 2 : EXPERTS + 2 + heads, :BUCKETS] = turned[:heads]
            gathered[group] = held[0].astype(BF16)
            for step in range(1, groups):
                to_group(step).start()
        elif number == 8:
            for step in range(1, groups):
                to_group(step).wait()
            total = gathered[0].astype(F32)
            for step in range(1, groups):
                total = total + gathered[step].astype(F32)
            small_out[...] = total

    exchange(
        math, rank, source, full, *rest[:-11], (y_own, y_across, y_along), ready_full, side=side, peers=peers, start=start
    )


def local_codes(routes_ref, code_ref, pair_class, half_index, half):
    tokens = routes_ref.shape[1]
    expert = lax.broadcasted_iota(jnp.int32, (EXPERTS, BLK), 0)
    earlier = (
        lax.broadcasted_iota(jnp.int32, (BLK, BLK), 0) < lax.broadcasted_iota(jnp.int32, (BLK, BLK), 1)
    ).astype(F32).astype(BF16)
    carry = jnp.zeros((EXPERTS, 1), F32)
    for block in range(tokens // BLK):
        cols = slice(block * BLK, (block + 1) * BLK)
        routes = routes_ref[:, cols]
        hits = [(routes[i : i + 1] == expert) for i in range(TOP)]
        chosen = sum(hit.astype(F32) for hit in hits)
        before = mm(chosen.astype(BF16), earlier) + carry
        carry = carry + jnp.sum(chosen, axis=1, keepdims=True)
        for i in range(TOP):
            slot = jnp.sum(jnp.where(hits[i], before, 0.0), axis=0, keepdims=True).astype(jnp.int32)
            route = routes[i : i + 1]
            owner = route // 2
            local = slot - half_index * half
            mine = (route - 2 * owner == pair_class) & (local >= 0) & (local < half)
            code_ref[i : i + 1, cols] = jnp.where(mine, owner * half + local, -1)


def dispatch_kernel(code_ref, routes_ref, router_ref, h_ref, dy_rows_ref, rows_ref, grads_ref, gate_ref, gates_ref):
    count, tokens = rows_ref.shape[0], h_ref.shape[0]

    @pl.when(pl.program_id(0) == 0)
    def _():
        expert = lax.broadcasted_iota(jnp.int32, (EXPERTS, tokens), 0)
        logits = mm(router_ref[...], h_ref[...], NT)
        picked = [
            jnp.sum(jnp.where(routes_ref[i : i + 1] == expert, logits, 0.0), axis=0, keepdims=True)
            for i in range(TOP)
        ]
        top = jnp.maximum(picked[0], picked[1])
        raised = [jnp.exp(value - top) for value in picked]
        total = raised[0] + raised[1]
        for i in range(TOP):
            gates_ref[i : i + 1] = raised[i] / total

    slot = lax.broadcasted_iota(jnp.int32, (count, tokens), 0) + pl.program_id(0) * count
    hits = [slot == code_ref[i : i + 1, :] for i in range(TOP)]
    take = jnp.where(hits[0] | hits[1], 1.0, 0.0).astype(BF16)
    weighted = jnp.where(hits[0], gates_ref[0:1, :], jnp.where(hits[1], gates_ref[1:2, :], 0.0))
    gate = jnp.sum(weighted, axis=1, keepdims=True)
    rows_ref[...] = mm(take, h_ref[...]).astype(BF16)
    grads_ref[...] = (dy_rows_ref[...].astype(F32) * gate).astype(BF16)
    gate_ref[...] = gate


def dispatch(code, routes_t, router_t, h, dy_rows):
    slots, width = dy_rows.shape
    tile = slots // 4
    row_spec = pl.BlockSpec((tile, width), lambda i: (i, 0))
    whole = lambda shape: pl.BlockSpec(shape, lambda i: (0, 0))
    return pl.pallas_call(
        dispatch_kernel,
        grid=(4,),
        in_specs=[whole(code.shape), whole(code.shape), whole(router_t.shape), whole(h.shape), row_spec],
        out_specs=[row_spec, row_spec, pl.BlockSpec((tile, 1), lambda i: (i, 0)), whole(code.shape)],
        out_shape=[jax.ShapeDtypeStruct((slots, width), BF16)] * 2
        + [jax.ShapeDtypeStruct((slots, 1), F32), jax.ShapeDtypeStruct(code.shape, F32)],
        compiler_params=params(),
        cost_estimate=cost(4 * slots * SEQ * width, 4 * MIB + 6 * slots * width),
    )(code, routes_t, router_t, h, dy_rows)


def gelu_parts(x):
    inner = 0.7978845608028654 * (x + 0.044715 * (x * x * x))
    bend = jnp.tanh(inner)
    half = 0.5 * (1.0 + bend)
    slope = half + 0.5 * x * (1.0 - bend * bend) * (
        0.7978845608028654 * (1.0 + 3.0 * 0.044715 * (x * x))
    )
    return x * half, slope


def partner_of(index, step):
    found = index
    for bit in (1, 2, 4):
        found = found + ((step // bit) % 2) * (1 - 2 * ((index // bit) % 2)) * bit
    return found


def expert_kernel(
    rows_in, grads_in, gate_in, up_in, down_in, far_gate,
    ret_out, back_out, own_gate, own_up, own_down, got_gate, got_up, got_down,
    rows, grads, weights, sums, parts, z_send, z_recv, y_send, y_recv, p_send, p_recv, r_send, r_recv, w_send, w_recv, g_send, g_recv, local,
):
    groups, half, width = rows.shape[1:]
    group, rank = lax.axis_index("expert"), lax.axis_index("tensor")
    pair_class, half_index = rank % 2, rank // 2
    across = {"tensor": rank + 1 - 2 * pair_class}
    along = {"tensor": rank + 2 - 4 * half_index}
    mesh_ids = pl.DeviceIdType.MESH
    moved = ((rows_in, rows, ret_out), (grads_in, grads, back_out))

    barrier = pltpu.get_barrier_semaphore()
    for step in range(1, groups):
        pl.semaphore_signal(
            barrier, inc=1, device_id={"expert": partner_of(group, step)}, device_id_type=mesh_ids
        )
    pl.semaphore_signal(barrier, inc=1, device_id=across, device_id_type=mesh_ids)
    pl.semaphore_signal(barrier, inc=1, device_id=along, device_id_type=mesh_ids)
    pl.semaphore_wait(barrier, groups + 1)

    def remote(source, target, send, recv, device):
        return pltpu.make_async_remote_copy(
            src_ref=source, dst_ref=target, send_sem=send, recv_sem=recv,
            device_id=device, device_id_type=mesh_ids,
        )

    def block(ref, number):
        return ref.at[pl.ds(pl.multiple_of(number * half, half), half)]

    def out_of(kind, step):
        source, held, _ = moved[kind]
        other = partner_of(group, step)
        return remote(
            block(source, other), held.at[0, group], z_send.at[kind, step], z_recv.at[kind, step], {"expert": other}
        )

    def forward(kind, step):
        held = moved[kind][1]
        other = partner_of(group, step)
        return remote(held.at[0, other], held.at[1, other], y_send.at[kind, step], y_recv.at[kind, step], along)

    def partial_sum(kind, step):
        held = moved[kind][1]
        other = partner_of(group, step)
        return remote(held.at[1, other], parts.at[kind, other], p_send.at[kind, step], p_recv.at[kind, step], along)

    def result(kind, step):
        other = partner_of(group, step)
        return remote(
            parts.at[kind, other], block(moved[kind][2], group), r_send.at[kind, step], r_recv.at[kind, step], {"expert": other}
        )

    def own_result(kind):
        return pltpu.make_async_copy(parts.at[kind, group], block(moved[kind][2], group), local.at[kind])

    own = [
        pltpu.make_async_copy(block(moved[kind][0], group), moved[kind][1].at[0, group], local.at[kind])
        for kind in range(2)
    ]
    for copy in own:
        copy.start()
    kept = [
        pltpu.make_async_copy(ref.at[pair_class], weights.at[number, 0], local.at[2 + number])
        for number, ref in enumerate((gate_in, up_in, down_in))
    ]
    kept.append(pltpu.make_async_copy(far_gate, weights.at[0, 1], local.at[5]))
    kept += [
        remote(ref.at[1 - pair_class], weights.at[number, 1], w_send.at[number - 1], w_recv.at[number - 1], across)
        for number, ref in ((1, up_in), (2, down_in))
    ]
    for copy in kept:
        copy.start()
    for step in range(1, groups):
        for kind in range(2):
            out_of(kind, step).start()

    def arrive(step):
        for kind in range(2):
            out_of(kind, step).wait()
            forward(kind, step).start()

    def give(step):
        for kind in range(2):
            partial_sum(kind, step).start()

    for number in range(3):
        for part in range(2):
            sums[number, part] = jnp.zeros(sums.shape[2:], F32)

    def finish(step):
        other = partner_of(group, step)
        for kind in range(2):
            partial_sum(kind, step).wait()
            held = moved[kind][1]
            parts[kind, other] = (parts[kind, other].astype(F32) + held[0, other].astype(F32)).astype(BF16)

        for kind in range(2):
            if step == 0:
                own_result(kind).start()
            else:
                result(kind, step).start()

    def act(plan):
        for action, step in plan:
            action(step)

    order = (0, 1, 4, 5, 2, 6, 3, 7)
    before = {
        0: [(arrive, 1), (arrive, 2), (arrive, 3), (arrive, 4)],
        1: [(give, 0)],
        2: [(arrive, 5)],
        3: [(give, 4), (finish, 0)],
        4: [(arrive, 6)],
        5: [(give, 5), (finish, 4)],
        6: [(arrive, 7)],
        7: [(give, 6), (finish, 5)],
    }
    ahead = [(give, 7)]
    last = [(give, 2), (finish, 6), (give, 3), (finish, 7), (give, 1), (finish, 2), (finish, 3), (finish, 1)]
    for copy in own:
        copy.wait()
    for kind in range(2):
        forward(kind, 0).start()

    def body(turn, carry):
        for number, plan in before.items():
            pl.when(turn == number)(partial(act, plan))

        @pl.when(turn == 0)
        def _():
            for copy in kept:
                copy.wait()

        step = sum((turn == number).astype(jnp.int32) * which for number, which in enumerate(order))
        for kind in range(2):
            forward(kind, step).wait()
        other = partner_of(group, step)
        tile = jnp.concatenate([rows[0, other], rows[1, other]], axis=0)
        grad = jnp.concatenate([grads[0, other], grads[1, other]], axis=0)
        ret = jnp.zeros(tile.shape, F32)
        back = jnp.zeros(tile.shape, F32)
        for part in range(2):
            w_gate, w_up, w_down = weights[0, part], weights[1, part], weights[2, part]
            gate_part = mm(tile, w_gate, NT)
            up_part = mm(tile, w_up, NT)
            grad_hidden = mm(grad, w_down, NT)
            bent, slope = gelu_parts(gate_part)
            hidden = (bent * up_part).astype(BF16)
            grad_gate = (grad_hidden * up_part * slope).astype(BF16)
            grad_up = (grad_hidden * bent).astype(BF16)
            ret = ret + mm(hidden, w_down)
            back = back + mm(grad_gate, w_gate) + mm(grad_up, w_up)
            sums[0, part] += mm(grad_gate, tile, TN)
            sums[1, part] += mm(grad_up, tile, TN)
            sums[2, part] += mm(hidden, grad, TN)
        for kind, value in enumerate((ret, back)):
            held = moved[kind][1]
            held[0, other] = value[:half].astype(BF16)
            held[1, other] = value[half:].astype(BF16)

        return carry

    lax.fori_loop(0, groups, body, 0)
    act(ahead)
    copies = []
    for number, (own_ref, got_ref) in enumerate(((own_gate, got_gate), (own_up, got_up), (own_down, got_down))):
        weights[number, 0] = sums[number, 1].astype(BF16)
        copies.append(remote(weights.at[number, 0], got_ref, g_send.at[number], g_recv.at[number], across))
        copies[-1].start()
        copies.append(pltpu.make_async_copy(sums.at[number, 0], own_ref, local.at[2 + number]))
        copies[-1].start()
    act(last)
    for copy in copies:
        copy.wait()
    for kind in range(2):
        own_result(kind).wait()
        for step in range(1, groups):
            result(kind, step).wait()


def run_experts(rows, grads, w_gate, w_up, w_down, far_gate):
    slots, width = rows.shape
    half = CAP // 2
    groups = slots // half
    units = w_gate.shape[1]
    anywhere = pl.BlockSpec(memory_space=pl.ANY)
    pair = pltpu.SemaphoreType.DMA((2, groups))
    return pl.pallas_call(
        expert_kernel,
        in_specs=[anywhere] * 6,
        out_specs=[anywhere] * 8,
        out_shape=[jax.ShapeDtypeStruct((slots, width), BF16)] * 2
        + [jax.ShapeDtypeStruct((units, width), F32)] * 3
        + [jax.ShapeDtypeStruct((units, width), BF16)] * 3,
        scratch_shapes=[
            pltpu.VMEM((2, groups, half, width), BF16),
            pltpu.VMEM((2, groups, half, width), BF16),
            pltpu.VMEM((3, 2, units, width), BF16),
            pltpu.VMEM((3, 2, units, width), F32),
            pltpu.VMEM((2, groups, half, width), BF16),
        ]
        + [pair] * 8
        + [pltpu.SemaphoreType.DMA((2,))] * 2
        + [pltpu.SemaphoreType.DMA((3,))] * 2
        + [pltpu.SemaphoreType.DMA((6,))],
        compiler_params=pltpu.CompilerParams(
            vmem_limit_bytes=60 * MIB, collective_id=1, has_side_effects=True
        ),
        cost_estimate=cost(72 * slots * units * width, 16 * slots * width + 30 * units * width),
    )(rows, grads, w_gate, w_up, w_down, far_gate)


def finish_kernel(
    rows_ref, y_ref, summed_ref, small_ref,
    output_ref, grad_ref, in_ref, out_ref, one_ref, two_ref, router_ref, bias_ref,
):
    step = pl.program_id(0)
    output_ref[...] = y_ref[...].astype(F32).T.astype(BF16)
    grad_ref[...] = rows_ref[...].astype(F32).T

    @pl.when(step < 3)
    def _():
        in_ref[...] = summed_ref[...].astype(F32)

    @pl.when(step == 3)
    def _():
        out_ref[...] = summed_ref[...].astype(F32)
        router_ref[...] = small_ref[:EXPERTS]
        two_ref[...] = small_ref[EXPERTS : EXPERTS + 1]
        one_ref[...] = small_ref[EXPERTS + 1 : EXPERTS + 2]
        bias_ref[...] = small_ref[EXPERTS + 2 : EXPERTS + 2 + bias_ref.shape[0], :BUCKETS]


def finish_outputs(rows, y_rows, summed, small, heads):
    tokens, width = rows.shape
    steps = 4
    tile, block = tokens // steps, summed.shape[0] // steps
    token_spec = pl.BlockSpec((tile, width), lambda i: (i, 0))
    feature_spec = pl.BlockSpec((width, tile), lambda i: (0, i))
    whole = lambda *shape: pl.BlockSpec(shape, lambda i: (0, 0))
    return pl.pallas_call(
        finish_kernel,
        grid=(steps,),
        in_specs=[
            token_spec,
            token_spec,
            pl.BlockSpec((block, width), lambda i: (i, 0)),
            whole(*small.shape),
        ],
        out_specs=[
            feature_spec,
            feature_spec,
            pl.BlockSpec((block, width), lambda i: (jnp.minimum(i, 2), 0)),
            whole(block, width),
            whole(1, width),
            whole(1, width),
            whole(EXPERTS, width),
            whole(heads, BUCKETS),
        ],
        out_shape=[
            jax.ShapeDtypeStruct((width, tokens), BF16),
            jax.ShapeDtypeStruct((width, tokens), F32),
            jax.ShapeDtypeStruct((3 * block, width), F32),
            jax.ShapeDtypeStruct((block, width), F32),
            jax.ShapeDtypeStruct((1, width), F32),
            jax.ShapeDtypeStruct((1, width), F32),
            jax.ShapeDtypeStruct((EXPERTS, width), F32),
            jax.ShapeDtypeStruct((heads, BUCKETS), F32),
        ],
        compiler_params=params(),
        cost_estimate=cost(0, 10 * rows.size + 6 * summed.size),
    )(rows, y_rows, summed, small)


def on_device(
    layer_input, gain_one, attn_in, rel_bias, attn_out, gain_two, router,
    expert_gate, expert_up, expert_down, routes, piece_starts, grad_out,
):
    width, tokens = layer_input.shape
    ranks = lax.axis_size("tensor")
    groups = lax.axis_size("expert")
    rank = lax.axis_index("tensor")
    pair_class, half_index = rank % 2, rank // 2
    half = CAP // 2

    def trade(weights):
        other = lax.dynamic_index_in_dim(weights, 1 - pair_class, 0, keepdims=False)
        return lax.ppermute(other, "tensor", [(r, r ^ 1) for r in range(ranks)])

    traded = trade(expert_gate)
    gain_col = gain_one[:, None]
    w_in = attn_in.reshape(-1, width)
    qkv, scale_one = project(layer_input, gain_col, w_in)
    tiles = bias_tiles(rel_bias)
    position = jnp.arange(SEQ, dtype=jnp.int32)[None, None, :]
    starts = piece_starts[:, :, None]
    inside = (position >= starts) & (position < starts + PIECE)
    last = jnp.max(jnp.where(inside, starts + (PIECE - 1), -1), axis=1)
    limits = jnp.maximum(last, position[0])[:, None, :]

    routes_t = routes.T
    place = jnp.stack([pair_class, half_index]).astype(jnp.int32)
    share = tokens // ranks

    def by_rank(rows):
        return rows.reshape(ranks, share, width)

    mixed, lse, sent = attend(qkv, tiles, limits, attn_out)
    sent, traded = lax.optimization_barrier((sent, traded))
    slots = groups * half
    h2, resid, scale_two, dy, dy_rows, code, code_cols, own_x = exchange_call(
        norm_two_kernel, 2, sent.shape, [by_rank(sent), layer_input, gain_two[None], grad_out, routes_t],
        [((share, width), F32), ((share, 1), F32), ((tokens, width), BF16), ((slots, width), BF16)]
        + [((TOP, tokens), jnp.int32), ((tokens, TOP), jnp.int32), ((share, width), BF16)],
        [pltpu.VMEM((width, share), BF16), pltpu.VMEM((width, tokens), BF16), pltpu.VMEM((tokens, width), BF16)]
        + [pltpu.VMEM((slots, width), BF16), pltpu.SemaphoreType.DMA((4,))],
        (1, 3),
        (2, 3),
    )
    rows, row_grads, gate_rows, gates = dispatch(code, routes_t, router.T, h2, dy_rows)
    ret, back, *weight_grads = run_experts(
        rows, row_grads, expert_gate, expert_up, expert_down, traded
    )
    grad_attn, grad_resid, grad_gain_two, grad_router, partial_y = exchange_call(
        norm_two_back_kernel, 3, (tokens, width),
        [ret, back, code, code_cols, gates, routes_t, dy_rows, gate_rows, router.T, h2]
        + [resid, scale_two, dy, gain_two[None]],
        [((share, width), F32), ((1, width), F32), ((EXPERTS, width), F32), ((tokens, width), BF16)],
        [
            pltpu.VMEM((ranks, share, width), BF16),
            pltpu.VMEM((slots, width), BF16),
            pltpu.VMEM((ranks + 3, EXPERTS, share), F32),
            pltpu.VMEM((2 * EXPERTS, share), BF16),
        ]
        + [pltpu.SemaphoreType.DMA((3,))] * 2
        + [pltpu.VMEM((slots, width), BF16)] * 2
        + [pltpu.VMEM((tokens, width), BF16), pltpu.VMEM((share, width), F32), pltpu.VMEM((share, width), BF16)]
        + [pltpu.VMEM((ranks, share, width), BF16), pltpu.SemaphoreType.DMA((9,))],
        (0, 6, 9, 10, 12),
        (3,),
    )

    dq, dk, dv, near, far, y_own = attend_back(
        qkv, tiles, limits, attn_out, grad_attn, lse, by_rank(partial_y), resid
    )
    dq, y_own = lax.optimization_barrier((dq, y_own))
    y_across = lax.ppermute(y_own, "tensor", [(r, r ^ 1) for r in range(ranks)])
    y_along = lax.ppermute(y_own, "tensor", [(r, r ^ 2) for r in range(ranks)])
    weight_rows, sent, grad_gain_one, grad_gate, grad_up, grad_down = project_back(
        place, layer_input, gain_col, gain_one[None], scale_one, w_in, mixed, grad_attn, (dq, dk, dv),
        weight_grads[:3], weight_grads[3:],
    )
    sent, y_across, y_along = lax.optimization_barrier((sent, y_across, y_along))
    summed = lax.psum(weight_rows, "expert")
    small_shape = (BUCKETS, width)
    grad_rows, y_full, small = exchange_call(
        norm_one_back_kernel, 4, sent.shape,
        [by_rank(sent), own_x, scale_one, grad_resid, gain_one[None], y_own, y_across, y_along]
        + [grad_gain_one, grad_gain_two, grad_router, near, far],
        [((ranks, share, width), BF16), (small_shape, F32)],
        [pltpu.VMEM((share, width), BF16), pltpu.VMEM((share, width), F32)]
        + [pltpu.VMEM((4, *small_shape), F32), pltpu.VMEM((groups, *small_shape), BF16), pltpu.VMEM(near.shape, F32), pltpu.VMEM((share, 1), F32)]
        + [pltpu.SemaphoreType.DMA((3,))]
        + [pltpu.SemaphoreType.DMA((2,))] * 2
        + [pltpu.SemaphoreType.DMA((groups,))] * 2,
        (1, 3, 11),
        (0,),
    )
    summed, grad_rows = lax.optimization_barrier((summed, grad_rows))
    layer_output, grad_input, grad_in, grad_attn_out, grad_one, grad_two, grad_router, grad_bias = finish_outputs(
        grad_rows, y_full.reshape(tokens, width), summed, small, rel_bias.shape[1]
    )
    return (
        layer_output,
        grad_input,
        grad_one[0],
        grad_in.reshape(attn_in.shape),
        grad_bias.T,
        grad_attn_out,
        grad_two[0],
        grad_router.T,
        grad_gate,
        grad_up,
        grad_down,
    )


def allowed_pairs(seq_starts):
    position = jnp.arange(SEQ, dtype=jnp.int32)
    inside = (position[:, None] >= seq_starts[None, :]) & (
        position[:, None] < seq_starts[None, :] + PIECE
    )
    numbers = jnp.arange(seq_starts.shape[0], dtype=jnp.int32) + 1
    piece_label = jnp.sum(inside.astype(jnp.int32) * numbers[None, :], axis=1)
    causal = position[None, :] <= position[:, None]
    shared = (piece_label[:, None] == piece_label[None, :]) & (piece_label[:, None] > 0)
    return causal | shared


def slot_table(routes):
    flat_routes = routes.reshape(-1)
    onehot = (flat_routes[:, None] == jnp.arange(EXPERTS, dtype=jnp.int32)[None, :]).astype(
        jnp.int32
    )
    blocks = onehot.reshape(-1, 128, EXPERTS).astype(F32)
    earlier = jnp.tril(jnp.ones((128, 128), F32), -1)
    inside = jnp.einsum("ij,bje->bie", earlier, blocks)
    count = blocks.shape[0]
    carried = jnp.einsum("ab,be->ae", jnp.tril(jnp.ones((count, count), F32), -1), jnp.sum(blocks, axis=1), precision=HIGH)
    before = (inside + carried[:, None, :]).astype(jnp.int32).reshape(onehot.shape)
    slot_number = jnp.sum(before * onehot, axis=1)
    kept_pairs = slot_number < CAP
    slot_index = jnp.where(kept_pairs, flat_routes * CAP + slot_number, EXPERTS * CAP)
    return (slot_index.reshape(routes.shape), kept_pairs.reshape(routes.shape))


def bucket_onehot():
    offsets = jnp.arange(2 * SEQ - 1, dtype=jnp.int32) - (SEQ - 1)
    return (bucket_of(offsets)[:, None] == jnp.arange(BUCKETS, dtype=jnp.int32)[None, :]).astype(
        jnp.float32
    )


def expand_line(line):
    head_count = line.shape[0]
    padded = jnp.concatenate([line, jnp.zeros((head_count, 1), line.dtype)], axis=1)
    tiled = jnp.tile(padded, (1, SEQ))[:, : SEQ * (2 * SEQ - 1)].reshape(
        head_count, SEQ, 2 * SEQ - 1
    )
    return tiled[:, :, SEQ - 1 :]


def fold_line(full_grid):
    head_count = full_grid.shape[0]
    padded = jnp.pad(full_grid, ((0, 0), (0, 0), (SEQ - 1, 0))).reshape(
        head_count, SEQ * (2 * SEQ - 1)
    )
    padded = jnp.pad(padded, ((0, 0), (0, SEQ))).reshape(head_count, SEQ, 2 * SEQ)
    return jnp.sum(padded, axis=1)[:, : 2 * SEQ - 1]


def reduce_heads(tensor_value):
    return lax.psum(tensor_value, "tensor")


def spread_slots(tensor_value):
    return lax.all_gather(tensor_value, "tensor", axis=2, tiled=True)


def owner_exchange(tensor_value):
    return lax.all_to_all(tensor_value, "expert", split_axis=0, concat_axis=0, tiled=True)


def expert_sums(tensor_value):
    return lax.psum_scatter(tensor_value, "tensor", scatter_dimension=2, tiled=True)


def norm_forward(resid, gain, model_width):
    scale = lax.rsqrt(jnp.sum(resid * resid, axis=1) / model_width + EPS)[:, None]
    return (scale, (resid * scale * gain).astype(jnp.bfloat16))


def norm_backward(resid, scale, gain, grad_normed, model_width):
    grad_gain = jnp.sum(grad_normed * resid * scale, axis=0)
    scaled = grad_normed * gain
    inner = jnp.sum(scaled * resid, axis=1)[:, None]
    return (grad_gain, scale * scaled - resid * scale**3 * inner / model_width)


def attend_scores(bias_full, queries, key_rows, seq_starts):
    scores = (
        jnp.einsum("qhe,khe->hqk", queries, key_rows, preferred_element_type=jnp.float32) * 0.125
        + bias_full
    )
    return jnp.where(allowed_pairs(seq_starts)[None], scores, NEG)


def attend_forward(bias_full, inputs):
    queries, key_rows, value_rows, seq_starts = inputs
    scores = attend_scores(bias_full, queries, key_rows, seq_starts)
    row_max = jnp.max(scores, axis=2, keepdims=True)
    exponent = jnp.exp(scores - row_max)
    row_sum_exp = jnp.sum(exponent, axis=2, keepdims=True)
    weights = (exponent / row_sum_exp).astype(jnp.bfloat16)
    mixed_heads = jnp.einsum(
        "hqk,khe->qhe", weights, value_rows, preferred_element_type=jnp.float32
    )
    return (mixed_heads.astype(jnp.bfloat16), (row_max + jnp.log(row_sum_exp))[:, :, 0])


def attend_backward(bias_full, running, inputs):
    queries, key_rows, value_rows, grad_heads, seq_starts, log_total = inputs
    scores = attend_scores(bias_full, queries, key_rows, seq_starts)
    probabilities = jnp.exp(scores - log_total[:, :, None])
    grad_probs = jnp.einsum(
        "qhe,khe->hqk", grad_heads, value_rows, preferred_element_type=jnp.float32
    )
    inner = jnp.sum(probabilities * grad_probs, axis=2, keepdims=True)
    grad_scores = (probabilities * (grad_probs - inner)).astype(jnp.bfloat16)
    grad_values = jnp.einsum(
        "hqk,qhe->khe",
        probabilities.astype(jnp.bfloat16),
        grad_heads,
        preferred_element_type=jnp.float32,
    )
    grad_queries = (
        jnp.einsum("hqk,khe->qhe", grad_scores, key_rows, preferred_element_type=jnp.float32)
        * 0.125
    )
    grad_keys = (
        jnp.einsum("hqk,qhe->khe", grad_scores, queries, preferred_element_type=jnp.float32) * 0.125
    )
    return (
        running + grad_scores.astype(jnp.float32),
        jnp.stack([grad_queries, grad_keys, grad_values]),
    )


def gelu_product(left, right):
    return jax.nn.gelu(left, approximate=True) * right


def expert_forward(received, weight_gate, weight_up, weight_down):
    gate_part = jnp.einsum(
        "secd,efd->secf", received, weight_gate, preferred_element_type=jnp.float32
    )
    up_part = jnp.einsum("secd,efd->secf", received, weight_up, preferred_element_type=jnp.float32)
    hidden = gelu_product(gate_part, up_part).astype(jnp.bfloat16)
    partial_out = jnp.einsum(
        "secf,efd->secd", hidden, weight_down, preferred_element_type=jnp.float32
    )
    return (gate_part, up_part, hidden, partial_out)


def expert_backward(
    received, gate_part, up_part, hidden, grad_rows_out, weight_gate, weight_up, weight_down
):
    grad_hidden = jnp.einsum(
        "secd,efd->secf", grad_rows_out, weight_down, preferred_element_type=jnp.float32
    )
    product_value, pullback = jax.vjp(gelu_product, gate_part, up_part)
    grad_gate_part, grad_up_part = pullback(grad_hidden)
    grad_gate_part = grad_gate_part.astype(jnp.bfloat16)
    grad_up_part = grad_up_part.astype(jnp.bfloat16)
    grad_down = jnp.einsum(
        "secf,secd->efd", hidden, grad_rows_out, preferred_element_type=jnp.float32
    )
    grad_gate_w = jnp.einsum(
        "secf,secd->efd", grad_gate_part, received, preferred_element_type=jnp.float32
    )
    grad_up_w = jnp.einsum(
        "secf,secd->efd", grad_up_part, received, preferred_element_type=jnp.float32
    )
    grad_rows_in = jnp.einsum(
        "secf,efd->secd", grad_gate_part, weight_gate, preferred_element_type=jnp.float32
    )
    grad_rows_in = grad_rows_in + jnp.einsum(
        "secf,efd->secd", grad_up_part, weight_up, preferred_element_type=jnp.float32
    )
    return (grad_gate_w, grad_up_w, grad_down, grad_rows_in)


def on_device_general(
    layer_input,
    gain_one,
    attn_in,
    rel_bias,
    attn_out,
    gain_two,
    router,
    expert_gate,
    expert_up,
    expert_down,
    routes,
    piece_starts,
    grad_out,
):
    tok_count = layer_input.shape[1]
    model_width = layer_input.shape[0]
    heads_here = rel_bias.shape[1]
    head_width = attn_in.shape[1] // heads_here
    seqs_here = piece_starts.shape[0]
    local_experts = expert_gate.shape[0]
    part_rows = CAP // lax.axis_size("tensor")
    share_start = lax.axis_index("tensor") * part_rows
    tokens = layer_input.T.astype(jnp.float32)
    scale_one, normed = norm_forward(tokens, gain_one, model_width)
    project = jnp.einsum("td,chd->cth", normed, attn_in, preferred_element_type=jnp.float32).astype(
        jnp.bfloat16
    )
    by_seq = project.reshape(3, seqs_here, SEQ, heads_here, head_width)
    onehot_line = bucket_onehot()
    bias_full = expand_line(jnp.dot(onehot_line, rel_bias, precision=HIGH).T)
    mixed_heads, log_total = lax.map(
        partial(attend_forward, bias_full), (by_seq[0], by_seq[1], by_seq[2], piece_starts)
    )
    mixed_heads = mixed_heads.reshape(tok_count, heads_here * head_width)
    resid = tokens + reduce_heads(
        jnp.dot(mixed_heads, attn_out, preferred_element_type=jnp.float32)
    )
    scale_two, normed_two = norm_forward(resid, gain_two, model_width)
    logits = jnp.dot(normed_two, router, preferred_element_type=jnp.float32)
    chosen = (routes[:, :, None] == jnp.arange(EXPERTS, dtype=jnp.int32)[None, None, :]).astype(
        jnp.float32
    )
    picked = jnp.sum(chosen * logits[:, None, :], axis=2)
    gate_weights = jax.nn.softmax(picked, axis=1)
    slot_index, kept_pairs = slot_table(routes)
    keep_float = kept_pairs.astype(jnp.float32)
    mix_weight = gate_weights * keep_float
    safe_index = jnp.minimum(slot_index, EXPERTS * CAP - 1)
    token_rows = jnp.repeat(normed_two, TOP, axis=0)
    buffer = (
        jnp.zeros((EXPERTS * CAP + 1, model_width), jnp.bfloat16)
        .at[slot_index.reshape(-1)]
        .set(token_rows)
    )
    buffer = buffer[: EXPERTS * CAP].reshape(-1, local_experts, CAP, model_width)
    received = lax.all_to_all(buffer, "expert", split_axis=0, concat_axis=0, tiled=True)
    gate_part, up_part, hidden, partial_out = expert_forward(
        received, expert_gate, expert_up, expert_down
    )
    returned = spread_slots(owner_exchange(expert_sums(partial_out).astype(jnp.bfloat16)))
    flat_ret = returned.reshape(EXPERTS * CAP, model_width)
    fetched = flat_ret[safe_index].astype(jnp.float32)
    output = resid + jnp.sum(mix_weight[:, :, None] * fetched, axis=1)
    grad_y = grad_out.T.astype(jnp.float32)
    grad_gates = jnp.sum(grad_y[:, None, :] * fetched, axis=2) * keep_float
    grad_picked = gate_weights * (
        grad_gates - jnp.sum(gate_weights * grad_gates, axis=1, keepdims=True)
    )
    grad_logits = jnp.sum(chosen * grad_picked[:, :, None], axis=1)
    grad_router = jnp.dot(normed_two.astype(jnp.float32).T, grad_logits, precision=HIGH)
    grad_normed_two = jnp.dot(grad_logits, router.astype(jnp.float32).T, precision=HIGH)
    slot_grads = (mix_weight[:, :, None] * grad_y[:, None, :]).astype(jnp.bfloat16)
    grad_ret = (
        jnp.zeros((EXPERTS * CAP + 1, model_width), jnp.bfloat16)
        .at[slot_index.reshape(-1)]
        .set(slot_grads.reshape(-1, model_width))
    )
    grad_ret = grad_ret[: EXPERTS * CAP].reshape(-1, local_experts, CAP, model_width)
    grad_share = lax.dynamic_slice_in_dim(grad_ret, share_start, part_rows, 2)
    grad_rows_out = spread_slots(owner_exchange(grad_share))
    grad_expert_gate, grad_expert_up, grad_expert_down, grad_rows_in = expert_backward(
        received, gate_part, up_part, hidden, grad_rows_out, expert_gate, expert_up, expert_down
    )
    grad_back = spread_slots(owner_exchange(expert_sums(grad_rows_in).astype(jnp.bfloat16)))
    flat_back = grad_back.reshape(EXPERTS * CAP, model_width).astype(jnp.float32)
    grad_normed_two = grad_normed_two + jnp.sum(
        flat_back[safe_index] * keep_float[:, :, None], axis=1
    )
    grad_gain_two, grad_resid = norm_backward(
        resid, scale_two, gain_two, grad_normed_two, model_width
    )
    grad_resid = grad_resid + grad_y
    grad_attn = grad_resid.astype(jnp.bfloat16)
    grad_attn_out = jnp.einsum(
        "th,td->hd", mixed_heads, grad_attn, preferred_element_type=jnp.float32
    )
    grad_mixed = jnp.einsum(
        "td,hd->th", grad_attn, attn_out, preferred_element_type=jnp.float32
    ).astype(jnp.bfloat16)
    grad_by_seq = grad_mixed.reshape(seqs_here, SEQ, heads_here, head_width)
    bias_grad_full, grad_project = lax.scan(
        partial(attend_backward, bias_full),
        jnp.zeros_like(bias_full),
        (by_seq[0], by_seq[1], by_seq[2], grad_by_seq, piece_starts, log_total),
    )
    grad_project = (
        jnp.moveaxis(grad_project, 1, 0)
        .reshape(3, tok_count, heads_here * head_width)
        .astype(jnp.bfloat16)
    )
    grad_attn_in = jnp.einsum(
        "cth,td->chd", grad_project, normed, preferred_element_type=jnp.float32
    )
    grad_normed = reduce_heads(
        jnp.einsum("cth,chd->td", grad_project, attn_in, preferred_element_type=jnp.float32)
    )
    grad_gain_one, grad_tokens = norm_backward(
        tokens, scale_one, gain_one, grad_normed, model_width
    )
    grad_tokens = grad_tokens + grad_resid
    grad_rel_bias = jnp.dot(onehot_line.T, fold_line(bias_grad_full).T, precision=HIGH)
    shared = (
        lax.psum(grad_gain_one.astype(jnp.bfloat16), "expert").astype(jnp.float32),
        lax.psum(grad_attn_in.astype(jnp.bfloat16), "expert").astype(jnp.float32),
        lax.psum(grad_rel_bias.astype(jnp.bfloat16), "expert").astype(jnp.float32),
        lax.psum(grad_attn_out.astype(jnp.bfloat16), "expert").astype(jnp.float32),
        lax.psum(grad_gain_two.astype(jnp.bfloat16), "expert").astype(jnp.float32),
        lax.psum(grad_router.astype(jnp.bfloat16), "expert").astype(jnp.float32),
    )
    return (
        output.astype(jnp.bfloat16).T,
        grad_tokens.T,
        shared[0],
        shared[1],
        shared[2],
        shared[3],
        shared[4],
        shared[5],
        grad_expert_gate,
        grad_expert_up,
        grad_expert_down,
    )


def solution(mesh):
    placed = (
        P(None, "expert"),
        P(),
        P(None, "tensor", None),
        P(None, "tensor"),
        P("tensor", None),
        P(),
        P(),
        P("expert", "tensor", None),
        P("expert", "tensor", None),
        P("expert", "tensor", None),
        P("expert", None),
        P("expert", None),
        P(None, "expert"),
    )
    paired = mesh.shape["tensor"] == 4 and mesh.shape["expert"] * 2 == EXPERTS
    return jax.shard_map(
        on_device if paired else on_device_general,
        mesh=mesh,
        in_specs=placed,
        out_specs=(
            P(None, "expert"),
            P(None, "expert"),
            P(),
            P(None, "tensor", None),
            P(None, "tensor"),
            P("tensor", None),
            P(),
            P(),
            P("expert", "tensor", None),
            P("expert", "tensor", None),
            P("expert", "tensor", None),
        ),
        check_vma=False,
    )
```

```python
from functools import partial

import jax
import jax.numpy as jnp
from jax import lax
from jax.experimental import pallas as pl
from jax.experimental.pallas import tpu as pltpu
from jax.sharding import PartitionSpec as P

EXPERTS = 16
BUCKETS = 32
TOP = 2
PIECE = 256
SEQ = 1024
CAP = 320
BLK = 256


EPS = 1e-06
NEG = -1e30
THRESHOLDS = (12, 16, 23, 32, 46, 64, 91)
HIGH = lax.Precision.HIGHEST
F32 = jnp.float32
BF16 = jnp.bfloat16
NN = (((1,), (0,)), ((), ()))
NT = (((1,), (1,)), ((), ()))
TN = (((0,), (0,)), ((), ()))
MIB = 1 << 20


def mm(left, right, dims=NN):
    return lax.dot_general(left, right, dims, preferred_element_type=F32)


def params(limit=56):
    return pltpu.CompilerParams(vmem_limit_bytes=limit * MIB)


def cost(flops, bytes_accessed, transcendentals=0):
    return pl.CostEstimate(
        flops=int(flops), bytes_accessed=int(bytes_accessed), transcendentals=int(transcendentals)
    )


def bucket_of(offset):
    magnitude = jnp.abs(offset)
    beyond = sum(((magnitude >= threshold).astype(jnp.int32) for threshold in THRESHOLDS))
    lower_part = jnp.where(magnitude < 8, magnitude, 8 + beyond)
    return lower_part + 16 * (offset > 0).astype(jnp.int32)


def project_kernel(x_ref, gain_ref, w_ref, out_ref, scale_ref):
    x = x_ref[...].astype(F32)
    scale = lax.rsqrt(jnp.sum(x * x, axis=0, keepdims=True) / x.shape[0] + EPS)
    normed = (x * scale * gain_ref[...]).astype(BF16)
    out_ref[...] = mm(w_ref[...], normed).astype(BF16)
    scale_ref[...] = scale


def project(x, gain, weights):
    width, tokens = x.shape
    rows = weights.shape[0]
    tile = 512
    return pl.pallas_call(
        project_kernel,
        grid=(tokens // tile,),
        in_specs=[
            pl.BlockSpec((width, tile), lambda i: (0, i)),
            pl.BlockSpec((width, 1), lambda i: (0, 0)),
            pl.BlockSpec((rows, width), lambda i: (0, 0)),
        ],
        out_specs=[
            pl.BlockSpec((rows, tile), lambda i: (0, i)),
            pl.BlockSpec((1, tile), lambda i: (0, i)),
        ],
        out_shape=[
            jax.ShapeDtypeStruct((rows, tokens), BF16),
            jax.ShapeDtypeStruct((1, tokens), F32),
        ],
        compiler_params=params(),
        cost_estimate=cost(2 * width * tokens * rows, 2 * width * tokens * 2),
    )(x, gain, weights)


def line_offsets(number):
    column = lax.broadcasted_iota(jnp.int32, (8, BLK), 1)
    return (number - 1) * BLK - column


def bias_tiles_kernel(table_ref, tiles_ref):
    row = lax.broadcasted_iota(jnp.int32, (BLK, BLK), 0)
    column = lax.broadcasted_iota(jnp.int32, (BLK, BLK), 1)
    buckets = [bucket_of(line_offsets(number)) for number in range(4)]
    for head in range(tiles_ref.shape[0]):
        far = table_ref[15, head]
        rolled = []
        for number, bucket in enumerate(buckets):
            value = jnp.zeros((8, BLK), F32)
            for index in range(BUCKETS):
                value = jnp.where(bucket == index, table_ref[index, head] - far, value)
            whole = jnp.broadcast_to(value[0:1], (BLK, BLK))
            rolled.append(pltpu.roll(whole, 0, 1, stride=1, stride_axis=0))
        for number in range(3):
            tiles_ref[head, number] = jnp.where(column >= row, rolled[number], rolled[number + 1])


def bias_tiles(table):
    heads = table.shape[1]
    return pl.pallas_call(
        bias_tiles_kernel,
        in_specs=[pl.BlockSpec(memory_space=pltpu.SMEM)],
        out_specs=pl.BlockSpec(memory_space=pltpu.VMEM),
        out_shape=jax.ShapeDtypeStruct((heads, 3, BLK, BLK), F32),
        compiler_params=params(),
        cost_estimate=cost(heads * 3 * BLK * BLK * 60, heads * 3 * BLK * BLK * 4),
    )(table)


def bias_fold(near_ref, far_ref):
    heads = near_ref.shape[0] // 2
    sums = jnp.zeros((BUCKETS, 128), F32)
    lane = lax.broadcasted_iota(jnp.int32, (BUCKETS, 128), 1)
    row = lax.broadcasted_iota(jnp.int32, (BLK, BLK), 0)
    column = lax.broadcasted_iota(jnp.int32, (BLK, BLK), 1)
    flip = jnp.where(row + column == BLK - 1, 1.0, 0.0).astype(BF16)
    apart = jnp.where(column == BLK - 1, 0, column + 1)
    ahead = apart <= row
    number_at = lax.broadcasted_iota(jnp.int32, (BUCKETS, BLK), 0)
    for head in range(heads):
        lines = [jnp.zeros((1, BLK), F32) for _ in range(4)]
        for number in range(3):
            grads = near_ref[head, number] + near_ref[heads + head, number]
            coarse = grads.astype(BF16)
            fine = (grads - coarse.astype(F32)).astype(BF16)
            flipped = mm(flip, coarse) + mm(flip, fine)
            rolled = pltpu.roll(flipped, 0, 1, stride=1, stride_axis=0)
            lines[number] += jnp.sum(jnp.where(ahead, rolled, 0.0), axis=0, keepdims=True)
            lines[number + 1] += jnp.sum(jnp.where(ahead, 0.0, rolled), axis=0, keepdims=True)
        total = jnp.zeros((BUCKETS, 1), F32)
        for number, line in enumerate(lines):
            bucket = bucket_of((number - 1) * BLK - apart[:1])
            total += jnp.sum(jnp.where(bucket == number_at, line, 0.0), axis=1, keepdims=True)
        distant = jnp.sum(far_ref[head] + far_ref[heads + head], axis=0, keepdims=True)
        distant = jnp.sum(distant, axis=1, keepdims=True)
        total += jnp.where(number_at[:, :1] == 15, distant, 0.0)
        sums = jnp.where(lane == head, total, sums)
    return sums


def key_count(query_block):
    return 2 * BLK if query_block < 2 else 4 * BLK


def block_scores(keys, queries, tile_of, limit, block):
    count = key_count(block)
    parts = []
    whole = mm(keys[:, :count], queries, TN)
    for key_block in range(count // BLK):
        part = whole[key_block * BLK : (key_block + 1) * BLK]
        shift = key_block - block
        if -1 <= shift <= 1:
            part = part + tile_of(shift)
        if shift >= 0:
            key_at = lax.broadcasted_iota(jnp.int32, (BLK, BLK), 0) + key_block * BLK
            part = jnp.where(key_at <= limit, part, NEG)
        parts.append(part)
    return jnp.concatenate(parts, axis=0)


def attend_half(qkv_ref, tiles_ref, limit_ref, mixed_ref, lse_ref, seq, half):
    heads = tiles_ref.shape[0]
    width = mixed_ref.shape[0] // heads
    base = pl.multiple_of(seq * SEQ, SEQ)

    def one_head(head, carry):
        at = lambda kind: pl.ds(pl.multiple_of((kind * heads + head) * width, width), width)
        keys, values = qkv_ref[at(1), pl.ds(base, SEQ)], qkv_ref[at(2), pl.ds(base, SEQ)]
        for block in (2 * half, 2 * half + 1):
            cols = pl.ds(pl.multiple_of(base + block * BLK, BLK), BLK)
            span = slice(block * BLK, (block + 1) * BLK)
            queries = qkv_ref[at(0), cols] * BF16(0.125)
            scores = block_scores(
                keys, queries, lambda shift: tiles_ref[head, shift + 1], limit_ref[seq, :, span], block
            )
            top = jnp.max(scores, axis=0, keepdims=True)
            exponent = jnp.exp(scores - top)
            total = jnp.sum(exponent, axis=0, keepdims=True)
            mixed = mm(values[:, : key_count(block)], exponent.astype(BF16)) / total
            mixed_ref[at(0), cols] = mixed.astype(BF16)
            lse_ref[seq * heads + head, :, span] = top + jnp.log(total)
        return carry

    lax.fori_loop(0, heads, one_head, 0)


def attend_back_kernel(
    q_ref, k_ref, v_ref, tiles_ref, limit_ref, w_ref, grad_ref, lse_ref, part_ref, resid_ref,
    dq_ref, dk_ref, dv_ref, near_ref, far_ref, y_ref,
    held, parts, total, turn_across, turn_along, from_across, from_along, sends, recvs, loads,
):
    rank = lax.axis_index("tensor")
    pair_class, half_index = rank % 2, rank // 2
    across, along, corner = rank + 1 - 2 * pair_class, rank + 2 - 4 * half_index, 3 - rank
    step = pl.program_id(0) * pl.num_programs(1) + pl.program_id(1)
    mesh_ids = pl.DeviceIdType.MESH
    middle = parts.shape[2] // 2
    low, high = slice(0, middle), slice(middle, 2 * middle)

    def remote(number, origin, target, other):
        return pltpu.make_async_remote_copy(
            src_ref=origin, dst_ref=target, send_sem=sends.at[number], recv_sem=recvs.at[number],
            device_id={"tensor": other}, device_id_type=mesh_ids,
        )

    first = (
        remote(0, part_ref.at[corner, :, low], turn_across, across),
        remote(1, part_ref.at[corner, :, high], turn_along, along),
    )
    second = remote(2, parts.at[0], from_across, across), remote(3, parts.at[1], from_along, along)
    local = [
        pltpu.make_async_copy(part_ref.at[other], parts.at[number], loads.at[number])
        for number, other in enumerate((across, along, rank))
    ]
    local.append(pltpu.make_async_copy(resid_ref, total, loads.at[3]))

    @pl.when(step == 0)
    def _():
        barrier = pltpu.get_barrier_semaphore()
        for other in (across, along):
            pl.semaphore_signal(barrier, inc=1, device_id={"tensor": other}, device_id_type=mesh_ids)
        pl.semaphore_wait(barrier, 2)
        for copy in first:
            copy.start()
        for copy in local:
            copy.start()

    @pl.when(step == 3)
    def _():
        for copy in (*first, *local):
            copy.wait()
        parts[0, :, high] = (parts[0, :, high].astype(F32) + turn_along[...].astype(F32)).astype(BF16)
        parts[1, :, low] = (parts[1, :, low].astype(F32) + turn_across[...].astype(F32)).astype(BF16)
        for copy in second:
            copy.start()

    head = pl.program_id(1)
    width = q_ref.shape[0]

    @pl.when(head == 0)
    def _():
        held[...] = mm(w_ref[...], grad_ref[...], NT).astype(BF16)

    queries = q_ref[...] * BF16(0.125)
    keys, values = k_ref[...], v_ref[...]
    grads = held[pl.ds(pl.multiple_of(head * width, width), width), :]
    near_ref[...] = jnp.zeros_like(near_ref)
    far = jnp.zeros((8, BLK), F32)
    grad_keys = jnp.zeros((width, SEQ), F32)
    grad_values = jnp.zeros((width, SEQ), F32)
    for block in range(SEQ // BLK):
        count = key_count(block)
        cols = slice(block * BLK, (block + 1) * BLK)
        scores = block_scores(
            keys, queries[:, cols], lambda shift: tiles_ref[0, shift + 1], limit_ref[0, :, cols], block
        )
        probs = jnp.exp(scores - lse_ref[0, :, cols])
        grad_probs = mm(values[:, :count], grads[:, cols], TN)
        inner = jnp.sum(probs * grad_probs, axis=0, keepdims=True)
        grad_scores = probs * (grad_probs - inner)
        for key_block in range(count // BLK):
            part = grad_scores[key_block * BLK : (key_block + 1) * BLK]
            shift = key_block - block
            if -1 <= shift <= 1:
                near_ref[0, shift + 1] += part
            elif shift < -1:
                far = far + jnp.sum(part.reshape(BLK // 8, 8, BLK), axis=0)
        rounded = grad_scores.astype(BF16)
        add_values = mm(grads[:, cols], probs.astype(BF16), NT)
        add_keys = mm(queries[:, cols], rounded, NT)
        if count == SEQ:
            grad_values = grad_values + add_values
            grad_keys = grad_keys + add_keys
        else:
            filler = jnp.zeros((width, SEQ - count), F32)
            grad_values = grad_values + jnp.concatenate([add_values, filler], axis=1)
            grad_keys = grad_keys + jnp.concatenate([add_keys, filler], axis=1)
        dq_ref[:, cols] = (mm(keys[:, :count], rounded) * 0.125).astype(BF16)
    dk_ref[...] = grad_keys.astype(BF16)
    dv_ref[...] = grad_values.astype(BF16)
    far_ref[0] = far

    @pl.when(step == 7)
    def _():
        for copy in second:
            copy.wait()
        summed = parts[2].astype(F32) + from_across[...].astype(F32) + from_along[...].astype(F32)
        y_ref[...] = (total[...] + summed).astype(BF16)


def attend_back(qkv, tiles, limits, attn_out, grad_attn, lse, part, resid):
    heads = tiles.shape[0]
    seqs = limits.shape[0]
    width = qkv.shape[0] // (3 * heads)
    model_width = attn_out.shape[1]
    share = part.shape[1]
    grad_spec = pl.BlockSpec((width, SEQ), lambda s, h: (h, s))
    anywhere = pl.BlockSpec(memory_space=pl.ANY)
    return pl.pallas_call(
        attend_back_kernel,
        grid=(seqs, heads),
        in_specs=[
            pl.BlockSpec((width, SEQ), lambda s, h: (h, s)),
            pl.BlockSpec((width, SEQ), lambda s, h: (heads + h, s)),
            pl.BlockSpec((width, SEQ), lambda s, h: (2 * heads + h, s)),
            pl.BlockSpec((1, 3, BLK, BLK), lambda s, h: (h, 0, 0, 0)),
            pl.BlockSpec((1, 1, SEQ), lambda s, h: (s, 0, 0)),
            pl.BlockSpec((heads * width, model_width), lambda s, h: (0, 0)),
            pl.BlockSpec((SEQ, model_width), lambda s, h: (s, 0)),
            pl.BlockSpec((1, 1, SEQ), lambda s, h: (s * heads + h, 0, 0)),
        ]
        + [anywhere] * 2,
        out_specs=[
            grad_spec,
            grad_spec,
            grad_spec,
            pl.BlockSpec((1, 3, BLK, BLK), lambda s, h: (s * heads + h, 0, 0, 0)),
            pl.BlockSpec((1, 8, BLK), lambda s, h: (s * heads + h, 0, 0)),
            pl.BlockSpec((share, model_width), lambda s, h: (0, 0)),
        ],
        out_shape=[jax.ShapeDtypeStruct((heads * width, seqs * SEQ), BF16)] * 3
        + [
            jax.ShapeDtypeStruct((seqs * heads, 3, BLK, BLK), F32),
            jax.ShapeDtypeStruct((seqs * heads, 8, BLK), F32),
        ]
        + [jax.ShapeDtypeStruct((share, model_width), BF16)],
        scratch_shapes=[
            pltpu.VMEM((heads * width, SEQ), BF16),
            pltpu.VMEM((3, share, model_width), BF16),
            pltpu.VMEM((share, model_width), F32),
            pltpu.VMEM((share, model_width // 2), BF16),
            pltpu.VMEM((share, model_width // 2), BF16),
            pltpu.VMEM((share, model_width), BF16),
            pltpu.VMEM((share, model_width), BF16),
            pltpu.SemaphoreType.DMA((4,)),
            pltpu.SemaphoreType.DMA((4,)),
            pltpu.SemaphoreType.DMA((4,)),
        ],
        compiler_params=pltpu.CompilerParams(
            vmem_limit_bytes=60 * MIB, collective_id=5, has_side_effects=True
        ),
        cost_estimate=cost(seqs * heads * SEQ * SEQ * 1280, seqs * heads * SEQ * 4096, seqs * heads * SEQ * SEQ),
    )(qkv, qkv, qkv, tiles, limits, attn_out, grad_attn, lse, part, resid)


def project_back_kernel(
    place_ref, x_ref, gain_ref, gain_row_ref, scale_ref, w_ref, mixed_ref, attn_ref, dq_ref, dk_ref, dv_ref, *refs
):
    step = pl.program_id(0)
    own_refs, got_refs, (weight_ref, out_ref, gain_grad_ref), placed_refs, total = (
        refs[:3], refs[3:6], refs[6:9], refs[9:12], refs[12]
    )
    for own_ref, got_ref, placed_ref in zip(own_refs, got_refs, placed_refs):
        placed_ref[place_ref[0]] = own_ref[...]
        placed_ref[1 - place_ref[0]] = got_ref[...].astype(F32)
    grads = jnp.concatenate([dq_ref[...], dk_ref[...], dv_ref[...]], axis=0)
    rows = grads.shape[0]
    normed = (x_ref[...].astype(F32) * scale_ref[...] * gain_ref[...]).astype(BF16)

    @pl.when(step == 0)
    def _():
        total[...] = jnp.zeros_like(total)

    total[:rows] += mm(grads, normed, NT)
    total[rows:] += mm(mixed_ref[...], attn_ref[...])
    out_ref[...] = mm(grads, w_ref[...], TN).astype(BF16)

    @pl.when(step == pl.num_programs(0) - 1)
    def _():
        weight_ref[...] = total[...].astype(BF16)
        through = jnp.sum(total[:rows] * w_ref[...].astype(F32), axis=0, keepdims=True)
        gain_grad_ref[...] = through / gain_row_ref[...]


def project_back(place, x, gain, gain_row, scale, weights, mixed, grad_attn, grads, owns, gots):
    width, tokens = x.shape
    rows = weights.shape[0]
    heads_width = mixed.shape[0]
    units = owns[0].shape[0]
    steps = 4
    tile = tokens // steps
    part = units // steps
    column = lambda count: pl.BlockSpec((count, tile), lambda i: (0, i))
    return pl.pallas_call(
        project_back_kernel,
        grid=(steps,),
        in_specs=[
            pl.BlockSpec(memory_space=pltpu.SMEM),
            column(width),
            pl.BlockSpec((width, 1), lambda i: (0, 0)),
            pl.BlockSpec((1, width), lambda i: (0, 0)),
            column(1),
            pl.BlockSpec((rows, width), lambda i: (0, 0)),
            column(heads_width),
            pl.BlockSpec((tile, width), lambda i: (i, 0)),
        ]
        + [column(rows // 3)] * 3
        + [pl.BlockSpec((part, width), lambda i: (i, 0))] * 6,
        out_specs=[
            pl.BlockSpec((rows + heads_width, width), lambda i: (0, 0)),
            pl.BlockSpec((tile, width), lambda i: (i, 0)),
            pl.BlockSpec((1, width), lambda i: (0, 0)),
        ]
        + [pl.BlockSpec((2, part, width), lambda i: (0, i, 0))] * 3,
        out_shape=[
            jax.ShapeDtypeStruct((rows + heads_width, width), BF16),
            jax.ShapeDtypeStruct((tokens, width), BF16),
            jax.ShapeDtypeStruct((1, width), F32),
        ]
        + [jax.ShapeDtypeStruct((2, units, width), F32)] * 3,
        scratch_shapes=[pltpu.VMEM((rows + heads_width, width), F32)],
        compiler_params=params(),
        cost_estimate=cost(5 * width * tokens * rows, 6 * width * tokens + 14 * units * width),
    )(place, x, gain, gain_row, scale, weights, mixed, grad_attn, *grads, *owns, *gots)


def exchange(
    math, rank, source, full_out, full, from_across, from_along, to_across, to_along, turn_across, turn_along, sends, recvs, outs, ready=None, ready_full=None, side=None, peers=(), fill=None, start=None, cut=None, later=None):
    pair_class, half_index = rank % 2, rank // 2
    across, along, corner = rank + 1 - 2 * pair_class, rank + 2 - 4 * half_index, 3 - rank
    mesh_ids = pl.DeviceIdType.MESH
    rows, width = source.shape[1:]
    chunks = 4
    size = rows // chunks
    cut = cut or width // 2
    low, high = slice(0, cut), slice(cut, width)
    barrier = pltpu.get_barrier_semaphore()
    near = (across, along, corner) if later else (across, along)
    for other in near:
        pl.semaphore_signal(barrier, inc=1, device_id={"tensor": other}, device_id_type=mesh_ids)
    for other in peers:
        pl.semaphore_signal(barrier, inc=1, device_id={"expert": other}, device_id_type=mesh_ids)
    pl.semaphore_wait(barrier, len(near) + len(peers))

    def remote(kind, chunk, origin, target, other):
        return pltpu.make_async_remote_copy(
            src_ref=origin, dst_ref=target, send_sem=sends.at[kind, chunk], recv_sem=recvs.at[kind, chunk],
            device_id={"tensor": other}, device_id_type=mesh_ids,
        )

    if start:
        start()
    if fill:
        fill(corner)
    spans = [slice(chunk * size, (chunk + 1) * size) for chunk in range(chunks)]
    first, second, third, fourth = [], [], [], []
    for chunk, span in enumerate(spans):
        pair = (
            remote(0, chunk, source.at[corner, span, low], turn_across.at[span, low], across),
            remote(1, chunk, source.at[corner, span, high], turn_along.at[span, high], along),
        )
        for copy in pair:
            copy.start()
        first.append(pair)
    if fill:
        fill(along)
        fill(across)
    leaving = []

    def leave(number, other):
        leaving.append(pltpu.make_async_copy(full.at[other], full_out.at[other], outs.at[number]))
        leaving[-1].start()

    if ready is not None:
        _, near_across, near_along = ready
        extra = [
            remote(8, 0, near_along.at[:, low], ready_full.at[along, :, low], across),
            remote(8, 1, near_across.at[:, high], ready_full.at[across, :, high], along),
        ]
        extra += [
            pltpu.make_async_copy(piece, ready_full.at[other], outs.at[4 + number])
            for number, (other, piece) in enumerate(zip((rank, across, along), ready))
        ]
        for copy in extra:
            copy.start()
    for chunk, span in enumerate(spans):
        if side:
            side(chunk)
        first[chunk][0].wait()
        to_along[span, low] = (source[along, span, low].astype(F32) + turn_across[span, low].astype(F32)).astype(BF16)
        to_along[span, high] = source[along, span, high]
        first[chunk][1].wait()
        to_across[span, low] = source[across, span, low]
        to_across[span, high] = (source[across, span, high].astype(F32) + turn_along[span, high].astype(F32)).astype(BF16)
        pair = (
            remote(2, chunk, to_across.at[span], from_across.at[span], across),
            remote(3, chunk, to_along.at[span], from_along.at[span], along),
        )
        for copy in pair:
            copy.start()
        second.append(pair)
    def pass_on(chunk):
        span = spans[chunk]
        for copy in third[chunk]:
            copy.wait()
        pair = (
            remote(6, chunk, full.at[along, span, low], full.at[along, span, low], across),
            remote(7, chunk, full.at[across, span, high], full.at[across, span, high], along),
        )
        for copy in pair:
            copy.start()
        fourth.append(pair)

    if fill:
        fill(rank)
    if later:
        later((across, along, corner))
    for chunk, span in enumerate(spans):
        if side:
            side(chunks + chunk)
        for copy in second[chunk]:
            copy.wait()
        total = source[rank, span].astype(F32) + from_across[span].astype(F32) + from_along[span].astype(F32)
        full[rank, span] = math(span, total).astype(BF16)
        pair = (
            remote(4, chunk, full.at[rank, span], full.at[rank, span], across),
            remote(5, chunk, full.at[rank, span], full.at[rank, span], along),
        )
        for copy in pair:
            copy.start()
        third.append(pair)
        if chunk:
            pass_on(chunk - 1)
    leave(0, rank)
    pass_on(chunks - 1)
    leave(1, across)
    leave(2, along)
    if ready is not None:
        for copy in extra:
            copy.wait()
    if side and later:
        side(2 * chunks)
    for pair in fourth:
        for copy in pair:
            copy.wait()
    leave(3, corner)
    if side and not later:
        side(2 * chunks)
    for copy in leaving:
        copy.wait()


def exchange_call(kernel, number, shape, operands, extra_shapes, scratch=(), in_hbm=(), out_hbm=()):
    tokens, width = shape
    ranks = 4
    rows = tokens // ranks
    here = pl.BlockSpec(memory_space=pltpu.VMEM)
    results = pl.pallas_call(
        kernel,
        in_specs=[pl.BlockSpec(memory_space=pl.ANY) if k in in_hbm else here for k in range(len(operands))],
        out_specs=[pl.BlockSpec(memory_space=pl.ANY)]
        + [pl.BlockSpec(memory_space=pl.ANY) if k in out_hbm else here for k in range(len(extra_shapes))],
        out_shape=[jax.ShapeDtypeStruct((ranks, rows, width), BF16)]
        + [jax.ShapeDtypeStruct(shape, kind) for shape, kind in extra_shapes],
        scratch_shapes=[pltpu.VMEM((ranks, rows, width), BF16)]
        + [pltpu.VMEM((rows, width), BF16)] * 6
        + [pltpu.SemaphoreType.DMA((9, 4))] * 2
        + [pltpu.SemaphoreType.DMA((7,))]
        + list(scratch),
        compiler_params=pltpu.CompilerParams(
            vmem_limit_bytes=60 * MIB, collective_id=number, has_side_effects=True
        ),
        cost_estimate=cost(40 * MIB, 200 * MIB),
    )(*operands)
    return results[0].reshape(tokens, width), *results[1:]


def norm_two_kernel(
    qkv_ref, tiles_ref, limit_ref, w_ref, x_ref, gain_ref, grad_out_ref, routes_ref, gate_ref,
    full, resid_ref, scale_ref, dy_out, dy_rows_out, code_ref, codes_ref, own_ref, mixed_ref, lse_ref, got_gate, *rest,
):
    source, held, grad_out, dy_ref, dy_rows_ref, load, send, recv = rest[-8:]
    rank = lax.axis_index("tensor")
    ranks, rows, width = source.shape
    loading = pltpu.make_async_copy(grad_out_ref, grad_out, load.at[1])
    storing = [
        pltpu.make_async_copy(dy_ref, dy_out, load.at[2]),
        pltpu.make_async_copy(dy_rows_ref, dy_rows_out, load.at[3]),
    ]

    pair_class = rank % 2
    part = got_gate.shape[0] // 2
    swaps = [
        pltpu.make_async_remote_copy(
            src_ref=gate_ref.at[1 - pair_class, pl.ds((2 + piece) * part, part)],
            dst_ref=got_gate.at[pl.ds(piece * part, part)],
            send_sem=send.at[piece],
            recv_sem=recv.at[piece],
            device_id={"tensor": rank + 1 - 2 * pair_class},
            device_id_type=pl.DeviceIdType.MESH,
        )
        for piece in range(2)
    ]

    def start():
        own.start()
        loading.start()
        swaps[0].start()

    def fill(shard):
        for half in range(2):
            pl.when(shard % 2 == half)(
                partial(attend_half, qkv_ref, tiles_ref, limit_ref, mixed_ref, lse_ref, shard // 2, half)
            )
        columns = pl.ds(pl.multiple_of(shard * rows, rows), rows)
        source[shard] = mm(mixed_ref[:, columns], w_ref[...], TN).astype(BF16)

    slots = dy_rows_ref.shape[0] // ranks
    own = pltpu.make_async_copy(x_ref.at[:, pl.ds(pl.multiple_of(rank * rows, rows), rows)], held, load.at[0])

    def math(span, total):
        resid = own_ref[span, :].astype(F32) + total
        scale = lax.rsqrt(jnp.sum(resid * resid, axis=1, keepdims=True) / resid.shape[1] + EPS)
        resid_ref[span, :] = resid
        scale_ref[span, :] = scale
        return resid * scale * gain_ref[...]

    def later(others):
        own.wait()
        own_ref[...] = held[...].astype(F32).T.astype(BF16)
        local_codes(routes_ref, code_ref, pair_class, rank // 2, CAP // 2)
        codes_ref[...] = jnp.concatenate([code_ref[...].astype(F32)] * 4, axis=0).T[:, :TOP].astype(jnp.int32)
        loading.wait()
        for number in range(ranks):
            span = slice(number * rows, (number + 1) * rows)
            dy_ref[span, :] = grad_out[:, span].astype(F32).T.astype(BF16)
        storing[0].start()

    def side(number):
        if number == 0:
            swaps[1].start()
        elif ranks <= number < 2 * ranks:
            begin = (number - ranks) * slots
            slot = lax.broadcasted_iota(jnp.int32, (slots, dy_ref.shape[0]), 0) + begin
            take = jnp.where((slot == code_ref[0:1]) | (slot == code_ref[1:2]), 1.0, 0.0).astype(BF16)
            dy_rows_ref[begin : begin + slots, :] = mm(take, dy_ref[...]).astype(BF16)
        elif number == 2 * ranks:
            storing[1].start()
            for copy in swaps + storing:
                copy.wait()

    exchange(
        math, rank, source, full, *rest[:-8], side=side, start=start, fill=fill, later=later, cut=3 * width // 8
    )


def norm_back(grad, value, scale, gain):
    scaled = grad * gain
    inner = jnp.sum(scaled * value, axis=1, keepdims=True)
    return scale * scaled - value * (scale * scale * scale) * (inner / value.shape[1])


def norm_two_back_kernel(
    ret_in, back_ref, code_ref, codes_ref, gates_ref, routes_ref, dy_rows_in, gate_ref, router_ref, h_in,
    resid_in, scale_ref, dy_in, gain_ref, full, grad_ref, gain_grad_ref, router_grad_ref, y_out, *rest,
):
    source, scaled, logit_parts, logit_own, send, recv, ret_ref, dy_rows_ref, h_ref, resid_ref, dy_ref, y_ref, load = rest[-13:]
    rank = lax.axis_index("tensor")
    rows = source.shape[1]
    slots, tokens = ret_ref.shape[0], code_ref.shape[1]
    ranks = tokens // rows
    copies = []
    own_dy = dy_in.at[pl.ds(pl.multiple_of(rank * rows, rows), rows)]
    pairs = ((ret_in, ret_ref), (dy_rows_in, dy_rows_ref), (resid_in, resid_ref), (own_dy, dy_ref), (h_in, h_ref))
    loading = [pltpu.make_async_copy(*pair, load.at[number]) for number, pair in enumerate(pairs)]
    storing = [
        pltpu.make_async_copy(y_ref.at[shard], y_out.at[pl.ds(shard * rows, rows)], load.at[5 + shard])
        for shard in range(ranks)
    ]

    def start():
        for copy in loading:
            copy.start()

    def later(others):
        for copy in loading:
            copy.wait()
        found = [jnp.zeros((1, tokens), F32) for _ in range(TOP)]
        tile = slots // 4
        for begin in range(0, slots, tile):
            span = slice(begin, begin + tile)
            ret = ret_ref[span, :].astype(F32)
            slot_grad = jnp.sum(dy_rows_ref[span, :].astype(F32) * ret, axis=1, keepdims=True)
            scaled[span, :] = (ret * gate_ref[span, :]).astype(BF16)
            slot = lax.broadcasted_iota(jnp.int32, (tile, tokens), 0) + begin
            for i in range(TOP):
                found[i] = found[i] + jnp.sum(
                    jnp.where(slot == code_ref[i : i + 1, :], slot_grad, 0.0), axis=0, keepdims=True
                )
        mean = gates_ref[0:1] * found[0] + gates_ref[1:2] * found[1]
        expert = lax.broadcasted_iota(jnp.int32, (EXPERTS, tokens), 0)
        logit = sum(
            jnp.where(routes_ref[i : i + 1] == expert, gates_ref[i : i + 1] * (found[i] - mean), 0.0)
            for i in range(TOP)
        )
        for shard in range(ranks):
            logit_parts[shard] = logit[:, shard * rows : (shard + 1) * rows]
        for number, other in enumerate(others):
            copies.append(
                pltpu.make_async_remote_copy(
                    src_ref=logit_parts.at[other], dst_ref=logit_parts.at[ranks + number], send_sem=send.at[number],
                    recv_sem=recv.at[number], device_id={"tensor": other}, device_id_type=pl.DeviceIdType.MESH,
                )
            )
            copies[-1].start()

    def places(shard):
        slot = lax.broadcasted_iota(jnp.int32, (rows, slots), 1)
        codes = codes_ref[pl.ds(pl.multiple_of(shard * rows, rows), rows), :]
        return jnp.where((slot == codes[:, 0:1]) | (slot == codes[:, 1:2]), 1.0, 0.0).astype(BF16)

    def fill(shard):
        source[shard] = mm(places(shard), back_ref[...]).astype(BF16)

    def side(number):
        if number == ranks:
            router_grad_ref[...] = sum(
                mm(logit_parts[shard].astype(BF16), h_ref[shard * rows : (shard + 1) * rows, :])
                for shard in range(ranks)
            )
            for copy in copies:
                copy.wait()
            logit = logit_parts[rank] + logit_parts[ranks] + logit_parts[ranks + 1] + logit_parts[ranks + 2]
            coarse = logit.astype(BF16)
            logit_own[:EXPERTS] = coarse
            logit_own[EXPERTS:] = (logit - coarse.astype(F32)).astype(BF16)
        elif number > ranks:
            shard = number - ranks - 1
            y_ref[shard] = mm(places(shard), scaled[...]).astype(BF16)
            storing[shard].start()
            if shard == ranks - 1:
                for copy in storing:
                    copy.wait()

    gain_grad_ref[...] = jnp.zeros_like(gain_grad_ref)

    def math(span, total):
        resid, scale = resid_ref[span, :], scale_ref[span, :]
        both = jnp.concatenate([router_ref[...], router_ref[...]], axis=0)
        total = total + mm(logit_own[:, span], both, TN)
        gain_grad_ref[...] += jnp.sum(total * resid * scale, axis=0, keepdims=True)
        grad = norm_back(total, resid, scale, gain_ref[...]) + dy_ref[span, :].astype(F32)
        grad_ref[span, :] = grad
        return grad

    exchange(math, rank, source, full, *rest[:-13], side=side, fill=fill, start=start, later=later)


def norm_one_back_kernel(
    source, x_in, scale_ref, grad_in, gain_ref, y_own, y_across, y_along, gain_one_ref, gain_two_ref, router_ref,
    near_ref, far_ref, full, ready_full, small_out, *rest,
):
    x_ref, grad_ref, held, gathered, near, scale, load, tensor_sends, tensor_recvs, expert_sends, expert_recvs = rest[-11:]
    rank, group = lax.axis_index("tensor"), lax.axis_index("expert")
    pair_class, half_index = rank % 2, rank // 2
    others = rank + 1 - 2 * pair_class, rank + 2 - 4 * half_index
    groups = expert_sends.shape[0]
    mesh_ids = pl.DeviceIdType.MESH
    peers = [partner_of(group, step) for step in range(1, groups)]
    heads = near_ref.shape[0] // 2
    rows = source.shape[1]
    pairs = ((near_ref, near), (x_in, x_ref), (grad_in, grad_ref))
    loading = [pltpu.make_async_copy(*pair, load.at[number]) for number, pair in enumerate(pairs)]

    def math(span, total):
        x = x_ref[span, :].astype(F32)
        return norm_back(total, x, scale[span, :], gain_ref[...]) + grad_ref[span, :]

    def to_rank(step):
        return pltpu.make_async_remote_copy(
            src_ref=held.at[step], dst_ref=held.at[2 + step], send_sem=tensor_sends.at[step],
            recv_sem=tensor_recvs.at[step], device_id={"tensor": others[step]}, device_id_type=mesh_ids,
        )

    def to_group(step):
        return pltpu.make_async_remote_copy(
            src_ref=gathered.at[group], dst_ref=gathered.at[group], send_sem=expert_sends.at[step],
            recv_sem=expert_recvs.at[step], device_id={"expert": peers[step - 1]}, device_id_type=mesh_ids,
        )

    def start():
        for copy in loading:
            copy.start()
        held[0] = jnp.zeros(small_out.shape, F32)
        held[0, :EXPERTS] = router_ref[...]
        held[0, EXPERTS : EXPERTS + 1] = gain_two_ref[...]
        held[0, EXPERTS + 1 : EXPERTS + 2] = gain_one_ref[...]
        to_rank(0).start()

    def side(number):
        if number == 0:
            own_scale = scale_ref[:, pl.ds(pl.multiple_of(rank * rows, rows), rows)]
            scale[...] = jnp.broadcast_to(own_scale, (8, rows)).T[:, :1]
            for copy in loading:
                copy.wait()
            small_out[:BUCKETS, :128] = bias_fold(near, far_ref)
        elif number == 1:
            to_rank(0).wait()
            held[1] = held[0] + held[2]
            to_rank(1).start()
        elif number == 5:
            to_rank(1).wait()
            turned = small_out[:BUCKETS, :128].T
            held[0] = held[1] + held[3]
            held[0, EXPERTS + 2 : EXPERTS + 2 + heads, :BUCKETS] = turned[:heads]
            gathered[group] = held[0].astype(BF16)
            for step in range(1, groups):
                to_group(step).start()
        elif number == 8:
            for step in range(1, groups):
                to_group(step).wait()
            total = gathered[0].astype(F32)
            for step in range(1, groups):
                total = total + gathered[step].astype(F32)
            small_out[...] = total

    exchange(
        math, rank, source, full, *rest[:-11], (y_own, y_across, y_along), ready_full, side=side, peers=peers, start=start
    )


def local_codes(routes_ref, code_ref, pair_class, half_index, half):
    tokens = routes_ref.shape[1]
    expert = lax.broadcasted_iota(jnp.int32, (EXPERTS, BLK), 0)
    earlier = (
        lax.broadcasted_iota(jnp.int32, (BLK, BLK), 0) < lax.broadcasted_iota(jnp.int32, (BLK, BLK), 1)
    ).astype(F32).astype(BF16)
    carry = jnp.zeros((EXPERTS, 1), F32)
    for block in range(tokens // BLK):
        cols = slice(block * BLK, (block + 1) * BLK)
        routes = routes_ref[:, cols]
        hits = [(routes[i : i + 1] == expert) for i in range(TOP)]
        chosen = sum(hit.astype(F32) for hit in hits)
        before = mm(chosen.astype(BF16), earlier) + carry
        carry = carry + jnp.sum(chosen, axis=1, keepdims=True)
        for i in range(TOP):
            slot = jnp.sum(jnp.where(hits[i], before, 0.0), axis=0, keepdims=True).astype(jnp.int32)
            route = routes[i : i + 1]
            owner = route // 2
            local = slot - half_index * half
            mine = (route - 2 * owner == pair_class) & (local >= 0) & (local < half)
            code_ref[i : i + 1, cols] = jnp.where(mine, owner * half + local, -1)


def dispatch_kernel(code_ref, routes_ref, router_ref, h_ref, dy_rows_ref, rows_ref, grads_ref, gate_ref, gates_ref):
    count, tokens = rows_ref.shape[0], h_ref.shape[0]

    @pl.when(pl.program_id(0) == 0)
    def _():
        expert = lax.broadcasted_iota(jnp.int32, (EXPERTS, tokens), 0)
        logits = mm(router_ref[...], h_ref[...], NT)
        picked = [
            jnp.sum(jnp.where(routes_ref[i : i + 1] == expert, logits, 0.0), axis=0, keepdims=True)
            for i in range(TOP)
        ]
        top = jnp.maximum(picked[0], picked[1])
        raised = [jnp.exp(value - top) for value in picked]
        total = raised[0] + raised[1]
        for i in range(TOP):
            gates_ref[i : i + 1] = raised[i] / total

    slot = lax.broadcasted_iota(jnp.int32, (count, tokens), 0) + pl.program_id(0) * count
    hits = [slot == code_ref[i : i + 1, :] for i in range(TOP)]
    take = jnp.where(hits[0] | hits[1], 1.0, 0.0).astype(BF16)
    weighted = jnp.where(hits[0], gates_ref[0:1, :], jnp.where(hits[1], gates_ref[1:2, :], 0.0))
    gate = jnp.sum(weighted, axis=1, keepdims=True)
    rows_ref[...] = mm(take, h_ref[...]).astype(BF16)
    grads_ref[...] = (dy_rows_ref[...].astype(F32) * gate).astype(BF16)
    gate_ref[...] = gate


def dispatch(code, routes_t, router_t, h, dy_rows):
    slots, width = dy_rows.shape
    tile = slots // 4
    row_spec = pl.BlockSpec((tile, width), lambda i: (i, 0))
    whole = lambda shape: pl.BlockSpec(shape, lambda i: (0, 0))
    return pl.pallas_call(
        dispatch_kernel,
        grid=(4,),
        in_specs=[whole(code.shape), whole(code.shape), whole(router_t.shape), whole(h.shape), row_spec],
        out_specs=[row_spec, row_spec, pl.BlockSpec((tile, 1), lambda i: (i, 0)), whole(code.shape)],
        out_shape=[jax.ShapeDtypeStruct((slots, width), BF16)] * 2
        + [jax.ShapeDtypeStruct((slots, 1), F32), jax.ShapeDtypeStruct(code.shape, F32)],
        compiler_params=params(),
        cost_estimate=cost(4 * slots * SEQ * width, 4 * MIB + 6 * slots * width),
    )(code, routes_t, router_t, h, dy_rows)


def gelu_parts(x):
    inner = 0.7978845608028654 * (x + 0.044715 * (x * x * x))
    bend = jnp.tanh(inner)
    half = 0.5 * (1.0 + bend)
    slope = half + 0.5 * x * (1.0 - bend * bend) * (
        0.7978845608028654 * (1.0 + 3.0 * 0.044715 * (x * x))
    )
    return x * half, slope


def partner_of(index, step):
    found = index
    for bit in (1, 2, 4):
        found = found + ((step // bit) % 2) * (1 - 2 * ((index // bit) % 2)) * bit
    return found


def expert_kernel(
    rows_in, grads_in, gate_in, up_in, down_in, far_gate, far_gate_too,
    ret_out, back_out, own_gate, own_up, own_down, got_gate, got_up, got_down,
    rows, grads, weights, sums, parts, z_send, z_recv, y_send, y_recv, p_send, p_recv, r_send, r_recv, w_send, w_recv, g_send, g_recv, local,
):
    groups, half, width = rows.shape[1:]
    group, rank = lax.axis_index("expert"), lax.axis_index("tensor")
    pair_class, half_index = rank % 2, rank // 2
    across = {"tensor": rank + 1 - 2 * pair_class}
    along = {"tensor": rank + 2 - 4 * half_index}
    mesh_ids = pl.DeviceIdType.MESH
    moved = ((rows_in, rows, ret_out), (grads_in, grads, back_out))

    barrier = pltpu.get_barrier_semaphore()
    for step in range(1, groups):
        pl.semaphore_signal(
            barrier, inc=1, device_id={"expert": partner_of(group, step)}, device_id_type=mesh_ids
        )
    pl.semaphore_signal(barrier, inc=1, device_id=across, device_id_type=mesh_ids)
    pl.semaphore_signal(barrier, inc=1, device_id=along, device_id_type=mesh_ids)
    pl.semaphore_wait(barrier, groups + 1)

    def remote(source, target, send, recv, device):
        return pltpu.make_async_remote_copy(
            src_ref=source, dst_ref=target, send_sem=send, recv_sem=recv,
            device_id=device, device_id_type=mesh_ids,
        )

    def block(ref, number):
        return ref.at[pl.ds(pl.multiple_of(number * half, half), half)]

    def out_of(kind, step):
        source, held, _ = moved[kind]
        other = partner_of(group, step)
        return remote(
            block(source, other), held.at[0, group], z_send.at[kind, step], z_recv.at[kind, step], {"expert": other}
        )

    def forward(kind, step):
        held = moved[kind][1]
        other = partner_of(group, step)
        return remote(held.at[0, other], held.at[1, other], y_send.at[kind, step], y_recv.at[kind, step], along)

    def partial_sum(kind, step):
        held = moved[kind][1]
        other = partner_of(group, step)
        return remote(held.at[1, other], parts.at[kind, other], p_send.at[kind, step], p_recv.at[kind, step], along)

    def result(kind, step):
        other = partner_of(group, step)
        return remote(
            parts.at[kind, other], block(moved[kind][2], group), r_send.at[kind, step], r_recv.at[kind, step], {"expert": other}
        )

    def own_result(kind):
        return pltpu.make_async_copy(parts.at[kind, group], block(moved[kind][2], group), local.at[kind])

    own = [
        pltpu.make_async_copy(block(moved[kind][0], group), moved[kind][1].at[0, group], local.at[kind])
        for kind in range(2)
    ]
    for copy in own:
        copy.start()
    kept = [
        pltpu.make_async_copy(ref.at[pair_class], weights.at[number, 0], local.at[2 + number])
        for number, ref in enumerate((gate_in, up_in, down_in))
    ]
    some = far_gate.shape[0]
    for number, ref in enumerate((far_gate, far_gate_too)):
        target = weights.at[0, 1, pl.ds(number * some, some)]
        kept.append(pltpu.make_async_copy(ref, target, local.at[5 + number]))
    kept += [
        remote(ref.at[1 - pair_class], weights.at[number, 1], w_send.at[number - 1], w_recv.at[number - 1], across)
        for number, ref in ((1, up_in), (2, down_in))
    ]
    for copy in kept:
        copy.start()
    for step in range(1, groups):
        for kind in range(2):
            out_of(kind, step).start()

    def arrive(step):
        for kind in range(2):
            out_of(kind, step).wait()
            forward(kind, step).start()

    def give(step):
        for kind in range(2):
            partial_sum(kind, step).start()

    for number in range(3):
        for part in range(2):
            sums[number, part] = jnp.zeros(sums.shape[2:], F32)

    def finish(step):
        other = partner_of(group, step)
        for kind in range(2):
            partial_sum(kind, step).wait()
            held = moved[kind][1]
            parts[kind, other] = (parts[kind, other].astype(F32) + held[0, other].astype(F32)).astype(BF16)

        for kind in range(2):
            if step == 0:
                own_result(kind).start()
            else:
                result(kind, step).start()

    def act(plan):
        for action, step in plan:
            action(step)

    order = (0, 1, 4, 5, 2, 6, 3, 7)
    before = {
        0: [(arrive, 1), (arrive, 2), (arrive, 3), (arrive, 4)],
        1: [(give, 0)],
        2: [(arrive, 5)],
        3: [(give, 4), (finish, 0)],
        4: [(arrive, 6)],
        5: [(give, 5), (finish, 4)],
        6: [(arrive, 7)],
        7: [(give, 6), (finish, 5)],
    }
    ahead = [(give, 7)]
    last = [(give, 2), (finish, 6), (give, 3), (finish, 7), (give, 1), (finish, 2), (finish, 3), (finish, 1)]
    for copy in own:
        copy.wait()
    for kind in range(2):
        forward(kind, 0).start()

    def body(turn, carry):
        for number, plan in before.items():
            pl.when(turn == number)(partial(act, plan))

        @pl.when(turn == 0)
        def _():
            for copy in kept:
                copy.wait()

        step = sum((turn == number).astype(jnp.int32) * which for number, which in enumerate(order))
        for kind in range(2):
            forward(kind, step).wait()
        other = partner_of(group, step)
        tile = jnp.concatenate([rows[0, other], rows[1, other]], axis=0)
        grad = jnp.concatenate([grads[0, other], grads[1, other]], axis=0)
        ret = jnp.zeros(tile.shape, F32)
        back = jnp.zeros(tile.shape, F32)
        for part in range(2):
            w_gate, w_up, w_down = weights[0, part], weights[1, part], weights[2, part]
            gate_part = mm(tile, w_gate, NT)
            up_part = mm(tile, w_up, NT)
            grad_hidden = mm(grad, w_down, NT)
            bent, slope = gelu_parts(gate_part)
            hidden = (bent * up_part).astype(BF16)
            grad_gate = (grad_hidden * up_part * slope).astype(BF16)
            grad_up = (grad_hidden * bent).astype(BF16)
            ret = ret + mm(hidden, w_down)
            back = back + mm(grad_gate, w_gate) + mm(grad_up, w_up)
            sums[0, part] += mm(grad_gate, tile, TN)
            sums[1, part] += mm(grad_up, tile, TN)
            sums[2, part] += mm(hidden, grad, TN)
        for kind, value in enumerate((ret, back)):
            held = moved[kind][1]
            held[0, other] = value[:half].astype(BF16)
            held[1, other] = value[half:].astype(BF16)

        return carry

    lax.fori_loop(0, groups, body, 0)
    act(ahead)
    copies = []
    for number, (own_ref, got_ref) in enumerate(((own_gate, got_gate), (own_up, got_up), (own_down, got_down))):
        weights[number, 0] = sums[number, 1].astype(BF16)
        copies.append(remote(weights.at[number, 0], got_ref, g_send.at[number], g_recv.at[number], across))
        copies[-1].start()
        copies.append(pltpu.make_async_copy(sums.at[number, 0], own_ref, local.at[2 + number]))
        copies[-1].start()
    act(last)
    for copy in copies:
        copy.wait()
    for kind in range(2):
        own_result(kind).wait()
        for step in range(1, groups):
            result(kind, step).wait()


def run_experts(rows, grads, w_gate, w_up, w_down, far_gate, far_gate_too):
    slots, width = rows.shape
    half = CAP // 2
    groups = slots // half
    units = w_gate.shape[1]
    anywhere = pl.BlockSpec(memory_space=pl.ANY)
    pair = pltpu.SemaphoreType.DMA((2, groups))
    return pl.pallas_call(
        expert_kernel,
        in_specs=[anywhere] * 7,
        out_specs=[anywhere] * 8,
        out_shape=[jax.ShapeDtypeStruct((slots, width), BF16)] * 2
        + [jax.ShapeDtypeStruct((units, width), F32)] * 3
        + [jax.ShapeDtypeStruct((units, width), BF16)] * 3,
        scratch_shapes=[
            pltpu.VMEM((2, groups, half, width), BF16),
            pltpu.VMEM((2, groups, half, width), BF16),
            pltpu.VMEM((3, 2, units, width), BF16),
            pltpu.VMEM((3, 2, units, width), F32),
            pltpu.VMEM((2, groups, half, width), BF16),
        ]
        + [pair] * 8
        + [pltpu.SemaphoreType.DMA((2,))] * 2
        + [pltpu.SemaphoreType.DMA((3,))] * 2
        + [pltpu.SemaphoreType.DMA((7,))],
        compiler_params=pltpu.CompilerParams(
            vmem_limit_bytes=60 * MIB, collective_id=1, has_side_effects=True
        ),
        cost_estimate=cost(72 * slots * units * width, 16 * slots * width + 30 * units * width),
    )(rows, grads, w_gate, w_up, w_down, far_gate, far_gate_too)


def finish_kernel(
    rows_ref, y_ref, summed_ref, small_ref,
    output_ref, grad_ref, in_ref, out_ref, one_ref, two_ref, router_ref, bias_ref,
):
    step = pl.program_id(0)
    output_ref[...] = y_ref[...].astype(F32).T.astype(BF16)
    grad_ref[...] = rows_ref[...].astype(F32).T

    @pl.when(step < 3)
    def _():
        in_ref[...] = summed_ref[...].astype(F32)

    @pl.when(step == 3)
    def _():
        out_ref[...] = summed_ref[...].astype(F32)
        router_ref[...] = small_ref[:EXPERTS]
        two_ref[...] = small_ref[EXPERTS : EXPERTS + 1]
        one_ref[...] = small_ref[EXPERTS + 1 : EXPERTS + 2]
        bias_ref[...] = small_ref[EXPERTS + 2 : EXPERTS + 2 + bias_ref.shape[0], :BUCKETS]


def finish_outputs(rows, y_rows, summed, small, heads):
    tokens, width = rows.shape
    steps = 4
    tile, block = tokens // steps, summed.shape[0] // steps
    token_spec = pl.BlockSpec((tile, width), lambda i: (i, 0))
    feature_spec = pl.BlockSpec((width, tile), lambda i: (0, i))
    whole = lambda *shape: pl.BlockSpec(shape, lambda i: (0, 0))
    return pl.pallas_call(
        finish_kernel,
        grid=(steps,),
        in_specs=[
            token_spec,
            token_spec,
            pl.BlockSpec((block, width), lambda i: (i, 0)),
            whole(*small.shape),
        ],
        out_specs=[
            feature_spec,
            feature_spec,
            pl.BlockSpec((block, width), lambda i: (jnp.minimum(i, 2), 0)),
            whole(block, width),
            whole(1, width),
            whole(1, width),
            whole(EXPERTS, width),
            whole(heads, BUCKETS),
        ],
        out_shape=[
            jax.ShapeDtypeStruct((width, tokens), BF16),
            jax.ShapeDtypeStruct((width, tokens), F32),
            jax.ShapeDtypeStruct((3 * block, width), F32),
            jax.ShapeDtypeStruct((block, width), F32),
            jax.ShapeDtypeStruct((1, width), F32),
            jax.ShapeDtypeStruct((1, width), F32),
            jax.ShapeDtypeStruct((EXPERTS, width), F32),
            jax.ShapeDtypeStruct((heads, BUCKETS), F32),
        ],
        compiler_params=params(),
        cost_estimate=cost(0, 10 * rows.size + 6 * summed.size),
    )(rows, y_rows, summed, small)


def on_device(
    layer_input, gain_one, attn_in, rel_bias, attn_out, gain_two, router,
    expert_gate, expert_up, expert_down, routes, piece_starts, grad_out,
):
    width, tokens = layer_input.shape
    ranks = lax.axis_size("tensor")
    groups = lax.axis_size("expert")
    rank = lax.axis_index("tensor")
    pair_class, half_index = rank % 2, rank // 2
    half = CAP // 2

    units = expert_gate.shape[1]
    other = lax.dynamic_slice(expert_gate, (1 - pair_class, 0, 0), (1, units // 2, width))[0]
    traded = lax.ppermute(other, "tensor", [(r, r ^ 1) for r in range(ranks)])
    gain_col = gain_one[:, None]
    w_in = attn_in.reshape(-1, width)
    qkv, scale_one = project(layer_input, gain_col, w_in)
    tiles = bias_tiles(rel_bias)
    position = jnp.arange(SEQ, dtype=jnp.int32)[None, None, :]
    starts = piece_starts[:, :, None]
    inside = (position >= starts) & (position < starts + PIECE)
    last = jnp.max(jnp.where(inside, starts + (PIECE - 1), -1), axis=1)
    limits = jnp.maximum(last, position[0])[:, None, :]

    routes_t = routes.T
    place = jnp.stack([pair_class, half_index]).astype(jnp.int32)
    share = tokens // ranks

    def by_rank(rows):
        return rows.reshape(ranks, share, width)

    qkv, traded = lax.optimization_barrier((qkv, traded))
    slots = groups * half
    heads = rel_bias.shape[1]
    h2, resid, scale_two, dy, dy_rows, code, code_cols, own_x, mixed, lse, traded_too = exchange_call(
        norm_two_kernel, 2, (tokens, width),
        [qkv, tiles, limits, attn_out, layer_input, gain_two[None], grad_out, routes_t, expert_gate],
        [((share, width), F32), ((share, 1), F32), ((tokens, width), BF16), ((slots, width), BF16)]
        + [((TOP, tokens), jnp.int32), ((tokens, TOP), jnp.int32), ((share, width), BF16)]
        + [(attn_out.shape[:1] + (tokens,), BF16), ((heads * tokens // SEQ, 1, SEQ), F32), (traded.shape, BF16)],
        [pltpu.VMEM((ranks, share, width), BF16), pltpu.VMEM((width, share), BF16), pltpu.VMEM((width, tokens), BF16)]
        + [pltpu.VMEM((tokens, width), BF16), pltpu.VMEM((slots, width), BF16), pltpu.SemaphoreType.DMA((4,))]
        + [pltpu.SemaphoreType.DMA((2,))] * 2,
        (4, 6, 8),
        (2, 3, 9),
    )
    rows, row_grads, gate_rows, gates = dispatch(code, routes_t, router.T, h2, dy_rows)
    ret, back, *weight_grads = run_experts(
        rows, row_grads, expert_gate, expert_up, expert_down, traded, traded_too
    )
    grad_attn, grad_resid, grad_gain_two, grad_router, partial_y = exchange_call(
        norm_two_back_kernel, 3, (tokens, width),
        [ret, back, code, code_cols, gates, routes_t, dy_rows, gate_rows, router.T, h2]
        + [resid, scale_two, dy, gain_two[None]],
        [((share, width), F32), ((1, width), F32), ((EXPERTS, width), F32), ((tokens, width), BF16)],
        [
            pltpu.VMEM((ranks, share, width), BF16),
            pltpu.VMEM((slots, width), BF16),
            pltpu.VMEM((ranks + 3, EXPERTS, share), F32),
            pltpu.VMEM((2 * EXPERTS, share), BF16),
        ]
        + [pltpu.SemaphoreType.DMA((3,))] * 2
        + [pltpu.VMEM((slots, width), BF16)] * 2
        + [pltpu.VMEM((tokens, width), BF16), pltpu.VMEM((share, width), F32), pltpu.VMEM((share, width), BF16)]
        + [pltpu.VMEM((ranks, share, width), BF16), pltpu.SemaphoreType.DMA((9,))],
        (0, 6, 9, 10, 12),
        (3,),
    )

    dq, dk, dv, near, far, y_own = attend_back(
        qkv, tiles, limits, attn_out, grad_attn, lse, by_rank(partial_y), resid
    )
    dq, y_own = lax.optimization_barrier((dq, y_own))
    y_across = lax.ppermute(y_own, "tensor", [(r, r ^ 1) for r in range(ranks)])
    y_along = lax.ppermute(y_own, "tensor", [(r, r ^ 2) for r in range(ranks)])
    weight_rows, sent, grad_gain_one, grad_gate, grad_up, grad_down = project_back(
        place, layer_input, gain_col, gain_one[None], scale_one, w_in, mixed, grad_attn, (dq, dk, dv),
        weight_grads[:3], weight_grads[3:],
    )
    sent, y_across, y_along = lax.optimization_barrier((sent, y_across, y_along))
    summed = lax.psum(weight_rows, "expert")
    small_shape = (BUCKETS, width)
    grad_rows, y_full, small = exchange_call(
        norm_one_back_kernel, 4, sent.shape,
        [by_rank(sent), own_x, scale_one, grad_resid, gain_one[None], y_own, y_across, y_along]
        + [grad_gain_one, grad_gain_two, grad_router, near, far],
        [((ranks, share, width), BF16), (small_shape, F32)],
        [pltpu.VMEM((share, width), BF16), pltpu.VMEM((share, width), F32)]
        + [pltpu.VMEM((4, *small_shape), F32), pltpu.VMEM((groups, *small_shape), BF16), pltpu.VMEM(near.shape, F32), pltpu.VMEM((share, 1), F32)]
        + [pltpu.SemaphoreType.DMA((3,))]
        + [pltpu.SemaphoreType.DMA((2,))] * 2
        + [pltpu.SemaphoreType.DMA((groups,))] * 2,
        (1, 3, 11),
        (0,),
    )
    summed, grad_rows = lax.optimization_barrier((summed, grad_rows))
    layer_output, grad_input, grad_in, grad_attn_out, grad_one, grad_two, grad_router, grad_bias = finish_outputs(
        grad_rows, y_full.reshape(tokens, width), summed, small, rel_bias.shape[1]
    )
    return (
        layer_output,
        grad_input,
        grad_one[0],
        grad_in.reshape(attn_in.shape),
        grad_bias.T,
        grad_attn_out,
        grad_two[0],
        grad_router.T,
        grad_gate,
        grad_up,
        grad_down,
    )


def allowed_pairs(seq_starts):
    position = jnp.arange(SEQ, dtype=jnp.int32)
    inside = (position[:, None] >= seq_starts[None, :]) & (
        position[:, None] < seq_starts[None, :] + PIECE
    )
    numbers = jnp.arange(seq_starts.shape[0], dtype=jnp.int32) + 1
    piece_label = jnp.sum(inside.astype(jnp.int32) * numbers[None, :], axis=1)
    causal = position[None, :] <= position[:, None]
    shared = (piece_label[:, None] == piece_label[None, :]) & (piece_label[:, None] > 0)
    return causal | shared


def slot_table(routes):
    flat_routes = routes.reshape(-1)
    onehot = (flat_routes[:, None] == jnp.arange(EXPERTS, dtype=jnp.int32)[None, :]).astype(
        jnp.int32
    )
    blocks = onehot.reshape(-1, 128, EXPERTS).astype(F32)
    earlier = jnp.tril(jnp.ones((128, 128), F32), -1)
    inside = jnp.einsum("ij,bje->bie", earlier, blocks)
    count = blocks.shape[0]
    carried = jnp.einsum("ab,be->ae", jnp.tril(jnp.ones((count, count), F32), -1), jnp.sum(blocks, axis=1), precision=HIGH)
    before = (inside + carried[:, None, :]).astype(jnp.int32).reshape(onehot.shape)
    slot_number = jnp.sum(before * onehot, axis=1)
    kept_pairs = slot_number < CAP
    slot_index = jnp.where(kept_pairs, flat_routes * CAP + slot_number, EXPERTS * CAP)
    return (slot_index.reshape(routes.shape), kept_pairs.reshape(routes.shape))


def bucket_onehot():
    offsets = jnp.arange(2 * SEQ - 1, dtype=jnp.int32) - (SEQ - 1)
    return (bucket_of(offsets)[:, None] == jnp.arange(BUCKETS, dtype=jnp.int32)[None, :]).astype(
        jnp.float32
    )


def expand_line(line):
    head_count = line.shape[0]
    padded = jnp.concatenate([line, jnp.zeros((head_count, 1), line.dtype)], axis=1)
    tiled = jnp.tile(padded, (1, SEQ))[:, : SEQ * (2 * SEQ - 1)].reshape(
        head_count, SEQ, 2 * SEQ - 1
    )
    return tiled[:, :, SEQ - 1 :]


def fold_line(full_grid):
    head_count = full_grid.shape[0]
    padded = jnp.pad(full_grid, ((0, 0), (0, 0), (SEQ - 1, 0))).reshape(
        head_count, SEQ * (2 * SEQ - 1)
    )
    padded = jnp.pad(padded, ((0, 0), (0, SEQ))).reshape(head_count, SEQ, 2 * SEQ)
    return jnp.sum(padded, axis=1)[:, : 2 * SEQ - 1]


def reduce_heads(tensor_value):
    return lax.psum(tensor_value, "tensor")


def spread_slots(tensor_value):
    return lax.all_gather(tensor_value, "tensor", axis=2, tiled=True)


def owner_exchange(tensor_value):
    return lax.all_to_all(tensor_value, "expert", split_axis=0, concat_axis=0, tiled=True)


def expert_sums(tensor_value):
    return lax.psum_scatter(tensor_value, "tensor", scatter_dimension=2, tiled=True)


def norm_forward(resid, gain, model_width):
    scale = lax.rsqrt(jnp.sum(resid * resid, axis=1) / model_width + EPS)[:, None]
    return (scale, (resid * scale * gain).astype(jnp.bfloat16))


def norm_backward(resid, scale, gain, grad_normed, model_width):
    grad_gain = jnp.sum(grad_normed * resid * scale, axis=0)
    scaled = grad_normed * gain
    inner = jnp.sum(scaled * resid, axis=1)[:, None]
    return (grad_gain, scale * scaled - resid * scale**3 * inner / model_width)


def attend_scores(bias_full, queries, key_rows, seq_starts):
    scores = (
        jnp.einsum("qhe,khe->hqk", queries, key_rows, preferred_element_type=jnp.float32) * 0.125
        + bias_full
    )
    return jnp.where(allowed_pairs(seq_starts)[None], scores, NEG)


def attend_forward(bias_full, inputs):
    queries, key_rows, value_rows, seq_starts = inputs
    scores = attend_scores(bias_full, queries, key_rows, seq_starts)
    row_max = jnp.max(scores, axis=2, keepdims=True)
    exponent = jnp.exp(scores - row_max)
    row_sum_exp = jnp.sum(exponent, axis=2, keepdims=True)
    weights = (exponent / row_sum_exp).astype(jnp.bfloat16)
    mixed_heads = jnp.einsum(
        "hqk,khe->qhe", weights, value_rows, preferred_element_type=jnp.float32
    )
    return (mixed_heads.astype(jnp.bfloat16), (row_max + jnp.log(row_sum_exp))[:, :, 0])


def attend_backward(bias_full, running, inputs):
    queries, key_rows, value_rows, grad_heads, seq_starts, log_total = inputs
    scores = attend_scores(bias_full, queries, key_rows, seq_starts)
    probabilities = jnp.exp(scores - log_total[:, :, None])
    grad_probs = jnp.einsum(
        "qhe,khe->hqk", grad_heads, value_rows, preferred_element_type=jnp.float32
    )
    inner = jnp.sum(probabilities * grad_probs, axis=2, keepdims=True)
    grad_scores = (probabilities * (grad_probs - inner)).astype(jnp.bfloat16)
    grad_values = jnp.einsum(
        "hqk,qhe->khe",
        probabilities.astype(jnp.bfloat16),
        grad_heads,
        preferred_element_type=jnp.float32,
    )
    grad_queries = (
        jnp.einsum("hqk,khe->qhe", grad_scores, key_rows, preferred_element_type=jnp.float32)
        * 0.125
    )
    grad_keys = (
        jnp.einsum("hqk,qhe->khe", grad_scores, queries, preferred_element_type=jnp.float32) * 0.125
    )
    return (
        running + grad_scores.astype(jnp.float32),
        jnp.stack([grad_queries, grad_keys, grad_values]),
    )


def gelu_product(left, right):
    return jax.nn.gelu(left, approximate=True) * right


def expert_forward(received, weight_gate, weight_up, weight_down):
    gate_part = jnp.einsum(
        "secd,efd->secf", received, weight_gate, preferred_element_type=jnp.float32
    )
    up_part = jnp.einsum("secd,efd->secf", received, weight_up, preferred_element_type=jnp.float32)
    hidden = gelu_product(gate_part, up_part).astype(jnp.bfloat16)
    partial_out = jnp.einsum(
        "secf,efd->secd", hidden, weight_down, preferred_element_type=jnp.float32
    )
    return (gate_part, up_part, hidden, partial_out)


def expert_backward(
    received, gate_part, up_part, hidden, grad_rows_out, weight_gate, weight_up, weight_down
):
    grad_hidden = jnp.einsum(
        "secd,efd->secf", grad_rows_out, weight_down, preferred_element_type=jnp.float32
    )
    product_value, pullback = jax.vjp(gelu_product, gate_part, up_part)
    grad_gate_part, grad_up_part = pullback(grad_hidden)
    grad_gate_part = grad_gate_part.astype(jnp.bfloat16)
    grad_up_part = grad_up_part.astype(jnp.bfloat16)
    grad_down = jnp.einsum(
        "secf,secd->efd", hidden, grad_rows_out, preferred_element_type=jnp.float32
    )
    grad_gate_w = jnp.einsum(
        "secf,secd->efd", grad_gate_part, received, preferred_element_type=jnp.float32
    )
    grad_up_w = jnp.einsum(
        "secf,secd->efd", grad_up_part, received, preferred_element_type=jnp.float32
    )
    grad_rows_in = jnp.einsum(
        "secf,efd->secd", grad_gate_part, weight_gate, preferred_element_type=jnp.float32
    )
    grad_rows_in = grad_rows_in + jnp.einsum(
        "secf,efd->secd", grad_up_part, weight_up, preferred_element_type=jnp.float32
    )
    return (grad_gate_w, grad_up_w, grad_down, grad_rows_in)


def on_device_general(
    layer_input,
    gain_one,
    attn_in,
    rel_bias,
    attn_out,
    gain_two,
    router,
    expert_gate,
    expert_up,
    expert_down,
    routes,
    piece_starts,
    grad_out,
):
    tok_count = layer_input.shape[1]
    model_width = layer_input.shape[0]
    heads_here = rel_bias.shape[1]
    head_width = attn_in.shape[1] // heads_here
    seqs_here = piece_starts.shape[0]
    local_experts = expert_gate.shape[0]
    part_rows = CAP // lax.axis_size("tensor")
    share_start = lax.axis_index("tensor") * part_rows
    tokens = layer_input.T.astype(jnp.float32)
    scale_one, normed = norm_forward(tokens, gain_one, model_width)
    project = jnp.einsum("td,chd->cth", normed, attn_in, preferred_element_type=jnp.float32).astype(
        jnp.bfloat16
    )
    by_seq = project.reshape(3, seqs_here, SEQ, heads_here, head_width)
    onehot_line = bucket_onehot()
    bias_full = expand_line(jnp.dot(onehot_line, rel_bias, precision=HIGH).T)
    mixed_heads, log_total = lax.map(
        partial(attend_forward, bias_full), (by_seq[0], by_seq[1], by_seq[2], piece_starts)
    )
    mixed_heads = mixed_heads.reshape(tok_count, heads_here * head_width)
    resid = tokens + reduce_heads(
        jnp.dot(mixed_heads, attn_out, preferred_element_type=jnp.float32)
    )
    scale_two, normed_two = norm_forward(resid, gain_two, model_width)
    logits = jnp.dot(normed_two, router, preferred_element_type=jnp.float32)
    chosen = (routes[:, :, None] == jnp.arange(EXPERTS, dtype=jnp.int32)[None, None, :]).astype(
        jnp.float32
    )
    picked = jnp.sum(chosen * logits[:, None, :], axis=2)
    gate_weights = jax.nn.softmax(picked, axis=1)
    slot_index, kept_pairs = slot_table(routes)
    keep_float = kept_pairs.astype(jnp.float32)
    mix_weight = gate_weights * keep_float
    safe_index = jnp.minimum(slot_index, EXPERTS * CAP - 1)
    token_rows = jnp.repeat(normed_two, TOP, axis=0)
    buffer = (
        jnp.zeros((EXPERTS * CAP + 1, model_width), jnp.bfloat16)
        .at[slot_index.reshape(-1)]
        .set(token_rows)
    )
    buffer = buffer[: EXPERTS * CAP].reshape(-1, local_experts, CAP, model_width)
    received = lax.all_to_all(buffer, "expert", split_axis=0, concat_axis=0, tiled=True)
    gate_part, up_part, hidden, partial_out = expert_forward(
        received, expert_gate, expert_up, expert_down
    )
    returned = spread_slots(owner_exchange(expert_sums(partial_out).astype(jnp.bfloat16)))
    flat_ret = returned.reshape(EXPERTS * CAP, model_width)
    fetched = flat_ret[safe_index].astype(jnp.float32)
    output = resid + jnp.sum(mix_weight[:, :, None] * fetched, axis=1)
    grad_y = grad_out.T.astype(jnp.float32)
    grad_gates = jnp.sum(grad_y[:, None, :] * fetched, axis=2) * keep_float
    grad_picked = gate_weights * (
        grad_gates - jnp.sum(gate_weights * grad_gates, axis=1, keepdims=True)
    )
    grad_logits = jnp.sum(chosen * grad_picked[:, :, None], axis=1)
    grad_router = jnp.dot(normed_two.astype(jnp.float32).T, grad_logits, precision=HIGH)
    grad_normed_two = jnp.dot(grad_logits, router.astype(jnp.float32).T, precision=HIGH)
    slot_grads = (mix_weight[:, :, None] * grad_y[:, None, :]).astype(jnp.bfloat16)
    grad_ret = (
        jnp.zeros((EXPERTS * CAP + 1, model_width), jnp.bfloat16)
        .at[slot_index.reshape(-1)]
        .set(slot_grads.reshape(-1, model_width))
    )
    grad_ret = grad_ret[: EXPERTS * CAP].reshape(-1, local_experts, CAP, model_width)
    grad_share = lax.dynamic_slice_in_dim(grad_ret, share_start, part_rows, 2)
    grad_rows_out = spread_slots(owner_exchange(grad_share))
    grad_expert_gate, grad_expert_up, grad_expert_down, grad_rows_in = expert_backward(
        received, gate_part, up_part, hidden, grad_rows_out, expert_gate, expert_up, expert_down
    )
    grad_back = spread_slots(owner_exchange(expert_sums(grad_rows_in).astype(jnp.bfloat16)))
    flat_back = grad_back.reshape(EXPERTS * CAP, model_width).astype(jnp.float32)
    grad_normed_two = grad_normed_two + jnp.sum(
        flat_back[safe_index] * keep_float[:, :, None], axis=1
    )
    grad_gain_two, grad_resid = norm_backward(
        resid, scale_two, gain_two, grad_normed_two, model_width
    )
    grad_resid = grad_resid + grad_y
    grad_attn = grad_resid.astype(jnp.bfloat16)
    grad_attn_out = jnp.einsum(
        "th,td->hd", mixed_heads, grad_attn, preferred_element_type=jnp.float32
    )
    grad_mixed = jnp.einsum(
        "td,hd->th", grad_attn, attn_out, preferred_element_type=jnp.float32
    ).astype(jnp.bfloat16)
    grad_by_seq = grad_mixed.reshape(seqs_here, SEQ, heads_here, head_width)
    bias_grad_full, grad_project = lax.scan(
        partial(attend_backward, bias_full),
        jnp.zeros_like(bias_full),
        (by_seq[0], by_seq[1], by_seq[2], grad_by_seq, piece_starts, log_total),
    )
    grad_project = (
        jnp.moveaxis(grad_project, 1, 0)
        .reshape(3, tok_count, heads_here * head_width)
        .astype(jnp.bfloat16)
    )
    grad_attn_in = jnp.einsum(
        "cth,td->chd", grad_project, normed, preferred_element_type=jnp.float32
    )
    grad_normed = reduce_heads(
        jnp.einsum("cth,chd->td", grad_project, attn_in, preferred_element_type=jnp.float32)
    )
    grad_gain_one, grad_tokens = norm_backward(
        tokens, scale_one, gain_one, grad_normed, model_width
    )
    grad_tokens = grad_tokens + grad_resid
    grad_rel_bias = jnp.dot(onehot_line.T, fold_line(bias_grad_full).T, precision=HIGH)
    shared = (
        lax.psum(grad_gain_one.astype(jnp.bfloat16), "expert").astype(jnp.float32),
        lax.psum(grad_attn_in.astype(jnp.bfloat16), "expert").astype(jnp.float32),
        lax.psum(grad_rel_bias.astype(jnp.bfloat16), "expert").astype(jnp.float32),
        lax.psum(grad_attn_out.astype(jnp.bfloat16), "expert").astype(jnp.float32),
        lax.psum(grad_gain_two.astype(jnp.bfloat16), "expert").astype(jnp.float32),
        lax.psum(grad_router.astype(jnp.bfloat16), "expert").astype(jnp.float32),
    )
    return (
        output.astype(jnp.bfloat16).T,
        grad_tokens.T,
        shared[0],
        shared[1],
        shared[2],
        shared[3],
        shared[4],
        shared[5],
        grad_expert_gate,
        grad_expert_up,
        grad_expert_down,
    )


def solution(mesh):
    placed = (
        P(None, "expert"),
        P(),
        P(None, "tensor", None),
        P(None, "tensor"),
        P("tensor", None),
        P(),
        P(),
        P("expert", "tensor", None),
        P("expert", "tensor", None),
        P("expert", "tensor", None),
        P("expert", None),
        P("expert", None),
        P(None, "expert"),
    )
    paired = mesh.shape["tensor"] == 4 and mesh.shape["expert"] * 2 == EXPERTS
    return jax.shard_map(
        on_device if paired else on_device_general,
        mesh=mesh,
        in_specs=placed,
        out_specs=(
            P(None, "expert"),
            P(None, "expert"),
            P(),
            P(None, "tensor", None),
            P(None, "tensor"),
            P("tensor", None),
            P(),
            P(),
            P("expert", "tensor", None),
            P("expert", "tensor", None),
            P("expert", "tensor", None),
        ),
        check_vma=False,
    )
```

```python
from functools import partial

import jax
import jax.numpy as jnp
from jax import lax
from jax.experimental import pallas as pl
from jax.experimental.pallas import tpu as pltpu
from jax.sharding import PartitionSpec as P

EXPERTS = 16
BUCKETS = 32
TOP = 2
PIECE = 256
SEQ = 1024
CAP = 320
BLK = 256


EPS = 1e-06
NEG = -1e30
THRESHOLDS = (12, 16, 23, 32, 46, 64, 91)
HIGH = lax.Precision.HIGHEST
F32 = jnp.float32
BF16 = jnp.bfloat16
NN = (((1,), (0,)), ((), ()))
NT = (((1,), (1,)), ((), ()))
TN = (((0,), (0,)), ((), ()))
MIB = 1 << 20


def mm(left, right, dims=NN):
    return lax.dot_general(left, right, dims, preferred_element_type=F32)


def params(limit=56):
    return pltpu.CompilerParams(vmem_limit_bytes=limit * MIB)


def cost(flops, bytes_accessed, transcendentals=0):
    return pl.CostEstimate(
        flops=int(flops), bytes_accessed=int(bytes_accessed), transcendentals=int(transcendentals)
    )


def bucket_of(offset):
    magnitude = jnp.abs(offset)
    beyond = sum(((magnitude >= threshold).astype(jnp.int32) for threshold in THRESHOLDS))
    lower_part = jnp.where(magnitude < 8, magnitude, 8 + beyond)
    return lower_part + 16 * (offset > 0).astype(jnp.int32)


def project_kernel(x_ref, gain_ref, w_ref, out_ref, scale_ref):
    x = x_ref[...].astype(F32)
    scale = lax.rsqrt(jnp.sum(x * x, axis=0, keepdims=True) / x.shape[0] + EPS)
    normed = (x * scale * gain_ref[...]).astype(BF16)
    out_ref[...] = mm(w_ref[...], normed).astype(BF16)
    scale_ref[...] = scale


def project(x, gain, weights):
    width, tokens = x.shape
    rows = weights.shape[0]
    tile = 512
    return pl.pallas_call(
        project_kernel,
        grid=(tokens // tile,),
        in_specs=[
            pl.BlockSpec((width, tile), lambda i: (0, i)),
            pl.BlockSpec((width, 1), lambda i: (0, 0)),
            pl.BlockSpec((rows, width), lambda i: (0, 0)),
        ],
        out_specs=[
            pl.BlockSpec((rows, tile), lambda i: (0, i)),
            pl.BlockSpec((1, tile), lambda i: (0, i)),
        ],
        out_shape=[
            jax.ShapeDtypeStruct((rows, tokens), BF16),
            jax.ShapeDtypeStruct((1, tokens), F32),
        ],
        compiler_params=params(),
        cost_estimate=cost(2 * width * tokens * rows, 2 * width * tokens * 2),
    )(x, gain, weights)


def line_offsets(number):
    column = lax.broadcasted_iota(jnp.int32, (8, BLK), 1)
    return (number - 1) * BLK - column


def bias_tiles_kernel(table_ref, tiles_ref):
    row = lax.broadcasted_iota(jnp.int32, (BLK, BLK), 0)
    column = lax.broadcasted_iota(jnp.int32, (BLK, BLK), 1)
    buckets = [bucket_of(line_offsets(number)) for number in range(4)]
    for head in range(tiles_ref.shape[0]):
        far = table_ref[15, head]
        rolled = []
        for number, bucket in enumerate(buckets):
            value = jnp.zeros((8, BLK), F32)
            for index in range(BUCKETS):
                value = jnp.where(bucket == index, table_ref[index, head] - far, value)
            whole = jnp.broadcast_to(value[0:1], (BLK, BLK))
            rolled.append(pltpu.roll(whole, 0, 1, stride=1, stride_axis=0))
        for number in range(3):
            tiles_ref[head, number] = jnp.where(column >= row, rolled[number], rolled[number + 1])


def bias_tiles(table):
    heads = table.shape[1]
    return pl.pallas_call(
        bias_tiles_kernel,
        in_specs=[pl.BlockSpec(memory_space=pltpu.SMEM)],
        out_specs=pl.BlockSpec(memory_space=pltpu.VMEM),
        out_shape=jax.ShapeDtypeStruct((heads, 3, BLK, BLK), F32),
        compiler_params=params(),
        cost_estimate=cost(heads * 3 * BLK * BLK * 60, heads * 3 * BLK * BLK * 4),
    )(table)


def bias_fold(near_ref, far_ref):
    heads = near_ref.shape[0] // 2
    sums = jnp.zeros((BUCKETS, 128), F32)
    lane = lax.broadcasted_iota(jnp.int32, (BUCKETS, 128), 1)
    row = lax.broadcasted_iota(jnp.int32, (BLK, BLK), 0)
    column = lax.broadcasted_iota(jnp.int32, (BLK, BLK), 1)
    flip = jnp.where(row + column == BLK - 1, 1.0, 0.0).astype(BF16)
    apart = jnp.where(column == BLK - 1, 0, column + 1)
    ahead = apart <= row
    number_at = lax.broadcasted_iota(jnp.int32, (BUCKETS, BLK), 0)
    for head in range(heads):
        lines = [jnp.zeros((1, BLK), F32) for _ in range(4)]
        for number in range(3):
            grads = near_ref[head, number] + near_ref[heads + head, number]
            coarse = grads.astype(BF16)
            fine = (grads - coarse.astype(F32)).astype(BF16)
            flipped = mm(flip, coarse) + mm(flip, fine)
            rolled = pltpu.roll(flipped, 0, 1, stride=1, stride_axis=0)
            lines[number] += jnp.sum(jnp.where(ahead, rolled, 0.0), axis=0, keepdims=True)
            lines[number + 1] += jnp.sum(jnp.where(ahead, 0.0, rolled), axis=0, keepdims=True)
        total = jnp.zeros((BUCKETS, 1), F32)
        for number, line in enumerate(lines):
            bucket = bucket_of((number - 1) * BLK - apart[:1])
            total += jnp.sum(jnp.where(bucket == number_at, line, 0.0), axis=1, keepdims=True)
        distant = jnp.sum(far_ref[head] + far_ref[heads + head], axis=0, keepdims=True)
        distant = jnp.sum(distant, axis=1, keepdims=True)
        total += jnp.where(number_at[:, :1] == 15, distant, 0.0)
        sums = jnp.where(lane == head, total, sums)
    return sums


def key_count(query_block):
    return 2 * BLK if query_block < 2 else 4 * BLK


def block_scores(keys, queries, tile_of, limit, block):
    count = key_count(block)
    parts = []
    whole = mm(keys[:, :count], queries, TN)
    for key_block in range(count // BLK):
        part = whole[key_block * BLK : (key_block + 1) * BLK]
        shift = key_block - block
        if -1 <= shift <= 1:
            part = part + tile_of(shift)
        if shift >= 0:
            key_at = lax.broadcasted_iota(jnp.int32, (BLK, BLK), 0) + key_block * BLK
            part = jnp.where(key_at <= limit, part, NEG)
        parts.append(part)
    return jnp.concatenate(parts, axis=0)


def attend_half(qkv_ref, tiles_ref, limit_ref, mixed_ref, lse_ref, seq, half):
    heads = tiles_ref.shape[0]
    width = mixed_ref.shape[0] // heads
    base = pl.multiple_of(seq * SEQ, SEQ)

    def one_head(head, carry):
        at = lambda kind: pl.ds(pl.multiple_of((kind * heads + head) * width, width), width)
        keys, values = qkv_ref[at(1), pl.ds(base, SEQ)], qkv_ref[at(2), pl.ds(base, SEQ)]
        for block in (2 * half, 2 * half + 1):
            cols = pl.ds(pl.multiple_of(base + block * BLK, BLK), BLK)
            span = slice(block * BLK, (block + 1) * BLK)
            queries = qkv_ref[at(0), cols] * BF16(0.125)
            scores = block_scores(
                keys, queries, lambda shift: tiles_ref[head, shift + 1], limit_ref[seq, :, span], block
            )
            top = jnp.max(scores, axis=0, keepdims=True)
            exponent = jnp.exp(scores - top)
            total = jnp.sum(exponent, axis=0, keepdims=True)
            mixed = mm(values[:, : key_count(block)], exponent.astype(BF16)) / total
            mixed_ref[at(0), cols] = mixed.astype(BF16)
            lse_ref[seq * heads + head, :, span] = top + jnp.log(total)
        return carry

    lax.fori_loop(0, heads, one_head, 0)


def attend_back_kernel(
    q_ref, k_ref, v_ref, tiles_ref, limit_ref, w_ref, grad_ref, lse_ref, part_ref, resid_ref,
    dq_ref, dk_ref, dv_ref, near_ref, far_ref, y_ref,
    held, parts, total, turn_across, turn_along, from_across, from_along, sends, recvs, loads,
):
    rank = lax.axis_index("tensor")
    pair_class, half_index = rank % 2, rank // 2
    across, along, corner = rank + 1 - 2 * pair_class, rank + 2 - 4 * half_index, 3 - rank
    step = pl.program_id(0) * pl.num_programs(1) + pl.program_id(1)
    mesh_ids = pl.DeviceIdType.MESH
    middle = parts.shape[2] // 2
    low, high = slice(0, middle), slice(middle, 2 * middle)

    def remote(number, origin, target, other):
        return pltpu.make_async_remote_copy(
            src_ref=origin, dst_ref=target, send_sem=sends.at[number], recv_sem=recvs.at[number],
            device_id={"tensor": other}, device_id_type=mesh_ids,
        )

    first = (
        remote(0, part_ref.at[corner, :, low], turn_across, across),
        remote(1, part_ref.at[corner, :, high], turn_along, along),
    )
    second = remote(2, parts.at[0], from_across, across), remote(3, parts.at[1], from_along, along)
    local = [
        pltpu.make_async_copy(part_ref.at[other], parts.at[number], loads.at[number])
        for number, other in enumerate((across, along, rank))
    ]
    local.append(pltpu.make_async_copy(resid_ref, total, loads.at[3]))

    @pl.when(step == 0)
    def _():
        barrier = pltpu.get_barrier_semaphore()
        for other in (across, along):
            pl.semaphore_signal(barrier, inc=1, device_id={"tensor": other}, device_id_type=mesh_ids)
        pl.semaphore_wait(barrier, 2)
        for copy in first:
            copy.start()
        for copy in local:
            copy.start()

    @pl.when(step == 3)
    def _():
        for copy in (*first, *local):
            copy.wait()
        parts[0, :, high] = (parts[0, :, high].astype(F32) + turn_along[...].astype(F32)).astype(BF16)
        parts[1, :, low] = (parts[1, :, low].astype(F32) + turn_across[...].astype(F32)).astype(BF16)
        for copy in second:
            copy.start()

    head = pl.program_id(1)
    width = q_ref.shape[0]

    @pl.when(head == 0)
    def _():
        held[...] = mm(w_ref[...], grad_ref[...], NT).astype(BF16)

    queries = q_ref[...] * BF16(0.125)
    keys, values = k_ref[...], v_ref[...]
    grads = held[pl.ds(pl.multiple_of(head * width, width), width), :]
    near_ref[...] = jnp.zeros_like(near_ref)
    far = jnp.zeros((8, BLK), F32)
    grad_keys = jnp.zeros((width, SEQ), F32)
    grad_values = jnp.zeros((width, SEQ), F32)
    for block in range(SEQ // BLK):
        count = key_count(block)
        cols = slice(block * BLK, (block + 1) * BLK)
        scores = block_scores(
            keys, queries[:, cols], lambda shift: tiles_ref[0, shift + 1], limit_ref[0, :, cols], block
        )
        probs = jnp.exp(scores - lse_ref[0, :, cols])
        grad_probs = mm(values[:, :count], grads[:, cols], TN)
        inner = jnp.sum(probs * grad_probs, axis=0, keepdims=True)
        grad_scores = probs * (grad_probs - inner)
        for key_block in range(count // BLK):
            part = grad_scores[key_block * BLK : (key_block + 1) * BLK]
            shift = key_block - block
            if -1 <= shift <= 1:
                near_ref[0, shift + 1] += part
            elif shift < -1:
                far = far + jnp.sum(part.reshape(BLK // 8, 8, BLK), axis=0)
        rounded = grad_scores.astype(BF16)
        add_values = mm(grads[:, cols], probs.astype(BF16), NT)
        add_keys = mm(queries[:, cols], rounded, NT)
        if count == SEQ:
            grad_values = grad_values + add_values
            grad_keys = grad_keys + add_keys
        else:
            filler = jnp.zeros((width, SEQ - count), F32)
            grad_values = grad_values + jnp.concatenate([add_values, filler], axis=1)
            grad_keys = grad_keys + jnp.concatenate([add_keys, filler], axis=1)
        dq_ref[:, cols] = (mm(keys[:, :count], rounded) * 0.125).astype(BF16)
    dk_ref[...] = grad_keys.astype(BF16)
    dv_ref[...] = grad_values.astype(BF16)
    far_ref[0] = far

    @pl.when(step == 7)
    def _():
        for copy in second:
            copy.wait()
        summed = parts[2].astype(F32) + from_across[...].astype(F32) + from_along[...].astype(F32)
        y_ref[...] = (total[...] + summed).astype(BF16)


def attend_back(qkv, tiles, limits, attn_out, grad_attn, lse, part, resid):
    heads = tiles.shape[0]
    seqs = limits.shape[0]
    width = qkv.shape[0] // (3 * heads)
    model_width = attn_out.shape[1]
    share = part.shape[1]
    grad_spec = pl.BlockSpec((width, SEQ), lambda s, h: (h, s))
    anywhere = pl.BlockSpec(memory_space=pl.ANY)
    return pl.pallas_call(
        attend_back_kernel,
        grid=(seqs, heads),
        in_specs=[
            pl.BlockSpec((width, SEQ), lambda s, h: (h, s)),
            pl.BlockSpec((width, SEQ), lambda s, h: (heads + h, s)),
            pl.BlockSpec((width, SEQ), lambda s, h: (2 * heads + h, s)),
            pl.BlockSpec((1, 3, BLK, BLK), lambda s, h: (h, 0, 0, 0)),
            pl.BlockSpec((1, 1, SEQ), lambda s, h: (s, 0, 0)),
            pl.BlockSpec((heads * width, model_width), lambda s, h: (0, 0)),
            pl.BlockSpec((SEQ, model_width), lambda s, h: (s, 0)),
            pl.BlockSpec((1, 1, SEQ), lambda s, h: (s * heads + h, 0, 0)),
        ]
        + [anywhere] * 2,
        out_specs=[
            grad_spec,
            grad_spec,
            grad_spec,
            pl.BlockSpec((1, 3, BLK, BLK), lambda s, h: (s * heads + h, 0, 0, 0)),
            pl.BlockSpec((1, 8, BLK), lambda s, h: (s * heads + h, 0, 0)),
            pl.BlockSpec((share, model_width), lambda s, h: (0, 0)),
        ],
        out_shape=[jax.ShapeDtypeStruct((heads * width, seqs * SEQ), BF16)] * 3
        + [
            jax.ShapeDtypeStruct((seqs * heads, 3, BLK, BLK), F32),
            jax.ShapeDtypeStruct((seqs * heads, 8, BLK), F32),
        ]
        + [jax.ShapeDtypeStruct((share, model_width), BF16)],
        scratch_shapes=[
            pltpu.VMEM((heads * width, SEQ), BF16),
            pltpu.VMEM((3, share, model_width), BF16),
            pltpu.VMEM((share, model_width), F32),
            pltpu.VMEM((share, model_width // 2), BF16),
            pltpu.VMEM((share, model_width // 2), BF16),
            pltpu.VMEM((share, model_width), BF16),
            pltpu.VMEM((share, model_width), BF16),
            pltpu.SemaphoreType.DMA((4,)),
            pltpu.SemaphoreType.DMA((4,)),
            pltpu.SemaphoreType.DMA((4,)),
        ],
        compiler_params=pltpu.CompilerParams(
            vmem_limit_bytes=60 * MIB, collective_id=5, has_side_effects=True
        ),
        cost_estimate=cost(seqs * heads * SEQ * SEQ * 1280, seqs * heads * SEQ * 4096, seqs * heads * SEQ * SEQ),
    )(qkv, qkv, qkv, tiles, limits, attn_out, grad_attn, lse, part, resid)


def project_back_kernel(
    place_ref, x_ref, gain_ref, gain_row_ref, scale_ref, w_ref, mixed_ref, attn_ref, dq_ref, dk_ref, dv_ref, *refs
):
    step = pl.program_id(0)
    own_refs, got_refs, (weight_ref, out_ref, gain_grad_ref), placed_refs, total = (
        refs[:3], refs[3:6], refs[6:9], refs[9:12], refs[12]
    )
    for own_ref, got_ref, placed_ref in zip(own_refs, got_refs, placed_refs):
        placed_ref[place_ref[0]] = own_ref[...]
        placed_ref[1 - place_ref[0]] = got_ref[...].astype(F32)
    grads = jnp.concatenate([dq_ref[...], dk_ref[...], dv_ref[...]], axis=0)
    rows = grads.shape[0]
    normed = (x_ref[...].astype(F32) * scale_ref[...] * gain_ref[...]).astype(BF16)

    @pl.when(step == 0)
    def _():
        total[...] = jnp.zeros_like(total)

    total[:rows] += mm(grads, normed, NT)
    total[rows:] += mm(mixed_ref[...], attn_ref[...])
    out_ref[...] = mm(grads, w_ref[...], TN).astype(BF16)

    @pl.when(step == pl.num_programs(0) - 1)
    def _():
        weight_ref[...] = total[...].astype(BF16)
        through = jnp.sum(total[:rows] * w_ref[...].astype(F32), axis=0, keepdims=True)
        gain_grad_ref[...] = through / gain_row_ref[...]


def project_back(place, x, gain, gain_row, scale, weights, mixed, grad_attn, grads, owns, gots):
    width, tokens = x.shape
    rows = weights.shape[0]
    heads_width = mixed.shape[0]
    units = owns[0].shape[0]
    steps = 4
    tile = tokens // steps
    part = units // steps
    column = lambda count: pl.BlockSpec((count, tile), lambda i: (0, i))
    return pl.pallas_call(
        project_back_kernel,
        grid=(steps,),
        in_specs=[
            pl.BlockSpec(memory_space=pltpu.SMEM),
            column(width),
            pl.BlockSpec((width, 1), lambda i: (0, 0)),
            pl.BlockSpec((1, width), lambda i: (0, 0)),
            column(1),
            pl.BlockSpec((rows, width), lambda i: (0, 0)),
            column(heads_width),
            pl.BlockSpec((tile, width), lambda i: (i, 0)),
        ]
        + [column(rows // 3)] * 3
        + [pl.BlockSpec((part, width), lambda i: (i, 0))] * 6,
        out_specs=[
            pl.BlockSpec((rows + heads_width, width), lambda i: (0, 0)),
            pl.BlockSpec((tile, width), lambda i: (i, 0)),
            pl.BlockSpec((1, width), lambda i: (0, 0)),
        ]
        + [pl.BlockSpec((2, part, width), lambda i: (0, i, 0))] * 3,
        out_shape=[
            jax.ShapeDtypeStruct((rows + heads_width, width), BF16),
            jax.ShapeDtypeStruct((tokens, width), BF16),
            jax.ShapeDtypeStruct((1, width), F32),
        ]
        + [jax.ShapeDtypeStruct((2, units, width), F32)] * 3,
        scratch_shapes=[pltpu.VMEM((rows + heads_width, width), F32)],
        compiler_params=params(),
        cost_estimate=cost(5 * width * tokens * rows, 6 * width * tokens + 14 * units * width),
    )(place, x, gain, gain_row, scale, weights, mixed, grad_attn, *grads, *owns, *gots)


def exchange(
    math, rank, source, full_out, full, from_across, from_along, to_across, to_along, turn_across, turn_along, sends, recvs, outs, ready=None, ready_full=None, side=None, peers=(), fill=None, start=None, cut=None, later=None):
    pair_class, half_index = rank % 2, rank // 2
    across, along, corner = rank + 1 - 2 * pair_class, rank + 2 - 4 * half_index, 3 - rank
    mesh_ids = pl.DeviceIdType.MESH
    rows, width = source.shape[1:]
    chunks = 4
    size = rows // chunks
    cut = cut or width // 2
    low, high = slice(0, cut), slice(cut, width)
    barrier = pltpu.get_barrier_semaphore()
    near = (across, along, corner) if later else (across, along)
    for other in near:
        pl.semaphore_signal(barrier, inc=1, device_id={"tensor": other}, device_id_type=mesh_ids)
    for other in peers:
        pl.semaphore_signal(barrier, inc=1, device_id={"expert": other}, device_id_type=mesh_ids)
    pl.semaphore_wait(barrier, len(near) + len(peers))

    def remote(kind, chunk, origin, target, other):
        return pltpu.make_async_remote_copy(
            src_ref=origin, dst_ref=target, send_sem=sends.at[kind, chunk], recv_sem=recvs.at[kind, chunk],
            device_id={"tensor": other}, device_id_type=mesh_ids,
        )

    if start:
        start()
    if fill:
        fill(corner)
    spans = [slice(chunk * size, (chunk + 1) * size) for chunk in range(chunks)]
    first, second, third, fourth = [], [], [], []
    for chunk, span in enumerate(spans):
        pair = (
            remote(0, chunk, source.at[corner, span, low], turn_across.at[span, low], across),
            remote(1, chunk, source.at[corner, span, high], turn_along.at[span, high], along),
        )
        for copy in pair:
            copy.start()
        first.append(pair)
    if fill:
        fill(along)
        fill(across)
    leaving = []

    def leave(number, other):
        leaving.append(pltpu.make_async_copy(full.at[other], full_out.at[other], outs.at[number]))
        leaving[-1].start()

    if ready is not None:
        _, near_across, near_along = ready
        extra = [
            remote(8, 0, near_along.at[:, low], ready_full.at[along, :, low], across),
            remote(8, 1, near_across.at[:, high], ready_full.at[across, :, high], along),
        ]
        extra += [
            pltpu.make_async_copy(piece, ready_full.at[other], outs.at[4 + number])
            for number, (other, piece) in enumerate(zip((rank, across, along), ready))
        ]
        for copy in extra:
            copy.start()
    for chunk, span in enumerate(spans):
        if side:
            side(chunk)
        first[chunk][0].wait()
        to_along[span, low] = (source[along, span, low].astype(F32) + turn_across[span, low].astype(F32)).astype(BF16)
        to_along[span, high] = source[along, span, high]
        first[chunk][1].wait()
        to_across[span, low] = source[across, span, low]
        to_across[span, high] = (source[across, span, high].astype(F32) + turn_along[span, high].astype(F32)).astype(BF16)
        pair = (
            remote(2, chunk, to_across.at[span], from_across.at[span], across),
            remote(3, chunk, to_along.at[span], from_along.at[span], along),
        )
        for copy in pair:
            copy.start()
        second.append(pair)
    def pass_on(chunk):
        span = spans[chunk]
        for copy in third[chunk]:
            copy.wait()
        pair = (
            remote(6, chunk, full.at[along, span, low], full.at[along, span, low], across),
            remote(7, chunk, full.at[across, span, high], full.at[across, span, high], along),
        )
        for copy in pair:
            copy.start()
        fourth.append(pair)

    if fill:
        fill(rank)
    if later:
        later((across, along, corner))
    for chunk, span in enumerate(spans):
        if side:
            side(chunks + chunk)
        for copy in second[chunk]:
            copy.wait()
        total = source[rank, span].astype(F32) + from_across[span].astype(F32) + from_along[span].astype(F32)
        full[rank, span] = math(span, total).astype(BF16)
        pair = (
            remote(4, chunk, full.at[rank, span], full.at[rank, span], across),
            remote(5, chunk, full.at[rank, span], full.at[rank, span], along),
        )
        for copy in pair:
            copy.start()
        third.append(pair)
        if chunk:
            pass_on(chunk - 1)
    leave(0, rank)
    pass_on(chunks - 1)
    leave(1, across)
    leave(2, along)
    if ready is not None:
        for copy in extra:
            copy.wait()
    if side and later:
        side(2 * chunks)
    for pair in fourth:
        for copy in pair:
            copy.wait()
    leave(3, corner)
    if side and not later:
        side(2 * chunks)
    for copy in leaving:
        copy.wait()


def exchange_call(kernel, number, shape, operands, extra_shapes, scratch=(), in_hbm=(), out_hbm=()):
    tokens, width = shape
    ranks = 4
    rows = tokens // ranks
    here = pl.BlockSpec(memory_space=pltpu.VMEM)
    results = pl.pallas_call(
        kernel,
        in_specs=[pl.BlockSpec(memory_space=pl.ANY) if k in in_hbm else here for k in range(len(operands))],
        out_specs=[pl.BlockSpec(memory_space=pl.ANY)]
        + [pl.BlockSpec(memory_space=pl.ANY) if k in out_hbm else here for k in range(len(extra_shapes))],
        out_shape=[jax.ShapeDtypeStruct((ranks, rows, width), BF16)]
        + [jax.ShapeDtypeStruct(shape, kind) for shape, kind in extra_shapes],
        scratch_shapes=[pltpu.VMEM((ranks, rows, width), BF16)]
        + [pltpu.VMEM((rows, width), BF16)] * 6
        + [pltpu.SemaphoreType.DMA((9, 4))] * 2
        + [pltpu.SemaphoreType.DMA((7,))]
        + list(scratch),
        compiler_params=pltpu.CompilerParams(
            vmem_limit_bytes=60 * MIB, collective_id=number, has_side_effects=True
        ),
        cost_estimate=cost(40 * MIB, 200 * MIB),
    )(*operands)
    return results[0].reshape(tokens, width), *results[1:]


def norm_two_kernel(
    qkv_ref, tiles_ref, limit_ref, w_ref, x_ref, gain_ref, grad_out_ref, routes_ref, gate_ref,
    full, resid_ref, scale_ref, dy_out, dy_rows_out, code_ref, codes_ref, own_ref, mixed_ref, lse_ref, got_gate, *rest,
):
    source, held, grad_out, dy_ref, dy_rows_ref, load, send, recv = rest[-8:]
    rank = lax.axis_index("tensor")
    ranks, rows, width = source.shape
    loading = pltpu.make_async_copy(grad_out_ref, grad_out, load.at[1])
    storing = [
        pltpu.make_async_copy(dy_ref, dy_out, load.at[2]),
        pltpu.make_async_copy(dy_rows_ref, dy_rows_out, load.at[3]),
    ]

    pair_class = rank % 2
    part = got_gate.shape[0] // 2
    swaps = [
        pltpu.make_async_remote_copy(
            src_ref=gate_ref.at[1 - pair_class, pl.ds((2 + piece) * part, part)],
            dst_ref=got_gate.at[pl.ds(piece * part, part)],
            send_sem=send.at[piece],
            recv_sem=recv.at[piece],
            device_id={"tensor": rank + 1 - 2 * pair_class},
            device_id_type=pl.DeviceIdType.MESH,
        )
        for piece in range(2)
    ]

    def start():
        own.start()
        loading.start()
        swaps[0].start()

    def fill(shard):
        for half in range(2):
            pl.when(shard % 2 == half)(
                partial(attend_half, qkv_ref, tiles_ref, limit_ref, mixed_ref, lse_ref, shard // 2, half)
            )
        columns = pl.ds(pl.multiple_of(shard * rows, rows), rows)
        source[shard] = mm(mixed_ref[:, columns], w_ref[...], TN).astype(BF16)

    slots = dy_rows_ref.shape[0] // ranks
    own = pltpu.make_async_copy(x_ref.at[:, pl.ds(pl.multiple_of(rank * rows, rows), rows)], held, load.at[0])

    def math(span, total):
        resid = own_ref[span, :].astype(F32) + total
        scale = lax.rsqrt(jnp.sum(resid * resid, axis=1, keepdims=True) / resid.shape[1] + EPS)
        resid_ref[span, :] = resid
        scale_ref[span, :] = scale
        return resid * scale * gain_ref[...]

    def later(others):
        own.wait()
        own_ref[...] = held[...].astype(F32).T.astype(BF16)
        local_codes(routes_ref, code_ref, pair_class, rank // 2, CAP // 2)
        codes_ref[...] = jnp.concatenate([code_ref[...].astype(F32)] * 4, axis=0).T[:, :TOP].astype(jnp.int32)
        loading.wait()
        for number in range(ranks):
            span = slice(number * rows, (number + 1) * rows)
            dy_ref[span, :] = grad_out[:, span].astype(F32).T.astype(BF16)
        storing[0].start()

    def side(number):
        if number == 0:
            swaps[1].start()
        elif ranks <= number < 2 * ranks:
            begin = (number - ranks) * slots
            slot = lax.broadcasted_iota(jnp.int32, (slots, dy_ref.shape[0]), 0) + begin
            take = jnp.where((slot == code_ref[0:1]) | (slot == code_ref[1:2]), 1.0, 0.0).astype(BF16)
            dy_rows_ref[begin : begin + slots, :] = mm(take, dy_ref[...]).astype(BF16)
        elif number == 2 * ranks:
            storing[1].start()
            for copy in swaps + storing:
                copy.wait()

    exchange(
        math, rank, source, full, *rest[:-8], side=side, start=start, fill=fill, later=later, cut=3 * width // 8
    )


def norm_back(grad, value, scale, gain):
    scaled = grad * gain
    inner = jnp.sum(scaled * value, axis=1, keepdims=True)
    return scale * scaled - value * (scale * scale * scale) * (inner / value.shape[1])


def norm_two_back_kernel(
    ret_in, back_ref, code_ref, codes_ref, gates_ref, routes_ref, dy_rows_in, gate_ref, router_ref, h_in,
    resid_in, scale_ref, dy_in, gain_ref, full, grad_ref, gain_grad_ref, router_grad_ref, y_out, *rest,
):
    source, scaled, logit_parts, logit_own, send, recv, ret_ref, dy_rows_ref, h_ref, resid_ref, dy_ref, y_ref, load = rest[-13:]
    rank = lax.axis_index("tensor")
    rows = source.shape[1]
    slots, tokens = ret_ref.shape[0], code_ref.shape[1]
    ranks = tokens // rows
    copies = []
    own_dy = dy_in.at[pl.ds(pl.multiple_of(rank * rows, rows), rows)]
    pairs = ((ret_in, ret_ref), (dy_rows_in, dy_rows_ref), (resid_in, resid_ref), (own_dy, dy_ref), (h_in, h_ref))
    loading = [pltpu.make_async_copy(*pair, load.at[number]) for number, pair in enumerate(pairs)]
    storing = [
        pltpu.make_async_copy(y_ref.at[shard], y_out.at[pl.ds(shard * rows, rows)], load.at[5 + shard])
        for shard in range(ranks)
    ]

    def start():
        for copy in loading:
            copy.start()

    def later(others):
        for copy in loading:
            copy.wait()
        found = [jnp.zeros((1, tokens), F32) for _ in range(TOP)]
        tile = slots // 4
        for begin in range(0, slots, tile):
            span = slice(begin, begin + tile)
            ret = ret_ref[span, :].astype(F32)
            slot_grad = jnp.sum(dy_rows_ref[span, :].astype(F32) * ret, axis=1, keepdims=True)
            scaled[span, :] = (ret * gate_ref[span, :]).astype(BF16)
            slot = lax.broadcasted_iota(jnp.int32, (tile, tokens), 0) + begin
            for i in range(TOP):
                found[i] = found[i] + jnp.sum(
                    jnp.where(slot == code_ref[i : i + 1, :], slot_grad, 0.0), axis=0, keepdims=True
                )
        mean = gates_ref[0:1] * found[0] + gates_ref[1:2] * found[1]
        expert = lax.broadcasted_iota(jnp.int32, (EXPERTS, tokens), 0)
        logit = sum(
            jnp.where(routes_ref[i : i + 1] == expert, gates_ref[i : i + 1] * (found[i] - mean), 0.0)
            for i in range(TOP)
        )
        for shard in range(ranks):
            logit_parts[shard] = logit[:, shard * rows : (shard + 1) * rows]
        for number, other in enumerate(others):
            copies.append(
                pltpu.make_async_remote_copy(
                    src_ref=logit_parts.at[other], dst_ref=logit_parts.at[ranks + number], send_sem=send.at[number],
                    recv_sem=recv.at[number], device_id={"tensor": other}, device_id_type=pl.DeviceIdType.MESH,
                )
            )
            copies[-1].start()

    def places(shard):
        slot = lax.broadcasted_iota(jnp.int32, (rows, slots), 1)
        codes = codes_ref[pl.ds(pl.multiple_of(shard * rows, rows), rows), :]
        return jnp.where((slot == codes[:, 0:1]) | (slot == codes[:, 1:2]), 1.0, 0.0).astype(BF16)

    def fill(shard):
        source[shard] = mm(places(shard), back_ref[...]).astype(BF16)

    def side(number):
        if number == ranks:
            router_grad_ref[...] = sum(
                mm(logit_parts[shard].astype(BF16), h_ref[shard * rows : (shard + 1) * rows, :])
                for shard in range(ranks)
            )
            for copy in copies:
                copy.wait()
            logit = logit_parts[rank] + logit_parts[ranks] + logit_parts[ranks + 1] + logit_parts[ranks + 2]
            coarse = logit.astype(BF16)
            logit_own[:EXPERTS] = coarse
            logit_own[EXPERTS:] = (logit - coarse.astype(F32)).astype(BF16)
        elif number > ranks:
            shard = number - ranks - 1
            y_ref[shard] = mm(places(shard), scaled[...]).astype(BF16)
            storing[shard].start()
            if shard == ranks - 1:
                for copy in storing:
                    copy.wait()

    gain_grad_ref[...] = jnp.zeros_like(gain_grad_ref)

    def math(span, total):
        resid, scale = resid_ref[span, :], scale_ref[span, :]
        both = jnp.concatenate([router_ref[...], router_ref[...]], axis=0)
        total = total + mm(logit_own[:, span], both, TN)
        gain_grad_ref[...] += jnp.sum(total * resid * scale, axis=0, keepdims=True)
        grad = norm_back(total, resid, scale, gain_ref[...]) + dy_ref[span, :].astype(F32)
        grad_ref[span, :] = grad
        return grad

    exchange(math, rank, source, full, *rest[:-13], side=side, fill=fill, start=start, later=later)


def norm_one_back_kernel(
    source, x_in, scale_ref, grad_in, gain_ref, y_own, y_across, y_along, gain_one_ref, gain_two_ref, router_ref,
    near_ref, far_ref, full, ready_full, small_out, *rest,
):
    x_ref, grad_ref, held, gathered, near, scale, load, tensor_sends, tensor_recvs, expert_sends, expert_recvs = rest[-11:]
    rank, group = lax.axis_index("tensor"), lax.axis_index("expert")
    pair_class, half_index = rank % 2, rank // 2
    others = rank + 1 - 2 * pair_class, rank + 2 - 4 * half_index
    groups = expert_sends.shape[0]
    mesh_ids = pl.DeviceIdType.MESH
    peers = [partner_of(group, step) for step in range(1, groups)]
    heads = near_ref.shape[0] // 2
    rows = source.shape[1]
    pairs = ((near_ref, near), (x_in, x_ref), (grad_in, grad_ref))
    loading = [pltpu.make_async_copy(*pair, load.at[number]) for number, pair in enumerate(pairs)]

    def math(span, total):
        x = x_ref[span, :].astype(F32)
        return norm_back(total, x, scale[span, :], gain_ref[...]) + grad_ref[span, :]

    def to_rank(step):
        return pltpu.make_async_remote_copy(
            src_ref=held.at[step], dst_ref=held.at[2 + step], send_sem=tensor_sends.at[step],
            recv_sem=tensor_recvs.at[step], device_id={"tensor": others[step]}, device_id_type=mesh_ids,
        )

    def to_group(step):
        return pltpu.make_async_remote_copy(
            src_ref=gathered.at[group], dst_ref=gathered.at[group], send_sem=expert_sends.at[step],
            recv_sem=expert_recvs.at[step], device_id={"expert": peers[step - 1]}, device_id_type=mesh_ids,
        )

    def start():
        for copy in loading:
            copy.start()
        held[0] = jnp.zeros(small_out.shape, F32)
        held[0, :EXPERTS] = router_ref[...]
        held[0, EXPERTS : EXPERTS + 1] = gain_two_ref[...]
        held[0, EXPERTS + 1 : EXPERTS + 2] = gain_one_ref[...]
        to_rank(0).start()

    def side(number):
        if number == 0:
            own_scale = scale_ref[:, pl.ds(pl.multiple_of(rank * rows, rows), rows)]
            scale[...] = jnp.broadcast_to(own_scale, (8, rows)).T[:, :1]
            for copy in loading:
                copy.wait()
            small_out[:BUCKETS, :128] = bias_fold(near, far_ref)
        elif number == 1:
            to_rank(0).wait()
            held[1] = held[0] + held[2]
            to_rank(1).start()
        elif number == 5:
            to_rank(1).wait()
            turned = small_out[:BUCKETS, :128].T
            held[0] = held[1] + held[3]
            held[0, EXPERTS + 2 : EXPERTS + 2 + heads, :BUCKETS] = turned[:heads]
            gathered[group] = held[0].astype(BF16)
            for step in range(1, groups):
                to_group(step).start()
        elif number == 8:
            for step in range(1, groups):
                to_group(step).wait()
            total = gathered[0].astype(F32)
            for step in range(1, groups):
                total = total + gathered[step].astype(F32)
            small_out[...] = total

    exchange(
        math, rank, source, full, *rest[:-11], (y_own, y_across, y_along), ready_full, side=side, peers=peers, start=start
    )


def local_codes(routes_ref, code_ref, pair_class, half_index, half):
    tokens = routes_ref.shape[1]
    expert = lax.broadcasted_iota(jnp.int32, (EXPERTS, BLK), 0)
    earlier = (
        lax.broadcasted_iota(jnp.int32, (BLK, BLK), 0) < lax.broadcasted_iota(jnp.int32, (BLK, BLK), 1)
    ).astype(F32).astype(BF16)
    carry = jnp.zeros((EXPERTS, 1), F32)
    for block in range(tokens // BLK):
        cols = slice(block * BLK, (block + 1) * BLK)
        routes = routes_ref[:, cols]
        hits = [(routes[i : i + 1] == expert) for i in range(TOP)]
        chosen = sum(hit.astype(F32) for hit in hits)
        before = mm(chosen.astype(BF16), earlier) + carry
        carry = carry + jnp.sum(chosen, axis=1, keepdims=True)
        for i in range(TOP):
            slot = jnp.sum(jnp.where(hits[i], before, 0.0), axis=0, keepdims=True).astype(jnp.int32)
            route = routes[i : i + 1]
            owner = route // 2
            local = slot - half_index * half
            mine = (route - 2 * owner == pair_class) & (local >= 0) & (local < half)
            code_ref[i : i + 1, cols] = jnp.where(mine, owner * half + local, -1)


def dispatch_kernel(code_ref, routes_ref, router_ref, h_ref, dy_rows_ref, rows_ref, grads_ref, gate_ref, gates_ref):
    count, tokens = rows_ref.shape[0], h_ref.shape[0]

    @pl.when(pl.program_id(0) == 0)
    def _():
        expert = lax.broadcasted_iota(jnp.int32, (EXPERTS, tokens), 0)
        logits = mm(router_ref[...], h_ref[...], NT)
        picked = [
            jnp.sum(jnp.where(routes_ref[i : i + 1] == expert, logits, 0.0), axis=0, keepdims=True)
            for i in range(TOP)
        ]
        top = jnp.maximum(picked[0], picked[1])
        raised = [jnp.exp(value - top) for value in picked]
        total = raised[0] + raised[1]
        for i in range(TOP):
            gates_ref[i : i + 1] = raised[i] / total

    slot = lax.broadcasted_iota(jnp.int32, (count, tokens), 0) + pl.program_id(0) * count
    hits = [slot == code_ref[i : i + 1, :] for i in range(TOP)]
    take = jnp.where(hits[0] | hits[1], 1.0, 0.0).astype(BF16)
    weighted = jnp.where(hits[0], gates_ref[0:1, :], jnp.where(hits[1], gates_ref[1:2, :], 0.0))
    gate = jnp.sum(weighted, axis=1, keepdims=True)
    rows_ref[...] = mm(take, h_ref[...]).astype(BF16)
    grads_ref[...] = (dy_rows_ref[...].astype(F32) * gate).astype(BF16)
    gate_ref[...] = gate


def dispatch(code, routes_t, router_t, h, dy_rows):
    slots, width = dy_rows.shape
    tile = slots // 4
    row_spec = pl.BlockSpec((tile, width), lambda i: (i, 0))
    whole = lambda shape: pl.BlockSpec(shape, lambda i: (0, 0))
    return pl.pallas_call(
        dispatch_kernel,
        grid=(4,),
        in_specs=[whole(code.shape), whole(code.shape), whole(router_t.shape), whole(h.shape), row_spec],
        out_specs=[row_spec, row_spec, pl.BlockSpec((tile, 1), lambda i: (i, 0)), whole(code.shape)],
        out_shape=[jax.ShapeDtypeStruct((slots, width), BF16)] * 2
        + [jax.ShapeDtypeStruct((slots, 1), F32), jax.ShapeDtypeStruct(code.shape, F32)],
        compiler_params=params(),
        cost_estimate=cost(4 * slots * SEQ * width, 4 * MIB + 6 * slots * width),
    )(code, routes_t, router_t, h, dy_rows)


def gelu_parts(x):
    inner = 0.7978845608028654 * (x + 0.044715 * (x * x * x))
    bend = jnp.tanh(inner)
    half = 0.5 * (1.0 + bend)
    slope = half + 0.5 * x * (1.0 - bend * bend) * (
        0.7978845608028654 * (1.0 + 3.0 * 0.044715 * (x * x))
    )
    return x * half, slope


def partner_of(index, step):
    found = index
    for bit in (1, 2, 4):
        found = found + ((step // bit) % 2) * (1 - 2 * ((index // bit) % 2)) * bit
    return found


def expert_kernel(
    rows_in, grads_in, gate_in, up_in, down_in, far_gate, far_gate_too,
    ret_out, back_out, own_gate, own_up, own_down, got_gate, got_up, got_down,
    rows, grads, weights, sums, parts, opened, z_send, z_recv, y_send, y_recv, p_send, p_recv, r_send, r_recv, w_send, w_recv, g_send, g_recv, local,
):
    groups, half, width = rows.shape[1:]
    group, rank = lax.axis_index("expert"), lax.axis_index("tensor")
    pair_class, half_index = rank % 2, rank // 2
    across = {"tensor": rank + 1 - 2 * pair_class}
    along = {"tensor": rank + 2 - 4 * half_index}
    mesh_ids = pl.DeviceIdType.MESH
    moved = ((rows_in, rows, ret_out), (grads_in, grads, back_out))

    barrier = pltpu.get_barrier_semaphore()
    for step in range(1, groups):
        pl.semaphore_signal(
            barrier, inc=1, device_id={"expert": partner_of(group, step)}, device_id_type=mesh_ids
        )
    pl.semaphore_signal(barrier, inc=1, device_id=across, device_id_type=mesh_ids)
    pl.semaphore_signal(barrier, inc=1, device_id=along, device_id_type=mesh_ids)
    pl.semaphore_wait(barrier, groups + 1)

    def remote(source, target, send, recv, device):
        return pltpu.make_async_remote_copy(
            src_ref=source, dst_ref=target, send_sem=send, recv_sem=recv,
            device_id=device, device_id_type=mesh_ids,
        )

    def block(ref, number):
        return ref.at[pl.ds(pl.multiple_of(number * half, half), half)]

    def out_of(kind, step):
        source, held, _ = moved[kind]
        other = partner_of(group, step)
        return remote(
            block(source, other), held.at[0, group], z_send.at[kind, step], z_recv.at[kind, step], {"expert": other}
        )

    def forward(kind, step):
        held = moved[kind][1]
        other = partner_of(group, step)
        return remote(held.at[0, other], held.at[1, other], y_send.at[kind, step], y_recv.at[kind, step], along)

    def partial_sum(kind, step):
        held = moved[kind][1]
        other = partner_of(group, step)
        return remote(held.at[1, other], parts.at[kind, other], p_send.at[kind, step], p_recv.at[kind, step], along)

    def result(kind, step):
        other = partner_of(group, step)
        return remote(
            parts.at[kind, other], block(moved[kind][2], group), r_send.at[kind, step], r_recv.at[kind, step], {"expert": other}
        )

    def own_result(kind):
        return pltpu.make_async_copy(parts.at[kind, group], block(moved[kind][2], group), local.at[kind])

    own = [
        pltpu.make_async_copy(block(moved[kind][0], group), moved[kind][1].at[0, group], local.at[kind])
        for kind in range(2)
    ]
    for copy in own:
        copy.start()
    kept = [
        pltpu.make_async_copy(ref.at[pair_class], weights.at[number, 0], local.at[2 + number])
        for number, ref in enumerate((gate_in, up_in, down_in))
    ]
    some = far_gate.shape[0]
    for number, ref in enumerate((far_gate, far_gate_too)):
        target = weights.at[0, 1, pl.ds(number * some, some)]
        kept.append(pltpu.make_async_copy(ref, target, local.at[5 + number]))
    kept += [
        remote(ref.at[1 - pair_class], weights.at[number, 1], w_send.at[number - 1], w_recv.at[number - 1], across)
        for number, ref in ((1, up_in), (2, down_in))
    ]
    for copy in kept:
        copy.start()
    for step in range(1, groups):
        for kind in range(2):
            out_of(kind, step).start()

    def arrive(step):
        for kind in range(2):
            out_of(kind, step).wait()
            forward(kind, step).start()

    def give(step):
        for kind in range(2):
            partial_sum(kind, step).start()

    for number in range(3):
        for part in range(2):
            sums[number, part] = jnp.zeros(sums.shape[2:], F32)

    def finish(step):
        other = partner_of(group, step)
        for kind in range(2):
            partial_sum(kind, step).wait()
            held = moved[kind][1]
            parts[kind, other] = (parts[kind, other].astype(F32) + held[0, other].astype(F32)).astype(BF16)

        for kind in range(2):
            if step == 0:
                own_result(kind).start()
            else:
                result(kind, step).start()

    def act(plan):
        for action, step in plan:
            action(step)

    order = ((0, 0, 0), (1, 0, 1), (2, 0, 2), (3, 0, 3), (2, 1, 2), (4, 0, 2), (4, 1, 2), (5, 0, 2), (5, 1, 2), (3, 1, 3), (1, 1, 1), (0, 1, 0), (6, 0, 0), (6, 1, 0), (7, 0, 0), (7, 1, 0))
    before = {
        0: [(arrive, 1), (arrive, 2)],
        1: [(arrive, 3)],
        2: [(arrive, 4)],
        3: [(arrive, 5)],
        5: [(give, 2)],
        7: [(give, 4)],
        8: [(arrive, 6)],
        10: [(finish, 2)],
        12: [(arrive, 7), (finish, 4), (give, 5)],
        14: [(give, 6)],
    }
    ahead = [(give, 7)]
    last = [(finish, 5), (give, 3), (finish, 6), (give, 1), (finish, 7), (give, 0), (finish, 3), (finish, 1), (finish, 0)]
    first_far = [part for _, part, _ in order].index(1)
    for copy in own:
        copy.wait()
    for kind in range(2):
        forward(kind, 0).start()

    def body(turn, carry):
        for number, plan in before.items():
            pl.when(turn == number)(partial(act, plan))

        @pl.when(turn == 0)
        def _():
            for copy in kept[:3]:
                copy.wait()

        @pl.when(turn == first_far)
        def _():
            for copy in kept[3:]:
                copy.wait()

        step, part, place = (
            sum((turn == number).astype(jnp.int32) * unit[k] for number, unit in enumerate(order)) for k in range(3)
        )
        other = partner_of(group, step)

        @pl.when(part == 0)
        def _():
            for kind in range(2):
                forward(kind, step).wait()

        tile = jnp.concatenate([rows[0, other], rows[1, other]], axis=0)
        grad = jnp.concatenate([grads[0, other], grads[1, other]], axis=0)
        w_gate, w_up, w_down = weights[0, part], weights[1, part], weights[2, part]
        gate_part = mm(tile, w_gate, NT)
        up_part = mm(tile, w_up, NT)
        grad_hidden = mm(grad, w_down, NT)
        bent, slope = gelu_parts(gate_part)
        hidden = (bent * up_part).astype(BF16)
        grad_gate = (grad_hidden * up_part * slope).astype(BF16)
        grad_up = (grad_hidden * bent).astype(BF16)
        results = mm(hidden, w_down), mm(grad_gate, w_gate) + mm(grad_up, w_up)
        sums[0, part] += mm(grad_gate, tile, TN)
        sums[1, part] += mm(grad_up, tile, TN)
        sums[2, part] += mm(hidden, grad, TN)

        @pl.when(part == 0)
        def _():
            for kind, value in enumerate(results):
                opened[place, kind] = value.astype(BF16)

        @pl.when(part == 1)
        def _():
            for kind, value in enumerate(results):
                held = moved[kind][1]
                value = value + opened[place, kind].astype(F32)
                held[0, other] = value[:half].astype(BF16)
                held[1, other] = value[half:].astype(BF16)

        return carry

    lax.fori_loop(0, len(order), body, 0)
    act(ahead)
    copies = []
    for number, (own_ref, got_ref) in enumerate(((own_gate, got_gate), (own_up, got_up), (own_down, got_down))):
        weights[number, 0] = sums[number, 1].astype(BF16)
        copies.append(remote(weights.at[number, 0], got_ref, g_send.at[number], g_recv.at[number], across))
        copies[-1].start()
        copies.append(pltpu.make_async_copy(sums.at[number, 0], own_ref, local.at[2 + number]))
        copies[-1].start()
    act(last)
    for copy in copies:
        copy.wait()
    for kind in range(2):
        own_result(kind).wait()
        for step in range(1, groups):
            result(kind, step).wait()


def run_experts(rows, grads, w_gate, w_up, w_down, far_gate, far_gate_too):
    slots, width = rows.shape
    half = CAP // 2
    groups = slots // half
    units = w_gate.shape[1]
    anywhere = pl.BlockSpec(memory_space=pl.ANY)
    pair = pltpu.SemaphoreType.DMA((2, groups))
    return pl.pallas_call(
        expert_kernel,
        in_specs=[anywhere] * 7,
        out_specs=[anywhere] * 8,
        out_shape=[jax.ShapeDtypeStruct((slots, width), BF16)] * 2
        + [jax.ShapeDtypeStruct((units, width), F32)] * 3
        + [jax.ShapeDtypeStruct((units, width), BF16)] * 3,
        scratch_shapes=[
            pltpu.VMEM((2, groups, half, width), BF16),
            pltpu.VMEM((2, groups, half, width), BF16),
            pltpu.VMEM((3, 2, units, width), BF16),
            pltpu.VMEM((3, 2, units, width), F32),
            pltpu.VMEM((2, groups, half, width), BF16),
            pltpu.VMEM((4, 2, 2 * half, width), BF16),
        ]
        + [pair] * 8
        + [pltpu.SemaphoreType.DMA((2,))] * 2
        + [pltpu.SemaphoreType.DMA((3,))] * 2
        + [pltpu.SemaphoreType.DMA((7,))],
        compiler_params=pltpu.CompilerParams(
            vmem_limit_bytes=60 * MIB, collective_id=1, has_side_effects=True
        ),
        cost_estimate=cost(72 * slots * units * width, 16 * slots * width + 30 * units * width),
    )(rows, grads, w_gate, w_up, w_down, far_gate, far_gate_too)


def finish_kernel(
    rows_ref, y_ref, summed_ref, small_ref,
    output_ref, grad_ref, in_ref, out_ref, one_ref, two_ref, router_ref, bias_ref,
):
    step = pl.program_id(0)
    output_ref[...] = y_ref[...].astype(F32).T.astype(BF16)
    grad_ref[...] = rows_ref[...].astype(F32).T

    @pl.when(step < 3)
    def _():
        in_ref[...] = summed_ref[...].astype(F32)

    @pl.when(step == 3)
    def _():
        out_ref[...] = summed_ref[...].astype(F32)
        router_ref[...] = small_ref[:EXPERTS]
        two_ref[...] = small_ref[EXPERTS : EXPERTS + 1]
        one_ref[...] = small_ref[EXPERTS + 1 : EXPERTS + 2]
        bias_ref[...] = small_ref[EXPERTS + 2 : EXPERTS + 2 + bias_ref.shape[0], :BUCKETS]


def finish_outputs(rows, y_rows, summed, small, heads):
    tokens, width = rows.shape
    steps = 4
    tile, block = tokens // steps, summed.shape[0] // steps
    token_spec = pl.BlockSpec((tile, width), lambda i: (i, 0))
    feature_spec = pl.BlockSpec((width, tile), lambda i: (0, i))
    whole = lambda *shape: pl.BlockSpec(shape, lambda i: (0, 0))
    return pl.pallas_call(
        finish_kernel,
        grid=(steps,),
        in_specs=[
            token_spec,
            token_spec,
            pl.BlockSpec((block, width), lambda i: (i, 0)),
            whole(*small.shape),
        ],
        out_specs=[
            feature_spec,
            feature_spec,
            pl.BlockSpec((block, width), lambda i: (jnp.minimum(i, 2), 0)),
            whole(block, width),
            whole(1, width),
            whole(1, width),
            whole(EXPERTS, width),
            whole(heads, BUCKETS),
        ],
        out_shape=[
            jax.ShapeDtypeStruct((width, tokens), BF16),
            jax.ShapeDtypeStruct((width, tokens), F32),
            jax.ShapeDtypeStruct((3 * block, width), F32),
            jax.ShapeDtypeStruct((block, width), F32),
            jax.ShapeDtypeStruct((1, width), F32),
            jax.ShapeDtypeStruct((1, width), F32),
            jax.ShapeDtypeStruct((EXPERTS, width), F32),
            jax.ShapeDtypeStruct((heads, BUCKETS), F32),
        ],
        compiler_params=params(),
        cost_estimate=cost(0, 10 * rows.size + 6 * summed.size),
    )(rows, y_rows, summed, small)


def on_device(
    layer_input, gain_one, attn_in, rel_bias, attn_out, gain_two, router,
    expert_gate, expert_up, expert_down, routes, piece_starts, grad_out,
):
    width, tokens = layer_input.shape
    ranks = lax.axis_size("tensor")
    groups = lax.axis_size("expert")
    rank = lax.axis_index("tensor")
    pair_class, half_index = rank % 2, rank // 2
    half = CAP // 2

    units = expert_gate.shape[1]
    other = lax.dynamic_slice(expert_gate, (1 - pair_class, 0, 0), (1, units // 2, width))[0]
    traded = lax.ppermute(other, "tensor", [(r, r ^ 1) for r in range(ranks)])
    gain_col = gain_one[:, None]
    w_in = attn_in.reshape(-1, width)
    qkv, scale_one = project(layer_input, gain_col, w_in)
    tiles = bias_tiles(rel_bias)
    position = jnp.arange(SEQ, dtype=jnp.int32)[None, None, :]
    starts = piece_starts[:, :, None]
    inside = (position >= starts) & (position < starts + PIECE)
    last = jnp.max(jnp.where(inside, starts + (PIECE - 1), -1), axis=1)
    limits = jnp.maximum(last, position[0])[:, None, :]

    routes_t = routes.T
    place = jnp.stack([pair_class, half_index]).astype(jnp.int32)
    share = tokens // ranks

    def by_rank(rows):
        return rows.reshape(ranks, share, width)

    qkv, traded = lax.optimization_barrier((qkv, traded))
    slots = groups * half
    heads = rel_bias.shape[1]
    h2, resid, scale_two, dy, dy_rows, code, code_cols, own_x, mixed, lse, traded_too = exchange_call(
        norm_two_kernel, 2, (tokens, width),
        [qkv, tiles, limits, attn_out, layer_input, gain_two[None], grad_out, routes_t, expert_gate],
        [((share, width), F32), ((share, 1), F32), ((tokens, width), BF16), ((slots, width), BF16)]
        + [((TOP, tokens), jnp.int32), ((tokens, TOP), jnp.int32), ((share, width), BF16)]
        + [(attn_out.shape[:1] + (tokens,), BF16), ((heads * tokens // SEQ, 1, SEQ), F32), (traded.shape, BF16)],
        [pltpu.VMEM((ranks, share, width), BF16), pltpu.VMEM((width, share), BF16), pltpu.VMEM((width, tokens), BF16)]
        + [pltpu.VMEM((tokens, width), BF16), pltpu.VMEM((slots, width), BF16), pltpu.SemaphoreType.DMA((4,))]
        + [pltpu.SemaphoreType.DMA((2,))] * 2,
        (4, 6, 8),
        (2, 3, 9),
    )
    rows, row_grads, gate_rows, gates = dispatch(code, routes_t, router.T, h2, dy_rows)
    ret, back, *weight_grads = run_experts(
        rows, row_grads, expert_gate, expert_up, expert_down, traded, traded_too
    )
    grad_attn, grad_resid, grad_gain_two, grad_router, partial_y = exchange_call(
        norm_two_back_kernel, 3, (tokens, width),
        [ret, back, code, code_cols, gates, routes_t, dy_rows, gate_rows, router.T, h2]
        + [resid, scale_two, dy, gain_two[None]],
        [((share, width), F32), ((1, width), F32), ((EXPERTS, width), F32), ((tokens, width), BF16)],
        [
            pltpu.VMEM((ranks, share, width), BF16),
            pltpu.VMEM((slots, width), BF16),
            pltpu.VMEM((ranks + 3, EXPERTS, share), F32),
            pltpu.VMEM((2 * EXPERTS, share), BF16),
        ]
        + [pltpu.SemaphoreType.DMA((3,))] * 2
        + [pltpu.VMEM((slots, width), BF16)] * 2
        + [pltpu.VMEM((tokens, width), BF16), pltpu.VMEM((share, width), F32), pltpu.VMEM((share, width), BF16)]
        + [pltpu.VMEM((ranks, share, width), BF16), pltpu.SemaphoreType.DMA((9,))],
        (0, 6, 9, 10, 12),
        (3,),
    )

    dq, dk, dv, near, far, y_own = attend_back(
        qkv, tiles, limits, attn_out, grad_attn, lse, by_rank(partial_y), resid
    )
    dq, y_own = lax.optimization_barrier((dq, y_own))
    y_across = lax.ppermute(y_own, "tensor", [(r, r ^ 1) for r in range(ranks)])
    y_along = lax.ppermute(y_own, "tensor", [(r, r ^ 2) for r in range(ranks)])
    weight_rows, sent, grad_gain_one, grad_gate, grad_up, grad_down = project_back(
        place, layer_input, gain_col, gain_one[None], scale_one, w_in, mixed, grad_attn, (dq, dk, dv),
        weight_grads[:3], weight_grads[3:],
    )
    sent, y_across, y_along = lax.optimization_barrier((sent, y_across, y_along))
    summed = lax.psum(weight_rows, "expert")
    small_shape = (BUCKETS, width)
    grad_rows, y_full, small = exchange_call(
        norm_one_back_kernel, 4, sent.shape,
        [by_rank(sent), own_x, scale_one, grad_resid, gain_one[None], y_own, y_across, y_along]
        + [grad_gain_one, grad_gain_two, grad_router, near, far],
        [((ranks, share, width), BF16), (small_shape, F32)],
        [pltpu.VMEM((share, width), BF16), pltpu.VMEM((share, width), F32)]
        + [pltpu.VMEM((4, *small_shape), F32), pltpu.VMEM((groups, *small_shape), BF16), pltpu.VMEM(near.shape, F32), pltpu.VMEM((share, 1), F32)]
        + [pltpu.SemaphoreType.DMA((3,))]
        + [pltpu.SemaphoreType.DMA((2,))] * 2
        + [pltpu.SemaphoreType.DMA((groups,))] * 2,
        (1, 3, 11),
        (0,),
    )
    summed, grad_rows = lax.optimization_barrier((summed, grad_rows))
    layer_output, grad_input, grad_in, grad_attn_out, grad_one, grad_two, grad_router, grad_bias = finish_outputs(
        grad_rows, y_full.reshape(tokens, width), summed, small, rel_bias.shape[1]
    )
    return (
        layer_output,
        grad_input,
        grad_one[0],
        grad_in.reshape(attn_in.shape),
        grad_bias.T,
        grad_attn_out,
        grad_two[0],
        grad_router.T,
        grad_gate,
        grad_up,
        grad_down,
    )


def allowed_pairs(seq_starts):
    position = jnp.arange(SEQ, dtype=jnp.int32)
    inside = (position[:, None] >= seq_starts[None, :]) & (
        position[:, None] < seq_starts[None, :] + PIECE
    )
    numbers = jnp.arange(seq_starts.shape[0], dtype=jnp.int32) + 1
    piece_label = jnp.sum(inside.astype(jnp.int32) * numbers[None, :], axis=1)
    causal = position[None, :] <= position[:, None]
    shared = (piece_label[:, None] == piece_label[None, :]) & (piece_label[:, None] > 0)
    return causal | shared


def slot_table(routes):
    flat_routes = routes.reshape(-1)
    onehot = (flat_routes[:, None] == jnp.arange(EXPERTS, dtype=jnp.int32)[None, :]).astype(
        jnp.int32
    )
    blocks = onehot.reshape(-1, 128, EXPERTS).astype(F32)
    earlier = jnp.tril(jnp.ones((128, 128), F32), -1)
    inside = jnp.einsum("ij,bje->bie", earlier, blocks)
    count = blocks.shape[0]
    carried = jnp.einsum("ab,be->ae", jnp.tril(jnp.ones((count, count), F32), -1), jnp.sum(blocks, axis=1), precision=HIGH)
    before = (inside + carried[:, None, :]).astype(jnp.int32).reshape(onehot.shape)
    slot_number = jnp.sum(before * onehot, axis=1)
    kept_pairs = slot_number < CAP
    slot_index = jnp.where(kept_pairs, flat_routes * CAP + slot_number, EXPERTS * CAP)
    return (slot_index.reshape(routes.shape), kept_pairs.reshape(routes.shape))


def bucket_onehot():
    offsets = jnp.arange(2 * SEQ - 1, dtype=jnp.int32) - (SEQ - 1)
    return (bucket_of(offsets)[:, None] == jnp.arange(BUCKETS, dtype=jnp.int32)[None, :]).astype(
        jnp.float32
    )


def expand_line(line):
    head_count = line.shape[0]
    padded = jnp.concatenate([line, jnp.zeros((head_count, 1), line.dtype)], axis=1)
    tiled = jnp.tile(padded, (1, SEQ))[:, : SEQ * (2 * SEQ - 1)].reshape(
        head_count, SEQ, 2 * SEQ - 1
    )
    return tiled[:, :, SEQ - 1 :]


def fold_line(full_grid):
    head_count = full_grid.shape[0]
    padded = jnp.pad(full_grid, ((0, 0), (0, 0), (SEQ - 1, 0))).reshape(
        head_count, SEQ * (2 * SEQ - 1)
    )
    padded = jnp.pad(padded, ((0, 0), (0, SEQ))).reshape(head_count, SEQ, 2 * SEQ)
    return jnp.sum(padded, axis=1)[:, : 2 * SEQ - 1]


def reduce_heads(tensor_value):
    return lax.psum(tensor_value, "tensor")


def spread_slots(tensor_value):
    return lax.all_gather(tensor_value, "tensor", axis=2, tiled=True)


def owner_exchange(tensor_value):
    return lax.all_to_all(tensor_value, "expert", split_axis=0, concat_axis=0, tiled=True)


def expert_sums(tensor_value):
    return lax.psum_scatter(tensor_value, "tensor", scatter_dimension=2, tiled=True)


def norm_forward(resid, gain, model_width):
    scale = lax.rsqrt(jnp.sum(resid * resid, axis=1) / model_width + EPS)[:, None]
    return (scale, (resid * scale * gain).astype(jnp.bfloat16))


def norm_backward(resid, scale, gain, grad_normed, model_width):
    grad_gain = jnp.sum(grad_normed * resid * scale, axis=0)
    scaled = grad_normed * gain
    inner = jnp.sum(scaled * resid, axis=1)[:, None]
    return (grad_gain, scale * scaled - resid * scale**3 * inner / model_width)


def attend_scores(bias_full, queries, key_rows, seq_starts):
    scores = (
        jnp.einsum("qhe,khe->hqk", queries, key_rows, preferred_element_type=jnp.float32) * 0.125
        + bias_full
    )
    return jnp.where(allowed_pairs(seq_starts)[None], scores, NEG)


def attend_forward(bias_full, inputs):
    queries, key_rows, value_rows, seq_starts = inputs
    scores = attend_scores(bias_full, queries, key_rows, seq_starts)
    row_max = jnp.max(scores, axis=2, keepdims=True)
    exponent = jnp.exp(scores - row_max)
    row_sum_exp = jnp.sum(exponent, axis=2, keepdims=True)
    weights = (exponent / row_sum_exp).astype(jnp.bfloat16)
    mixed_heads = jnp.einsum(
        "hqk,khe->qhe", weights, value_rows, preferred_element_type=jnp.float32
    )
    return (mixed_heads.astype(jnp.bfloat16), (row_max + jnp.log(row_sum_exp))[:, :, 0])


def attend_backward(bias_full, running, inputs):
    queries, key_rows, value_rows, grad_heads, seq_starts, log_total = inputs
    scores = attend_scores(bias_full, queries, key_rows, seq_starts)
    probabilities = jnp.exp(scores - log_total[:, :, None])
    grad_probs = jnp.einsum(
        "qhe,khe->hqk", grad_heads, value_rows, preferred_element_type=jnp.float32
    )
    inner = jnp.sum(probabilities * grad_probs, axis=2, keepdims=True)
    grad_scores = (probabilities * (grad_probs - inner)).astype(jnp.bfloat16)
    grad_values = jnp.einsum(
        "hqk,qhe->khe",
        probabilities.astype(jnp.bfloat16),
        grad_heads,
        preferred_element_type=jnp.float32,
    )
    grad_queries = (
        jnp.einsum("hqk,khe->qhe", grad_scores, key_rows, preferred_element_type=jnp.float32)
        * 0.125
    )
    grad_keys = (
        jnp.einsum("hqk,qhe->khe", grad_scores, queries, preferred_element_type=jnp.float32) * 0.125
    )
    return (
        running + grad_scores.astype(jnp.float32),
        jnp.stack([grad_queries, grad_keys, grad_values]),
    )


def gelu_product(left, right):
    return jax.nn.gelu(left, approximate=True) * right


def expert_forward(received, weight_gate, weight_up, weight_down):
    gate_part = jnp.einsum(
        "secd,efd->secf", received, weight_gate, preferred_element_type=jnp.float32
    )
    up_part = jnp.einsum("secd,efd->secf", received, weight_up, preferred_element_type=jnp.float32)
    hidden = gelu_product(gate_part, up_part).astype(jnp.bfloat16)
    partial_out = jnp.einsum(
        "secf,efd->secd", hidden, weight_down, preferred_element_type=jnp.float32
    )
    return (gate_part, up_part, hidden, partial_out)


def expert_backward(
    received, gate_part, up_part, hidden, grad_rows_out, weight_gate, weight_up, weight_down
):
    grad_hidden = jnp.einsum(
        "secd,efd->secf", grad_rows_out, weight_down, preferred_element_type=jnp.float32
    )
    product_value, pullback = jax.vjp(gelu_product, gate_part, up_part)
    grad_gate_part, grad_up_part = pullback(grad_hidden)
    grad_gate_part = grad_gate_part.astype(jnp.bfloat16)
    grad_up_part = grad_up_part.astype(jnp.bfloat16)
    grad_down = jnp.einsum(
        "secf,secd->efd", hidden, grad_rows_out, preferred_element_type=jnp.float32
    )
    grad_gate_w = jnp.einsum(
        "secf,secd->efd", grad_gate_part, received, preferred_element_type=jnp.float32
    )
    grad_up_w = jnp.einsum(
        "secf,secd->efd", grad_up_part, received, preferred_element_type=jnp.float32
    )
    grad_rows_in = jnp.einsum(
        "secf,efd->secd", grad_gate_part, weight_gate, preferred_element_type=jnp.float32
    )
    grad_rows_in = grad_rows_in + jnp.einsum(
        "secf,efd->secd", grad_up_part, weight_up, preferred_element_type=jnp.float32
    )
    return (grad_gate_w, grad_up_w, grad_down, grad_rows_in)


def on_device_general(
    layer_input,
    gain_one,
    attn_in,
    rel_bias,
    attn_out,
    gain_two,
    router,
    expert_gate,
    expert_up,
    expert_down,
    routes,
    piece_starts,
    grad_out,
):
    tok_count = layer_input.shape[1]
    model_width = layer_input.shape[0]
    heads_here = rel_bias.shape[1]
    head_width = attn_in.shape[1] // heads_here
    seqs_here = piece_starts.shape[0]
    local_experts = expert_gate.shape[0]
    part_rows = CAP // lax.axis_size("tensor")
    share_start = lax.axis_index("tensor") * part_rows
    tokens = layer_input.T.astype(jnp.float32)
    scale_one, normed = norm_forward(tokens, gain_one, model_width)
    project = jnp.einsum("td,chd->cth", normed, attn_in, preferred_element_type=jnp.float32).astype(
        jnp.bfloat16
    )
    by_seq = project.reshape(3, seqs_here, SEQ, heads_here, head_width)
    onehot_line = bucket_onehot()
    bias_full = expand_line(jnp.dot(onehot_line, rel_bias, precision=HIGH).T)
    mixed_heads, log_total = lax.map(
        partial(attend_forward, bias_full), (by_seq[0], by_seq[1], by_seq[2], piece_starts)
    )
    mixed_heads = mixed_heads.reshape(tok_count, heads_here * head_width)
    resid = tokens + reduce_heads(
        jnp.dot(mixed_heads, attn_out, preferred_element_type=jnp.float32)
    )
    scale_two, normed_two = norm_forward(resid, gain_two, model_width)
    logits = jnp.dot(normed_two, router, preferred_element_type=jnp.float32)
    chosen = (routes[:, :, None] == jnp.arange(EXPERTS, dtype=jnp.int32)[None, None, :]).astype(
        jnp.float32
    )
    picked = jnp.sum(chosen * logits[:, None, :], axis=2)
    gate_weights = jax.nn.softmax(picked, axis=1)
    slot_index, kept_pairs = slot_table(routes)
    keep_float = kept_pairs.astype(jnp.float32)
    mix_weight = gate_weights * keep_float
    safe_index = jnp.minimum(slot_index, EXPERTS * CAP - 1)
    token_rows = jnp.repeat(normed_two, TOP, axis=0)
    buffer = (
        jnp.zeros((EXPERTS * CAP + 1, model_width), jnp.bfloat16)
        .at[slot_index.reshape(-1)]
        .set(token_rows)
    )
    buffer = buffer[: EXPERTS * CAP].reshape(-1, local_experts, CAP, model_width)
    received = lax.all_to_all(buffer, "expert", split_axis=0, concat_axis=0, tiled=True)
    gate_part, up_part, hidden, partial_out = expert_forward(
        received, expert_gate, expert_up, expert_down
    )
    returned = spread_slots(owner_exchange(expert_sums(partial_out).astype(jnp.bfloat16)))
    flat_ret = returned.reshape(EXPERTS * CAP, model_width)
    fetched = flat_ret[safe_index].astype(jnp.float32)
    output = resid + jnp.sum(mix_weight[:, :, None] * fetched, axis=1)
    grad_y = grad_out.T.astype(jnp.float32)
    grad_gates = jnp.sum(grad_y[:, None, :] * fetched, axis=2) * keep_float
    grad_picked = gate_weights * (
        grad_gates - jnp.sum(gate_weights * grad_gates, axis=1, keepdims=True)
    )
    grad_logits = jnp.sum(chosen * grad_picked[:, :, None], axis=1)
    grad_router = jnp.dot(normed_two.astype(jnp.float32).T, grad_logits, precision=HIGH)
    grad_normed_two = jnp.dot(grad_logits, router.astype(jnp.float32).T, precision=HIGH)
    slot_grads = (mix_weight[:, :, None] * grad_y[:, None, :]).astype(jnp.bfloat16)
    grad_ret = (
        jnp.zeros((EXPERTS * CAP + 1, model_width), jnp.bfloat16)
        .at[slot_index.reshape(-1)]
        .set(slot_grads.reshape(-1, model_width))
    )
    grad_ret = grad_ret[: EXPERTS * CAP].reshape(-1, local_experts, CAP, model_width)
    grad_share = lax.dynamic_slice_in_dim(grad_ret, share_start, part_rows, 2)
    grad_rows_out = spread_slots(owner_exchange(grad_share))
    grad_expert_gate, grad_expert_up, grad_expert_down, grad_rows_in = expert_backward(
        received, gate_part, up_part, hidden, grad_rows_out, expert_gate, expert_up, expert_down
    )
    grad_back = spread_slots(owner_exchange(expert_sums(grad_rows_in).astype(jnp.bfloat16)))
    flat_back = grad_back.reshape(EXPERTS * CAP, model_width).astype(jnp.float32)
    grad_normed_two = grad_normed_two + jnp.sum(
        flat_back[safe_index] * keep_float[:, :, None], axis=1
    )
    grad_gain_two, grad_resid = norm_backward(
        resid, scale_two, gain_two, grad_normed_two, model_width
    )
    grad_resid = grad_resid + grad_y
    grad_attn = grad_resid.astype(jnp.bfloat16)
    grad_attn_out = jnp.einsum(
        "th,td->hd", mixed_heads, grad_attn, preferred_element_type=jnp.float32
    )
    grad_mixed = jnp.einsum(
        "td,hd->th", grad_attn, attn_out, preferred_element_type=jnp.float32
    ).astype(jnp.bfloat16)
    grad_by_seq = grad_mixed.reshape(seqs_here, SEQ, heads_here, head_width)
    bias_grad_full, grad_project = lax.scan(
        partial(attend_backward, bias_full),
        jnp.zeros_like(bias_full),
        (by_seq[0], by_seq[1], by_seq[2], grad_by_seq, piece_starts, log_total),
    )
    grad_project = (
        jnp.moveaxis(grad_project, 1, 0)
        .reshape(3, tok_count, heads_here * head_width)
        .astype(jnp.bfloat16)
    )
    grad_attn_in = jnp.einsum(
        "cth,td->chd", grad_project, normed, preferred_element_type=jnp.float32
    )
    grad_normed = reduce_heads(
        jnp.einsum("cth,chd->td", grad_project, attn_in, preferred_element_type=jnp.float32)
    )
    grad_gain_one, grad_tokens = norm_backward(
        tokens, scale_one, gain_one, grad_normed, model_width
    )
    grad_tokens = grad_tokens + grad_resid
    grad_rel_bias = jnp.dot(onehot_line.T, fold_line(bias_grad_full).T, precision=HIGH)
    shared = (
        lax.psum(grad_gain_one.astype(jnp.bfloat16), "expert").astype(jnp.float32),
        lax.psum(grad_attn_in.astype(jnp.bfloat16), "expert").astype(jnp.float32),
        lax.psum(grad_rel_bias.astype(jnp.bfloat16), "expert").astype(jnp.float32),
        lax.psum(grad_attn_out.astype(jnp.bfloat16), "expert").astype(jnp.float32),
        lax.psum(grad_gain_two.astype(jnp.bfloat16), "expert").astype(jnp.float32),
        lax.psum(grad_router.astype(jnp.bfloat16), "expert").astype(jnp.float32),
    )
    return (
        output.astype(jnp.bfloat16).T,
        grad_tokens.T,
        shared[0],
        shared[1],
        shared[2],
        shared[3],
        shared[4],
        shared[5],
        grad_expert_gate,
        grad_expert_up,
        grad_expert_down,
    )


def solution(mesh):
    placed = (
        P(None, "expert"),
        P(),
        P(None, "tensor", None),
        P(None, "tensor"),
        P("tensor", None),
        P(),
        P(),
        P("expert", "tensor", None),
        P("expert", "tensor", None),
        P("expert", "tensor", None),
        P("expert", None),
        P("expert", None),
        P(None, "expert"),
    )
    paired = mesh.shape["tensor"] == 4 and mesh.shape["expert"] * 2 == EXPERTS
    return jax.shard_map(
        on_device if paired else on_device_general,
        mesh=mesh,
        in_specs=placed,
        out_specs=(
            P(None, "expert"),
            P(None, "expert"),
            P(),
            P(None, "tensor", None),
            P(None, "tensor"),
            P("tensor", None),
            P(),
            P(),
            P("expert", "tensor", None),
            P("expert", "tensor", None),
            P("expert", "tensor", None),
        ),
        check_vma=False,
    )
```

```python
from functools import partial

import jax
import jax.numpy as jnp
from jax import lax
from jax.experimental import pallas as pl
from jax.experimental.pallas import tpu as pltpu
from jax.sharding import PartitionSpec as P

EXPERTS = 16
BUCKETS = 32
TOP = 2
PIECE = 256
SEQ = 1024
CAP = 320
BLK = 256


EPS = 1e-06
NEG = -1e30
THRESHOLDS = (12, 16, 23, 32, 46, 64, 91)
HIGH = lax.Precision.HIGHEST
F32 = jnp.float32
BF16 = jnp.bfloat16
NN = (((1,), (0,)), ((), ()))
NT = (((1,), (1,)), ((), ()))
TN = (((0,), (0,)), ((), ()))
MIB = 1 << 20


def mm(left, right, dims=NN):
    return lax.dot_general(left, right, dims, preferred_element_type=F32)


def params(limit=56):
    return pltpu.CompilerParams(vmem_limit_bytes=limit * MIB)


def cost(flops, bytes_accessed, transcendentals=0):
    return pl.CostEstimate(
        flops=int(flops), bytes_accessed=int(bytes_accessed), transcendentals=int(transcendentals)
    )


def bucket_of(offset):
    magnitude = jnp.abs(offset)
    beyond = sum(((magnitude >= threshold).astype(jnp.int32) for threshold in THRESHOLDS))
    lower_part = jnp.where(magnitude < 8, magnitude, 8 + beyond)
    return lower_part + 16 * (offset > 0).astype(jnp.int32)


def as_column(line):
    return jnp.broadcast_to(line, (8, line.shape[1])).T[:, :1]


def project_kernel(x_ref, gain_ref, w_ref, table_ref, out_ref, scale_ref, tiles_ref):
    x = x_ref[...].astype(F32)
    scale = lax.rsqrt(jnp.sum(x * x, axis=0, keepdims=True) / x.shape[0] + EPS)
    normed = (x * scale * as_column(gain_ref[...])).astype(BF16)
    out_ref[...] = mm(w_ref[...], normed).astype(BF16)
    scale_ref[...] = scale
    bias_tiles(table_ref, pl.program_id(0), tiles_ref)


def project(x, gain, weights, table):
    width, tokens = x.shape
    rows = weights.shape[0]
    heads = table.shape[0]
    tile = tokens // heads
    return pl.pallas_call(
        project_kernel,
        grid=(heads,),
        in_specs=[
            pl.BlockSpec((width, tile), lambda i: (0, i)),
            pl.BlockSpec((1, width), lambda i: (0, 0)),
            pl.BlockSpec((rows, width), lambda i: (0, 0)),
            pl.BlockSpec(memory_space=pltpu.SMEM),
        ],
        out_specs=[
            pl.BlockSpec((rows, tile), lambda i: (0, i)),
            pl.BlockSpec((1, tile), lambda i: (0, i)),
            pl.BlockSpec((1, 3, BLK, BLK), lambda i: (i, 0, 0, 0)),
        ],
        out_shape=[
            jax.ShapeDtypeStruct((rows, tokens), BF16),
            jax.ShapeDtypeStruct((1, tokens), F32),
            jax.ShapeDtypeStruct((heads, 3, BLK, BLK), F32),
        ],
        compiler_params=params(),
        cost_estimate=cost(2 * width * tokens * rows, 2 * width * tokens * 2),
    )(x, gain, weights, table)


def line_offsets(number):
    column = lax.broadcasted_iota(jnp.int32, (8, BLK), 1)
    return (number - 1) * BLK - column


def bias_tiles(table_ref, head, tiles_ref):
    row = lax.broadcasted_iota(jnp.int32, (BLK, BLK), 0)
    column = lax.broadcasted_iota(jnp.int32, (BLK, BLK), 1)
    far = table_ref[head, 15]
    rolled = []
    for number in range(4):
        bucket = bucket_of(line_offsets(number))
        value = jnp.zeros((8, BLK), F32)
        for index in range(BUCKETS):
            value = jnp.where(bucket == index, table_ref[head, index] - far, value)
        whole = jnp.broadcast_to(value[0:1], (BLK, BLK))
        rolled.append(pltpu.roll(whole, 0, 1, stride=1, stride_axis=0))
    for number in range(3):
        tiles_ref[0, number] = jnp.where(column >= row, rolled[number], rolled[number + 1])


def bias_fold(near_ref, far_ref):
    heads = near_ref.shape[0] // 2
    sums = jnp.zeros((BUCKETS, 128), F32)
    lane = lax.broadcasted_iota(jnp.int32, (BUCKETS, 128), 1)
    row = lax.broadcasted_iota(jnp.int32, (BLK, BLK), 0)
    column = lax.broadcasted_iota(jnp.int32, (BLK, BLK), 1)
    flip = jnp.where(row + column == BLK - 1, 1.0, 0.0).astype(BF16)
    apart = jnp.where(column == BLK - 1, 0, column + 1)
    ahead = apart <= row
    number_at = lax.broadcasted_iota(jnp.int32, (BUCKETS, BLK), 0)
    for head in range(heads):
        lines = [jnp.zeros((1, BLK), F32) for _ in range(4)]
        for number in range(3):
            grads = near_ref[head, number] + near_ref[heads + head, number]
            coarse = grads.astype(BF16)
            fine = (grads - coarse.astype(F32)).astype(BF16)
            flipped = mm(flip, coarse) + mm(flip, fine)
            rolled = pltpu.roll(flipped, 0, 1, stride=1, stride_axis=0)
            lines[number] += jnp.sum(jnp.where(ahead, rolled, 0.0), axis=0, keepdims=True)
            lines[number + 1] += jnp.sum(jnp.where(ahead, 0.0, rolled), axis=0, keepdims=True)
        total = jnp.zeros((BUCKETS, 1), F32)
        for number, line in enumerate(lines):
            bucket = bucket_of((number - 1) * BLK - apart[:1])
            total += jnp.sum(jnp.where(bucket == number_at, line, 0.0), axis=1, keepdims=True)
        distant = jnp.sum(far_ref[head] + far_ref[heads + head], axis=0, keepdims=True)
        distant = jnp.sum(distant, axis=1, keepdims=True)
        total += jnp.where(number_at[:, :1] == 15, distant, 0.0)
        sums = jnp.where(lane == head, total, sums)
    return sums


def key_count(query_block):
    return 2 * BLK if query_block < 2 else 4 * BLK


def block_scores(keys, queries, tile_of, limit, block):
    count = key_count(block)
    parts = []
    whole = mm(keys[:, :count], queries, TN)
    for key_block in range(count // BLK):
        part = whole[key_block * BLK : (key_block + 1) * BLK]
        shift = key_block - block
        if -1 <= shift <= 1:
            part = part + tile_of(shift)
        if shift >= 0:
            key_at = lax.broadcasted_iota(jnp.int32, (BLK, BLK), 0) + key_block * BLK
            part = jnp.where(key_at <= limit, part, NEG)
        parts.append(part)
    return jnp.concatenate(parts, axis=0)


def attend_half(qkv_ref, tiles_ref, limit_ref, mixed_ref, lse_ref, seq, half):
    heads = tiles_ref.shape[0]
    width = mixed_ref.shape[0] // heads
    base = pl.multiple_of(seq * SEQ, SEQ)

    def one_head(head, carry):
        at = lambda kind: pl.ds(pl.multiple_of((kind * heads + head) * width, width), width)
        keys, values = qkv_ref[at(1), pl.ds(base, SEQ)], qkv_ref[at(2), pl.ds(base, SEQ)]
        for block in (2 * half, 2 * half + 1):
            cols = pl.ds(pl.multiple_of(base + block * BLK, BLK), BLK)
            span = slice(block * BLK, (block + 1) * BLK)
            queries = qkv_ref[at(0), cols] * BF16(0.125)
            scores = block_scores(
                keys, queries, lambda shift: tiles_ref[head, shift + 1], limit_ref[seq, :, span], block
            )
            top = jnp.max(scores, axis=0, keepdims=True)
            exponent = jnp.exp(scores - top)
            total = jnp.sum(exponent, axis=0, keepdims=True)
            mixed = mm(values[:, : key_count(block)], exponent.astype(BF16)) / total
            mixed_ref[at(0), cols] = mixed.astype(BF16)
            lse_ref[seq * heads + head, :, span] = top + jnp.log(total)
        return carry

    lax.fori_loop(0, heads, one_head, 0)


def attend_back_kernel(
    q_ref, k_ref, v_ref, tiles_ref, limit_ref, w_ref, grad_ref, lse_ref, part_ref, resid_ref,
    dq_ref, dk_ref, dv_ref, near_ref, far_ref, y_ref,
    held, parts, total, turn_across, turn_along, from_across, from_along, sends, recvs, loads,
):
    rank = lax.axis_index("tensor")
    pair_class, half_index = rank % 2, rank // 2
    across, along, corner = rank + 1 - 2 * pair_class, rank + 2 - 4 * half_index, 3 - rank
    step = pl.program_id(0) * pl.num_programs(1) + pl.program_id(1)
    mesh_ids = pl.DeviceIdType.MESH
    middle = parts.shape[2] // 2
    low, high = slice(0, middle), slice(middle, 2 * middle)

    def remote(number, origin, target, other):
        return pltpu.make_async_remote_copy(
            src_ref=origin, dst_ref=target, send_sem=sends.at[number], recv_sem=recvs.at[number],
            device_id={"tensor": other}, device_id_type=mesh_ids,
        )

    first = (
        remote(0, part_ref.at[corner, :, low], turn_across, across),
        remote(1, part_ref.at[corner, :, high], turn_along, along),
    )
    second = remote(2, parts.at[0], from_across, across), remote(3, parts.at[1], from_along, along)
    local = [
        pltpu.make_async_copy(part_ref.at[other], parts.at[number], loads.at[number])
        for number, other in enumerate((across, along, rank))
    ]
    local.append(pltpu.make_async_copy(resid_ref, total, loads.at[3]))

    @pl.when(step == 0)
    def _():
        barrier = pltpu.get_barrier_semaphore()
        for other in (across, along):
            pl.semaphore_signal(barrier, inc=1, device_id={"tensor": other}, device_id_type=mesh_ids)
        pl.semaphore_wait(barrier, 2)
        for copy in first:
            copy.start()
        for copy in local:
            copy.start()

    @pl.when(step == 3)
    def _():
        for copy in (*first, *local):
            copy.wait()
        parts[0, :, high] = (parts[0, :, high].astype(F32) + turn_along[...].astype(F32)).astype(BF16)
        parts[1, :, low] = (parts[1, :, low].astype(F32) + turn_across[...].astype(F32)).astype(BF16)
        for copy in second:
            copy.start()

    head = pl.program_id(1)
    width = q_ref.shape[0]

    @pl.when(head == 0)
    def _():
        held[...] = mm(w_ref[...], grad_ref[...], NT).astype(BF16)

    queries = q_ref[...] * BF16(0.125)
    keys, values = k_ref[...], v_ref[...]
    grads = held[pl.ds(pl.multiple_of(head * width, width), width), :]
    near_ref[...] = jnp.zeros_like(near_ref)
    far = jnp.zeros((8, BLK), F32)
    grad_keys = jnp.zeros((width, SEQ), F32)
    grad_values = jnp.zeros((width, SEQ), F32)
    for block in range(SEQ // BLK):
        count = key_count(block)
        cols = slice(block * BLK, (block + 1) * BLK)
        scores = block_scores(
            keys, queries[:, cols], lambda shift: tiles_ref[0, shift + 1], limit_ref[0, :, cols], block
        )
        probs = jnp.exp(scores - lse_ref[0, :, cols])
        grad_probs = mm(values[:, :count], grads[:, cols], TN)
        inner = jnp.sum(probs * grad_probs, axis=0, keepdims=True)
        grad_scores = probs * (grad_probs - inner)
        for key_block in range(count // BLK):
            part = grad_scores[key_block * BLK : (key_block + 1) * BLK]
            shift = key_block - block
            if -1 <= shift <= 1:
                near_ref[0, shift + 1] += part
            elif shift < -1:
                far = far + jnp.sum(part.reshape(BLK // 8, 8, BLK), axis=0)
        rounded = grad_scores.astype(BF16)
        add_values = mm(grads[:, cols], probs.astype(BF16), NT)
        add_keys = mm(queries[:, cols], rounded, NT)
        if count == SEQ:
            grad_values = grad_values + add_values
            grad_keys = grad_keys + add_keys
        else:
            filler = jnp.zeros((width, SEQ - count), F32)
            grad_values = grad_values + jnp.concatenate([add_values, filler], axis=1)
            grad_keys = grad_keys + jnp.concatenate([add_keys, filler], axis=1)
        dq_ref[:, cols] = (mm(keys[:, :count], rounded) * 0.125).astype(BF16)
    dk_ref[...] = grad_keys.astype(BF16)
    dv_ref[...] = grad_values.astype(BF16)
    far_ref[0] = far

    @pl.when(step == 7)
    def _():
        for copy in second:
            copy.wait()
        summed = parts[2].astype(F32) + from_across[...].astype(F32) + from_along[...].astype(F32)
        y_ref[...] = (total[...] + summed).astype(BF16)


def attend_back(qkv, tiles, limits, attn_out, grad_attn, lse, part, resid):
    heads = tiles.shape[0]
    seqs = limits.shape[0]
    width = qkv.shape[0] // (3 * heads)
    model_width = attn_out.shape[1]
    share = part.shape[1]
    grad_spec = pl.BlockSpec((width, SEQ), lambda s, h: (h, s))
    anywhere = pl.BlockSpec(memory_space=pl.ANY)
    return pl.pallas_call(
        attend_back_kernel,
        grid=(seqs, heads),
        in_specs=[
            pl.BlockSpec((width, SEQ), lambda s, h: (h, s)),
            pl.BlockSpec((width, SEQ), lambda s, h: (heads + h, s)),
            pl.BlockSpec((width, SEQ), lambda s, h: (2 * heads + h, s)),
            pl.BlockSpec((1, 3, BLK, BLK), lambda s, h: (h, 0, 0, 0)),
            pl.BlockSpec((1, 1, SEQ), lambda s, h: (s, 0, 0)),
            pl.BlockSpec((heads * width, model_width), lambda s, h: (0, 0)),
            pl.BlockSpec((SEQ, model_width), lambda s, h: (s, 0)),
            pl.BlockSpec((1, 1, SEQ), lambda s, h: (s * heads + h, 0, 0)),
        ]
        + [anywhere] * 2,
        out_specs=[
            grad_spec,
            grad_spec,
            grad_spec,
            pl.BlockSpec((1, 3, BLK, BLK), lambda s, h: (s * heads + h, 0, 0, 0)),
            pl.BlockSpec((1, 8, BLK), lambda s, h: (s * heads + h, 0, 0)),
            pl.BlockSpec((share, model_width), lambda s, h: (0, 0)),
        ],
        out_shape=[jax.ShapeDtypeStruct((heads * width, seqs * SEQ), BF16)] * 3
        + [
            jax.ShapeDtypeStruct((seqs * heads, 3, BLK, BLK), F32),
            jax.ShapeDtypeStruct((seqs * heads, 8, BLK), F32),
        ]
        + [jax.ShapeDtypeStruct((share, model_width), BF16)],
        scratch_shapes=[
            pltpu.VMEM((heads * width, SEQ), BF16),
            pltpu.VMEM((3, share, model_width), BF16),
            pltpu.VMEM((share, model_width), F32),
            pltpu.VMEM((share, model_width // 2), BF16),
            pltpu.VMEM((share, model_width // 2), BF16),
            pltpu.VMEM((share, model_width), BF16),
            pltpu.VMEM((share, model_width), BF16),
            pltpu.SemaphoreType.DMA((4,)),
            pltpu.SemaphoreType.DMA((4,)),
            pltpu.SemaphoreType.DMA((4,)),
        ],
        compiler_params=pltpu.CompilerParams(
            vmem_limit_bytes=60 * MIB, collective_id=5, has_side_effects=True
        ),
        cost_estimate=cost(seqs * heads * SEQ * SEQ * 1280, seqs * heads * SEQ * 4096, seqs * heads * SEQ * SEQ),
    )(qkv, qkv, qkv, tiles, limits, attn_out, grad_attn, lse, part, resid)


def project_back_kernel(
    place_ref, x_ref, gain_ref, scale_ref, w_ref, mixed_ref, attn_ref, dq_ref, dk_ref, dv_ref, *refs
):
    step = pl.program_id(0)
    own_refs, got_refs, (weight_ref, out_ref, gain_grad_ref), placed_refs, total = (
        refs[:3], refs[3:6], refs[6:9], refs[9:12], refs[12]
    )
    for own_ref, got_ref, placed_ref in zip(own_refs, got_refs, placed_refs):
        placed_ref[place_ref[0]] = own_ref[...]
        placed_ref[1 - place_ref[0]] = got_ref[...].astype(F32)
    grads = jnp.concatenate([dq_ref[...], dk_ref[...], dv_ref[...]], axis=0)
    rows = grads.shape[0]
    normed = (x_ref[...].astype(F32) * scale_ref[...] * as_column(gain_ref[...])).astype(BF16)

    @pl.when(step == 0)
    def _():
        total[...] = jnp.zeros_like(total)

    total[:rows] += mm(grads, normed, NT)
    total[rows:] += mm(mixed_ref[...], attn_ref[...])
    out_ref[...] = mm(grads, w_ref[...], TN).astype(BF16)

    @pl.when(step == pl.num_programs(0) - 1)
    def _():
        weight_ref[...] = total[...].astype(BF16)
        through = jnp.sum(total[:rows] * w_ref[...].astype(F32), axis=0, keepdims=True)
        gain_grad_ref[...] = through / gain_ref[...]


def project_back(place, x, gain, scale, weights, mixed, grad_attn, grads, owns, gots):
    width, tokens = x.shape
    rows = weights.shape[0]
    heads_width = mixed.shape[0]
    units = owns[0].shape[0]
    steps = 4
    tile = tokens // steps
    part = units // steps
    column = lambda count: pl.BlockSpec((count, tile), lambda i: (0, i))
    return pl.pallas_call(
        project_back_kernel,
        grid=(steps,),
        in_specs=[
            pl.BlockSpec(memory_space=pltpu.SMEM),
            column(width),
            pl.BlockSpec((1, width), lambda i: (0, 0)),
            column(1),
            pl.BlockSpec((rows, width), lambda i: (0, 0)),
            column(heads_width),
            pl.BlockSpec((tile, width), lambda i: (i, 0)),
        ]
        + [column(rows // 3)] * 3
        + [pl.BlockSpec((part, width), lambda i: (i, 0))] * 6,
        out_specs=[
            pl.BlockSpec((rows + heads_width, width), lambda i: (0, 0)),
            pl.BlockSpec((tile, width), lambda i: (i, 0)),
            pl.BlockSpec((1, width), lambda i: (0, 0)),
        ]
        + [pl.BlockSpec((2, part, width), lambda i: (0, i, 0))] * 3,
        out_shape=[
            jax.ShapeDtypeStruct((rows + heads_width, width), BF16),
            jax.ShapeDtypeStruct((tokens, width), BF16),
            jax.ShapeDtypeStruct((1, width), F32),
        ]
        + [jax.ShapeDtypeStruct((2, units, width), F32)] * 3,
        scratch_shapes=[pltpu.VMEM((rows + heads_width, width), F32)],
        compiler_params=params(),
        cost_estimate=cost(5 * width * tokens * rows, 6 * width * tokens + 14 * units * width),
    )(place, x, gain, scale, weights, mixed, grad_attn, *grads, *owns, *gots)


def exchange(
    math, rank, source, full_out, full, from_across, from_along, to_across, to_along, turn_across, turn_along, sends, recvs, outs, ready=None, ready_full=None, side=None, peers=(), fill=None, start=None, cut=None, later=None):
    pair_class, half_index = rank % 2, rank // 2
    across, along, corner = rank + 1 - 2 * pair_class, rank + 2 - 4 * half_index, 3 - rank
    mesh_ids = pl.DeviceIdType.MESH
    rows, width = source.shape[1:]
    chunks = 4
    size = rows // chunks
    cut = cut or width // 2
    low, high = slice(0, cut), slice(cut, width)
    barrier = pltpu.get_barrier_semaphore()
    near = (across, along, corner) if later else (across, along)
    for other in near:
        pl.semaphore_signal(barrier, inc=1, device_id={"tensor": other}, device_id_type=mesh_ids)
    for other in peers:
        pl.semaphore_signal(barrier, inc=1, device_id={"expert": other}, device_id_type=mesh_ids)
    pl.semaphore_wait(barrier, len(near) + len(peers))

    def remote(kind, chunk, origin, target, other):
        return pltpu.make_async_remote_copy(
            src_ref=origin, dst_ref=target, send_sem=sends.at[kind, chunk], recv_sem=recvs.at[kind, chunk],
            device_id={"tensor": other}, device_id_type=mesh_ids,
        )

    if start:
        start()
    if fill:
        fill(corner)
    spans = [slice(chunk * size, (chunk + 1) * size) for chunk in range(chunks)]
    first, second, third, fourth = [], [], [], []
    for chunk, span in enumerate(spans):
        pair = (
            remote(0, chunk, source.at[corner, span, low], turn_across.at[span, low], across),
            remote(1, chunk, source.at[corner, span, high], turn_along.at[span, high], along),
        )
        for copy in pair:
            copy.start()
        first.append(pair)
    if fill:
        fill(along)
        fill(across)
    leaving = []

    def leave(number, other):
        leaving.append(pltpu.make_async_copy(full.at[other], full_out.at[other], outs.at[number]))
        leaving[-1].start()

    if ready is not None:
        _, near_across, near_along = ready
        extra = [
            remote(8, 0, near_along.at[:, low], ready_full.at[along, :, low], across),
            remote(8, 1, near_across.at[:, high], ready_full.at[across, :, high], along),
        ]
        extra += [
            pltpu.make_async_copy(piece, ready_full.at[other], outs.at[4 + number])
            for number, (other, piece) in enumerate(zip((rank, across, along), ready))
        ]
        for copy in extra:
            copy.start()
    for chunk, span in enumerate(spans):
        if side:
            side(chunk)
        first[chunk][0].wait()
        to_along[span, low] = (source[along, span, low].astype(F32) + turn_across[span, low].astype(F32)).astype(BF16)
        to_along[span, high] = source[along, span, high]
        first[chunk][1].wait()
        to_across[span, low] = source[across, span, low]
        to_across[span, high] = (source[across, span, high].astype(F32) + turn_along[span, high].astype(F32)).astype(BF16)
        pair = (
            remote(2, chunk, to_across.at[span], from_across.at[span], across),
            remote(3, chunk, to_along.at[span], from_along.at[span], along),
        )
        for copy in pair:
            copy.start()
        second.append(pair)
    def pass_on(chunk):
        span = spans[chunk]
        for copy in third[chunk]:
            copy.wait()
        pair = (
            remote(6, chunk, full.at[along, span, low], full.at[along, span, low], across),
            remote(7, chunk, full.at[across, span, high], full.at[across, span, high], along),
        )
        for copy in pair:
            copy.start()
        fourth.append(pair)

    if fill:
        fill(rank)
    if later:
        later((across, along, corner))
    for chunk, span in enumerate(spans):
        if side:
            side(chunks + chunk)
        for copy in second[chunk]:
            copy.wait()
        total = source[rank, span].astype(F32) + from_across[span].astype(F32) + from_along[span].astype(F32)
        full[rank, span] = math(span, total).astype(BF16)
        pair = (
            remote(4, chunk, full.at[rank, span], full.at[rank, span], across),
            remote(5, chunk, full.at[rank, span], full.at[rank, span], along),
        )
        for copy in pair:
            copy.start()
        third.append(pair)
        if chunk:
            pass_on(chunk - 1)
    leave(0, rank)
    pass_on(chunks - 1)
    leave(1, across)
    leave(2, along)
    if ready is not None:
        for copy in extra:
            copy.wait()
    if side and later:
        side(2 * chunks)
    for pair in fourth:
        for copy in pair:
            copy.wait()
    leave(3, corner)
    if side and not later:
        side(2 * chunks)
    for copy in leaving:
        copy.wait()


def exchange_call(kernel, number, shape, operands, extra_shapes, scratch=(), in_hbm=(), out_hbm=()):
    tokens, width = shape
    ranks = 4
    rows = tokens // ranks
    here = pl.BlockSpec(memory_space=pltpu.VMEM)
    results = pl.pallas_call(
        kernel,
        in_specs=[pl.BlockSpec(memory_space=pl.ANY) if k in in_hbm else here for k in range(len(operands))],
        out_specs=[pl.BlockSpec(memory_space=pl.ANY)]
        + [pl.BlockSpec(memory_space=pl.ANY) if k in out_hbm else here for k in range(len(extra_shapes))],
        out_shape=[jax.ShapeDtypeStruct((ranks, rows, width), BF16)]
        + [jax.ShapeDtypeStruct(shape, kind) for shape, kind in extra_shapes],
        scratch_shapes=[pltpu.VMEM((ranks, rows, width), BF16)]
        + [pltpu.VMEM((rows, width), BF16)] * 6
        + [pltpu.SemaphoreType.DMA((9, 4))] * 2
        + [pltpu.SemaphoreType.DMA((7,))]
        + list(scratch),
        compiler_params=pltpu.CompilerParams(
            vmem_limit_bytes=60 * MIB, collective_id=number, has_side_effects=True
        ),
        cost_estimate=cost(40 * MIB, 200 * MIB),
    )(*operands)
    return results[0].reshape(tokens, width), *results[1:]


def norm_two_kernel(
    qkv_ref, tiles_ref, limit_ref, w_ref, x_ref, gain_ref, grad_out_ref, routes_ref, gate_ref,
    full, resid_ref, scale_ref, dy_out, dy_rows_out, code_ref, codes_ref, own_ref, mixed_ref, lse_ref, got_gate, *rest,
):
    source, held, grad_out, dy_ref, dy_rows_ref, load, send, recv = rest[-8:]
    rank = lax.axis_index("tensor")
    ranks, rows, width = source.shape
    loading = pltpu.make_async_copy(grad_out_ref, grad_out, load.at[1])
    storing = [
        pltpu.make_async_copy(dy_ref, dy_out, load.at[2]),
        pltpu.make_async_copy(dy_rows_ref, dy_rows_out, load.at[3]),
    ]

    pair_class = rank % 2
    part = got_gate.shape[0] // 2
    swaps = [
        pltpu.make_async_remote_copy(
            src_ref=gate_ref.at[1 - pair_class, pl.ds((2 + piece) * part, part)],
            dst_ref=got_gate.at[pl.ds(piece * part, part)],
            send_sem=send.at[piece],
            recv_sem=recv.at[piece],
            device_id={"tensor": rank + 1 - 2 * pair_class},
            device_id_type=pl.DeviceIdType.MESH,
        )
        for piece in range(2)
    ]

    def start():
        own.start()
        loading.start()
        swaps[0].start()

    def fill(shard):
        for half in range(2):
            pl.when(shard % 2 == half)(
                partial(attend_half, qkv_ref, tiles_ref, limit_ref, mixed_ref, lse_ref, shard // 2, half)
            )
        columns = pl.ds(pl.multiple_of(shard * rows, rows), rows)
        source[shard] = mm(mixed_ref[:, columns], w_ref[...], TN).astype(BF16)

    slots = dy_rows_ref.shape[0] // ranks
    own = pltpu.make_async_copy(x_ref.at[:, pl.ds(pl.multiple_of(rank * rows, rows), rows)], held, load.at[0])

    def math(span, total):
        resid = own_ref[span, :].astype(F32) + total
        scale = lax.rsqrt(jnp.sum(resid * resid, axis=1, keepdims=True) / resid.shape[1] + EPS)
        resid_ref[span, :] = resid
        scale_ref[span, :] = scale
        return resid * scale * gain_ref[...]

    def later(others):
        own.wait()
        own_ref[...] = held[...].astype(F32).T.astype(BF16)
        local_codes(routes_ref, code_ref, pair_class, rank // 2, CAP // 2)
        codes_ref[...] = jnp.concatenate([code_ref[...].astype(F32)] * 4, axis=0).T[:, :TOP].astype(jnp.int32)
        loading.wait()
        for number in range(ranks):
            span = slice(number * rows, (number + 1) * rows)
            dy_ref[span, :] = grad_out[:, span].astype(F32).T.astype(BF16)
        storing[0].start()

    def side(number):
        if number == 0:
            swaps[1].start()
        elif ranks <= number < 2 * ranks:
            begin = (number - ranks) * slots
            slot = lax.broadcasted_iota(jnp.int32, (slots, dy_ref.shape[0]), 0) + begin
            take = jnp.where((slot == code_ref[0:1]) | (slot == code_ref[1:2]), 1.0, 0.0).astype(BF16)
            dy_rows_ref[begin : begin + slots, :] = mm(take, dy_ref[...]).astype(BF16)
        elif number == 2 * ranks:
            storing[1].start()
            for copy in swaps + storing:
                copy.wait()

    exchange(
        math, rank, source, full, *rest[:-8], side=side, start=start, fill=fill, later=later, cut=3 * width // 8
    )


def norm_back(grad, value, scale, gain):
    scaled = grad * gain
    inner = jnp.sum(scaled * value, axis=1, keepdims=True)
    return scale * scaled - value * (scale * scale * scale) * (inner / value.shape[1])


def norm_two_back_kernel(
    ret_in, back_ref, code_ref, codes_ref, gates_ref, routes_ref, dy_rows_in, gate_ref, router_ref, h_in,
    resid_in, scale_ref, dy_in, gain_ref, full, grad_ref, gain_grad_ref, router_grad_ref, y_out, *rest,
):
    source, scaled, logit_parts, logit_own, send, recv, ret_ref, dy_rows_ref, h_ref, resid_ref, dy_ref, y_ref, load = rest[-13:]
    rank = lax.axis_index("tensor")
    rows = source.shape[1]
    slots, tokens = ret_ref.shape[0], code_ref.shape[1]
    ranks = tokens // rows
    copies = []
    own_dy = dy_in.at[pl.ds(pl.multiple_of(rank * rows, rows), rows)]
    pairs = ((ret_in, ret_ref), (dy_rows_in, dy_rows_ref), (resid_in, resid_ref), (own_dy, dy_ref), (h_in, h_ref))
    loading = [pltpu.make_async_copy(*pair, load.at[number]) for number, pair in enumerate(pairs)]
    storing = [
        pltpu.make_async_copy(y_ref.at[shard], y_out.at[pl.ds(shard * rows, rows)], load.at[5 + shard])
        for shard in range(ranks)
    ]

    def start():
        for copy in loading:
            copy.start()

    def later(others):
        for copy in loading:
            copy.wait()
        found = [jnp.zeros((1, tokens), F32) for _ in range(TOP)]
        tile = slots // 4
        for begin in range(0, slots, tile):
            span = slice(begin, begin + tile)
            ret = ret_ref[span, :].astype(F32)
            slot_grad = jnp.sum(dy_rows_ref[span, :].astype(F32) * ret, axis=1, keepdims=True)
            scaled[span, :] = (ret * gate_ref[span, :]).astype(BF16)
            slot = lax.broadcasted_iota(jnp.int32, (tile, tokens), 0) + begin
            for i in range(TOP):
                found[i] = found[i] + jnp.sum(
                    jnp.where(slot == code_ref[i : i + 1, :], slot_grad, 0.0), axis=0, keepdims=True
                )
        mean = gates_ref[0:1] * found[0] + gates_ref[1:2] * found[1]
        expert = lax.broadcasted_iota(jnp.int32, (EXPERTS, tokens), 0)
        logit = sum(
            jnp.where(routes_ref[i : i + 1] == expert, gates_ref[i : i + 1] * (found[i] - mean), 0.0)
            for i in range(TOP)
        )
        for shard in range(ranks):
            logit_parts[shard] = logit[:, shard * rows : (shard + 1) * rows]
        for number, other in enumerate(others):
            copies.append(
                pltpu.make_async_remote_copy(
                    src_ref=logit_parts.at[other], dst_ref=logit_parts.at[ranks + number], send_sem=send.at[number],
                    recv_sem=recv.at[number], device_id={"tensor": other}, device_id_type=pl.DeviceIdType.MESH,
                )
            )
            copies[-1].start()

    def places(shard):
        slot = lax.broadcasted_iota(jnp.int32, (rows, slots), 1)
        codes = codes_ref[pl.ds(pl.multiple_of(shard * rows, rows), rows), :]
        return jnp.where((slot == codes[:, 0:1]) | (slot == codes[:, 1:2]), 1.0, 0.0).astype(BF16)

    def fill(shard):
        source[shard] = mm(places(shard), back_ref[...]).astype(BF16)

    def side(number):
        if number == ranks:
            router_grad_ref[...] = sum(
                mm(logit_parts[shard].astype(BF16), h_ref[shard * rows : (shard + 1) * rows, :])
                for shard in range(ranks)
            )
            for copy in copies:
                copy.wait()
            logit = logit_parts[rank] + logit_parts[ranks] + logit_parts[ranks + 1] + logit_parts[ranks + 2]
            coarse = logit.astype(BF16)
            logit_own[:EXPERTS] = coarse
            logit_own[EXPERTS:] = (logit - coarse.astype(F32)).astype(BF16)
        elif number > ranks:
            shard = number - ranks - 1
            y_ref[shard] = mm(places(shard), scaled[...]).astype(BF16)
            storing[shard].start()
            if shard == ranks - 1:
                for copy in storing:
                    copy.wait()

    gain_grad_ref[...] = jnp.zeros_like(gain_grad_ref)

    def math(span, total):
        resid, scale = resid_ref[span, :], scale_ref[span, :]
        both = jnp.concatenate([router_ref[...], router_ref[...]], axis=0)
        total = total + mm(logit_own[:, span], both, TN)
        gain_grad_ref[...] += jnp.sum(total * resid * scale, axis=0, keepdims=True)
        grad = norm_back(total, resid, scale, gain_ref[...]) + dy_ref[span, :].astype(F32)
        grad_ref[span, :] = grad
        return grad

    exchange(math, rank, source, full, *rest[:-13], side=side, fill=fill, start=start, later=later)


def norm_one_back_kernel(
    source, x_in, scale_ref, grad_in, gain_ref, y_own, y_across, y_along, gain_one_ref, gain_two_ref, router_ref,
    near_ref, far_ref, full, ready_full, small_out, *rest,
):
    x_ref, grad_ref, held, gathered, near, scale, load, tensor_sends, tensor_recvs, expert_sends, expert_recvs = rest[-11:]
    rank, group = lax.axis_index("tensor"), lax.axis_index("expert")
    pair_class, half_index = rank % 2, rank // 2
    others = rank + 1 - 2 * pair_class, rank + 2 - 4 * half_index
    groups = expert_sends.shape[0]
    mesh_ids = pl.DeviceIdType.MESH
    peers = [partner_of(group, step) for step in range(1, groups)]
    heads = near_ref.shape[0] // 2
    rows = source.shape[1]
    pairs = ((near_ref, near), (x_in, x_ref), (grad_in, grad_ref))
    loading = [pltpu.make_async_copy(*pair, load.at[number]) for number, pair in enumerate(pairs)]

    def math(span, total):
        x = x_ref[span, :].astype(F32)
        return norm_back(total, x, scale[span, :], gain_ref[...]) + grad_ref[span, :]

    def to_rank(step):
        return pltpu.make_async_remote_copy(
            src_ref=held.at[step], dst_ref=held.at[2 + step], send_sem=tensor_sends.at[step],
            recv_sem=tensor_recvs.at[step], device_id={"tensor": others[step]}, device_id_type=mesh_ids,
        )

    def to_group(step):
        return pltpu.make_async_remote_copy(
            src_ref=gathered.at[group], dst_ref=gathered.at[group], send_sem=expert_sends.at[step],
            recv_sem=expert_recvs.at[step], device_id={"expert": peers[step - 1]}, device_id_type=mesh_ids,
        )

    def start():
        for copy in loading:
            copy.start()
        held[0] = jnp.zeros(small_out.shape, F32)
        held[0, :EXPERTS] = router_ref[...]
        held[0, EXPERTS : EXPERTS + 1] = gain_two_ref[...]
        held[0, EXPERTS + 1 : EXPERTS + 2] = gain_one_ref[...]
        to_rank(0).start()

    def side(number):
        if number == 0:
            own_scale = scale_ref[:, pl.ds(pl.multiple_of(rank * rows, rows), rows)]
            scale[...] = jnp.broadcast_to(own_scale, (8, rows)).T[:, :1]
            for copy in loading:
                copy.wait()
            small_out[:BUCKETS, :128] = bias_fold(near, far_ref)
        elif number == 1:
            to_rank(0).wait()
            held[1] = held[0] + held[2]
            to_rank(1).start()
        elif number == 5:
            to_rank(1).wait()
            turned = small_out[:BUCKETS, :128].T
            held[0] = held[1] + held[3]
            held[0, EXPERTS + 2 : EXPERTS + 2 + heads, :BUCKETS] = turned[:heads]
            gathered[group] = held[0].astype(BF16)
            for step in range(1, groups):
                to_group(step).start()
        elif number == 8:
            for step in range(1, groups):
                to_group(step).wait()
            total = gathered[0].astype(F32)
            for step in range(1, groups):
                total = total + gathered[step].astype(F32)
            small_out[...] = total

    exchange(
        math, rank, source, full, *rest[:-11], (y_own, y_across, y_along), ready_full, side=side, peers=peers, start=start
    )


def local_codes(routes_ref, code_ref, pair_class, half_index, half):
    tokens = routes_ref.shape[1]
    expert = lax.broadcasted_iota(jnp.int32, (EXPERTS, BLK), 0)
    earlier = (
        lax.broadcasted_iota(jnp.int32, (BLK, BLK), 0) < lax.broadcasted_iota(jnp.int32, (BLK, BLK), 1)
    ).astype(F32).astype(BF16)
    carry = jnp.zeros((EXPERTS, 1), F32)
    for block in range(tokens // BLK):
        cols = slice(block * BLK, (block + 1) * BLK)
        routes = routes_ref[:, cols]
        hits = [(routes[i : i + 1] == expert) for i in range(TOP)]
        chosen = sum(hit.astype(F32) for hit in hits)
        before = mm(chosen.astype(BF16), earlier) + carry
        carry = carry + jnp.sum(chosen, axis=1, keepdims=True)
        for i in range(TOP):
            slot = jnp.sum(jnp.where(hits[i], before, 0.0), axis=0, keepdims=True).astype(jnp.int32)
            route = routes[i : i + 1]
            owner = route // 2
            local = slot - half_index * half
            mine = (route - 2 * owner == pair_class) & (local >= 0) & (local < half)
            code_ref[i : i + 1, cols] = jnp.where(mine, owner * half + local, -1)


def dispatch_kernel(code_ref, routes_ref, router_ref, h_ref, dy_rows_ref, rows_ref, grads_ref, gate_ref, gates_ref):
    count, tokens = rows_ref.shape[0], h_ref.shape[0]

    @pl.when(pl.program_id(0) == 0)
    def _():
        expert = lax.broadcasted_iota(jnp.int32, (EXPERTS, tokens), 0)
        logits = mm(router_ref[...], h_ref[...], NT)
        picked = [
            jnp.sum(jnp.where(routes_ref[i : i + 1] == expert, logits, 0.0), axis=0, keepdims=True)
            for i in range(TOP)
        ]
        top = jnp.maximum(picked[0], picked[1])
        raised = [jnp.exp(value - top) for value in picked]
        total = raised[0] + raised[1]
        for i in range(TOP):
            gates_ref[i : i + 1] = raised[i] / total

    slot = lax.broadcasted_iota(jnp.int32, (count, tokens), 0) + pl.program_id(0) * count
    hits = [slot == code_ref[i : i + 1, :] for i in range(TOP)]
    take = jnp.where(hits[0] | hits[1], 1.0, 0.0).astype(BF16)
    weighted = jnp.where(hits[0], gates_ref[0:1, :], jnp.where(hits[1], gates_ref[1:2, :], 0.0))
    gate = jnp.sum(weighted, axis=1, keepdims=True)
    rows_ref[...] = mm(take, h_ref[...]).astype(BF16)
    grads_ref[...] = (dy_rows_ref[...].astype(F32) * gate).astype(BF16)
    gate_ref[...] = gate


def dispatch(code, routes_t, router_t, h, dy_rows):
    slots, width = dy_rows.shape
    tile = slots // 4
    row_spec = pl.BlockSpec((tile, width), lambda i: (i, 0))
    whole = lambda shape: pl.BlockSpec(shape, lambda i: (0, 0))
    return pl.pallas_call(
        dispatch_kernel,
        grid=(4,),
        in_specs=[whole(code.shape), whole(code.shape), whole(router_t.shape), whole(h.shape), row_spec],
        out_specs=[row_spec, row_spec, pl.BlockSpec((tile, 1), lambda i: (i, 0)), whole(code.shape)],
        out_shape=[jax.ShapeDtypeStruct((slots, width), BF16)] * 2
        + [jax.ShapeDtypeStruct((slots, 1), F32), jax.ShapeDtypeStruct(code.shape, F32)],
        compiler_params=params(),
        cost_estimate=cost(4 * slots * SEQ * width, 4 * MIB + 6 * slots * width),
    )(code, routes_t, router_t, h, dy_rows)


def gelu_parts(x):
    inner = 0.7978845608028654 * (x + 0.044715 * (x * x * x))
    bend = jnp.tanh(inner)
    half = 0.5 * (1.0 + bend)
    slope = half + 0.5 * x * (1.0 - bend * bend) * (
        0.7978845608028654 * (1.0 + 3.0 * 0.044715 * (x * x))
    )
    return x * half, slope


def partner_of(index, step):
    found = index
    for bit in (1, 2, 4):
        found = found + ((step // bit) % 2) * (1 - 2 * ((index // bit) % 2)) * bit
    return found


def expert_kernel(
    rows_in, grads_in, gate_in, up_in, down_in, far_gate, far_gate_too,
    ret_out, back_out, own_gate, own_up, own_down, got_gate, got_up, got_down,
    rows, grads, weights, sums, parts, opened, z_send, z_recv, y_send, y_recv, p_send, p_recv, r_send, r_recv, w_send, w_recv, g_send, g_recv, local,
):
    groups, half, width = rows.shape[1:]
    group, rank = lax.axis_index("expert"), lax.axis_index("tensor")
    pair_class, half_index = rank % 2, rank // 2
    across = {"tensor": rank + 1 - 2 * pair_class}
    along = {"tensor": rank + 2 - 4 * half_index}
    mesh_ids = pl.DeviceIdType.MESH
    moved = ((rows_in, rows, ret_out), (grads_in, grads, back_out))

    barrier = pltpu.get_barrier_semaphore()
    for step in range(1, groups):
        pl.semaphore_signal(
            barrier, inc=1, device_id={"expert": partner_of(group, step)}, device_id_type=mesh_ids
        )
    pl.semaphore_signal(barrier, inc=1, device_id=across, device_id_type=mesh_ids)
    pl.semaphore_signal(barrier, inc=1, device_id=along, device_id_type=mesh_ids)
    pl.semaphore_wait(barrier, groups + 1)

    def remote(source, target, send, recv, device):
        return pltpu.make_async_remote_copy(
            src_ref=source, dst_ref=target, send_sem=send, recv_sem=recv,
            device_id=device, device_id_type=mesh_ids,
        )

    def block(ref, number):
        return ref.at[pl.ds(pl.multiple_of(number * half, half), half)]

    def out_of(kind, step):
        source, held, _ = moved[kind]
        other = partner_of(group, step)
        return remote(
            block(source, other), held.at[0, group], z_send.at[kind, step], z_recv.at[kind, step], {"expert": other}
        )

    def forward(kind, step):
        held = moved[kind][1]
        other = partner_of(group, step)
        return remote(held.at[0, other], held.at[1, other], y_send.at[kind, step], y_recv.at[kind, step], along)

    def partial_sum(kind, step):
        held = moved[kind][1]
        other = partner_of(group, step)
        return remote(held.at[1, other], parts.at[kind, other], p_send.at[kind, step], p_recv.at[kind, step], along)

    def result(kind, step):
        other = partner_of(group, step)
        return remote(
            parts.at[kind, other], block(moved[kind][2], group), r_send.at[kind, step], r_recv.at[kind, step], {"expert": other}
        )

    def own_result(kind):
        return pltpu.make_async_copy(parts.at[kind, group], block(moved[kind][2], group), local.at[kind])

    own = [
        pltpu.make_async_copy(block(moved[kind][0], group), moved[kind][1].at[0, group], local.at[kind])
        for kind in range(2)
    ]
    for copy in own:
        copy.start()
    kept = [
        pltpu.make_async_copy(ref.at[pair_class], weights.at[number, 0], local.at[2 + number])
        for number, ref in enumerate((gate_in, up_in, down_in))
    ]
    some = far_gate.shape[0]
    for number, ref in enumerate((far_gate, far_gate_too)):
        target = weights.at[0, 1, pl.ds(number * some, some)]
        kept.append(pltpu.make_async_copy(ref, target, local.at[5 + number]))
    kept += [
        remote(ref.at[1 - pair_class], weights.at[number, 1], w_send.at[number - 1], w_recv.at[number - 1], across)
        for number, ref in ((1, up_in), (2, down_in))
    ]
    for copy in kept:
        copy.start()
    for step in range(1, groups):
        for kind in range(2):
            out_of(kind, step).start()

    def arrive(step):
        for kind in range(2):
            out_of(kind, step).wait()
            forward(kind, step).start()

    def give(step):
        for kind in range(2):
            partial_sum(kind, step).start()

    for number in range(3):
        for part in range(2):
            sums[number, part] = jnp.zeros(sums.shape[2:], F32)

    def finish(step):
        other = partner_of(group, step)
        for kind in range(2):
            partial_sum(kind, step).wait()
            held = moved[kind][1]
            parts[kind, other] = (parts[kind, other].astype(F32) + held[0, other].astype(F32)).astype(BF16)

        for kind in range(2):
            if step == 0:
                own_result(kind).start()
            else:
                result(kind, step).start()

    def act(plan):
        for action, step in plan:
            action(step)

    order = ((0, 0, 0), (1, 0, 1), (2, 0, 2), (3, 0, 3), (2, 1, 2), (4, 0, 2), (4, 1, 2), (5, 0, 2), (5, 1, 2), (3, 1, 3), (1, 1, 1), (0, 1, 0), (6, 0, 0), (6, 1, 0), (7, 0, 0), (7, 1, 0))
    before = {
        0: [(arrive, 1), (arrive, 2)],
        1: [(arrive, 3)],
        2: [(arrive, 4)],
        3: [(arrive, 5)],
        5: [(give, 2)],
        7: [(give, 4)],
        8: [(arrive, 6)],
        10: [(finish, 2)],
        12: [(arrive, 7), (finish, 4), (give, 5)],
        14: [(give, 6)],
    }
    ahead = [(give, 7)]
    last = [(finish, 5), (give, 3), (finish, 6), (give, 1), (finish, 7), (give, 0), (finish, 3), (finish, 1), (finish, 0)]
    first_far = [part for _, part, _ in order].index(1)
    for copy in own:
        copy.wait()
    for kind in range(2):
        forward(kind, 0).start()

    def body(turn, carry):
        for number, plan in before.items():
            pl.when(turn == number)(partial(act, plan))

        @pl.when(turn == 0)
        def _():
            for copy in kept[:3]:
                copy.wait()

        @pl.when(turn == first_far)
        def _():
            for copy in kept[3:]:
                copy.wait()

        step, part, place = (
            sum((turn == number).astype(jnp.int32) * unit[k] for number, unit in enumerate(order)) for k in range(3)
        )
        other = partner_of(group, step)

        @pl.when(part == 0)
        def _():
            for kind in range(2):
                forward(kind, step).wait()

        tile = jnp.concatenate([rows[0, other], rows[1, other]], axis=0)
        grad = jnp.concatenate([grads[0, other], grads[1, other]], axis=0)
        w_gate, w_up, w_down = weights[0, part], weights[1, part], weights[2, part]
        gate_part = mm(tile, w_gate, NT)
        up_part = mm(tile, w_up, NT)
        grad_hidden = mm(grad, w_down, NT)
        bent, slope = gelu_parts(gate_part)
        hidden = (bent * up_part).astype(BF16)
        grad_gate = (grad_hidden * up_part * slope).astype(BF16)
        grad_up = (grad_hidden * bent).astype(BF16)
        results = mm(hidden, w_down), mm(grad_gate, w_gate) + mm(grad_up, w_up)
        sums[0, part] += mm(grad_gate, tile, TN)
        sums[1, part] += mm(grad_up, tile, TN)
        sums[2, part] += mm(hidden, grad, TN)

        @pl.when(part == 0)
        def _():
            for kind, value in enumerate(results):
                opened[place, kind] = value.astype(BF16)

        @pl.when(part == 1)
        def _():
            for kind, value in enumerate(results):
                held = moved[kind][1]
                value = value + opened[place, kind].astype(F32)
                held[0, other] = value[:half].astype(BF16)
                held[1, other] = value[half:].astype(BF16)

        return carry

    lax.fori_loop(0, len(order), body, 0)
    act(ahead)
    copies = []
    for number, (own_ref, got_ref) in enumerate(((own_gate, got_gate), (own_up, got_up), (own_down, got_down))):
        weights[number, 0] = sums[number, 1].astype(BF16)
        copies.append(remote(weights.at[number, 0], got_ref, g_send.at[number], g_recv.at[number], across))
        copies[-1].start()
        copies.append(pltpu.make_async_copy(sums.at[number, 0], own_ref, local.at[2 + number]))
        copies[-1].start()
    act(last)
    for copy in copies:
        copy.wait()
    for kind in range(2):
        own_result(kind).wait()
        for step in range(1, groups):
            result(kind, step).wait()


def run_experts(rows, grads, w_gate, w_up, w_down, far_gate, far_gate_too):
    slots, width = rows.shape
    half = CAP // 2
    groups = slots // half
    units = w_gate.shape[1]
    anywhere = pl.BlockSpec(memory_space=pl.ANY)
    pair = pltpu.SemaphoreType.DMA((2, groups))
    return pl.pallas_call(
        expert_kernel,
        in_specs=[anywhere] * 7,
        out_specs=[anywhere] * 8,
        out_shape=[jax.ShapeDtypeStruct((slots, width), BF16)] * 2
        + [jax.ShapeDtypeStruct((units, width), F32)] * 3
        + [jax.ShapeDtypeStruct((units, width), BF16)] * 3,
        scratch_shapes=[
            pltpu.VMEM((2, groups, half, width), BF16),
            pltpu.VMEM((2, groups, half, width), BF16),
            pltpu.VMEM((3, 2, units, width), BF16),
            pltpu.VMEM((3, 2, units, width), F32),
            pltpu.VMEM((2, groups, half, width), BF16),
            pltpu.VMEM((4, 2, 2 * half, width), BF16),
        ]
        + [pair] * 8
        + [pltpu.SemaphoreType.DMA((2,))] * 2
        + [pltpu.SemaphoreType.DMA((3,))] * 2
        + [pltpu.SemaphoreType.DMA((7,))],
        compiler_params=pltpu.CompilerParams(
            vmem_limit_bytes=60 * MIB, collective_id=1, has_side_effects=True
        ),
        cost_estimate=cost(72 * slots * units * width, 16 * slots * width + 30 * units * width),
    )(rows, grads, w_gate, w_up, w_down, far_gate, far_gate_too)


def finish_kernel(
    rows_ref, y_ref, summed_ref, small_ref,
    output_ref, grad_ref, in_ref, out_ref, one_ref, two_ref, router_ref, bias_ref,
):
    step = pl.program_id(0)
    output_ref[...] = y_ref[...].astype(F32).T.astype(BF16)
    grad_ref[...] = rows_ref[...].astype(F32).T

    @pl.when(step < 3)
    def _():
        in_ref[...] = summed_ref[...].astype(F32)

    @pl.when(step == 3)
    def _():
        out_ref[...] = summed_ref[...].astype(F32)
        router_ref[...] = small_ref[:EXPERTS]
        two_ref[...] = small_ref[EXPERTS : EXPERTS + 1]
        one_ref[...] = small_ref[EXPERTS + 1 : EXPERTS + 2]
        bias_ref[...] = small_ref[EXPERTS + 2 : EXPERTS + 2 + bias_ref.shape[0], :BUCKETS]


def finish_outputs(rows, y_rows, summed, small, heads):
    tokens, width = rows.shape
    steps = 4
    tile, block = tokens // steps, summed.shape[0] // steps
    token_spec = pl.BlockSpec((tile, width), lambda i: (i, 0))
    feature_spec = pl.BlockSpec((width, tile), lambda i: (0, i))
    whole = lambda *shape: pl.BlockSpec(shape, lambda i: (0, 0))
    return pl.pallas_call(
        finish_kernel,
        grid=(steps,),
        in_specs=[
            token_spec,
            token_spec,
            pl.BlockSpec((block, width), lambda i: (i, 0)),
            whole(*small.shape),
        ],
        out_specs=[
            feature_spec,
            feature_spec,
            pl.BlockSpec((block, width), lambda i: (jnp.minimum(i, 2), 0)),
            whole(block, width),
            whole(1, width),
            whole(1, width),
            whole(EXPERTS, width),
            whole(heads, BUCKETS),
        ],
        out_shape=[
            jax.ShapeDtypeStruct((width, tokens), BF16),
            jax.ShapeDtypeStruct((width, tokens), F32),
            jax.ShapeDtypeStruct((3 * block, width), F32),
            jax.ShapeDtypeStruct((block, width), F32),
            jax.ShapeDtypeStruct((1, width), F32),
            jax.ShapeDtypeStruct((1, width), F32),
            jax.ShapeDtypeStruct((EXPERTS, width), F32),
            jax.ShapeDtypeStruct((heads, BUCKETS), F32),
        ],
        compiler_params=params(),
        cost_estimate=cost(0, 10 * rows.size + 6 * summed.size),
    )(rows, y_rows, summed, small)


def on_device(
    layer_input, gain_one, attn_in, rel_bias, attn_out, gain_two, router,
    expert_gate, expert_up, expert_down, routes, piece_starts, grad_out,
):
    width, tokens = layer_input.shape
    ranks = lax.axis_size("tensor")
    groups = lax.axis_size("expert")
    rank = lax.axis_index("tensor")
    pair_class, half_index = rank % 2, rank // 2
    half = CAP // 2

    units = expert_gate.shape[1]
    other = lax.dynamic_slice(expert_gate, (1 - pair_class, 0, 0), (1, units // 2, width))[0]
    traded = lax.ppermute(other, "tensor", [(r, r ^ 1) for r in range(ranks)])
    w_in = attn_in.reshape(-1, width)
    qkv, scale_one, tiles = project(layer_input, gain_one[None], w_in, rel_bias.T)
    position = jnp.arange(SEQ, dtype=jnp.int32)[None, None, :]
    starts = piece_starts[:, :, None]
    inside = (position >= starts) & (position < starts + PIECE)
    last = jnp.max(jnp.where(inside, starts + (PIECE - 1), -1), axis=1)
    limits = jnp.maximum(last, position[0])[:, None, :]

    routes_t = routes.T
    place = jnp.stack([pair_class, half_index]).astype(jnp.int32)
    share = tokens // ranks

    def by_rank(rows):
        return rows.reshape(ranks, share, width)

    qkv, traded = lax.optimization_barrier((qkv, traded))
    slots = groups * half
    heads = rel_bias.shape[1]
    h2, resid, scale_two, dy, dy_rows, code, code_cols, own_x, mixed, lse, traded_too = exchange_call(
        norm_two_kernel, 2, (tokens, width),
        [qkv, tiles, limits, attn_out, layer_input, gain_two[None], grad_out, routes_t, expert_gate],
        [((share, width), F32), ((share, 1), F32), ((tokens, width), BF16), ((slots, width), BF16)]
        + [((TOP, tokens), jnp.int32), ((tokens, TOP), jnp.int32), ((share, width), BF16)]
        + [(attn_out.shape[:1] + (tokens,), BF16), ((heads * tokens // SEQ, 1, SEQ), F32), (traded.shape, BF16)],
        [pltpu.VMEM((ranks, share, width), BF16), pltpu.VMEM((width, share), BF16), pltpu.VMEM((width, tokens), BF16)]
        + [pltpu.VMEM((tokens, width), BF16), pltpu.VMEM((slots, width), BF16), pltpu.SemaphoreType.DMA((4,))]
        + [pltpu.SemaphoreType.DMA((2,))] * 2,
        (4, 6, 8),
        (2, 3, 9),
    )
    rows, row_grads, gate_rows, gates = dispatch(code, routes_t, router.T, h2, dy_rows)
    ret, back, *weight_grads = run_experts(
        rows, row_grads, expert_gate, expert_up, expert_down, traded, traded_too
    )
    grad_attn, grad_resid, grad_gain_two, grad_router, partial_y = exchange_call(
        norm_two_back_kernel, 3, (tokens, width),
        [ret, back, code, code_cols, gates, routes_t, dy_rows, gate_rows, router.T, h2]
        + [resid, scale_two, dy, gain_two[None]],
        [((share, width), F32), ((1, width), F32), ((EXPERTS, width), F32), ((tokens, width), BF16)],
        [
            pltpu.VMEM((ranks, share, width), BF16),
            pltpu.VMEM((slots, width), BF16),
            pltpu.VMEM((ranks + 3, EXPERTS, share), F32),
            pltpu.VMEM((2 * EXPERTS, share), BF16),
        ]
        + [pltpu.SemaphoreType.DMA((3,))] * 2
        + [pltpu.VMEM((slots, width), BF16)] * 2
        + [pltpu.VMEM((tokens, width), BF16), pltpu.VMEM((share, width), F32), pltpu.VMEM((share, width), BF16)]
        + [pltpu.VMEM((ranks, share, width), BF16), pltpu.SemaphoreType.DMA((9,))],
        (0, 6, 9, 10, 12),
        (3,),
    )

    dq, dk, dv, near, far, y_own = attend_back(
        qkv, tiles, limits, attn_out, grad_attn, lse, by_rank(partial_y), resid
    )
    dq, y_own = lax.optimization_barrier((dq, y_own))
    y_across = lax.ppermute(y_own, "tensor", [(r, r ^ 1) for r in range(ranks)])
    y_along = lax.ppermute(y_own, "tensor", [(r, r ^ 2) for r in range(ranks)])
    weight_rows, sent, grad_gain_one, grad_gate, grad_up, grad_down = project_back(
        place, layer_input, gain_one[None], scale_one, w_in, mixed, grad_attn, (dq, dk, dv),
        weight_grads[:3], weight_grads[3:],
    )
    sent, y_across, y_along = lax.optimization_barrier((sent, y_across, y_along))
    summed = lax.psum(weight_rows, "expert")
    small_shape = (BUCKETS, width)
    grad_rows, y_full, small = exchange_call(
        norm_one_back_kernel, 4, sent.shape,
        [by_rank(sent), own_x, scale_one, grad_resid, gain_one[None], y_own, y_across, y_along]
        + [grad_gain_one, grad_gain_two, grad_router, near, far],
        [((ranks, share, width), BF16), (small_shape, F32)],
        [pltpu.VMEM((share, width), BF16), pltpu.VMEM((share, width), F32)]
        + [pltpu.VMEM((4, *small_shape), F32), pltpu.VMEM((groups, *small_shape), BF16), pltpu.VMEM(near.shape, F32), pltpu.VMEM((share, 1), F32)]
        + [pltpu.SemaphoreType.DMA((3,))]
        + [pltpu.SemaphoreType.DMA((2,))] * 2
        + [pltpu.SemaphoreType.DMA((groups,))] * 2,
        (1, 3, 11),
        (0,),
    )
    summed, grad_rows = lax.optimization_barrier((summed, grad_rows))
    layer_output, grad_input, grad_in, grad_attn_out, grad_one, grad_two, grad_router, grad_bias = finish_outputs(
        grad_rows, y_full.reshape(tokens, width), summed, small, rel_bias.shape[1]
    )
    return (
        layer_output,
        grad_input,
        grad_one[0],
        grad_in.reshape(attn_in.shape),
        grad_bias.T,
        grad_attn_out,
        grad_two[0],
        grad_router.T,
        grad_gate,
        grad_up,
        grad_down,
    )


def allowed_pairs(seq_starts):
    position = jnp.arange(SEQ, dtype=jnp.int32)
    inside = (position[:, None] >= seq_starts[None, :]) & (
        position[:, None] < seq_starts[None, :] + PIECE
    )
    numbers = jnp.arange(seq_starts.shape[0], dtype=jnp.int32) + 1
    piece_label = jnp.sum(inside.astype(jnp.int32) * numbers[None, :], axis=1)
    causal = position[None, :] <= position[:, None]
    shared = (piece_label[:, None] == piece_label[None, :]) & (piece_label[:, None] > 0)
    return causal | shared


def slot_table(routes):
    flat_routes = routes.reshape(-1)
    onehot = (flat_routes[:, None] == jnp.arange(EXPERTS, dtype=jnp.int32)[None, :]).astype(
        jnp.int32
    )
    blocks = onehot.reshape(-1, 128, EXPERTS).astype(F32)
    earlier = jnp.tril(jnp.ones((128, 128), F32), -1)
    inside = jnp.einsum("ij,bje->bie", earlier, blocks)
    count = blocks.shape[0]
    carried = jnp.einsum("ab,be->ae", jnp.tril(jnp.ones((count, count), F32), -1), jnp.sum(blocks, axis=1), precision=HIGH)
    before = (inside + carried[:, None, :]).astype(jnp.int32).reshape(onehot.shape)
    slot_number = jnp.sum(before * onehot, axis=1)
    kept_pairs = slot_number < CAP
    slot_index = jnp.where(kept_pairs, flat_routes * CAP + slot_number, EXPERTS * CAP)
    return (slot_index.reshape(routes.shape), kept_pairs.reshape(routes.shape))


def bucket_onehot():
    offsets = jnp.arange(2 * SEQ - 1, dtype=jnp.int32) - (SEQ - 1)
    return (bucket_of(offsets)[:, None] == jnp.arange(BUCKETS, dtype=jnp.int32)[None, :]).astype(
        jnp.float32
    )


def expand_line(line):
    head_count = line.shape[0]
    padded = jnp.concatenate([line, jnp.zeros((head_count, 1), line.dtype)], axis=1)
    tiled = jnp.tile(padded, (1, SEQ))[:, : SEQ * (2 * SEQ - 1)].reshape(
        head_count, SEQ, 2 * SEQ - 1
    )
    return tiled[:, :, SEQ - 1 :]


def fold_line(full_grid):
    head_count = full_grid.shape[0]
    padded = jnp.pad(full_grid, ((0, 0), (0, 0), (SEQ - 1, 0))).reshape(
        head_count, SEQ * (2 * SEQ - 1)
    )
    padded = jnp.pad(padded, ((0, 0), (0, SEQ))).reshape(head_count, SEQ, 2 * SEQ)
    return jnp.sum(padded, axis=1)[:, : 2 * SEQ - 1]


def reduce_heads(tensor_value):
    return lax.psum(tensor_value, "tensor")


def spread_slots(tensor_value):
    return lax.all_gather(tensor_value, "tensor", axis=2, tiled=True)


def owner_exchange(tensor_value):
    return lax.all_to_all(tensor_value, "expert", split_axis=0, concat_axis=0, tiled=True)


def expert_sums(tensor_value):
    return lax.psum_scatter(tensor_value, "tensor", scatter_dimension=2, tiled=True)


def norm_forward(resid, gain, model_width):
    scale = lax.rsqrt(jnp.sum(resid * resid, axis=1) / model_width + EPS)[:, None]
    return (scale, (resid * scale * gain).astype(jnp.bfloat16))


def norm_backward(resid, scale, gain, grad_normed, model_width):
    grad_gain = jnp.sum(grad_normed * resid * scale, axis=0)
    scaled = grad_normed * gain
    inner = jnp.sum(scaled * resid, axis=1)[:, None]
    return (grad_gain, scale * scaled - resid * scale**3 * inner / model_width)


def attend_scores(bias_full, queries, key_rows, seq_starts):
    scores = (
        jnp.einsum("qhe,khe->hqk", queries, key_rows, preferred_element_type=jnp.float32) * 0.125
        + bias_full
    )
    return jnp.where(allowed_pairs(seq_starts)[None], scores, NEG)


def attend_forward(bias_full, inputs):
    queries, key_rows, value_rows, seq_starts = inputs
    scores = attend_scores(bias_full, queries, key_rows, seq_starts)
    row_max = jnp.max(scores, axis=2, keepdims=True)
    exponent = jnp.exp(scores - row_max)
    row_sum_exp = jnp.sum(exponent, axis=2, keepdims=True)
    weights = (exponent / row_sum_exp).astype(jnp.bfloat16)
    mixed_heads = jnp.einsum(
        "hqk,khe->qhe", weights, value_rows, preferred_element_type=jnp.float32
    )
    return (mixed_heads.astype(jnp.bfloat16), (row_max + jnp.log(row_sum_exp))[:, :, 0])


def attend_backward(bias_full, running, inputs):
    queries, key_rows, value_rows, grad_heads, seq_starts, log_total = inputs
    scores = attend_scores(bias_full, queries, key_rows, seq_starts)
    probabilities = jnp.exp(scores - log_total[:, :, None])
    grad_probs = jnp.einsum(
        "qhe,khe->hqk", grad_heads, value_rows, preferred_element_type=jnp.float32
    )
    inner = jnp.sum(probabilities * grad_probs, axis=2, keepdims=True)
    grad_scores = (probabilities * (grad_probs - inner)).astype(jnp.bfloat16)
    grad_values = jnp.einsum(
        "hqk,qhe->khe",
        probabilities.astype(jnp.bfloat16),
        grad_heads,
        preferred_element_type=jnp.float32,
    )
    grad_queries = (
        jnp.einsum("hqk,khe->qhe", grad_scores, key_rows, preferred_element_type=jnp.float32)
        * 0.125
    )
    grad_keys = (
        jnp.einsum("hqk,qhe->khe", grad_scores, queries, preferred_element_type=jnp.float32) * 0.125
    )
    return (
        running + grad_scores.astype(jnp.float32),
        jnp.stack([grad_queries, grad_keys, grad_values]),
    )


def gelu_product(left, right):
    return jax.nn.gelu(left, approximate=True) * right


def expert_forward(received, weight_gate, weight_up, weight_down):
    gate_part = jnp.einsum(
        "secd,efd->secf", received, weight_gate, preferred_element_type=jnp.float32
    )
    up_part = jnp.einsum("secd,efd->secf", received, weight_up, preferred_element_type=jnp.float32)
    hidden = gelu_product(gate_part, up_part).astype(jnp.bfloat16)
    partial_out = jnp.einsum(
        "secf,efd->secd", hidden, weight_down, preferred_element_type=jnp.float32
    )
    return (gate_part, up_part, hidden, partial_out)


def expert_backward(
    received, gate_part, up_part, hidden, grad_rows_out, weight_gate, weight_up, weight_down
):
    grad_hidden = jnp.einsum(
        "secd,efd->secf", grad_rows_out, weight_down, preferred_element_type=jnp.float32
    )
    product_value, pullback = jax.vjp(gelu_product, gate_part, up_part)
    grad_gate_part, grad_up_part = pullback(grad_hidden)
    grad_gate_part = grad_gate_part.astype(jnp.bfloat16)
    grad_up_part = grad_up_part.astype(jnp.bfloat16)
    grad_down = jnp.einsum(
        "secf,secd->efd", hidden, grad_rows_out, preferred_element_type=jnp.float32
    )
    grad_gate_w = jnp.einsum(
        "secf,secd->efd", grad_gate_part, received, preferred_element_type=jnp.float32
    )
    grad_up_w = jnp.einsum(
        "secf,secd->efd", grad_up_part, received, preferred_element_type=jnp.float32
    )
    grad_rows_in = jnp.einsum(
        "secf,efd->secd", grad_gate_part, weight_gate, preferred_element_type=jnp.float32
    )
    grad_rows_in = grad_rows_in + jnp.einsum(
        "secf,efd->secd", grad_up_part, weight_up, preferred_element_type=jnp.float32
    )
    return (grad_gate_w, grad_up_w, grad_down, grad_rows_in)


def on_device_general(
    layer_input,
    gain_one,
    attn_in,
    rel_bias,
    attn_out,
    gain_two,
    router,
    expert_gate,
    expert_up,
    expert_down,
    routes,
    piece_starts,
    grad_out,
):
    tok_count = layer_input.shape[1]
    model_width = layer_input.shape[0]
    heads_here = rel_bias.shape[1]
    head_width = attn_in.shape[1] // heads_here
    seqs_here = piece_starts.shape[0]
    local_experts = expert_gate.shape[0]
    part_rows = CAP // lax.axis_size("tensor")
    share_start = lax.axis_index("tensor") * part_rows
    tokens = layer_input.T.astype(jnp.float32)
    scale_one, normed = norm_forward(tokens, gain_one, model_width)
    project = jnp.einsum("td,chd->cth", normed, attn_in, preferred_element_type=jnp.float32).astype(
        jnp.bfloat16
    )
    by_seq = project.reshape(3, seqs_here, SEQ, heads_here, head_width)
    onehot_line = bucket_onehot()
    bias_full = expand_line(jnp.dot(onehot_line, rel_bias, precision=HIGH).T)
    mixed_heads, log_total = lax.map(
        partial(attend_forward, bias_full), (by_seq[0], by_seq[1], by_seq[2], piece_starts)
    )
    mixed_heads = mixed_heads.reshape(tok_count, heads_here * head_width)
    resid = tokens + reduce_heads(
        jnp.dot(mixed_heads, attn_out, preferred_element_type=jnp.float32)
    )
    scale_two, normed_two = norm_forward(resid, gain_two, model_width)
    logits = jnp.dot(normed_two, router, preferred_element_type=jnp.float32)
    chosen = (routes[:, :, None] == jnp.arange(EXPERTS, dtype=jnp.int32)[None, None, :]).astype(
        jnp.float32
    )
    picked = jnp.sum(chosen * logits[:, None, :], axis=2)
    gate_weights = jax.nn.softmax(picked, axis=1)
    slot_index, kept_pairs = slot_table(routes)
    keep_float = kept_pairs.astype(jnp.float32)
    mix_weight = gate_weights * keep_float
    safe_index = jnp.minimum(slot_index, EXPERTS * CAP - 1)
    token_rows = jnp.repeat(normed_two, TOP, axis=0)
    buffer = (
        jnp.zeros((EXPERTS * CAP + 1, model_width), jnp.bfloat16)
        .at[slot_index.reshape(-1)]
        .set(token_rows)
    )
    buffer = buffer[: EXPERTS * CAP].reshape(-1, local_experts, CAP, model_width)
    received = lax.all_to_all(buffer, "expert", split_axis=0, concat_axis=0, tiled=True)
    gate_part, up_part, hidden, partial_out = expert_forward(
        received, expert_gate, expert_up, expert_down
    )
    returned = spread_slots(owner_exchange(expert_sums(partial_out).astype(jnp.bfloat16)))
    flat_ret = returned.reshape(EXPERTS * CAP, model_width)
    fetched = flat_ret[safe_index].astype(jnp.float32)
    output = resid + jnp.sum(mix_weight[:, :, None] * fetched, axis=1)
    grad_y = grad_out.T.astype(jnp.float32)
    grad_gates = jnp.sum(grad_y[:, None, :] * fetched, axis=2) * keep_float
    grad_picked = gate_weights * (
        grad_gates - jnp.sum(gate_weights * grad_gates, axis=1, keepdims=True)
    )
    grad_logits = jnp.sum(chosen * grad_picked[:, :, None], axis=1)
    grad_router = jnp.dot(normed_two.astype(jnp.float32).T, grad_logits, precision=HIGH)
    grad_normed_two = jnp.dot(grad_logits, router.astype(jnp.float32).T, precision=HIGH)
    slot_grads = (mix_weight[:, :, None] * grad_y[:, None, :]).astype(jnp.bfloat16)
    grad_ret = (
        jnp.zeros((EXPERTS * CAP + 1, model_width), jnp.bfloat16)
        .at[slot_index.reshape(-1)]
        .set(slot_grads.reshape(-1, model_width))
    )
    grad_ret = grad_ret[: EXPERTS * CAP].reshape(-1, local_experts, CAP, model_width)
    grad_share = lax.dynamic_slice_in_dim(grad_ret, share_start, part_rows, 2)
    grad_rows_out = spread_slots(owner_exchange(grad_share))
    grad_expert_gate, grad_expert_up, grad_expert_down, grad_rows_in = expert_backward(
        received, gate_part, up_part, hidden, grad_rows_out, expert_gate, expert_up, expert_down
    )
    grad_back = spread_slots(owner_exchange(expert_sums(grad_rows_in).astype(jnp.bfloat16)))
    flat_back = grad_back.reshape(EXPERTS * CAP, model_width).astype(jnp.float32)
    grad_normed_two = grad_normed_two + jnp.sum(
        flat_back[safe_index] * keep_float[:, :, None], axis=1
    )
    grad_gain_two, grad_resid = norm_backward(
        resid, scale_two, gain_two, grad_normed_two, model_width
    )
    grad_resid = grad_resid + grad_y
    grad_attn = grad_resid.astype(jnp.bfloat16)
    grad_attn_out = jnp.einsum(
        "th,td->hd", mixed_heads, grad_attn, preferred_element_type=jnp.float32
    )
    grad_mixed = jnp.einsum(
        "td,hd->th", grad_attn, attn_out, preferred_element_type=jnp.float32
    ).astype(jnp.bfloat16)
    grad_by_seq = grad_mixed.reshape(seqs_here, SEQ, heads_here, head_width)
    bias_grad_full, grad_project = lax.scan(
        partial(attend_backward, bias_full),
        jnp.zeros_like(bias_full),
        (by_seq[0], by_seq[1], by_seq[2], grad_by_seq, piece_starts, log_total),
    )
    grad_project = (
        jnp.moveaxis(grad_project, 1, 0)
        .reshape(3, tok_count, heads_here * head_width)
        .astype(jnp.bfloat16)
    )
    grad_attn_in = jnp.einsum(
        "cth,td->chd", grad_project, normed, preferred_element_type=jnp.float32
    )
    grad_normed = reduce_heads(
        jnp.einsum("cth,chd->td", grad_project, attn_in, preferred_element_type=jnp.float32)
    )
    grad_gain_one, grad_tokens = norm_backward(
        tokens, scale_one, gain_one, grad_normed, model_width
    )
    grad_tokens = grad_tokens + grad_resid
    grad_rel_bias = jnp.dot(onehot_line.T, fold_line(bias_grad_full).T, precision=HIGH)
    shared = (
        lax.psum(grad_gain_one.astype(jnp.bfloat16), "expert").astype(jnp.float32),
        lax.psum(grad_attn_in.astype(jnp.bfloat16), "expert").astype(jnp.float32),
        lax.psum(grad_rel_bias.astype(jnp.bfloat16), "expert").astype(jnp.float32),
        lax.psum(grad_attn_out.astype(jnp.bfloat16), "expert").astype(jnp.float32),
        lax.psum(grad_gain_two.astype(jnp.bfloat16), "expert").astype(jnp.float32),
        lax.psum(grad_router.astype(jnp.bfloat16), "expert").astype(jnp.float32),
    )
    return (
        output.astype(jnp.bfloat16).T,
        grad_tokens.T,
        shared[0],
        shared[1],
        shared[2],
        shared[3],
        shared[4],
        shared[5],
        grad_expert_gate,
        grad_expert_up,
        grad_expert_down,
    )


def solution(mesh):
    placed = (
        P(None, "expert"),
        P(),
        P(None, "tensor", None),
        P(None, "tensor"),
        P("tensor", None),
        P(),
        P(),
        P("expert", "tensor", None),
        P("expert", "tensor", None),
        P("expert", "tensor", None),
        P("expert", None),
        P("expert", None),
        P(None, "expert"),
    )
    paired = mesh.shape["tensor"] == 4 and mesh.shape["expert"] * 2 == EXPERTS
    return jax.shard_map(
        on_device if paired else on_device_general,
        mesh=mesh,
        in_specs=placed,
        out_specs=(
            P(None, "expert"),
            P(None, "expert"),
            P(),
            P(None, "tensor", None),
            P(None, "tensor"),
            P("tensor", None),
            P(),
            P(),
            P("expert", "tensor", None),
            P("expert", "tensor", None),
            P("expert", "tensor", None),
        ),
        check_vma=False,
    )
```

```python
from functools import partial

import jax
import jax.numpy as jnp
from jax import lax
from jax.experimental import pallas as pl
from jax.experimental.pallas import tpu as pltpu
from jax.sharding import PartitionSpec as P

EXPERTS = 16
BUCKETS = 32
TOP = 2
PIECE = 256
SEQ = 1024
CAP = 320
BLK = 256


EPS = 1e-06
NEG = -1e30
THRESHOLDS = (12, 16, 23, 32, 46, 64, 91)
HIGH = lax.Precision.HIGHEST
F32 = jnp.float32
BF16 = jnp.bfloat16
NN = (((1,), (0,)), ((), ()))
NT = (((1,), (1,)), ((), ()))
TN = (((0,), (0,)), ((), ()))
MIB = 1 << 20


def mm(left, right, dims=NN):
    return lax.dot_general(left, right, dims, preferred_element_type=F32)


def params(limit=56):
    return pltpu.CompilerParams(vmem_limit_bytes=limit * MIB)


def cost(flops, bytes_accessed, transcendentals=0):
    return pl.CostEstimate(
        flops=int(flops), bytes_accessed=int(bytes_accessed), transcendentals=int(transcendentals)
    )


def bucket_of(offset):
    magnitude = jnp.abs(offset)
    beyond = sum(((magnitude >= threshold).astype(jnp.int32) for threshold in THRESHOLDS))
    lower_part = jnp.where(magnitude < 8, magnitude, 8 + beyond)
    return lower_part + 16 * (offset > 0).astype(jnp.int32)


def as_column(line):
    return jnp.broadcast_to(line, (8, line.shape[1])).T[:, :1]


def project_kernel(x_ref, gain_ref, w_ref, table_ref, out_ref, scale_ref, tiles_ref):
    x = x_ref[...].astype(F32)
    scale = lax.rsqrt(jnp.sum(x * x, axis=0, keepdims=True) / x.shape[0] + EPS)
    normed = (x * scale * as_column(gain_ref[...])).astype(BF16)
    out_ref[...] = mm(w_ref[...], normed).astype(BF16)
    scale_ref[...] = scale
    bias_tiles(table_ref, pl.program_id(0), tiles_ref)


def project(x, gain, weights, table):
    width, tokens = x.shape
    rows = weights.shape[0]
    heads = table.shape[0]
    tile = tokens // heads
    return pl.pallas_call(
        project_kernel,
        grid=(heads,),
        in_specs=[
            pl.BlockSpec((width, tile), lambda i: (0, i)),
            pl.BlockSpec((1, width), lambda i: (0, 0)),
            pl.BlockSpec((rows, width), lambda i: (0, 0)),
            pl.BlockSpec(memory_space=pltpu.SMEM),
        ],
        out_specs=[
            pl.BlockSpec((rows, tile), lambda i: (0, i)),
            pl.BlockSpec((1, tile), lambda i: (0, i)),
            pl.BlockSpec((1, 3, BLK, BLK), lambda i: (i, 0, 0, 0)),
        ],
        out_shape=[
            jax.ShapeDtypeStruct((rows, tokens), BF16),
            jax.ShapeDtypeStruct((1, tokens), F32),
            jax.ShapeDtypeStruct((heads, 3, BLK, BLK), F32),
        ],
        compiler_params=params(),
        cost_estimate=cost(2 * width * tokens * rows, 2 * width * tokens * 2),
    )(x, gain, weights, table)


def line_offsets(number):
    column = lax.broadcasted_iota(jnp.int32, (8, BLK), 1)
    return (number - 1) * BLK - column


def bias_tiles(table_ref, head, tiles_ref):
    row = lax.broadcasted_iota(jnp.int32, (BLK, BLK), 0)
    column = lax.broadcasted_iota(jnp.int32, (BLK, BLK), 1)
    far = table_ref[head, 15]
    rolled = []
    for number in range(4):
        bucket = bucket_of(line_offsets(number))
        value = jnp.zeros((8, BLK), F32)
        for index in range(BUCKETS):
            value = jnp.where(bucket == index, table_ref[head, index] - far, value)
        whole = jnp.broadcast_to(value[0:1], (BLK, BLK))
        rolled.append(pltpu.roll(whole, 0, 1, stride=1, stride_axis=0))
    for number in range(3):
        tiles_ref[0, number] = jnp.where(column >= row, rolled[number], rolled[number + 1])


def bias_fold(near_ref, far_ref):
    heads = near_ref.shape[0] // 2
    sums = jnp.zeros((BUCKETS, 128), F32)
    lane = lax.broadcasted_iota(jnp.int32, (BUCKETS, 128), 1)
    row = lax.broadcasted_iota(jnp.int32, (BLK, BLK), 0)
    column = lax.broadcasted_iota(jnp.int32, (BLK, BLK), 1)
    flip = jnp.where(row + column == BLK - 1, 1.0, 0.0).astype(BF16)
    apart = jnp.where(column == BLK - 1, 0, column + 1)
    ahead = apart <= row
    number_at = lax.broadcasted_iota(jnp.int32, (BUCKETS, BLK), 0)
    for head in range(heads):
        lines = [jnp.zeros((1, BLK), F32) for _ in range(4)]
        for number in range(3):
            grads = near_ref[head, number] + near_ref[heads + head, number]
            coarse = grads.astype(BF16)
            fine = (grads - coarse.astype(F32)).astype(BF16)
            flipped = mm(flip, coarse) + mm(flip, fine)
            rolled = pltpu.roll(flipped, 0, 1, stride=1, stride_axis=0)
            lines[number] += jnp.sum(jnp.where(ahead, rolled, 0.0), axis=0, keepdims=True)
            lines[number + 1] += jnp.sum(jnp.where(ahead, 0.0, rolled), axis=0, keepdims=True)
        total = jnp.zeros((BUCKETS, 1), F32)
        for number, line in enumerate(lines):
            bucket = bucket_of((number - 1) * BLK - apart[:1])
            total += jnp.sum(jnp.where(bucket == number_at, line, 0.0), axis=1, keepdims=True)
        distant = jnp.sum(far_ref[head] + far_ref[heads + head], axis=0, keepdims=True)
        distant = jnp.sum(distant, axis=1, keepdims=True)
        total += jnp.where(number_at[:, :1] == 15, distant, 0.0)
        sums = jnp.where(lane == head, total, sums)
    return sums


def key_count(query_block):
    return 2 * BLK if query_block < 2 else 4 * BLK


def block_scores(keys, queries, tile_of, limit, block):
    count = key_count(block)
    parts = []
    whole = mm(keys[:, :count], queries, TN)
    for key_block in range(count // BLK):
        part = whole[key_block * BLK : (key_block + 1) * BLK]
        shift = key_block - block
        if -1 <= shift <= 1:
            part = part + tile_of(shift)
        if shift >= 0:
            key_at = lax.broadcasted_iota(jnp.int32, (BLK, BLK), 0) + key_block * BLK
            part = jnp.where(key_at <= limit, part, NEG)
        parts.append(part)
    return jnp.concatenate(parts, axis=0)


def attend_half(qkv_ref, tiles_ref, limit_ref, mixed_ref, lse_ref, seq, half):
    heads = tiles_ref.shape[0]
    width = mixed_ref.shape[0] // heads
    base = pl.multiple_of(seq * SEQ, SEQ)

    def one_head(head, carry):
        at = lambda kind: pl.ds(pl.multiple_of((kind * heads + head) * width, width), width)
        keys, values = qkv_ref[at(1), pl.ds(base, SEQ)], qkv_ref[at(2), pl.ds(base, SEQ)]
        for block in (2 * half, 2 * half + 1):
            cols = pl.ds(pl.multiple_of(base + block * BLK, BLK), BLK)
            span = slice(block * BLK, (block + 1) * BLK)
            queries = qkv_ref[at(0), cols] * BF16(0.125)
            scores = block_scores(
                keys, queries, lambda shift: tiles_ref[head, shift + 1], limit_ref[seq, :, span], block
            )
            top = jnp.max(scores, axis=0, keepdims=True)
            exponent = jnp.exp(scores - top)
            total = jnp.sum(exponent, axis=0, keepdims=True)
            mixed = mm(values[:, : key_count(block)], exponent.astype(BF16)) / total
            mixed_ref[at(0), cols] = mixed.astype(BF16)
            lse_ref[seq * heads + head, :, span] = top + jnp.log(total)
        return carry

    lax.fori_loop(0, heads, one_head, 0)


def attend_back_kernel(
    q_ref, k_ref, v_ref, tiles_ref, limit_ref, w_ref, grad_ref, lse_ref, part_ref, resid_ref,
    dq_ref, dk_ref, dv_ref, near_ref, far_ref, y_ref,
    held, parts, total, turn_across, turn_along, from_across, from_along, sends, recvs, loads,
):
    rank = lax.axis_index("tensor")
    pair_class, half_index = rank % 2, rank // 2
    across, along, corner = rank + 1 - 2 * pair_class, rank + 2 - 4 * half_index, 3 - rank
    step = pl.program_id(0) * pl.num_programs(1) + pl.program_id(1)
    mesh_ids = pl.DeviceIdType.MESH
    middle = parts.shape[2] // 2
    low, high = slice(0, middle), slice(middle, 2 * middle)

    def remote(number, origin, target, other):
        return pltpu.make_async_remote_copy(
            src_ref=origin, dst_ref=target, send_sem=sends.at[number], recv_sem=recvs.at[number],
            device_id={"tensor": other}, device_id_type=mesh_ids,
        )

    first = (
        remote(0, part_ref.at[corner, :, low], turn_across, across),
        remote(1, part_ref.at[corner, :, high], turn_along, along),
    )
    second = remote(2, parts.at[0], from_across, across), remote(3, parts.at[1], from_along, along)
    local = [
        pltpu.make_async_copy(part_ref.at[other], parts.at[number], loads.at[number])
        for number, other in enumerate((across, along, rank))
    ]
    local.append(pltpu.make_async_copy(resid_ref, total, loads.at[3]))

    @pl.when(step == 0)
    def _():
        barrier = pltpu.get_barrier_semaphore()
        for other in (across, along):
            pl.semaphore_signal(barrier, inc=1, device_id={"tensor": other}, device_id_type=mesh_ids)
        pl.semaphore_wait(barrier, 2)
        for copy in first:
            copy.start()
        for copy in local:
            copy.start()

    @pl.when(step == 3)
    def _():
        for copy in (*first, *local):
            copy.wait()
        parts[0, :, high] = (parts[0, :, high].astype(F32) + turn_along[...].astype(F32)).astype(BF16)
        parts[1, :, low] = (parts[1, :, low].astype(F32) + turn_across[...].astype(F32)).astype(BF16)
        for copy in second:
            copy.start()

    head = pl.program_id(1)
    width = q_ref.shape[0]

    @pl.when(head == 0)
    def _():
        held[...] = mm(w_ref[...], grad_ref[...], NT).astype(BF16)

    queries = q_ref[...] * BF16(0.125)
    keys, values = k_ref[...], v_ref[...]
    grads = held[pl.ds(pl.multiple_of(head * width, width), width), :]
    near_ref[...] = jnp.zeros_like(near_ref)
    far = jnp.zeros((8, BLK), F32)
    grad_keys = jnp.zeros((width, SEQ), F32)
    grad_values = jnp.zeros((width, SEQ), F32)
    for block in range(SEQ // BLK):
        count = key_count(block)
        cols = slice(block * BLK, (block + 1) * BLK)
        scores = block_scores(
            keys, queries[:, cols], lambda shift: tiles_ref[0, shift + 1], limit_ref[0, :, cols], block
        )
        probs = jnp.exp(scores - lse_ref[0, :, cols])
        grad_probs = mm(values[:, :count], grads[:, cols], TN)
        inner = jnp.sum(probs * grad_probs, axis=0, keepdims=True)
        grad_scores = probs * (grad_probs - inner)
        for key_block in range(count // BLK):
            part = grad_scores[key_block * BLK : (key_block + 1) * BLK]
            shift = key_block - block
            if -1 <= shift <= 1:
                near_ref[0, shift + 1] += part
            elif shift < -1:
                far = far + jnp.sum(part.reshape(BLK // 8, 8, BLK), axis=0)
        rounded = grad_scores.astype(BF16)
        add_values = mm(grads[:, cols], probs.astype(BF16), NT)
        add_keys = mm(queries[:, cols], rounded, NT)
        if count == SEQ:
            grad_values = grad_values + add_values
            grad_keys = grad_keys + add_keys
        else:
            filler = jnp.zeros((width, SEQ - count), F32)
            grad_values = grad_values + jnp.concatenate([add_values, filler], axis=1)
            grad_keys = grad_keys + jnp.concatenate([add_keys, filler], axis=1)
        dq_ref[:, cols] = (mm(keys[:, :count], rounded) * 0.125).astype(BF16)
    dk_ref[...] = grad_keys.astype(BF16)
    dv_ref[...] = grad_values.astype(BF16)
    far_ref[0] = far

    @pl.when(step == 7)
    def _():
        for copy in second:
            copy.wait()
        summed = parts[2].astype(F32) + from_across[...].astype(F32) + from_along[...].astype(F32)
        y_ref[...] = (total[...] + summed).astype(BF16)


def attend_back(qkv, tiles, limits, attn_out, grad_attn, lse, part, resid):
    heads = tiles.shape[0]
    seqs = limits.shape[0]
    width = qkv.shape[0] // (3 * heads)
    model_width = attn_out.shape[1]
    share = part.shape[1]
    grad_spec = pl.BlockSpec((width, SEQ), lambda s, h: (h, s))
    anywhere = pl.BlockSpec(memory_space=pl.ANY)
    return pl.pallas_call(
        attend_back_kernel,
        grid=(seqs, heads),
        in_specs=[
            pl.BlockSpec((width, SEQ), lambda s, h: (h, s)),
            pl.BlockSpec((width, SEQ), lambda s, h: (heads + h, s)),
            pl.BlockSpec((width, SEQ), lambda s, h: (2 * heads + h, s)),
            pl.BlockSpec((1, 3, BLK, BLK), lambda s, h: (h, 0, 0, 0)),
            pl.BlockSpec((1, 1, SEQ), lambda s, h: (s, 0, 0)),
            pl.BlockSpec((heads * width, model_width), lambda s, h: (0, 0)),
            pl.BlockSpec((SEQ, model_width), lambda s, h: (s, 0)),
            pl.BlockSpec((1, 1, SEQ), lambda s, h: (s * heads + h, 0, 0)),
        ]
        + [anywhere] * 2,
        out_specs=[
            grad_spec,
            grad_spec,
            grad_spec,
            pl.BlockSpec((1, 3, BLK, BLK), lambda s, h: (s * heads + h, 0, 0, 0)),
            pl.BlockSpec((1, 8, BLK), lambda s, h: (s * heads + h, 0, 0)),
            pl.BlockSpec((share, model_width), lambda s, h: (0, 0)),
        ],
        out_shape=[jax.ShapeDtypeStruct((heads * width, seqs * SEQ), BF16)] * 3
        + [
            jax.ShapeDtypeStruct((seqs * heads, 3, BLK, BLK), F32),
            jax.ShapeDtypeStruct((seqs * heads, 8, BLK), F32),
        ]
        + [jax.ShapeDtypeStruct((share, model_width), BF16)],
        scratch_shapes=[
            pltpu.VMEM((heads * width, SEQ), BF16),
            pltpu.VMEM((3, share, model_width), BF16),
            pltpu.VMEM((share, model_width), F32),
            pltpu.VMEM((share, model_width // 2), BF16),
            pltpu.VMEM((share, model_width // 2), BF16),
            pltpu.VMEM((share, model_width), BF16),
            pltpu.VMEM((share, model_width), BF16),
            pltpu.SemaphoreType.DMA((4,)),
            pltpu.SemaphoreType.DMA((4,)),
            pltpu.SemaphoreType.DMA((4,)),
        ],
        compiler_params=pltpu.CompilerParams(
            vmem_limit_bytes=60 * MIB, collective_id=5, has_side_effects=True
        ),
        cost_estimate=cost(seqs * heads * SEQ * SEQ * 1280, seqs * heads * SEQ * 4096, seqs * heads * SEQ * SEQ),
    )(qkv, qkv, qkv, tiles, limits, attn_out, grad_attn, lse, part, resid)


def project_back_kernel(
    place_ref, x_ref, gain_ref, scale_ref, w_ref, mixed_ref, attn_ref, dq_ref, dk_ref, dv_ref, *refs
):
    step = pl.program_id(0)
    own_refs, got_refs, (weight_ref, out_ref, gain_grad_ref), placed_refs, total = (
        refs[:3], refs[3:6], refs[6:9], refs[9:12], refs[12]
    )
    for own_ref, got_ref, placed_ref in zip(own_refs, got_refs, placed_refs):
        placed_ref[place_ref[0]] = own_ref[...]
        placed_ref[1 - place_ref[0]] = got_ref[...].astype(F32)
    grads = jnp.concatenate([dq_ref[...], dk_ref[...], dv_ref[...]], axis=0)
    rows = grads.shape[0]
    normed = (x_ref[...].astype(F32) * scale_ref[...] * as_column(gain_ref[...])).astype(BF16)

    @pl.when(step == 0)
    def _():
        total[...] = jnp.zeros_like(total)

    total[:rows] += mm(grads, normed, NT)
    total[rows:] += mm(mixed_ref[...], attn_ref[...])
    out_ref[...] = mm(grads, w_ref[...], TN).astype(BF16)

    @pl.when(step == pl.num_programs(0) - 1)
    def _():
        weight_ref[...] = total[...].astype(BF16)
        through = jnp.sum(total[:rows] * w_ref[...].astype(F32), axis=0, keepdims=True)
        gain_grad_ref[...] = through / gain_ref[...]


def project_back(place, x, gain, scale, weights, mixed, grad_attn, grads, owns, gots):
    width, tokens = x.shape
    rows = weights.shape[0]
    heads_width = mixed.shape[0]
    units = owns[0].shape[0]
    steps = 4
    tile = tokens // steps
    part = units // steps
    column = lambda count: pl.BlockSpec((count, tile), lambda i: (0, i))
    return pl.pallas_call(
        project_back_kernel,
        grid=(steps,),
        in_specs=[
            pl.BlockSpec(memory_space=pltpu.SMEM),
            column(width),
            pl.BlockSpec((1, width), lambda i: (0, 0)),
            column(1),
            pl.BlockSpec((rows, width), lambda i: (0, 0)),
            column(heads_width),
            pl.BlockSpec((tile, width), lambda i: (i, 0)),
        ]
        + [column(rows // 3)] * 3
        + [pl.BlockSpec((part, width), lambda i: (i, 0))] * 6,
        out_specs=[
            pl.BlockSpec((rows + heads_width, width), lambda i: (0, 0)),
            pl.BlockSpec((tile, width), lambda i: (i, 0)),
            pl.BlockSpec((1, width), lambda i: (0, 0)),
        ]
        + [pl.BlockSpec((2, part, width), lambda i: (0, i, 0))] * 3,
        out_shape=[
            jax.ShapeDtypeStruct((rows + heads_width, width), BF16),
            jax.ShapeDtypeStruct((tokens, width), BF16),
            jax.ShapeDtypeStruct((1, width), F32),
        ]
        + [jax.ShapeDtypeStruct((2, units, width), F32)] * 3,
        scratch_shapes=[pltpu.VMEM((rows + heads_width, width), F32)],
        compiler_params=params(),
        cost_estimate=cost(5 * width * tokens * rows, 6 * width * tokens + 14 * units * width),
    )(place, x, gain, scale, weights, mixed, grad_attn, *grads, *owns, *gots)


def exchange(
    math, rank, source, full_out, full, from_across, from_along, to_across, to_along, turn_across, turn_along, sends, recvs, outs, ready=None, ready_full=None, side=None, peers=(), fill=None, start=None, cut=None, later=None):
    pair_class, half_index = rank % 2, rank // 2
    across, along, corner = rank + 1 - 2 * pair_class, rank + 2 - 4 * half_index, 3 - rank
    mesh_ids = pl.DeviceIdType.MESH
    rows, width = source.shape[1:]
    chunks = 4
    size = rows // chunks
    cut = cut or width // 2
    low, high = slice(0, cut), slice(cut, width)
    barrier = pltpu.get_barrier_semaphore()
    near = (across, along, corner) if later else (across, along)
    for other in near:
        pl.semaphore_signal(barrier, inc=1, device_id={"tensor": other}, device_id_type=mesh_ids)
    for other in peers:
        pl.semaphore_signal(barrier, inc=1, device_id={"expert": other}, device_id_type=mesh_ids)
    pl.semaphore_wait(barrier, len(near) + len(peers))

    def remote(kind, chunk, origin, target, other):
        return pltpu.make_async_remote_copy(
            src_ref=origin, dst_ref=target, send_sem=sends.at[kind, chunk], recv_sem=recvs.at[kind, chunk],
            device_id={"tensor": other}, device_id_type=mesh_ids,
        )

    if start:
        start()
    if fill:
        fill(corner)
    spans = [slice(chunk * size, (chunk + 1) * size) for chunk in range(chunks)]
    first, second, third, fourth = [], [], [], []
    for chunk, span in enumerate(spans):
        pair = (
            remote(0, chunk, source.at[corner, span, low], turn_across.at[span, low], across),
            remote(1, chunk, source.at[corner, span, high], turn_along.at[span, high], along),
        )
        for copy in pair:
            copy.start()
        first.append(pair)
    if fill:
        fill(along)
        fill(across)
    leaving = []

    def leave(number, other):
        leaving.append(pltpu.make_async_copy(full.at[other], full_out.at[other], outs.at[number]))
        leaving[-1].start()

    if ready is not None:
        _, near_across, near_along = ready
        extra = [
            remote(8, 0, near_along.at[:, low], ready_full.at[along, :, low], across),
            remote(8, 1, near_across.at[:, high], ready_full.at[across, :, high], along),
        ]
        extra += [
            pltpu.make_async_copy(piece, ready_full.at[other], outs.at[4 + number])
            for number, (other, piece) in enumerate(zip((rank, across, along), ready))
        ]
        for copy in extra:
            copy.start()
    for chunk, span in enumerate(spans):
        if side:
            side(chunk)
        first[chunk][0].wait()
        to_along[span, low] = (source[along, span, low].astype(F32) + turn_across[span, low].astype(F32)).astype(BF16)
        to_along[span, high] = source[along, span, high]
        first[chunk][1].wait()
        to_across[span, low] = source[across, span, low]
        to_across[span, high] = (source[across, span, high].astype(F32) + turn_along[span, high].astype(F32)).astype(BF16)
        pair = (
            remote(2, chunk, to_across.at[span], from_across.at[span], across),
            remote(3, chunk, to_along.at[span], from_along.at[span], along),
        )
        for copy in pair:
            copy.start()
        second.append(pair)
    def pass_on(chunk):
        span = spans[chunk]
        for copy in third[chunk]:
            copy.wait()
        pair = (
            remote(6, chunk, full.at[along, span, low], full.at[along, span, low], across),
            remote(7, chunk, full.at[across, span, high], full.at[across, span, high], along),
        )
        for copy in pair:
            copy.start()
        fourth.append(pair)

    if fill:
        fill(rank)
    if later:
        later((across, along, corner))
    for chunk, span in enumerate(spans):
        if side:
            side(chunks + chunk)
        for copy in second[chunk]:
            copy.wait()
        total = source[rank, span].astype(F32) + from_across[span].astype(F32) + from_along[span].astype(F32)
        full[rank, span] = math(span, total).astype(BF16)
        pair = (
            remote(4, chunk, full.at[rank, span], full.at[rank, span], across),
            remote(5, chunk, full.at[rank, span], full.at[rank, span], along),
        )
        for copy in pair:
            copy.start()
        third.append(pair)
        if chunk:
            pass_on(chunk - 1)
    leave(0, rank)
    pass_on(chunks - 1)
    leave(1, across)
    leave(2, along)
    if ready is not None:
        for copy in extra:
            copy.wait()
    if side and later:
        side(2 * chunks)
    for pair in fourth:
        for copy in pair:
            copy.wait()
    leave(3, corner)
    if side and not later:
        side(2 * chunks)
    for copy in leaving:
        copy.wait()


def exchange_call(kernel, number, shape, operands, extra_shapes, scratch=(), in_hbm=(), out_hbm=()):
    tokens, width = shape
    ranks = 4
    rows = tokens // ranks
    here = pl.BlockSpec(memory_space=pltpu.VMEM)
    results = pl.pallas_call(
        kernel,
        in_specs=[pl.BlockSpec(memory_space=pl.ANY) if k in in_hbm else here for k in range(len(operands))],
        out_specs=[pl.BlockSpec(memory_space=pl.ANY)]
        + [pl.BlockSpec(memory_space=pl.ANY) if k in out_hbm else here for k in range(len(extra_shapes))],
        out_shape=[jax.ShapeDtypeStruct((ranks, rows, width), BF16)]
        + [jax.ShapeDtypeStruct(shape, kind) for shape, kind in extra_shapes],
        scratch_shapes=[pltpu.VMEM((ranks, rows, width), BF16)]
        + [pltpu.VMEM((rows, width), BF16)] * 6
        + [pltpu.SemaphoreType.DMA((9, 4))] * 2
        + [pltpu.SemaphoreType.DMA((7,))]
        + list(scratch),
        compiler_params=pltpu.CompilerParams(
            vmem_limit_bytes=60 * MIB, collective_id=number, has_side_effects=True
        ),
        cost_estimate=cost(40 * MIB, 200 * MIB),
    )(*operands)
    return results[0].reshape(tokens, width), *results[1:]


def norm_two_kernel(
    qkv_ref, tiles_ref, limit_ref, w_ref, x_ref, gain_ref, grad_out_ref, routes_ref, gate_ref,
    full, resid_ref, scale_ref, dy_out, dy_rows_out, code_ref, codes_ref, own_ref, mixed_ref, lse_ref, got_gate, *rest,
):
    source, held, grad_out, dy_ref, dy_rows_ref, load, send, recv = rest[-8:]
    rank = lax.axis_index("tensor")
    ranks, rows, width = source.shape
    loading = pltpu.make_async_copy(grad_out_ref, grad_out, load.at[1])
    storing = [
        pltpu.make_async_copy(dy_ref, dy_out, load.at[2]),
        pltpu.make_async_copy(dy_rows_ref, dy_rows_out, load.at[3]),
    ]

    pair_class = rank % 2
    part = got_gate.shape[0] // 2
    swaps = [
        pltpu.make_async_remote_copy(
            src_ref=gate_ref.at[1 - pair_class, pl.ds(gate_ref.shape[1] - (2 - piece) * part, part)],
            dst_ref=got_gate.at[pl.ds(piece * part, part)],
            send_sem=send.at[piece],
            recv_sem=recv.at[piece],
            device_id={"tensor": rank + 1 - 2 * pair_class},
            device_id_type=pl.DeviceIdType.MESH,
        )
        for piece in range(2)
    ]

    def start():
        own.start()
        loading.start()
        swaps[0].start()

    def fill(shard):
        for half in range(2):
            pl.when(shard % 2 == half)(
                partial(attend_half, qkv_ref, tiles_ref, limit_ref, mixed_ref, lse_ref, shard // 2, half)
            )
        columns = pl.ds(pl.multiple_of(shard * rows, rows), rows)
        source[shard] = mm(mixed_ref[:, columns], w_ref[...], TN).astype(BF16)

    slots = dy_rows_ref.shape[0] // ranks
    own = pltpu.make_async_copy(x_ref.at[:, pl.ds(pl.multiple_of(rank * rows, rows), rows)], held, load.at[0])

    def math(span, total):
        resid = own_ref[span, :].astype(F32) + total
        scale = lax.rsqrt(jnp.sum(resid * resid, axis=1, keepdims=True) / resid.shape[1] + EPS)
        resid_ref[span, :] = resid
        scale_ref[span, :] = scale
        return resid * scale * gain_ref[...]

    def later(others):
        own.wait()
        own_ref[...] = held[...].astype(F32).T.astype(BF16)
        local_codes(routes_ref, code_ref, pair_class, rank // 2, CAP // 2)
        codes_ref[...] = jnp.concatenate([code_ref[...].astype(F32)] * 4, axis=0).T[:, :TOP].astype(jnp.int32)
        loading.wait()
        for number in range(ranks):
            span = slice(number * rows, (number + 1) * rows)
            dy_ref[span, :] = grad_out[:, span].astype(F32).T.astype(BF16)
        storing[0].start()

    def side(number):
        if number == 0:
            swaps[1].start()
        elif ranks <= number < 2 * ranks:
            begin = (number - ranks) * slots
            slot = lax.broadcasted_iota(jnp.int32, (slots, dy_ref.shape[0]), 0) + begin
            take = jnp.where((slot == code_ref[0:1]) | (slot == code_ref[1:2]), 1.0, 0.0).astype(BF16)
            dy_rows_ref[begin : begin + slots, :] = mm(take, dy_ref[...]).astype(BF16)
        elif number == 2 * ranks:
            storing[1].start()
            for copy in swaps + storing:
                copy.wait()

    exchange(
        math, rank, source, full, *rest[:-8], side=side, start=start, fill=fill, later=later, cut=width // 4
    )


def norm_back(grad, value, scale, gain):
    scaled = grad * gain
    inner = jnp.sum(scaled * value, axis=1, keepdims=True)
    return scale * scaled - value * (scale * scale * scale) * (inner / value.shape[1])


def norm_two_back_kernel(
    ret_in, back_ref, code_ref, codes_ref, gates_ref, routes_ref, dy_rows_in, gate_ref, router_ref, h_in,
    resid_in, scale_ref, dy_in, gain_ref, full, grad_ref, gain_grad_ref, router_grad_ref, y_out, *rest,
):
    source, scaled, logit_parts, logit_own, send, recv, ret_ref, dy_rows_ref, h_ref, resid_ref, dy_ref, y_ref, load = rest[-13:]
    rank = lax.axis_index("tensor")
    rows = source.shape[1]
    slots, tokens = ret_ref.shape[0], code_ref.shape[1]
    ranks = tokens // rows
    copies = []
    own_dy = dy_in.at[pl.ds(pl.multiple_of(rank * rows, rows), rows)]
    pairs = ((ret_in, ret_ref), (dy_rows_in, dy_rows_ref), (resid_in, resid_ref), (own_dy, dy_ref), (h_in, h_ref))
    loading = [pltpu.make_async_copy(*pair, load.at[number]) for number, pair in enumerate(pairs)]
    storing = [
        pltpu.make_async_copy(y_ref.at[shard], y_out.at[pl.ds(shard * rows, rows)], load.at[5 + shard])
        for shard in range(ranks)
    ]

    def start():
        for copy in loading:
            copy.start()

    def later(others):
        for copy in loading:
            copy.wait()
        found = [jnp.zeros((1, tokens), F32) for _ in range(TOP)]
        tile = slots // 4
        for begin in range(0, slots, tile):
            span = slice(begin, begin + tile)
            ret = ret_ref[span, :].astype(F32)
            slot_grad = jnp.sum(dy_rows_ref[span, :].astype(F32) * ret, axis=1, keepdims=True)
            scaled[span, :] = (ret * gate_ref[span, :]).astype(BF16)
            slot = lax.broadcasted_iota(jnp.int32, (tile, tokens), 0) + begin
            for i in range(TOP):
                found[i] = found[i] + jnp.sum(
                    jnp.where(slot == code_ref[i : i + 1, :], slot_grad, 0.0), axis=0, keepdims=True
                )
        mean = gates_ref[0:1] * found[0] + gates_ref[1:2] * found[1]
        expert = lax.broadcasted_iota(jnp.int32, (EXPERTS, tokens), 0)
        logit = sum(
            jnp.where(routes_ref[i : i + 1] == expert, gates_ref[i : i + 1] * (found[i] - mean), 0.0)
            for i in range(TOP)
        )
        for shard in range(ranks):
            logit_parts[shard] = logit[:, shard * rows : (shard + 1) * rows]
        for number, other in enumerate(others):
            copies.append(
                pltpu.make_async_remote_copy(
                    src_ref=logit_parts.at[other], dst_ref=logit_parts.at[ranks + number], send_sem=send.at[number],
                    recv_sem=recv.at[number], device_id={"tensor": other}, device_id_type=pl.DeviceIdType.MESH,
                )
            )
            copies[-1].start()

    def places(shard):
        slot = lax.broadcasted_iota(jnp.int32, (rows, slots), 1)
        codes = codes_ref[pl.ds(pl.multiple_of(shard * rows, rows), rows), :]
        return jnp.where((slot == codes[:, 0:1]) | (slot == codes[:, 1:2]), 1.0, 0.0).astype(BF16)

    def fill(shard):
        source[shard] = mm(places(shard), back_ref[...]).astype(BF16)

    def side(number):
        if number == ranks:
            router_grad_ref[...] = sum(
                mm(logit_parts[shard].astype(BF16), h_ref[shard * rows : (shard + 1) * rows, :])
                for shard in range(ranks)
            )
            for copy in copies:
                copy.wait()
            logit = logit_parts[rank] + logit_parts[ranks] + logit_parts[ranks + 1] + logit_parts[ranks + 2]
            coarse = logit.astype(BF16)
            logit_own[:EXPERTS] = coarse
            logit_own[EXPERTS:] = (logit - coarse.astype(F32)).astype(BF16)
        elif number > ranks:
            shard = number - ranks - 1
            y_ref[shard] = mm(places(shard), scaled[...]).astype(BF16)
            storing[shard].start()
            if shard == ranks - 1:
                for copy in storing:
                    copy.wait()

    gain_grad_ref[...] = jnp.zeros_like(gain_grad_ref)

    def math(span, total):
        resid, scale = resid_ref[span, :], scale_ref[span, :]
        both = jnp.concatenate([router_ref[...], router_ref[...]], axis=0)
        total = total + mm(logit_own[:, span], both, TN)
        gain_grad_ref[...] += jnp.sum(total * resid * scale, axis=0, keepdims=True)
        grad = norm_back(total, resid, scale, gain_ref[...]) + dy_ref[span, :].astype(F32)
        grad_ref[span, :] = grad
        return grad

    exchange(math, rank, source, full, *rest[:-13], side=side, fill=fill, start=start, later=later)


def norm_one_back_kernel(
    source, x_in, scale_ref, grad_in, gain_ref, y_own, y_across, y_along, gain_one_ref, gain_two_ref, router_ref,
    near_ref, far_ref, full, ready_full, small_out, *rest,
):
    x_ref, grad_ref, held, gathered, near, scale, load, tensor_sends, tensor_recvs, expert_sends, expert_recvs = rest[-11:]
    rank, group = lax.axis_index("tensor"), lax.axis_index("expert")
    pair_class, half_index = rank % 2, rank // 2
    others = rank + 1 - 2 * pair_class, rank + 2 - 4 * half_index
    groups = expert_sends.shape[0]
    mesh_ids = pl.DeviceIdType.MESH
    peers = [partner_of(group, step) for step in range(1, groups)]
    heads = near_ref.shape[0] // 2
    rows = source.shape[1]
    pairs = ((near_ref, near), (x_in, x_ref), (grad_in, grad_ref))
    loading = [pltpu.make_async_copy(*pair, load.at[number]) for number, pair in enumerate(pairs)]

    def math(span, total):
        x = x_ref[span, :].astype(F32)
        return norm_back(total, x, scale[span, :], gain_ref[...]) + grad_ref[span, :]

    def to_rank(step):
        return pltpu.make_async_remote_copy(
            src_ref=held.at[step], dst_ref=held.at[2 + step], send_sem=tensor_sends.at[step],
            recv_sem=tensor_recvs.at[step], device_id={"tensor": others[step]}, device_id_type=mesh_ids,
        )

    def to_group(step):
        return pltpu.make_async_remote_copy(
            src_ref=gathered.at[group], dst_ref=gathered.at[group], send_sem=expert_sends.at[step],
            recv_sem=expert_recvs.at[step], device_id={"expert": peers[step - 1]}, device_id_type=mesh_ids,
        )

    def start():
        for copy in loading:
            copy.start()
        held[0] = jnp.zeros(small_out.shape, F32)
        held[0, :EXPERTS] = router_ref[...]
        held[0, EXPERTS : EXPERTS + 1] = gain_two_ref[...]
        held[0, EXPERTS + 1 : EXPERTS + 2] = gain_one_ref[...]
        to_rank(0).start()

    def side(number):
        if number == 0:
            own_scale = scale_ref[:, pl.ds(pl.multiple_of(rank * rows, rows), rows)]
            scale[...] = jnp.broadcast_to(own_scale, (8, rows)).T[:, :1]
            for copy in loading:
                copy.wait()
            small_out[:BUCKETS, :128] = bias_fold(near, far_ref)
        elif number == 1:
            to_rank(0).wait()
            held[1] = held[0] + held[2]
            to_rank(1).start()
        elif number == 5:
            to_rank(1).wait()
            turned = small_out[:BUCKETS, :128].T
            held[0] = held[1] + held[3]
            held[0, EXPERTS + 2 : EXPERTS + 2 + heads, :BUCKETS] = turned[:heads]
            gathered[group] = held[0].astype(BF16)
            for step in range(1, groups):
                to_group(step).start()
        elif number == 8:
            for step in range(1, groups):
                to_group(step).wait()
            total = gathered[0].astype(F32)
            for step in range(1, groups):
                total = total + gathered[step].astype(F32)
            small_out[...] = total

    exchange(
        math, rank, source, full, *rest[:-11], (y_own, y_across, y_along), ready_full, side=side, peers=peers, start=start
    )


def local_codes(routes_ref, code_ref, pair_class, half_index, half):
    tokens = routes_ref.shape[1]
    expert = lax.broadcasted_iota(jnp.int32, (EXPERTS, BLK), 0)
    earlier = (
        lax.broadcasted_iota(jnp.int32, (BLK, BLK), 0) < lax.broadcasted_iota(jnp.int32, (BLK, BLK), 1)
    ).astype(F32).astype(BF16)
    carry = jnp.zeros((EXPERTS, 1), F32)
    for block in range(tokens // BLK):
        cols = slice(block * BLK, (block + 1) * BLK)
        routes = routes_ref[:, cols]
        hits = [(routes[i : i + 1] == expert) for i in range(TOP)]
        chosen = sum(hit.astype(F32) for hit in hits)
        before = mm(chosen.astype(BF16), earlier) + carry
        carry = carry + jnp.sum(chosen, axis=1, keepdims=True)
        for i in range(TOP):
            slot = jnp.sum(jnp.where(hits[i], before, 0.0), axis=0, keepdims=True).astype(jnp.int32)
            route = routes[i : i + 1]
            owner = route // 2
            local = slot - half_index * half
            mine = (route - 2 * owner == pair_class) & (local >= 0) & (local < half)
            code_ref[i : i + 1, cols] = jnp.where(mine, owner * half + local, -1)


def dispatch_kernel(code_ref, routes_ref, router_ref, h_ref, dy_rows_ref, rows_ref, grads_ref, gate_ref, gates_ref):
    count, tokens = rows_ref.shape[0], h_ref.shape[0]

    @pl.when(pl.program_id(0) == 0)
    def _():
        expert = lax.broadcasted_iota(jnp.int32, (EXPERTS, tokens), 0)
        logits = mm(router_ref[...], h_ref[...], NT)
        picked = [
            jnp.sum(jnp.where(routes_ref[i : i + 1] == expert, logits, 0.0), axis=0, keepdims=True)
            for i in range(TOP)
        ]
        top = jnp.maximum(picked[0], picked[1])
        raised = [jnp.exp(value - top) for value in picked]
        total = raised[0] + raised[1]
        for i in range(TOP):
            gates_ref[i : i + 1] = raised[i] / total

    slot = lax.broadcasted_iota(jnp.int32, (count, tokens), 0) + pl.program_id(0) * count
    hits = [slot == code_ref[i : i + 1, :] for i in range(TOP)]
    take = jnp.where(hits[0] | hits[1], 1.0, 0.0).astype(BF16)
    weighted = jnp.where(hits[0], gates_ref[0:1, :], jnp.where(hits[1], gates_ref[1:2, :], 0.0))
    gate = jnp.sum(weighted, axis=1, keepdims=True)
    rows_ref[...] = mm(take, h_ref[...]).astype(BF16)
    grads_ref[...] = (dy_rows_ref[...].astype(F32) * gate).astype(BF16)
    gate_ref[...] = gate


def dispatch(code, routes_t, router_t, h, dy_rows):
    slots, width = dy_rows.shape
    tile = slots // 4
    row_spec = pl.BlockSpec((tile, width), lambda i: (i, 0))
    whole = lambda shape: pl.BlockSpec(shape, lambda i: (0, 0))
    return pl.pallas_call(
        dispatch_kernel,
        grid=(4,),
        in_specs=[whole(code.shape), whole(code.shape), whole(router_t.shape), whole(h.shape), row_spec],
        out_specs=[row_spec, row_spec, pl.BlockSpec((tile, 1), lambda i: (i, 0)), whole(code.shape)],
        out_shape=[jax.ShapeDtypeStruct((slots, width), BF16)] * 2
        + [jax.ShapeDtypeStruct((slots, 1), F32), jax.ShapeDtypeStruct(code.shape, F32)],
        compiler_params=params(),
        cost_estimate=cost(4 * slots * SEQ * width, 4 * MIB + 6 * slots * width),
    )(code, routes_t, router_t, h, dy_rows)


def gelu_parts(x):
    inner = 0.7978845608028654 * (x + 0.044715 * (x * x * x))
    bend = jnp.tanh(inner)
    half = 0.5 * (1.0 + bend)
    slope = half + 0.5 * x * (1.0 - bend * bend) * (
        0.7978845608028654 * (1.0 + 3.0 * 0.044715 * (x * x))
    )
    return x * half, slope


def partner_of(index, step):
    found = index
    for bit in (1, 2, 4):
        found = found + ((step // bit) % 2) * (1 - 2 * ((index // bit) % 2)) * bit
    return found


def expert_kernel(
    rows_in, grads_in, gate_in, up_in, down_in, far_gate, far_gate_too,
    ret_out, back_out, own_gate, own_up, own_down, got_gate, got_up, got_down,
    rows, grads, weights, sums, parts, opened, z_send, z_recv, y_send, y_recv, p_send, p_recv, r_send, r_recv, w_send, w_recv, g_send, g_recv, local,
):
    groups, half, width = rows.shape[1:]
    group, rank = lax.axis_index("expert"), lax.axis_index("tensor")
    pair_class, half_index = rank % 2, rank // 2
    across = {"tensor": rank + 1 - 2 * pair_class}
    along = {"tensor": rank + 2 - 4 * half_index}
    mesh_ids = pl.DeviceIdType.MESH
    moved = ((rows_in, rows, ret_out), (grads_in, grads, back_out))

    barrier = pltpu.get_barrier_semaphore()
    for step in range(1, groups):
        pl.semaphore_signal(
            barrier, inc=1, device_id={"expert": partner_of(group, step)}, device_id_type=mesh_ids
        )
    pl.semaphore_signal(barrier, inc=1, device_id=across, device_id_type=mesh_ids)
    pl.semaphore_signal(barrier, inc=1, device_id=along, device_id_type=mesh_ids)
    pl.semaphore_wait(barrier, groups + 1)

    def remote(source, target, send, recv, device):
        return pltpu.make_async_remote_copy(
            src_ref=source, dst_ref=target, send_sem=send, recv_sem=recv,
            device_id=device, device_id_type=mesh_ids,
        )

    def block(ref, number):
        return ref.at[pl.ds(pl.multiple_of(number * half, half), half)]

    def out_of(kind, step):
        source, held, _ = moved[kind]
        other = partner_of(group, step)
        return remote(
            block(source, other), held.at[0, group], z_send.at[kind, step], z_recv.at[kind, step], {"expert": other}
        )

    def forward(kind, step):
        held = moved[kind][1]
        other = partner_of(group, step)
        return remote(held.at[0, other], held.at[1, other], y_send.at[kind, step], y_recv.at[kind, step], along)

    def partial_sum(kind, step):
        held = moved[kind][1]
        other = partner_of(group, step)
        return remote(held.at[1, other], parts.at[kind, other], p_send.at[kind, step], p_recv.at[kind, step], along)

    def result(kind, step):
        other = partner_of(group, step)
        return remote(
            parts.at[kind, other], block(moved[kind][2], group), r_send.at[kind, step], r_recv.at[kind, step], {"expert": other}
        )

    def own_result(kind):
        return pltpu.make_async_copy(parts.at[kind, group], block(moved[kind][2], group), local.at[kind])

    own = [
        pltpu.make_async_copy(block(moved[kind][0], group), moved[kind][1].at[0, group], local.at[kind])
        for kind in range(2)
    ]
    for copy in own:
        copy.start()
    kept = [
        pltpu.make_async_copy(ref.at[pair_class], weights.at[number, 0], local.at[2 + number])
        for number, ref in enumerate((gate_in, up_in, down_in))
    ]
    for number, ref in enumerate((far_gate, far_gate_too)):
        target = weights.at[0, 1, pl.ds(number * far_gate.shape[0], ref.shape[0])]
        kept.append(pltpu.make_async_copy(ref, target, local.at[5 + number]))
    kept += [
        remote(ref.at[1 - pair_class], weights.at[number, 1], w_send.at[number - 1], w_recv.at[number - 1], across)
        for number, ref in ((1, up_in), (2, down_in))
    ]
    for copy in kept:
        copy.start()
    for step in range(1, groups):
        for kind in range(2):
            out_of(kind, step).start()

    def arrive(step):
        for kind in range(2):
            out_of(kind, step).wait()
            forward(kind, step).start()

    def give(step):
        for kind in range(2):
            partial_sum(kind, step).start()

    for number in range(3):
        for part in range(2):
            sums[number, part] = jnp.zeros(sums.shape[2:], F32)

    def finish(step):
        other = partner_of(group, step)
        for kind in range(2):
            partial_sum(kind, step).wait()
            held = moved[kind][1]
            parts[kind, other] = (parts[kind, other].astype(F32) + held[0, other].astype(F32)).astype(BF16)

        for kind in range(2):
            if step == 0:
                own_result(kind).start()
            else:
                result(kind, step).start()

    def act(plan):
        for action, step in plan:
            action(step)

    order = ((0, 0, 0), (1, 0, 1), (2, 0, 2), (3, 0, 3), (2, 1, 2), (4, 0, 2), (4, 1, 2), (5, 0, 2), (5, 1, 2), (3, 1, 3), (1, 1, 1), (0, 1, 0), (6, 0, 0), (6, 1, 0), (7, 0, 0), (7, 1, 0))
    before = {
        0: [(arrive, 1), (arrive, 2)],
        1: [(arrive, 3)],
        2: [(arrive, 4)],
        3: [(arrive, 5)],
        5: [(give, 2)],
        7: [(give, 4)],
        8: [(arrive, 6)],
        10: [(finish, 2)],
        12: [(arrive, 7), (finish, 4), (give, 5)],
        14: [(give, 6)],
    }
    ahead = [(give, 7)]
    last = [(finish, 5), (give, 3), (finish, 6), (give, 1), (finish, 7), (give, 0), (finish, 3), (finish, 1), (finish, 0)]
    first_far = [part for _, part, _ in order].index(1)
    for copy in own:
        copy.wait()
    for kind in range(2):
        forward(kind, 0).start()

    def body(turn, carry):
        for number, plan in before.items():
            pl.when(turn == number)(partial(act, plan))

        @pl.when(turn == 0)
        def _():
            for copy in kept[:3]:
                copy.wait()

        @pl.when(turn == first_far)
        def _():
            for copy in kept[3:]:
                copy.wait()

        step, part, place = (
            sum((turn == number).astype(jnp.int32) * unit[k] for number, unit in enumerate(order)) for k in range(3)
        )
        other = partner_of(group, step)

        @pl.when(part == 0)
        def _():
            for kind in range(2):
                forward(kind, step).wait()

        tile = jnp.concatenate([rows[0, other], rows[1, other]], axis=0)
        grad = jnp.concatenate([grads[0, other], grads[1, other]], axis=0)
        w_gate, w_up, w_down = weights[0, part], weights[1, part], weights[2, part]
        gate_part = mm(tile, w_gate, NT)
        up_part = mm(tile, w_up, NT)
        grad_hidden = mm(grad, w_down, NT)
        bent, slope = gelu_parts(gate_part)
        hidden = (bent * up_part).astype(BF16)
        grad_gate = (grad_hidden * up_part * slope).astype(BF16)
        grad_up = (grad_hidden * bent).astype(BF16)
        results = mm(hidden, w_down), mm(grad_gate, w_gate) + mm(grad_up, w_up)
        sums[0, part] += mm(grad_gate, tile, TN)
        sums[1, part] += mm(grad_up, tile, TN)
        sums[2, part] += mm(hidden, grad, TN)

        @pl.when(part == 0)
        def _():
            for kind, value in enumerate(results):
                opened[place, kind] = value.astype(BF16)

        @pl.when(part == 1)
        def _():
            for kind, value in enumerate(results):
                held = moved[kind][1]
                value = value + opened[place, kind].astype(F32)
                held[0, other] = value[:half].astype(BF16)
                held[1, other] = value[half:].astype(BF16)

        return carry

    lax.fori_loop(0, len(order), body, 0)
    act(ahead)
    copies = []
    for number, (own_ref, got_ref) in enumerate(((own_gate, got_gate), (own_up, got_up), (own_down, got_down))):
        weights[number, 0] = sums[number, 1].astype(BF16)
        copies.append(remote(weights.at[number, 0], got_ref, g_send.at[number], g_recv.at[number], across))
        copies[-1].start()
        copies.append(pltpu.make_async_copy(sums.at[number, 0], own_ref, local.at[2 + number]))
        copies[-1].start()
    act(last)
    for copy in copies:
        copy.wait()
    for kind in range(2):
        own_result(kind).wait()
        for step in range(1, groups):
            result(kind, step).wait()


def run_experts(rows, grads, w_gate, w_up, w_down, far_gate, far_gate_too):
    slots, width = rows.shape
    half = CAP // 2
    groups = slots // half
    units = w_gate.shape[1]
    anywhere = pl.BlockSpec(memory_space=pl.ANY)
    pair = pltpu.SemaphoreType.DMA((2, groups))
    return pl.pallas_call(
        expert_kernel,
        in_specs=[anywhere] * 7,
        out_specs=[anywhere] * 8,
        out_shape=[jax.ShapeDtypeStruct((slots, width), BF16)] * 2
        + [jax.ShapeDtypeStruct((units, width), F32)] * 3
        + [jax.ShapeDtypeStruct((units, width), BF16)] * 3,
        scratch_shapes=[
            pltpu.VMEM((2, groups, half, width), BF16),
            pltpu.VMEM((2, groups, half, width), BF16),
            pltpu.VMEM((3, 2, units, width), BF16),
            pltpu.VMEM((3, 2, units, width), F32),
            pltpu.VMEM((2, groups, half, width), BF16),
            pltpu.VMEM((4, 2, 2 * half, width), BF16),
        ]
        + [pair] * 8
        + [pltpu.SemaphoreType.DMA((2,))] * 2
        + [pltpu.SemaphoreType.DMA((3,))] * 2
        + [pltpu.SemaphoreType.DMA((7,))],
        compiler_params=pltpu.CompilerParams(
            vmem_limit_bytes=60 * MIB, collective_id=1, has_side_effects=True
        ),
        cost_estimate=cost(72 * slots * units * width, 16 * slots * width + 30 * units * width),
    )(rows, grads, w_gate, w_up, w_down, far_gate, far_gate_too)


def finish_kernel(
    rows_ref, y_ref, summed_ref, small_ref,
    output_ref, grad_ref, in_ref, out_ref, one_ref, two_ref, router_ref, bias_ref,
):
    step = pl.program_id(0)
    output_ref[...] = y_ref[...].astype(F32).T.astype(BF16)
    grad_ref[...] = rows_ref[...].astype(F32).T

    @pl.when(step < 3)
    def _():
        in_ref[...] = summed_ref[...].astype(F32)

    @pl.when(step == 3)
    def _():
        out_ref[...] = summed_ref[...].astype(F32)
        router_ref[...] = small_ref[:EXPERTS]
        two_ref[...] = small_ref[EXPERTS : EXPERTS + 1]
        one_ref[...] = small_ref[EXPERTS + 1 : EXPERTS + 2]
        bias_ref[...] = small_ref[EXPERTS + 2 : EXPERTS + 2 + bias_ref.shape[0], :BUCKETS]


def finish_outputs(rows, y_rows, summed, small, heads):
    tokens, width = rows.shape
    steps = 4
    tile, block = tokens // steps, summed.shape[0] // steps
    token_spec = pl.BlockSpec((tile, width), lambda i: (i, 0))
    feature_spec = pl.BlockSpec((width, tile), lambda i: (0, i))
    whole = lambda *shape: pl.BlockSpec(shape, lambda i: (0, 0))
    return pl.pallas_call(
        finish_kernel,
        grid=(steps,),
        in_specs=[
            token_spec,
            token_spec,
            pl.BlockSpec((block, width), lambda i: (i, 0)),
            whole(*small.shape),
        ],
        out_specs=[
            feature_spec,
            feature_spec,
            pl.BlockSpec((block, width), lambda i: (jnp.minimum(i, 2), 0)),
            whole(block, width),
            whole(1, width),
            whole(1, width),
            whole(EXPERTS, width),
            whole(heads, BUCKETS),
        ],
        out_shape=[
            jax.ShapeDtypeStruct((width, tokens), BF16),
            jax.ShapeDtypeStruct((width, tokens), F32),
            jax.ShapeDtypeStruct((3 * block, width), F32),
            jax.ShapeDtypeStruct((block, width), F32),
            jax.ShapeDtypeStruct((1, width), F32),
            jax.ShapeDtypeStruct((1, width), F32),
            jax.ShapeDtypeStruct((EXPERTS, width), F32),
            jax.ShapeDtypeStruct((heads, BUCKETS), F32),
        ],
        compiler_params=params(),
        cost_estimate=cost(0, 10 * rows.size + 6 * summed.size),
    )(rows, y_rows, summed, small)


def on_device(
    layer_input, gain_one, attn_in, rel_bias, attn_out, gain_two, router,
    expert_gate, expert_up, expert_down, routes, piece_starts, grad_out,
):
    width, tokens = layer_input.shape
    ranks = lax.axis_size("tensor")
    groups = lax.axis_size("expert")
    rank = lax.axis_index("tensor")
    pair_class, half_index = rank % 2, rank // 2
    half = CAP // 2

    units = expert_gate.shape[1]
    other = lax.dynamic_slice(expert_gate, (1 - pair_class, 0, 0), (1, units // 11 * 4, width))[0]
    traded = lax.ppermute(other, "tensor", [(r, r ^ 1) for r in range(ranks)])
    w_in = attn_in.reshape(-1, width)
    qkv, scale_one, tiles = project(layer_input, gain_one[None], w_in, rel_bias.T)
    position = jnp.arange(SEQ, dtype=jnp.int32)[None, None, :]
    starts = piece_starts[:, :, None]
    inside = (position >= starts) & (position < starts + PIECE)
    last = jnp.max(jnp.where(inside, starts + (PIECE - 1), -1), axis=1)
    limits = jnp.maximum(last, position[0])[:, None, :]

    routes_t = routes.T
    place = jnp.stack([pair_class, half_index]).astype(jnp.int32)
    share = tokens // ranks

    def by_rank(rows):
        return rows.reshape(ranks, share, width)

    qkv, traded = lax.optimization_barrier((qkv, traded))
    slots = groups * half
    heads = rel_bias.shape[1]
    h2, resid, scale_two, dy, dy_rows, code, code_cols, own_x, mixed, lse, traded_too = exchange_call(
        norm_two_kernel, 2, (tokens, width),
        [qkv, tiles, limits, attn_out, layer_input, gain_two[None], grad_out, routes_t, expert_gate],
        [((share, width), F32), ((share, 1), F32), ((tokens, width), BF16), ((slots, width), BF16)]
        + [((TOP, tokens), jnp.int32), ((tokens, TOP), jnp.int32), ((share, width), BF16)]
        + [(attn_out.shape[:1] + (tokens,), BF16), ((heads * tokens // SEQ, 1, SEQ), F32), ((units - traded.shape[0], width), BF16)],
        [pltpu.VMEM((ranks, share, width), BF16), pltpu.VMEM((width, share), BF16), pltpu.VMEM((width, tokens), BF16)]
        + [pltpu.VMEM((tokens, width), BF16), pltpu.VMEM((slots, width), BF16), pltpu.SemaphoreType.DMA((4,))]
        + [pltpu.SemaphoreType.DMA((2,))] * 2,
        (4, 6, 8),
        (2, 3, 9),
    )
    rows, row_grads, gate_rows, gates = dispatch(code, routes_t, router.T, h2, dy_rows)
    ret, back, *weight_grads = run_experts(
        rows, row_grads, expert_gate, expert_up, expert_down, traded, traded_too
    )
    grad_attn, grad_resid, grad_gain_two, grad_router, partial_y = exchange_call(
        norm_two_back_kernel, 3, (tokens, width),
        [ret, back, code, code_cols, gates, routes_t, dy_rows, gate_rows, router.T, h2]
        + [resid, scale_two, dy, gain_two[None]],
        [((share, width), F32), ((1, width), F32), ((EXPERTS, width), F32), ((tokens, width), BF16)],
        [
            pltpu.VMEM((ranks, share, width), BF16),
            pltpu.VMEM((slots, width), BF16),
            pltpu.VMEM((ranks + 3, EXPERTS, share), F32),
            pltpu.VMEM((2 * EXPERTS, share), BF16),
        ]
        + [pltpu.SemaphoreType.DMA((3,))] * 2
        + [pltpu.VMEM((slots, width), BF16)] * 2
        + [pltpu.VMEM((tokens, width), BF16), pltpu.VMEM((share, width), F32), pltpu.VMEM((share, width), BF16)]
        + [pltpu.VMEM((ranks, share, width), BF16), pltpu.SemaphoreType.DMA((9,))],
        (0, 6, 9, 10, 12),
        (3,),
    )

    dq, dk, dv, near, far, y_own = attend_back(
        qkv, tiles, limits, attn_out, grad_attn, lse, by_rank(partial_y), resid
    )
    dq, y_own = lax.optimization_barrier((dq, y_own))
    y_across = lax.ppermute(y_own, "tensor", [(r, r ^ 1) for r in range(ranks)])
    y_along = lax.ppermute(y_own, "tensor", [(r, r ^ 2) for r in range(ranks)])
    weight_rows, sent, grad_gain_one, grad_gate, grad_up, grad_down = project_back(
        place, layer_input, gain_one[None], scale_one, w_in, mixed, grad_attn, (dq, dk, dv),
        weight_grads[:3], weight_grads[3:],
    )
    sent, y_across, y_along = lax.optimization_barrier((sent, y_across, y_along))
    summed = lax.psum(weight_rows, "expert")
    small_shape = (BUCKETS, width)
    grad_rows, y_full, small = exchange_call(
        norm_one_back_kernel, 4, sent.shape,
        [by_rank(sent), own_x, scale_one, grad_resid, gain_one[None], y_own, y_across, y_along]
        + [grad_gain_one, grad_gain_two, grad_router, near, far],
        [((ranks, share, width), BF16), (small_shape, F32)],
        [pltpu.VMEM((share, width), BF16), pltpu.VMEM((share, width), F32)]
        + [pltpu.VMEM((4, *small_shape), F32), pltpu.VMEM((groups, *small_shape), BF16), pltpu.VMEM(near.shape, F32), pltpu.VMEM((share, 1), F32)]
        + [pltpu.SemaphoreType.DMA((3,))]
        + [pltpu.SemaphoreType.DMA((2,))] * 2
        + [pltpu.SemaphoreType.DMA((groups,))] * 2,
        (1, 3, 11),
        (0,),
    )
    summed, grad_rows = lax.optimization_barrier((summed, grad_rows))
    layer_output, grad_input, grad_in, grad_attn_out, grad_one, grad_two, grad_router, grad_bias = finish_outputs(
        grad_rows, y_full.reshape(tokens, width), summed, small, rel_bias.shape[1]
    )
    return (
        layer_output,
        grad_input,
        grad_one[0],
        grad_in.reshape(attn_in.shape),
        grad_bias.T,
        grad_attn_out,
        grad_two[0],
        grad_router.T,
        grad_gate,
        grad_up,
        grad_down,
    )


def allowed_pairs(seq_starts):
    position = jnp.arange(SEQ, dtype=jnp.int32)
    inside = (position[:, None] >= seq_starts[None, :]) & (
        position[:, None] < seq_starts[None, :] + PIECE
    )
    numbers = jnp.arange(seq_starts.shape[0], dtype=jnp.int32) + 1
    piece_label = jnp.sum(inside.astype(jnp.int32) * numbers[None, :], axis=1)
    causal = position[None, :] <= position[:, None]
    shared = (piece_label[:, None] == piece_label[None, :]) & (piece_label[:, None] > 0)
    return causal | shared


def slot_table(routes):
    flat_routes = routes.reshape(-1)
    onehot = (flat_routes[:, None] == jnp.arange(EXPERTS, dtype=jnp.int32)[None, :]).astype(
        jnp.int32
    )
    blocks = onehot.reshape(-1, 128, EXPERTS).astype(F32)
    earlier = jnp.tril(jnp.ones((128, 128), F32), -1)
    inside = jnp.einsum("ij,bje->bie", earlier, blocks)
    count = blocks.shape[0]
    carried = jnp.einsum("ab,be->ae", jnp.tril(jnp.ones((count, count), F32), -1), jnp.sum(blocks, axis=1), precision=HIGH)
    before = (inside + carried[:, None, :]).astype(jnp.int32).reshape(onehot.shape)
    slot_number = jnp.sum(before * onehot, axis=1)
    kept_pairs = slot_number < CAP
    slot_index = jnp.where(kept_pairs, flat_routes * CAP + slot_number, EXPERTS * CAP)
    return (slot_index.reshape(routes.shape), kept_pairs.reshape(routes.shape))


def bucket_onehot():
    offsets = jnp.arange(2 * SEQ - 1, dtype=jnp.int32) - (SEQ - 1)
    return (bucket_of(offsets)[:, None] == jnp.arange(BUCKETS, dtype=jnp.int32)[None, :]).astype(
        jnp.float32
    )


def expand_line(line):
    head_count = line.shape[0]
    padded = jnp.concatenate([line, jnp.zeros((head_count, 1), line.dtype)], axis=1)
    tiled = jnp.tile(padded, (1, SEQ))[:, : SEQ * (2 * SEQ - 1)].reshape(
        head_count, SEQ, 2 * SEQ - 1
    )
    return tiled[:, :, SEQ - 1 :]


def fold_line(full_grid):
    head_count = full_grid.shape[0]
    padded = jnp.pad(full_grid, ((0, 0), (0, 0), (SEQ - 1, 0))).reshape(
        head_count, SEQ * (2 * SEQ - 1)
    )
    padded = jnp.pad(padded, ((0, 0), (0, SEQ))).reshape(head_count, SEQ, 2 * SEQ)
    return jnp.sum(padded, axis=1)[:, : 2 * SEQ - 1]


def reduce_heads(tensor_value):
    return lax.psum(tensor_value, "tensor")


def spread_slots(tensor_value):
    return lax.all_gather(tensor_value, "tensor", axis=2, tiled=True)


def owner_exchange(tensor_value):
    return lax.all_to_all(tensor_value, "expert", split_axis=0, concat_axis=0, tiled=True)


def expert_sums(tensor_value):
    return lax.psum_scatter(tensor_value, "tensor", scatter_dimension=2, tiled=True)


def norm_forward(resid, gain, model_width):
    scale = lax.rsqrt(jnp.sum(resid * resid, axis=1) / model_width + EPS)[:, None]
    return (scale, (resid * scale * gain).astype(jnp.bfloat16))


def norm_backward(resid, scale, gain, grad_normed, model_width):
    grad_gain = jnp.sum(grad_normed * resid * scale, axis=0)
    scaled = grad_normed * gain
    inner = jnp.sum(scaled * resid, axis=1)[:, None]
    return (grad_gain, scale * scaled - resid * scale**3 * inner / model_width)


def attend_scores(bias_full, queries, key_rows, seq_starts):
    scores = (
        jnp.einsum("qhe,khe->hqk", queries, key_rows, preferred_element_type=jnp.float32) * 0.125
        + bias_full
    )
    return jnp.where(allowed_pairs(seq_starts)[None], scores, NEG)


def attend_forward(bias_full, inputs):
    queries, key_rows, value_rows, seq_starts = inputs
    scores = attend_scores(bias_full, queries, key_rows, seq_starts)
    row_max = jnp.max(scores, axis=2, keepdims=True)
    exponent = jnp.exp(scores - row_max)
    row_sum_exp = jnp.sum(exponent, axis=2, keepdims=True)
    weights = (exponent / row_sum_exp).astype(jnp.bfloat16)
    mixed_heads = jnp.einsum(
        "hqk,khe->qhe", weights, value_rows, preferred_element_type=jnp.float32
    )
    return (mixed_heads.astype(jnp.bfloat16), (row_max + jnp.log(row_sum_exp))[:, :, 0])


def attend_backward(bias_full, running, inputs):
    queries, key_rows, value_rows, grad_heads, seq_starts, log_total = inputs
    scores = attend_scores(bias_full, queries, key_rows, seq_starts)
    probabilities = jnp.exp(scores - log_total[:, :, None])
    grad_probs = jnp.einsum(
        "qhe,khe->hqk", grad_heads, value_rows, preferred_element_type=jnp.float32
    )
    inner = jnp.sum(probabilities * grad_probs, axis=2, keepdims=True)
    grad_scores = (probabilities * (grad_probs - inner)).astype(jnp.bfloat16)
    grad_values = jnp.einsum(
        "hqk,qhe->khe",
        probabilities.astype(jnp.bfloat16),
        grad_heads,
        preferred_element_type=jnp.float32,
    )
    grad_queries = (
        jnp.einsum("hqk,khe->qhe", grad_scores, key_rows, preferred_element_type=jnp.float32)
        * 0.125
    )
    grad_keys = (
        jnp.einsum("hqk,qhe->khe", grad_scores, queries, preferred_element_type=jnp.float32) * 0.125
    )
    return (
        running + grad_scores.astype(jnp.float32),
        jnp.stack([grad_queries, grad_keys, grad_values]),
    )


def gelu_product(left, right):
    return jax.nn.gelu(left, approximate=True) * right


def expert_forward(received, weight_gate, weight_up, weight_down):
    gate_part = jnp.einsum(
        "secd,efd->secf", received, weight_gate, preferred_element_type=jnp.float32
    )
    up_part = jnp.einsum("secd,efd->secf", received, weight_up, preferred_element_type=jnp.float32)
    hidden = gelu_product(gate_part, up_part).astype(jnp.bfloat16)
    partial_out = jnp.einsum(
        "secf,efd->secd", hidden, weight_down, preferred_element_type=jnp.float32
    )
    return (gate_part, up_part, hidden, partial_out)


def expert_backward(
    received, gate_part, up_part, hidden, grad_rows_out, weight_gate, weight_up, weight_down
):
    grad_hidden = jnp.einsum(
        "secd,efd->secf", grad_rows_out, weight_down, preferred_element_type=jnp.float32
    )
    product_value, pullback = jax.vjp(gelu_product, gate_part, up_part)
    grad_gate_part, grad_up_part = pullback(grad_hidden)
    grad_gate_part = grad_gate_part.astype(jnp.bfloat16)
    grad_up_part = grad_up_part.astype(jnp.bfloat16)
    grad_down = jnp.einsum(
        "secf,secd->efd", hidden, grad_rows_out, preferred_element_type=jnp.float32
    )
    grad_gate_w = jnp.einsum(
        "secf,secd->efd", grad_gate_part, received, preferred_element_type=jnp.float32
    )
    grad_up_w = jnp.einsum(
        "secf,secd->efd", grad_up_part, received, preferred_element_type=jnp.float32
    )
    grad_rows_in = jnp.einsum(
        "secf,efd->secd", grad_gate_part, weight_gate, preferred_element_type=jnp.float32
    )
    grad_rows_in = grad_rows_in + jnp.einsum(
        "secf,efd->secd", grad_up_part, weight_up, preferred_element_type=jnp.float32
    )
    return (grad_gate_w, grad_up_w, grad_down, grad_rows_in)


def on_device_general(
    layer_input,
    gain_one,
    attn_in,
    rel_bias,
    attn_out,
    gain_two,
    router,
    expert_gate,
    expert_up,
    expert_down,
    routes,
    piece_starts,
    grad_out,
):
    tok_count = layer_input.shape[1]
    model_width = layer_input.shape[0]
    heads_here = rel_bias.shape[1]
    head_width = attn_in.shape[1] // heads_here
    seqs_here = piece_starts.shape[0]
    local_experts = expert_gate.shape[0]
    part_rows = CAP // lax.axis_size("tensor")
    share_start = lax.axis_index("tensor") * part_rows
    tokens = layer_input.T.astype(jnp.float32)
    scale_one, normed = norm_forward(tokens, gain_one, model_width)
    project = jnp.einsum("td,chd->cth", normed, attn_in, preferred_element_type=jnp.float32).astype(
        jnp.bfloat16
    )
    by_seq = project.reshape(3, seqs_here, SEQ, heads_here, head_width)
    onehot_line = bucket_onehot()
    bias_full = expand_line(jnp.dot(onehot_line, rel_bias, precision=HIGH).T)
    mixed_heads, log_total = lax.map(
        partial(attend_forward, bias_full), (by_seq[0], by_seq[1], by_seq[2], piece_starts)
    )
    mixed_heads = mixed_heads.reshape(tok_count, heads_here * head_width)
    resid = tokens + reduce_heads(
        jnp.dot(mixed_heads, attn_out, preferred_element_type=jnp.float32)
    )
    scale_two, normed_two = norm_forward(resid, gain_two, model_width)
    logits = jnp.dot(normed_two, router, preferred_element_type=jnp.float32)
    chosen = (routes[:, :, None] == jnp.arange(EXPERTS, dtype=jnp.int32)[None, None, :]).astype(
        jnp.float32
    )
    picked = jnp.sum(chosen * logits[:, None, :], axis=2)
    gate_weights = jax.nn.softmax(picked, axis=1)
    slot_index, kept_pairs = slot_table(routes)
    keep_float = kept_pairs.astype(jnp.float32)
    mix_weight = gate_weights * keep_float
    safe_index = jnp.minimum(slot_index, EXPERTS * CAP - 1)
    token_rows = jnp.repeat(normed_two, TOP, axis=0)
    buffer = (
        jnp.zeros((EXPERTS * CAP + 1, model_width), jnp.bfloat16)
        .at[slot_index.reshape(-1)]
        .set(token_rows)
    )
    buffer = buffer[: EXPERTS * CAP].reshape(-1, local_experts, CAP, model_width)
    received = lax.all_to_all(buffer, "expert", split_axis=0, concat_axis=0, tiled=True)
    gate_part, up_part, hidden, partial_out = expert_forward(
        received, expert_gate, expert_up, expert_down
    )
    returned = spread_slots(owner_exchange(expert_sums(partial_out).astype(jnp.bfloat16)))
    flat_ret = returned.reshape(EXPERTS * CAP, model_width)
    fetched = flat_ret[safe_index].astype(jnp.float32)
    output = resid + jnp.sum(mix_weight[:, :, None] * fetched, axis=1)
    grad_y = grad_out.T.astype(jnp.float32)
    grad_gates = jnp.sum(grad_y[:, None, :] * fetched, axis=2) * keep_float
    grad_picked = gate_weights * (
        grad_gates - jnp.sum(gate_weights * grad_gates, axis=1, keepdims=True)
    )
    grad_logits = jnp.sum(chosen * grad_picked[:, :, None], axis=1)
    grad_router = jnp.dot(normed_two.astype(jnp.float32).T, grad_logits, precision=HIGH)
    grad_normed_two = jnp.dot(grad_logits, router.astype(jnp.float32).T, precision=HIGH)
    slot_grads = (mix_weight[:, :, None] * grad_y[:, None, :]).astype(jnp.bfloat16)
    grad_ret = (
        jnp.zeros((EXPERTS * CAP + 1, model_width), jnp.bfloat16)
        .at[slot_index.reshape(-1)]
        .set(slot_grads.reshape(-1, model_width))
    )
    grad_ret = grad_ret[: EXPERTS * CAP].reshape(-1, local_experts, CAP, model_width)
    grad_share = lax.dynamic_slice_in_dim(grad_ret, share_start, part_rows, 2)
    grad_rows_out = spread_slots(owner_exchange(grad_share))
    grad_expert_gate, grad_expert_up, grad_expert_down, grad_rows_in = expert_backward(
        received, gate_part, up_part, hidden, grad_rows_out, expert_gate, expert_up, expert_down
    )
    grad_back = spread_slots(owner_exchange(expert_sums(grad_rows_in).astype(jnp.bfloat16)))
    flat_back = grad_back.reshape(EXPERTS * CAP, model_width).astype(jnp.float32)
    grad_normed_two = grad_normed_two + jnp.sum(
        flat_back[safe_index] * keep_float[:, :, None], axis=1
    )
    grad_gain_two, grad_resid = norm_backward(
        resid, scale_two, gain_two, grad_normed_two, model_width
    )
    grad_resid = grad_resid + grad_y
    grad_attn = grad_resid.astype(jnp.bfloat16)
    grad_attn_out = jnp.einsum(
        "th,td->hd", mixed_heads, grad_attn, preferred_element_type=jnp.float32
    )
    grad_mixed = jnp.einsum(
        "td,hd->th", grad_attn, attn_out, preferred_element_type=jnp.float32
    ).astype(jnp.bfloat16)
    grad_by_seq = grad_mixed.reshape(seqs_here, SEQ, heads_here, head_width)
    bias_grad_full, grad_project = lax.scan(
        partial(attend_backward, bias_full),
        jnp.zeros_like(bias_full),
        (by_seq[0], by_seq[1], by_seq[2], grad_by_seq, piece_starts, log_total),
    )
    grad_project = (
        jnp.moveaxis(grad_project, 1, 0)
        .reshape(3, tok_count, heads_here * head_width)
        .astype(jnp.bfloat16)
    )
    grad_attn_in = jnp.einsum(
        "cth,td->chd", grad_project, normed, preferred_element_type=jnp.float32
    )
    grad_normed = reduce_heads(
        jnp.einsum("cth,chd->td", grad_project, attn_in, preferred_element_type=jnp.float32)
    )
    grad_gain_one, grad_tokens = norm_backward(
        tokens, scale_one, gain_one, grad_normed, model_width
    )
    grad_tokens = grad_tokens + grad_resid
    grad_rel_bias = jnp.dot(onehot_line.T, fold_line(bias_grad_full).T, precision=HIGH)
    shared = (
        lax.psum(grad_gain_one.astype(jnp.bfloat16), "expert").astype(jnp.float32),
        lax.psum(grad_attn_in.astype(jnp.bfloat16), "expert").astype(jnp.float32),
        lax.psum(grad_rel_bias.astype(jnp.bfloat16), "expert").astype(jnp.float32),
        lax.psum(grad_attn_out.astype(jnp.bfloat16), "expert").astype(jnp.float32),
        lax.psum(grad_gain_two.astype(jnp.bfloat16), "expert").astype(jnp.float32),
        lax.psum(grad_router.astype(jnp.bfloat16), "expert").astype(jnp.float32),
    )
    return (
        output.astype(jnp.bfloat16).T,
        grad_tokens.T,
        shared[0],
        shared[1],
        shared[2],
        shared[3],
        shared[4],
        shared[5],
        grad_expert_gate,
        grad_expert_up,
        grad_expert_down,
    )


def solution(mesh):
    placed = (
        P(None, "expert"),
        P(),
        P(None, "tensor", None),
        P(None, "tensor"),
        P("tensor", None),
        P(),
        P(),
        P("expert", "tensor", None),
        P("expert", "tensor", None),
        P("expert", "tensor", None),
        P("expert", None),
        P("expert", None),
        P(None, "expert"),
    )
    paired = mesh.shape["tensor"] == 4 and mesh.shape["expert"] * 2 == EXPERTS
    return jax.shard_map(
        on_device if paired else on_device_general,
        mesh=mesh,
        in_specs=placed,
        out_specs=(
            P(None, "expert"),
            P(None, "expert"),
            P(),
            P(None, "tensor", None),
            P(None, "tensor"),
            P("tensor", None),
            P(),
            P(),
            P("expert", "tensor", None),
            P("expert", "tensor", None),
            P("expert", "tensor", None),
        ),
        check_vma=False,
    )
```
